32 devices in a mesh: gx: 4 (over y, core), gy: 8 (over z, x).
Axes of the slice: x: 2, y: 2, z: 4, core: 2. Of those that a mesh axis runs over, the one named last changes fastest.
Arguments:
- tokens: bfloat16 [16384, 2048], P('gy', 'gx'), may hold values from -6 to 6
- query_weight: bfloat16 [2048, 2048], P('gy', 'gx'), may hold values from -0.125 to 0.125
- key_weight: bfloat16 [2048, 2048], P('gy', 'gx'), may hold values from -0.125 to 0.125
- value_weight: bfloat16 [2048, 2048], P('gy', 'gx'), may hold values from -0.125 to 0.125
- output_weight: bfloat16 [2048, 2048], P('gx', 'gy'), may hold values from -0.125 to 0.125
- gate_weight: bfloat16 [2048, 8192], P('gy', 'gx'), may hold values from -0.125 to 0.125
- up_weight: bfloat16 [2048, 8192], P('gy', 'gx'), may hold values from -0.125 to 0.125
- down_weight: bfloat16 [8192, 2048], P('gx', 'gy'), may hold values from -0.0625 to 0.0625
- query_gain: float32 [2048], P('gx'), may hold values from 0.25 to 1.75
- key_gain: float32 [2048], P('gx'), may hold values from 0.25 to 1.75
- attn_gain: float32 [2048], P('gx'), may hold values from 0.25 to 1.75
- mlp_gain: float32 [2048], P('gx'), may hold values from 0.25 to 1.75
- seq_ids: int32 [8, 2048], P('gy'), may hold values from 0 to 3, never falling along the last dimension, each value on 1 to 1024 neighbouring positions
- out_grad: bfloat16 [16384, 2048], P('gy', 'gx'), may hold values from -6 to 6
Outputs:
- result: bfloat16 [16384, 2048], P('gy', 'gx')
- token_grad: float32 [16384, 2048], P('gy', 'gx')
- query_weight_grad: float32 [2048, 2048], P('gy', 'gx')
- key_weight_grad: float32 [2048, 2048], P('gy', 'gx')
- value_weight_grad: float32 [2048, 2048], P('gy', 'gx')
- output_weight_grad: float32 [2048, 2048], P('gx', 'gy')
- gate_weight_grad: float32 [2048, 8192], P('gy', 'gx')
- up_weight_grad: float32 [2048, 8192], P('gy', 'gx')
- down_weight_grad: float32 [8192, 2048], P('gx', 'gy')
- query_gain_grad: float32 [2048], P('gx')
- key_gain_grad: float32 [2048], P('gx')
- attn_gain_grad: float32 [2048], P('gx')
- mlp_gain_grad: float32 [2048], P('gx')
The draws below stay inside these ranges and needn't reach their ends.
Inputs may be any that keep to these rules, and one draw needn't show every extreme that they name: `seq_ids`: in each row of 2048 tokens the numbers never fall, every number appears, each sequence has 1 to 1024 tokens and one has exactly 1024.
All inputs are finite; a program needn't handle non-finite values.
Results may differ from the reference program's by a relative error of at most 0.024.
Values may be sent and summed in bfloat16 or wider, within the bound.
A program may use at most 320 MiB of HBM per device.

```python
import math
import jax
import jax.numpy as jnp
import numpy as np
from jax import lax

D = 2048
HEADS = 16
HEAD = 128
FF = 8192
TOK_BLOCK = 2048
MAX_LEN = 1024
SEGS = 4
BLOCKS = 8
TOKENS = 16384


def steps_of(stream_key, extent, pieces, low, largest):
    def one(position, shards_of):
        draws = jax.random.uniform(jax.random.fold_in(jax.random.fold_in(stream_key, 6), position), (shards_of,), jnp.float32, low / len(pieces), largest / len(pieces))
        return jnp.repeat(jnp.exp(draws), extent[position] // shards_of).reshape((-1,) + (1,) * (len(extent) - position - 1))

    loudness = one(*pieces[0])
    for cut in pieces[1:]:
        loudness = loudness * one(*cut)
    return loudness


def split_up(count, total, bound, skew):
    weights = [(1 << 20) // math.isqrt(grade ** skew) + 1 for grade in range(2, count + 1)]
    spare, counts = total - bound - (count - 1), [1] * (count - 1)
    while spare > 0:
        candidates = [i for i in range(count - 1) if counts[i] < bound]
        whole, budget = sum([weights[i] for i in candidates]), spare
        for i in candidates:
            extra = min(bound - counts[i], max(1, budget * weights[i] // whole), spare)
            counts[i] = counts[i] + extra
            spare = spare - extra
    return np.array([bound] + counts)


def uneven(rng, count, total, most, skew):
    if count == 2:
        one = jax.random.randint(rng, (), max(1, total - most), min(most, total - 1) + 1)
        return jnp.stack([one, total - one])
    tallies = jnp.asarray(split_up(count, total, most, skew), jnp.int32)
    pairs = (count - 1) // 2
    donor, taker = tallies[1:1 + 2 * pairs:2], tallies[2:2 + 2 * pairs:2]
    slack = jnp.minimum(donor - 1, most - taker)
    moved = jax.random.randint(jax.random.fold_in(rng, 1), (pairs,), 0, 1 << 20) % (slack + 1)
    tallies = tallies.at[1:1 + 2 * pairs:2].set(donor - moved).at[2:2 + 2 * pairs:2].set(taker + moved)
    return tallies[jax.random.permutation(jax.random.fold_in(rng, 2), count)]


def gaussian(key, extent, deviation, reach, split=(), kind=jnp.bfloat16):
    level = steps_of(key, extent, split, -0.22, 0.18) if split else 1.0
    entries = jax.random.normal(key, extent, jnp.float32) * deviation * level
    return jnp.minimum(jnp.maximum(entries, -reach), reach).astype(kind)


def setup_inputs(seed: int = 0) -> dict:
    key_list = jax.random.split(jax.random.key(seed), 15)
    tokens = gaussian(key_list[0], (TOKENS, D), 1.0, 6.0, ((0, 8), (1, 4)))
    query_weight = gaussian(key_list[1], (D, D), D ** -0.5, 0.125, ((0, 8), (1, 4)))
    key_weight = gaussian(key_list[2], (D, D), D ** -0.5, 0.125, ((0, 8), (1, 4)))
    value_weight = gaussian(key_list[3], (D, D), D ** -0.5, 0.125, ((0, 8), (1, 4)))
    output_weight = gaussian(key_list[4], (D, D), D ** -0.5, 0.125, ((0, 4), (1, 8)))
    gate_weight = gaussian(key_list[5], (D, FF), D ** -0.5, 0.125, ((0, 8), (1, 4)))
    up_weight = gaussian(key_list[6], (D, FF), D ** -0.5, 0.125, ((0, 8), (1, 4)))
    down_weight = gaussian(key_list[7], (FF, D), FF ** -0.5, 0.0625, ((0, 4), (1, 8)))
    query_gain = jnp.clip(1.0 + 0.15 * jax.random.normal(key_list[8], (D,), jnp.float32), 0.25, 1.75)
    key_gain = jnp.clip(1.0 + 0.15 * jax.random.normal(key_list[9], (D,), jnp.float32), 0.25, 1.75)
    attn_gain = jnp.clip(1.0 + 0.15 * jax.random.normal(key_list[10], (D,), jnp.float32), 0.25, 1.75)
    mlp_gain = jnp.clip(1.0 + 0.15 * jax.random.normal(key_list[11], (D,), jnp.float32), 0.25, 1.75)
    seq_ids = jax.vmap(lambda own: jnp.searchsorted(jnp.cumsum(uneven(own, SEGS, TOK_BLOCK, MAX_LEN, 2)), jnp.arange(TOK_BLOCK), side="right"))(jax.random.split(key_list[12], BLOCKS)).reshape((BLOCKS, TOK_BLOCK)).astype(jnp.int32)
    out_grad = gaussian(key_list[13], (TOKENS, D), 1.0, 6.0, ((0, 8), (1, 4)))
    return {"tokens": tokens, "query_weight": query_weight, "key_weight": key_weight, "value_weight": value_weight, "output_weight": output_weight, "gate_weight": gate_weight, "up_weight": up_weight, "down_weight": down_weight, "query_gain": query_gain, "key_gain": key_gain, "attn_gain": attn_gain, "mlp_gain": mlp_gain, "seq_ids": seq_ids, "out_grad": out_grad}


EPS = 1e-06
THETA = 500000.0
NEGATIVE = -1e+30

@jax.custom_vjp
def low(v):
    return lax.optimization_barrier(v.astype(jnp.bfloat16)).astype(jnp.float32)

@jax.custom_vjp
def low_back(v):
    return v

def low_keep(v):
    return (low(v), None)

def low_pass(kept, grad):
    return (grad,)

def back_keep(v):
    return (v, None)

def back_low(kept, grad):
    return (low(grad),)
low.defvjp(low_keep, low_pass)
low_back.defvjp(back_keep, back_low)

def mult(left, right):
    return jnp.dot(left, right, precision=lax.Precision.HIGHEST, preferred_element_type=jnp.float32)

def normalize(values, gain):
    return values * lax.rsqrt(lax.optimization_barrier(jnp.mean(values * values, axis=-1, keepdims=True)) + EPS) * gain

def token_positions(segment):
    length = segment.shape[0]
    labels = jnp.arange(SEGS, dtype=jnp.int32)
    member = (segment[:, None] == labels[None, :]).astype(jnp.int32)
    totals = lax.optimization_barrier(jnp.sum(member, axis=0))
    starts = jnp.cumsum(totals) - totals
    opening = lax.optimization_barrier(jnp.sum(member * starts[None, :], axis=1))
    return jnp.arange(length, dtype=jnp.int32) - opening

def rotary_tables(segment):
    place = token_positions(segment).astype(jnp.float32)
    halves = HEAD // 2
    inverse = jnp.exp(jnp.arange(halves, dtype=jnp.float32) * (-2.0 * math.log(THETA) / HEAD))
    angle = place[:, None] * inverse[None, :]
    return (jnp.cos(angle), jnp.sin(angle))

def rotate(values, cosine, sine):
    halves = values.shape[-1] // 2
    former = values[..., :halves]
    latter = values[..., halves:]
    cosine = cosine[:, None, :]
    sine = sine[:, None, :]
    return jnp.concatenate([former * cosine - latter * sine, latter * cosine + former * sine], axis=-1)

def head_attention(inputs, segment):
    query, key, value = inputs
    order = jnp.arange(segment.shape[0], dtype=jnp.int32)
    allowed = (segment[:, None] == segment[None, :]) & (order[None, :] <= order[:, None])
    scores = low_back(mult(query, key.T) * (1.0 / math.sqrt(HEAD)))
    scores = jnp.where(allowed, scores, NEGATIVE)
    probability = low(jax.nn.softmax(scores, axis=-1))
    return mult(probability, value)

def block_forward(rows, segment, params):
    query_weight, key_weight, value_weight, output_weight, gate_weight, up_weight, down_weight, query_gain, key_gain, attn_gain, mlp_gain = params
    length = rows.shape[0]
    cosine, sine = rotary_tables(segment)
    query_raw = low_back(mult(rows, query_weight))
    key_raw = low_back(mult(rows, key_weight))
    value_raw = low_back(mult(rows, value_weight))
    queries = low(rotate(normalize(query_raw, query_gain).reshape(length, HEADS, HEAD), cosine, sine))
    keys = low(rotate(normalize(key_raw, key_gain).reshape(length, HEADS, HEAD), cosine, sine))
    values = low(value_raw).reshape(length, HEADS, HEAD)

    def one_head(inputs):
        return head_attention(inputs, segment)
    heads_out = lax.map(jax.checkpoint(one_head), (queries.transpose(1, 0, 2), keys.transpose(1, 0, 2), values.transpose(1, 0, 2)))
    attended = low(low_back(heads_out.transpose(1, 0, 2).reshape(length, D)))
    attn_raw = low_back(mult(attended, output_weight))
    mixed = rows + normalize(attn_raw, attn_gain)
    mixed_low = low(mixed)
    gate = low_back(mult(mixed_low, gate_weight))
    up_part = low_back(mult(mixed_low, up_weight))
    hidden = low(jax.nn.silu(gate) * up_part)
    mlp_raw = low_back(mult(hidden, down_weight))
    return mixed + normalize(mlp_raw, mlp_gain)

def reference(tokens, query_weight, key_weight, value_weight, output_weight, gate_weight, up_weight, down_weight, query_gain, key_gain, attn_gain, mlp_gain, seq_ids, out_grad):

    def layer(all_rows, *params):
        shaped = all_rows.reshape(BLOCKS, TOK_BLOCK, D)

        def block_step(rows, segment):
            return block_forward(rows, segment, params)
        checked = jax.checkpoint(block_step)

        def scan_step(running, inputs):
            return (running, checked(inputs[0], inputs[1]))
        _, outputs = lax.scan(scan_step, jnp.zeros((), jnp.float32), (shaped, seq_ids))
        return outputs.reshape(TOKENS, D)
    result, pullback = jax.vjp(layer, tokens.astype(jnp.float32), query_weight.astype(jnp.float32), key_weight.astype(jnp.float32), value_weight.astype(jnp.float32), output_weight.astype(jnp.float32), gate_weight.astype(jnp.float32), up_weight.astype(jnp.float32), down_weight.astype(jnp.float32), query_gain.astype(jnp.float32), key_gain.astype(jnp.float32), attn_gain.astype(jnp.float32), mlp_gain.astype(jnp.float32))
    grads = pullback(out_grad.astype(jnp.float32))
    return (result.astype(jnp.bfloat16), grads[0], grads[1], grads[2], grads[3], grads[4], grads[5], grads[6], grads[7], grads[8], grads[9], grads[10], grads[11])
```

```python
import math

import jax
import jax.numpy as jnp
import numpy as np
from jax import lax
from jax.sharding import PartitionSpec as P

D = 2048
HEAD = 128
MAX_LEN = 1024
SEGS = 4


EPS = 1e-06
THETA = 500000.0
NEGATIVE = -1e30


def token_positions(segment):
    length = segment.shape[0]
    labels = jnp.arange(SEGS, dtype=jnp.int32)
    member = (segment[:, None] == labels[None, :]).astype(jnp.int32)
    totals = jnp.sum(member, axis=0)
    starts = jnp.cumsum(totals) - totals
    opening = jnp.sum(member * starts[None, :], axis=1)
    return jnp.arange(length, dtype=jnp.int32) - opening


def rotary_tables(segment):
    place = token_positions(segment).astype(jnp.float32)
    halves = HEAD // 2
    inverse = jnp.exp(jnp.arange(halves, dtype=jnp.float32) * (-2.0 * math.log(THETA) / HEAD))
    angle = place[:, None] * inverse[None, :]
    return (jnp.cos(angle), jnp.sin(angle))


def rotate(values, cosine, sine):
    halves = values.shape[-1] // 2
    former = values[..., :halves]
    latter = values[..., halves:]
    cosine = cosine[:, None, :]
    sine = sine[:, None, :]
    return jnp.concatenate(
        [former * cosine - latter * sine, latter * cosine + former * sine], axis=-1
    )


def gather_features(values):
    return lax.all_gather(values, "gx", axis=1, tiled=True)


def row_totals(values):
    return lax.psum(values, "gx")


def reduce_features(partial_value):
    return lax.psum_scatter(
        partial_value.astype(jnp.bfloat16), "gx", scatter_dimension=1, tiled=True
    ).astype(jnp.float32)


def ring_order():
    count = lax.axis_size("gy")
    width = 2 if count < 16 else 4
    rows = count // width
    path = [(0, 0)]
    for row in range(rows):
        columns = range(1, width) if row % 2 == 0 else range(width - 1, 0, -1)
        path += [(row, column) for column in columns]
    path += [(row, 0) for row in range(rows - 1, 0, -1)]
    return [row * width + column for row, column in path]


def ring_hops():
    order = ring_order()
    count = len(order)
    ahead = [(order[i], order[(i + 1) % count]) for i in range(count)]
    back = [(order[(i + 1) % count], order[i]) for i in range(count)]
    return (ahead, back)


def ring_owner(offset):
    order = ring_order()
    count = len(order)
    place = np.zeros(count, np.int32)
    place[np.array(order)] = np.arange(count)
    own = jnp.asarray(place)[lax.axis_index("gy")]
    return jnp.asarray(np.array(order, np.int32))[(own + offset) % count]


def place_block(whole, block, owner, part, axis):
    shard = whole.shape[axis] // lax.axis_size("gy")
    half = block.shape[0]
    if axis == 0:
        return lax.dynamic_update_slice(whole, block, (owner * shard + part * half, 0))
    return lax.dynamic_update_slice(whole, block, (part * half, owner * shard))


def ring_gather(shard, axis):
    count = lax.axis_size("gy")
    ahead, back = ring_hops()
    half = shard.shape[0] // 2
    shape = list(shard.shape)
    shape[axis] *= count
    whole = jnp.zeros(shape, shard.dtype)
    first, second = shard[:half], shard[half:]
    own = ring_owner(0)
    whole = place_block(place_block(whole, first, own, 0, axis), second, own, 1, axis)
    for step in range(1, count):
        first = lax.ppermute(first, "gy", ahead)
        second = lax.ppermute(second, "gy", back)
        whole = place_block(whole, first, ring_owner(-step), 0, axis)
        whole = place_block(whole, second, ring_owner(step), 1, axis)
    return whole


def ring_scatter(product, axis):
    count = lax.axis_size("gy")
    ahead, back = ring_hops()
    shard = product.shape[axis] // count

    def part(owner, which):
        if axis == 0:
            return lax.dynamic_slice(
                product,
                (owner * shard + which * (shard // 2), 0),
                (shard // 2, product.shape[1]),
            )
        half = product.shape[0] // 2
        return lax.dynamic_slice(product, (which * half, owner * shard), (half, shard))

    first = part(ring_owner(-1), 0)
    second = part(ring_owner(1), 1)
    for step in range(1, count):
        first = lax.ppermute(first, "gy", ahead)
        second = lax.ppermute(second, "gy", back)
        first = first.astype(jnp.float32) + part(ring_owner(-1 - step), 0).astype(jnp.float32)
        second = second.astype(jnp.float32) + part(ring_owner(1 + step), 1).astype(jnp.float32)
        if step < count - 1:
            first = first.astype(jnp.bfloat16)
            second = second.astype(jnp.bfloat16)
    return jnp.concatenate([first, second], axis=0)


def project_in(full_rows, weight):
    return jnp.dot(full_rows, weight, preferred_element_type=jnp.float32)


def project_back(grads, weight):
    return reduce_features(
        lax.dot_general(
            grads, weight, (((1,), (1,)), ((), ())), preferred_element_type=jnp.float32
        )
    )


def project_out(values, weight):
    return reduce_features(jnp.dot(values, weight, preferred_element_type=jnp.float32))


def columns_back(full_grads, weight):
    return lax.dot_general(
        full_grads, weight, (((1,), (1,)), ((), ())), preferred_element_type=jnp.float32
    )


def grads_of_rows(full_rows, grads):
    product = lax.dot_general(
        full_rows, grads, (((0,), (0,)), ((), ())), preferred_element_type=jnp.float32
    )
    return ring_scatter(product.astype(jnp.bfloat16), 0)


def grads_of_columns(values, full_grads):
    product = lax.dot_general(
        values, full_grads, (((0,), (0,)), ((), ())), preferred_element_type=jnp.float32
    )
    return ring_scatter(product.astype(jnp.bfloat16), 1)


def norm_factor(raw):
    squares = row_totals(jnp.sum(raw * raw, axis=1, keepdims=True))
    return lax.rsqrt(squares / D + EPS)


def norm_back(upstream, raw, factor, gain):
    projected = row_totals(jnp.sum(gain * upstream * raw, axis=1, keepdims=True))
    raw_grad = factor * gain * upstream - raw * factor**3 * projected / D
    gain_part = jnp.sum(upstream * raw * factor, axis=0)
    return (raw_grad, gain_part)


def block_layout(length):
    row_block = min(512, length)
    key_span = min(length, MAX_LEN + row_block)
    return (row_block, key_span)


def block_scores(queries, keys, segment, block_index, row_block, key_span):
    length = queries.shape[0]
    start_row = block_index * row_block
    key_start = jnp.clip(start_row + row_block - key_span, 0, length - key_span)
    query_rows = lax.dynamic_slice_in_dim(queries, start_row, row_block)
    key_rows = lax.dynamic_slice_in_dim(keys, key_start, key_span)
    scores = jnp.einsum(
        "qhd,khd->hqk", query_rows, key_rows, preferred_element_type=jnp.float32
    ) * (1.0 / math.sqrt(HEAD))
    query_index = start_row + jnp.arange(row_block, dtype=jnp.int32)
    key_index = key_start + jnp.arange(key_span, dtype=jnp.int32)
    query_doc = lax.dynamic_slice_in_dim(segment, start_row, row_block)
    key_doc = lax.dynamic_slice_in_dim(segment, key_start, key_span)
    allowed = (query_doc[:, None] == key_doc[None, :]) & (
        key_index[None, :] <= query_index[:, None]
    )
    return (jnp.where(allowed[None], scores, NEGATIVE), start_row, key_start, query_rows, key_rows)


def attend(queries, keys, values, segment):
    length = queries.shape[0]
    row_block, key_span = block_layout(length)

    def forward_block(block_index):
        scores, start_row, key_start, query_rows, key_rows = block_scores(
            queries, keys, segment, block_index, row_block, key_span
        )
        value_rows = lax.dynamic_slice_in_dim(values, key_start, key_span)
        row_peak = jnp.max(scores, axis=-1, keepdims=True)
        raised = jnp.exp(scores - row_peak)
        row_total = jnp.sum(raised, axis=-1, keepdims=True)
        probability = (raised / row_total).astype(jnp.bfloat16)
        attn_rows = jnp.einsum(
            "hqk,khd->qhd", probability, value_rows, preferred_element_type=jnp.float32
        )
        return (attn_rows, (row_peak + jnp.log(row_total))[..., 0])

    attn_rows, log_total = lax.map(forward_block, jnp.arange(length // row_block, dtype=jnp.int32))
    return (attn_rows.reshape(queries.shape), log_total)


def attend_back(queries, keys, values, segment, log_total, upstream):
    length = queries.shape[0]
    row_block, key_span = block_layout(length)
    factor = 1.0 / math.sqrt(HEAD)

    def backward_block(accumulated, inputs):
        block_index, block_total = inputs
        key_grad, value_grad = accumulated
        scores, start_row, key_start, query_rows, key_rows = block_scores(
            queries, keys, segment, block_index, row_block, key_span
        )
        value_rows = lax.dynamic_slice_in_dim(values, key_start, key_span)
        upstream_rows = lax.dynamic_slice_in_dim(upstream, start_row, row_block)
        probability = jnp.exp(scores - block_total[..., None])
        prob_grad = jnp.einsum(
            "qhd,khd->hqk", upstream_rows, value_rows, preferred_element_type=jnp.float32
        )
        score_grad = (
            probability * (prob_grad - jnp.sum(probability * prob_grad, axis=-1, keepdims=True))
        ).astype(jnp.bfloat16)
        query_grad = (
            jnp.einsum("hqk,khd->qhd", score_grad, key_rows, preferred_element_type=jnp.float32)
            * factor
        )
        key_part = (
            jnp.einsum("hqk,qhd->khd", score_grad, query_rows, preferred_element_type=jnp.float32)
            * factor
        )
        value_part = jnp.einsum(
            "hqk,qhd->khd",
            probability.astype(jnp.bfloat16),
            upstream_rows,
            preferred_element_type=jnp.float32,
        )
        key_grad = lax.dynamic_update_slice_in_dim(
            key_grad,
            lax.dynamic_slice_in_dim(key_grad, key_start, key_span) + key_part,
            key_start,
            0,
        )
        value_grad = lax.dynamic_update_slice_in_dim(
            value_grad,
            lax.dynamic_slice_in_dim(value_grad, key_start, key_span) + value_part,
            key_start,
            0,
        )
        return ((key_grad, value_grad), query_grad)

    zero_start = jnp.zeros(queries.shape, jnp.float32)
    block_order = jnp.arange(length // row_block, dtype=jnp.int32)
    (key_grad, value_grad), query_grad = lax.scan(
        backward_block, (zero_start, zero_start), (block_order, log_total)
    )
    return (query_grad.reshape(queries.shape), key_grad, value_grad)


def shards(
    tokens,
    query_weight,
    key_weight,
    value_weight,
    output_weight,
    gate_weight,
    up_weight,
    down_weight,
    query_gain,
    key_gain,
    attn_gain,
    mlp_gain,
    seq_ids,
    out_grad,
):
    segment = seq_ids[0]
    cosine, sine = rotary_tables(segment)
    length = tokens.shape[0]
    local_width = tokens.shape[1]
    local_heads = local_width // HEAD
    head_shape = (length, local_heads, HEAD)
    inputs = gather_features(tokens)
    attn_stack = ring_gather(
        jnp.concatenate([query_weight, key_weight, value_weight], axis=1), 0
    )
    output_weight = ring_gather(output_weight, 1)
    projected = project_in(inputs, attn_stack)
    query_raw = projected[:, :local_width]
    key_raw = projected[:, local_width : 2 * local_width]
    value_raw = projected[:, 2 * local_width :]
    squares = row_totals(
        jnp.concatenate(
            [
                jnp.sum(query_raw * query_raw, axis=1, keepdims=True),
                jnp.sum(key_raw * key_raw, axis=1, keepdims=True),
            ],
            axis=1,
        )
    )
    query_factor = lax.rsqrt(squares[:, :1] / D + EPS)
    key_factor = lax.rsqrt(squares[:, 1:] / D + EPS)
    queries = rotate(
        (query_raw * query_factor * query_gain).reshape(head_shape), cosine, sine
    ).astype(jnp.bfloat16)
    keys_rot = rotate((key_raw * key_factor * key_gain).reshape(head_shape), cosine, sine).astype(
        jnp.bfloat16
    )
    values_low = value_raw.astype(jnp.bfloat16).reshape(head_shape)
    attended_raw, log_total = attend(queries, keys_rot, values_low, segment)
    attended = attended_raw.reshape(length, local_width).astype(jnp.bfloat16)
    attn_raw = project_out(attended, output_weight)
    attn_factor = norm_factor(attn_raw)
    mixed = tokens.astype(jnp.float32) + attn_raw * attn_factor * attn_gain
    mixed_low = mixed.astype(jnp.bfloat16)
    mlp_inputs = gather_features(mixed_low)
    mlp_stack = ring_gather(jnp.concatenate([gate_weight, up_weight], axis=1), 0)
    down_weight = ring_gather(down_weight, 1)
    gate_up = project_in(mlp_inputs, mlp_stack)
    hidden_width = gate_weight.shape[1]
    gate = gate_up[:, :hidden_width]
    up_part = gate_up[:, hidden_width:]
    sigmoid_gate = jax.nn.sigmoid(gate)
    hidden = (gate * sigmoid_gate * up_part).astype(jnp.bfloat16)
    mlp_raw = project_out(hidden, down_weight)
    mlp_factor = norm_factor(mlp_raw)
    result = (mixed + mlp_raw * mlp_factor * mlp_gain).astype(jnp.bfloat16)
    upstream = out_grad.astype(jnp.float32)
    mlp_grad, mlp_gain_part = norm_back(upstream, mlp_raw, mlp_factor, mlp_gain)
    mlp_full = gather_features(mlp_grad.astype(jnp.bfloat16))
    down_weight_grad = grads_of_columns(hidden, mlp_full)
    hidden_grad = columns_back(mlp_full, down_weight)
    gate_grad = (hidden_grad * up_part * sigmoid_gate * (1.0 + gate * (1.0 - sigmoid_gate))).astype(
        jnp.bfloat16
    )
    up_grad = (hidden_grad * gate * sigmoid_gate).astype(jnp.bfloat16)
    gate_up_grad = jnp.concatenate([gate_grad, up_grad], axis=1)
    mlp_weight_grads = grads_of_rows(mlp_inputs, gate_up_grad)
    gate_weight_grad = mlp_weight_grads[:, :hidden_width]
    up_weight_grad = mlp_weight_grads[:, hidden_width:]
    mixed_grad = upstream + project_back(gate_up_grad, mlp_stack)
    attn_grad, attn_gain_part = norm_back(mixed_grad, attn_raw, attn_factor, attn_gain)
    attn_full = gather_features(attn_grad.astype(jnp.bfloat16))
    output_weight_grad = grads_of_columns(attended, attn_full)
    attended_grad = columns_back(attn_full, output_weight).astype(jnp.bfloat16).reshape(head_shape)
    query_post, key_post, value_post = attend_back(
        queries, keys_rot, values_low, segment, log_total, attended_grad
    )
    query_normed_grad = rotate(query_post, cosine, -sine).reshape(length, local_width)
    key_normed_grad = rotate(key_post, cosine, -sine).reshape(length, local_width)
    projections = row_totals(
        jnp.concatenate(
            [
                jnp.sum(query_gain * query_normed_grad * query_raw, axis=1, keepdims=True),
                jnp.sum(key_gain * key_normed_grad * key_raw, axis=1, keepdims=True),
            ],
            axis=1,
        )
    )
    query_grad = (
        query_factor * query_gain * query_normed_grad
        - query_raw * query_factor**3 * projections[:, :1] / D
    ).astype(jnp.bfloat16)
    key_grad = (
        key_factor * key_gain * key_normed_grad - key_raw * key_factor**3 * projections[:, 1:] / D
    ).astype(jnp.bfloat16)
    value_grad = value_post.reshape(length, local_width).astype(jnp.bfloat16)
    query_gain_part = jnp.sum(query_normed_grad * query_raw * query_factor, axis=0)
    key_gain_part = jnp.sum(key_normed_grad * key_raw * key_factor, axis=0)
    projection_grad = jnp.concatenate([query_grad, key_grad, value_grad], axis=1)
    attn_weight_grads = grads_of_rows(inputs, projection_grad)
    query_weight_grad = attn_weight_grads[:, :local_width]
    key_weight_grad = attn_weight_grads[:, local_width : 2 * local_width]
    value_weight_grad = attn_weight_grads[:, 2 * local_width :]
    token_grad = mixed_grad + project_back(projection_grad, attn_stack)
    query_gain_grad, key_gain_grad, attn_gain_grad, mlp_gain_grad = lax.psum(
        (query_gain_part, key_gain_part, attn_gain_part, mlp_gain_part), "gy"
    )
    return (
        result,
        token_grad,
        query_weight_grad,
        key_weight_grad,
        value_weight_grad,
        output_weight_grad,
        gate_weight_grad,
        up_weight_grad,
        down_weight_grad,
        query_gain_grad,
        key_gain_grad,
        attn_gain_grad,
        mlp_gain_grad,
    )


def solution(mesh):
    return jax.shard_map(
        shards,
        mesh=mesh,
        in_specs=(
            P("gy", "gx"),
            P("gy", "gx"),
            P("gy", "gx"),
            P("gy", "gx"),
            P("gx", "gy"),
            P("gy", "gx"),
            P("gy", "gx"),
            P("gx", "gy"),
            P("gx"),
            P("gx"),
            P("gx"),
            P("gx"),
            P("gy", None),
            P("gy", "gx"),
        ),
        out_specs=(
            P("gy", "gx"),
            P("gy", "gx"),
            P("gy", "gx"),
            P("gy", "gx"),
            P("gy", "gx"),
            P("gx", "gy"),
            P("gy", "gx"),
            P("gy", "gx"),
            P("gx", "gy"),
            P("gx"),
            P("gx"),
            P("gx"),
            P("gx"),
        ),
        check_vma=False,
    )
```

```python
import math

import jax
import jax.numpy as jnp
from jax import lax
from jax.experimental import pallas as pl
from jax.experimental.pallas import tpu as pltpu
from jax.sharding import PartitionSpec as P

D = 2048
HEAD = 128
MAX_LEN = 1024
SEGS = 4


EPS = 1e-06
THETA = 500000.0
NEGATIVE = -1e30


MESH = pl.DeviceIdType.MESH
HBM = pl.BlockSpec(memory_space=pltpu.HBM)
VMEM = pl.BlockSpec(memory_space=pltpu.VMEM)
LOW = jnp.bfloat16
WIDE = jnp.float32
MIB = 1 << 20
LAG = 2
STATS = 128


def core_here():
    return lax.rem(lax.axis_index("gx"), 2)


def chip_here():
    return lax.div(lax.axis_index("gx"), 2)


def other_core():
    return lax.axis_index("gx") + 1 - 2 * core_here()


def peer_at(shift):
    return lax.rem(lax.axis_index("gx") + 2 * shift, lax.axis_size("gx"))


def ring_place():
    count = lax.axis_size("gy")
    index = lax.axis_index("gy")
    row, side = lax.div(index, 2), lax.rem(index, 2)
    return side * row + (1 - side) * (count - 1 - row)


def ring_device(place):
    count = lax.axis_size("gy")
    place = lax.rem(place + 2 * count, count)
    back = lax.div(place, count // 2)
    row = (1 - back) * place + back * (count - 1 - place)
    return 2 * row + 1 - back


def greet(gx, ring):
    barrier = pltpu.get_barrier_semaphore()
    partners = []
    if gx:
        partners.append({"gx": other_core()})
        partners += [{"gx": peer_at(k)} for k in range(1, lax.axis_size("gx") // 2)]
    if ring:
        place = ring_place()
        partners += [{"gy": ring_device(place + 1)}, {"gy": ring_device(place - 1)}]
    for partner in partners:
        pl.semaphore_signal(barrier, inc=1, device_id=partner, device_id_type=MESH)
    pl.semaphore_wait(barrier, len(partners))


def remote(source, target, send, recv, device):
    return pltpu.make_async_remote_copy(
        src_ref=source,
        dst_ref=target,
        send_sem=send,
        recv_sem=recv,
        device_id=device,
        device_id_type=MESH,
    )


def loop(count, body):
    def step(index, carry):
        body(index)
        return carry

    lax.fori_loop(0, count, step, 0)


def aligned(value, factor):
    return pl.multiple_of(value, factor)


class RingGather:
    def __init__(self, sources, slot, parts, send, recv, local):
        self.sources, self.slot, self.parts = sources, slot, parts
        self.send, self.recv, self.local = send, recv, local
        self.count = lax.axis_size("gy")

    @staticmethod
    def scratch(parts):
        count = lax.axis_size("gy")
        return [
            pltpu.SemaphoreType.DMA((count - 1, 2, parts)),
            pltpu.SemaphoreType.DMA((count - 1, 2, parts)),
            pltpu.SemaphoreType.DMA((2,)),
        ]

    def copy(self, way, step, part, behind):
        place = ring_place()
        sign = 1 - 2 * way
        spot = self.slot(way, ring_device(place - sign * (step + behind)), part)
        return remote(
            spot,
            spot,
            self.send.at[step, way, part],
            self.recv.at[step, way, part],
            {"gy": ring_device(place + sign)},
        )

    def begin(self):
        place = [
            pltpu.make_async_copy(
                self.sources[way], self.slot(way, lax.axis_index("gy"), None), self.local.at[way]
            )
            for way in range(2)
        ]
        for item in place:
            item.start()
        for item in place:
            item.wait()
        for part in range(self.parts):
            for way in range(2):
                self.copy(way, 0, part, 0).start()

    def forward(self, step):
        for part in range(self.parts):
            for way in range(2):
                self.copy(way, step - 1, part, 1).wait_recv()
                self.copy(way, step, part, 0).start()

    def end(self):
        for part in range(self.parts):
            for way in range(2):
                self.copy(way, self.count - 2, part, 1).wait_recv()

        def drain(step):
            for part in range(self.parts):
                for way in range(2):
                    self.copy(way, step, part, 0).wait_send()

        loop(self.count - 1, drain)


class RingScatter:
    def __init__(self, product, total, sums, land, send, recv, credit, slots, parts):
        self.product, self.total, self.sums, self.land = product, total, sums, land
        self.send, self.recv, self.credit = send, recv, credit
        self.slots, self.parts = slots, parts
        self.count = lax.axis_size("gy")
        self.rows = total.shape[1] // parts

    @staticmethod
    def scratch(rows, columns, slots, parts):
        count = lax.axis_size("gy")
        return [
            pltpu.VMEM((2, rows, columns), WIDE),
            pltpu.VMEM((2, rows, columns), LOW),
            pltpu.VMEM((slots, 2, rows, columns), LOW),
            pltpu.SemaphoreType.DMA((count - 1, 2, parts)),
            pltpu.SemaphoreType.DMA((count - 1, 2, parts)),
            pltpu.SemaphoreType.REGULAR((2, parts)),
        ]

    def copy(self, way, step, part):
        place = ring_place()
        rows = pl.ds(part * self.rows, self.rows)
        return remote(
            self.sums.at[way, rows],
            self.land.at[lax.rem(step, self.slots), way, rows],
            self.send.at[step, way, part],
            self.recv.at[step, way, part],
            {"gy": ring_device(place + 1 - 2 * way)},
        )

    def owner(self, way, step):
        sign = 1 - 2 * way
        return ring_device(ring_place() - sign * (1 + step))

    def step(self, step):
        last = self.count - 1
        for way in range(2):
            self.product(way, self.owner(way, step))
        for part in range(self.parts):
            for way in range(2):
                base = part * self.rows
                tile = min(self.rows, 32)

                @pl.when(step >= 1)
                def _():
                    self.copy(way, step - 1, part).wait_recv()
                    slot = lax.rem(step - 1, self.slots)

                    @pl.loop(0, self.rows // tile)
                    def _(index):
                        rows = pl.ds(aligned(base + index * tile, tile), tile)
                        self.total[way, rows] += self.land[slot, way, rows].astype(WIDE)

                    @pl.when(step - 1 + self.slots < last)
                    def _():
                        upstream = ring_device(ring_place() - (1 - 2 * way))
                        pl.semaphore_signal(
                            self.credit.at[way, part],
                            inc=1,
                            device_id={"gy": upstream},
                            device_id_type=MESH,
                        )

                @pl.when(step < last)
                def _():
                    @pl.when(step >= 1)
                    def _():
                        self.copy(way, step - 1, part).wait_send()

                    @pl.loop(0, self.rows // tile)
                    def _(index):
                        rows = pl.ds(aligned(base + index * tile, tile), tile)
                        self.sums[way, rows] = self.total[way, rows].astype(LOW)

                    @pl.when(step >= self.slots)
                    def _():
                        pl.semaphore_wait(self.credit.at[way, part], 1)

                    self.copy(way, step, part).start()

    def end(self):
        for part in range(self.parts):
            for way in range(2):
                self.copy(way, self.count - 2, part).wait_send()


class Reduce:
    def __init__(self, refs, core_land, cross_land, rows, width, scatter):
        (
            self.keep,
            self.core_send,
            self.core_stage,
            self.cross,
            self.cross_stage,
            self.raw,
            self.core_sems,
            self.cross_send_sems,
            self.cross_recv_sems,
            self.stage_sems,
        ) = refs
        self.core_land, self.cross_land = core_land, cross_land
        self.rows, self.width, self.scatter = rows, width, scatter
        self.chips = lax.axis_size("gx") // 2

    @staticmethod
    def scratch(rows, chunks, width, scatter):
        chips = lax.axis_size("gx") // 2
        half = chips * width
        part = width if scatter else half
        return [
            pltpu.VMEM((2, rows, half), LOW),
            pltpu.VMEM((2, rows, half), LOW),
            pltpu.VMEM((rows, half), LOW),
            pltpu.VMEM((LAG + 2, rows, half), LOW),
            pltpu.VMEM((chips - 1, rows, part), LOW),
            pltpu.VMEM((rows, part), WIDE),
            pltpu.SemaphoreType.DMA((2, chunks)),
            pltpu.SemaphoreType.DMA((chips - 1, chunks)),
            pltpu.SemaphoreType.DMA((chips - 1, chunks)),
            pltpu.SemaphoreType.DMA((chips,)),
        ]

    @staticmethod
    def landing(rows, chunks, width, scatter):
        chips = lax.axis_size("gx") // 2
        half = chips * width
        part = width if scatter else half
        return [
            jax.ShapeDtypeStruct((chunks, rows, half), LOW),
            jax.ShapeDtypeStruct((chips - 1, chunks, rows, part), LOW),
        ]

    def core_copy(self, chunk):
        return remote(
            self.core_send.at[lax.rem(chunk, 2)],
            self.core_land.at[chunk],
            self.core_sems.at[0, chunk],
            self.core_sems.at[1, chunk],
            {"gx": other_core()},
        )

    def cross_copy(self, shift, chunk):
        source = self.cross.at[lax.rem(chunk, LAG + 2)]
        if self.scatter:
            block = lax.rem(chip_here() + shift, self.chips)
            source = source.at[:, pl.ds(aligned(block * self.width, self.width), self.width)]
        return remote(
            source,
            self.cross_land.at[shift - 1, chunk],
            self.cross_send_sems.at[shift - 1, chunk],
            self.cross_recv_sems.at[shift - 1, chunk],
            {"gx": peer_at(shift)},
        )

    def produce(self, chunk, dot):
        @pl.when(chunk >= 2)
        def _():
            self.core_copy(chunk - 2).wait_send()

        slot = lax.rem(chunk, 2)
        core = core_here()
        for chip in range(self.chips):
            place = aligned((2 * chip + 1 - core) * self.width, self.width)
            self.core_send[slot, :, chip * self.width : (chip + 1) * self.width] = dot(
                place
            ).astype(LOW)
        self.core_copy(chunk).start()
        for chip in range(self.chips):
            place = aligned((2 * chip + core) * self.width, self.width)
            self.keep[slot, :, chip * self.width : (chip + 1) * self.width] = dot(
                place
            ).astype(LOW)

    def core_stage_copy(self, chunk):
        return pltpu.make_async_copy(
            self.core_land.at[chunk], self.core_stage, self.stage_sems.at[0]
        )

    def core_fetch(self, chunk):
        self.core_copy(chunk).wait_recv()
        self.core_stage_copy(chunk).start()

    def core_sum(self, chunk):
        slot, place = lax.rem(chunk, 2), lax.rem(chunk, LAG + 2)
        self.core_stage_copy(chunk).wait()

        @pl.when(chunk >= LAG + 2)
        def _():
            for shift in range(1, self.chips):
                self.cross_copy(shift, chunk - LAG - 2).wait_send()

        @pl.loop(0, self.rows // 32)
        def _(index):
            rows = pl.ds(aligned(index * 32, 32), 32)
            self.cross[place, rows] = (
                self.keep[slot, rows].astype(WIDE) + self.core_stage[rows].astype(WIDE)
            ).astype(LOW)

        for shift in range(1, self.chips):
            self.cross_copy(shift, chunk).start()

    def cross_stage_copy(self, shift, chunk):
        return pltpu.make_async_copy(
            self.cross_land.at[shift - 1, chunk],
            self.cross_stage.at[shift - 1],
            self.stage_sems.at[shift],
        )

    def cross_fetch(self, chunk):
        for shift in range(1, self.chips):
            self.cross_copy(shift, chunk).wait_recv()
            self.cross_stage_copy(shift, chunk).start()

    def cross_sum(self, chunk):
        place = lax.rem(chunk, LAG + 2)
        for shift in range(1, self.chips):
            self.cross_stage_copy(shift, chunk).wait()

        @pl.loop(0, self.rows // 32)
        def _(index):
            rows = pl.ds(aligned(index * 32, 32), 32)
            if self.scatter:
                block = pl.ds(aligned(chip_here() * self.width, self.width), self.width)
                total = self.cross[place, rows, block].astype(WIDE)
            else:
                total = self.cross[place, rows].astype(WIDE)
            for shift in range(1, self.chips):
                total = total + self.cross_stage[shift - 1, rows].astype(WIDE)
            self.raw[rows] = total

    def end(self, chunks):
        for chunk in (chunks - 2, chunks - 1):
            self.core_copy(chunk).wait_send()
        for chunk in range(chunks - LAG - 2, chunks):
            for shift in range(1, self.chips):
                self.cross_copy(shift, chunk).wait_send()


class Stats:
    def __init__(self, mine, land, sems):
        self.mine, self.land, self.sems = mine, land, sems

    @staticmethod
    def scratch(rows, chunks):
        return [
            pltpu.VMEM((2, rows, STATS), WIDE),
            pltpu.VMEM((chunks, rows, STATS), WIDE),
            pltpu.SemaphoreType.DMA((2, chunks)),
        ]

    def copy(self, chunk):
        return remote(
            self.mine.at[lax.rem(chunk, 2)],
            self.land.at[chunk],
            self.sems.at[0, chunk],
            self.sems.at[1, chunk],
            {"gx": other_core()},
        )

    def clear(self, chunk):
        @pl.when(chunk >= 2)
        def _():
            self.copy(chunk - 2).wait_send()

    def put(self, chunk, rows, first, second):
        lane = lax.broadcasted_iota(jnp.int32, (first.shape[0], STATS), 1)
        self.mine[lax.rem(chunk, 2), rows] = jnp.where(lane < STATS // 2, first, second)

    def get(self, chunk, rows):
        total = self.mine[lax.rem(chunk, 2), rows] + self.land[chunk, rows]
        return (total[:, :1], total[:, STATS // 2 : STATS // 2 + 1])

    def end(self, chunks):
        for chunk in (chunks - 2, chunks - 1):
            self.copy(chunk).wait_send()


class Spread:
    def __init__(self, buffer, whole, local, send, recv, rows, width):
        self.buffer, self.whole = buffer, whole
        self.local, self.send, self.recv = local, send, recv
        self.rows, self.width = rows, width
        self.chips = lax.axis_size("gx") // 2

    @staticmethod
    def scratch(rows, chunks, width):
        chips = lax.axis_size("gx") // 2
        return [
            pltpu.VMEM((2, rows, chips * width), LOW),
            pltpu.SemaphoreType.DMA((2, chips)),
            pltpu.SemaphoreType.DMA((chunks, chips)),
            pltpu.SemaphoreType.DMA((chunks, chips)),
        ]

    def pair(self, chunk, chip, core):
        slot = lax.rem(chunk, 2)
        source = self.buffer.at[slot, :, chip * self.width : (chip + 1) * self.width]
        rows = pl.ds(aligned(chunk * self.rows, self.rows), self.rows)
        columns = pl.ds(aligned((2 * chip + core) * self.width, self.width), self.width)
        target = self.whole.at[rows, columns]
        here = pltpu.make_async_copy(source, target, self.local.at[slot, chip])
        away = remote(
            source,
            target,
            self.send.at[chunk, chip],
            self.recv.at[chunk, chip],
            {"gx": other_core()},
        )
        return (here, away)

    def clear(self, chunk):
        @pl.when(chunk >= 2)
        def _():
            self.settle(chunk - 2)

    def settle(self, chunk):
        for chip in range(self.chips):
            here, away = self.pair(chunk, chip, core_here())
            here.wait()
            away.wait_send()

    def go(self, chunk):
        for chip in range(self.chips):
            here, away = self.pair(chunk, chip, core_here())
            here.start()
            away.start()

    def end(self, chunks):
        for chunk in (chunks - 2, chunks - 1):
            self.settle(chunk)

        def arrive(chunk):
            for chip in range(self.chips):
                self.pair(chunk, chip, 1 - core_here())[1].wait_recv()

        loop(chunks, arrive)


def row_slice(chunk, rows):
    return pl.ds(aligned(chunk * rows, rows), rows)


def core_columns(source, chunk, rows, width, buffer, sems, first):
    return [
        pltpu.make_async_copy(
            source.at[
                row_slice(chunk, rows),
                pl.ds(aligned((2 * chip + core_here()) * width, width), width),
            ],
            buffer.at[:, chip * width : (chip + 1) * width],
            sems.at[first + chip],
        )
        for chip in range(lax.axis_size("gx") // 2)
    ]


def tiles(rows, body):
    @pl.loop(0, rows // 32)
    def _(index):
        body(pl.ds(aligned(index * 32, 32), 32))


def schedule(chunks, reduce, multiply, fetch, sums, finish, before=None, ring_steps=0):
    def iteration(step):
        if before is not None:

            @pl.when(step < ring_steps)
            def _():
                before(step)

        @pl.when((step >= 1) & (step <= chunks))
        def _():
            reduce.core_fetch(step - 1)

        @pl.when((step >= 1 + LAG) & (step < chunks + 1 + LAG))
        def _():
            reduce.cross_fetch(step - 1 - LAG)

        @pl.when((step >= 1 + LAG) & (step < chunks + 2 + LAG))
        def _():
            fetch(step - 1 - LAG)

        @pl.when(step < chunks)
        def _():
            reduce.produce(step, lambda place: multiply(step, place))

        @pl.when((step >= 1) & (step <= chunks))
        def _():
            reduce.core_sum(step - 1)

        @pl.when((step >= 2 + LAG) & (step < chunks + 2 + LAG))
        def _():
            finish(step - 2 - LAG)

        @pl.when((step >= 1 + LAG) & (step < chunks + 1 + LAG))
        def _():
            reduce.cross_sum(step - 1 - LAG)
            sums(step - 1 - LAG)

    loop(chunks + 2 + LAG, iteration)


def take(refs, counts):
    groups, start = [], 0
    for count in counts:
        groups.append(refs[start : start + count])
        start += count
    return groups


def attn_out(attended, weight, gain, tokens, out_grad, gate_shard, up_shard, collective):
    length, width = attended.shape
    chips = lax.axis_size("gx") // 2
    half = chips * width
    count = lax.axis_size("gy")
    chunks = count
    rows = length // chunks
    hidden = gate_shard.shape[1]
    shard = gate_shard.shape[0]
    ring_parts = 2
    part_rows = shard // ring_parts

    groups = [
        Reduce.scratch(rows, chunks, width, False),
        Stats.scratch(rows, chunks),
        Spread.scratch(rows, chunks, width),
        RingGather.scratch(ring_parts),
        [
            pltpu.VMEM((rows, half), LOW),
            pltpu.VMEM((2, rows, half), WIDE),
            pltpu.VMEM((2, rows, half), LOW),
            pltpu.SemaphoreType.DMA((chips,)),
            pltpu.SemaphoreType.DMA((2,)),
            pltpu.SemaphoreType.DMA((2,)),
            pltpu.SemaphoreType.DMA((chips,)),
            pltpu.SemaphoreType.DMA((chips, 2)),
        ],
    ]

    def kernel(*refs):
        ins, outs, *scratch = take(refs, [7, 8] + [len(g) for g in groups])
        attended, weight, gain, tokens, out_grad, gate_shard, up_shard = ins
        raw_out, mixed_out, low_out, gate_full, up_full, upstream, core_land, cross_land = outs
        reduce = Reduce(scratch[0], core_land, cross_land, rows, width, False)
        stats = Stats(*scratch[1])
        buffer, local, send, recv = scratch[2]
        spread = Spread(buffer, low_out, local, send, recv, rows, width)
        token_buf, mixed_buf, raw_buf, token_sems, mixed_sems, raw_sems, own_sem, up_sems = scratch[4]
        full = (gate_full, up_full)

        def slot(way, owner, part):
            base = owner * shard
            if part is None:
                return full[way].at[pl.ds(aligned(base, shard), shard)]
            return full[way].at[pl.ds(aligned(base + part * part_rows, part_rows), part_rows)]

        ring = RingGather((gate_shard, up_shard), slot, ring_parts, *scratch[3])
        greet(True, True)
        ring.begin()

        def up_block(chip):
            return upstream.at[:, pl.ds(aligned(chip * width, width), width)]

        own = pltpu.make_async_copy(out_grad, up_block(chip_here()), own_sem.at[0])
        own.start()
        crossings = [
            remote(
                out_grad,
                up_block(chip_here()),
                up_sems.at[shift, 0],
                up_sems.at[shift, 1],
                {"gx": peer_at(shift)},
            )
            for shift in range(1, chips)
        ]

        def before(step):
            @pl.when((step >= 1) & (step < count - 1))
            def _():
                ring.forward(step)

            @pl.when(step == 4)
            def _():
                for item in crossings:
                    item.start()

        def multiply(chunk, place):
            return jnp.dot(
                attended[row_slice(chunk, rows)],
                weight[:, pl.ds(place, width)],
                preferred_element_type=WIDE,
            )

        def token_copies(chunk):
            return core_columns(tokens, chunk, rows, width, token_buf, token_sems, 0)

        def fetch(chunk):
            @pl.when(chunk >= 1)
            def _():
                for item in token_copies(chunk - 1):
                    item.start()

        def mixed_copy(chunk):
            slot = lax.rem(chunk, 2)
            return pltpu.make_async_copy(
                mixed_buf.at[slot, :, pl.ds(aligned(chip_here() * width, width), width)],
                mixed_out.at[row_slice(chunk, rows)],
                mixed_sems.at[slot],
            )

        def raw_copy(chunk):
            slot = lax.rem(chunk, 2)
            return pltpu.make_async_copy(
                raw_buf.at[slot], raw_out.at[row_slice(chunk, rows)], raw_sems.at[slot]
            )

        def sums(chunk):
            stats.clear(chunk)

            @pl.when(chunk >= 2)
            def _():
                raw_copy(chunk - 2).wait()

            def tile(at):
                raw = reduce.raw[at]
                raw_buf[lax.rem(chunk, 2), at] = raw.astype(LOW)
                squares = jnp.sum(raw * raw, axis=1, keepdims=True)
                stats.put(chunk, at, squares, squares)

            tiles(rows, tile)
            stats.copy(chunk).start()
            raw_copy(chunk).start()

        def finish(chunk):
            slot = lax.rem(chunk, 2)
            for item in token_copies(chunk):
                item.wait()
            stats.copy(chunk).wait_recv()
            spread.clear(chunk)

            @pl.when(chunk >= 2)
            def _():
                mixed_copy(chunk - 2).wait()

            def tile(at):
                squares, _ = stats.get(chunk, at)
                factor = lax.rsqrt(squares / D + EPS)
                mixed = token_buf[at].astype(WIDE) + reduce.raw[at] * factor * gain[...]
                mixed_buf[slot, at] = mixed
                spread.buffer[slot, at] = mixed.astype(LOW)

            tiles(rows, tile)
            spread.go(chunk)
            mixed_copy(chunk).start()

        schedule(chunks, reduce, multiply, fetch, sums, finish, before, count)
        ring.end()
        own.wait()
        for item in crossings:
            item.wait()
        reduce.end(chunks)
        stats.end(chunks)
        spread.end(chunks)
        for chunk in (chunks - 2, chunks - 1):
            mixed_copy(chunk).wait()
            raw_copy(chunk).wait()

    shape = jax.ShapeDtypeStruct
    out = pl.pallas_call(
        kernel,
        out_shape=[
            shape((length, half), LOW),
            shape((length, width), WIDE),
            shape((length, D), LOW),
            shape((shard * count, hidden), LOW),
            shape((shard * count, hidden), LOW),
            shape((length, half), LOW),
        ]
        + Reduce.landing(rows, chunks, width, False),
        in_specs=[VMEM, VMEM, VMEM, HBM, HBM, HBM, HBM],
        out_specs=[HBM] * 8,
        scratch_shapes=[item for group in groups for item in group],
        compiler_params=pltpu.CompilerParams(
            collective_id=collective, has_side_effects=True, vmem_limit_bytes=60 * MIB
        ),
        cost_estimate=pl.CostEstimate(
            flops=2 * length * width * D, bytes_accessed=8 * length * D, transcendentals=0
        ),
    )(attended, weight, gain, tokens, out_grad, gate_shard, up_shard)
    return out[:6]


def mlp_out(hidden, weight, gain, mixed, upstream, collective):
    length, inner = hidden.shape
    width = mixed.shape[1]
    chips = lax.axis_size("gx") // 2
    half = chips * width
    chunks = lax.axis_size("gy")
    rows = length // chunks

    groups = [
        Reduce.scratch(rows, chunks, width, False),
        Stats.scratch(rows, chunks),
        Spread.scratch(rows, chunks, width),
        [
            pltpu.VMEM((2, rows, half), LOW),
            pltpu.VMEM((rows, width), WIDE),
            pltpu.VMEM((2, rows, width), LOW),
            pltpu.SemaphoreType.DMA((2,)),
            pltpu.SemaphoreType.DMA((1,)),
            pltpu.SemaphoreType.DMA((2,)),
        ],
    ]

    def kernel(*refs):
        ins, outs, *scratch = take(refs, [5, 5] + [len(g) for g in groups])
        hidden, weight, gain, mixed, upstream = ins
        result, grad_out, gain_grad, core_land, cross_land = outs
        reduce = Reduce(scratch[0], core_land, cross_land, rows, width, False)
        stats = Stats(*scratch[1])
        buffer, local, send, recv = scratch[2]
        spread = Spread(buffer, grad_out, local, send, recv, rows, width)
        up_buf, mixed_buf, result_buf, up_sems, mixed_sems, result_sems = scratch[3]
        greet(True, False)
        gain_grad[...] = jnp.zeros_like(gain_grad)

        def multiply(chunk, place):
            return jnp.dot(
                hidden[row_slice(chunk, rows)],
                weight[:, pl.ds(place, width)],
                preferred_element_type=WIDE,
            )

        def up_copy(chunk):
            slot = lax.rem(chunk, 2)
            return pltpu.make_async_copy(
                upstream.at[row_slice(chunk, rows)], up_buf.at[slot], up_sems.at[slot]
            )

        def mixed_copy(chunk):
            return pltpu.make_async_copy(
                mixed.at[row_slice(chunk, rows)], mixed_buf, mixed_sems.at[0]
            )

        def result_copy(chunk):
            slot = lax.rem(chunk, 2)
            return pltpu.make_async_copy(
                result_buf.at[slot], result.at[row_slice(chunk, rows)], result_sems.at[slot]
            )

        def fetch(chunk):
            @pl.when(chunk < chunks)
            def _():
                up_copy(chunk).start()

            @pl.when(chunk >= 1)
            def _():
                mixed_copy(chunk - 1).start()

        def sums(chunk):
            slot = lax.rem(chunk, 2)
            stats.clear(chunk)
            up_copy(chunk).wait()

            def tile(at):
                raw = reduce.raw[at]
                up = up_buf[slot, at].astype(WIDE)
                squares = jnp.sum(raw * raw, axis=1, keepdims=True)
                projected = jnp.sum(gain[...] * up * raw, axis=1, keepdims=True)
                stats.put(chunk, at, squares, projected)

            tiles(rows, tile)
            stats.copy(chunk).start()

        def finish(chunk):
            slot = lax.rem(chunk, 2)
            mixed_copy(chunk).wait()
            stats.copy(chunk).wait_recv()
            spread.clear(chunk)

            @pl.when(chunk >= 2)
            def _():
                result_copy(chunk - 2).wait()

            block = pl.ds(aligned(chip_here() * width, width), width)

            def tile(at):
                squares, projected = stats.get(chunk, at)
                factor = lax.rsqrt(squares / D + EPS)
                raw = reduce.raw[at]
                up = up_buf[slot, at].astype(WIDE)
                spread.buffer[slot, at] = (
                    factor * gain[...] * up - raw * (factor * factor * factor * projected / D)
                ).astype(LOW)
                gain_grad[...] += jnp.sum(up * raw * factor, axis=0, keepdims=True)
                result_buf[slot, at] = (
                    mixed_buf[at] + reduce.raw[at, block] * factor * gain[:, block]
                ).astype(LOW)

            tiles(rows, tile)
            spread.go(chunk)
            result_copy(chunk).start()

        schedule(chunks, reduce, multiply, fetch, sums, finish)
        reduce.end(chunks)
        stats.end(chunks)
        spread.end(chunks)
        for chunk in (chunks - 2, chunks - 1):
            result_copy(chunk).wait()

    shape = jax.ShapeDtypeStruct
    out = pl.pallas_call(
        kernel,
        out_shape=[
            shape((length, width), LOW),
            shape((length, D), LOW),
            shape((1, half), WIDE),
        ]
        + Reduce.landing(rows, chunks, width, False),
        in_specs=[VMEM, VMEM, VMEM, HBM, HBM],
        out_specs=[HBM, HBM, VMEM, HBM, HBM],
        scratch_shapes=[item for group in groups for item in group],
        compiler_params=pltpu.CompilerParams(
            collective_id=collective, has_side_effects=True, vmem_limit_bytes=60 * MIB
        ),
        cost_estimate=pl.CostEstimate(
            flops=2 * length * inner * D, bytes_accessed=8 * length * D, transcendentals=0
        ),
    )(hidden, weight, gain, mixed, upstream)
    return out[:3]


def mlp_back(gate_grad, up_grad, gate_full, up_full, inputs, gain, upstream, attn_raw, collective):
    length, inner = gate_grad.shape
    half = attn_raw.shape[1]
    chips = lax.axis_size("gx") // 2
    width = half // chips
    count = lax.axis_size("gy")
    chunks = count
    rows = length // chunks
    shard = D // count
    slots, parts = 2, 2

    groups = [
        Reduce.scratch(rows, chunks, width, False),
        Stats.scratch(rows, chunks),
        Spread.scratch(rows, chunks, width),
        RingScatter.scratch(shard, inner, slots, parts),
        [
            pltpu.VMEM((2, length, shard), LOW),
            pltpu.VMEM((rows, half), LOW),
            pltpu.VMEM((2, rows, half), LOW),
            pltpu.SemaphoreType.DMA((2,)),
            pltpu.SemaphoreType.DMA((1,)),
            pltpu.SemaphoreType.DMA((2,)),
            pltpu.SemaphoreType.DMA((1,)),
            pltpu.SemaphoreType.DMA((2,)),
        ],
    ]

    def kernel(*refs):
        ins, outs, *scratch = take(refs, [8, 7] + [len(g) for g in groups])
        gate_grad, up_grad, gate_full, up_full, inputs, gain, upstream, attn_raw = ins
        mixed_out, grad_out, gain_grad, gate_out, up_out, core_land, cross_land = outs
        reduce = Reduce(scratch[0], core_land, cross_land, rows, width, False)
        stats = Stats(*scratch[1])
        buffer, local, send, recv = scratch[2]
        spread = Spread(buffer, grad_out, local, send, recv, rows, width)
        total, summed, land, ring_send, ring_recv, credit = scratch[3]
        left, up_buf, raw_buf, left_sems, up_sems, raw_sems, mixed_sems, out_sems = scratch[4]
        grads = (gate_grad, up_grad)

        def left_copy(way, owner):
            return pltpu.make_async_copy(
                inputs.at[:, pl.ds(aligned(owner * shard, shard), shard)],
                left.at[way],
                left_sems.at[way],
            )

        def product(way, owner):
            left_copy(way, owner).wait()
            tile = 512

            @pl.loop(0, inner // tile)
            def _(index):
                columns = pl.ds(aligned(index * tile, tile), tile)
                total[way, :, columns] = lax.dot_general(
                    left[way],
                    grads[way][:, columns],
                    (((0,), (0,)), ((), ())),
                    preferred_element_type=WIDE,
                )

        ring = RingScatter(
            product, total, summed, land, ring_send, ring_recv, credit, slots, parts
        )
        for way in range(2):
            left_copy(way, ring.owner(way, 0)).start()
        greet(True, True)
        gain_grad[...] = jnp.zeros_like(gain_grad)

        def before(step):
            ring.step(step)

            @pl.when(step + 1 < count)
            def _():
                for way in range(2):
                    left_copy(way, ring.owner(way, step + 1)).start()

        def multiply(chunk, place):
            at = row_slice(chunk, rows)
            return lax.dot_general(
                gate_grad[at],
                gate_full[pl.ds(place, width)],
                (((1,), (1,)), ((), ())),
                preferred_element_type=WIDE,
            ) + lax.dot_general(
                up_grad[at],
                up_full[pl.ds(place, width)],
                (((1,), (1,)), ((), ())),
                preferred_element_type=WIDE,
            )

        def up_copy(chunk):
            return pltpu.make_async_copy(
                upstream.at[row_slice(chunk, rows)], up_buf, up_sems.at[0]
            )

        def raw_copy(chunk):
            slot = lax.rem(chunk, 2)
            return pltpu.make_async_copy(
                attn_raw.at[row_slice(chunk, rows)], raw_buf.at[slot], raw_sems.at[slot]
            )

        def mixed_copy(chunk):
            return pltpu.make_async_copy(
                reduce.raw.at[:, pl.ds(aligned(chip_here() * width, width), width)],
                mixed_out.at[row_slice(chunk, rows)],
                mixed_sems.at[0],
            )

        def fetch(chunk):
            @pl.when(chunk < chunks)
            def _():
                up_copy(chunk).start()
                raw_copy(chunk).start()

        def sums(chunk):
            slot = lax.rem(chunk, 2)
            stats.clear(chunk)
            up_copy(chunk).wait()
            raw_copy(chunk).wait()

            def tile(at):
                upward = reduce.raw[at] + up_buf[at].astype(WIDE)
                reduce.raw[at] = upward
                raw = raw_buf[slot, at].astype(WIDE)
                squares = jnp.sum(raw * raw, axis=1, keepdims=True)
                projected = jnp.sum(gain[...] * upward * raw, axis=1, keepdims=True)
                stats.put(chunk, at, squares, projected)

            tiles(rows, tile)
            stats.copy(chunk).start()
            mixed_copy(chunk).start()

        def finish(chunk):
            slot = lax.rem(chunk, 2)
            stats.copy(chunk).wait_recv()
            spread.clear(chunk)

            def tile(at):
                squares, projected = stats.get(chunk, at)
                factor = lax.rsqrt(squares / D + EPS)
                upward = reduce.raw[at]
                raw = raw_buf[slot, at].astype(WIDE)
                spread.buffer[slot, at] = (
                    factor * gain[...] * upward
                    - raw * (factor * factor * factor * projected / D)
                ).astype(LOW)
                gain_grad[...] += jnp.sum(upward * raw * factor, axis=0, keepdims=True)

            tiles(rows, tile)
            spread.go(chunk)
            mixed_copy(chunk).wait()

        schedule(chunks, reduce, multiply, fetch, sums, finish, before, count)
        writes = [
            pltpu.make_async_copy(total.at[way], (gate_out, up_out)[way], out_sems.at[way])
            for way in range(2)
        ]
        for item in writes:
            item.start()
        ring.end()
        reduce.end(chunks)
        stats.end(chunks)
        spread.end(chunks)
        for item in writes:
            item.wait()

    shape = jax.ShapeDtypeStruct
    out = pl.pallas_call(
        kernel,
        out_shape=[
            shape((length, width), WIDE),
            shape((length, D), LOW),
            shape((1, half), WIDE),
            shape((shard, inner), WIDE),
            shape((shard, inner), WIDE),
        ]
        + Reduce.landing(rows, chunks, width, False),
        in_specs=[VMEM, VMEM, VMEM, VMEM, HBM, VMEM, HBM, HBM],
        out_specs=[HBM, HBM, VMEM, HBM, HBM, HBM, HBM],
        scratch_shapes=[item for group in groups for item in group],
        compiler_params=pltpu.CompilerParams(
            collective_id=collective, has_side_effects=True, vmem_limit_bytes=60 * MIB
        ),
        cost_estimate=pl.CostEstimate(
            flops=8 * length * inner * D, bytes_accessed=16 * length * D, transcendentals=0
        ),
    )(gate_grad, up_grad, gate_full, up_full, inputs, gain, upstream, attn_raw)
    return out[:5]


def gather_in(tokens, stack, collective):
    length, width = tokens.shape
    shard, columns = stack.shape
    count = lax.axis_size("gy")
    chunks = count
    rows = length // chunks
    chips = lax.axis_size("gx") // 2
    side = columns // 2
    parts = 1

    groups = [
        RingGather.scratch(parts),
        [
            pltpu.SemaphoreType.DMA((1,)),
            pltpu.SemaphoreType.DMA((2,)),
            pltpu.SemaphoreType.DMA((chips - 1, chunks, 2)),
            pltpu.SemaphoreType.DMA((chips - 1, chunks, 2)),
        ],
    ]

    def kernel(*refs):
        ins, outs, *scratch = take(refs, [2, 2] + [len(g) for g in groups])
        tokens, stack = ins
        whole, full = outs
        own_sem, core_sems, cross_sems, pass_sems = scratch[1]

        def slot(way, owner, part):
            return full.at[
                pl.ds(aligned(owner * shard, shard), shard), way * side : (way + 1) * side
            ]

        sources = [stack.at[:, way * side : (way + 1) * side] for way in range(2)]
        ring = RingGather(sources, slot, parts, *scratch[0])

        def block(rank, chunk):
            at = pl.ds(aligned(rank * width, width), width)
            if chunk is None:
                return whole.at[:, at]
            return whole.at[row_slice(chunk, rows), at]

        here = lax.axis_index("gx")
        own = pltpu.make_async_copy(tokens, block(here, None), own_sem.at[0])
        core = remote(
            tokens, block(here, None), core_sems.at[0], core_sems.at[1], {"gx": other_core()}
        )

        def cross(shift, chunk):
            return remote(
                tokens.at[row_slice(chunk, rows)],
                block(here, chunk),
                cross_sems.at[shift - 1, chunk, 0],
                cross_sems.at[shift - 1, chunk, 1],
                {"gx": peer_at(shift)},
            )

        def onward(shift, chunk):
            spot = block(peer_at(chips - shift), chunk)
            return remote(
                spot,
                spot,
                pass_sems.at[shift - 1, chunk, 0],
                pass_sems.at[shift - 1, chunk, 1],
                {"gx": other_core()},
            )

        own.start()
        greet(True, True)

        def send(chunk):
            for shift in range(1, chips):
                cross(shift, chunk).start()

        loop(chunks, send)
        core.start()
        ring.begin()

        def step(chunk):
            @pl.when((chunk >= 1) & (chunk < count - 1))
            def _():
                ring.forward(chunk)

            for shift in range(1, chips):
                cross(shift, chunk).wait_recv()
                onward(shift, chunk).start()

        loop(chunks, step)
        ring.end()

        def drain(chunk):
            for shift in range(1, chips):
                cross(shift, chunk).wait_send()
                onward(shift, chunk).wait()

        loop(chunks, drain)
        own.wait()
        core.wait()

    shape = jax.ShapeDtypeStruct
    return pl.pallas_call(
        kernel,
        out_shape=[shape((length, D), LOW), shape((shard * count, columns), LOW)],
        in_specs=[HBM, HBM],
        out_specs=[HBM, HBM],
        scratch_shapes=[item for group in groups for item in group],
        compiler_params=pltpu.CompilerParams(
            collective_id=collective, has_side_effects=True, vmem_limit_bytes=16 * MIB
        ),
    )(tokens, stack)


def mlp_in(inputs, gate_full, up_full):
    length = inputs.shape[0]
    inner = gate_full.shape[1]
    rows = 256
    tile = 512

    def kernel(inputs, gate_weight, up_weight, hidden, gate_out, up_out):
        @pl.loop(0, inner // tile)
        def _(index):
            at = pl.ds(aligned(index * tile, tile), tile)
            gate = jnp.dot(inputs[...], gate_weight[:, at], preferred_element_type=WIDE)
            up = jnp.dot(inputs[...], up_weight[:, at], preferred_element_type=WIDE)
            hidden[:, at] = (gate * jax.nn.sigmoid(gate) * up).astype(LOW)
            gate_out[:, at] = gate.astype(LOW)
            up_out[:, at] = up.astype(LOW)

    block = pl.BlockSpec((rows, inner), lambda i: (i, 0))
    shape = jax.ShapeDtypeStruct((length, inner), LOW)
    return pl.pallas_call(
        kernel,
        grid=(length // rows,),
        out_shape=[shape] * 3,
        in_specs=[pl.BlockSpec((rows, D), lambda i: (i, 0)), VMEM, VMEM],
        out_specs=[block] * 3,
        compiler_params=pltpu.CompilerParams(vmem_limit_bytes=56 * MIB),
        cost_estimate=pl.CostEstimate(
            flops=4 * length * inner * D,
            bytes_accessed=2 * length * (D + 3 * inner) + 4 * D * inner,
            transcendentals=length * inner,
        ),
    )(inputs, gate_full, up_full)


def hidden_back(grad, weight, hidden, gate, up, collective):
    length, inner = hidden.shape
    count = lax.axis_size("gy")
    chunks = count
    rows = length // chunks
    shard = D // count
    side = inner // 2
    slots, parts = count - 1, 2
    tile = min(512, inner)

    groups = [
        RingScatter.scratch(side, shard, slots, parts),
        [
            pltpu.VMEM((2, 2, rows, inner), LOW),
            pltpu.VMEM((2, 2, rows, inner), LOW),
            pltpu.SemaphoreType.DMA((2, 2)),
            pltpu.SemaphoreType.DMA((2, 2)),
            pltpu.SemaphoreType.DMA((2,)),
        ],
    ]

    def kernel(*refs):
        ins, outs, *scratch = take(refs, [5, 3] + [len(g) for g in groups])
        grad, weight, hidden, gate, up = ins
        gate_grad, up_grad, weight_grad = outs
        total, summed, land, ring_send, ring_recv, credit = scratch[0]
        given, made, given_sems, made_sems, out_sems = scratch[1]

        def product(way, owner):
            columns = pl.ds(aligned(owner * shard, shard), shard)
            step = min(256, side)

            @pl.loop(0, side // step)
            def _(index):
                at = pl.ds(aligned(index * step, step), step)
                take_at = pl.ds(aligned(way * side + index * step, step), step)
                total[way, at] = lax.dot_general(
                    hidden[:, take_at],
                    grad[:, columns],
                    (((0,), (0,)), ((), ())),
                    preferred_element_type=WIDE,
                )

        ring = RingScatter(
            product, total, summed, land, ring_send, ring_recv, credit, slots, parts
        )

        def load(chunk):
            slot = lax.rem(chunk, 2)
            return [
                pltpu.make_async_copy(
                    (gate, up)[which].at[row_slice(chunk, rows)],
                    given.at[slot, which],
                    given_sems.at[slot, which],
                )
                for which in range(2)
            ]

        def store(chunk):
            slot = lax.rem(chunk, 2)
            return [
                pltpu.make_async_copy(
                    made.at[slot, which],
                    (gate_grad, up_grad)[which].at[row_slice(chunk, rows)],
                    made_sems.at[slot, which],
                )
                for which in range(2)
            ]

        for item in load(0):
            item.start()
        greet(False, True)

        def iteration(step):
            slot = lax.rem(step, 2)
            ring.step(step)

            @pl.when(step + 1 < chunks)
            def _():
                for item in load(step + 1):
                    item.start()

            @pl.when(step >= 2)
            def _():
                for item in store(step - 2):
                    item.wait()

            for item in load(step):
                item.wait()

            @pl.loop(0, inner // tile)
            def _(index):
                at = pl.ds(aligned(index * tile, tile), tile)
                hidden_grad = lax.dot_general(
                    grad[row_slice(step, rows)],
                    weight[at],
                    (((1,), (1,)), ((), ())),
                    preferred_element_type=WIDE,
                )
                gate = given[slot, 0, :, at].astype(WIDE)
                up = given[slot, 1, :, at].astype(WIDE)
                sigma = jax.nn.sigmoid(gate)
                made[slot, 0, :, at] = (
                    hidden_grad * up * sigma * (1.0 + gate * (1.0 - sigma))
                ).astype(LOW)
                made[slot, 1, :, at] = (hidden_grad * gate * sigma).astype(LOW)

            for item in store(step):
                item.start()

        loop(chunks, iteration)
        writes = [
            pltpu.make_async_copy(
                total.at[way], weight_grad.at[way * side : (way + 1) * side], out_sems.at[way]
            )
            for way in range(2)
        ]
        for item in writes:
            item.start()
        for chunk in (chunks - 2, chunks - 1):
            for item in store(chunk):
                item.wait()
        ring.end()
        for item in writes:
            item.wait()

    shape = jax.ShapeDtypeStruct
    return pl.pallas_call(
        kernel,
        out_shape=[
            shape((length, inner), LOW),
            shape((length, inner), LOW),
            shape((inner, shard), WIDE),
        ],
        in_specs=[VMEM, VMEM, VMEM, HBM, HBM],
        out_specs=[HBM, HBM, HBM],
        scratch_shapes=[item for group in groups for item in group],
        compiler_params=pltpu.CompilerParams(
            collective_id=collective, has_side_effects=True, vmem_limit_bytes=60 * MIB
        ),
        cost_estimate=pl.CostEstimate(
            flops=4 * length * inner * D, bytes_accessed=16 * length * D, transcendentals=0
        ),
    )(grad, weight, hidden, gate, up)


def attn_in_back(grads, stack, inputs, mixed_grad, collective):
    length, columns = grads.shape
    width = mixed_grad.shape[1]
    count = lax.axis_size("gy")
    chunks = count
    rows = length // chunks
    shard = D // count
    side = columns // 2
    slots, parts = count - 1, 2
    tile = 256 if side % 256 == 0 else 128

    groups = [
        Reduce.scratch(rows, chunks, width, True),
        RingScatter.scratch(shard, side, slots, parts),
        [
            pltpu.VMEM((2, length, shard), LOW),
            pltpu.VMEM((rows, width), WIDE),
            pltpu.VMEM((2, rows, width), WIDE),
            pltpu.SemaphoreType.DMA((2,)),
            pltpu.SemaphoreType.DMA((1,)),
            pltpu.SemaphoreType.DMA((2,)),
            pltpu.SemaphoreType.DMA((2,)),
        ],
    ]

    def kernel(*refs):
        ins, outs, *scratch = take(refs, [4, 4] + [len(g) for g in groups])
        grads, stack, inputs, mixed_grad = ins
        token_grad, weight_grad, core_land, cross_land = outs
        reduce = Reduce(scratch[0], core_land, cross_land, rows, width, True)
        total, summed, land, ring_send, ring_recv, credit = scratch[1]
        left, mixed_buf, token_buf, left_sems, mixed_sems, token_sems, out_sems = scratch[2]

        def left_copy(way, owner):
            return pltpu.make_async_copy(
                inputs.at[:, pl.ds(aligned(owner * shard, shard), shard)],
                left.at[way],
                left_sems.at[way],
            )

        def product(way, owner):
            left_copy(way, owner).wait()

            @pl.loop(0, side // tile)
            def _(index):
                at = pl.ds(aligned(index * tile, tile), tile)
                take_at = pl.ds(aligned(way * side + index * tile, tile), tile)
                total[way, :, at] = lax.dot_general(
                    left[way],
                    grads[:, take_at],
                    (((0,), (0,)), ((), ())),
                    preferred_element_type=WIDE,
                )

        ring = RingScatter(
            product, total, summed, land, ring_send, ring_recv, credit, slots, parts
        )
        for way in range(2):
            left_copy(way, ring.owner(way, 0)).start()
        greet(True, True)

        def before(step):
            ring.step(step)

            @pl.when(step + 1 < count)
            def _():
                for way in range(2):
                    left_copy(way, ring.owner(way, step + 1)).start()

        def multiply(chunk, place):
            return lax.dot_general(
                grads[row_slice(chunk, rows)],
                stack[pl.ds(place, width)],
                (((1,), (1,)), ((), ())),
                preferred_element_type=WIDE,
            )

        def mixed_copy(chunk):
            return pltpu.make_async_copy(
                mixed_grad.at[row_slice(chunk, rows)], mixed_buf, mixed_sems.at[0]
            )

        def token_copy(chunk):
            slot = lax.rem(chunk, 2)
            return pltpu.make_async_copy(
                token_buf.at[slot], token_grad.at[row_slice(chunk, rows)], token_sems.at[slot]
            )

        def fetch(chunk):
            @pl.when(chunk >= 1)
            def _():
                mixed_copy(chunk - 1).start()

        def sums(chunk):
            pass

        def finish(chunk):
            slot = lax.rem(chunk, 2)
            mixed_copy(chunk).wait()

            @pl.when(chunk >= 2)
            def _():
                token_copy(chunk - 2).wait()

            def some(at):
                token_buf[slot, at] = mixed_buf[at] + reduce.raw[at]

            tiles(rows, some)
            token_copy(chunk).start()

        schedule(chunks, reduce, multiply, fetch, sums, finish, before, count)
        writes = [
            pltpu.make_async_copy(
                total.at[way], weight_grad.at[:, way * side : (way + 1) * side], out_sems.at[way]
            )
            for way in range(2)
        ]
        for item in writes:
            item.start()
        ring.end()
        reduce.end(chunks)
        for chunk in (chunks - 2, chunks - 1):
            token_copy(chunk).wait()
        for item in writes:
            item.wait()

    shape = jax.ShapeDtypeStruct
    out = pl.pallas_call(
        kernel,
        out_shape=[shape((length, width), WIDE), shape((shard, columns), WIDE)]
        + Reduce.landing(rows, chunks, width, True),
        in_specs=[VMEM, VMEM, HBM, HBM],
        out_specs=[HBM] * 4,
        scratch_shapes=[item for group in groups for item in group],
        compiler_params=pltpu.CompilerParams(
            collective_id=collective, has_side_effects=True, vmem_limit_bytes=60 * MIB
        ),
        cost_estimate=pl.CostEstimate(
            flops=4 * length * columns * D, bytes_accessed=8 * length * D, transcendentals=0
        ),
    )(grads, stack, inputs, mixed_grad)
    return out[:2]


def token_positions(segment):
    length = segment.shape[0]
    labels = jnp.arange(SEGS, dtype=jnp.int32)
    member = (segment[:, None] == labels[None, :]).astype(jnp.int32)
    totals = jnp.sum(member, axis=0)
    starts = jnp.cumsum(totals) - totals
    opening = jnp.sum(member * starts[None, :], axis=1)
    return jnp.arange(length, dtype=jnp.int32) - opening


def rotary_tables(segment):
    place = token_positions(segment).astype(jnp.float32)
    halves = HEAD // 2
    inverse = jnp.exp(jnp.arange(halves, dtype=jnp.float32) * (-2.0 * math.log(THETA) / HEAD))
    angle = place[:, None] * inverse[None, :]
    return (jnp.cos(angle), jnp.sin(angle))


def rotate(values, cosine, sine):
    halves = values.shape[-1] // 2
    former = values[..., :halves]
    latter = values[..., halves:]
    cosine = cosine[:, None, :]
    sine = sine[:, None, :]
    return jnp.concatenate(
        [former * cosine - latter * sine, latter * cosine + former * sine], axis=-1
    )


def row_totals(values):
    return lax.psum(values, "gx")


def block_layout(length):
    row_block = min(512, length)
    key_span = min(length, MAX_LEN + row_block)
    return (row_block, key_span)


def block_scores(queries, keys, segment, block_index, row_block, key_span):
    length = queries.shape[0]
    start_row = block_index * row_block
    key_start = jnp.clip(start_row + row_block - key_span, 0, length - key_span)
    query_rows = lax.dynamic_slice_in_dim(queries, start_row, row_block)
    key_rows = lax.dynamic_slice_in_dim(keys, key_start, key_span)
    scores = jnp.einsum(
        "qhd,khd->hqk", query_rows, key_rows, preferred_element_type=jnp.float32
    ) * (1.0 / math.sqrt(HEAD))
    query_index = start_row + jnp.arange(row_block, dtype=jnp.int32)
    key_index = key_start + jnp.arange(key_span, dtype=jnp.int32)
    query_doc = lax.dynamic_slice_in_dim(segment, start_row, row_block)
    key_doc = lax.dynamic_slice_in_dim(segment, key_start, key_span)
    allowed = (query_doc[:, None] == key_doc[None, :]) & (
        key_index[None, :] <= query_index[:, None]
    )
    return (jnp.where(allowed[None], scores, NEGATIVE), start_row, key_start, query_rows, key_rows)


def attend(queries, keys, values, segment):
    length = queries.shape[0]
    row_block, key_span = block_layout(length)

    def forward_block(block_index):
        scores, start_row, key_start, query_rows, key_rows = block_scores(
            queries, keys, segment, block_index, row_block, key_span
        )
        value_rows = lax.dynamic_slice_in_dim(values, key_start, key_span)
        row_peak = jnp.max(scores, axis=-1, keepdims=True)
        raised = jnp.exp(scores - row_peak)
        row_total = jnp.sum(raised, axis=-1, keepdims=True)
        probability = (raised / row_total).astype(jnp.bfloat16)
        attn_rows = jnp.einsum(
            "hqk,khd->qhd", probability, value_rows, preferred_element_type=jnp.float32
        )
        return (attn_rows, (row_peak + jnp.log(row_total))[..., 0])

    attn_rows, log_total = lax.map(forward_block, jnp.arange(length // row_block, dtype=jnp.int32))
    return (attn_rows.reshape(queries.shape), log_total)


def attend_back(queries, keys, values, segment, log_total, upstream):
    length = queries.shape[0]
    row_block, key_span = block_layout(length)
    factor = 1.0 / math.sqrt(HEAD)

    def backward_block(accumulated, inputs):
        block_index, block_total = inputs
        key_grad, value_grad = accumulated
        scores, start_row, key_start, query_rows, key_rows = block_scores(
            queries, keys, segment, block_index, row_block, key_span
        )
        value_rows = lax.dynamic_slice_in_dim(values, key_start, key_span)
        upstream_rows = lax.dynamic_slice_in_dim(upstream, start_row, row_block)
        probability = jnp.exp(scores - block_total[..., None])
        prob_grad = jnp.einsum(
            "qhd,khd->hqk", upstream_rows, value_rows, preferred_element_type=jnp.float32
        )
        score_grad = (
            probability * (prob_grad - jnp.sum(probability * prob_grad, axis=-1, keepdims=True))
        ).astype(jnp.bfloat16)
        query_grad = (
            jnp.einsum("hqk,khd->qhd", score_grad, key_rows, preferred_element_type=jnp.float32)
            * factor
        )
        key_part = (
            jnp.einsum("hqk,qhd->khd", score_grad, query_rows, preferred_element_type=jnp.float32)
            * factor
        )
        value_part = jnp.einsum(
            "hqk,qhd->khd",
            probability.astype(jnp.bfloat16),
            upstream_rows,
            preferred_element_type=jnp.float32,
        )
        key_grad = lax.dynamic_update_slice_in_dim(
            key_grad,
            lax.dynamic_slice_in_dim(key_grad, key_start, key_span) + key_part,
            key_start,
            0,
        )
        value_grad = lax.dynamic_update_slice_in_dim(
            value_grad,
            lax.dynamic_slice_in_dim(value_grad, key_start, key_span) + value_part,
            key_start,
            0,
        )
        return ((key_grad, value_grad), query_grad)

    zero_start = jnp.zeros(queries.shape, jnp.float32)
    block_order = jnp.arange(length // row_block, dtype=jnp.int32)
    (key_grad, value_grad), query_grad = lax.scan(
        backward_block, (zero_start, zero_start), (block_order, log_total)
    )
    return (query_grad.reshape(queries.shape), key_grad, value_grad)


def half_gain(gain):
    whole = lax.all_gather(gain, "gx", axis=0)
    core = lax.rem(lax.axis_index("gx"), 2)
    pairs = whole.reshape(whole.shape[0] // 2, 2, whole.shape[1])
    return lax.dynamic_index_in_dim(pairs, core, 1, keepdims=False).reshape(1, -1)


def own_part(values, width):
    chip = lax.div(lax.axis_index("gx"), 2)
    return lax.dynamic_slice_in_dim(values[0], chip * width, width)


def shards(
    tokens,
    query_weight,
    key_weight,
    value_weight,
    output_weight,
    gate_weight,
    up_weight,
    down_weight,
    query_gain,
    key_gain,
    attn_gain,
    mlp_gain,
    seq_ids,
    out_grad,
):
    segment = seq_ids[0]
    cosine, sine = rotary_tables(segment)
    length = tokens.shape[0]
    local_width = tokens.shape[1]
    local_heads = local_width // HEAD
    head_shape = (length, local_heads, HEAD)
    attn_half = half_gain(attn_gain)
    mlp_half = half_gain(mlp_gain)
    inputs, attn_stack = gather_in(
        tokens, jnp.concatenate([query_weight, key_weight, value_weight], axis=1), 1
    )
    inputs, output_weight, down_weight = lax.optimization_barrier(
        (inputs, output_weight, down_weight)
    )
    output_full = lax.all_gather(output_weight, "gy", axis=1, tiled=True)
    down_full = lax.all_gather(down_weight, "gy", axis=1, tiled=True)
    projected = jnp.dot(inputs, attn_stack, preferred_element_type=jnp.float32)
    query_raw = projected[:, :local_width]
    key_raw = projected[:, local_width : 2 * local_width]
    value_raw = projected[:, 2 * local_width :]
    squares = row_totals(
        jnp.concatenate(
            [
                jnp.sum(query_raw * query_raw, axis=1, keepdims=True),
                jnp.sum(key_raw * key_raw, axis=1, keepdims=True),
            ],
            axis=1,
        )
    )
    query_factor = lax.rsqrt(squares[:, :1] / D + EPS)
    key_factor = lax.rsqrt(squares[:, 1:] / D + EPS)
    queries = rotate(
        (query_raw * query_factor * query_gain).reshape(head_shape), cosine, sine
    ).astype(jnp.bfloat16)
    keys_rot = rotate((key_raw * key_factor * key_gain).reshape(head_shape), cosine, sine).astype(
        jnp.bfloat16
    )
    values_low = value_raw.astype(jnp.bfloat16).reshape(head_shape)
    attended_raw, log_total = attend(queries, keys_rot, values_low, segment)
    attended = attended_raw.reshape(length, local_width).astype(jnp.bfloat16)
    attn_raw, mixed, mlp_inputs, gate_full, up_full, upstream = attn_out(
        attended, output_full, attn_half, inputs, out_grad, gate_weight, up_weight, 2
    )
    hidden, gate, up = mlp_in(mlp_inputs, gate_full, up_full)
    result, mlp_full, mlp_gain_part = mlp_out(hidden, down_full, mlp_half, mixed, upstream, 3)
    gate_grad, up_grad, down_weight_grad = hidden_back(mlp_full, down_full, hidden, gate, up, 4)
    mixed_grad, attn_full, attn_gain_part, gate_weight_grad, up_weight_grad = mlp_back(
        gate_grad, up_grad, gate_full, up_full, mlp_inputs, attn_half, upstream, attn_raw, 5
    )
    output_product = lax.dot_general(
        attended, attn_full, (((0,), (0,)), ((), ())), preferred_element_type=jnp.float32
    )
    output_weight_grad = lax.psum_scatter(
        output_product.astype(jnp.bfloat16), "gy", scatter_dimension=1, tiled=True
    ).astype(jnp.float32)
    attended_grad = lax.dot_general(
        attn_full, output_full, (((1,), (1,)), ((), ())), preferred_element_type=jnp.float32
    )
    attended_grad = attended_grad.astype(jnp.bfloat16).reshape(head_shape)
    query_post, key_post, value_post = attend_back(
        queries, keys_rot, values_low, segment, log_total, attended_grad
    )
    query_normed_grad = rotate(query_post, cosine, -sine).reshape(length, local_width)
    key_normed_grad = rotate(key_post, cosine, -sine).reshape(length, local_width)
    projections = row_totals(
        jnp.concatenate(
            [
                jnp.sum(query_gain * query_normed_grad * query_raw, axis=1, keepdims=True),
                jnp.sum(key_gain * key_normed_grad * key_raw, axis=1, keepdims=True),
            ],
            axis=1,
        )
    )
    query_grad = (
        query_factor * query_gain * query_normed_grad
        - query_raw * query_factor**3 * projections[:, :1] / D
    ).astype(jnp.bfloat16)
    key_grad = (
        key_factor * key_gain * key_normed_grad - key_raw * key_factor**3 * projections[:, 1:] / D
    ).astype(jnp.bfloat16)
    value_grad = value_post.reshape(length, local_width).astype(jnp.bfloat16)
    query_gain_part = jnp.sum(query_normed_grad * query_raw * query_factor, axis=0)
    key_gain_part = jnp.sum(key_normed_grad * key_raw * key_factor, axis=0)
    projection_grad = jnp.concatenate([query_grad, key_grad, value_grad], axis=1)
    token_grad, attn_weight_grads = attn_in_back(projection_grad, attn_stack, inputs, mixed_grad, 6)
    query_weight_grad = attn_weight_grads[:, :local_width]
    key_weight_grad = attn_weight_grads[:, local_width : 2 * local_width]
    value_weight_grad = attn_weight_grads[:, 2 * local_width :]
    query_gain_grad, key_gain_grad, attn_gain_grad, mlp_gain_grad = lax.psum(
        (
            query_gain_part,
            key_gain_part,
            own_part(attn_gain_part, local_width),
            own_part(mlp_gain_part, local_width),
        ),
        "gy",
    )
    return (
        result,
        token_grad,
        query_weight_grad,
        key_weight_grad,
        value_weight_grad,
        output_weight_grad,
        gate_weight_grad,
        up_weight_grad,
        down_weight_grad,
        query_gain_grad,
        key_gain_grad,
        attn_gain_grad,
        mlp_gain_grad,
    )


def solution(mesh):
    return jax.shard_map(
        shards,
        mesh=mesh,
        in_specs=(
            P("gy", "gx"),
            P("gy", "gx"),
            P("gy", "gx"),
            P("gy", "gx"),
            P("gx", "gy"),
            P("gy", "gx"),
            P("gy", "gx"),
            P("gx", "gy"),
            P("gx"),
            P("gx"),
            P("gx"),
            P("gx"),
            P("gy", None),
            P("gy", "gx"),
        ),
        out_specs=(
            P("gy", "gx"),
            P("gy", "gx"),
            P("gy", "gx"),
            P("gy", "gx"),
            P("gy", "gx"),
            P("gx", "gy"),
            P("gy", "gx"),
            P("gy", "gx"),
            P("gx", "gy"),
            P("gx"),
            P("gx"),
            P("gx"),
            P("gx"),
        ),
        check_vma=False,
    )
```

```python
import math

import jax
import jax.numpy as jnp
from jax import lax
from jax.experimental import pallas as pl
from jax.experimental.pallas import tpu as pltpu
from jax.sharding import PartitionSpec as P

D = 2048
HEAD = 128
MAX_LEN = 1024
SEGS = 4


EPS = 1e-06
THETA = 500000.0
NEGATIVE = -1e30


MESH = pl.DeviceIdType.MESH
HBM = pl.BlockSpec(memory_space=pltpu.HBM)
VMEM = pl.BlockSpec(memory_space=pltpu.VMEM)
LOW = jnp.bfloat16
WIDE = jnp.float32
MIB = 1 << 20
LAG = 2
STATS = 128


def core_here():
    return lax.rem(lax.axis_index("gx"), 2)


def chip_here():
    return lax.div(lax.axis_index("gx"), 2)


def other_core():
    return lax.axis_index("gx") + 1 - 2 * core_here()


def peer_at(shift):
    return lax.rem(lax.axis_index("gx") + 2 * shift, lax.axis_size("gx"))


def rank_at(shift):
    return lax.rem(lax.axis_index("gx") + shift, lax.axis_size("gx"))


def ring_place():
    count = lax.axis_size("gy")
    index = lax.axis_index("gy")
    row, side = lax.div(index, 2), lax.rem(index, 2)
    return side * row + (1 - side) * (count - 1 - row)


def ring_device(place):
    count = lax.axis_size("gy")
    place = lax.rem(place + 2 * count, count)
    back = lax.div(place, count // 2)
    row = (1 - back) * place + back * (count - 1 - place)
    return 2 * row + 1 - back


def greet(gx, ring):
    barrier = pltpu.get_barrier_semaphore()
    partners = []
    if gx == "all":
        partners += [{"gx": rank_at(k)} for k in range(1, lax.axis_size("gx"))]
    elif gx:
        partners.append({"gx": other_core()})
        partners += [{"gx": peer_at(k)} for k in range(1, lax.axis_size("gx") // 2)]
    if ring:
        place = ring_place()
        partners += [{"gy": ring_device(place + 1)}, {"gy": ring_device(place - 1)}]
    for partner in partners:
        pl.semaphore_signal(barrier, inc=1, device_id=partner, device_id_type=MESH)
    pl.semaphore_wait(barrier, len(partners))


def remote(source, target, send, recv, device):
    return pltpu.make_async_remote_copy(
        src_ref=source,
        dst_ref=target,
        send_sem=send,
        recv_sem=recv,
        device_id=device,
        device_id_type=MESH,
    )


def loop(count, body):
    def step(index, carry):
        body(index)
        return carry

    lax.fori_loop(0, count, step, 0)


def aligned(value, factor):
    return pl.multiple_of(value, factor)


class RingGather:
    def __init__(self, sources, slot, parts, send, recv, local):
        self.sources, self.slot, self.parts = sources, slot, parts
        self.send, self.recv, self.local = send, recv, local
        self.count = lax.axis_size("gy")

    @staticmethod
    def scratch(parts):
        count = lax.axis_size("gy")
        return [
            pltpu.SemaphoreType.DMA((count - 1, 2, parts)),
            pltpu.SemaphoreType.DMA((count - 1, 2, parts)),
            pltpu.SemaphoreType.DMA((2,)),
        ]

    def copy(self, way, step, part, behind):
        place = ring_place()
        sign = 1 - 2 * way
        spot = self.slot(way, ring_device(place - sign * (step + behind)), part)
        return remote(
            spot,
            spot,
            self.send.at[step, way, part],
            self.recv.at[step, way, part],
            {"gy": ring_device(place + sign)},
        )

    def begin(self):
        place = [
            pltpu.make_async_copy(
                self.sources[way], self.slot(way, lax.axis_index("gy"), None), self.local.at[way]
            )
            for way in range(2)
        ]
        for item in place:
            item.start()
        for item in place:
            item.wait()
        for part in range(self.parts):
            for way in range(2):
                self.copy(way, 0, part, 0).start()

    @property
    def events(self):
        return (self.count - 2) * self.parts

    def event(self, index):
        step, part = 1 + lax.div(index, self.parts), lax.rem(index, self.parts)
        for way in range(2):
            self.copy(way, step - 1, part, 1).wait_recv()
            self.copy(way, step, part, 0).start()

    def end(self):
        for part in range(self.parts):
            for way in range(2):
                self.copy(way, self.count - 2, part, 1).wait_recv()

        def drain(step):
            for part in range(self.parts):
                for way in range(2):
                    self.copy(way, step, part, 0).wait_send()

        loop(self.count - 1, drain)


class RingScatter:
    def __init__(self, product, total, sums, land, send, recv, credit, slots, parts):
        self.product, self.total, self.sums, self.land = product, total, sums, land
        self.send, self.recv, self.credit = send, recv, credit
        self.slots, self.parts = slots, parts
        self.count = lax.axis_size("gy")
        self.rows = total.shape[1] // parts

    @staticmethod
    def scratch(rows, columns, slots, parts):
        count = lax.axis_size("gy")
        return [
            pltpu.VMEM((2, rows, columns), WIDE),
            pltpu.VMEM((2, rows, columns), LOW),
            pltpu.VMEM((slots, 2, rows, columns), LOW),
            pltpu.SemaphoreType.DMA((count - 1, 2, parts)),
            pltpu.SemaphoreType.DMA((count - 1, 2, parts)),
            pltpu.SemaphoreType.REGULAR((2, parts)),
        ]

    def copy(self, way, step, part):
        place = ring_place()
        rows = pl.ds(aligned(part * self.rows, self.rows), self.rows)
        return remote(
            self.sums.at[way, rows],
            self.land.at[lax.rem(step, self.slots), way, rows],
            self.send.at[step, way, part],
            self.recv.at[step, way, part],
            {"gy": ring_device(place + 1 - 2 * way)},
        )

    def owner(self, way, step):
        sign = 1 - 2 * way
        return ring_device(ring_place() - sign * (1 + step))

    @property
    def events(self):
        return self.count * self.parts

    def event(self, index):
        step, part = lax.div(index, self.parts), lax.rem(index, self.parts)
        last = self.count - 1
        tile = min(self.rows, 32)

        @pl.when(part == 0)
        def _():
            for way in range(2):
                self.product(way, step)

        for way in range(2):
            base = part * self.rows

            @pl.when(step >= 1)
            def _():
                self.copy(way, step - 1, part).wait_recv()
                slot = lax.rem(step - 1, self.slots)

                @pl.loop(0, self.rows // tile)
                def _(index):
                    rows = pl.ds(aligned(base + index * tile, tile), tile)
                    self.total[way, rows] += self.land[slot, way, rows].astype(WIDE)

                @pl.when(step - 1 + self.slots < last)
                def _():
                    upstream = ring_device(ring_place() - (1 - 2 * way))
                    pl.semaphore_signal(
                        self.credit.at[way, part],
                        inc=1,
                        device_id={"gy": upstream},
                        device_id_type=MESH,
                    )

            @pl.when(step < last)
            def _():
                @pl.when(step >= 1)
                def _():
                    self.copy(way, step - 1, part).wait_send()

                @pl.loop(0, self.rows // tile)
                def _(index):
                    rows = pl.ds(aligned(base + index * tile, tile), tile)
                    self.sums[way, rows] = self.total[way, rows].astype(LOW)

                @pl.when(step >= self.slots)
                def _():
                    pl.semaphore_wait(self.credit.at[way, part], 1)

                self.copy(way, step, part).start()

    def end(self):
        for part in range(self.parts):
            for way in range(2):
                self.copy(way, self.count - 2, part).wait_send()


class Reduce:
    def __init__(self, refs, core_land, cross_land, rows, width, scatter):
        (
            self.keep,
            self.core_send,
            self.core_stage,
            self.cross,
            self.cross_stage,
            self.raw,
            self.core_sems,
            self.cross_send_sems,
            self.cross_recv_sems,
            self.stage_sems,
        ) = refs
        self.core_land, self.cross_land = core_land, cross_land
        self.rows, self.width, self.scatter = rows, width, scatter
        self.chips = lax.axis_size("gx") // 2

    @staticmethod
    def scratch(rows, chunks, width, scatter):
        chips = lax.axis_size("gx") // 2
        half = chips * width
        part = width if scatter else half
        return [
            pltpu.VMEM((2, rows, half), LOW),
            pltpu.VMEM((2, rows, half), LOW),
            pltpu.VMEM((rows, half), LOW),
            pltpu.VMEM((LAG + 2, rows, half), LOW),
            pltpu.VMEM((chips - 1, rows, part), LOW),
            pltpu.VMEM((rows, part), WIDE),
            pltpu.SemaphoreType.DMA((2, chunks)),
            pltpu.SemaphoreType.DMA((chips - 1, chunks)),
            pltpu.SemaphoreType.DMA((chips - 1, chunks)),
            pltpu.SemaphoreType.DMA((chips,)),
        ]

    @staticmethod
    def landing(rows, chunks, width, scatter):
        chips = lax.axis_size("gx") // 2
        half = chips * width
        part = width if scatter else half
        return [
            jax.ShapeDtypeStruct((chunks, rows, half), LOW),
            jax.ShapeDtypeStruct((chips - 1, chunks, rows, part), LOW),
        ]

    def core_copy(self, chunk):
        return remote(
            self.core_send.at[lax.rem(chunk, 2)],
            self.core_land.at[chunk],
            self.core_sems.at[0, chunk],
            self.core_sems.at[1, chunk],
            {"gx": other_core()},
        )

    def cross_copy(self, shift, chunk):
        source = self.cross.at[lax.rem(chunk, LAG + 2)]
        if self.scatter:
            block = lax.rem(chip_here() + shift, self.chips)
            source = source.at[:, pl.ds(aligned(block * self.width, self.width), self.width)]
        return remote(
            source,
            self.cross_land.at[shift - 1, chunk],
            self.cross_send_sems.at[shift - 1, chunk],
            self.cross_recv_sems.at[shift - 1, chunk],
            {"gx": peer_at(shift)},
        )

    def produce(self, chunk, dot):
        @pl.when(chunk >= 2)
        def _():
            self.core_copy(chunk - 2).wait_send()

        slot = lax.rem(chunk, 2)
        core = core_here()
        for chip in range(self.chips):
            place = aligned((2 * chip + 1 - core) * self.width, self.width)
            self.core_send[slot, :, chip * self.width : (chip + 1) * self.width] = dot(
                place
            ).astype(LOW)
        self.core_copy(chunk).start()
        for chip in range(self.chips):
            place = aligned((2 * chip + core) * self.width, self.width)
            self.keep[slot, :, chip * self.width : (chip + 1) * self.width] = dot(
                place
            ).astype(LOW)

    def core_stage_copy(self, chunk):
        return pltpu.make_async_copy(
            self.core_land.at[chunk], self.core_stage, self.stage_sems.at[0]
        )

    def core_fetch(self, chunk):
        self.core_copy(chunk).wait_recv()
        self.core_stage_copy(chunk).start()

    def core_sum(self, chunk):
        slot, place = lax.rem(chunk, 2), lax.rem(chunk, LAG + 2)
        self.core_stage_copy(chunk).wait()

        @pl.when(chunk >= LAG + 2)
        def _():
            for shift in range(1, self.chips):
                self.cross_copy(shift, chunk - LAG - 2).wait_send()

        @pl.loop(0, self.rows // 32)
        def _(index):
            rows = pl.ds(aligned(index * 32, 32), 32)
            self.cross[place, rows] = (
                self.keep[slot, rows].astype(WIDE) + self.core_stage[rows].astype(WIDE)
            ).astype(LOW)

        for shift in range(1, self.chips):
            self.cross_copy(shift, chunk).start()

    def cross_stage_copy(self, shift, chunk):
        return pltpu.make_async_copy(
            self.cross_land.at[shift - 1, chunk],
            self.cross_stage.at[shift - 1],
            self.stage_sems.at[shift],
        )

    def cross_fetch(self, chunk):
        for shift in range(1, self.chips):
            self.cross_copy(shift, chunk).wait_recv()
            self.cross_stage_copy(shift, chunk).start()

    def cross_sum(self, chunk):
        place = lax.rem(chunk, LAG + 2)
        for shift in range(1, self.chips):
            self.cross_stage_copy(shift, chunk).wait()

        @pl.loop(0, self.rows // 32)
        def _(index):
            rows = pl.ds(aligned(index * 32, 32), 32)
            if self.scatter:
                block = pl.ds(aligned(chip_here() * self.width, self.width), self.width)
                total = self.cross[place, rows, block].astype(WIDE)
            else:
                total = self.cross[place, rows].astype(WIDE)
            for shift in range(1, self.chips):
                total = total + self.cross_stage[shift - 1, rows].astype(WIDE)
            self.raw[rows] = total

    def end(self, chunks):
        for chunk in (chunks - 2, chunks - 1):
            self.core_copy(chunk).wait_send()
        for chunk in range(chunks - LAG - 2, chunks):
            for shift in range(1, self.chips):
                self.cross_copy(shift, chunk).wait_send()


class Stats:
    def __init__(self, mine, land, sems):
        self.mine, self.land, self.sems = mine, land, sems

    @staticmethod
    def scratch(rows, chunks):
        return [
            pltpu.VMEM((2, rows, STATS), WIDE),
            pltpu.VMEM((chunks, rows, STATS), WIDE),
            pltpu.SemaphoreType.DMA((2, chunks)),
        ]

    def copy(self, chunk):
        return remote(
            self.mine.at[lax.rem(chunk, 2)],
            self.land.at[chunk],
            self.sems.at[0, chunk],
            self.sems.at[1, chunk],
            {"gx": other_core()},
        )

    def clear(self, chunk):
        @pl.when(chunk >= 2)
        def _():
            self.copy(chunk - 2).wait_send()

    def put(self, chunk, rows, first, second):
        lane = lax.broadcasted_iota(jnp.int32, (first.shape[0], STATS), 1)
        self.mine[lax.rem(chunk, 2), rows] = jnp.where(lane < STATS // 2, first, second)

    def get(self, chunk, rows):
        total = self.mine[lax.rem(chunk, 2), rows] + self.land[chunk, rows]
        return (total[:, :1], total[:, STATS // 2 : STATS // 2 + 1])

    def end(self, chunks):
        for chunk in (chunks - 2, chunks - 1):
            self.copy(chunk).wait_send()


class Spread:
    def __init__(self, buffer, whole, local, send, recv, rows, width):
        self.buffer, self.whole = buffer, whole
        self.local, self.send, self.recv = local, send, recv
        self.rows, self.width = rows, width
        self.chips = lax.axis_size("gx") // 2

    @staticmethod
    def scratch(rows, chunks, width):
        chips = lax.axis_size("gx") // 2
        return [
            pltpu.VMEM((2, rows, chips * width), LOW),
            pltpu.SemaphoreType.DMA((2, chips)),
            pltpu.SemaphoreType.DMA((chunks, chips)),
            pltpu.SemaphoreType.DMA((chunks, chips)),
        ]

    def pair(self, chunk, chip, core):
        slot = lax.rem(chunk, 2)
        source = self.buffer.at[slot, :, chip * self.width : (chip + 1) * self.width]
        rows = pl.ds(aligned(chunk * self.rows, self.rows), self.rows)
        columns = pl.ds(aligned((2 * chip + core) * self.width, self.width), self.width)
        target = self.whole.at[rows, columns]
        here = pltpu.make_async_copy(source, target, self.local.at[slot, chip])
        away = remote(
            source,
            target,
            self.send.at[chunk, chip],
            self.recv.at[chunk, chip],
            {"gx": other_core()},
        )
        return (here, away)

    def clear(self, chunk):
        @pl.when(chunk >= 2)
        def _():
            self.settle(chunk - 2)

    def settle(self, chunk):
        for chip in range(self.chips):
            here, away = self.pair(chunk, chip, core_here())
            here.wait()
            away.wait_send()

    def go(self, chunk):
        for chip in range(self.chips):
            here, away = self.pair(chunk, chip, core_here())
            here.start()
            away.start()

    def end(self, chunks):
        for chunk in (chunks - 2, chunks - 1):
            self.settle(chunk)

        def arrive(chunk):
            for chip in range(self.chips):
                self.pair(chunk, chip, 1 - core_here())[1].wait_recv()

        loop(chunks, arrive)


def row_slice(chunk, rows):
    return pl.ds(aligned(chunk * rows, rows), rows)


def core_columns(source, chunk, rows, width, buffer, sems, first):
    return [
        pltpu.make_async_copy(
            source.at[
                row_slice(chunk, rows),
                pl.ds(aligned((2 * chip + core_here()) * width, width), width),
            ],
            buffer.at[:, chip * width : (chip + 1) * width],
            sems.at[first + chip],
        )
        for chip in range(lax.axis_size("gx") // 2)
    ]


def tiles(rows, body):
    @pl.loop(0, rows // 32)
    def _(index):
        body(pl.ds(aligned(index * 32, 32), 32))


def schedule(chunks, reduce, multiply, fetch, sums, finish, event=None, events=0):
    steps = chunks + 2 + LAG

    def iteration(step):
        if event is not None:
            low = lax.div(step * events, steps)
            high = lax.div((step + 1) * events, steps)

            def some(index, carry):
                event(index)
                return carry

            lax.fori_loop(low, high, some, 0)

        @pl.when((step >= 1) & (step <= chunks))
        def _():
            reduce.core_fetch(step - 1)

        @pl.when((step >= 1 + LAG) & (step < chunks + 1 + LAG))
        def _():
            reduce.cross_fetch(step - 1 - LAG)

        @pl.when((step >= 1 + LAG) & (step < chunks + 2 + LAG))
        def _():
            fetch(step - 1 - LAG)

        @pl.when(step < chunks)
        def _():
            reduce.produce(step, lambda place: multiply(step, place))

        @pl.when((step >= 1) & (step <= chunks))
        def _():
            reduce.core_sum(step - 1)

        @pl.when((step >= 2 + LAG) & (step < chunks + 2 + LAG))
        def _():
            finish(step - 2 - LAG)

        @pl.when((step >= 1 + LAG) & (step < chunks + 1 + LAG))
        def _():
            reduce.cross_sum(step - 1 - LAG)
            sums(step - 1 - LAG)

    loop(steps, iteration)


def take(refs, counts):
    groups, start = [], 0
    for count in counts:
        groups.append(refs[start : start + count])
        start += count
    return groups


class Columns:
    def __init__(self, source, shard, left, turned, sem):
        self.source, self.shard = source, shard
        self.left, self.turned, self.sem = left, turned, sem

    @staticmethod
    def scratch(length, shard):
        return [
            pltpu.VMEM((length, shard), LOW),
            pltpu.VMEM((shard, length), LOW),
            pltpu.SemaphoreType.DMA((1,)),
        ]

    def copy(self, owner):
        at = pl.ds(aligned(owner * self.shard, self.shard), self.shard)
        return pltpu.make_async_copy(self.source.at[:, at], self.left, self.sem.at[0])

    def take(self, ring, way, step):
        self.copy(ring.owner(way, step)).wait()
        self.turned[...] = self.left[...].T
        if way == 0:
            self.copy(ring.owner(1, step)).start()
        else:

            @pl.when(step + 1 < ring.count)
            def _():
                self.copy(ring.owner(0, step + 1)).start()


def attn_out(attended, weight, gain, tokens, gate_shard, up_shard, collective):
    length, width = attended.shape
    chips = lax.axis_size("gx") // 2
    half = chips * width
    count = lax.axis_size("gy")
    chunks = count
    rows = length // chunks
    hidden = gate_shard.shape[1]
    shard = gate_shard.shape[0]
    ring_parts = 2
    part_rows = shard // ring_parts

    groups = [
        Reduce.scratch(rows, chunks, width, False),
        Stats.scratch(rows, chunks),
        Spread.scratch(rows, chunks, width),
        RingGather.scratch(ring_parts),
        [
            pltpu.VMEM((rows, half), LOW),
            pltpu.VMEM((2, rows, half), WIDE),
            pltpu.VMEM((2, rows, half), LOW),
            pltpu.SemaphoreType.DMA((chips,)),
            pltpu.SemaphoreType.DMA((2,)),
            pltpu.SemaphoreType.DMA((2,)),
        ],
    ]

    def kernel(*refs):
        ins, outs, *scratch = take(refs, [6, 7] + [len(g) for g in groups])
        attended, weight, gain, tokens, gate_shard, up_shard = ins
        raw_out, mixed_out, low_out, gate_full, up_full, core_land, cross_land = outs
        reduce = Reduce(scratch[0], core_land, cross_land, rows, width, False)
        stats = Stats(*scratch[1])
        buffer, local, send, recv = scratch[2]
        spread = Spread(buffer, low_out, local, send, recv, rows, width)
        token_buf, mixed_buf, raw_buf, token_sems, mixed_sems, raw_sems = scratch[4]
        full = (gate_full, up_full)

        def slot(way, owner, part):
            base = owner * shard
            if part is None:
                return full[way].at[pl.ds(aligned(base, shard), shard)]
            return full[way].at[pl.ds(aligned(base + part * part_rows, part_rows), part_rows)]

        ring = RingGather((gate_shard, up_shard), slot, ring_parts, *scratch[3])
        greet(True, True)
        ring.begin()

        def multiply(chunk, place):
            return jnp.dot(
                attended[row_slice(chunk, rows)],
                weight[:, pl.ds(place, width)],
                preferred_element_type=WIDE,
            )

        def token_copies(chunk):
            return core_columns(tokens, chunk, rows, width, token_buf, token_sems, 0)

        def fetch(chunk):
            @pl.when(chunk >= 1)
            def _():
                for item in token_copies(chunk - 1):
                    item.start()

        def mixed_copy(chunk):
            slot = lax.rem(chunk, 2)
            return pltpu.make_async_copy(
                mixed_buf.at[slot, :, pl.ds(aligned(chip_here() * width, width), width)],
                mixed_out.at[row_slice(chunk, rows)],
                mixed_sems.at[slot],
            )

        def raw_copy(chunk):
            slot = lax.rem(chunk, 2)
            return pltpu.make_async_copy(
                raw_buf.at[slot], raw_out.at[row_slice(chunk, rows)], raw_sems.at[slot]
            )

        def sums(chunk):
            stats.clear(chunk)

            @pl.when(chunk >= 2)
            def _():
                raw_copy(chunk - 2).wait()

            def tile(at):
                raw = reduce.raw[at]
                raw_buf[lax.rem(chunk, 2), at] = raw.astype(LOW)
                squares = jnp.sum(raw * raw, axis=1, keepdims=True)
                stats.put(chunk, at, squares, squares)

            tiles(rows, tile)
            stats.copy(chunk).start()
            raw_copy(chunk).start()

        def finish(chunk):
            slot = lax.rem(chunk, 2)
            for item in token_copies(chunk):
                item.wait()
            stats.copy(chunk).wait_recv()
            spread.clear(chunk)

            @pl.when(chunk >= 2)
            def _():
                mixed_copy(chunk - 2).wait()

            def tile(at):
                squares, _ = stats.get(chunk, at)
                factor = lax.rsqrt(squares / D + EPS)
                mixed = token_buf[at].astype(WIDE) + reduce.raw[at] * factor * gain[...]
                mixed_buf[slot, at] = mixed
                spread.buffer[slot, at] = mixed.astype(LOW)

            tiles(rows, tile)
            spread.go(chunk)
            mixed_copy(chunk).start()

        schedule(chunks, reduce, multiply, fetch, sums, finish, ring.event, ring.events)
        ring.end()
        reduce.end(chunks)
        stats.end(chunks)
        spread.end(chunks)
        for chunk in (chunks - 2, chunks - 1):
            mixed_copy(chunk).wait()
            raw_copy(chunk).wait()

    shape = jax.ShapeDtypeStruct
    out = pl.pallas_call(
        kernel,
        out_shape=[
            shape((length, half), LOW),
            shape((length, width), WIDE),
            shape((length, D), LOW),
            shape((shard * count, hidden), LOW),
            shape((shard * count, hidden), LOW),
        ]
        + Reduce.landing(rows, chunks, width, False),
        in_specs=[VMEM, VMEM, VMEM, HBM, HBM, HBM],
        out_specs=[HBM] * 7,
        scratch_shapes=[item for group in groups for item in group],
        compiler_params=pltpu.CompilerParams(
            collective_id=collective, has_side_effects=True, vmem_limit_bytes=60 * MIB
        ),
        cost_estimate=pl.CostEstimate(
            flops=2 * length * width * D, bytes_accessed=8 * length * D, transcendentals=0
        ),
    )(attended, weight, gain, tokens, gate_shard, up_shard)
    return out[:5]


def mlp_out(hidden, weight, gain, mixed, upstream, collective):
    length, inner = hidden.shape
    width = mixed.shape[1]
    chips = lax.axis_size("gx") // 2
    half = chips * width
    chunks = lax.axis_size("gy")
    rows = length // chunks

    groups = [
        Reduce.scratch(rows, chunks, width, False),
        Stats.scratch(rows, chunks),
        Spread.scratch(rows, chunks, width),
        [
            pltpu.VMEM((2, rows, half), LOW),
            pltpu.VMEM((rows, width), WIDE),
            pltpu.VMEM((2, rows, width), LOW),
            pltpu.SemaphoreType.DMA((2,)),
            pltpu.SemaphoreType.DMA((1,)),
            pltpu.SemaphoreType.DMA((2,)),
        ],
    ]

    def kernel(*refs):
        ins, outs, *scratch = take(refs, [5, 5] + [len(g) for g in groups])
        hidden, weight, gain, mixed, upstream = ins
        result, grad_out, gain_grad, core_land, cross_land = outs
        reduce = Reduce(scratch[0], core_land, cross_land, rows, width, False)
        stats = Stats(*scratch[1])
        buffer, local, send, recv = scratch[2]
        spread = Spread(buffer, grad_out, local, send, recv, rows, width)
        up_buf, mixed_buf, result_buf, up_sems, mixed_sems, result_sems = scratch[3]
        greet(True, False)
        gain_grad[...] = jnp.zeros_like(gain_grad)

        def multiply(chunk, place):
            return jnp.dot(
                hidden[row_slice(chunk, rows)],
                weight[:, pl.ds(place, width)],
                preferred_element_type=WIDE,
            )

        def up_copy(chunk):
            slot = lax.rem(chunk, 2)
            return pltpu.make_async_copy(
                upstream.at[row_slice(chunk, rows)], up_buf.at[slot], up_sems.at[slot]
            )

        def mixed_copy(chunk):
            return pltpu.make_async_copy(
                mixed.at[row_slice(chunk, rows)], mixed_buf, mixed_sems.at[0]
            )

        def result_copy(chunk):
            slot = lax.rem(chunk, 2)
            return pltpu.make_async_copy(
                result_buf.at[slot], result.at[row_slice(chunk, rows)], result_sems.at[slot]
            )

        def fetch(chunk):
            @pl.when(chunk < chunks)
            def _():
                up_copy(chunk).start()

            @pl.when(chunk >= 1)
            def _():
                mixed_copy(chunk - 1).start()

        def sums(chunk):
            slot = lax.rem(chunk, 2)
            stats.clear(chunk)
            up_copy(chunk).wait()

            def tile(at):
                raw = reduce.raw[at]
                up = up_buf[slot, at].astype(WIDE)
                squares = jnp.sum(raw * raw, axis=1, keepdims=True)
                projected = jnp.sum(gain[...] * up * raw, axis=1, keepdims=True)
                stats.put(chunk, at, squares, projected)

            tiles(rows, tile)
            stats.copy(chunk).start()

        def finish(chunk):
            slot = lax.rem(chunk, 2)
            mixed_copy(chunk).wait()
            stats.copy(chunk).wait_recv()
            spread.clear(chunk)

            @pl.when(chunk >= 2)
            def _():
                result_copy(chunk - 2).wait()

            block = pl.ds(aligned(chip_here() * width, width), width)

            def tile(at):
                squares, projected = stats.get(chunk, at)
                factor = lax.rsqrt(squares / D + EPS)
                raw = reduce.raw[at]
                up = up_buf[slot, at].astype(WIDE)
                spread.buffer[slot, at] = (
                    factor * gain[...] * up - raw * (factor * factor * factor * projected / D)
                ).astype(LOW)
                gain_grad[...] += jnp.sum(up * raw * factor, axis=0, keepdims=True)
                result_buf[slot, at] = (
                    mixed_buf[at] + reduce.raw[at, block] * factor * gain[:, block]
                ).astype(LOW)

            tiles(rows, tile)
            spread.go(chunk)
            result_copy(chunk).start()

        schedule(chunks, reduce, multiply, fetch, sums, finish)
        reduce.end(chunks)
        stats.end(chunks)
        spread.end(chunks)
        for chunk in (chunks - 2, chunks - 1):
            result_copy(chunk).wait()

    shape = jax.ShapeDtypeStruct
    out = pl.pallas_call(
        kernel,
        out_shape=[
            shape((length, width), LOW),
            shape((length, D), LOW),
            shape((1, half), WIDE),
        ]
        + Reduce.landing(rows, chunks, width, False),
        in_specs=[VMEM, VMEM, VMEM, HBM, HBM],
        out_specs=[HBM, HBM, VMEM, HBM, HBM],
        scratch_shapes=[item for group in groups for item in group],
        compiler_params=pltpu.CompilerParams(
            collective_id=collective, has_side_effects=True, vmem_limit_bytes=60 * MIB
        ),
        cost_estimate=pl.CostEstimate(
            flops=2 * length * inner * D, bytes_accessed=8 * length * D, transcendentals=0
        ),
    )(hidden, weight, gain, mixed, upstream)
    return out[:3]


def mlp_back(gate_grad, up_grad, gate_full, up_full, inputs, gain, upstream, attn_raw, collective):
    length, inner = gate_grad.shape
    half = attn_raw.shape[1]
    chips = lax.axis_size("gx") // 2
    width = half // chips
    count = lax.axis_size("gy")
    chunks = count
    rows = length // chunks
    shard = D // count
    slots, parts = 2, 2

    groups = [
        Reduce.scratch(rows, chunks, width, False),
        Stats.scratch(rows, chunks),
        Spread.scratch(rows, chunks, width),
        RingScatter.scratch(shard, inner, slots, parts),
        [
            pltpu.VMEM((rows, half), LOW),
            pltpu.VMEM((2, rows, half), LOW),
            pltpu.SemaphoreType.DMA((1,)),
            pltpu.SemaphoreType.DMA((2,)),
            pltpu.SemaphoreType.DMA((1,)),
            pltpu.SemaphoreType.DMA((2,)),
        ],
        Columns.scratch(length, shard),
    ]

    def kernel(*refs):
        ins, outs, *scratch = take(refs, [8, 7] + [len(g) for g in groups])
        gate_grad, up_grad, gate_full, up_full, inputs, gain, upstream, attn_raw = ins
        mixed_out, grad_out, gain_grad, gate_out, up_out, core_land, cross_land = outs
        reduce = Reduce(scratch[0], core_land, cross_land, rows, width, False)
        stats = Stats(*scratch[1])
        buffer, local, send, recv = scratch[2]
        spread = Spread(buffer, grad_out, local, send, recv, rows, width)
        total, summed, land, ring_send, ring_recv, credit = scratch[3]
        up_buf, raw_buf, up_sems, raw_sems, mixed_sems, out_sems = scratch[4]
        left = Columns(inputs, shard, *scratch[5])
        grads = (gate_grad, up_grad)

        def product(way, step):
            left.take(ring, way, step)
            tile = 512

            @pl.loop(0, inner // tile)
            def _(index):
                columns = pl.ds(aligned(index * tile, tile), tile)
                total[way, :, columns] = jnp.dot(
                    left.turned[...], grads[way][:, columns], preferred_element_type=WIDE
                )

        ring = RingScatter(
            product, total, summed, land, ring_send, ring_recv, credit, slots, parts
        )
        left.copy(ring.owner(0, 0)).start()
        greet(True, True)
        gain_grad[...] = jnp.zeros_like(gain_grad)

        def multiply(chunk, place):
            at = row_slice(chunk, rows)
            return lax.dot_general(
                gate_grad[at],
                gate_full[pl.ds(place, width)],
                (((1,), (1,)), ((), ())),
                preferred_element_type=WIDE,
            ) + lax.dot_general(
                up_grad[at],
                up_full[pl.ds(place, width)],
                (((1,), (1,)), ((), ())),
                preferred_element_type=WIDE,
            )

        def up_copy(chunk):
            return pltpu.make_async_copy(
                upstream.at[row_slice(chunk, rows)], up_buf, up_sems.at[0]
            )

        def raw_copy(chunk):
            slot = lax.rem(chunk, 2)
            return pltpu.make_async_copy(
                attn_raw.at[row_slice(chunk, rows)], raw_buf.at[slot], raw_sems.at[slot]
            )

        def mixed_copy(chunk):
            return pltpu.make_async_copy(
                reduce.raw.at[:, pl.ds(aligned(chip_here() * width, width), width)],
                mixed_out.at[row_slice(chunk, rows)],
                mixed_sems.at[0],
            )

        def fetch(chunk):
            @pl.when(chunk < chunks)
            def _():
                up_copy(chunk).start()
                raw_copy(chunk).start()

        def sums(chunk):
            slot = lax.rem(chunk, 2)
            stats.clear(chunk)
            up_copy(chunk).wait()
            raw_copy(chunk).wait()

            def tile(at):
                upward = reduce.raw[at] + up_buf[at].astype(WIDE)
                reduce.raw[at] = upward
                raw = raw_buf[slot, at].astype(WIDE)
                squares = jnp.sum(raw * raw, axis=1, keepdims=True)
                projected = jnp.sum(gain[...] * upward * raw, axis=1, keepdims=True)
                stats.put(chunk, at, squares, projected)

            tiles(rows, tile)
            stats.copy(chunk).start()
            mixed_copy(chunk).start()

        def finish(chunk):
            slot = lax.rem(chunk, 2)
            stats.copy(chunk).wait_recv()
            spread.clear(chunk)

            def tile(at):
                squares, projected = stats.get(chunk, at)
                factor = lax.rsqrt(squares / D + EPS)
                upward = reduce.raw[at]
                raw = raw_buf[slot, at].astype(WIDE)
                spread.buffer[slot, at] = (
                    factor * gain[...] * upward
                    - raw * (factor * factor * factor * projected / D)
                ).astype(LOW)
                gain_grad[...] += jnp.sum(upward * raw * factor, axis=0, keepdims=True)

            tiles(rows, tile)
            spread.go(chunk)
            mixed_copy(chunk).wait()

        schedule(chunks, reduce, multiply, fetch, sums, finish, ring.event, ring.events)
        writes = [
            pltpu.make_async_copy(total.at[way], (gate_out, up_out)[way], out_sems.at[way])
            for way in range(2)
        ]
        for item in writes:
            item.start()
        ring.end()
        reduce.end(chunks)
        stats.end(chunks)
        spread.end(chunks)
        for item in writes:
            item.wait()

    shape = jax.ShapeDtypeStruct
    out = pl.pallas_call(
        kernel,
        out_shape=[
            shape((length, width), WIDE),
            shape((length, D), LOW),
            shape((1, half), WIDE),
            shape((shard, inner), WIDE),
            shape((shard, inner), WIDE),
        ]
        + Reduce.landing(rows, chunks, width, False),
        in_specs=[VMEM, VMEM, VMEM, VMEM, HBM, VMEM, HBM, HBM],
        out_specs=[HBM, HBM, VMEM, HBM, HBM, HBM, HBM],
        scratch_shapes=[item for group in groups for item in group],
        compiler_params=pltpu.CompilerParams(
            collective_id=collective, has_side_effects=True, vmem_limit_bytes=60 * MIB
        ),
        cost_estimate=pl.CostEstimate(
            flops=8 * length * inner * D, bytes_accessed=16 * length * D, transcendentals=0
        ),
    )(gate_grad, up_grad, gate_full, up_full, inputs, gain, upstream, attn_raw)
    return out[:5]


class Total:
    def __init__(self, land, send, recv):
        self.land, self.send, self.recv = land, send, recv
        self.count = lax.axis_size("gx")

    @staticmethod
    def scratch(length):
        others = lax.axis_size("gx") - 1
        return [
            pltpu.VMEM((others, 8, length), WIDE),
            pltpu.SemaphoreType.DMA((others,)),
            pltpu.SemaphoreType.DMA((others,)),
        ]

    def copies(self, mine):
        return [
            remote(
                mine,
                self.land.at[shift - 1],
                self.send.at[shift - 1],
                self.recv.at[shift - 1],
                {"gx": rank_at(shift)},
            )
            for shift in range(1, self.count)
        ]

    def start(self, mine):
        for item in self.copies(mine):
            item.start()

    def finish(self, mine):
        for item in self.copies(mine):
            item.wait()
        total = mine[...]
        for shift in range(1, self.count):
            total = total + self.land[shift - 1]
        return total


def gather_in(tokens, stack, collective):
    length, width = tokens.shape
    shard, columns = stack.shape
    count = lax.axis_size("gy")
    chunks = count
    rows = length // chunks
    chips = lax.axis_size("gx") // 2
    side = columns // 2
    parts = 1

    groups = [
        RingGather.scratch(parts),
        [
            pltpu.SemaphoreType.DMA((1,)),
            pltpu.SemaphoreType.DMA((2,)),
            pltpu.SemaphoreType.DMA((chips - 1, chunks, 2)),
            pltpu.SemaphoreType.DMA((chips - 1, chunks, 2)),
        ],
        [
            pltpu.VMEM((D, columns), LOW),
            pltpu.VMEM((2, rows, D), LOW),
            pltpu.VMEM((2, 2, rows, width), WIDE),
            pltpu.VMEM((2, rows, width), LOW),
            pltpu.VMEM((length, STATS), WIDE),
            pltpu.VMEM((8, length), WIDE),
            pltpu.SemaphoreType.DMA((1,)),
            pltpu.SemaphoreType.DMA((2,)),
            pltpu.SemaphoreType.DMA((2, 3)),
        ],
        Total.scratch(length),
    ]

    def kernel(*refs):
        ins, outs, *scratch = take(refs, [2, 6] + [len(g) for g in groups])
        tokens, stack = ins
        whole, full, query_raw, key_raw, values, squares = outs
        own_sem, core_sems, cross_sems, pass_sems = scratch[1]
        weight, row_buf, raw_buf, value_buf, stats, mine = scratch[2][:6]
        weight_sem, row_sems, out_sems = scratch[2][6:]
        total = Total(*scratch[3])

        def slot(way, owner, part):
            return full.at[
                pl.ds(aligned(owner * shard, shard), shard), way * side : (way + 1) * side
            ]

        sources = [stack.at[:, way * side : (way + 1) * side] for way in range(2)]
        ring = RingGather(sources, slot, parts, *scratch[0])

        def block(rank, chunk):
            at = pl.ds(aligned(rank * width, width), width)
            if chunk is None:
                return whole.at[:, at]
            return whole.at[row_slice(chunk, rows), at]

        here = lax.axis_index("gx")
        own = pltpu.make_async_copy(tokens, block(here, None), own_sem.at[0])
        core = remote(
            tokens, block(here, None), core_sems.at[0], core_sems.at[1], {"gx": other_core()}
        )

        def cross(shift, chunk):
            return remote(
                tokens.at[row_slice(chunk, rows)],
                block(here, chunk),
                cross_sems.at[shift - 1, chunk, 0],
                cross_sems.at[shift - 1, chunk, 1],
                {"gx": peer_at(shift)},
            )

        def onward(shift, chunk):
            spot = block(peer_at(chips - shift), chunk)
            return remote(
                spot,
                spot,
                pass_sems.at[shift - 1, chunk, 0],
                pass_sems.at[shift - 1, chunk, 1],
                {"gx": other_core()},
            )

        own.start()
        greet("all", True)
        ring.begin()

        def send(chunk):
            for shift in range(1, chips):
                cross(shift, chunk).start()

        loop(chunks, send)
        core.start()

        def step(chunk):
            for shift in range(1, chips):
                cross(shift, chunk).wait_recv()
                onward(shift, chunk).start()

            @pl.when(chunk < ring.events)
            def _():
                ring.event(chunk)

        loop(chunks, step)
        ring.end()
        fetch = pltpu.make_async_copy(full, weight, weight_sem.at[0])
        fetch.start()

        def drain(chunk):
            for shift in range(1, chips):
                cross(shift, chunk).wait_send()
                onward(shift, chunk).wait()

        loop(chunks, drain)
        own.wait()
        core.wait()

        def row_copy(chunk):
            slot = lax.rem(chunk, 2)
            return pltpu.make_async_copy(
                whole.at[row_slice(chunk, rows)], row_buf.at[slot], row_sems.at[slot]
            )

        def stores(chunk):
            slot, at = lax.rem(chunk, 2), row_slice(chunk, rows)
            return [
                pltpu.make_async_copy(raw_buf.at[slot, 0], query_raw.at[at], out_sems.at[slot, 0]),
                pltpu.make_async_copy(raw_buf.at[slot, 1], key_raw.at[at], out_sems.at[slot, 1]),
                pltpu.make_async_copy(value_buf.at[slot], values.at[at], out_sems.at[slot, 2]),
            ]

        row_copy(0).start()
        fetch.wait()
        lane = lax.broadcasted_iota(jnp.int32, (rows, STATS), 1)

        def project(chunk):
            slot = lax.rem(chunk, 2)
            row_copy(chunk).wait()

            @pl.when(chunk + 1 < chunks)
            def _():
                row_copy(chunk + 1).start()

            @pl.when(chunk >= 2)
            def _():
                for item in stores(chunk - 2):
                    item.wait()

            some = []
            for which in range(2):
                raw = jnp.dot(
                    row_buf[slot],
                    weight[:, which * width : (which + 1) * width],
                    preferred_element_type=WIDE,
                )
                raw_buf[slot, which] = raw
                some.append(jnp.sum(raw * raw, axis=1, keepdims=True))
            value_buf[slot] = jnp.dot(
                row_buf[slot], weight[:, 2 * width :], preferred_element_type=WIDE
            ).astype(LOW)
            stats[row_slice(chunk, rows)] = jnp.where(lane == 0, some[0], some[1])
            for item in stores(chunk):
                item.start()

        loop(chunks, project)
        mine[...] = stats[...].T[:8]
        total.start(mine)
        for chunk in (chunks - 2, chunks - 1):
            for item in stores(chunk):
                item.wait()
        squares[...] = total.finish(mine)

    shape = jax.ShapeDtypeStruct
    return pl.pallas_call(
        kernel,
        out_shape=[
            shape((length, D), LOW),
            shape((shard * count, columns), LOW),
            shape((length, width), WIDE),
            shape((length, width), WIDE),
            shape((length, width), LOW),
            shape((8, length), WIDE),
        ],
        in_specs=[HBM, HBM],
        out_specs=[HBM] * 5 + [VMEM],
        scratch_shapes=[item for group in groups for item in group],
        compiler_params=pltpu.CompilerParams(
            collective_id=collective, has_side_effects=True, vmem_limit_bytes=40 * MIB
        ),
        cost_estimate=pl.CostEstimate(
            flops=2 * length * columns * D, bytes_accessed=8 * length * D, transcendentals=0
        ),
    )(tokens, stack)


def mlp_in(inputs, gate_full, up_full):
    length = inputs.shape[0]
    inner = gate_full.shape[1]
    rows = 256
    tile = 512

    def kernel(inputs, gate_weight, up_weight, hidden, gate_out, up_out):
        @pl.loop(0, inner // tile)
        def _(index):
            at = pl.ds(aligned(index * tile, tile), tile)
            gate = jnp.dot(inputs[...], gate_weight[:, at], preferred_element_type=WIDE)
            up = jnp.dot(inputs[...], up_weight[:, at], preferred_element_type=WIDE)
            hidden[:, at] = (gate * jax.nn.sigmoid(gate) * up).astype(LOW)
            gate_out[:, at] = gate.astype(LOW)
            up_out[:, at] = up.astype(LOW)

    block = pl.BlockSpec((rows, inner), lambda i: (i, 0))
    shape = jax.ShapeDtypeStruct((length, inner), LOW)
    return pl.pallas_call(
        kernel,
        grid=(length // rows,),
        out_shape=[shape] * 3,
        in_specs=[pl.BlockSpec((rows, D), lambda i: (i, 0)), VMEM, VMEM],
        out_specs=[block] * 3,
        compiler_params=pltpu.CompilerParams(vmem_limit_bytes=56 * MIB),
        cost_estimate=pl.CostEstimate(
            flops=4 * length * inner * D,
            bytes_accessed=2 * length * (D + 3 * inner) + 4 * D * inner,
            transcendentals=length * inner,
        ),
    )(inputs, gate_full, up_full)


def hidden_back(grad, weight, hidden, gate, up, collective):
    length, inner = hidden.shape
    count = lax.axis_size("gy")
    chunks = count
    rows = length // chunks
    shard = D // count
    side = inner // 2
    slots, parts = count - 1, 2
    tile = min(512, inner)

    groups = [
        RingScatter.scratch(shard, side, slots, parts),
        [
            pltpu.VMEM((2, 2, rows, inner), LOW),
            pltpu.VMEM((2, 2, rows, inner), LOW),
            pltpu.SemaphoreType.DMA((2, 2)),
            pltpu.SemaphoreType.DMA((2, 2)),
            pltpu.SemaphoreType.DMA((2,)),
            pltpu.VMEM((shard, length), LOW),
        ],
    ]

    def kernel(*refs):
        ins, outs, *scratch = take(refs, [5, 3] + [len(g) for g in groups])
        grad, weight, hidden, gate, up = ins
        gate_grad, up_grad, weight_grad = outs
        total, summed, land, ring_send, ring_recv, credit = scratch[0]
        given, made, given_sems, made_sems, out_sems, turned = scratch[1]

        def product(way, step):
            columns = pl.ds(aligned(ring.owner(way, step) * shard, shard), shard)
            turned[...] = grad[:, columns].T
            size = min(512, side)

            @pl.loop(0, side // size)
            def _(index):
                at = pl.ds(aligned(index * size, size), size)
                take_at = pl.ds(aligned(way * side + index * size, size), size)
                total[way, :, at] = jnp.dot(
                    turned[...], hidden[:, take_at], preferred_element_type=WIDE
                )

        ring = RingScatter(
            product, total, summed, land, ring_send, ring_recv, credit, slots, parts
        )

        def load(chunk):
            slot = lax.rem(chunk, 2)
            return [
                pltpu.make_async_copy(
                    (gate, up)[which].at[row_slice(chunk, rows)],
                    given.at[slot, which],
                    given_sems.at[slot, which],
                )
                for which in range(2)
            ]

        def store(chunk):
            slot = lax.rem(chunk, 2)
            return [
                pltpu.make_async_copy(
                    made.at[slot, which],
                    (gate_grad, up_grad)[which].at[row_slice(chunk, rows)],
                    made_sems.at[slot, which],
                )
                for which in range(2)
            ]

        for item in load(0):
            item.start()
        greet(False, True)

        def iteration(step):
            slot = lax.rem(step, 2)
            for part in range(parts):
                ring.event(step * parts + part)

            @pl.when(step + 1 < chunks)
            def _():
                for item in load(step + 1):
                    item.start()

            @pl.when(step >= 2)
            def _():
                for item in store(step - 2):
                    item.wait()

            for item in load(step):
                item.wait()

            @pl.loop(0, inner // tile)
            def _(index):
                at = pl.ds(aligned(index * tile, tile), tile)
                hidden_grad = lax.dot_general(
                    grad[row_slice(step, rows)],
                    weight[at],
                    (((1,), (1,)), ((), ())),
                    preferred_element_type=WIDE,
                )
                gate = given[slot, 0, :, at].astype(WIDE)
                up = given[slot, 1, :, at].astype(WIDE)
                sigma = jax.nn.sigmoid(gate)
                made[slot, 0, :, at] = (
                    hidden_grad * up * sigma * (1.0 + gate * (1.0 - sigma))
                ).astype(LOW)
                made[slot, 1, :, at] = (hidden_grad * gate * sigma).astype(LOW)

            for item in store(step):
                item.start()

        loop(chunks, iteration)
        writes = [
            pltpu.make_async_copy(
                total.at[way], weight_grad.at[:, way * side : (way + 1) * side], out_sems.at[way]
            )
            for way in range(2)
        ]
        for item in writes:
            item.start()
        for chunk in (chunks - 2, chunks - 1):
            for item in store(chunk):
                item.wait()
        ring.end()
        for item in writes:
            item.wait()

    shape = jax.ShapeDtypeStruct
    return pl.pallas_call(
        kernel,
        out_shape=[
            shape((length, inner), LOW),
            shape((length, inner), LOW),
            shape((shard, inner), WIDE),
        ],
        in_specs=[VMEM, VMEM, VMEM, HBM, HBM],
        out_specs=[HBM, HBM, HBM],
        scratch_shapes=[item for group in groups for item in group],
        compiler_params=pltpu.CompilerParams(
            collective_id=collective, has_side_effects=True, vmem_limit_bytes=60 * MIB
        ),
        cost_estimate=pl.CostEstimate(
            flops=4 * length * inner * D, bytes_accessed=16 * length * D, transcendentals=0
        ),
    )(grad, weight, hidden, gate, up)


def attn_in_back(
    query_back,
    key_back,
    value_grad,
    query_raw,
    key_raw,
    factors,
    projections,
    query_gain,
    key_gain,
    stack,
    inputs,
    mixed_grad,
    collective,
):
    length, columns = value_grad.shape[0], stack.shape[1]
    width = mixed_grad.shape[1]
    count = lax.axis_size("gy")
    chunks = count
    rows = length // chunks
    shard = D // count
    side = columns // 2
    slots, parts = count - 1, 2
    tile = 256 if side % 256 == 0 else 128

    groups = [
        Reduce.scratch(rows, chunks, width, True),
        RingScatter.scratch(shard, side, slots, parts),
        [
            pltpu.VMEM((rows, width), WIDE),
            pltpu.VMEM((2, rows, width), WIDE),
            pltpu.VMEM((length, columns), LOW),
            pltpu.VMEM((length, STATS), WIDE),
            pltpu.SemaphoreType.DMA((1,)),
            pltpu.SemaphoreType.DMA((2,)),
            pltpu.SemaphoreType.DMA((2,)),
        ],
        Columns.scratch(length, shard),
        Total.scratch(length),
    ]

    def kernel(*refs):
        ins, outs, *scratch = take(refs, [12, 4] + [len(g) for g in groups])
        query_back, key_back, value_grad, query_raw, key_raw, factors = ins[:6]
        projections, query_gain, key_gain, stack, inputs, mixed_grad = ins[6:]
        token_grad, weight_grad, core_land, cross_land = outs
        reduce = Reduce(scratch[0], core_land, cross_land, rows, width, True)
        total, summed, land, ring_send, ring_recv, credit = scratch[1]
        mixed_buf, token_buf, grads, projected, mixed_sems, token_sems, out_sems = scratch[2]
        left = Columns(inputs, shard, *scratch[3])
        total_sum = Total(*scratch[4])

        def product(way, step):
            left.take(ring, way, step)

            @pl.loop(0, side // tile)
            def _(index):
                at = pl.ds(aligned(index * tile, tile), tile)
                take_at = pl.ds(aligned(way * side + index * tile, tile), tile)
                total[way, :, at] = jnp.dot(
                    left.turned[...], grads[:, take_at], preferred_element_type=WIDE
                )

        ring = RingScatter(
            product, total, summed, land, ring_send, ring_recv, credit, slots, parts
        )
        left.copy(ring.owner(0, 0)).start()
        greet("all", True)
        total_sum.start(projections)
        grads[:, 2 * width :] = value_grad[...]
        sums_here = total_sum.finish(projections)
        projected[...] = jnp.concatenate([sums_here] * (STATS // 8), axis=0).T
        pairs = ((query_back, query_raw, query_gain), (key_back, key_raw, key_gain))

        @pl.loop(0, length // 32)
        def _(index):
            at = row_slice(index, 32)
            for which, (back, raw, gain) in enumerate(pairs):
                factor = factors[at, which : which + 1]
                pull = factor * factor * factor * projected[at, which : which + 1] / D
                grads[at, which * width : (which + 1) * width] = (
                    factor * gain[...] * back[at] - raw[at] * pull
                ).astype(LOW)

        def multiply(chunk, place):
            return lax.dot_general(
                grads[row_slice(chunk, rows)],
                stack[pl.ds(place, width)],
                (((1,), (1,)), ((), ())),
                preferred_element_type=WIDE,
            )

        def mixed_copy(chunk):
            return pltpu.make_async_copy(
                mixed_grad.at[row_slice(chunk, rows)], mixed_buf, mixed_sems.at[0]
            )

        def token_copy(chunk):
            slot = lax.rem(chunk, 2)
            return pltpu.make_async_copy(
                token_buf.at[slot], token_grad.at[row_slice(chunk, rows)], token_sems.at[slot]
            )

        def fetch(chunk):
            @pl.when(chunk >= 1)
            def _():
                mixed_copy(chunk - 1).start()

        def sums(chunk):
            pass

        def finish(chunk):
            slot = lax.rem(chunk, 2)
            mixed_copy(chunk).wait()

            @pl.when(chunk >= 2)
            def _():
                token_copy(chunk - 2).wait()

            def some(at):
                token_buf[slot, at] = mixed_buf[at] + reduce.raw[at]

            tiles(rows, some)
            token_copy(chunk).start()

        schedule(chunks, reduce, multiply, fetch, sums, finish, ring.event, ring.events)
        writes = [
            pltpu.make_async_copy(
                total.at[way], weight_grad.at[:, way * side : (way + 1) * side], out_sems.at[way]
            )
            for way in range(2)
        ]
        for item in writes:
            item.start()
        ring.end()
        reduce.end(chunks)
        for chunk in (chunks - 2, chunks - 1):
            token_copy(chunk).wait()
        for item in writes:
            item.wait()

    shape = jax.ShapeDtypeStruct
    out = pl.pallas_call(
        kernel,
        out_shape=[shape((length, width), WIDE), shape((shard, columns), WIDE)]
        + Reduce.landing(rows, chunks, width, True),
        in_specs=[VMEM] * 10 + [HBM, HBM],
        out_specs=[HBM] * 4,
        scratch_shapes=[item for group in groups for item in group],
        compiler_params=pltpu.CompilerParams(
            collective_id=collective, has_side_effects=True, vmem_limit_bytes=60 * MIB
        ),
        cost_estimate=pl.CostEstimate(
            flops=4 * length * columns * D, bytes_accessed=8 * length * D, transcendentals=0
        ),
    )(
        query_back,
        key_back,
        value_grad,
        query_raw,
        key_raw,
        factors,
        projections,
        query_gain,
        key_gain,
        stack,
        inputs,
        mixed_grad,
    )
    return out[:2]


def token_positions(segment):
    length = segment.shape[0]
    labels = jnp.arange(SEGS, dtype=jnp.int32)
    member = (segment[:, None] == labels[None, :]).astype(jnp.int32)
    totals = jnp.sum(member, axis=0)
    starts = jnp.cumsum(totals) - totals
    opening = jnp.sum(member * starts[None, :], axis=1)
    return jnp.arange(length, dtype=jnp.int32) - opening


def rotary_tables(segment):
    place = token_positions(segment).astype(jnp.float32)
    halves = HEAD // 2
    inverse = jnp.exp(jnp.arange(halves, dtype=jnp.float32) * (-2.0 * math.log(THETA) / HEAD))
    angle = place[:, None] * inverse[None, :]
    return (jnp.cos(angle), jnp.sin(angle))


def rotate(values, cosine, sine):
    halves = values.shape[-1] // 2
    former = values[..., :halves]
    latter = values[..., halves:]
    cosine = cosine[:, None, :]
    sine = sine[:, None, :]
    return jnp.concatenate(
        [former * cosine - latter * sine, latter * cosine + former * sine], axis=-1
    )


BLOCK = 256
LANES = 128
SCALE = 1.0 / math.sqrt(HEAD)
SCALE_TWO = SCALE * math.log2(math.e)


def turn(values, cosine, sine):
    return values * cosine + pltpu.roll(values, HEAD // 2, 1) * sine


def head_columns(head):
    return slice(head * HEAD, (head + 1) * HEAD)


def nt(left, right):
    return lax.dot_general(left, right, (((1,), (1,)), ((), ())), preferred_element_type=WIDE)


def attend(first_block, query_raw, key_raw, values, factors, query_gain, key_gain, tables, starts):
    length, width = query_raw.shape
    heads = width // HEAD

    def kernel(
        first_block,
        query_raw,
        key_raw,
        values,
        factors,
        query_gain,
        key_gain,
        cosine,
        sine,
        starts,
        queries,
        keys,
        attended,
        peaks,
        peak_columns,
    ):
        @pl.loop(0, length // BLOCK)
        def _(index):
            at = row_slice(index, BLOCK)
            cos, sin = cosine[at], sine[at]
            pairs = ((query_raw, query_gain, queries), (key_raw, key_gain, keys))
            for which, (raw, gain, out) in enumerate(pairs):
                factor = factors[at, which : which + 1]
                for head in range(heads):
                    columns = head_columns(head)
                    normed = raw[at, columns] * factor * gain[:, columns]
                    out[at, columns] = turn(normed, cos, sin).astype(LOW)

        lane = lax.broadcasted_iota(jnp.int32, (BLOCK, LANES), 1)
        row_index = lax.broadcasted_iota(jnp.int32, (BLOCK, BLOCK), 0)
        column_index = lax.broadcasted_iota(jnp.int32, (BLOCK, BLOCK), 1)

        def query_block(index):
            at = row_slice(index, BLOCK)
            start = starts[at]

            def key_block(other, carry):
                there = row_slice(other, BLOCK)
                key_place = column_index + other * BLOCK
                allowed = (key_place >= start) & (key_place <= row_index + index * BLOCK)
                made = []
                for head in range(heads):
                    columns = head_columns(head)
                    peak, total, rows = carry[head]
                    scores = nt(queries[at, columns], keys[there, columns]) * SCALE_TWO
                    scores = jnp.where(allowed, scores, NEGATIVE)
                    higher = jnp.maximum(peak, jnp.max(scores, axis=1, keepdims=True))
                    raised = jnp.exp2(scores - higher)
                    shrink = jnp.exp2(peak - higher)
                    total = total * shrink + jnp.sum(raised, axis=1, keepdims=True)
                    rows = rows * shrink + jnp.dot(
                        raised.astype(LOW), values[there, columns], preferred_element_type=WIDE
                    )
                    made.append((higher, total, rows))
                return tuple(made)

            empty = (
                jnp.full((BLOCK, 1), NEGATIVE, WIDE),
                jnp.zeros((BLOCK, 1), WIDE),
                jnp.zeros((BLOCK, HEAD), WIDE),
            )
            done = lax.fori_loop(first_block[index], index + 1, key_block, (empty,) * heads)
            column = jnp.zeros((BLOCK, LANES), WIDE)
            for head in range(heads):
                peak, total, rows = done[head]
                attended[at, head_columns(head)] = (rows / total).astype(LOW)
                column = jnp.where(lane == head, peak + jnp.log2(total), column)
            peak_columns[at] = column

        loop(length // BLOCK, query_block)
        peaks[...] = peak_columns[...].T[:8]

    shape = jax.ShapeDtypeStruct
    smem = pl.BlockSpec(memory_space=pltpu.SMEM)
    return pl.pallas_call(
        kernel,
        out_shape=[
            shape((length, width), LOW),
            shape((length, width), LOW),
            shape((length, width), LOW),
            shape((8, length), WIDE),
        ],
        in_specs=[smem] + [VMEM] * 9,
        out_specs=[VMEM] * 4,
        scratch_shapes=[pltpu.VMEM((length, LANES), WIDE)],
        compiler_params=pltpu.CompilerParams(vmem_limit_bytes=48 * MIB),
        cost_estimate=pl.CostEstimate(
            flops=2 * length * MAX_LEN * width,
            bytes_accessed=16 * length * width,
            transcendentals=length * MAX_LEN * heads // 2,
        ),
    )(first_block, query_raw, key_raw, values, factors, query_gain, key_gain, *tables, starts)


def attend_back(
    last_block,
    queries,
    keys,
    values,
    attended,
    upstream,
    peaks,
    query_raw,
    key_raw,
    factors,
    query_gain,
    key_gain,
    tables,
    start_row,
):
    length, width = query_raw.shape
    heads = width // HEAD

    def kernel(
        last_block,
        queries,
        keys,
        values,
        attended,
        upstream,
        peaks,
        query_raw,
        key_raw,
        factors,
        query_gain,
        key_gain,
        cosine,
        sine,
        start_row,
        query_out,
        key_out,
        value_out,
        projections,
        query_gain_grad,
        key_gain_grad,
        query_sum,
        key_sum,
        value_sum,
        columns_scratch,
        deltas,
    ):
        lane = lax.broadcasted_iota(jnp.int32, (BLOCK, LANES), 1)
        query_gain_grad[...] = jnp.zeros_like(query_gain_grad)
        key_gain_grad[...] = jnp.zeros_like(key_gain_grad)

        def prepare(index):
            at = row_slice(index, BLOCK)
            column = jnp.zeros((BLOCK, LANES), WIDE)
            for head in range(heads):
                columns = head_columns(head)
                delta = jnp.sum(
                    attended[at, columns].astype(WIDE) * upstream[at, columns].astype(WIDE),
                    axis=1,
                    keepdims=True,
                )
                column = jnp.where(lane == head, delta, column)
            columns_scratch[at] = column
            query_sum[at] = jnp.zeros((BLOCK, width), WIDE)

        loop(length // BLOCK, prepare)
        deltas[...] = columns_scratch[...].T[:8]
        row_index = lax.broadcasted_iota(jnp.int32, (BLOCK, BLOCK), 0)
        column_index = lax.broadcasted_iota(jnp.int32, (BLOCK, BLOCK), 1)

        def turn_back(at, summed, raw, gain, factor, out, gain_grad):
            cos, sin = cosine[at], sine[at]
            share = jnp.zeros((BLOCK, 1), WIDE)
            for head in range(heads):
                columns = head_columns(head)
                normed = turn(summed(head) * SCALE, cos, -sin)
                out[at, columns] = normed
                weighed = normed * raw[at, columns]
                share += jnp.sum(gain[:, columns] * weighed, axis=1, keepdims=True)
                gain_grad[:, columns] += jnp.sum(weighed * factor, axis=0, keepdims=True)
            return share

        def key_block(index):
            at = row_slice(index, BLOCK)
            key_sum[...] = jnp.zeros_like(key_sum)
            value_sum[...] = jnp.zeros_like(value_sum)

            def query_block(other, carry):
                there = row_slice(other, BLOCK)
                key_place = row_index + index * BLOCK
                allowed = (key_place >= start_row[:, there]) & (
                    key_place <= column_index + other * BLOCK
                )
                for head in range(heads):
                    columns = head_columns(head)
                    scores = nt(keys[at, columns], queries[there, columns]) * SCALE_TWO
                    scores = jnp.where(allowed, scores, NEGATIVE)
                    chance = jnp.exp2(scores - peaks[head : head + 1, there])
                    value_sum[:, columns] += jnp.dot(
                        chance.astype(LOW), upstream[there, columns], preferred_element_type=WIDE
                    )
                    chance_grad = nt(values[at, columns], upstream[there, columns])
                    score_grad = (chance * (chance_grad - deltas[head : head + 1, there])).astype(LOW)
                    key_sum[:, columns] += jnp.dot(
                        score_grad, queries[there, columns], preferred_element_type=WIDE
                    )
                    query_sum[there, columns] += lax.dot_general(
                        score_grad,
                        keys[at, columns],
                        (((0,), (0,)), ((), ())),
                        preferred_element_type=WIDE,
                    )
                return carry

            lax.fori_loop(index, last_block[index] + 1, query_block, 0)
            value_out[at] = value_sum[...].astype(LOW)
            share = turn_back(
                at,
                lambda head: key_sum[:, head_columns(head)],
                key_raw,
                key_gain,
                factors[at, 1:2],
                key_out,
                key_gain_grad,
            )
            columns_scratch[at] = jnp.where(lane == 1, share, 0.0)

        loop(length // BLOCK, key_block)

        def finish(index):
            at = row_slice(index, BLOCK)
            share = turn_back(
                at,
                lambda head: query_sum[at, head_columns(head)],
                query_raw,
                query_gain,
                factors[at, 0:1],
                query_out,
                query_gain_grad,
            )
            columns_scratch[at] += jnp.where(lane == 0, share, 0.0)

        loop(length // BLOCK, finish)
        projections[...] = columns_scratch[...].T[:8]

    shape = jax.ShapeDtypeStruct
    smem = pl.BlockSpec(memory_space=pltpu.SMEM)
    return pl.pallas_call(
        kernel,
        out_shape=[
            shape((length, width), WIDE),
            shape((length, width), WIDE),
            shape((length, width), LOW),
            shape((8, length), WIDE),
            shape((1, width), WIDE),
            shape((1, width), WIDE),
        ],
        in_specs=[smem] + [VMEM] * 14,
        out_specs=[VMEM] * 6,
        scratch_shapes=[
            pltpu.VMEM((length, width), WIDE),
            pltpu.VMEM((BLOCK, width), WIDE),
            pltpu.VMEM((BLOCK, width), WIDE),
            pltpu.VMEM((length, LANES), WIDE),
            pltpu.VMEM((8, length), WIDE),
        ],
        compiler_params=pltpu.CompilerParams(vmem_limit_bytes=52 * MIB),
        cost_estimate=pl.CostEstimate(
            flops=5 * length * MAX_LEN * width,
            bytes_accessed=32 * length * width,
            transcendentals=length * MAX_LEN * heads // 2,
        ),
    )(
        last_block,
        queries,
        keys,
        values,
        attended,
        upstream,
        peaks,
        query_raw,
        key_raw,
        factors,
        query_gain,
        key_gain,
        *tables,
        start_row,
    )


def half_gain(gain):
    whole = lax.all_gather(gain, "gx", axis=0)
    core = lax.rem(lax.axis_index("gx"), 2)
    pairs = whole.reshape(whole.shape[0] // 2, 2, whole.shape[1])
    return lax.dynamic_index_in_dim(pairs, core, 1, keepdims=False).reshape(1, -1)


def gather_chips(values):
    count = lax.axis_size("gx")
    chip = lax.div(lax.axis_index("gx"), 2)
    width = values.shape[1]
    whole = jnp.zeros((values.shape[0], count // 2 * width), values.dtype)
    for shift in range(count // 2):
        moved = values
        if shift:
            moved = lax.ppermute(values, "gx", [(i, (i + 2 * shift) % count) for i in range(count)])
        place = lax.rem(chip - shift + count // 2, count // 2) * width
        whole = lax.dynamic_update_slice(whole, moved, (0, place))
    return whole


def own_part(values, width):
    chip = lax.div(lax.axis_index("gx"), 2)
    return lax.dynamic_slice_in_dim(values[0], chip * width, width)


def shards(
    tokens,
    query_weight,
    key_weight,
    value_weight,
    output_weight,
    gate_weight,
    up_weight,
    down_weight,
    query_gain,
    key_gain,
    attn_gain,
    mlp_gain,
    seq_ids,
    out_grad,
):
    segment = seq_ids[0]
    length = tokens.shape[0]
    local_width = tokens.shape[1]
    cosine, sine = rotary_tables(segment)
    tables = (
        jnp.concatenate([cosine, cosine], axis=1),
        jnp.concatenate([-sine, sine], axis=1),
    )
    order = jnp.arange(length, dtype=jnp.int32)
    starts = order - token_positions(segment)
    blocks = length // BLOCK
    first_block = starts.reshape(blocks, BLOCK)[:, 0] // BLOCK
    closing = segment.reshape(blocks, BLOCK)[:, -1]
    ends = jnp.sum((segment[None, :] <= closing[:, None]).astype(jnp.int32), axis=1) - 1
    last_block = ends // BLOCK
    attn_half = half_gain(attn_gain)
    mlp_half = half_gain(mlp_gain)
    query_gain, key_gain = query_gain.reshape(1, -1), key_gain.reshape(1, -1)
    upstream = gather_chips(out_grad)
    inputs, attn_stack, query_raw, key_raw, values, squares = gather_in(
        tokens, jnp.concatenate([query_weight, key_weight, value_weight], axis=1), 1
    )
    squares, output_weight, down_weight = lax.optimization_barrier(
        (squares, output_weight, down_weight)
    )
    output_full = lax.all_gather(output_weight, "gy", axis=1, tiled=True)
    down_full = lax.all_gather(down_weight, "gy", axis=1, tiled=True)
    factors = lax.rsqrt(squares[:2].T / D + EPS)
    queries, keys, attended, peaks = attend(
        first_block,
        query_raw,
        key_raw,
        values,
        factors,
        query_gain,
        key_gain,
        tables,
        starts[:, None],
    )
    attn_raw, mixed, mlp_inputs, gate_full, up_full = attn_out(
        attended, output_full, attn_half, inputs, gate_weight, up_weight, 2
    )
    hidden, gate, up = mlp_in(mlp_inputs, gate_full, up_full)
    result, mlp_full, mlp_gain_part = mlp_out(hidden, down_full, mlp_half, mixed, upstream, 3)
    gate_grad, up_grad, down_turned = hidden_back(mlp_full, down_full, hidden, gate, up, 4)
    down_weight_grad = down_turned.T
    mixed_grad, attn_full, attn_gain_part, gate_weight_grad, up_weight_grad = mlp_back(
        gate_grad, up_grad, gate_full, up_full, mlp_inputs, attn_half, upstream, attn_raw, 5
    )
    output_product = lax.dot_general(
        attended, attn_full, (((0,), (0,)), ((), ())), preferred_element_type=jnp.float32
    )
    output_weight_grad = lax.psum_scatter(
        output_product.astype(jnp.bfloat16), "gy", scatter_dimension=1, tiled=True
    ).astype(jnp.float32)
    attended_grad = lax.dot_general(
        attn_full, output_full, (((1,), (1,)), ((), ())), preferred_element_type=jnp.float32
    ).astype(jnp.bfloat16)
    query_back, key_back, value_grad, projections, query_gain_part, key_gain_part = attend_back(
        last_block,
        queries,
        keys,
        values,
        attended,
        attended_grad,
        peaks,
        query_raw,
        key_raw,
        factors,
        query_gain,
        key_gain,
        tables,
        starts[None, :],
    )
    token_grad, attn_weight_grads = attn_in_back(
        query_back,
        key_back,
        value_grad,
        query_raw,
        key_raw,
        factors,
        projections,
        query_gain,
        key_gain,
        attn_stack,
        inputs,
        mixed_grad,
        6,
    )
    query_weight_grad = attn_weight_grads[:, :local_width]
    key_weight_grad = attn_weight_grads[:, local_width : 2 * local_width]
    value_weight_grad = attn_weight_grads[:, 2 * local_width :]
    query_gain_grad, key_gain_grad, attn_gain_grad, mlp_gain_grad = lax.psum(
        (
            query_gain_part[0],
            key_gain_part[0],
            own_part(attn_gain_part, local_width),
            own_part(mlp_gain_part, local_width),
        ),
        "gy",
    )
    return (
        result,
        token_grad,
        query_weight_grad,
        key_weight_grad,
        value_weight_grad,
        output_weight_grad,
        gate_weight_grad,
        up_weight_grad,
        down_weight_grad,
        query_gain_grad,
        key_gain_grad,
        attn_gain_grad,
        mlp_gain_grad,
    )


def solution(mesh):
    return jax.shard_map(
        shards,
        mesh=mesh,
        in_specs=(
            P("gy", "gx"),
            P("gy", "gx"),
            P("gy", "gx"),
            P("gy", "gx"),
            P("gx", "gy"),
            P("gy", "gx"),
            P("gy", "gx"),
            P("gx", "gy"),
            P("gx"),
            P("gx"),
            P("gx"),
            P("gx"),
            P("gy", None),
            P("gy", "gx"),
        ),
        out_specs=(
            P("gy", "gx"),
            P("gy", "gx"),
            P("gy", "gx"),
            P("gy", "gx"),
            P("gy", "gx"),
            P("gx", "gy"),
            P("gy", "gx"),
            P("gy", "gx"),
            P("gx", "gy"),
            P("gx"),
            P("gx"),
            P("gx"),
            P("gx"),
        ),
        check_vma=False,
    )
```

```python
import math

import jax
import jax.numpy as jnp
from jax import lax
from jax.experimental import pallas as pl
from jax.experimental.pallas import tpu as pltpu
from jax.sharding import PartitionSpec as P

D = 2048
HEAD = 128
MAX_LEN = 1024
SEGS = 4


EPS = 1e-06
THETA = 500000.0
NEGATIVE = -1e30


MESH = pl.DeviceIdType.MESH
HBM = pl.BlockSpec(memory_space=pltpu.HBM)
VMEM = pl.BlockSpec(memory_space=pltpu.VMEM)
LOW = jnp.bfloat16
WIDE = jnp.float32
MIB = 1 << 20
LAG = 2
STATS = 128


def core_here():
    return lax.rem(lax.axis_index("gx"), 2)


def chip_here():
    return lax.div(lax.axis_index("gx"), 2)


def other_core():
    return lax.axis_index("gx") + 1 - 2 * core_here()


def peer_at(shift):
    return lax.rem(lax.axis_index("gx") + 2 * shift, lax.axis_size("gx"))


def rank_at(shift):
    return lax.rem(lax.axis_index("gx") + shift, lax.axis_size("gx"))


def block_at(shift):
    return lax.rem(lax.axis_index("gy") + shift, lax.axis_size("gy"))


def ring_place():
    count = lax.axis_size("gy")
    index = lax.axis_index("gy")
    row, side = lax.div(index, 2), lax.rem(index, 2)
    return side * row + (1 - side) * (count - 1 - row)


def ring_device(place):
    count = lax.axis_size("gy")
    place = lax.rem(place + 2 * count, count)
    back = lax.div(place, count // 2)
    row = (1 - back) * place + back * (count - 1 - place)
    return 2 * row + 1 - back


def greet(gx, ring, all_blocks=False):
    barrier = pltpu.get_barrier_semaphore()
    partners = []
    if all_blocks:
        partners += [{"gy": block_at(k)} for k in range(1, lax.axis_size("gy"))]
    if gx == "all":
        partners += [{"gx": rank_at(k)} for k in range(1, lax.axis_size("gx"))]
    elif gx:
        partners.append({"gx": other_core()})
        partners += [{"gx": peer_at(k)} for k in range(1, lax.axis_size("gx") // 2)]
    if ring:
        place = ring_place()
        partners += [{"gy": ring_device(place + 1)}, {"gy": ring_device(place - 1)}]
    for partner in partners:
        pl.semaphore_signal(barrier, inc=1, device_id=partner, device_id_type=MESH)
    pl.semaphore_wait(barrier, len(partners))


def remote(source, target, send, recv, device):
    return pltpu.make_async_remote_copy(
        src_ref=source,
        dst_ref=target,
        send_sem=send,
        recv_sem=recv,
        device_id=device,
        device_id_type=MESH,
    )


def loop(count, body):
    def step(index, carry):
        body(index)
        return carry

    lax.fori_loop(0, count, step, 0)


def aligned(value, factor):
    return pl.multiple_of(value, factor)


class RingGather:
    def __init__(self, sources, slot, parts, send, recv, local):
        self.sources, self.slot, self.parts = sources, slot, parts
        self.send, self.recv, self.local = send, recv, local
        self.count = lax.axis_size("gy")

    @staticmethod
    def scratch(parts):
        count = lax.axis_size("gy")
        return [
            pltpu.SemaphoreType.DMA((count - 1, 2, parts)),
            pltpu.SemaphoreType.DMA((count - 1, 2, parts)),
            pltpu.SemaphoreType.DMA((2, parts)),
        ]

    def copy(self, way, step, part, behind):
        place = ring_place()
        sign = 1 - 2 * way
        spot = self.slot(way, ring_device(place - sign * (step + behind)), part)
        return remote(
            spot,
            spot,
            self.send.at[step, way, part],
            self.recv.at[step, way, part],
            {"gy": ring_device(place + sign)},
        )

    def begin(self):
        place = [
            pltpu.make_async_copy(
                self.sources(way, part),
                self.slot(way, lax.axis_index("gy"), part),
                self.local.at[way, part],
            )
            for way in range(2)
            for part in range(self.parts)
        ]
        for item in place:
            item.start()
        for item in place:
            item.wait()
        for part in range(self.parts):
            for way in range(2):
                self.copy(way, 0, part, 0).start()

    @property
    def events(self):
        return (self.count - 2) * self.parts

    def event(self, index):
        step = 1 + lax.div(index, self.parts)
        for part in range(self.parts):

            @pl.when(lax.rem(index, self.parts) == part)
            def _():
                for way in range(2):
                    self.copy(way, step - 1, part, 1).wait_recv()
                    self.copy(way, step, part, 0).start()

    def end(self):
        for part in range(self.parts):
            for way in range(2):
                self.copy(way, self.count - 2, part, 1).wait_recv()

        def drain(step):
            for part in range(self.parts):
                for way in range(2):
                    self.copy(way, step, part, 0).wait_send()

        loop(self.count - 1, drain)


class RingScatter:
    def __init__(self, product, total, sums, land, send, recv, credit, slots, parts):
        self.product, self.total, self.sums, self.land = product, total, sums, land
        self.send, self.recv, self.credit = send, recv, credit
        self.slots, self.parts = slots, parts
        self.count = lax.axis_size("gy")
        self.rows = total.shape[1] // parts

    @staticmethod
    def scratch(rows, columns, slots, parts):
        count = lax.axis_size("gy")
        return [
            pltpu.VMEM((2, rows, columns), WIDE),
            pltpu.VMEM((2, rows, columns), LOW),
            pltpu.VMEM((slots, 2, rows, columns), LOW),
            pltpu.SemaphoreType.DMA((count - 1, 2, parts)),
            pltpu.SemaphoreType.DMA((count - 1, 2, parts)),
            pltpu.SemaphoreType.REGULAR((2, parts)),
        ]

    def copy(self, way, step, part):
        place = ring_place()
        rows = pl.ds(aligned(part * self.rows, self.rows), self.rows)
        return remote(
            self.sums.at[way, rows],
            self.land.at[lax.rem(step, self.slots), way, rows],
            self.send.at[step, way, part],
            self.recv.at[step, way, part],
            {"gy": ring_device(place + 1 - 2 * way)},
        )

    def owner(self, way, step):
        sign = 1 - 2 * way
        return ring_device(ring_place() - sign * (1 + step))

    @property
    def events(self):
        return self.count * self.parts

    def event(self, index):
        step, part = lax.div(index, self.parts), lax.rem(index, self.parts)
        last = self.count - 1
        tile = min(self.rows, 32)

        @pl.when(part == 0)
        def _():
            for way in range(2):
                self.product(way, step)

        for way in range(2):
            base = part * self.rows

            @pl.when(step >= 1)
            def _():
                self.copy(way, step - 1, part).wait_recv()
                slot = lax.rem(step - 1, self.slots)

                @pl.loop(0, self.rows // tile)
                def _(index):
                    rows = pl.ds(aligned(base + index * tile, tile), tile)
                    self.total[way, rows] += self.land[slot, way, rows].astype(WIDE)

                @pl.when(step - 1 + self.slots < last)
                def _():
                    upstream = ring_device(ring_place() - (1 - 2 * way))
                    pl.semaphore_signal(
                        self.credit.at[way, part],
                        inc=1,
                        device_id={"gy": upstream},
                        device_id_type=MESH,
                    )

            @pl.when(step < last)
            def _():
                @pl.when(step >= 1)
                def _():
                    self.copy(way, step - 1, part).wait_send()

                @pl.loop(0, self.rows // tile)
                def _(index):
                    rows = pl.ds(aligned(base + index * tile, tile), tile)
                    self.sums[way, rows] = self.total[way, rows].astype(LOW)

                @pl.when(step >= self.slots)
                def _():
                    pl.semaphore_wait(self.credit.at[way, part], 1)

                self.copy(way, step, part).start()

    def end(self):
        for part in range(self.parts):
            for way in range(2):
                self.copy(way, self.count - 2, part).wait_send()


class Reduce:
    def __init__(self, refs, core_land, cross_land, rows, width, scatter):
        (
            self.keep,
            self.core_send,
            self.core_stage,
            self.cross,
            self.cross_stage,
            self.raw,
            self.core_sems,
            self.cross_send_sems,
            self.cross_recv_sems,
            self.stage_sems,
        ) = refs
        self.core_land, self.cross_land = core_land, cross_land
        self.rows, self.width, self.scatter = rows, width, scatter
        self.chips = lax.axis_size("gx") // 2

    @staticmethod
    def scratch(rows, chunks, width, scatter):
        chips = lax.axis_size("gx") // 2
        half = chips * width
        part = width if scatter else half
        return [
            pltpu.VMEM((2, rows, half), LOW),
            pltpu.VMEM((2, rows, half), LOW),
            pltpu.VMEM((rows, half), LOW),
            pltpu.VMEM((LAG + 2, rows, half), LOW),
            pltpu.VMEM((chips - 1, rows, part), LOW),
            pltpu.VMEM((rows, part), WIDE),
            pltpu.SemaphoreType.DMA((2, chunks)),
            pltpu.SemaphoreType.DMA((chips - 1, chunks)),
            pltpu.SemaphoreType.DMA((chips - 1, chunks)),
            pltpu.SemaphoreType.DMA((chips,)),
        ]

    @staticmethod
    def landing(rows, chunks, width, scatter):
        chips = lax.axis_size("gx") // 2
        half = chips * width
        part = width if scatter else half
        return [
            jax.ShapeDtypeStruct((chunks, rows, half), LOW),
            jax.ShapeDtypeStruct((chips - 1, chunks, rows, part), LOW),
        ]

    def core_copy(self, chunk):
        return remote(
            self.core_send.at[lax.rem(chunk, 2)],
            self.core_land.at[chunk],
            self.core_sems.at[0, chunk],
            self.core_sems.at[1, chunk],
            {"gx": other_core()},
        )

    def cross_copy(self, shift, chunk):
        source = self.cross.at[lax.rem(chunk, LAG + 2)]
        if self.scatter:
            block = lax.rem(chip_here() + shift, self.chips)
            source = source.at[:, pl.ds(aligned(block * self.width, self.width), self.width)]
        return remote(
            source,
            self.cross_land.at[shift - 1, chunk],
            self.cross_send_sems.at[shift - 1, chunk],
            self.cross_recv_sems.at[shift - 1, chunk],
            {"gx": peer_at(shift)},
        )

    def produce(self, chunk, dot):
        @pl.when(chunk >= 2)
        def _():
            self.core_copy(chunk - 2).wait_send()

        slot = lax.rem(chunk, 2)
        core = core_here()
        for chip in range(self.chips):
            place = aligned((2 * chip + 1 - core) * self.width, self.width)
            self.core_send[slot, :, chip * self.width : (chip + 1) * self.width] = dot(
                place
            ).astype(LOW)
        self.core_copy(chunk).start()
        for chip in range(self.chips):
            place = aligned((2 * chip + core) * self.width, self.width)
            self.keep[slot, :, chip * self.width : (chip + 1) * self.width] = dot(
                place
            ).astype(LOW)

    def core_stage_copy(self, chunk):
        return pltpu.make_async_copy(
            self.core_land.at[chunk], self.core_stage, self.stage_sems.at[0]
        )

    def core_fetch(self, chunk):
        self.core_copy(chunk).wait_recv()
        self.core_stage_copy(chunk).start()

    def core_sum(self, chunk):
        slot, place = lax.rem(chunk, 2), lax.rem(chunk, LAG + 2)
        self.core_stage_copy(chunk).wait()

        @pl.when(chunk >= LAG + 2)
        def _():
            for shift in range(1, self.chips):
                self.cross_copy(shift, chunk - LAG - 2).wait_send()

        @pl.loop(0, self.rows // 32)
        def _(index):
            rows = pl.ds(aligned(index * 32, 32), 32)
            self.cross[place, rows] = (
                self.keep[slot, rows].astype(WIDE) + self.core_stage[rows].astype(WIDE)
            ).astype(LOW)

        for shift in range(1, self.chips):
            self.cross_copy(shift, chunk).start()

    def cross_stage_copy(self, shift, chunk):
        return pltpu.make_async_copy(
            self.cross_land.at[shift - 1, chunk],
            self.cross_stage.at[shift - 1],
            self.stage_sems.at[shift],
        )

    def cross_fetch(self, chunk):
        for shift in range(1, self.chips):
            self.cross_copy(shift, chunk).wait_recv()
            self.cross_stage_copy(shift, chunk).start()

    def cross_sum(self, chunk):
        place = lax.rem(chunk, LAG + 2)
        for shift in range(1, self.chips):
            self.cross_stage_copy(shift, chunk).wait()

        @pl.loop(0, self.rows // 32)
        def _(index):
            rows = pl.ds(aligned(index * 32, 32), 32)
            if self.scatter:
                block = pl.ds(aligned(chip_here() * self.width, self.width), self.width)
                total = self.cross[place, rows, block].astype(WIDE)
            else:
                total = self.cross[place, rows].astype(WIDE)
            for shift in range(1, self.chips):
                total = total + self.cross_stage[shift - 1, rows].astype(WIDE)
            self.raw[rows] = total

    def end(self, chunks):
        for chunk in (chunks - 2, chunks - 1):
            self.core_copy(chunk).wait_send()
        for chunk in range(chunks - LAG - 2, chunks):
            for shift in range(1, self.chips):
                self.cross_copy(shift, chunk).wait_send()


class Stats:
    def __init__(self, mine, land, sems):
        self.mine, self.land, self.sems = mine, land, sems

    @staticmethod
    def scratch(rows, chunks):
        return [
            pltpu.VMEM((2, rows, STATS), WIDE),
            pltpu.VMEM((chunks, rows, STATS), WIDE),
            pltpu.SemaphoreType.DMA((2, chunks)),
        ]

    def copy(self, chunk):
        return remote(
            self.mine.at[lax.rem(chunk, 2)],
            self.land.at[chunk],
            self.sems.at[0, chunk],
            self.sems.at[1, chunk],
            {"gx": other_core()},
        )

    def clear(self, chunk):
        @pl.when(chunk >= 2)
        def _():
            self.copy(chunk - 2).wait_send()

    def put(self, chunk, rows, first, second):
        lane = lax.broadcasted_iota(jnp.int32, (first.shape[0], STATS), 1)
        self.mine[lax.rem(chunk, 2), rows] = jnp.where(lane < STATS // 2, first, second)

    def get(self, chunk, rows):
        total = self.mine[lax.rem(chunk, 2), rows] + self.land[chunk, rows]
        return (total[:, :1], total[:, STATS // 2 : STATS // 2 + 1])

    def end(self, chunks):
        for chunk in (chunks - 2, chunks - 1):
            self.copy(chunk).wait_send()


class Spread:
    def __init__(self, buffer, whole, local, send, recv, rows, width):
        self.buffer, self.whole = buffer, whole
        self.local, self.send, self.recv = local, send, recv
        self.rows, self.width = rows, width
        self.chips = lax.axis_size("gx") // 2

    @staticmethod
    def scratch(rows, chunks, width):
        chips = lax.axis_size("gx") // 2
        return [
            pltpu.VMEM((2, rows, chips * width), LOW),
            pltpu.SemaphoreType.DMA((2, chips)),
            pltpu.SemaphoreType.DMA((chunks, chips)),
            pltpu.SemaphoreType.DMA((chunks, chips)),
        ]

    def pair(self, chunk, chip, core):
        slot = lax.rem(chunk, 2)
        source = self.buffer.at[slot, :, chip * self.width : (chip + 1) * self.width]
        rows = pl.ds(aligned(chunk * self.rows, self.rows), self.rows)
        columns = pl.ds(aligned((2 * chip + core) * self.width, self.width), self.width)
        target = self.whole.at[rows, columns]
        here = pltpu.make_async_copy(source, target, self.local.at[slot, chip])
        away = remote(
            source,
            target,
            self.send.at[chunk, chip],
            self.recv.at[chunk, chip],
            {"gx": other_core()},
        )
        return (here, away)

    def clear(self, chunk):
        @pl.when(chunk >= 2)
        def _():
            self.settle(chunk - 2)

    def settle(self, chunk):
        for chip in range(self.chips):
            here, away = self.pair(chunk, chip, core_here())
            here.wait()
            away.wait_send()

    def go(self, chunk):
        for chip in range(self.chips):
            here, away = self.pair(chunk, chip, core_here())
            here.start()
            away.start()

    def end(self, chunks):
        for chunk in (chunks - 2, chunks - 1):
            self.settle(chunk)

        def arrive(chunk):
            for chip in range(self.chips):
                self.pair(chunk, chip, 1 - core_here())[1].wait_recv()

        loop(chunks, arrive)


def row_slice(chunk, rows):
    return pl.ds(aligned(chunk * rows, rows), rows)


def core_columns(source, chunk, rows, width, buffer, sems, first):
    return [
        pltpu.make_async_copy(
            source.at[
                row_slice(chunk, rows),
                pl.ds(aligned((2 * chip + core_here()) * width, width), width),
            ],
            buffer.at[:, chip * width : (chip + 1) * width],
            sems.at[first + chip],
        )
        for chip in range(lax.axis_size("gx") // 2)
    ]


def tiles(rows, body):
    @pl.loop(0, rows // 32)
    def _(index):
        body(pl.ds(aligned(index * 32, 32), 32))


def schedule(chunks, reduce, multiply, fetch, sums, finish, event=None, events=0, prepare=None):
    steps = chunks + 2 + LAG

    def iteration(step):
        if event is not None:
            low = lax.div(step * events, steps)
            high = lax.div((step + 1) * events, steps)

            def some(index, carry):
                event(index)
                return carry

            lax.fori_loop(low, high, some, 0)

        @pl.when((step >= 1) & (step <= chunks))
        def _():
            reduce.core_fetch(step - 1)

        @pl.when((step >= 1 + LAG) & (step < chunks + 1 + LAG))
        def _():
            reduce.cross_fetch(step - 1 - LAG)

        @pl.when((step >= 1 + LAG) & (step < chunks + 2 + LAG))
        def _():
            fetch(step - 1 - LAG)

        @pl.when(step < chunks)
        def _():
            if prepare is not None:
                prepare(step)
            reduce.produce(step, lambda place: multiply(step, place))

        @pl.when((step >= 1) & (step <= chunks))
        def _():
            reduce.core_sum(step - 1)

        @pl.when((step >= 2 + LAG) & (step < chunks + 2 + LAG))
        def _():
            finish(step - 2 - LAG)

        @pl.when((step >= 1 + LAG) & (step < chunks + 1 + LAG))
        def _():
            reduce.cross_sum(step - 1 - LAG)
            sums(step - 1 - LAG)

    loop(steps, iteration)


def take(refs, counts):
    groups, start = [], 0
    for count in counts:
        groups.append(refs[start : start + count])
        start += count
    return groups


class Columns:
    def __init__(self, source, shard, left, turned, sem):
        self.source, self.shard = source, shard
        self.left, self.turned, self.sem = left, turned, sem

    @staticmethod
    def scratch(length, shard):
        return [
            pltpu.VMEM((length, shard), LOW),
            pltpu.VMEM((shard, length), LOW),
            pltpu.SemaphoreType.DMA((1,)),
        ]

    def copy(self, owner):
        at = pl.ds(aligned(owner * self.shard, self.shard), self.shard)
        return pltpu.make_async_copy(self.source.at[:, at], self.left, self.sem.at[0])

    def take(self, ring, way, step):
        self.copy(ring.owner(way, step)).wait()
        self.turned[...] = self.left[...].T
        if way == 0:
            self.copy(ring.owner(1, step)).start()
        else:

            @pl.when(step + 1 < ring.count)
            def _():
                self.copy(ring.owner(0, step + 1)).start()


def attn_out(
    attended, weight, gain, tokens, out_grad, gate_shard, up_shard, down_shard, collective
):
    length, width = attended.shape
    chips = lax.axis_size("gx") // 2
    half = chips * width
    count = lax.axis_size("gy")
    chunks = count
    rows = length // chunks
    hidden = gate_shard.shape[1]
    shard = gate_shard.shape[0]
    part_rows = shard // 2
    side = hidden // 2
    down_columns = down_shard.shape[1]

    groups = [
        Reduce.scratch(rows, chunks, width, False),
        Stats.scratch(rows, chunks),
        Spread.scratch(rows, chunks, width),
        RingGather.scratch(3),
        [
            pltpu.VMEM((rows, half), LOW),
            pltpu.VMEM((2, rows, half), WIDE),
            pltpu.VMEM((2, rows, half), LOW),
            pltpu.SemaphoreType.DMA((chips,)),
            pltpu.SemaphoreType.DMA((2,)),
            pltpu.SemaphoreType.DMA((2,)),
            pltpu.SemaphoreType.DMA((1,)),
            pltpu.SemaphoreType.DMA((chips - 1, chunks, 2)),
        ],
    ]

    def kernel(*refs):
        ins, outs, *scratch = take(refs, [8, 9] + [len(g) for g in groups])
        attended, weight, gain, tokens, out_grad, gate_shard, up_shard, down_shard = ins
        raw_out, mixed_out, low_out, gate_full, up_full, down_full, upstream = outs[:7]
        core_land, cross_land = outs[7:]
        reduce = Reduce(scratch[0], core_land, cross_land, rows, width, False)
        stats = Stats(*scratch[1])
        buffer, local, send, recv = scratch[2]
        spread = Spread(buffer, low_out, local, send, recv, rows, width)
        token_buf, mixed_buf, raw_buf = scratch[4][:3]
        token_sems, mixed_sems, raw_sems, own_sem, up_sems = scratch[4][3:]
        full = (gate_full, up_full)
        shards_here = (gate_shard, up_shard)

        def slot(way, owner, part):
            if part == 2:
                columns = pl.ds(aligned(owner * down_columns, down_columns), down_columns)
                return down_full.at[way * side : (way + 1) * side, columns]
            base = owner * shard + part * part_rows
            return full[way].at[pl.ds(aligned(base, part_rows), part_rows)]

        def source(way, part):
            if part == 2:
                return down_shard.at[way * side : (way + 1) * side]
            return shards_here[way].at[part * part_rows : (part + 1) * part_rows]

        ring = RingGather(source, slot, 3, *scratch[3])
        up_place = pl.ds(aligned(chip_here() * width, width), width)
        own = pltpu.make_async_copy(out_grad, upstream.at[:, up_place], own_sem.at[0])

        def crossings(chunk):
            at = row_slice(chunk, rows)
            return [
                remote(
                    out_grad.at[at],
                    upstream.at[at, up_place],
                    up_sems.at[shift - 1, chunk, 0],
                    up_sems.at[shift - 1, chunk, 1],
                    {"gx": peer_at(shift)},
                )
                for shift in range(1, chips)
            ]

        own.start()
        greet(True, True)
        ring.begin()

        def multiply(chunk, place):
            return jnp.dot(
                attended[row_slice(chunk, rows)],
                weight[:, pl.ds(place, width)],
                preferred_element_type=WIDE,
            )

        def prepare(chunk):
            for item in crossings(chunk):
                item.start()

        def token_copies(chunk):
            return core_columns(tokens, chunk, rows, width, token_buf, token_sems, 0)

        def fetch(chunk):
            @pl.when(chunk >= 1)
            def _():
                for item in token_copies(chunk - 1):
                    item.start()

        def mixed_copy(chunk):
            slot = lax.rem(chunk, 2)
            return pltpu.make_async_copy(
                mixed_buf.at[slot, :, pl.ds(aligned(chip_here() * width, width), width)],
                mixed_out.at[row_slice(chunk, rows)],
                mixed_sems.at[slot],
            )

        def raw_copy(chunk):
            slot = lax.rem(chunk, 2)
            return pltpu.make_async_copy(
                raw_buf.at[slot], raw_out.at[row_slice(chunk, rows)], raw_sems.at[slot]
            )

        def sums(chunk):
            stats.clear(chunk)

            @pl.when(chunk >= 2)
            def _():
                raw_copy(chunk - 2).wait()

            def tile(at):
                raw = reduce.raw[at]
                raw_buf[lax.rem(chunk, 2), at] = raw.astype(LOW)
                squares = jnp.sum(raw * raw, axis=1, keepdims=True)
                stats.put(chunk, at, squares, squares)

            tiles(rows, tile)
            stats.copy(chunk).start()
            raw_copy(chunk).start()

        def finish(chunk):
            slot = lax.rem(chunk, 2)
            for item in token_copies(chunk):
                item.wait()
            stats.copy(chunk).wait_recv()
            spread.clear(chunk)

            @pl.when(chunk >= 2)
            def _():
                mixed_copy(chunk - 2).wait()

            def tile(at):
                squares, _ = stats.get(chunk, at)
                factor = lax.rsqrt(squares / D + EPS)
                mixed = token_buf[at].astype(WIDE) + reduce.raw[at] * factor * gain[...]
                mixed_buf[slot, at] = mixed
                spread.buffer[slot, at] = mixed.astype(LOW)

            tiles(rows, tile)
            spread.go(chunk)
            mixed_copy(chunk).start()

        schedule(chunks, reduce, multiply, fetch, sums, finish, ring.event, ring.events, prepare)
        ring.end()
        own.wait()

        def drain(chunk):
            for item in crossings(chunk):
                item.wait()

        loop(chunks, drain)
        reduce.end(chunks)
        stats.end(chunks)
        spread.end(chunks)
        for chunk in (chunks - 2, chunks - 1):
            mixed_copy(chunk).wait()
            raw_copy(chunk).wait()

    shape = jax.ShapeDtypeStruct
    out = pl.pallas_call(
        kernel,
        out_shape=[
            shape((length, half), LOW),
            shape((length, width), WIDE),
            shape((length, D), LOW),
            shape((shard * count, hidden), LOW),
            shape((shard * count, hidden), LOW),
            shape((hidden, down_columns * count), LOW),
            shape((length, half), LOW),
        ]
        + Reduce.landing(rows, chunks, width, False),
        in_specs=[VMEM, VMEM, VMEM, HBM, HBM, HBM, HBM, HBM],
        out_specs=[HBM] * 9,
        scratch_shapes=[item for group in groups for item in group],
        compiler_params=pltpu.CompilerParams(
            collective_id=collective, has_side_effects=True, vmem_limit_bytes=60 * MIB
        ),
        cost_estimate=pl.CostEstimate(
            flops=2 * length * width * D, bytes_accessed=8 * length * D, transcendentals=0
        ),
    )(attended, weight, gain, tokens, out_grad, gate_shard, up_shard, down_shard)
    return out[:7]


def mlp_forward(inputs, gate_full, up_full, down_full, gain, mixed, upstream, collective):
    length, inner = inputs.shape[0], gate_full.shape[1]
    width = mixed.shape[1]
    chips = lax.axis_size("gx") // 2
    half = chips * width
    chunks = lax.axis_size("gy")
    rows = length // chunks
    tile = min(512, inner)
    pieces = inner // tile

    groups = [
        Reduce.scratch(rows, chunks, width, False),
        Stats.scratch(rows, chunks),
        Spread.scratch(rows, chunks, width),
        [
            pltpu.VMEM((2, rows, half), LOW),
            pltpu.VMEM((rows, width), WIDE),
            pltpu.VMEM((2, rows, width), LOW),
            pltpu.SemaphoreType.DMA((2,)),
            pltpu.SemaphoreType.DMA((1,)),
            pltpu.SemaphoreType.DMA((2,)),
        ],
        [
            pltpu.VMEM((D, inner), LOW),
            pltpu.VMEM((D, inner), LOW),
            pltpu.VMEM((inner, D), LOW),
            pltpu.VMEM((2, rows, D), LOW),
            pltpu.VMEM((2, 3, rows, inner), LOW),
            pltpu.SemaphoreType.DMA((pieces, 2)),
            pltpu.SemaphoreType.DMA((1,)),
            pltpu.SemaphoreType.DMA((2,)),
            pltpu.SemaphoreType.DMA((2, 3)),
        ],
    ]

    def kernel(*refs):
        ins, outs, *scratch = take(refs, [7, 8] + [len(g) for g in groups])
        inputs, gate_full, up_full, down_full, gain, mixed, upstream = ins
        result, grad_out, gain_grad, hidden_out, gate_out, up_out, core_land, cross_land = outs
        gate_weight, up_weight, weight, row_buf, made = scratch[4][:5]
        piece_sems, weight_sem, row_sems, made_sems = scratch[4][5:]
        reduce = Reduce(scratch[0], core_land, cross_land, rows, width, False)
        stats = Stats(*scratch[1])
        buffer, local, send, recv = scratch[2]
        spread = Spread(buffer, grad_out, local, send, recv, rows, width)
        up_buf, mixed_buf, result_buf, up_sems, mixed_sems, result_sems = scratch[3]

        def piece_copies(piece):
            at = pl.ds(aligned(piece * tile, tile), tile)
            return [
                pltpu.make_async_copy(gate_full.at[:, at], gate_weight.at[:, at], piece_sems.at[piece, 0]),
                pltpu.make_async_copy(up_full.at[:, at], up_weight.at[:, at], piece_sems.at[piece, 1]),
            ]

        weight_copy = pltpu.make_async_copy(down_full, weight, weight_sem.at[0])

        def row_copy(chunk):
            slot = lax.rem(chunk, 2)
            return pltpu.make_async_copy(
                inputs.at[row_slice(chunk, rows)], row_buf.at[slot], row_sems.at[slot]
            )

        def stores(chunk):
            slot, at = lax.rem(chunk, 2), row_slice(chunk, rows)
            return [
                pltpu.make_async_copy(made.at[slot, which], out.at[at], made_sems.at[slot, which])
                for which, out in enumerate((hidden_out, gate_out, up_out))
            ]

        row_copy(0).start()
        for piece in range(pieces):
            for item in piece_copies(piece):
                item.start()
        weight_copy.start()
        greet(True, False)
        gain_grad[...] = jnp.zeros_like(gain_grad)

        def prepare(chunk):
            slot = lax.rem(chunk, 2)
            row_copy(chunk).wait()

            @pl.when(chunk + 1 < chunks)
            def _():
                row_copy(chunk + 1).start()

            @pl.when(chunk >= 2)
            def _():
                for item in stores(chunk - 2):
                    item.wait()

            @pl.loop(0, pieces)
            def _(piece):
                @pl.when(chunk == 0)
                def _():
                    for item in piece_copies(piece):
                        item.wait()

                at = pl.ds(aligned(piece * tile, tile), tile)
                gate = jnp.dot(row_buf[slot], gate_weight[:, at], preferred_element_type=WIDE)
                up = jnp.dot(row_buf[slot], up_weight[:, at], preferred_element_type=WIDE)
                made[slot, 0, :, at] = (gate * jax.nn.sigmoid(gate) * up).astype(LOW)
                made[slot, 1, :, at] = gate.astype(LOW)
                made[slot, 2, :, at] = up.astype(LOW)

            @pl.when(chunk == 0)
            def _():
                weight_copy.wait()

            for item in stores(chunk):
                item.start()

        def multiply(chunk, place):
            return jnp.dot(
                made[lax.rem(chunk, 2), 0],
                weight[:, pl.ds(place, width)],
                preferred_element_type=WIDE,
            )

        def up_copy(chunk):
            slot = lax.rem(chunk, 2)
            return pltpu.make_async_copy(
                upstream.at[row_slice(chunk, rows)], up_buf.at[slot], up_sems.at[slot]
            )

        def mixed_copy(chunk):
            return pltpu.make_async_copy(
                mixed.at[row_slice(chunk, rows)], mixed_buf, mixed_sems.at[0]
            )

        def result_copy(chunk):
            slot = lax.rem(chunk, 2)
            return pltpu.make_async_copy(
                result_buf.at[slot], result.at[row_slice(chunk, rows)], result_sems.at[slot]
            )

        def fetch(chunk):
            @pl.when(chunk < chunks)
            def _():
                up_copy(chunk).start()

            @pl.when(chunk >= 1)
            def _():
                mixed_copy(chunk - 1).start()

        def sums(chunk):
            slot = lax.rem(chunk, 2)
            stats.clear(chunk)
            up_copy(chunk).wait()

            def tile(at):
                raw = reduce.raw[at]
                up = up_buf[slot, at].astype(WIDE)
                squares = jnp.sum(raw * raw, axis=1, keepdims=True)
                projected = jnp.sum(gain[...] * up * raw, axis=1, keepdims=True)
                stats.put(chunk, at, squares, projected)

            tiles(rows, tile)
            stats.copy(chunk).start()

        def finish(chunk):
            slot = lax.rem(chunk, 2)
            mixed_copy(chunk).wait()
            stats.copy(chunk).wait_recv()
            spread.clear(chunk)

            @pl.when(chunk >= 2)
            def _():
                result_copy(chunk - 2).wait()

            block = pl.ds(aligned(chip_here() * width, width), width)

            def tile(at):
                squares, projected = stats.get(chunk, at)
                factor = lax.rsqrt(squares / D + EPS)
                raw = reduce.raw[at]
                up = up_buf[slot, at].astype(WIDE)
                spread.buffer[slot, at] = (
                    factor * gain[...] * up - raw * (factor * factor * factor * projected / D)
                ).astype(LOW)
                gain_grad[...] += jnp.sum(up * raw * factor, axis=0, keepdims=True)
                result_buf[slot, at] = (
                    mixed_buf[at] + reduce.raw[at, block] * factor * gain[:, block]
                ).astype(LOW)

            tiles(rows, tile)
            spread.go(chunk)
            result_copy(chunk).start()

        schedule(chunks, reduce, multiply, fetch, sums, finish, prepare=prepare)
        reduce.end(chunks)
        stats.end(chunks)
        spread.end(chunks)
        for chunk in (chunks - 2, chunks - 1):
            result_copy(chunk).wait()
            for item in stores(chunk):
                item.wait()

    shape = jax.ShapeDtypeStruct
    out = pl.pallas_call(
        kernel,
        out_shape=[
            shape((length, width), LOW),
            shape((length, D), LOW),
            shape((1, half), WIDE),
            shape((length, inner), LOW),
            shape((length, inner), LOW),
            shape((length, inner), LOW),
        ]
        + Reduce.landing(rows, chunks, width, False),
        in_specs=[HBM] * 4 + [VMEM, HBM, HBM],
        out_specs=[HBM, HBM, VMEM] + [HBM] * 5,
        scratch_shapes=[item for group in groups for item in group],
        compiler_params=pltpu.CompilerParams(
            collective_id=collective, has_side_effects=True, vmem_limit_bytes=60 * MIB
        ),
        cost_estimate=pl.CostEstimate(
            flops=6 * length * inner * D, bytes_accessed=16 * length * D, transcendentals=0
        ),
    )(inputs, gate_full, up_full, down_full, gain, mixed, upstream)
    return out[:6]


def mlp_back(gate_grad, up_grad, gate_full, up_full, inputs, gain, upstream, attn_raw, collective):
    length, inner = gate_grad.shape
    half = attn_raw.shape[1]
    chips = lax.axis_size("gx") // 2
    width = half // chips
    count = lax.axis_size("gy")
    chunks = count
    rows = length // chunks
    shard = D // count
    slots, parts = 2, 2

    groups = [
        Reduce.scratch(rows, chunks, width, False),
        Stats.scratch(rows, chunks),
        Spread.scratch(rows, chunks, width),
        RingScatter.scratch(shard, inner, slots, parts),
        [
            pltpu.VMEM((rows, half), LOW),
            pltpu.VMEM((2, rows, half), LOW),
            pltpu.SemaphoreType.DMA((1,)),
            pltpu.SemaphoreType.DMA((2,)),
            pltpu.SemaphoreType.DMA((1,)),
            pltpu.SemaphoreType.DMA((2,)),
        ],
        Columns.scratch(length, shard),
    ]

    def kernel(*refs):
        ins, outs, *scratch = take(refs, [8, 7] + [len(g) for g in groups])
        gate_grad, up_grad, gate_full, up_full, inputs, gain, upstream, attn_raw = ins
        mixed_out, grad_out, gain_grad, gate_out, up_out, core_land, cross_land = outs
        reduce = Reduce(scratch[0], core_land, cross_land, rows, width, False)
        stats = Stats(*scratch[1])
        buffer, local, send, recv = scratch[2]
        spread = Spread(buffer, grad_out, local, send, recv, rows, width)
        total, summed, land, ring_send, ring_recv, credit = scratch[3]
        up_buf, raw_buf, up_sems, raw_sems, mixed_sems, out_sems = scratch[4]
        left = Columns(inputs, shard, *scratch[5])
        grads = (gate_grad, up_grad)

        def product(way, step):
            left.take(ring, way, step)
            tile = 512

            @pl.loop(0, inner // tile)
            def _(index):
                columns = pl.ds(aligned(index * tile, tile), tile)
                total[way, :, columns] = jnp.dot(
                    left.turned[...], grads[way][:, columns], preferred_element_type=WIDE
                )

        ring = RingScatter(
            product, total, summed, land, ring_send, ring_recv, credit, slots, parts
        )
        left.copy(ring.owner(0, 0)).start()
        greet(True, True)
        gain_grad[...] = jnp.zeros_like(gain_grad)

        def multiply(chunk, place):
            at = row_slice(chunk, rows)
            return lax.dot_general(
                gate_grad[at],
                gate_full[pl.ds(place, width)],
                (((1,), (1,)), ((), ())),
                preferred_element_type=WIDE,
            ) + lax.dot_general(
                up_grad[at],
                up_full[pl.ds(place, width)],
                (((1,), (1,)), ((), ())),
                preferred_element_type=WIDE,
            )

        def up_copy(chunk):
            return pltpu.make_async_copy(
                upstream.at[row_slice(chunk, rows)], up_buf, up_sems.at[0]
            )

        def raw_copy(chunk):
            slot = lax.rem(chunk, 2)
            return pltpu.make_async_copy(
                attn_raw.at[row_slice(chunk, rows)], raw_buf.at[slot], raw_sems.at[slot]
            )

        def mixed_copy(chunk):
            return pltpu.make_async_copy(
                reduce.raw.at[:, pl.ds(aligned(chip_here() * width, width), width)],
                mixed_out.at[row_slice(chunk, rows)],
                mixed_sems.at[0],
            )

        def fetch(chunk):
            @pl.when(chunk < chunks)
            def _():
                up_copy(chunk).start()
                raw_copy(chunk).start()

        def sums(chunk):
            slot = lax.rem(chunk, 2)
            stats.clear(chunk)
            up_copy(chunk).wait()
            raw_copy(chunk).wait()

            def tile(at):
                upward = reduce.raw[at] + up_buf[at].astype(WIDE)
                reduce.raw[at] = upward
                raw = raw_buf[slot, at].astype(WIDE)
                squares = jnp.sum(raw * raw, axis=1, keepdims=True)
                projected = jnp.sum(gain[...] * upward * raw, axis=1, keepdims=True)
                stats.put(chunk, at, squares, projected)

            tiles(rows, tile)
            stats.copy(chunk).start()
            mixed_copy(chunk).start()

        def finish(chunk):
            slot = lax.rem(chunk, 2)
            stats.copy(chunk).wait_recv()
            spread.clear(chunk)

            def tile(at):
                squares, projected = stats.get(chunk, at)
                factor = lax.rsqrt(squares / D + EPS)
                upward = reduce.raw[at]
                raw = raw_buf[slot, at].astype(WIDE)
                spread.buffer[slot, at] = (
                    factor * gain[...] * upward
                    - raw * (factor * factor * factor * projected / D)
                ).astype(LOW)
                gain_grad[...] += jnp.sum(upward * raw * factor, axis=0, keepdims=True)

            tiles(rows, tile)
            spread.go(chunk)
            mixed_copy(chunk).wait()

        schedule(chunks, reduce, multiply, fetch, sums, finish, ring.event, ring.events)
        writes = [
            pltpu.make_async_copy(total.at[way], (gate_out, up_out)[way], out_sems.at[way])
            for way in range(2)
        ]
        for item in writes:
            item.start()
        ring.end()
        reduce.end(chunks)
        stats.end(chunks)
        spread.end(chunks)
        for item in writes:
            item.wait()

    shape = jax.ShapeDtypeStruct
    out = pl.pallas_call(
        kernel,
        out_shape=[
            shape((length, width), WIDE),
            shape((length, D), LOW),
            shape((1, half), WIDE),
            shape((shard, inner), WIDE),
            shape((shard, inner), WIDE),
        ]
        + Reduce.landing(rows, chunks, width, False),
        in_specs=[VMEM, VMEM, VMEM, VMEM, HBM, VMEM, HBM, HBM],
        out_specs=[HBM, HBM, VMEM, HBM, HBM, HBM, HBM],
        scratch_shapes=[item for group in groups for item in group],
        compiler_params=pltpu.CompilerParams(
            collective_id=collective, has_side_effects=True, vmem_limit_bytes=60 * MIB
        ),
        cost_estimate=pl.CostEstimate(
            flops=8 * length * inner * D, bytes_accessed=16 * length * D, transcendentals=0
        ),
    )(gate_grad, up_grad, gate_full, up_full, inputs, gain, upstream, attn_raw)
    return out[:5]


class Total:
    def __init__(self, land, send, recv):
        self.land, self.send, self.recv = land, send, recv
        self.count = lax.axis_size("gx")

    @staticmethod
    def scratch(length):
        others = lax.axis_size("gx") - 1
        return [
            pltpu.VMEM((others, 8, length), WIDE),
            pltpu.SemaphoreType.DMA((others,)),
            pltpu.SemaphoreType.DMA((others,)),
        ]

    def copies(self, mine):
        return [
            remote(
                mine,
                self.land.at[shift - 1],
                self.send.at[shift - 1],
                self.recv.at[shift - 1],
                {"gx": rank_at(shift)},
            )
            for shift in range(1, self.count)
        ]

    def start(self, mine):
        for item in self.copies(mine):
            item.start()

    def finish(self, mine):
        for item in self.copies(mine):
            item.wait()
        total = mine[...]
        for shift in range(1, self.count):
            total = total + self.land[shift - 1]
        return total


def gather_in(tokens, stack, gains, collective):
    length, width = tokens.shape
    shard, columns = stack.shape
    count = lax.axis_size("gy")
    chunks = count
    rows = length // chunks
    chips = lax.axis_size("gx") // 2
    side = columns // 2
    parts = 1

    groups = [
        RingGather.scratch(parts),
        [
            pltpu.SemaphoreType.DMA((1,)),
            pltpu.SemaphoreType.DMA((2,)),
            pltpu.SemaphoreType.DMA((chips - 1, chunks, 2)),
            pltpu.SemaphoreType.DMA((chips - 1, chunks, 2)),
        ],
        [
            pltpu.VMEM((D, columns), LOW),
            pltpu.VMEM((2, rows, D), LOW),
            pltpu.VMEM((2, 2, rows, width), WIDE),
            pltpu.VMEM((2, rows, width), LOW),
            pltpu.VMEM((length, STATS), WIDE),
            pltpu.VMEM((8, length), WIDE),
            pltpu.SemaphoreType.DMA((1,)),
            pltpu.SemaphoreType.DMA((2,)),
            pltpu.SemaphoreType.DMA((2, 3)),
        ],
        Total.scratch(length),
        [
            pltpu.VMEM((chips - 1, 8, width), WIDE),
            pltpu.SemaphoreType.DMA((chips - 1, 2)),
        ],
    ]

    def kernel(*refs):
        ins, outs, *scratch = take(refs, [3, 7] + [len(g) for g in groups])
        tokens, stack, gains = ins
        whole, full, query_raw, key_raw, values, squares, halves = outs
        gain_land, gain_sems = scratch[4]
        own_sem, core_sems, cross_sems, pass_sems = scratch[1]
        weight, row_buf, raw_buf, value_buf, stats, mine = scratch[2][:6]
        weight_sem, row_sems, out_sems = scratch[2][6:]
        total = Total(*scratch[3])

        def slot(way, owner, part):
            return full.at[
                pl.ds(aligned(owner * shard, shard), shard), way * side : (way + 1) * side
            ]

        def source(way, part):
            return stack.at[:, way * side : (way + 1) * side]

        ring = RingGather(source, slot, parts, *scratch[0])

        def block(rank, chunk):
            at = pl.ds(aligned(rank * width, width), width)
            if chunk is None:
                return whole.at[:, at]
            return whole.at[row_slice(chunk, rows), at]

        here = lax.axis_index("gx")
        own = pltpu.make_async_copy(tokens, block(here, None), own_sem.at[0])
        core = remote(
            tokens, block(here, None), core_sems.at[0], core_sems.at[1], {"gx": other_core()}
        )

        def cross(shift, chunk):
            return remote(
                tokens.at[row_slice(chunk, rows)],
                block(here, chunk),
                cross_sems.at[shift - 1, chunk, 0],
                cross_sems.at[shift - 1, chunk, 1],
                {"gx": peer_at(shift)},
            )

        def onward(shift, chunk):
            spot = block(peer_at(chips - shift), chunk)
            return remote(
                spot,
                spot,
                pass_sems.at[shift - 1, chunk, 0],
                pass_sems.at[shift - 1, chunk, 1],
                {"gx": other_core()},
            )

        gain_copies = [
            remote(
                gains,
                gain_land.at[shift - 1],
                gain_sems.at[shift - 1, 0],
                gain_sems.at[shift - 1, 1],
                {"gx": peer_at(shift)},
            )
            for shift in range(1, chips)
        ]
        own.start()
        greet("all", True)
        for item in gain_copies:
            item.start()
        ring.begin()

        def send(chunk):
            for shift in range(1, chips):
                cross(shift, chunk).start()

        loop(chunks, send)
        core.start()

        def step(chunk):
            for shift in range(1, chips):
                cross(shift, chunk).wait_recv()
                onward(shift, chunk).start()

            @pl.when(chunk < ring.events)
            def _():
                ring.event(chunk)

        loop(chunks, step)
        ring.end()
        fetch = pltpu.make_async_copy(full, weight, weight_sem.at[0])
        fetch.start()

        def drain(chunk):
            for shift in range(1, chips):
                cross(shift, chunk).wait_send()
                onward(shift, chunk).wait()

        loop(chunks, drain)
        own.wait()
        core.wait()

        def row_copy(chunk):
            slot = lax.rem(chunk, 2)
            return pltpu.make_async_copy(
                whole.at[row_slice(chunk, rows)], row_buf.at[slot], row_sems.at[slot]
            )

        def stores(chunk):
            slot, at = lax.rem(chunk, 2), row_slice(chunk, rows)
            return [
                pltpu.make_async_copy(raw_buf.at[slot, 0], query_raw.at[at], out_sems.at[slot, 0]),
                pltpu.make_async_copy(raw_buf.at[slot, 1], key_raw.at[at], out_sems.at[slot, 1]),
                pltpu.make_async_copy(value_buf.at[slot], values.at[at], out_sems.at[slot, 2]),
            ]

        row_copy(0).start()
        fetch.wait()
        lane = lax.broadcasted_iota(jnp.int32, (rows, STATS), 1)

        def project(chunk):
            slot = lax.rem(chunk, 2)
            row_copy(chunk).wait()

            @pl.when(chunk + 1 < chunks)
            def _():
                row_copy(chunk + 1).start()

            @pl.when(chunk >= 2)
            def _():
                for item in stores(chunk - 2):
                    item.wait()

            some = []
            for which in range(2):
                raw = jnp.dot(
                    row_buf[slot],
                    weight[:, which * width : (which + 1) * width],
                    preferred_element_type=WIDE,
                )
                raw_buf[slot, which] = raw
                some.append(jnp.sum(raw * raw, axis=1, keepdims=True))
            value_buf[slot] = jnp.dot(
                row_buf[slot], weight[:, 2 * width :], preferred_element_type=WIDE
            ).astype(LOW)
            stats[row_slice(chunk, rows)] = jnp.where(lane == 0, some[0], some[1])
            for item in stores(chunk):
                item.start()

        loop(chunks, project)
        mine[...] = stats[...].T[:8]
        total.start(mine)
        for chunk in (chunks - 2, chunks - 1):
            for item in stores(chunk):
                item.wait()
        squares[...] = total.finish(mine)
        halves[:, pl.ds(aligned(chip_here() * width, width), width)] = gains[...]
        for shift in range(1, chips):
            gain_copies[shift - 1].wait()
            chip = lax.rem(chip_here() + chips - shift, chips)
            halves[:, pl.ds(aligned(chip * width, width), width)] = gain_land[shift - 1]

    shape = jax.ShapeDtypeStruct
    return pl.pallas_call(
        kernel,
        out_shape=[
            shape((length, D), LOW),
            shape((shard * count, columns), LOW),
            shape((length, width), WIDE),
            shape((length, width), WIDE),
            shape((length, width), LOW),
            shape((8, length), WIDE),
            shape((8, chips * width), WIDE),
        ],
        in_specs=[HBM, HBM, VMEM],
        out_specs=[HBM] * 5 + [VMEM, VMEM],
        scratch_shapes=[item for group in groups for item in group],
        compiler_params=pltpu.CompilerParams(
            collective_id=collective, has_side_effects=True, vmem_limit_bytes=40 * MIB
        ),
        cost_estimate=pl.CostEstimate(
            flops=2 * length * columns * D, bytes_accessed=8 * length * D, transcendentals=0
        ),
    )(tokens, stack, gains)


def hidden_back(grad, weight, hidden, gate, up, collective):
    length, inner = hidden.shape
    count = lax.axis_size("gy")
    chunks = count
    rows = length // chunks
    shard = D // count
    side = inner // 2
    slots, parts = count - 1, 2
    tile = min(512, inner)

    groups = [
        RingScatter.scratch(shard, side, slots, parts),
        [
            pltpu.VMEM((2, 2, rows, inner), LOW),
            pltpu.VMEM((2, 2, rows, inner), LOW),
            pltpu.SemaphoreType.DMA((2, 2)),
            pltpu.SemaphoreType.DMA((2, 2)),
            pltpu.SemaphoreType.DMA((2,)),
            pltpu.VMEM((shard, length), LOW),
        ],
    ]

    def kernel(*refs):
        ins, outs, *scratch = take(refs, [5, 3] + [len(g) for g in groups])
        grad, weight, hidden, gate, up = ins
        gate_grad, up_grad, weight_grad = outs
        total, summed, land, ring_send, ring_recv, credit = scratch[0]
        given, made, given_sems, made_sems, out_sems, turned = scratch[1]

        def product(way, step):
            columns = pl.ds(aligned(ring.owner(way, step) * shard, shard), shard)
            turned[...] = grad[:, columns].T
            size = min(512, side)

            @pl.loop(0, side // size)
            def _(index):
                at = pl.ds(aligned(index * size, size), size)
                take_at = pl.ds(aligned(way * side + index * size, size), size)
                total[way, :, at] = jnp.dot(
                    turned[...], hidden[:, take_at], preferred_element_type=WIDE
                )

        ring = RingScatter(
            product, total, summed, land, ring_send, ring_recv, credit, slots, parts
        )

        def load(chunk):
            slot = lax.rem(chunk, 2)
            return [
                pltpu.make_async_copy(
                    (gate, up)[which].at[row_slice(chunk, rows)],
                    given.at[slot, which],
                    given_sems.at[slot, which],
                )
                for which in range(2)
            ]

        def store(chunk):
            slot = lax.rem(chunk, 2)
            return [
                pltpu.make_async_copy(
                    made.at[slot, which],
                    (gate_grad, up_grad)[which].at[row_slice(chunk, rows)],
                    made_sems.at[slot, which],
                )
                for which in range(2)
            ]

        for item in load(0):
            item.start()
        greet(False, True)

        def iteration(step):
            slot = lax.rem(step, 2)
            for part in range(parts):
                ring.event(step * parts + part)

            @pl.when(step + 1 < chunks)
            def _():
                for item in load(step + 1):
                    item.start()

            @pl.when(step >= 2)
            def _():
                for item in store(step - 2):
                    item.wait()

            for item in load(step):
                item.wait()

            @pl.loop(0, inner // tile)
            def _(index):
                at = pl.ds(aligned(index * tile, tile), tile)
                hidden_grad = lax.dot_general(
                    grad[row_slice(step, rows)],
                    weight[at],
                    (((1,), (1,)), ((), ())),
                    preferred_element_type=WIDE,
                )
                gate = given[slot, 0, :, at].astype(WIDE)
                up = given[slot, 1, :, at].astype(WIDE)
                sigma = jax.nn.sigmoid(gate)
                made[slot, 0, :, at] = (
                    hidden_grad * up * sigma * (1.0 + gate * (1.0 - sigma))
                ).astype(LOW)
                made[slot, 1, :, at] = (hidden_grad * gate * sigma).astype(LOW)

            for item in store(step):
                item.start()

        loop(chunks, iteration)
        writes = [
            pltpu.make_async_copy(
                total.at[way], weight_grad.at[:, way * side : (way + 1) * side], out_sems.at[way]
            )
            for way in range(2)
        ]
        for item in writes:
            item.start()
        for chunk in (chunks - 2, chunks - 1):
            for item in store(chunk):
                item.wait()
        ring.end()
        for item in writes:
            item.wait()

    shape = jax.ShapeDtypeStruct
    return pl.pallas_call(
        kernel,
        out_shape=[
            shape((length, inner), LOW),
            shape((length, inner), LOW),
            shape((shard, inner), WIDE),
        ],
        in_specs=[VMEM, VMEM, VMEM, HBM, HBM],
        out_specs=[HBM, HBM, HBM],
        scratch_shapes=[item for group in groups for item in group],
        compiler_params=pltpu.CompilerParams(
            collective_id=collective, has_side_effects=True, vmem_limit_bytes=60 * MIB
        ),
        cost_estimate=pl.CostEstimate(
            flops=4 * length * inner * D, bytes_accessed=16 * length * D, transcendentals=0
        ),
    )(grad, weight, hidden, gate, up)


def attn_in_back(
    query_back,
    key_back,
    value_grad,
    query_raw,
    key_raw,
    factors,
    projections,
    query_gain,
    key_gain,
    stack,
    inputs,
    mixed_grad,
    gain_parts,
    collective,
):
    length, columns = value_grad.shape[0], stack.shape[1]
    width = mixed_grad.shape[1]
    count = lax.axis_size("gy")
    chunks = count
    rows = length // chunks
    shard = D // count
    side = columns // 2
    slots, parts = count - 1, 2
    tile = 256 if side % 256 == 0 else 128

    groups = [
        Reduce.scratch(rows, chunks, width, True),
        RingScatter.scratch(shard, side, slots, parts),
        [
            pltpu.VMEM((rows, width), WIDE),
            pltpu.VMEM((2, rows, width), WIDE),
            pltpu.VMEM((length, columns), LOW),
            pltpu.VMEM((length, STATS), WIDE),
            pltpu.SemaphoreType.DMA((1,)),
            pltpu.SemaphoreType.DMA((2,)),
            pltpu.SemaphoreType.DMA((2,)),
        ],
        Columns.scratch(length, shard),
        Total.scratch(length),
        [
            pltpu.VMEM((8, width), WIDE),
            pltpu.VMEM((count - 1, 8, width), WIDE),
            pltpu.SemaphoreType.DMA((count - 1, 2)),
        ],
    ]

    def kernel(*refs):
        ins, outs, *scratch = take(refs, [16, 5] + [len(g) for g in groups])
        query_back, key_back, value_grad, query_raw, key_raw, factors = ins[:6]
        projections, query_gain, key_gain, stack, inputs, mixed_grad = ins[6:12]
        gain_parts = ins[12:]
        token_grad, weight_grad, gain_grads, core_land, cross_land = outs
        gain_mine, gain_land, gain_sems = scratch[5]
        reduce = Reduce(scratch[0], core_land, cross_land, rows, width, True)
        total, summed, land, ring_send, ring_recv, credit = scratch[1]
        mixed_buf, token_buf, grads, projected, mixed_sems, token_sems, out_sems = scratch[2]
        left = Columns(inputs, shard, *scratch[3])
        total_sum = Total(*scratch[4])

        def product(way, step):
            left.take(ring, way, step)

            @pl.loop(0, side // tile)
            def _(index):
                at = pl.ds(aligned(index * tile, tile), tile)
                take_at = pl.ds(aligned(way * side + index * tile, tile), tile)
                total[way, :, at] = jnp.dot(
                    left.turned[...], grads[:, take_at], preferred_element_type=WIDE
                )

        ring = RingScatter(
            product, total, summed, land, ring_send, ring_recv, credit, slots, parts
        )
        left.copy(ring.owner(0, 0)).start()
        chip_columns = pl.ds(aligned(chip_here() * width, width), width)
        gain_mine[...] = jnp.zeros_like(gain_mine)
        for which, part in enumerate(gain_parts):
            gain_mine[which : which + 1] = part[...] if which < 2 else part[:, chip_columns]
        greet("all", False, True)
        total_sum.start(projections)
        gain_copies = [
            remote(
                gain_mine,
                gain_land.at[shift - 1],
                gain_sems.at[shift - 1, 0],
                gain_sems.at[shift - 1, 1],
                {"gy": block_at(shift)},
            )
            for shift in range(1, count)
        ]
        for item in gain_copies:
            item.start()
        grads[:, 2 * width :] = value_grad[...]
        sums_here = total_sum.finish(projections)
        projected[...] = jnp.concatenate([sums_here] * (STATS // 8), axis=0).T
        pairs = ((query_back, query_raw, query_gain), (key_back, key_raw, key_gain))

        @pl.loop(0, length // 32)
        def _(index):
            at = row_slice(index, 32)
            for which, (back, raw, gain) in enumerate(pairs):
                factor = factors[at, which : which + 1]
                pull = factor * factor * factor * projected[at, which : which + 1] / D
                grads[at, which * width : (which + 1) * width] = (
                    factor * gain[...] * back[at] - raw[at] * pull
                ).astype(LOW)

        def multiply(chunk, place):
            return lax.dot_general(
                grads[row_slice(chunk, rows)],
                stack[pl.ds(place, width)],
                (((1,), (1,)), ((), ())),
                preferred_element_type=WIDE,
            )

        def mixed_copy(chunk):
            return pltpu.make_async_copy(
                mixed_grad.at[row_slice(chunk, rows)], mixed_buf, mixed_sems.at[0]
            )

        def token_copy(chunk):
            slot = lax.rem(chunk, 2)
            return pltpu.make_async_copy(
                token_buf.at[slot], token_grad.at[row_slice(chunk, rows)], token_sems.at[slot]
            )

        def fetch(chunk):
            @pl.when(chunk >= 1)
            def _():
                mixed_copy(chunk - 1).start()

        def sums(chunk):
            pass

        def finish(chunk):
            slot = lax.rem(chunk, 2)
            mixed_copy(chunk).wait()

            @pl.when(chunk >= 2)
            def _():
                token_copy(chunk - 2).wait()

            def some(at):
                token_buf[slot, at] = mixed_buf[at] + reduce.raw[at]

            tiles(rows, some)
            token_copy(chunk).start()

        schedule(chunks, reduce, multiply, fetch, sums, finish, ring.event, ring.events)
        writes = [
            pltpu.make_async_copy(
                total.at[way], weight_grad.at[:, way * side : (way + 1) * side], out_sems.at[way]
            )
            for way in range(2)
        ]
        for item in writes:
            item.start()
        gain_total = gain_mine[...]
        for shift in range(1, count):
            gain_copies[shift - 1].wait()
            gain_total = gain_total + gain_land[shift - 1]
        gain_grads[...] = gain_total
        ring.end()
        reduce.end(chunks)
        for chunk in (chunks - 2, chunks - 1):
            token_copy(chunk).wait()
        for item in writes:
            item.wait()

    shape = jax.ShapeDtypeStruct
    out = pl.pallas_call(
        kernel,
        out_shape=[
            shape((length, width), WIDE),
            shape((shard, columns), WIDE),
            shape((8, width), WIDE),
        ]
        + Reduce.landing(rows, chunks, width, True),
        in_specs=[VMEM] * 10 + [HBM, HBM] + [VMEM] * 4,
        out_specs=[HBM, HBM, VMEM, HBM, HBM],
        scratch_shapes=[item for group in groups for item in group],
        compiler_params=pltpu.CompilerParams(
            collective_id=collective, has_side_effects=True, vmem_limit_bytes=60 * MIB
        ),
        cost_estimate=pl.CostEstimate(
            flops=4 * length * columns * D, bytes_accessed=8 * length * D, transcendentals=0
        ),
    )(
        query_back,
        key_back,
        value_grad,
        query_raw,
        key_raw,
        factors,
        projections,
        query_gain,
        key_gain,
        stack,
        inputs,
        mixed_grad,
        *gain_parts,
    )
    return out[:3]


def token_positions(segment):
    length = segment.shape[0]
    labels = jnp.arange(SEGS, dtype=jnp.int32)
    member = (segment[:, None] == labels[None, :]).astype(jnp.int32)
    totals = jnp.sum(member, axis=0)
    starts = jnp.cumsum(totals) - totals
    opening = jnp.sum(member * starts[None, :], axis=1)
    return jnp.arange(length, dtype=jnp.int32) - opening


def rotary_tables(segment):
    place = token_positions(segment).astype(jnp.float32)
    halves = HEAD // 2
    inverse = jnp.exp(jnp.arange(halves, dtype=jnp.float32) * (-2.0 * math.log(THETA) / HEAD))
    angle = place[:, None] * inverse[None, :]
    return (jnp.cos(angle), jnp.sin(angle))


BLOCK = 256
LANES = 128
SCALE = 1.0 / math.sqrt(HEAD)
SCALE_TWO = SCALE * math.log2(math.e)


def turn(values, cosine, sine):
    return values * cosine + pltpu.roll(values, HEAD // 2, 1) * sine


def head_columns(head):
    return slice(head * HEAD, (head + 1) * HEAD)


def nt(left, right):
    return lax.dot_general(left, right, (((1,), (1,)), ((), ())), preferred_element_type=WIDE)


def attend(first_block, query_raw, key_raw, values, factors, query_gain, key_gain, tables, starts):
    length, width = query_raw.shape
    heads = width // HEAD

    def kernel(
        first_block,
        query_raw,
        key_raw,
        values,
        factors,
        query_gain,
        key_gain,
        cosine,
        sine,
        starts,
        queries,
        keys,
        attended,
        peaks,
        peak_columns,
    ):
        @pl.loop(0, length // BLOCK)
        def _(index):
            at = row_slice(index, BLOCK)
            cos, sin = cosine[at], sine[at]
            pairs = ((query_raw, query_gain, queries), (key_raw, key_gain, keys))
            for which, (raw, gain, out) in enumerate(pairs):
                factor = factors[at, which : which + 1]
                for head in range(heads):
                    columns = head_columns(head)
                    normed = raw[at, columns] * factor * gain[:, columns]
                    out[at, columns] = turn(normed, cos, sin).astype(LOW)

        lane = lax.broadcasted_iota(jnp.int32, (BLOCK, LANES), 1)
        row_index = lax.broadcasted_iota(jnp.int32, (BLOCK, BLOCK), 0)
        column_index = lax.broadcasted_iota(jnp.int32, (BLOCK, BLOCK), 1)

        def query_block(index):
            at = row_slice(index, BLOCK)
            start = starts[at]

            def key_block(other, carry):
                there = row_slice(other, BLOCK)
                key_place = column_index + other * BLOCK
                allowed = (key_place >= start) & (key_place <= row_index + index * BLOCK)
                made = []
                for head in range(heads):
                    columns = head_columns(head)
                    peak, total, rows = carry[head]
                    scores = nt(queries[at, columns], keys[there, columns]) * SCALE_TWO
                    scores = jnp.where(allowed, scores, NEGATIVE)
                    higher = jnp.maximum(peak, jnp.max(scores, axis=1, keepdims=True))
                    raised = jnp.exp2(scores - higher)
                    shrink = jnp.exp2(peak - higher)
                    total = total * shrink + jnp.sum(raised, axis=1, keepdims=True)
                    rows = rows * shrink + jnp.dot(
                        raised.astype(LOW), values[there, columns], preferred_element_type=WIDE
                    )
                    made.append((higher, total, rows))
                return tuple(made)

            empty = (
                jnp.full((BLOCK, 1), NEGATIVE, WIDE),
                jnp.zeros((BLOCK, 1), WIDE),
                jnp.zeros((BLOCK, HEAD), WIDE),
            )
            done = lax.fori_loop(first_block[index], index + 1, key_block, (empty,) * heads)
            column = jnp.zeros((BLOCK, LANES), WIDE)
            for head in range(heads):
                peak, total, rows = done[head]
                attended[at, head_columns(head)] = (rows / total).astype(LOW)
                column = jnp.where(lane == head, peak + jnp.log2(total), column)
            peak_columns[at] = column

        loop(length // BLOCK, query_block)
        peaks[...] = peak_columns[...].T[:8]

    shape = jax.ShapeDtypeStruct
    smem = pl.BlockSpec(memory_space=pltpu.SMEM)
    return pl.pallas_call(
        kernel,
        out_shape=[
            shape((length, width), LOW),
            shape((length, width), LOW),
            shape((length, width), LOW),
            shape((8, length), WIDE),
        ],
        in_specs=[smem] + [VMEM] * 9,
        out_specs=[VMEM] * 4,
        scratch_shapes=[pltpu.VMEM((length, LANES), WIDE)],
        compiler_params=pltpu.CompilerParams(vmem_limit_bytes=48 * MIB),
        cost_estimate=pl.CostEstimate(
            flops=2 * length * MAX_LEN * width,
            bytes_accessed=16 * length * width,
            transcendentals=length * MAX_LEN * heads // 2,
        ),
    )(first_block, query_raw, key_raw, values, factors, query_gain, key_gain, *tables, starts)


def attend_back(
    last_block,
    queries,
    keys,
    values,
    attended,
    upstream,
    peaks,
    query_raw,
    key_raw,
    factors,
    query_gain,
    key_gain,
    tables,
    start_row,
):
    length, width = query_raw.shape
    heads = width // HEAD

    def kernel(
        last_block,
        queries,
        keys,
        values,
        attended,
        upstream,
        peaks,
        query_raw,
        key_raw,
        factors,
        query_gain,
        key_gain,
        cosine,
        sine,
        start_row,
        query_out,
        key_out,
        value_out,
        projections,
        query_gain_grad,
        key_gain_grad,
        query_sum,
        key_sum,
        value_sum,
        columns_scratch,
        deltas,
    ):
        lane = lax.broadcasted_iota(jnp.int32, (BLOCK, LANES), 1)
        query_gain_grad[...] = jnp.zeros_like(query_gain_grad)
        key_gain_grad[...] = jnp.zeros_like(key_gain_grad)

        def prepare(index):
            at = row_slice(index, BLOCK)
            column = jnp.zeros((BLOCK, LANES), WIDE)
            for head in range(heads):
                columns = head_columns(head)
                delta = jnp.sum(
                    attended[at, columns].astype(WIDE) * upstream[at, columns].astype(WIDE),
                    axis=1,
                    keepdims=True,
                )
                column = jnp.where(lane == head, delta, column)
            columns_scratch[at] = column
            query_sum[at] = jnp.zeros((BLOCK, width), WIDE)

        loop(length // BLOCK, prepare)
        deltas[...] = columns_scratch[...].T[:8]
        row_index = lax.broadcasted_iota(jnp.int32, (BLOCK, BLOCK), 0)
        column_index = lax.broadcasted_iota(jnp.int32, (BLOCK, BLOCK), 1)

        def turn_back(at, summed, raw, gain, factor, out, gain_grad):
            cos, sin = cosine[at], sine[at]
            share = jnp.zeros((BLOCK, 1), WIDE)
            for head in range(heads):
                columns = head_columns(head)
                normed = turn(summed(head) * SCALE, cos, -sin)
                out[at, columns] = normed
                weighed = normed * raw[at, columns]
                share += jnp.sum(gain[:, columns] * weighed, axis=1, keepdims=True)
                gain_grad[:, columns] += jnp.sum(weighed * factor, axis=0, keepdims=True)
            return share

        def key_block(index):
            at = row_slice(index, BLOCK)
            key_sum[...] = jnp.zeros_like(key_sum)
            value_sum[...] = jnp.zeros_like(value_sum)

            def query_block(other, carry):
                there = row_slice(other, BLOCK)
                key_place = row_index + index * BLOCK
                allowed = (key_place >= start_row[:, there]) & (
                    key_place <= column_index + other * BLOCK
                )
                for head in range(heads):
                    columns = head_columns(head)
                    scores = nt(keys[at, columns], queries[there, columns]) * SCALE_TWO
                    scores = jnp.where(allowed, scores, NEGATIVE)
                    chance = jnp.exp2(scores - peaks[head : head + 1, there])
                    value_sum[:, columns] += jnp.dot(
                        chance.astype(LOW), upstream[there, columns], preferred_element_type=WIDE
                    )
                    chance_grad = nt(values[at, columns], upstream[there, columns])
                    score_grad = (chance * (chance_grad - deltas[head : head + 1, there])).astype(LOW)
                    key_sum[:, columns] += jnp.dot(
                        score_grad, queries[there, columns], preferred_element_type=WIDE
                    )
                    query_sum[there, columns] += lax.dot_general(
                        score_grad,
                        keys[at, columns],
                        (((0,), (0,)), ((), ())),
                        preferred_element_type=WIDE,
                    )
                return carry

            lax.fori_loop(index, last_block[index] + 1, query_block, 0)
            value_out[at] = value_sum[...].astype(LOW)
            share = turn_back(
                at,
                lambda head: key_sum[:, head_columns(head)],
                key_raw,
                key_gain,
                factors[at, 1:2],
                key_out,
                key_gain_grad,
            )
            columns_scratch[at] = jnp.where(lane == 1, share, 0.0)

        loop(length // BLOCK, key_block)

        def finish(index):
            at = row_slice(index, BLOCK)
            share = turn_back(
                at,
                lambda head: query_sum[at, head_columns(head)],
                query_raw,
                query_gain,
                factors[at, 0:1],
                query_out,
                query_gain_grad,
            )
            columns_scratch[at] += jnp.where(lane == 0, share, 0.0)

        loop(length // BLOCK, finish)
        projections[...] = columns_scratch[...].T[:8]

    shape = jax.ShapeDtypeStruct
    smem = pl.BlockSpec(memory_space=pltpu.SMEM)
    return pl.pallas_call(
        kernel,
        out_shape=[
            shape((length, width), WIDE),
            shape((length, width), WIDE),
            shape((length, width), LOW),
            shape((8, length), WIDE),
            shape((1, width), WIDE),
            shape((1, width), WIDE),
        ],
        in_specs=[smem] + [VMEM] * 14,
        out_specs=[VMEM] * 6,
        scratch_shapes=[
            pltpu.VMEM((length, width), WIDE),
            pltpu.VMEM((BLOCK, width), WIDE),
            pltpu.VMEM((BLOCK, width), WIDE),
            pltpu.VMEM((length, LANES), WIDE),
            pltpu.VMEM((8, length), WIDE),
        ],
        compiler_params=pltpu.CompilerParams(vmem_limit_bytes=52 * MIB),
        cost_estimate=pl.CostEstimate(
            flops=5 * length * MAX_LEN * width,
            bytes_accessed=32 * length * width,
            transcendentals=length * MAX_LEN * heads // 2,
        ),
    )(
        last_block,
        queries,
        keys,
        values,
        attended,
        upstream,
        peaks,
        query_raw,
        key_raw,
        factors,
        query_gain,
        key_gain,
        *tables,
        start_row,
    )


def shards(
    tokens,
    query_weight,
    key_weight,
    value_weight,
    output_weight,
    gate_weight,
    up_weight,
    down_weight,
    query_gain,
    key_gain,
    attn_gain,
    mlp_gain,
    seq_ids,
    out_grad,
):
    segment = seq_ids[0]
    length = tokens.shape[0]
    local_width = tokens.shape[1]
    cosine, sine = rotary_tables(segment)
    tables = (
        jnp.concatenate([cosine, cosine], axis=1),
        jnp.concatenate([-sine, sine], axis=1),
    )
    order = jnp.arange(length, dtype=jnp.int32)
    starts = order - token_positions(segment)
    blocks = length // BLOCK
    first_block = starts.reshape(blocks, BLOCK)[:, 0] // BLOCK
    closing = segment.reshape(blocks, BLOCK)[:, -1]
    ends = jnp.sum((segment[None, :] <= closing[:, None]).astype(jnp.int32), axis=1) - 1
    last_block = ends // BLOCK
    gains = jnp.concatenate([attn_gain[None], mlp_gain[None], jnp.zeros((6, local_width))], axis=0)
    query_gain, key_gain = query_gain.reshape(1, -1), key_gain.reshape(1, -1)
    inputs, attn_stack, query_raw, key_raw, values, squares, halves = gather_in(
        tokens, jnp.concatenate([query_weight, key_weight, value_weight], axis=1), gains, 1
    )
    attn_half, mlp_half = halves[:1], halves[1:2]
    squares, output_weight = lax.optimization_barrier((squares, output_weight))
    output_full = lax.all_gather(output_weight, "gy", axis=1, tiled=True)
    factors = lax.rsqrt(squares[:2].T / D + EPS)
    queries, keys, attended, peaks = attend(
        first_block,
        query_raw,
        key_raw,
        values,
        factors,
        query_gain,
        key_gain,
        tables,
        starts[:, None],
    )
    attn_raw, mixed, mlp_inputs, gate_full, up_full, down_full, upstream = attn_out(
        attended, output_full, attn_half, inputs, out_grad, gate_weight, up_weight, down_weight, 2
    )
    result, mlp_full, mlp_gain_part, hidden, gate, up = mlp_forward(
        mlp_inputs, gate_full, up_full, down_full, mlp_half, mixed, upstream, 3
    )
    gate_grad, up_grad, down_turned = hidden_back(mlp_full, down_full, hidden, gate, up, 4)
    down_weight_grad = down_turned.T
    mixed_grad, attn_full, attn_gain_part, gate_weight_grad, up_weight_grad = mlp_back(
        gate_grad, up_grad, gate_full, up_full, mlp_inputs, attn_half, upstream, attn_raw, 5
    )
    output_product = lax.dot_general(
        attended, attn_full, (((0,), (0,)), ((), ())), preferred_element_type=jnp.float32
    )
    output_weight_grad = lax.psum_scatter(
        output_product.astype(jnp.bfloat16), "gy", scatter_dimension=1, tiled=True
    ).astype(jnp.float32)
    attended_grad = lax.dot_general(
        attn_full, output_full, (((1,), (1,)), ((), ())), preferred_element_type=jnp.float32
    ).astype(jnp.bfloat16)
    query_back, key_back, value_grad, projections, query_gain_part, key_gain_part = attend_back(
        last_block,
        queries,
        keys,
        values,
        attended,
        attended_grad,
        peaks,
        query_raw,
        key_raw,
        factors,
        query_gain,
        key_gain,
        tables,
        starts[None, :],
    )
    token_grad, attn_weight_grads, gain_grads = attn_in_back(
        query_back,
        key_back,
        value_grad,
        query_raw,
        key_raw,
        factors,
        projections,
        query_gain,
        key_gain,
        attn_stack,
        inputs,
        mixed_grad,
        (query_gain_part, key_gain_part, attn_gain_part, mlp_gain_part),
        6,
    )
    query_weight_grad = attn_weight_grads[:, :local_width]
    key_weight_grad = attn_weight_grads[:, local_width : 2 * local_width]
    value_weight_grad = attn_weight_grads[:, 2 * local_width :]
    query_gain_grad, key_gain_grad, attn_gain_grad, mlp_gain_grad = (gain_grads[i] for i in range(4))
    return (
        result,
        token_grad,
        query_weight_grad,
        key_weight_grad,
        value_weight_grad,
        output_weight_grad,
        gate_weight_grad,
        up_weight_grad,
        down_weight_grad,
        query_gain_grad,
        key_gain_grad,
        attn_gain_grad,
        mlp_gain_grad,
    )


def solution(mesh):
    return jax.shard_map(
        shards,
        mesh=mesh,
        in_specs=(
            P("gy", "gx"),
            P("gy", "gx"),
            P("gy", "gx"),
            P("gy", "gx"),
            P("gx", "gy"),
            P("gy", "gx"),
            P("gy", "gx"),
            P("gx", "gy"),
            P("gx"),
            P("gx"),
            P("gx"),
            P("gx"),
            P("gy", None),
            P("gy", "gx"),
        ),
        out_specs=(
            P("gy", "gx"),
            P("gy", "gx"),
            P("gy", "gx"),
            P("gy", "gx"),
            P("gy", "gx"),
            P("gx", "gy"),
            P("gy", "gx"),
            P("gy", "gx"),
            P("gx", "gy"),
            P("gx"),
            P("gx"),
            P("gx"),
            P("gx"),
        ),
        check_vma=False,
    )
```

```python
import math

import jax
import jax.numpy as jnp
from jax import lax
from jax.experimental import pallas as pl
from jax.experimental.pallas import tpu as pltpu
from jax.sharding import PartitionSpec as P

D = 2048
HEAD = 128
MAX_LEN = 1024
SEGS = 4


EPS = 1e-06
THETA = 500000.0
NEGATIVE = -1e30


MESH = pl.DeviceIdType.MESH
HBM = pl.BlockSpec(memory_space=pltpu.HBM)
VMEM = pl.BlockSpec(memory_space=pltpu.VMEM)
LOW = jnp.bfloat16
WIDE = jnp.float32
MIB = 1 << 20
LAG = 2
STATS = 128


def core_here():
    return lax.rem(lax.axis_index("gx"), 2)


def chip_here():
    return lax.div(lax.axis_index("gx"), 2)


def other_core():
    return lax.axis_index("gx") + 1 - 2 * core_here()


def peer_at(shift):
    return lax.rem(lax.axis_index("gx") + 2 * shift, lax.axis_size("gx"))


def rank_at(shift):
    return lax.rem(lax.axis_index("gx") + shift, lax.axis_size("gx"))


def block_at(shift):
    return lax.rem(lax.axis_index("gy") + shift, lax.axis_size("gy"))


def ring_place():
    count = lax.axis_size("gy")
    index = lax.axis_index("gy")
    row, side = lax.div(index, 2), lax.rem(index, 2)
    return side * row + (1 - side) * (count - 1 - row)


def ring_device(place):
    count = lax.axis_size("gy")
    place = lax.rem(place + 2 * count, count)
    back = lax.div(place, count // 2)
    row = (1 - back) * place + back * (count - 1 - place)
    return 2 * row + 1 - back


def greet(gx, ring, all_blocks=False):
    barrier = pltpu.get_barrier_semaphore()
    partners = []
    if all_blocks:
        partners += [{"gy": block_at(k)} for k in range(1, lax.axis_size("gy"))]
    if gx == "all":
        partners += [{"gx": rank_at(k)} for k in range(1, lax.axis_size("gx"))]
    elif gx:
        partners.append({"gx": other_core()})
        partners += [{"gx": peer_at(k)} for k in range(1, lax.axis_size("gx") // 2)]
    if ring:
        place = ring_place()
        partners += [{"gy": ring_device(place + 1)}, {"gy": ring_device(place - 1)}]
    for partner in partners:
        pl.semaphore_signal(barrier, inc=1, device_id=partner, device_id_type=MESH)
    pl.semaphore_wait(barrier, len(partners))


def remote(source, target, send, recv, device):
    return pltpu.make_async_remote_copy(
        src_ref=source,
        dst_ref=target,
        send_sem=send,
        recv_sem=recv,
        device_id=device,
        device_id_type=MESH,
    )


def loop(count, body):
    def step(index, carry):
        body(index)
        return carry

    lax.fori_loop(0, count, step, 0)


def aligned(value, factor):
    return pl.multiple_of(value, factor)


class RingGather:
    def __init__(self, sources, slot, parts, send, recv, local):
        self.sources, self.slot, self.parts = sources, slot, parts
        self.send, self.recv, self.local = send, recv, local
        self.count = lax.axis_size("gy")

    @staticmethod
    def scratch(parts):
        count = lax.axis_size("gy")
        return [
            pltpu.SemaphoreType.DMA((count - 1, 2, parts)),
            pltpu.SemaphoreType.DMA((count - 1, 2, parts)),
            pltpu.SemaphoreType.DMA((2, parts)),
        ]

    def copy(self, way, step, part, behind):
        place = ring_place()
        sign = 1 - 2 * way
        spot = self.slot(way, ring_device(place - sign * (step + behind)), part)
        return remote(
            spot,
            spot,
            self.send.at[step, way, part],
            self.recv.at[step, way, part],
            {"gy": ring_device(place + sign)},
        )

    def begin(self):
        place = [
            pltpu.make_async_copy(
                self.sources(way, part),
                self.slot(way, lax.axis_index("gy"), part),
                self.local.at[way, part],
            )
            for way in range(2)
            for part in range(self.parts)
        ]
        for item in place:
            item.start()
        for item in place:
            item.wait()
        for part in range(self.parts):
            for way in range(2):
                self.copy(way, 0, part, 0).start()

    @property
    def events(self):
        return (self.count - 2) * self.parts

    def event(self, index):
        step = 1 + lax.div(index, self.parts)
        for part in range(self.parts):

            @pl.when(lax.rem(index, self.parts) == part)
            def _():
                for way in range(2):
                    self.copy(way, step - 1, part, 1).wait_recv()
                    self.copy(way, step, part, 0).start()

    def end(self):
        for part in range(self.parts):
            for way in range(2):
                self.copy(way, self.count - 2, part, 1).wait_recv()

        def drain(step):
            for part in range(self.parts):
                for way in range(2):
                    self.copy(way, step, part, 0).wait_send()

        loop(self.count - 1, drain)


class RingScatter:
    def __init__(self, product, total, sums, land, send, recv, credit, slots, parts):
        self.product, self.total, self.sums, self.land = product, total, sums, land
        self.send, self.recv, self.credit = send, recv, credit
        self.slots, self.parts = slots, parts
        self.count = lax.axis_size("gy")
        self.rows = total.shape[1] // parts

    @staticmethod
    def scratch(rows, columns, slots, parts):
        count = lax.axis_size("gy")
        return [
            pltpu.VMEM((2, rows, columns), WIDE),
            pltpu.VMEM((2, rows, columns), LOW),
            pltpu.VMEM((slots, 2, rows, columns), LOW),
            pltpu.SemaphoreType.DMA((count - 1, 2, parts)),
            pltpu.SemaphoreType.DMA((count - 1, 2, parts)),
            pltpu.SemaphoreType.REGULAR((2, parts)),
        ]

    def copy(self, way, step, part):
        place = ring_place()
        rows = pl.ds(aligned(part * self.rows, self.rows), self.rows)
        return remote(
            self.sums.at[way, rows],
            self.land.at[lax.rem(step, self.slots), way, rows],
            self.send.at[step, way, part],
            self.recv.at[step, way, part],
            {"gy": ring_device(place + 1 - 2 * way)},
        )

    def owner(self, way, step):
        sign = 1 - 2 * way
        return ring_device(ring_place() - sign * (1 + step))

    @property
    def events(self):
        return self.count * self.parts

    def event(self, index):
        step, part = lax.div(index, self.parts), lax.rem(index, self.parts)
        last = self.count - 1
        tile = min(self.rows, 32)

        @pl.when(part == 0)
        def _():
            for way in range(2):
                self.product(way, step)

        for way in range(2):
            base = part * self.rows

            @pl.when(step >= 1)
            def _():
                self.copy(way, step - 1, part).wait_recv()
                slot = lax.rem(step - 1, self.slots)

                @pl.loop(0, self.rows // tile)
                def _(index):
                    rows = pl.ds(aligned(base + index * tile, tile), tile)
                    self.total[way, rows] += self.land[slot, way, rows].astype(WIDE)

                @pl.when(step - 1 + self.slots < last)
                def _():
                    upstream = ring_device(ring_place() - (1 - 2 * way))
                    pl.semaphore_signal(
                        self.credit.at[way, part],
                        inc=1,
                        device_id={"gy": upstream},
                        device_id_type=MESH,
                    )

            @pl.when(step < last)
            def _():
                @pl.when(step >= 1)
                def _():
                    self.copy(way, step - 1, part).wait_send()

                @pl.loop(0, self.rows // tile)
                def _(index):
                    rows = pl.ds(aligned(base + index * tile, tile), tile)
                    self.sums[way, rows] = self.total[way, rows].astype(LOW)

                @pl.when(step >= self.slots)
                def _():
                    pl.semaphore_wait(self.credit.at[way, part], 1)

                self.copy(way, step, part).start()

    def end(self):
        for part in range(self.parts):
            for way in range(2):
                self.copy(way, self.count - 2, part).wait_send()


class Reduce:
    def __init__(self, refs, core_land, cross_land, rows, width, scatter):
        (
            self.keep,
            self.core_send,
            self.core_stage,
            self.cross,
            self.cross_stage,
            self.raw,
            self.core_sems,
            self.cross_send_sems,
            self.cross_recv_sems,
            self.stage_sems,
        ) = refs
        self.core_land, self.cross_land = core_land, cross_land
        self.rows, self.width, self.scatter = rows, width, scatter
        self.chips = lax.axis_size("gx") // 2

    @staticmethod
    def scratch(rows, chunks, width, scatter):
        chips = lax.axis_size("gx") // 2
        half = chips * width
        part = width if scatter else half
        return [
            pltpu.VMEM((2, rows, half), LOW),
            pltpu.VMEM((2, rows, half), LOW),
            pltpu.VMEM((rows, half), LOW),
            pltpu.VMEM((LAG + 2, chips, rows, width) if scatter else (LAG + 2, rows, half), LOW),
            pltpu.VMEM((chips - 1, rows, part), LOW),
            pltpu.VMEM((rows, part), WIDE),
            pltpu.SemaphoreType.DMA((2, chunks)),
            pltpu.SemaphoreType.DMA((chips - 1, chunks)),
            pltpu.SemaphoreType.DMA((chips - 1, chunks)),
            pltpu.SemaphoreType.DMA((chips,)),
        ]

    @staticmethod
    def landing(rows, chunks, width, scatter):
        chips = lax.axis_size("gx") // 2
        half = chips * width
        part = width if scatter else half
        return [
            jax.ShapeDtypeStruct((chunks, rows, half), LOW),
            jax.ShapeDtypeStruct((chips - 1, chunks, rows, part), LOW),
        ]

    def core_copy(self, chunk):
        return remote(
            self.core_send.at[lax.rem(chunk, 2)],
            self.core_land.at[chunk],
            self.core_sems.at[0, chunk],
            self.core_sems.at[1, chunk],
            {"gx": other_core()},
        )

    def cross_copy(self, shift, chunk):
        source = self.cross.at[lax.rem(chunk, LAG + 2)]
        if self.scatter:
            block = lax.rem(chip_here() + shift, self.chips)
            source = source.at[block]
        return remote(
            source,
            self.cross_land.at[shift - 1, chunk],
            self.cross_send_sems.at[shift - 1, chunk],
            self.cross_recv_sems.at[shift - 1, chunk],
            {"gx": peer_at(shift)},
        )

    def produce(self, chunk, dot):
        @pl.when(chunk >= 2)
        def _():
            self.core_copy(chunk - 2).wait_send()

        slot = lax.rem(chunk, 2)
        core = core_here()
        for chip in range(self.chips):
            place = aligned((2 * chip + 1 - core) * self.width, self.width)
            self.core_send[slot, :, chip * self.width : (chip + 1) * self.width] = dot(
                place
            ).astype(LOW)
        self.core_copy(chunk).start()
        for chip in range(self.chips):
            place = aligned((2 * chip + core) * self.width, self.width)
            self.keep[slot, :, chip * self.width : (chip + 1) * self.width] = dot(
                place
            ).astype(LOW)

    def core_stage_copy(self, chunk):
        return pltpu.make_async_copy(
            self.core_land.at[chunk], self.core_stage, self.stage_sems.at[0]
        )

    def core_fetch(self, chunk):
        self.core_copy(chunk).wait_recv()
        self.core_stage_copy(chunk).start()

    def core_sum(self, chunk):
        slot, place = lax.rem(chunk, 2), lax.rem(chunk, LAG + 2)
        self.core_stage_copy(chunk).wait()

        @pl.when(chunk >= LAG + 2)
        def _():
            for shift in range(1, self.chips):
                self.cross_copy(shift, chunk - LAG - 2).wait_send()

        @pl.loop(0, self.rows // 32)
        def _(index):
            rows = pl.ds(aligned(index * 32, 32), 32)
            total = self.keep[slot, rows].astype(WIDE) + self.core_stage[rows].astype(WIDE)
            if self.scatter:
                for chip in range(self.chips):
                    columns = slice(chip * self.width, (chip + 1) * self.width)
                    self.cross[place, chip, rows] = total[:, columns].astype(LOW)
            else:
                self.cross[place, rows] = total.astype(LOW)

        for shift in range(1, self.chips):
            self.cross_copy(shift, chunk).start()

    def cross_stage_copy(self, shift, chunk):
        return pltpu.make_async_copy(
            self.cross_land.at[shift - 1, chunk],
            self.cross_stage.at[shift - 1],
            self.stage_sems.at[shift],
        )

    def cross_fetch(self, chunk):
        for shift in range(1, self.chips):
            self.cross_copy(shift, chunk).wait_recv()
            self.cross_stage_copy(shift, chunk).start()

    def cross_sum(self, chunk):
        place = lax.rem(chunk, LAG + 2)
        for shift in range(1, self.chips):
            self.cross_stage_copy(shift, chunk).wait()

        @pl.loop(0, self.rows // 32)
        def _(index):
            rows = pl.ds(aligned(index * 32, 32), 32)
            if self.scatter:
                total = self.cross[place, chip_here(), rows].astype(WIDE)
            else:
                total = self.cross[place, rows].astype(WIDE)
            for shift in range(1, self.chips):
                total = total + self.cross_stage[shift - 1, rows].astype(WIDE)
            self.raw[rows] = total

    def end(self, chunks):
        for chunk in (chunks - 2, chunks - 1):
            self.core_copy(chunk).wait_send()
        for chunk in range(chunks - LAG - 2, chunks):
            for shift in range(1, self.chips):
                self.cross_copy(shift, chunk).wait_send()


class Stats:
    def __init__(self, mine, land, sems):
        self.mine, self.land, self.sems = mine, land, sems

    @staticmethod
    def scratch(rows, chunks):
        return [
            pltpu.VMEM((2, rows, STATS), WIDE),
            pltpu.VMEM((chunks, rows, STATS), WIDE),
            pltpu.SemaphoreType.DMA((2, chunks)),
        ]

    def copy(self, chunk):
        return remote(
            self.mine.at[lax.rem(chunk, 2)],
            self.land.at[chunk],
            self.sems.at[0, chunk],
            self.sems.at[1, chunk],
            {"gx": other_core()},
        )

    def clear(self, chunk):
        @pl.when(chunk >= 2)
        def _():
            self.copy(chunk - 2).wait_send()

    def put(self, chunk, rows, first, second):
        lane = lax.broadcasted_iota(jnp.int32, (first.shape[0], STATS), 1)
        self.mine[lax.rem(chunk, 2), rows] = jnp.where(lane < STATS // 2, first, second)

    def get(self, chunk, rows):
        total = self.mine[lax.rem(chunk, 2), rows] + self.land[chunk, rows]
        return (total[:, :1], total[:, STATS // 2 : STATS // 2 + 1])

    def end(self, chunks):
        for chunk in (chunks - 2, chunks - 1):
            self.copy(chunk).wait_send()


class Spread:
    def __init__(self, buffer, whole, local, send, recv, rows, width):
        self.buffer, self.whole = buffer, whole
        self.local, self.send, self.recv = local, send, recv
        self.rows, self.width = rows, width
        self.chips = lax.axis_size("gx") // 2

    @staticmethod
    def scratch(rows, chunks, width):
        chips = lax.axis_size("gx") // 2
        return [
            pltpu.VMEM((2, chips, rows, width), LOW),
            pltpu.SemaphoreType.DMA((2, chips)),
            pltpu.SemaphoreType.DMA((chunks, chips)),
            pltpu.SemaphoreType.DMA((chunks, chips)),
        ]

    def pair(self, chunk, chip, core):
        slot = lax.rem(chunk, 2)
        source = self.buffer.at[slot, chip]
        rows = pl.ds(aligned(chunk * self.rows, self.rows), self.rows)
        rank = 2 * chip + core
        if len(self.whole.shape) == 3:
            target = self.whole.at[rank, rows]
        else:
            columns = pl.ds(aligned(rank * self.width, self.width), self.width)
            target = self.whole.at[rows, columns]
        here = pltpu.make_async_copy(source, target, self.local.at[slot, chip])
        away = remote(
            source,
            target,
            self.send.at[chunk, chip],
            self.recv.at[chunk, chip],
            {"gx": other_core()},
        )
        return (here, away)

    def put(self, chunk, rows, values):
        for chip in range(self.chips):
            columns = slice(chip * self.width, (chip + 1) * self.width)
            self.buffer[lax.rem(chunk, 2), chip, rows] = values[:, columns].astype(LOW)

    def clear(self, chunk):
        @pl.when(chunk >= 2)
        def _():
            self.settle(chunk - 2)

    def settle(self, chunk):
        for chip in range(self.chips):
            here, away = self.pair(chunk, chip, core_here())
            here.wait()
            away.wait_send()

    def go(self, chunk):
        for chip in range(self.chips):
            here, away = self.pair(chunk, chip, core_here())
            here.start()
            away.start()

    def end(self, chunks):
        for chunk in (chunks - 2, chunks - 1):
            self.settle(chunk)

        def arrive(chunk):
            for chip in range(self.chips):
                self.pair(chunk, chip, 1 - core_here())[1].wait_recv()

        loop(chunks, arrive)


def row_slice(chunk, rows):
    return pl.ds(aligned(chunk * rows, rows), rows)


def core_blocks(source, chunk, rows, width, buffer, sems):
    return [
        pltpu.make_async_copy(
            source.at[2 * chip + core_here(), row_slice(chunk, rows)],
            buffer.at[:, chip * width : (chip + 1) * width],
            sems.at[chip],
        )
        for chip in range(lax.axis_size("gx") // 2)
    ]


def all_blocks(source, rows, width, buffer, sems):
    return [
        pltpu.make_async_copy(
            source.at[rank] if rows is None else source.at[rank, rows],
            buffer.at[:, rank * width : (rank + 1) * width],
            sems.at[rank],
        )
        for rank in range(source.shape[0])
    ]


def tiles(rows, body):
    @pl.loop(0, rows // 32)
    def _(index):
        body(pl.ds(aligned(index * 32, 32), 32))


def schedule(chunks, reduce, multiply, fetch, sums, finish, event=None, events=0, prepare=None):
    steps = chunks + 2 + LAG

    def iteration(step):
        if event is not None:
            low = lax.div(step * events, steps)
            high = lax.div((step + 1) * events, steps)

            def some(index, carry):
                event(index)
                return carry

            lax.fori_loop(low, high, some, 0)

        @pl.when((step >= 1) & (step <= chunks))
        def _():
            reduce.core_fetch(step - 1)

        @pl.when((step >= 1 + LAG) & (step < chunks + 1 + LAG))
        def _():
            reduce.cross_fetch(step - 1 - LAG)

        @pl.when((step >= 1 + LAG) & (step < chunks + 2 + LAG))
        def _():
            fetch(step - 1 - LAG)

        @pl.when(step < chunks)
        def _():
            if prepare is not None:
                prepare(step)
            reduce.produce(step, lambda place: multiply(step, place))

        @pl.when((step >= 1) & (step <= chunks))
        def _():
            reduce.core_sum(step - 1)

        @pl.when((step >= 2 + LAG) & (step < chunks + 2 + LAG))
        def _():
            finish(step - 2 - LAG)

        @pl.when((step >= 1 + LAG) & (step < chunks + 1 + LAG))
        def _():
            reduce.cross_sum(step - 1 - LAG)
            sums(step - 1 - LAG)

    loop(steps, iteration)


def take(refs, counts):
    groups, start = [], 0
    for count in counts:
        groups.append(refs[start : start + count])
        start += count
    return groups


class Columns:
    def __init__(self, source, shard, left, turned, sem):
        self.source, self.shard = source, shard
        self.left, self.turned, self.sem = left, turned, sem

    @staticmethod
    def scratch(length, shard):
        return [
            pltpu.VMEM((length, shard), LOW),
            pltpu.VMEM((shard, length), LOW),
            pltpu.SemaphoreType.DMA((1,)),
        ]

    def copy(self, owner):
        each = self.source.shape[2] // self.shard
        at = pl.ds(aligned(lax.rem(owner, each) * self.shard, self.shard), self.shard)
        source = self.source.at[lax.div(owner, each), :, at]
        return pltpu.make_async_copy(source, self.left, self.sem.at[0])

    def take(self, ring, way, step):
        self.copy(ring.owner(way, step)).wait()
        self.turned[...] = self.left[...].T
        if way == 0:
            self.copy(ring.owner(1, step)).start()
        else:

            @pl.when(step + 1 < ring.count)
            def _():
                self.copy(ring.owner(0, step + 1)).start()


def attn_out(
    attended, weight, gain, tokens, out_grad, gate_shard, up_shard, down_shard, collective
):
    length, width = attended.shape
    chips = lax.axis_size("gx") // 2
    half = chips * width
    count = lax.axis_size("gy")
    chunks = count
    rows = length // chunks
    hidden = gate_shard.shape[1]
    shard = gate_shard.shape[0]
    part_rows = shard // 2
    side = hidden // 2
    down_columns = down_shard.shape[1]

    groups = [
        Reduce.scratch(rows, chunks, width, False),
        Stats.scratch(rows, chunks),
        Spread.scratch(rows, chunks, width),
        RingGather.scratch(3),
        [
            pltpu.VMEM((rows, half), LOW),
            pltpu.VMEM((2, rows, half), WIDE),
            pltpu.VMEM((2, rows, half), LOW),
            pltpu.SemaphoreType.DMA((chips,)),
            pltpu.SemaphoreType.DMA((2,)),
            pltpu.SemaphoreType.DMA((2,)),
            pltpu.SemaphoreType.DMA((1,)),
            pltpu.SemaphoreType.DMA((chips - 1, chunks, 2)),
        ],
    ]

    def kernel(*refs):
        ins, outs, *scratch = take(refs, [8, 9] + [len(g) for g in groups])
        attended, weight, gain, tokens, out_grad, gate_shard, up_shard, down_shard = ins
        raw_out, mixed_out, low_out, gate_full, up_full, down_full, upstream = outs[:7]
        core_land, cross_land = outs[7:]
        reduce = Reduce(scratch[0], core_land, cross_land, rows, width, False)
        stats = Stats(*scratch[1])
        buffer, local, send, recv = scratch[2]
        spread = Spread(buffer, low_out, local, send, recv, rows, width)
        token_buf, mixed_buf, raw_buf = scratch[4][:3]
        token_sems, mixed_sems, raw_sems, own_sem, up_sems = scratch[4][3:]
        full = (gate_full, up_full)
        shards_here = (gate_shard, up_shard)

        def slot(way, owner, part):
            if part == 2:
                return down_full.at[owner, way * side : (way + 1) * side]
            base = owner * shard + part * part_rows
            return full[way].at[pl.ds(aligned(base, part_rows), part_rows)]

        def source(way, part):
            if part == 2:
                return down_shard.at[way * side : (way + 1) * side]
            return shards_here[way].at[part * part_rows : (part + 1) * part_rows]

        ring = RingGather(source, slot, 3, *scratch[3])
        up_place = pl.ds(aligned(chip_here() * width, width), width)
        own = pltpu.make_async_copy(out_grad, upstream.at[:, up_place], own_sem.at[0])

        def crossings(chunk):
            at = row_slice(chunk, rows)
            return [
                remote(
                    out_grad.at[at],
                    upstream.at[at, up_place],
                    up_sems.at[shift - 1, chunk, 0],
                    up_sems.at[shift - 1, chunk, 1],
                    {"gx": peer_at(shift)},
                )
                for shift in range(1, chips)
            ]

        own.start()
        greet(True, True)
        ring.begin()

        def multiply(chunk, place):
            return jnp.dot(
                attended[row_slice(chunk, rows)],
                weight[:, pl.ds(place, width)],
                preferred_element_type=WIDE,
            )

        def prepare(chunk):
            for item in crossings(chunk):
                item.start()

        def token_copies(chunk):
            return core_blocks(tokens, chunk, rows, width, token_buf, token_sems)

        def fetch(chunk):
            @pl.when(chunk >= 1)
            def _():
                for item in token_copies(chunk - 1):
                    item.start()

        def mixed_copy(chunk):
            slot = lax.rem(chunk, 2)
            return pltpu.make_async_copy(
                mixed_buf.at[slot, :, pl.ds(aligned(chip_here() * width, width), width)],
                mixed_out.at[row_slice(chunk, rows)],
                mixed_sems.at[slot],
            )

        def raw_copy(chunk):
            slot = lax.rem(chunk, 2)
            return pltpu.make_async_copy(
                raw_buf.at[slot], raw_out.at[row_slice(chunk, rows)], raw_sems.at[slot]
            )

        def sums(chunk):
            stats.clear(chunk)

            @pl.when(chunk >= 2)
            def _():
                raw_copy(chunk - 2).wait()

            def tile(at):
                raw = reduce.raw[at]
                raw_buf[lax.rem(chunk, 2), at] = raw.astype(LOW)
                squares = jnp.sum(raw * raw, axis=1, keepdims=True)
                stats.put(chunk, at, squares, squares)

            tiles(rows, tile)
            stats.copy(chunk).start()
            raw_copy(chunk).start()

        def finish(chunk):
            slot = lax.rem(chunk, 2)
            for item in token_copies(chunk):
                item.wait()
            stats.copy(chunk).wait_recv()
            spread.clear(chunk)

            @pl.when(chunk >= 2)
            def _():
                mixed_copy(chunk - 2).wait()

            def tile(at):
                squares, _ = stats.get(chunk, at)
                factor = lax.rsqrt(squares / D + EPS)
                mixed = token_buf[at].astype(WIDE) + reduce.raw[at] * factor * gain[...]
                mixed_buf[slot, at] = mixed
                spread.put(chunk, at, mixed)

            tiles(rows, tile)
            spread.go(chunk)
            mixed_copy(chunk).start()

        schedule(chunks, reduce, multiply, fetch, sums, finish, ring.event, ring.events, prepare)
        ring.end()
        own.wait()

        def drain(chunk):
            for item in crossings(chunk):
                item.wait()

        loop(chunks, drain)
        reduce.end(chunks)
        stats.end(chunks)
        spread.end(chunks)
        for chunk in (chunks - 2, chunks - 1):
            mixed_copy(chunk).wait()
            raw_copy(chunk).wait()

    shape = jax.ShapeDtypeStruct
    out = pl.pallas_call(
        kernel,
        out_shape=[
            shape((length, half), LOW),
            shape((length, width), WIDE),
            shape((2 * chips, length, width), LOW),
            shape((shard * count, hidden), LOW),
            shape((shard * count, hidden), LOW),
            shape((count, hidden, down_columns), LOW),
            shape((length, half), LOW),
        ]
        + Reduce.landing(rows, chunks, width, False),
        in_specs=[VMEM, VMEM, VMEM, HBM, HBM, HBM, HBM, HBM],
        out_specs=[HBM] * 9,
        scratch_shapes=[item for group in groups for item in group],
        compiler_params=pltpu.CompilerParams(
            collective_id=collective, has_side_effects=True, vmem_limit_bytes=60 * MIB
        ),
        cost_estimate=pl.CostEstimate(
            flops=2 * length * width * D, bytes_accessed=8 * length * D, transcendentals=0
        ),
    )(attended, weight, gain, tokens, out_grad, gate_shard, up_shard, down_shard)
    return out[:7]


def mlp_forward(inputs, gate_full, up_full, down_full, gain, mixed, upstream, collective):
    length, inner = inputs.shape[1], gate_full.shape[1]
    width = mixed.shape[1]
    ranks = inputs.shape[0]
    down_columns = down_full.shape[2]
    chips = lax.axis_size("gx") // 2
    half = chips * width
    chunks = lax.axis_size("gy")
    rows = length // chunks
    tile = min(512, inner)
    pieces = inner // tile

    groups = [
        Reduce.scratch(rows, chunks, width, False),
        Stats.scratch(rows, chunks),
        Spread.scratch(rows, chunks, width),
        [
            pltpu.VMEM((2, rows, half), LOW),
            pltpu.VMEM((rows, width), WIDE),
            pltpu.VMEM((2, rows, width), LOW),
            pltpu.SemaphoreType.DMA((2,)),
            pltpu.SemaphoreType.DMA((1,)),
            pltpu.SemaphoreType.DMA((2,)),
        ],
        [
            pltpu.VMEM((D, inner), LOW),
            pltpu.VMEM((D, inner), LOW),
            pltpu.VMEM((inner, D), LOW),
            pltpu.VMEM((2, rows, D), LOW),
            pltpu.VMEM((2, 3, rows, inner), LOW),
            pltpu.SemaphoreType.DMA((pieces, 2)),
            pltpu.SemaphoreType.DMA((chunks,)),
            pltpu.SemaphoreType.DMA((2, ranks)),
            pltpu.SemaphoreType.DMA((2, 3)),
        ],
    ]

    def kernel(*refs):
        ins, outs, *scratch = take(refs, [7, 8] + [len(g) for g in groups])
        inputs, gate_full, up_full, down_full, gain, mixed, upstream = ins
        result, grad_out, gain_grad, hidden_out, gate_out, up_out, core_land, cross_land = outs
        gate_weight, up_weight, weight, row_buf, made = scratch[4][:5]
        piece_sems, weight_sem, row_sems, made_sems = scratch[4][5:]
        reduce = Reduce(scratch[0], core_land, cross_land, rows, width, False)
        stats = Stats(*scratch[1])
        buffer, local, send, recv = scratch[2]
        spread = Spread(buffer, grad_out, local, send, recv, rows, width)
        up_buf, mixed_buf, result_buf, up_sems, mixed_sems, result_sems = scratch[3]

        def piece_copies(piece):
            at = pl.ds(aligned(piece * tile, tile), tile)
            return [
                pltpu.make_async_copy(gate_full.at[:, at], gate_weight.at[:, at], piece_sems.at[piece, 0]),
                pltpu.make_async_copy(up_full.at[:, at], up_weight.at[:, at], piece_sems.at[piece, 1]),
            ]

        weight_copies = all_blocks(down_full, None, down_columns, weight, weight_sem)

        def row_copy(chunk):
            slot = lax.rem(chunk, 2)
            return all_blocks(
                inputs, row_slice(chunk, rows), width, row_buf.at[slot], row_sems.at[slot]
            )

        def stores(chunk):
            slot, at = lax.rem(chunk, 2), row_slice(chunk, rows)
            return [
                pltpu.make_async_copy(made.at[slot, which], out.at[at], made_sems.at[slot, which])
                for which, out in enumerate((hidden_out, gate_out, up_out))
            ]

        for item in row_copy(0):
            item.start()
        for piece in range(pieces):
            for item in piece_copies(piece):
                item.start()
        for item in weight_copies:
            item.start()
        greet(True, False)
        gain_grad[...] = jnp.zeros_like(gain_grad)

        def prepare(chunk):
            slot = lax.rem(chunk, 2)
            for item in row_copy(chunk):
                item.wait()

            @pl.when(chunk + 1 < chunks)
            def _():
                for item in row_copy(chunk + 1):
                    item.start()

            @pl.when(chunk >= 2)
            def _():
                for item in stores(chunk - 2):
                    item.wait()

            @pl.loop(0, pieces)
            def _(piece):
                @pl.when(chunk == 0)
                def _():
                    for item in piece_copies(piece):
                        item.wait()

                at = pl.ds(aligned(piece * tile, tile), tile)
                gate = jnp.dot(row_buf[slot], gate_weight[:, at], preferred_element_type=WIDE)
                up = jnp.dot(row_buf[slot], up_weight[:, at], preferred_element_type=WIDE)
                made[slot, 0, :, at] = (gate * jax.nn.sigmoid(gate) * up).astype(LOW)
                made[slot, 1, :, at] = gate.astype(LOW)
                made[slot, 2, :, at] = up.astype(LOW)

            @pl.when(chunk == 0)
            def _():
                for item in weight_copies:
                    item.wait()

            for item in stores(chunk):
                item.start()

        def multiply(chunk, place):
            return jnp.dot(
                made[lax.rem(chunk, 2), 0],
                weight[:, pl.ds(place, width)],
                preferred_element_type=WIDE,
            )

        def up_copy(chunk):
            slot = lax.rem(chunk, 2)
            return pltpu.make_async_copy(
                upstream.at[row_slice(chunk, rows)], up_buf.at[slot], up_sems.at[slot]
            )

        def mixed_copy(chunk):
            return pltpu.make_async_copy(
                mixed.at[row_slice(chunk, rows)], mixed_buf, mixed_sems.at[0]
            )

        def result_copy(chunk):
            slot = lax.rem(chunk, 2)
            return pltpu.make_async_copy(
                result_buf.at[slot], result.at[row_slice(chunk, rows)], result_sems.at[slot]
            )

        def fetch(chunk):
            @pl.when(chunk < chunks)
            def _():
                up_copy(chunk).start()

            @pl.when(chunk >= 1)
            def _():
                mixed_copy(chunk - 1).start()

        def sums(chunk):
            slot = lax.rem(chunk, 2)
            stats.clear(chunk)
            up_copy(chunk).wait()

            def tile(at):
                raw = reduce.raw[at]
                up = up_buf[slot, at].astype(WIDE)
                squares = jnp.sum(raw * raw, axis=1, keepdims=True)
                projected = jnp.sum(gain[...] * up * raw, axis=1, keepdims=True)
                stats.put(chunk, at, squares, projected)

            tiles(rows, tile)
            stats.copy(chunk).start()

        def finish(chunk):
            slot = lax.rem(chunk, 2)
            mixed_copy(chunk).wait()
            stats.copy(chunk).wait_recv()
            spread.clear(chunk)

            @pl.when(chunk >= 2)
            def _():
                result_copy(chunk - 2).wait()

            block = pl.ds(aligned(chip_here() * width, width), width)

            def tile(at):
                squares, projected = stats.get(chunk, at)
                factor = lax.rsqrt(squares / D + EPS)
                raw = reduce.raw[at]
                up = up_buf[slot, at].astype(WIDE)
                pull = factor * factor * factor * projected / D
                spread.put(chunk, at, factor * gain[...] * up - raw * pull)
                gain_grad[...] += jnp.sum(up * raw * factor, axis=0, keepdims=True)
                result_buf[slot, at] = (
                    mixed_buf[at] + reduce.raw[at, block] * factor * gain[:, block]
                ).astype(LOW)

            tiles(rows, tile)
            spread.go(chunk)
            result_copy(chunk).start()

        schedule(chunks, reduce, multiply, fetch, sums, finish, prepare=prepare)
        reduce.end(chunks)
        stats.end(chunks)
        spread.end(chunks)
        for chunk in (chunks - 2, chunks - 1):
            result_copy(chunk).wait()
            for item in stores(chunk):
                item.wait()

    shape = jax.ShapeDtypeStruct
    out = pl.pallas_call(
        kernel,
        out_shape=[
            shape((length, width), LOW),
            shape((2 * chips, length, width), LOW),
            shape((1, half), WIDE),
            shape((length, inner), LOW),
            shape((length, inner), LOW),
            shape((length, inner), LOW),
        ]
        + Reduce.landing(rows, chunks, width, False),
        in_specs=[HBM] * 4 + [VMEM, HBM, HBM],
        out_specs=[HBM, HBM, VMEM] + [HBM] * 5,
        scratch_shapes=[item for group in groups for item in group],
        compiler_params=pltpu.CompilerParams(
            collective_id=collective, has_side_effects=True, vmem_limit_bytes=60 * MIB
        ),
        cost_estimate=pl.CostEstimate(
            flops=6 * length * inner * D, bytes_accessed=16 * length * D, transcendentals=0
        ),
    )(inputs, gate_full, up_full, down_full, gain, mixed, upstream)
    return out[:6]


def mlp_back(gate_grad, up_grad, gate_full, up_full, inputs, gain, upstream, attn_raw, collective):
    length, inner = gate_grad.shape
    half = attn_raw.shape[1]
    chips = lax.axis_size("gx") // 2
    width = half // chips
    count = lax.axis_size("gy")
    chunks = count
    rows = length // chunks
    shard = D // count
    slots, parts = 2, 2

    groups = [
        Reduce.scratch(rows, chunks, width, False),
        Stats.scratch(rows, chunks),
        Spread.scratch(rows, chunks, width),
        RingScatter.scratch(shard, inner, slots, parts),
        [
            pltpu.VMEM((rows, half), LOW),
            pltpu.VMEM((2, rows, half), LOW),
            pltpu.SemaphoreType.DMA((1,)),
            pltpu.SemaphoreType.DMA((2,)),
            pltpu.SemaphoreType.DMA((1,)),
            pltpu.SemaphoreType.DMA((2,)),
        ],
        Columns.scratch(length, shard),
    ]

    def kernel(*refs):
        ins, outs, *scratch = take(refs, [8, 7] + [len(g) for g in groups])
        gate_grad, up_grad, gate_full, up_full, inputs, gain, upstream, attn_raw = ins
        mixed_out, grad_out, gain_grad, gate_out, up_out, core_land, cross_land = outs
        reduce = Reduce(scratch[0], core_land, cross_land, rows, width, False)
        stats = Stats(*scratch[1])
        buffer, local, send, recv = scratch[2]
        spread = Spread(buffer, grad_out, local, send, recv, rows, width)
        total, summed, land, ring_send, ring_recv, credit = scratch[3]
        up_buf, raw_buf, up_sems, raw_sems, mixed_sems, out_sems = scratch[4]
        left = Columns(inputs, shard, *scratch[5])
        grads = (gate_grad, up_grad)

        def product(way, step):
            left.take(ring, way, step)
            tile = 512

            @pl.loop(0, inner // tile)
            def _(index):
                columns = pl.ds(aligned(index * tile, tile), tile)
                total[way, :, columns] = jnp.dot(
                    left.turned[...], grads[way][:, columns], preferred_element_type=WIDE
                )

        ring = RingScatter(
            product, total, summed, land, ring_send, ring_recv, credit, slots, parts
        )
        left.copy(ring.owner(0, 0)).start()
        greet(True, True)
        gain_grad[...] = jnp.zeros_like(gain_grad)

        def multiply(chunk, place):
            at = row_slice(chunk, rows)
            return lax.dot_general(
                gate_grad[at],
                gate_full[pl.ds(place, width)],
                (((1,), (1,)), ((), ())),
                preferred_element_type=WIDE,
            ) + lax.dot_general(
                up_grad[at],
                up_full[pl.ds(place, width)],
                (((1,), (1,)), ((), ())),
                preferred_element_type=WIDE,
            )

        def up_copy(chunk):
            return pltpu.make_async_copy(
                upstream.at[row_slice(chunk, rows)], up_buf, up_sems.at[0]
            )

        def raw_copy(chunk):
            slot = lax.rem(chunk, 2)
            return pltpu.make_async_copy(
                attn_raw.at[row_slice(chunk, rows)], raw_buf.at[slot], raw_sems.at[slot]
            )

        def mixed_copy(chunk):
            return pltpu.make_async_copy(
                reduce.raw.at[:, pl.ds(aligned(chip_here() * width, width), width)],
                mixed_out.at[row_slice(chunk, rows)],
                mixed_sems.at[0],
            )

        def fetch(chunk):
            @pl.when(chunk < chunks)
            def _():
                up_copy(chunk).start()
                raw_copy(chunk).start()

        def sums(chunk):
            slot = lax.rem(chunk, 2)
            stats.clear(chunk)
            up_copy(chunk).wait()
            raw_copy(chunk).wait()

            def tile(at):
                upward = reduce.raw[at] + up_buf[at].astype(WIDE)
                reduce.raw[at] = upward
                raw = raw_buf[slot, at].astype(WIDE)
                squares = jnp.sum(raw * raw, axis=1, keepdims=True)
                projected = jnp.sum(gain[...] * upward * raw, axis=1, keepdims=True)
                stats.put(chunk, at, squares, projected)

            tiles(rows, tile)
            stats.copy(chunk).start()
            mixed_copy(chunk).start()

        def finish(chunk):
            slot = lax.rem(chunk, 2)
            stats.copy(chunk).wait_recv()
            spread.clear(chunk)

            def tile(at):
                squares, projected = stats.get(chunk, at)
                factor = lax.rsqrt(squares / D + EPS)
                upward = reduce.raw[at]
                raw = raw_buf[slot, at].astype(WIDE)
                pull = factor * factor * factor * projected / D
                spread.put(chunk, at, factor * gain[...] * upward - raw * pull)
                gain_grad[...] += jnp.sum(upward * raw * factor, axis=0, keepdims=True)

            tiles(rows, tile)
            spread.go(chunk)
            mixed_copy(chunk).wait()

        schedule(chunks, reduce, multiply, fetch, sums, finish, ring.event, ring.events)
        writes = [
            pltpu.make_async_copy(total.at[way], (gate_out, up_out)[way], out_sems.at[way])
            for way in range(2)
        ]
        for item in writes:
            item.start()
        ring.end()
        reduce.end(chunks)
        stats.end(chunks)
        spread.end(chunks)
        for item in writes:
            item.wait()

    shape = jax.ShapeDtypeStruct
    out = pl.pallas_call(
        kernel,
        out_shape=[
            shape((length, width), WIDE),
            shape((length, D), LOW),
            shape((1, half), WIDE),
            shape((shard, inner), WIDE),
            shape((shard, inner), WIDE),
        ]
        + Reduce.landing(rows, chunks, width, False),
        in_specs=[VMEM, VMEM, VMEM, VMEM, HBM, VMEM, HBM, HBM],
        out_specs=[HBM, HBM, VMEM, HBM, HBM, HBM, HBM],
        scratch_shapes=[item for group in groups for item in group],
        compiler_params=pltpu.CompilerParams(
            collective_id=collective, has_side_effects=True, vmem_limit_bytes=60 * MIB
        ),
        cost_estimate=pl.CostEstimate(
            flops=8 * length * inner * D, bytes_accessed=16 * length * D, transcendentals=0
        ),
    )(gate_grad, up_grad, gate_full, up_full, inputs, gain, upstream, attn_raw)
    return out[:5]


class Total:
    def __init__(self, land, send, recv):
        self.land, self.send, self.recv = land, send, recv
        self.count = lax.axis_size("gx")

    @staticmethod
    def scratch(length):
        others = lax.axis_size("gx") - 1
        return [
            pltpu.VMEM((others, 8, length), WIDE),
            pltpu.SemaphoreType.DMA((others,)),
            pltpu.SemaphoreType.DMA((others,)),
        ]

    def copies(self, mine):
        return [
            remote(
                mine,
                self.land.at[shift - 1],
                self.send.at[shift - 1],
                self.recv.at[shift - 1],
                {"gx": rank_at(shift)},
            )
            for shift in range(1, self.count)
        ]

    def start(self, mine):
        for item in self.copies(mine):
            item.start()

    def finish(self, mine):
        for item in self.copies(mine):
            item.wait()
        total = mine[...]
        for shift in range(1, self.count):
            total = total + self.land[shift - 1]
        return total


def gather_in(tokens, stack, gains, collective):
    length, width = tokens.shape
    _, shard, side = stack.shape
    columns = 2 * side
    count = lax.axis_size("gy")
    chunks = count
    rows = length // chunks
    chips = lax.axis_size("gx") // 2
    parts = 1

    groups = [
        RingGather.scratch(parts),
        [
            pltpu.SemaphoreType.DMA((1,)),
            pltpu.SemaphoreType.DMA((2,)),
            pltpu.SemaphoreType.DMA((chips - 1, chunks, 2)),
            pltpu.SemaphoreType.DMA((chips - 1, chunks, 2)),
        ],
        [
            pltpu.VMEM((D, columns), LOW),
            pltpu.VMEM((2, rows, D), LOW),
            pltpu.VMEM((2, 2, rows, width), WIDE),
            pltpu.VMEM((2, rows, width), LOW),
            pltpu.VMEM((length, STATS), WIDE),
            pltpu.VMEM((8, length), WIDE),
            pltpu.SemaphoreType.DMA((2,)),
            pltpu.SemaphoreType.DMA((2, 2 * chips)),
            pltpu.SemaphoreType.DMA((2, 3)),
        ],
        Total.scratch(length),
        [
            pltpu.VMEM((chips - 1, 8, width), WIDE),
            pltpu.SemaphoreType.DMA((chips - 1, 2)),
        ],
    ]

    def kernel(*refs):
        ins, outs, *scratch = take(refs, [3, 7] + [len(g) for g in groups])
        tokens, stack, gains = ins
        whole, full, query_raw, key_raw, values, squares, halves = outs
        gain_land, gain_sems = scratch[4]
        own_sem, core_sems, cross_sems, pass_sems = scratch[1]
        weight, row_buf, raw_buf, value_buf, stats, mine = scratch[2][:6]
        weight_sem, row_sems, out_sems = scratch[2][6:]
        total = Total(*scratch[3])

        def slot(way, owner, part):
            return full.at[way, pl.ds(aligned(owner * shard, shard), shard)]

        def source(way, part):
            return stack.at[way]

        ring = RingGather(source, slot, parts, *scratch[0])

        def block(rank, chunk):
            if chunk is None:
                return whole.at[rank]
            return whole.at[rank, row_slice(chunk, rows)]

        here = lax.axis_index("gx")
        own = pltpu.make_async_copy(tokens, block(here, None), own_sem.at[0])
        core = remote(
            tokens, block(here, None), core_sems.at[0], core_sems.at[1], {"gx": other_core()}
        )

        def cross(shift, chunk):
            return remote(
                tokens.at[row_slice(chunk, rows)],
                block(here, chunk),
                cross_sems.at[shift - 1, chunk, 0],
                cross_sems.at[shift - 1, chunk, 1],
                {"gx": peer_at(shift)},
            )

        def onward(shift, chunk):
            spot = block(peer_at(chips - shift), chunk)
            return remote(
                spot,
                spot,
                pass_sems.at[shift - 1, chunk, 0],
                pass_sems.at[shift - 1, chunk, 1],
                {"gx": other_core()},
            )

        gain_copies = [
            remote(
                gains,
                gain_land.at[shift - 1],
                gain_sems.at[shift - 1, 0],
                gain_sems.at[shift - 1, 1],
                {"gx": peer_at(shift)},
            )
            for shift in range(1, chips)
        ]
        own.start()
        greet("all", True)
        for item in gain_copies:
            item.start()
        ring.begin()

        def send(chunk):
            for shift in range(1, chips):
                cross(shift, chunk).start()

        loop(chunks, send)
        core.start()

        def step(chunk):
            for shift in range(1, chips):
                cross(shift, chunk).wait_recv()
                onward(shift, chunk).start()

            @pl.when(chunk < ring.events)
            def _():
                ring.event(chunk)

        loop(chunks, step)
        ring.end()
        fetches = all_blocks(full, None, side, weight, weight_sem)
        for item in fetches:
            item.start()

        def drain(chunk):
            for shift in range(1, chips):
                cross(shift, chunk).wait_send()
                onward(shift, chunk).wait()

        loop(chunks, drain)
        own.wait()
        core.wait()

        def row_copy(chunk):
            slot = lax.rem(chunk, 2)
            return all_blocks(
                whole, row_slice(chunk, rows), width, row_buf.at[slot], row_sems.at[slot]
            )

        def stores(chunk):
            slot, at = lax.rem(chunk, 2), row_slice(chunk, rows)
            return [
                pltpu.make_async_copy(raw_buf.at[slot, 0], query_raw.at[at], out_sems.at[slot, 0]),
                pltpu.make_async_copy(raw_buf.at[slot, 1], key_raw.at[at], out_sems.at[slot, 1]),
                pltpu.make_async_copy(value_buf.at[slot], values.at[at], out_sems.at[slot, 2]),
            ]

        for item in row_copy(0):
            item.start()
        for item in fetches:
            item.wait()
        lane = lax.broadcasted_iota(jnp.int32, (rows, STATS), 1)

        def project(chunk):
            slot = lax.rem(chunk, 2)
            for item in row_copy(chunk):
                item.wait()

            @pl.when(chunk + 1 < chunks)
            def _():
                for item in row_copy(chunk + 1):
                    item.start()

            @pl.when(chunk >= 2)
            def _():
                for item in stores(chunk - 2):
                    item.wait()

            some = []
            for which in range(2):
                raw = jnp.dot(
                    row_buf[slot],
                    weight[:, which * width : (which + 1) * width],
                    preferred_element_type=WIDE,
                )
                raw_buf[slot, which] = raw
                some.append(jnp.sum(raw * raw, axis=1, keepdims=True))
            value_buf[slot] = jnp.dot(
                row_buf[slot], weight[:, 2 * width :], preferred_element_type=WIDE
            ).astype(LOW)
            stats[row_slice(chunk, rows)] = jnp.where(lane == 0, some[0], some[1])
            for item in stores(chunk):
                item.start()

        loop(chunks, project)
        mine[...] = stats[...].T[:8]
        total.start(mine)
        for chunk in (chunks - 2, chunks - 1):
            for item in stores(chunk):
                item.wait()
        squares[...] = total.finish(mine)
        halves[:, pl.ds(aligned(chip_here() * width, width), width)] = gains[...]
        for shift in range(1, chips):
            gain_copies[shift - 1].wait()
            chip = lax.rem(chip_here() + chips - shift, chips)
            halves[:, pl.ds(aligned(chip * width, width), width)] = gain_land[shift - 1]

    shape = jax.ShapeDtypeStruct
    return pl.pallas_call(
        kernel,
        out_shape=[
            shape((2 * chips, length, width), LOW),
            shape((2, shard * count, side), LOW),
            shape((length, width), WIDE),
            shape((length, width), WIDE),
            shape((length, width), LOW),
            shape((8, length), WIDE),
            shape((8, chips * width), WIDE),
        ],
        in_specs=[HBM, HBM, VMEM],
        out_specs=[HBM] * 5 + [VMEM, VMEM],
        scratch_shapes=[item for group in groups for item in group],
        compiler_params=pltpu.CompilerParams(
            collective_id=collective, has_side_effects=True, vmem_limit_bytes=40 * MIB
        ),
        cost_estimate=pl.CostEstimate(
            flops=2 * length * columns * D, bytes_accessed=8 * length * D, transcendentals=0
        ),
    )(tokens, stack, gains)


def hidden_back(blocks, slots_of_weight, hidden, gate, up, collective):
    length, inner = hidden.shape
    count = lax.axis_size("gy")
    chunks = count
    rows = length // chunks
    shard = D // count
    side = inner // 2
    slots, parts = count - 1, 2
    tile = min(512, inner)

    groups = [
        RingScatter.scratch(shard, side, slots, parts),
        [
            pltpu.VMEM((2, 2, rows, inner), LOW),
            pltpu.VMEM((2, 2, rows, inner), LOW),
            pltpu.SemaphoreType.DMA((2, 2)),
            pltpu.SemaphoreType.DMA((2, 2)),
            pltpu.SemaphoreType.DMA((2,)),
            pltpu.VMEM((shard, length), LOW),
        ],
        [
            pltpu.VMEM((length, D), LOW),
            pltpu.VMEM((inner, D), LOW),
            pltpu.SemaphoreType.DMA((blocks.shape[0],)),
            pltpu.SemaphoreType.DMA((count,)),
        ],
    ]

    def kernel(*refs):
        ins, outs, *scratch = take(refs, [5, 3] + [len(g) for g in groups])
        blocks, slots_of_weight, hidden, gate, up = ins
        grad, weight, grad_sems, weight_sems = scratch[2]
        gate_grad, up_grad, weight_grad = outs
        total, summed, land, ring_send, ring_recv, credit = scratch[0]
        given, made, given_sems, made_sems, out_sems, turned = scratch[1]

        def product(way, step):
            columns = pl.ds(aligned(ring.owner(way, step) * shard, shard), shard)
            turned[...] = grad[:, columns].T
            size = min(512, side)

            @pl.loop(0, side // size)
            def _(index):
                at = pl.ds(aligned(index * size, size), size)
                take_at = pl.ds(aligned(way * side + index * size, size), size)
                total[way, :, at] = jnp.dot(
                    turned[...], hidden[:, take_at], preferred_element_type=WIDE
                )

        ring = RingScatter(
            product, total, summed, land, ring_send, ring_recv, credit, slots, parts
        )

        def load(chunk):
            slot = lax.rem(chunk, 2)
            return [
                pltpu.make_async_copy(
                    (gate, up)[which].at[row_slice(chunk, rows)],
                    given.at[slot, which],
                    given_sems.at[slot, which],
                )
                for which in range(2)
            ]

        def store(chunk):
            slot = lax.rem(chunk, 2)
            return [
                pltpu.make_async_copy(
                    made.at[slot, which],
                    (gate_grad, up_grad)[which].at[row_slice(chunk, rows)],
                    made_sems.at[slot, which],
                )
                for which in range(2)
            ]

        grad_copies = all_blocks(blocks, None, blocks.shape[2], grad, grad_sems)
        weight_copies = all_blocks(slots_of_weight, None, shard, weight, weight_sems)
        for item in grad_copies + weight_copies + load(0):
            item.start()
        greet(False, True)
        for item in grad_copies:
            item.wait()

        def iteration(step):
            slot = lax.rem(step, 2)
            for part in range(parts):
                ring.event(step * parts + part)

            @pl.when(step + 1 < chunks)
            def _():
                for item in load(step + 1):
                    item.start()

            @pl.when(step >= 2)
            def _():
                for item in store(step - 2):
                    item.wait()

            for item in load(step):
                item.wait()

            @pl.when(step == 0)
            def _():
                for item in weight_copies:
                    item.wait()

            @pl.loop(0, inner // tile)
            def _(index):
                at = pl.ds(aligned(index * tile, tile), tile)
                hidden_grad = lax.dot_general(
                    grad[row_slice(step, rows)],
                    weight[at],
                    (((1,), (1,)), ((), ())),
                    preferred_element_type=WIDE,
                )
                gate = given[slot, 0, :, at].astype(WIDE)
                up = given[slot, 1, :, at].astype(WIDE)
                sigma = jax.nn.sigmoid(gate)
                made[slot, 0, :, at] = (
                    hidden_grad * up * sigma * (1.0 + gate * (1.0 - sigma))
                ).astype(LOW)
                made[slot, 1, :, at] = (hidden_grad * gate * sigma).astype(LOW)

            for item in store(step):
                item.start()

        loop(chunks, iteration)
        writes = [
            pltpu.make_async_copy(
                total.at[way], weight_grad.at[:, way * side : (way + 1) * side], out_sems.at[way]
            )
            for way in range(2)
        ]
        for item in writes:
            item.start()
        for chunk in (chunks - 2, chunks - 1):
            for item in store(chunk):
                item.wait()
        ring.end()
        for item in writes:
            item.wait()

    shape = jax.ShapeDtypeStruct
    return pl.pallas_call(
        kernel,
        out_shape=[
            shape((length, inner), LOW),
            shape((length, inner), LOW),
            shape((shard, inner), WIDE),
        ],
        in_specs=[HBM, HBM, VMEM, HBM, HBM],
        out_specs=[HBM, HBM, HBM],
        scratch_shapes=[item for group in groups for item in group],
        compiler_params=pltpu.CompilerParams(
            collective_id=collective, has_side_effects=True, vmem_limit_bytes=60 * MIB
        ),
        cost_estimate=pl.CostEstimate(
            flops=4 * length * inner * D, bytes_accessed=16 * length * D, transcendentals=0
        ),
    )(blocks, slots_of_weight, hidden, gate, up)


def attn_in_back(
    query_back,
    key_back,
    value_grad,
    query_raw,
    key_raw,
    factors,
    projections,
    query_gain,
    key_gain,
    stack,
    inputs,
    mixed_grad,
    gain_parts,
    collective,
):
    length, columns = value_grad.shape[0], 2 * stack.shape[2]
    width = mixed_grad.shape[1]
    count = lax.axis_size("gy")
    chunks = count
    rows = length // chunks
    shard = D // count
    side = columns // 2
    slots, parts = count - 1, 2
    tile = 256 if side % 256 == 0 else 128

    groups = [
        Reduce.scratch(rows, chunks, width, True),
        RingScatter.scratch(shard, side, slots, parts),
        [
            pltpu.VMEM((rows, width), WIDE),
            pltpu.VMEM((2, rows, width), WIDE),
            pltpu.VMEM((length, columns), LOW),
            pltpu.VMEM((length, STATS), WIDE),
            pltpu.SemaphoreType.DMA((1,)),
            pltpu.SemaphoreType.DMA((2,)),
            pltpu.SemaphoreType.DMA((2,)),
        ],
        Columns.scratch(length, shard),
        Total.scratch(length),
        [
            pltpu.VMEM((8, width), WIDE),
            pltpu.VMEM((count - 1, 8, width), WIDE),
            pltpu.SemaphoreType.DMA((count - 1, 2)),
        ],
    ]

    def kernel(*refs):
        ins, outs, *scratch = take(refs, [16, 5] + [len(g) for g in groups])
        query_back, key_back, value_grad, query_raw, key_raw, factors = ins[:6]
        projections, query_gain, key_gain, stack, inputs, mixed_grad = ins[6:12]
        gain_parts = ins[12:]
        token_grad, weight_grad, gain_grads, core_land, cross_land = outs
        gain_mine, gain_land, gain_sems = scratch[5]
        reduce = Reduce(scratch[0], core_land, cross_land, rows, width, True)
        total, summed, land, ring_send, ring_recv, credit = scratch[1]
        mixed_buf, token_buf, grads, projected, mixed_sems, token_sems, out_sems = scratch[2]
        left = Columns(inputs, shard, *scratch[3])
        total_sum = Total(*scratch[4])

        def product(way, step):
            left.take(ring, way, step)

            @pl.loop(0, side // tile)
            def _(index):
                at = pl.ds(aligned(index * tile, tile), tile)
                take_at = pl.ds(aligned(way * side + index * tile, tile), tile)
                total[way, :, at] = jnp.dot(
                    left.turned[...], grads[:, take_at], preferred_element_type=WIDE
                )

        ring = RingScatter(
            product, total, summed, land, ring_send, ring_recv, credit, slots, parts
        )
        left.copy(ring.owner(0, 0)).start()
        chip_columns = pl.ds(aligned(chip_here() * width, width), width)
        gain_mine[...] = jnp.zeros_like(gain_mine)
        for which, part in enumerate(gain_parts):
            gain_mine[which : which + 1] = part[...] if which < 2 else part[:, chip_columns]
        greet("all", False, True)
        total_sum.start(projections)
        gain_copies = [
            remote(
                gain_mine,
                gain_land.at[shift - 1],
                gain_sems.at[shift - 1, 0],
                gain_sems.at[shift - 1, 1],
                {"gy": block_at(shift)},
            )
            for shift in range(1, count)
        ]
        for item in gain_copies:
            item.start()
        grads[:, 2 * width :] = value_grad[...]
        sums_here = total_sum.finish(projections)
        projected[...] = jnp.concatenate([sums_here] * (STATS // 8), axis=0).T
        pairs = ((query_back, query_raw, query_gain), (key_back, key_raw, key_gain))

        @pl.loop(0, length // 32)
        def _(index):
            at = row_slice(index, 32)
            for which, (back, raw, gain) in enumerate(pairs):
                factor = factors[at, which : which + 1]
                pull = factor * factor * factor * projected[at, which : which + 1] / D
                grads[at, which * width : (which + 1) * width] = (
                    factor * gain[...] * back[at] - raw[at] * pull
                ).astype(LOW)

        def multiply(chunk, place):
            at = row_slice(chunk, rows)
            return nt(grads[at, :side], stack[0, pl.ds(place, width)]) + nt(
                grads[at, side:], stack[1, pl.ds(place, width)]
            )

        def mixed_copy(chunk):
            return pltpu.make_async_copy(
                mixed_grad.at[row_slice(chunk, rows)], mixed_buf, mixed_sems.at[0]
            )

        def token_copy(chunk):
            slot = lax.rem(chunk, 2)
            return pltpu.make_async_copy(
                token_buf.at[slot], token_grad.at[row_slice(chunk, rows)], token_sems.at[slot]
            )

        def fetch(chunk):
            @pl.when(chunk >= 1)
            def _():
                mixed_copy(chunk - 1).start()

        def sums(chunk):
            pass

        def finish(chunk):
            slot = lax.rem(chunk, 2)
            mixed_copy(chunk).wait()

            @pl.when(chunk >= 2)
            def _():
                token_copy(chunk - 2).wait()

            def some(at):
                token_buf[slot, at] = mixed_buf[at] + reduce.raw[at]

            tiles(rows, some)
            token_copy(chunk).start()

        schedule(chunks, reduce, multiply, fetch, sums, finish, ring.event, ring.events)
        writes = [
            pltpu.make_async_copy(
                total.at[way], weight_grad.at[:, way * side : (way + 1) * side], out_sems.at[way]
            )
            for way in range(2)
        ]
        for item in writes:
            item.start()
        gain_total = gain_mine[...]
        for shift in range(1, count):
            gain_copies[shift - 1].wait()
            gain_total = gain_total + gain_land[shift - 1]
        gain_grads[...] = gain_total
        ring.end()
        reduce.end(chunks)
        for chunk in (chunks - 2, chunks - 1):
            token_copy(chunk).wait()
        for item in writes:
            item.wait()

    shape = jax.ShapeDtypeStruct
    out = pl.pallas_call(
        kernel,
        out_shape=[
            shape((length, width), WIDE),
            shape((shard, columns), WIDE),
            shape((8, width), WIDE),
        ]
        + Reduce.landing(rows, chunks, width, True),
        in_specs=[VMEM] * 10 + [HBM, HBM] + [VMEM] * 4,
        out_specs=[HBM, HBM, VMEM, HBM, HBM],
        scratch_shapes=[item for group in groups for item in group],
        compiler_params=pltpu.CompilerParams(
            collective_id=collective, has_side_effects=True, vmem_limit_bytes=60 * MIB
        ),
        cost_estimate=pl.CostEstimate(
            flops=4 * length * columns * D, bytes_accessed=8 * length * D, transcendentals=0
        ),
    )(
        query_back,
        key_back,
        value_grad,
        query_raw,
        key_raw,
        factors,
        projections,
        query_gain,
        key_gain,
        stack,
        inputs,
        mixed_grad,
        *gain_parts,
    )
    return out[:3]


def token_positions(segment):
    length = segment.shape[0]
    labels = jnp.arange(SEGS, dtype=jnp.int32)
    member = (segment[:, None] == labels[None, :]).astype(jnp.int32)
    totals = jnp.sum(member, axis=0)
    starts = jnp.cumsum(totals) - totals
    opening = jnp.sum(member * starts[None, :], axis=1)
    return jnp.arange(length, dtype=jnp.int32) - opening


def rotary_tables(segment):
    place = token_positions(segment).astype(jnp.float32)
    halves = HEAD // 2
    inverse = jnp.exp(jnp.arange(halves, dtype=jnp.float32) * (-2.0 * math.log(THETA) / HEAD))
    angle = place[:, None] * inverse[None, :]
    return (jnp.cos(angle), jnp.sin(angle))


BLOCK = 256
LANES = 128
SCALE = 1.0 / math.sqrt(HEAD)
SCALE_TWO = SCALE * math.log2(math.e)


def turn(values, cosine, sine):
    return values * cosine + pltpu.roll(values, HEAD // 2, 1) * sine


def head_columns(head):
    return slice(head * HEAD, (head + 1) * HEAD)


def nt(left, right):
    return lax.dot_general(left, right, (((1,), (1,)), ((), ())), preferred_element_type=WIDE)


def attend(first_block, query_raw, key_raw, values, factors, query_gain, key_gain, tables, starts):
    length, width = query_raw.shape
    heads = width // HEAD

    def kernel(
        first_block,
        query_raw,
        key_raw,
        values,
        factors,
        query_gain,
        key_gain,
        cosine,
        sine,
        starts,
        queries,
        keys,
        attended,
        peaks,
        peak_columns,
    ):
        @pl.loop(0, length // BLOCK)
        def _(index):
            at = row_slice(index, BLOCK)
            cos, sin = cosine[at], sine[at]
            pairs = ((query_raw, query_gain, queries), (key_raw, key_gain, keys))
            for which, (raw, gain, out) in enumerate(pairs):
                factor = factors[at, which : which + 1]
                for head in range(heads):
                    columns = head_columns(head)
                    normed = raw[at, columns] * factor * gain[:, columns]
                    out[at, columns] = turn(normed, cos, sin).astype(LOW)

        lane = lax.broadcasted_iota(jnp.int32, (BLOCK, LANES), 1)
        row_index = lax.broadcasted_iota(jnp.int32, (BLOCK, BLOCK), 0)
        column_index = lax.broadcasted_iota(jnp.int32, (BLOCK, BLOCK), 1)

        def query_block(index):
            at = row_slice(index, BLOCK)
            start = starts[at]

            def key_block(other, carry):
                there = row_slice(other, BLOCK)
                key_place = column_index + other * BLOCK
                allowed = (key_place >= start) & (key_place <= row_index + index * BLOCK)
                made = []
                for head in range(heads):
                    columns = head_columns(head)
                    peak, total, rows = carry[head]
                    scores = nt(queries[at, columns], keys[there, columns]) * SCALE_TWO
                    scores = jnp.where(allowed, scores, NEGATIVE)
                    higher = jnp.maximum(peak, jnp.max(scores, axis=1, keepdims=True))
                    raised = jnp.exp2(scores - higher)
                    shrink = jnp.exp2(peak - higher)
                    total = total * shrink + jnp.sum(raised, axis=1, keepdims=True)
                    rows = rows * shrink + jnp.dot(
                        raised.astype(LOW), values[there, columns], preferred_element_type=WIDE
                    )
                    made.append((higher, total, rows))
                return tuple(made)

            empty = (
                jnp.full((BLOCK, 1), NEGATIVE, WIDE),
                jnp.zeros((BLOCK, 1), WIDE),
                jnp.zeros((BLOCK, HEAD), WIDE),
            )
            done = lax.fori_loop(first_block[index], index + 1, key_block, (empty,) * heads)
            column = jnp.zeros((BLOCK, LANES), WIDE)
            for head in range(heads):
                peak, total, rows = done[head]
                attended[at, head_columns(head)] = (rows / total).astype(LOW)
                column = jnp.where(lane == head, peak + jnp.log2(total), column)
            peak_columns[at] = column

        loop(length // BLOCK, query_block)
        peaks[...] = peak_columns[...].T[:8]

    shape = jax.ShapeDtypeStruct
    smem = pl.BlockSpec(memory_space=pltpu.SMEM)
    return pl.pallas_call(
        kernel,
        out_shape=[
            shape((length, width), LOW),
            shape((length, width), LOW),
            shape((length, width), LOW),
            shape((8, length), WIDE),
        ],
        in_specs=[smem] + [VMEM] * 9,
        out_specs=[VMEM] * 4,
        scratch_shapes=[pltpu.VMEM((length, LANES), WIDE)],
        compiler_params=pltpu.CompilerParams(vmem_limit_bytes=48 * MIB),
        cost_estimate=pl.CostEstimate(
            flops=2 * length * MAX_LEN * width,
            bytes_accessed=16 * length * width,
            transcendentals=length * MAX_LEN * heads // 2,
        ),
    )(first_block, query_raw, key_raw, values, factors, query_gain, key_gain, *tables, starts)


def attend_back(
    last_block,
    queries,
    keys,
    values,
    attended,
    upstream,
    peaks,
    query_raw,
    key_raw,
    factors,
    query_gain,
    key_gain,
    tables,
    start_row,
):
    length, width = query_raw.shape
    heads = width // HEAD

    def kernel(
        last_block,
        queries,
        keys,
        values,
        attended,
        upstream,
        peaks,
        query_raw,
        key_raw,
        factors,
        query_gain,
        key_gain,
        cosine,
        sine,
        start_row,
        query_out,
        key_out,
        value_out,
        projections,
        query_gain_grad,
        key_gain_grad,
        query_sum,
        key_sum,
        value_sum,
        columns_scratch,
        deltas,
    ):
        lane = lax.broadcasted_iota(jnp.int32, (BLOCK, LANES), 1)
        query_gain_grad[...] = jnp.zeros_like(query_gain_grad)
        key_gain_grad[...] = jnp.zeros_like(key_gain_grad)

        def prepare(index):
            at = row_slice(index, BLOCK)
            column = jnp.zeros((BLOCK, LANES), WIDE)
            for head in range(heads):
                columns = head_columns(head)
                delta = jnp.sum(
                    attended[at, columns].astype(WIDE) * upstream[at, columns].astype(WIDE),
                    axis=1,
                    keepdims=True,
                )
                column = jnp.where(lane == head, delta, column)
            columns_scratch[at] = column
            query_sum[at] = jnp.zeros((BLOCK, width), WIDE)

        loop(length // BLOCK, prepare)
        deltas[...] = columns_scratch[...].T[:8]
        row_index = lax.broadcasted_iota(jnp.int32, (BLOCK, BLOCK), 0)
        column_index = lax.broadcasted_iota(jnp.int32, (BLOCK, BLOCK), 1)

        def turn_back(at, summed, raw, gain, factor, out, gain_grad):
            cos, sin = cosine[at], sine[at]
            share = jnp.zeros((BLOCK, 1), WIDE)
            for head in range(heads):
                columns = head_columns(head)
                normed = turn(summed(head) * SCALE, cos, -sin)
                out[at, columns] = normed
                weighed = normed * raw[at, columns]
                share += jnp.sum(gain[:, columns] * weighed, axis=1, keepdims=True)
                gain_grad[:, columns] += jnp.sum(weighed * factor, axis=0, keepdims=True)
            return share

        def key_block(index):
            at = row_slice(index, BLOCK)
            key_sum[...] = jnp.zeros_like(key_sum)
            value_sum[...] = jnp.zeros_like(value_sum)

            def query_block(other, carry):
                there = row_slice(other, BLOCK)
                key_place = row_index + index * BLOCK
                allowed = (key_place >= start_row[:, there]) & (
                    key_place <= column_index + other * BLOCK
                )
                for head in range(heads):
                    columns = head_columns(head)
                    scores = nt(keys[at, columns], queries[there, columns]) * SCALE_TWO
                    scores = jnp.where(allowed, scores, NEGATIVE)
                    chance = jnp.exp2(scores - peaks[head : head + 1, there])
                    value_sum[:, columns] += jnp.dot(
                        chance.astype(LOW), upstream[there, columns], preferred_element_type=WIDE
                    )
                    chance_grad = nt(values[at, columns], upstream[there, columns])
                    score_grad = (chance * (chance_grad - deltas[head : head + 1, there])).astype(LOW)
                    key_sum[:, columns] += jnp.dot(
                        score_grad, queries[there, columns], preferred_element_type=WIDE
                    )
                    query_sum[there, columns] += lax.dot_general(
                        score_grad,
                        keys[at, columns],
                        (((0,), (0,)), ((), ())),
                        preferred_element_type=WIDE,
                    )
                return carry

            lax.fori_loop(index, last_block[index] + 1, query_block, 0)
            value_out[at] = value_sum[...].astype(LOW)
            share = turn_back(
                at,
                lambda head: key_sum[:, head_columns(head)],
                key_raw,
                key_gain,
                factors[at, 1:2],
                key_out,
                key_gain_grad,
            )
            columns_scratch[at] = jnp.where(lane == 1, share, 0.0)

        loop(length // BLOCK, key_block)

        def finish(index):
            at = row_slice(index, BLOCK)
            share = turn_back(
                at,
                lambda head: query_sum[at, head_columns(head)],
                query_raw,
                query_gain,
                factors[at, 0:1],
                query_out,
                query_gain_grad,
            )
            columns_scratch[at] += jnp.where(lane == 0, share, 0.0)

        loop(length // BLOCK, finish)
        projections[...] = columns_scratch[...].T[:8]

    shape = jax.ShapeDtypeStruct
    smem = pl.BlockSpec(memory_space=pltpu.SMEM)
    return pl.pallas_call(
        kernel,
        out_shape=[
            shape((length, width), WIDE),
            shape((length, width), WIDE),
            shape((length, width), LOW),
            shape((8, length), WIDE),
            shape((1, width), WIDE),
            shape((1, width), WIDE),
        ],
        in_specs=[smem] + [VMEM] * 14,
        out_specs=[VMEM] * 6,
        scratch_shapes=[
            pltpu.VMEM((length, width), WIDE),
            pltpu.VMEM((BLOCK, width), WIDE),
            pltpu.VMEM((BLOCK, width), WIDE),
            pltpu.VMEM((length, LANES), WIDE),
            pltpu.VMEM((8, length), WIDE),
        ],
        compiler_params=pltpu.CompilerParams(vmem_limit_bytes=52 * MIB),
        cost_estimate=pl.CostEstimate(
            flops=5 * length * MAX_LEN * width,
            bytes_accessed=32 * length * width,
            transcendentals=length * MAX_LEN * heads // 2,
        ),
    )(
        last_block,
        queries,
        keys,
        values,
        attended,
        upstream,
        peaks,
        query_raw,
        key_raw,
        factors,
        query_gain,
        key_gain,
        *tables,
        start_row,
    )


def shards(
    tokens,
    query_weight,
    key_weight,
    value_weight,
    output_weight,
    gate_weight,
    up_weight,
    down_weight,
    query_gain,
    key_gain,
    attn_gain,
    mlp_gain,
    seq_ids,
    out_grad,
):
    segment = seq_ids[0]
    length = tokens.shape[0]
    local_width = tokens.shape[1]
    cosine, sine = rotary_tables(segment)
    tables = (
        jnp.concatenate([cosine, cosine], axis=1),
        jnp.concatenate([-sine, sine], axis=1),
    )
    order = jnp.arange(length, dtype=jnp.int32)
    starts = order - token_positions(segment)
    blocks = length // BLOCK
    first_block = starts.reshape(blocks, BLOCK)[:, 0] // BLOCK
    closing = segment.reshape(blocks, BLOCK)[:, -1]
    ends = jnp.sum((segment[None, :] <= closing[:, None]).astype(jnp.int32), axis=1) - 1
    last_block = ends // BLOCK
    gains = jnp.concatenate([attn_gain[None], mlp_gain[None], jnp.zeros((6, local_width))], axis=0)
    query_gain, key_gain = query_gain.reshape(1, -1), key_gain.reshape(1, -1)
    middle = local_width // 2
    pairs = (
        (query_weight, key_weight[:, :middle]),
        (key_weight[:, middle:], value_weight),
    )
    inputs, attn_stack, query_raw, key_raw, values, squares, halves = gather_in(
        tokens, jnp.stack([jnp.concatenate(pair, axis=1) for pair in pairs]), gains, 1
    )
    attn_half, mlp_half = halves[:1], halves[1:2]
    squares, output_weight = lax.optimization_barrier((squares, output_weight))
    output_full = lax.all_gather(output_weight, "gy", axis=1, tiled=True)
    factors = lax.rsqrt(squares[:2].T / D + EPS)
    queries, keys, attended, peaks = attend(
        first_block,
        query_raw,
        key_raw,
        values,
        factors,
        query_gain,
        key_gain,
        tables,
        starts[:, None],
    )
    attn_raw, mixed, mlp_inputs, gate_full, up_full, down_full, upstream = attn_out(
        attended, output_full, attn_half, inputs, out_grad, gate_weight, up_weight, down_weight, 2
    )
    result, mlp_full, mlp_gain_part, hidden, gate, up = mlp_forward(
        mlp_inputs, gate_full, up_full, down_full, mlp_half, mixed, upstream, 3
    )
    gate_grad, up_grad, down_turned = hidden_back(mlp_full, down_full, hidden, gate, up, 4)
    down_weight_grad = down_turned.T
    mixed_grad, attn_full, attn_gain_part, gate_weight_grad, up_weight_grad = mlp_back(
        gate_grad, up_grad, gate_full, up_full, mlp_inputs, attn_half, upstream, attn_raw, 5
    )
    output_product = lax.dot_general(
        attended, attn_full, (((0,), (0,)), ((), ())), preferred_element_type=jnp.float32
    )
    output_weight_grad = lax.psum_scatter(
        output_product.astype(jnp.bfloat16), "gy", scatter_dimension=1, tiled=True
    ).astype(jnp.float32)
    attended_grad = lax.dot_general(
        attn_full, output_full, (((1,), (1,)), ((), ())), preferred_element_type=jnp.float32
    ).astype(jnp.bfloat16)
    query_back, key_back, value_grad, projections, query_gain_part, key_gain_part = attend_back(
        last_block,
        queries,
        keys,
        values,
        attended,
        attended_grad,
        peaks,
        query_raw,
        key_raw,
        factors,
        query_gain,
        key_gain,
        tables,
        starts[None, :],
    )
    token_grad, attn_weight_grads, gain_grads = attn_in_back(
        query_back,
        key_back,
        value_grad,
        query_raw,
        key_raw,
        factors,
        projections,
        query_gain,
        key_gain,
        attn_stack,
        inputs,
        mixed_grad,
        (query_gain_part, key_gain_part, attn_gain_part, mlp_gain_part),
        6,
    )
    query_weight_grad = attn_weight_grads[:, :local_width]
    key_weight_grad = attn_weight_grads[:, local_width : 2 * local_width]
    value_weight_grad = attn_weight_grads[:, 2 * local_width :]
    query_gain_grad, key_gain_grad, attn_gain_grad, mlp_gain_grad = (gain_grads[i] for i in range(4))
    return (
        result,
        token_grad,
        query_weight_grad,
        key_weight_grad,
        value_weight_grad,
        output_weight_grad,
        gate_weight_grad,
        up_weight_grad,
        down_weight_grad,
        query_gain_grad,
        key_gain_grad,
        attn_gain_grad,
        mlp_gain_grad,
    )


def solution(mesh):
    return jax.shard_map(
        shards,
        mesh=mesh,
        in_specs=(
            P("gy", "gx"),
            P("gy", "gx"),
            P("gy", "gx"),
            P("gy", "gx"),
            P("gx", "gy"),
            P("gy", "gx"),
            P("gy", "gx"),
            P("gx", "gy"),
            P("gx"),
            P("gx"),
            P("gx"),
            P("gx"),
            P("gy", None),
            P("gy", "gx"),
        ),
        out_specs=(
            P("gy", "gx"),
            P("gy", "gx"),
            P("gy", "gx"),
            P("gy", "gx"),
            P("gy", "gx"),
            P("gx", "gy"),
            P("gy", "gx"),
            P("gy", "gx"),
            P("gx", "gy"),
            P("gx"),
            P("gx"),
            P("gx"),
            P("gx"),
        ),
        check_vma=False,
    )
```

```python
import math

import jax
import jax.numpy as jnp
from jax import lax
from jax.experimental import pallas as pl
from jax.experimental.pallas import tpu as pltpu
from jax.sharding import PartitionSpec as P

D = 2048
HEAD = 128
MAX_LEN = 1024
SEGS = 4


EPS = 1e-06
THETA = 500000.0
NEGATIVE = -1e30


MESH = pl.DeviceIdType.MESH
HBM = pl.BlockSpec(memory_space=pltpu.HBM)
VMEM = pl.BlockSpec(memory_space=pltpu.VMEM)
LOW = jnp.bfloat16
WIDE = jnp.float32
MIB = 1 << 20
LAG = 2
STATS = 128


def core_here():
    return lax.rem(lax.axis_index("gx"), 2)


def chip_here():
    return lax.div(lax.axis_index("gx"), 2)


def other_core():
    return lax.axis_index("gx") + 1 - 2 * core_here()


def peer_at(shift):
    return lax.rem(lax.axis_index("gx") + 2 * shift, lax.axis_size("gx"))


def rank_at(shift):
    return lax.rem(lax.axis_index("gx") + shift, lax.axis_size("gx"))


def block_at(shift):
    return lax.rem(lax.axis_index("gy") + shift, lax.axis_size("gy"))


def ring_place():
    count = lax.axis_size("gy")
    index = lax.axis_index("gy")
    row, side = lax.div(index, 2), lax.rem(index, 2)
    return side * row + (1 - side) * (count - 1 - row)


def ring_device(place):
    count = lax.axis_size("gy")
    place = lax.rem(place + 2 * count, count)
    back = lax.div(place, count // 2)
    row = (1 - back) * place + back * (count - 1 - place)
    return 2 * row + 1 - back


def greet(gx, ring, all_blocks=False):
    barrier = pltpu.get_barrier_semaphore()
    partners = []
    if all_blocks:
        partners += [{"gy": block_at(k)} for k in range(1, lax.axis_size("gy"))]
    if gx == "all":
        partners += [{"gx": rank_at(k)} for k in range(1, lax.axis_size("gx"))]
    elif gx:
        partners.append({"gx": other_core()})
        partners += [{"gx": peer_at(k)} for k in range(1, lax.axis_size("gx") // 2)]
    if ring:
        place = ring_place()
        partners += [{"gy": ring_device(place + 1)}, {"gy": ring_device(place - 1)}]
    for partner in partners:
        pl.semaphore_signal(barrier, inc=1, device_id=partner, device_id_type=MESH)
    pl.semaphore_wait(barrier, len(partners))


def remote(source, target, send, recv, device):
    return pltpu.make_async_remote_copy(
        src_ref=source,
        dst_ref=target,
        send_sem=send,
        recv_sem=recv,
        device_id=device,
        device_id_type=MESH,
    )


def loop(count, body):
    def step(index, carry):
        body(index)
        return carry

    lax.fori_loop(0, count, step, 0)


def aligned(value, factor):
    return pl.multiple_of(value, factor)


class RingGather:
    def __init__(self, sources, slot, spill, parts, send, recv, local, spilled):
        self.sources, self.slot, self.spill, self.parts = sources, slot, spill, parts
        self.send, self.recv, self.local, self.spilled = send, recv, local, spilled
        self.count = lax.axis_size("gy")

    @staticmethod
    def scratch(parts):
        count = lax.axis_size("gy")
        return [
            pltpu.SemaphoreType.DMA((count - 1, 2, parts)),
            pltpu.SemaphoreType.DMA((count - 1, 2, parts)),
            pltpu.SemaphoreType.DMA((2, parts)),
            pltpu.SemaphoreType.DMA((count, 2, parts)),
        ]

    def spill_copy(self, way, step, part):
        place = ring_place()
        owner = ring_device(place - (1 - 2 * way) * step)
        return pltpu.make_async_copy(
            self.slot(way, owner, part),
            self.spill(way, owner, part),
            self.spilled.at[step, way, part],
        )

    def copy(self, way, step, part, behind):
        place = ring_place()
        sign = 1 - 2 * way
        spot = self.slot(way, ring_device(place - sign * (step + behind)), part)
        return remote(
            spot,
            spot,
            self.send.at[step, way, part],
            self.recv.at[step, way, part],
            {"gy": ring_device(place + sign)},
        )

    def begin(self):
        place = [
            pltpu.make_async_copy(
                self.sources(way, part),
                self.slot(way, lax.axis_index("gy"), part),
                self.local.at[way, part],
            )
            for way in range(2)
            for part in range(self.parts)
        ]
        for item in place:
            item.start()
        for item in place:
            item.wait()
        for part in range(self.parts):
            for way in range(2):
                self.copy(way, 0, part, 0).start()
                self.spill_copy(way, 0, part).start()

    @property
    def events(self):
        return (self.count - 2) * self.parts

    def event(self, index):
        step = 1 + lax.div(index, self.parts)
        for part in range(self.parts):

            @pl.when(lax.rem(index, self.parts) == part)
            def _():
                for way in range(2):
                    self.copy(way, step - 1, part, 1).wait_recv()
                    self.copy(way, step, part, 0).start()
                    self.spill_copy(way, step, part).start()

    def end(self):
        for part in range(self.parts):
            for way in range(2):
                self.copy(way, self.count - 2, part, 1).wait_recv()
                self.spill_copy(way, self.count - 1, part).start()

        def drain(step):
            for part in range(self.parts):
                for way in range(2):
                    self.copy(way, step, part, 0).wait_send()

        loop(self.count - 1, drain)

    def settle(self):
        def drain(step):
            for part in range(self.parts):
                for way in range(2):
                    self.spill_copy(way, step, part).wait()

        loop(self.count, drain)


class RingScatter:
    def __init__(self, product, total, sums, land, send, recv, credit, slots, parts):
        self.product, self.total, self.sums, self.land = product, total, sums, land
        self.send, self.recv, self.credit = send, recv, credit
        self.slots, self.parts = slots, parts
        self.count = lax.axis_size("gy")
        self.rows = total.shape[1] // parts

    @staticmethod
    def scratch(rows, columns, slots, parts):
        count = lax.axis_size("gy")
        return [
            pltpu.VMEM((2, rows, columns), WIDE),
            pltpu.VMEM((2, rows, columns), LOW),
            pltpu.VMEM((slots, 2, rows, columns), LOW),
            pltpu.SemaphoreType.DMA((count - 1, 2, parts)),
            pltpu.SemaphoreType.DMA((count - 1, 2, parts)),
            pltpu.SemaphoreType.REGULAR((2, parts)),
        ]

    def copy(self, way, step, part):
        place = ring_place()
        rows = pl.ds(aligned(part * self.rows, self.rows), self.rows)
        return remote(
            self.sums.at[way, rows],
            self.land.at[lax.rem(step, self.slots), way, rows],
            self.send.at[step, way, part],
            self.recv.at[step, way, part],
            {"gy": ring_device(place + 1 - 2 * way)},
        )

    def owner(self, way, step):
        sign = 1 - 2 * way
        return ring_device(ring_place() - sign * (1 + step))

    @property
    def events(self):
        return self.count * self.parts

    def event(self, index):
        step, part = lax.div(index, self.parts), lax.rem(index, self.parts)
        last = self.count - 1
        tile = min(self.rows, 32)

        @pl.when(part == 0)
        def _():
            for way in range(2):
                self.product(way, step)

        for way in range(2):
            base = part * self.rows

            @pl.when(step >= 1)
            def _():
                self.copy(way, step - 1, part).wait_recv()
                slot = lax.rem(step - 1, self.slots)

                @pl.loop(0, self.rows // tile)
                def _(index):
                    rows = pl.ds(aligned(base + index * tile, tile), tile)
                    self.total[way, rows] += self.land[slot, way, rows].astype(WIDE)

                @pl.when(step - 1 + self.slots < last)
                def _():
                    upstream = ring_device(ring_place() - (1 - 2 * way))
                    pl.semaphore_signal(
                        self.credit.at[way, part],
                        inc=1,
                        device_id={"gy": upstream},
                        device_id_type=MESH,
                    )

            @pl.when(step < last)
            def _():
                @pl.when(step >= 1)
                def _():
                    self.copy(way, step - 1, part).wait_send()

                @pl.loop(0, self.rows // tile)
                def _(index):
                    rows = pl.ds(aligned(base + index * tile, tile), tile)
                    self.sums[way, rows] = self.total[way, rows].astype(LOW)

                @pl.when(step >= self.slots)
                def _():
                    pl.semaphore_wait(self.credit.at[way, part], 1)

                self.copy(way, step, part).start()

    def end(self):
        for part in range(self.parts):
            for way in range(2):
                self.copy(way, self.count - 2, part).wait_send()


class Reduce:
    def __init__(self, refs, core_land, cross_land, rows, width, scatter):
        (
            self.keep,
            self.core_send,
            self.core_stage,
            self.cross,
            self.cross_stage,
            self.raw,
            self.core_sems,
            self.cross_send_sems,
            self.cross_recv_sems,
            self.stage_sems,
        ) = refs
        self.core_land, self.cross_land = core_land, cross_land
        self.rows, self.width, self.scatter = rows, width, scatter
        self.chips = lax.axis_size("gx") // 2

    @staticmethod
    def scratch(rows, chunks, width, scatter):
        chips = lax.axis_size("gx") // 2
        half = chips * width
        part = width if scatter else half
        return [
            pltpu.VMEM((2, rows, half), LOW),
            pltpu.VMEM((2, rows, half), LOW),
            pltpu.VMEM((rows, half), LOW),
            pltpu.VMEM((LAG + 2, chips, rows, width) if scatter else (LAG + 2, rows, half), LOW),
            pltpu.VMEM((chips - 1, rows, part), LOW),
            pltpu.VMEM((rows, part), WIDE),
            pltpu.SemaphoreType.DMA((2, chunks)),
            pltpu.SemaphoreType.DMA((chips - 1, chunks)),
            pltpu.SemaphoreType.DMA((chips - 1, chunks)),
            pltpu.SemaphoreType.DMA((chips,)),
        ]

    @staticmethod
    def landing(rows, chunks, width, scatter):
        chips = lax.axis_size("gx") // 2
        half = chips * width
        part = width if scatter else half
        return [
            jax.ShapeDtypeStruct((chunks, rows, half), LOW),
            jax.ShapeDtypeStruct((chips - 1, chunks, rows, part), LOW),
        ]

    def core_copy(self, chunk):
        return remote(
            self.core_send.at[lax.rem(chunk, 2)],
            self.core_land.at[chunk],
            self.core_sems.at[0, chunk],
            self.core_sems.at[1, chunk],
            {"gx": other_core()},
        )

    def cross_copy(self, shift, chunk):
        source = self.cross.at[lax.rem(chunk, LAG + 2)]
        if self.scatter:
            block = lax.rem(chip_here() + shift, self.chips)
            source = source.at[block]
        return remote(
            source,
            self.cross_land.at[shift - 1, chunk],
            self.cross_send_sems.at[shift - 1, chunk],
            self.cross_recv_sems.at[shift - 1, chunk],
            {"gx": peer_at(shift)},
        )

    def produce(self, chunk, dot):
        @pl.when(chunk >= 2)
        def _():
            self.core_copy(chunk - 2).wait_send()

        slot = lax.rem(chunk, 2)
        core = core_here()
        for chip in range(self.chips):
            place = aligned((2 * chip + 1 - core) * self.width, self.width)
            self.core_send[slot, :, chip * self.width : (chip + 1) * self.width] = dot(
                place
            ).astype(LOW)
        self.core_copy(chunk).start()
        for chip in range(self.chips):
            place = aligned((2 * chip + core) * self.width, self.width)
            self.keep[slot, :, chip * self.width : (chip + 1) * self.width] = dot(
                place
            ).astype(LOW)

    def core_stage_copy(self, chunk):
        return pltpu.make_async_copy(
            self.core_land.at[chunk], self.core_stage, self.stage_sems.at[0]
        )

    def core_fetch(self, chunk):
        self.core_copy(chunk).wait_recv()
        self.core_stage_copy(chunk).start()

    def core_sum(self, chunk):
        slot, place = lax.rem(chunk, 2), lax.rem(chunk, LAG + 2)
        self.core_stage_copy(chunk).wait()

        @pl.when(chunk >= LAG + 2)
        def _():
            for shift in range(1, self.chips):
                self.cross_copy(shift, chunk - LAG - 2).wait_send()

        @pl.loop(0, self.rows // 32)
        def _(index):
            rows = pl.ds(aligned(index * 32, 32), 32)
            total = self.keep[slot, rows].astype(WIDE) + self.core_stage[rows].astype(WIDE)
            if self.scatter:
                for chip in range(self.chips):
                    columns = slice(chip * self.width, (chip + 1) * self.width)
                    self.cross[place, chip, rows] = total[:, columns].astype(LOW)
            else:
                self.cross[place, rows] = total.astype(LOW)

        for shift in range(1, self.chips):
            self.cross_copy(shift, chunk).start()

    def cross_stage_copy(self, shift, chunk):
        return pltpu.make_async_copy(
            self.cross_land.at[shift - 1, chunk],
            self.cross_stage.at[shift - 1],
            self.stage_sems.at[shift],
        )

    def cross_fetch(self, chunk):
        for shift in range(1, self.chips):
            self.cross_copy(shift, chunk).wait_recv()
            self.cross_stage_copy(shift, chunk).start()

    def cross_sum(self, chunk):
        place = lax.rem(chunk, LAG + 2)
        for shift in range(1, self.chips):
            self.cross_stage_copy(shift, chunk).wait()

        @pl.loop(0, self.rows // 32)
        def _(index):
            rows = pl.ds(aligned(index * 32, 32), 32)
            if self.scatter:
                total = self.cross[place, chip_here(), rows].astype(WIDE)
            else:
                total = self.cross[place, rows].astype(WIDE)
            for shift in range(1, self.chips):
                total = total + self.cross_stage[shift - 1, rows].astype(WIDE)
            self.raw[rows] = total

    def end(self, chunks):
        for chunk in (chunks - 2, chunks - 1):
            self.core_copy(chunk).wait_send()
        for chunk in range(chunks - LAG - 2, chunks):
            for shift in range(1, self.chips):
                self.cross_copy(shift, chunk).wait_send()


class Stats:
    def __init__(self, mine, land, sems):
        self.mine, self.land, self.sems = mine, land, sems

    @staticmethod
    def scratch(rows, chunks):
        return [
            pltpu.VMEM((2, rows, STATS), WIDE),
            pltpu.VMEM((chunks, rows, STATS), WIDE),
            pltpu.SemaphoreType.DMA((2, chunks)),
        ]

    def copy(self, chunk):
        return remote(
            self.mine.at[lax.rem(chunk, 2)],
            self.land.at[chunk],
            self.sems.at[0, chunk],
            self.sems.at[1, chunk],
            {"gx": other_core()},
        )

    def clear(self, chunk):
        @pl.when(chunk >= 2)
        def _():
            self.copy(chunk - 2).wait_send()

    def put(self, chunk, rows, first, second):
        lane = lax.broadcasted_iota(jnp.int32, (first.shape[0], STATS), 1)
        self.mine[lax.rem(chunk, 2), rows] = jnp.where(lane < STATS // 2, first, second)

    def get(self, chunk, rows):
        total = self.mine[lax.rem(chunk, 2), rows] + self.land[chunk, rows]
        return (total[:, :1], total[:, STATS // 2 : STATS // 2 + 1])

    def end(self, chunks):
        for chunk in (chunks - 2, chunks - 1):
            self.copy(chunk).wait_send()


class Spread:
    def __init__(self, buffer, whole, local, send, recv, rows, width):
        self.buffer, self.whole = buffer, whole
        self.local, self.send, self.recv = local, send, recv
        self.rows, self.width = rows, width
        self.chips = lax.axis_size("gx") // 2

    @staticmethod
    def scratch(rows, chunks, width):
        chips = lax.axis_size("gx") // 2
        return [
            pltpu.VMEM((2, chips, rows, width), LOW),
            pltpu.SemaphoreType.DMA((2, chips)),
            pltpu.SemaphoreType.DMA((chunks, chips)),
            pltpu.SemaphoreType.DMA((chunks, chips)),
        ]

    def pair(self, chunk, chip, core):
        slot = lax.rem(chunk, 2)
        source = self.buffer.at[slot, chip]
        rows = pl.ds(aligned(chunk * self.rows, self.rows), self.rows)
        rank = 2 * chip + core
        if len(self.whole.shape) == 3:
            target = self.whole.at[rank, rows]
        else:
            columns = pl.ds(aligned(rank * self.width, self.width), self.width)
            target = self.whole.at[rows, columns]
        here = pltpu.make_async_copy(source, target, self.local.at[slot, chip])
        away = remote(
            source,
            target,
            self.send.at[chunk, chip],
            self.recv.at[chunk, chip],
            {"gx": other_core()},
        )
        return (here, away)

    def put(self, chunk, rows, values):
        for chip in range(self.chips):
            columns = slice(chip * self.width, (chip + 1) * self.width)
            self.buffer[lax.rem(chunk, 2), chip, rows] = values[:, columns].astype(LOW)

    def clear(self, chunk):
        @pl.when(chunk >= 2)
        def _():
            self.settle(chunk - 2)

    def settle(self, chunk):
        for chip in range(self.chips):
            here, away = self.pair(chunk, chip, core_here())
            here.wait()
            away.wait_send()

    def go(self, chunk):
        for chip in range(self.chips):
            here, away = self.pair(chunk, chip, core_here())
            here.start()
            away.start()

    def end(self, chunks):
        for chunk in (chunks - 2, chunks - 1):
            self.settle(chunk)

        def arrive(chunk):
            for chip in range(self.chips):
                self.pair(chunk, chip, 1 - core_here())[1].wait_recv()

        loop(chunks, arrive)


def row_slice(chunk, rows):
    return pl.ds(aligned(chunk * rows, rows), rows)


def core_blocks(source, chunk, rows, width, buffer, sems):
    return [
        pltpu.make_async_copy(
            source.at[2 * chip + core_here(), row_slice(chunk, rows)],
            buffer.at[:, chip * width : (chip + 1) * width],
            sems.at[chip],
        )
        for chip in range(lax.axis_size("gx") // 2)
    ]


def all_blocks(source, rows, width, buffer, sems):
    return [
        pltpu.make_async_copy(
            source.at[rank] if rows is None else source.at[rank, rows],
            buffer.at[:, rank * width : (rank + 1) * width],
            sems.at[rank],
        )
        for rank in range(source.shape[0])
    ]


def tiles(rows, body):
    @pl.loop(0, rows // 32)
    def _(index):
        body(pl.ds(aligned(index * 32, 32), 32))


def schedule(chunks, reduce, multiply, fetch, sums, finish, event=None, events=0, prepare=None):
    steps = chunks + 2 + LAG

    def iteration(step):
        if event is not None:
            low = lax.div(step * events, steps)
            high = lax.div((step + 1) * events, steps)

            def some(index, carry):
                event(index)
                return carry

            lax.fori_loop(low, high, some, 0)

        @pl.when((step >= 1) & (step <= chunks))
        def _():
            reduce.core_fetch(step - 1)

        @pl.when((step >= 1 + LAG) & (step < chunks + 1 + LAG))
        def _():
            reduce.cross_fetch(step - 1 - LAG)

        @pl.when((step >= 1 + LAG) & (step < chunks + 2 + LAG))
        def _():
            fetch(step - 1 - LAG)

        @pl.when(step < chunks)
        def _():
            if prepare is not None:
                prepare(step)
            reduce.produce(step, lambda place: multiply(step, place))

        @pl.when((step >= 1) & (step <= chunks))
        def _():
            reduce.core_sum(step - 1)

        @pl.when((step >= 2 + LAG) & (step < chunks + 2 + LAG))
        def _():
            finish(step - 2 - LAG)

        @pl.when((step >= 1 + LAG) & (step < chunks + 1 + LAG))
        def _():
            reduce.cross_sum(step - 1 - LAG)
            sums(step - 1 - LAG)

    loop(steps, iteration)


def take(refs, counts):
    groups, start = [], 0
    for count in counts:
        groups.append(refs[start : start + count])
        start += count
    return groups


class Columns:
    def __init__(self, source, shard, left, turned, sem):
        self.source, self.shard = source, shard
        self.left, self.turned, self.sem = left, turned, sem

    @staticmethod
    def scratch(length, shard):
        return [
            pltpu.VMEM((length, shard), LOW),
            pltpu.VMEM((shard, length), LOW),
            pltpu.SemaphoreType.DMA((1,)),
        ]

    def copy(self, owner):
        each = self.source.shape[2] // self.shard
        at = pl.ds(aligned(lax.rem(owner, each) * self.shard, self.shard), self.shard)
        source = self.source.at[lax.div(owner, each), :, at]
        return pltpu.make_async_copy(source, self.left, self.sem.at[0])

    def take(self, ring, way, step):
        self.copy(ring.owner(way, step)).wait()
        self.turned[...] = self.left[...].T
        if way == 0:
            self.copy(ring.owner(1, step)).start()
        else:

            @pl.when(step + 1 < ring.count)
            def _():
                self.copy(ring.owner(0, step + 1)).start()


def attn_out(
    attended, weight, gain, tokens, out_grad, gate_shard, up_shard, down_shard, collective
):
    length, width = attended.shape
    chips = lax.axis_size("gx") // 2
    half = chips * width
    count = lax.axis_size("gy")
    chunks = count
    rows = length // chunks
    hidden = gate_shard.shape[1]
    shard = gate_shard.shape[0]
    part_rows = shard // 2
    side = hidden // 2
    down_columns = down_shard.shape[1]

    groups = [
        Reduce.scratch(rows, chunks, width, False),
        Stats.scratch(rows, chunks),
        Spread.scratch(rows, chunks, width),
        RingGather.scratch(3),
        [
            pltpu.VMEM((rows, half), LOW),
            pltpu.VMEM((2, rows, half), WIDE),
            pltpu.VMEM((2, rows, half), LOW),
            pltpu.SemaphoreType.DMA((chips,)),
            pltpu.SemaphoreType.DMA((2,)),
            pltpu.SemaphoreType.DMA((2,)),
            pltpu.SemaphoreType.DMA((2,)),
            pltpu.SemaphoreType.DMA((chips - 1, chunks, 2)),
        ],
        [
            pltpu.VMEM((2, D, hidden), LOW),
            pltpu.VMEM((count, hidden, down_columns), LOW),
            pltpu.VMEM((chips, length, width), LOW),
        ],
    ]

    def kernel(*refs):
        ins, outs, *scratch = take(refs, [8, 9] + [len(g) for g in groups])
        attended, weight, gain, tokens, out_grad, gate_shard, up_shard, down_shard = ins
        raw_out, mixed_out, low_out, gate_full, up_full, down_full, upstream = outs[:7]
        core_land, cross_land = outs[7:]
        reduce = Reduce(scratch[0], core_land, cross_land, rows, width, False)
        stats = Stats(*scratch[1])
        buffer, local, send, recv = scratch[2]
        spread = Spread(buffer, low_out, local, send, recv, rows, width)
        token_buf, mixed_buf, raw_buf = scratch[4][:3]
        token_sems, mixed_sems, raw_sems, own_sem, up_sems = scratch[4][3:]
        held, held_down, up_land = scratch[5]
        shards_here = (gate_shard, up_shard)

        def place_in(full, down):
            def slot(way, owner, part):
                if part == 2:
                    return down.at[owner, way * side : (way + 1) * side]
                base = owner * shard + part * part_rows
                return full[way].at[pl.ds(aligned(base, part_rows), part_rows)]

            return slot

        slot = place_in((held.at[0], held.at[1]), held_down)
        spill = place_in((gate_full, up_full), down_full)

        def source(way, part):
            if part == 2:
                return down_shard.at[way * side : (way + 1) * side]
            return shards_here[way].at[part * part_rows : (part + 1) * part_rows]

        ring = RingGather(source, slot, spill, 3, *scratch[3])
        own = pltpu.make_async_copy(out_grad, up_land.at[chip_here()], own_sem.at[0])
        up_spill = pltpu.make_async_copy(up_land, upstream, own_sem.at[1])

        def crossings(chunk):
            at = row_slice(chunk, rows)
            return [
                remote(
                    up_land.at[chip_here(), at],
                    up_land.at[chip_here(), at],
                    up_sems.at[shift - 1, chunk, 0],
                    up_sems.at[shift - 1, chunk, 1],
                    {"gx": peer_at(shift)},
                )
                for shift in range(1, chips)
            ]

        own.start()
        greet(True, True)
        ring.begin()
        own.wait()

        def multiply(chunk, place):
            return jnp.dot(
                attended[row_slice(chunk, rows)],
                weight[:, pl.ds(place, width)],
                preferred_element_type=WIDE,
            )

        def prepare(chunk):
            for item in crossings(chunk):
                item.start()

        def token_copies(chunk):
            return core_blocks(tokens, chunk, rows, width, token_buf, token_sems)

        def fetch(chunk):
            @pl.when(chunk >= 1)
            def _():
                for item in token_copies(chunk - 1):
                    item.start()

        def mixed_copy(chunk):
            slot = lax.rem(chunk, 2)
            return pltpu.make_async_copy(
                mixed_buf.at[slot, :, pl.ds(aligned(chip_here() * width, width), width)],
                mixed_out.at[row_slice(chunk, rows)],
                mixed_sems.at[slot],
            )

        def raw_copy(chunk):
            slot = lax.rem(chunk, 2)
            return pltpu.make_async_copy(
                raw_buf.at[slot], raw_out.at[row_slice(chunk, rows)], raw_sems.at[slot]
            )

        def sums(chunk):
            stats.clear(chunk)

            @pl.when(chunk >= 2)
            def _():
                raw_copy(chunk - 2).wait()

            def tile(at):
                raw = reduce.raw[at]
                raw_buf[lax.rem(chunk, 2), at] = raw.astype(LOW)
                squares = jnp.sum(raw * raw, axis=1, keepdims=True)
                stats.put(chunk, at, squares, squares)

            tiles(rows, tile)
            stats.copy(chunk).start()
            raw_copy(chunk).start()

        def finish(chunk):
            slot = lax.rem(chunk, 2)
            for item in token_copies(chunk):
                item.wait()
            stats.copy(chunk).wait_recv()
            spread.clear(chunk)

            @pl.when(chunk >= 2)
            def _():
                mixed_copy(chunk - 2).wait()

            def tile(at):
                squares, _ = stats.get(chunk, at)
                factor = lax.rsqrt(squares / D + EPS)
                mixed = token_buf[at].astype(WIDE) + reduce.raw[at] * factor * gain[...]
                mixed_buf[slot, at] = mixed
                spread.put(chunk, at, mixed)

            tiles(rows, tile)
            spread.go(chunk)
            mixed_copy(chunk).start()

        schedule(chunks, reduce, multiply, fetch, sums, finish, ring.event, ring.events, prepare)
        def drain(chunk):
            for item in crossings(chunk):
                item.wait()

        loop(chunks, drain)
        up_spill.start()
        ring.end()
        up_spill.wait()
        ring.settle()
        reduce.end(chunks)
        stats.end(chunks)
        spread.end(chunks)
        for chunk in (chunks - 2, chunks - 1):
            mixed_copy(chunk).wait()
            raw_copy(chunk).wait()

    shape = jax.ShapeDtypeStruct
    out = pl.pallas_call(
        kernel,
        out_shape=[
            shape((length, half), LOW),
            shape((length, width), WIDE),
            shape((2 * chips, length, width), LOW),
            shape((shard * count, hidden), LOW),
            shape((shard * count, hidden), LOW),
            shape((count, hidden, down_columns), LOW),
            shape((chips, length, width), LOW),
        ]
        + Reduce.landing(rows, chunks, width, False),
        in_specs=[VMEM, VMEM, VMEM, HBM, HBM, HBM, HBM, HBM],
        out_specs=[HBM] * 9,
        scratch_shapes=[item for group in groups for item in group],
        compiler_params=pltpu.CompilerParams(
            collective_id=collective, has_side_effects=True, vmem_limit_bytes=60 * MIB
        ),
        cost_estimate=pl.CostEstimate(
            flops=2 * length * width * D, bytes_accessed=8 * length * D, transcendentals=0
        ),
    )(attended, weight, gain, tokens, out_grad, gate_shard, up_shard, down_shard)
    return out[:7]


def mlp_forward(inputs, gate_full, up_full, down_full, gain, mixed, upstream, collective):
    length, inner = inputs.shape[1], gate_full.shape[1]
    width = mixed.shape[1]
    ranks = inputs.shape[0]
    down_columns = down_full.shape[2]
    chips = lax.axis_size("gx") // 2
    half = chips * width
    chunks = lax.axis_size("gy")
    rows = length // chunks
    tile = min(512, inner)
    pieces = inner // tile

    groups = [
        Reduce.scratch(rows, chunks, width, False),
        Stats.scratch(rows, chunks),
        Spread.scratch(rows, chunks, width),
        [
            pltpu.VMEM((2, rows, half), LOW),
            pltpu.VMEM((rows, width), WIDE),
            pltpu.VMEM((2, rows, width), LOW),
            pltpu.SemaphoreType.DMA((2, chips)),
            pltpu.SemaphoreType.DMA((1,)),
            pltpu.SemaphoreType.DMA((2,)),
        ],
        [
            pltpu.VMEM((D, inner), LOW),
            pltpu.VMEM((D, inner), LOW),
            pltpu.VMEM((inner, D), LOW),
            pltpu.VMEM((2, rows, D), LOW),
            pltpu.VMEM((2, 3, rows, inner), LOW),
            pltpu.SemaphoreType.DMA((pieces, 2)),
            pltpu.SemaphoreType.DMA((chunks,)),
            pltpu.SemaphoreType.DMA((2, ranks)),
            pltpu.SemaphoreType.DMA((2, 3)),
        ],
    ]

    def kernel(*refs):
        ins, outs, *scratch = take(refs, [7, 8] + [len(g) for g in groups])
        inputs, gate_full, up_full, down_full, gain, mixed, upstream = ins
        result, grad_out, gain_grad, hidden_out, gate_out, up_out, core_land, cross_land = outs
        gate_weight, up_weight, weight, row_buf, made = scratch[4][:5]
        piece_sems, weight_sem, row_sems, made_sems = scratch[4][5:]
        reduce = Reduce(scratch[0], core_land, cross_land, rows, width, False)
        stats = Stats(*scratch[1])
        buffer, local, send, recv = scratch[2]
        spread = Spread(buffer, grad_out, local, send, recv, rows, width)
        up_buf, mixed_buf, result_buf, up_sems, mixed_sems, result_sems = scratch[3]

        def piece_copies(piece):
            at = pl.ds(aligned(piece * tile, tile), tile)
            return [
                pltpu.make_async_copy(gate_full.at[:, at], gate_weight.at[:, at], piece_sems.at[piece, 0]),
                pltpu.make_async_copy(up_full.at[:, at], up_weight.at[:, at], piece_sems.at[piece, 1]),
            ]

        weight_copies = all_blocks(down_full, None, down_columns, weight, weight_sem)

        def row_copy(chunk):
            slot = lax.rem(chunk, 2)
            return all_blocks(
                inputs, row_slice(chunk, rows), width, row_buf.at[slot], row_sems.at[slot]
            )

        def stores(chunk):
            slot, at = lax.rem(chunk, 2), row_slice(chunk, rows)
            return [
                pltpu.make_async_copy(made.at[slot, which], out.at[at], made_sems.at[slot, which])
                for which, out in enumerate((hidden_out, gate_out, up_out))
            ]

        for item in row_copy(0):
            item.start()
        for piece in range(pieces):
            for item in piece_copies(piece):
                item.start()
        for item in weight_copies:
            item.start()
        greet(True, False)
        gain_grad[...] = jnp.zeros_like(gain_grad)

        def prepare(chunk):
            slot = lax.rem(chunk, 2)
            for item in row_copy(chunk):
                item.wait()

            @pl.when(chunk + 1 < chunks)
            def _():
                for item in row_copy(chunk + 1):
                    item.start()

            @pl.when(chunk >= 2)
            def _():
                for item in stores(chunk - 2):
                    item.wait()

            @pl.loop(0, pieces)
            def _(piece):
                @pl.when(chunk == 0)
                def _():
                    for item in piece_copies(piece):
                        item.wait()

                at = pl.ds(aligned(piece * tile, tile), tile)
                gate = jnp.dot(row_buf[slot], gate_weight[:, at], preferred_element_type=WIDE)
                up = jnp.dot(row_buf[slot], up_weight[:, at], preferred_element_type=WIDE)
                made[slot, 0, :, at] = (gate * jax.nn.sigmoid(gate) * up).astype(LOW)
                made[slot, 1, :, at] = gate.astype(LOW)
                made[slot, 2, :, at] = up.astype(LOW)

            @pl.when(chunk == 0)
            def _():
                for item in weight_copies:
                    item.wait()

            for item in stores(chunk):
                item.start()

        def multiply(chunk, place):
            return jnp.dot(
                made[lax.rem(chunk, 2), 0],
                weight[:, pl.ds(place, width)],
                preferred_element_type=WIDE,
            )

        def up_copy(chunk):
            slot = lax.rem(chunk, 2)
            return all_blocks(
                upstream, row_slice(chunk, rows), width, up_buf.at[slot], up_sems.at[slot]
            )

        def mixed_copy(chunk):
            return pltpu.make_async_copy(
                mixed.at[row_slice(chunk, rows)], mixed_buf, mixed_sems.at[0]
            )

        def result_copy(chunk):
            slot = lax.rem(chunk, 2)
            return pltpu.make_async_copy(
                result_buf.at[slot], result.at[row_slice(chunk, rows)], result_sems.at[slot]
            )

        def fetch(chunk):
            @pl.when(chunk < chunks)
            def _():
                for item in up_copy(chunk):
                    item.start()

            @pl.when(chunk >= 1)
            def _():
                mixed_copy(chunk - 1).start()

        def sums(chunk):
            slot = lax.rem(chunk, 2)
            stats.clear(chunk)
            for item in up_copy(chunk):
                item.wait()

            def tile(at):
                raw = reduce.raw[at]
                up = up_buf[slot, at].astype(WIDE)
                squares = jnp.sum(raw * raw, axis=1, keepdims=True)
                projected = jnp.sum(gain[...] * up * raw, axis=1, keepdims=True)
                stats.put(chunk, at, squares, projected)

            tiles(rows, tile)
            stats.copy(chunk).start()

        def finish(chunk):
            slot = lax.rem(chunk, 2)
            mixed_copy(chunk).wait()
            stats.copy(chunk).wait_recv()
            spread.clear(chunk)

            @pl.when(chunk >= 2)
            def _():
                result_copy(chunk - 2).wait()

            block = pl.ds(aligned(chip_here() * width, width), width)

            def tile(at):
                squares, projected = stats.get(chunk, at)
                factor = lax.rsqrt(squares / D + EPS)
                raw = reduce.raw[at]
                up = up_buf[slot, at].astype(WIDE)
                pull = factor * factor * factor * projected / D
                spread.put(chunk, at, factor * gain[...] * up - raw * pull)
                gain_grad[...] += jnp.sum(up * raw * factor, axis=0, keepdims=True)
                result_buf[slot, at] = (
                    mixed_buf[at] + reduce.raw[at, block] * factor * gain[:, block]
                ).astype(LOW)

            tiles(rows, tile)
            spread.go(chunk)
            result_copy(chunk).start()

        schedule(chunks, reduce, multiply, fetch, sums, finish, prepare=prepare)
        reduce.end(chunks)
        stats.end(chunks)
        spread.end(chunks)
        for chunk in (chunks - 2, chunks - 1):
            result_copy(chunk).wait()
            for item in stores(chunk):
                item.wait()

    shape = jax.ShapeDtypeStruct
    out = pl.pallas_call(
        kernel,
        out_shape=[
            shape((length, width), LOW),
            shape((2 * chips, length, width), LOW),
            shape((1, half), WIDE),
            shape((length, inner), LOW),
            shape((length, inner), LOW),
            shape((length, inner), LOW),
        ]
        + Reduce.landing(rows, chunks, width, False),
        in_specs=[HBM] * 4 + [VMEM, HBM, HBM],
        out_specs=[HBM, HBM, VMEM] + [HBM] * 5,
        scratch_shapes=[item for group in groups for item in group],
        compiler_params=pltpu.CompilerParams(
            collective_id=collective, has_side_effects=True, vmem_limit_bytes=60 * MIB
        ),
        cost_estimate=pl.CostEstimate(
            flops=6 * length * inner * D, bytes_accessed=16 * length * D, transcendentals=0
        ),
    )(inputs, gate_full, up_full, down_full, gain, mixed, upstream)
    return out[:6]


def mlp_back(gate_grad, up_grad, gate_full, up_full, inputs, gain, upstream, attn_raw, collective):
    length, inner = gate_grad.shape
    half = attn_raw.shape[1]
    chips = lax.axis_size("gx") // 2
    width = half // chips
    count = lax.axis_size("gy")
    chunks = count
    rows = length // chunks
    shard = D // count
    slots, parts = 2, 2

    groups = [
        Reduce.scratch(rows, chunks, width, False),
        Stats.scratch(rows, chunks),
        Spread.scratch(rows, chunks, width),
        RingScatter.scratch(shard, inner, slots, parts),
        [
            pltpu.VMEM((rows, half), LOW),
            pltpu.VMEM((2, rows, half), LOW),
            pltpu.SemaphoreType.DMA((chips,)),
            pltpu.SemaphoreType.DMA((2,)),
            pltpu.SemaphoreType.DMA((1,)),
            pltpu.SemaphoreType.DMA((2,)),
        ],
        Columns.scratch(length, shard),
    ]

    def kernel(*refs):
        ins, outs, *scratch = take(refs, [8, 7] + [len(g) for g in groups])
        gate_grad, up_grad, gate_full, up_full, inputs, gain, upstream, attn_raw = ins
        mixed_out, grad_out, gain_grad, gate_out, up_out, core_land, cross_land = outs
        reduce = Reduce(scratch[0], core_land, cross_land, rows, width, False)
        stats = Stats(*scratch[1])
        buffer, local, send, recv = scratch[2]
        spread = Spread(buffer, grad_out, local, send, recv, rows, width)
        total, summed, land, ring_send, ring_recv, credit = scratch[3]
        up_buf, raw_buf, up_sems, raw_sems, mixed_sems, out_sems = scratch[4]
        left = Columns(inputs, shard, *scratch[5])
        grads = (gate_grad, up_grad)

        def product(way, step):
            left.take(ring, way, step)
            tile = 512

            @pl.loop(0, inner // tile)
            def _(index):
                columns = pl.ds(aligned(index * tile, tile), tile)
                total[way, :, columns] = jnp.dot(
                    left.turned[...], grads[way][:, columns], preferred_element_type=WIDE
                )

        ring = RingScatter(
            product, total, summed, land, ring_send, ring_recv, credit, slots, parts
        )
        left.copy(ring.owner(0, 0)).start()
        greet(True, True)
        gain_grad[...] = jnp.zeros_like(gain_grad)

        def multiply(chunk, place):
            at = row_slice(chunk, rows)
            return lax.dot_general(
                gate_grad[at],
                gate_full[pl.ds(place, width)],
                (((1,), (1,)), ((), ())),
                preferred_element_type=WIDE,
            ) + lax.dot_general(
                up_grad[at],
                up_full[pl.ds(place, width)],
                (((1,), (1,)), ((), ())),
                preferred_element_type=WIDE,
            )

        def up_copy(chunk):
            return all_blocks(upstream, row_slice(chunk, rows), width, up_buf, up_sems)

        def raw_copy(chunk):
            slot = lax.rem(chunk, 2)
            return pltpu.make_async_copy(
                attn_raw.at[row_slice(chunk, rows)], raw_buf.at[slot], raw_sems.at[slot]
            )

        def mixed_copy(chunk):
            return pltpu.make_async_copy(
                reduce.raw.at[:, pl.ds(aligned(chip_here() * width, width), width)],
                mixed_out.at[row_slice(chunk, rows)],
                mixed_sems.at[0],
            )

        def fetch(chunk):
            @pl.when(chunk < chunks)
            def _():
                for item in up_copy(chunk):
                    item.start()
                raw_copy(chunk).start()

        def sums(chunk):
            slot = lax.rem(chunk, 2)
            stats.clear(chunk)
            for item in up_copy(chunk):
                item.wait()
            raw_copy(chunk).wait()

            def tile(at):
                upward = reduce.raw[at] + up_buf[at].astype(WIDE)
                reduce.raw[at] = upward
                raw = raw_buf[slot, at].astype(WIDE)
                squares = jnp.sum(raw * raw, axis=1, keepdims=True)
                projected = jnp.sum(gain[...] * upward * raw, axis=1, keepdims=True)
                stats.put(chunk, at, squares, projected)

            tiles(rows, tile)
            stats.copy(chunk).start()
            mixed_copy(chunk).start()

        def finish(chunk):
            slot = lax.rem(chunk, 2)
            stats.copy(chunk).wait_recv()
            spread.clear(chunk)

            def tile(at):
                squares, projected = stats.get(chunk, at)
                factor = lax.rsqrt(squares / D + EPS)
                upward = reduce.raw[at]
                raw = raw_buf[slot, at].astype(WIDE)
                pull = factor * factor * factor * projected / D
                spread.put(chunk, at, factor * gain[...] * upward - raw * pull)
                gain_grad[...] += jnp.sum(upward * raw * factor, axis=0, keepdims=True)

            tiles(rows, tile)
            spread.go(chunk)
            mixed_copy(chunk).wait()

        schedule(chunks, reduce, multiply, fetch, sums, finish, ring.event, ring.events)
        writes = [
            pltpu.make_async_copy(total.at[way], (gate_out, up_out)[way], out_sems.at[way])
            for way in range(2)
        ]
        for item in writes:
            item.start()
        ring.end()
        reduce.end(chunks)
        stats.end(chunks)
        spread.end(chunks)
        for item in writes:
            item.wait()

    shape = jax.ShapeDtypeStruct
    out = pl.pallas_call(
        kernel,
        out_shape=[
            shape((length, width), WIDE),
            shape((length, D), LOW),
            shape((1, half), WIDE),
            shape((shard, inner), WIDE),
            shape((shard, inner), WIDE),
        ]
        + Reduce.landing(rows, chunks, width, False),
        in_specs=[VMEM, VMEM, VMEM, VMEM, HBM, VMEM, HBM, HBM],
        out_specs=[HBM, HBM, VMEM, HBM, HBM, HBM, HBM],
        scratch_shapes=[item for group in groups for item in group],
        compiler_params=pltpu.CompilerParams(
            collective_id=collective, has_side_effects=True, vmem_limit_bytes=60 * MIB
        ),
        cost_estimate=pl.CostEstimate(
            flops=8 * length * inner * D, bytes_accessed=16 * length * D, transcendentals=0
        ),
    )(gate_grad, up_grad, gate_full, up_full, inputs, gain, upstream, attn_raw)
    return out[:5]


class Total:
    def __init__(self, land, send, recv):
        self.land, self.send, self.recv = land, send, recv
        self.count = lax.axis_size("gx")

    @staticmethod
    def scratch(length):
        others = lax.axis_size("gx") - 1
        return [
            pltpu.VMEM((others, 8, length), WIDE),
            pltpu.SemaphoreType.DMA((others,)),
            pltpu.SemaphoreType.DMA((others,)),
        ]

    def copies(self, mine):
        return [
            remote(
                mine,
                self.land.at[shift - 1],
                self.send.at[shift - 1],
                self.recv.at[shift - 1],
                {"gx": rank_at(shift)},
            )
            for shift in range(1, self.count)
        ]

    def start(self, mine):
        for item in self.copies(mine):
            item.start()

    def finish(self, mine):
        for item in self.copies(mine):
            item.wait()
        total = mine[...]
        for shift in range(1, self.count):
            total = total + self.land[shift - 1]
        return total


def gather_in(tokens, stack, gains, collective):
    length, width = tokens.shape
    _, shard, side = stack.shape
    columns = 2 * side
    count = lax.axis_size("gy")
    chunks = count
    rows = length // chunks
    chips = lax.axis_size("gx") // 2
    parts = 1

    groups = [
        RingGather.scratch(parts),
        [
            pltpu.SemaphoreType.DMA((1,)),
            pltpu.SemaphoreType.DMA((2,)),
            pltpu.SemaphoreType.DMA((chips - 1, chunks, 2)),
            pltpu.SemaphoreType.DMA((chips - 1, chunks, 2)),
        ],
        [
            pltpu.VMEM((2, D, side), LOW),
            pltpu.VMEM((2 * chips, length, width), LOW),
            pltpu.VMEM((2, 2, rows, width), WIDE),
            pltpu.VMEM((2, rows, width), LOW),
            pltpu.VMEM((length, STATS), WIDE),
            pltpu.VMEM((8, length), WIDE),
            pltpu.SemaphoreType.DMA((2,)),
            pltpu.SemaphoreType.DMA((2, 3)),
        ],
        Total.scratch(length),
        [
            pltpu.VMEM((chips - 1, 8, width), WIDE),
            pltpu.SemaphoreType.DMA((chips - 1, 2)),
        ],
    ]

    def kernel(*refs):
        ins, outs, *scratch = take(refs, [3, 7] + [len(g) for g in groups])
        tokens, stack, gains = ins
        whole, full, query_raw, key_raw, values, squares, halves = outs
        gain_land, gain_sems = scratch[4]
        own_sem, core_sems, cross_sems, pass_sems = scratch[1]
        weight, held, raw_buf, value_buf, stats, mine = scratch[2][:6]
        copy_sems, out_sems = scratch[2][6:]
        total = Total(*scratch[3])

        def slot(way, owner, part):
            return weight.at[way, pl.ds(aligned(owner * shard, shard), shard)]

        def spill(way, owner, part):
            return full.at[way, pl.ds(aligned(owner * shard, shard), shard)]

        def source(way, part):
            return stack.at[way]

        ring = RingGather(source, slot, spill, parts, *scratch[0])

        def block(rank, chunk):
            if chunk is None:
                return held.at[rank]
            return held.at[rank, row_slice(chunk, rows)]

        here = lax.axis_index("gx")
        own = pltpu.make_async_copy(tokens, block(here, None), own_sem.at[0])
        core = remote(
            block(here, None), block(here, None), core_sems.at[0], core_sems.at[1], {"gx": other_core()}
        )

        def cross(shift, chunk):
            return remote(
                block(here, chunk),
                block(here, chunk),
                cross_sems.at[shift - 1, chunk, 0],
                cross_sems.at[shift - 1, chunk, 1],
                {"gx": peer_at(shift)},
            )

        def onward(shift, chunk):
            spot = block(peer_at(chips - shift), chunk)
            return remote(
                spot,
                spot,
                pass_sems.at[shift - 1, chunk, 0],
                pass_sems.at[shift - 1, chunk, 1],
                {"gx": other_core()},
            )

        gain_copies = [
            remote(
                gains,
                gain_land.at[shift - 1],
                gain_sems.at[shift - 1, 0],
                gain_sems.at[shift - 1, 1],
                {"gx": peer_at(shift)},
            )
            for shift in range(1, chips)
        ]
        own.start()
        greet("all", True)
        for item in gain_copies:
            item.start()
        ring.begin()
        own.wait()

        def send(chunk):
            for shift in range(1, chips):
                cross(shift, chunk).start()

        loop(chunks, send)
        core.start()

        def step(chunk):
            for shift in range(1, chips):
                cross(shift, chunk).wait_recv()
                onward(shift, chunk).start()

            @pl.when(chunk < ring.events)
            def _():
                ring.event(chunk)

        loop(chunks, step)
        ring.end()

        def drain(chunk):
            for shift in range(1, chips):
                cross(shift, chunk).wait_send()
                onward(shift, chunk).wait()

        loop(chunks, drain)
        core.wait()
        whole_copy = pltpu.make_async_copy(held, whole, copy_sems.at[0])
        whole_copy.start()

        def stores(chunk):
            slot, at = lax.rem(chunk, 2), row_slice(chunk, rows)
            return [
                pltpu.make_async_copy(raw_buf.at[slot, 0], query_raw.at[at], out_sems.at[slot, 0]),
                pltpu.make_async_copy(raw_buf.at[slot, 1], key_raw.at[at], out_sems.at[slot, 1]),
                pltpu.make_async_copy(value_buf.at[slot], values.at[at], out_sems.at[slot, 2]),
            ]

        lane = lax.broadcasted_iota(jnp.int32, (rows, STATS), 1)

        def project(chunk):
            slot = lax.rem(chunk, 2)
            @pl.when(chunk >= 2)
            def _():
                for item in stores(chunk - 2):
                    item.wait()

            at = row_slice(chunk, rows)
            middle = side - width

            def against(way, columns):
                raw = jnp.zeros((rows, columns.stop - columns.start), WIDE)
                for rank in range(2 * chips):
                    raw = raw + jnp.dot(
                        held[rank, at],
                        weight[way, rank * width : (rank + 1) * width, columns],
                        preferred_element_type=WIDE,
                    )
                return raw

            some = []
            raw_buf[slot, 0] = against(0, slice(0, width))
            raw_buf[slot, 1, :, :middle] = against(0, slice(width, side))
            raw_buf[slot, 1, :, middle:] = against(1, slice(0, middle))
            value_buf[slot] = against(1, slice(middle, side)).astype(LOW)
            for which in range(2):
                raw = raw_buf[slot, which]
                some.append(jnp.sum(raw * raw, axis=1, keepdims=True))
            stats[row_slice(chunk, rows)] = jnp.where(lane == 0, some[0], some[1])
            for item in stores(chunk):
                item.start()

        loop(chunks, project)
        mine[...] = stats[...].T[:8]
        total.start(mine)
        for chunk in (chunks - 2, chunks - 1):
            for item in stores(chunk):
                item.wait()
        squares[...] = total.finish(mine)
        whole_copy.wait()
        ring.settle()
        halves[:, pl.ds(aligned(chip_here() * width, width), width)] = gains[...]
        for shift in range(1, chips):
            gain_copies[shift - 1].wait()
            chip = lax.rem(chip_here() + chips - shift, chips)
            halves[:, pl.ds(aligned(chip * width, width), width)] = gain_land[shift - 1]

    shape = jax.ShapeDtypeStruct
    return pl.pallas_call(
        kernel,
        out_shape=[
            shape((2 * chips, length, width), LOW),
            shape((2, shard * count, side), LOW),
            shape((length, width), WIDE),
            shape((length, width), WIDE),
            shape((length, width), LOW),
            shape((8, length), WIDE),
            shape((8, chips * width), WIDE),
        ],
        in_specs=[HBM, HBM, VMEM],
        out_specs=[HBM] * 5 + [VMEM, VMEM],
        scratch_shapes=[item for group in groups for item in group],
        compiler_params=pltpu.CompilerParams(
            collective_id=collective, has_side_effects=True, vmem_limit_bytes=40 * MIB
        ),
        cost_estimate=pl.CostEstimate(
            flops=2 * length * columns * D, bytes_accessed=8 * length * D, transcendentals=0
        ),
    )(tokens, stack, gains)


def hidden_back(blocks, slots_of_weight, hidden, gate, up, collective):
    length, inner = hidden.shape
    count = lax.axis_size("gy")
    chunks = count
    rows = length // chunks
    shard = D // count
    side = inner // 2
    slots, parts = count - 1, 2
    tile = min(512, inner)

    groups = [
        RingScatter.scratch(shard, side, slots, parts),
        [
            pltpu.VMEM((2, 2, rows, inner), LOW),
            pltpu.VMEM((2, 2, rows, inner), LOW),
            pltpu.SemaphoreType.DMA((2, 2)),
            pltpu.SemaphoreType.DMA((2, 2)),
            pltpu.SemaphoreType.DMA((2,)),
            pltpu.VMEM((shard, length), LOW),
        ],
        [
            pltpu.VMEM((length, D), LOW),
            pltpu.VMEM((inner, D), LOW),
            pltpu.SemaphoreType.DMA((blocks.shape[0],)),
            pltpu.SemaphoreType.DMA((count,)),
        ],
    ]

    def kernel(*refs):
        ins, outs, *scratch = take(refs, [5, 3] + [len(g) for g in groups])
        blocks, slots_of_weight, hidden, gate, up = ins
        grad, weight, grad_sems, weight_sems = scratch[2]
        gate_grad, up_grad, weight_grad = outs
        total, summed, land, ring_send, ring_recv, credit = scratch[0]
        given, made, given_sems, made_sems, out_sems, turned = scratch[1]

        def product(way, step):
            columns = pl.ds(aligned(ring.owner(way, step) * shard, shard), shard)
            turned[...] = grad[:, columns].T
            size = min(512, side)

            @pl.loop(0, side // size)
            def _(index):
                at = pl.ds(aligned(index * size, size), size)
                take_at = pl.ds(aligned(way * side + index * size, size), size)
                total[way, :, at] = jnp.dot(
                    turned[...], hidden[:, take_at], preferred_element_type=WIDE
                )

        ring = RingScatter(
            product, total, summed, land, ring_send, ring_recv, credit, slots, parts
        )

        def load(chunk):
            slot = lax.rem(chunk, 2)
            return [
                pltpu.make_async_copy(
                    (gate, up)[which].at[row_slice(chunk, rows)],
                    given.at[slot, which],
                    given_sems.at[slot, which],
                )
                for which in range(2)
            ]

        def store(chunk):
            slot = lax.rem(chunk, 2)
            return [
                pltpu.make_async_copy(
                    made.at[slot, which],
                    (gate_grad, up_grad)[which].at[row_slice(chunk, rows)],
                    made_sems.at[slot, which],
                )
                for which in range(2)
            ]

        grad_copies = all_blocks(blocks, None, blocks.shape[2], grad, grad_sems)
        weight_copies = all_blocks(slots_of_weight, None, shard, weight, weight_sems)
        for item in grad_copies + weight_copies + load(0):
            item.start()
        greet(False, True)
        for item in grad_copies:
            item.wait()

        def iteration(step):
            slot = lax.rem(step, 2)
            for part in range(parts):
                ring.event(step * parts + part)

            @pl.when(step + 1 < chunks)
            def _():
                for item in load(step + 1):
                    item.start()

            @pl.when(step >= 2)
            def _():
                for item in store(step - 2):
                    item.wait()

            for item in load(step):
                item.wait()

            @pl.when(step == 0)
            def _():
                for item in weight_copies:
                    item.wait()

            @pl.loop(0, inner // tile)
            def _(index):
                at = pl.ds(aligned(index * tile, tile), tile)
                hidden_grad = lax.dot_general(
                    grad[row_slice(step, rows)],
                    weight[at],
                    (((1,), (1,)), ((), ())),
                    preferred_element_type=WIDE,
                )
                gate = given[slot, 0, :, at].astype(WIDE)
                up = given[slot, 1, :, at].astype(WIDE)
                sigma = jax.nn.sigmoid(gate)
                made[slot, 0, :, at] = (
                    hidden_grad * up * sigma * (1.0 + gate * (1.0 - sigma))
                ).astype(LOW)
                made[slot, 1, :, at] = (hidden_grad * gate * sigma).astype(LOW)

            for item in store(step):
                item.start()

        loop(chunks, iteration)
        writes = [
            pltpu.make_async_copy(
                total.at[way], weight_grad.at[:, way * side : (way + 1) * side], out_sems.at[way]
            )
            for way in range(2)
        ]
        for item in writes:
            item.start()
        for chunk in (chunks - 2, chunks - 1):
            for item in store(chunk):
                item.wait()
        ring.end()
        for item in writes:
            item.wait()

    shape = jax.ShapeDtypeStruct
    return pl.pallas_call(
        kernel,
        out_shape=[
            shape((length, inner), LOW),
            shape((length, inner), LOW),
            shape((shard, inner), WIDE),
        ],
        in_specs=[HBM, HBM, VMEM, HBM, HBM],
        out_specs=[HBM, HBM, HBM],
        scratch_shapes=[item for group in groups for item in group],
        compiler_params=pltpu.CompilerParams(
            collective_id=collective, has_side_effects=True, vmem_limit_bytes=60 * MIB
        ),
        cost_estimate=pl.CostEstimate(
            flops=4 * length * inner * D, bytes_accessed=16 * length * D, transcendentals=0
        ),
    )(blocks, slots_of_weight, hidden, gate, up)


def attn_in_back(
    query_back,
    key_back,
    value_grad,
    query_raw,
    key_raw,
    factors,
    projections,
    query_gain,
    key_gain,
    stack,
    inputs,
    mixed_grad,
    gain_parts,
    collective,
):
    length, columns = value_grad.shape[0], 2 * stack.shape[2]
    width = mixed_grad.shape[1]
    count = lax.axis_size("gy")
    chunks = count
    rows = length // chunks
    shard = D // count
    side = columns // 2
    slots, parts = count - 1, 2
    tile = 256 if side % 256 == 0 else 128

    groups = [
        Reduce.scratch(rows, chunks, width, True),
        RingScatter.scratch(shard, side, slots, parts),
        [
            pltpu.VMEM((rows, width), WIDE),
            pltpu.VMEM((2, rows, width), WIDE),
            pltpu.VMEM((length, columns), LOW),
            pltpu.VMEM((length, STATS), WIDE),
            pltpu.SemaphoreType.DMA((1,)),
            pltpu.SemaphoreType.DMA((2,)),
            pltpu.SemaphoreType.DMA((2,)),
        ],
        Columns.scratch(length, shard),
        Total.scratch(length),
        [
            pltpu.VMEM((8, width), WIDE),
            pltpu.VMEM((count - 1, 8, width), WIDE),
            pltpu.SemaphoreType.DMA((count - 1, 2)),
        ],
    ]

    def kernel(*refs):
        ins, outs, *scratch = take(refs, [16, 5] + [len(g) for g in groups])
        query_back, key_back, value_grad, query_raw, key_raw, factors = ins[:6]
        projections, query_gain, key_gain, stack, inputs, mixed_grad = ins[6:12]
        gain_parts = ins[12:]
        token_grad, weight_grad, gain_grads, core_land, cross_land = outs
        gain_mine, gain_land, gain_sems = scratch[5]
        reduce = Reduce(scratch[0], core_land, cross_land, rows, width, True)
        total, summed, land, ring_send, ring_recv, credit = scratch[1]
        mixed_buf, token_buf, grads, projected, mixed_sems, token_sems, out_sems = scratch[2]
        left = Columns(inputs, shard, *scratch[3])
        total_sum = Total(*scratch[4])

        def product(way, step):
            left.take(ring, way, step)

            @pl.loop(0, side // tile)
            def _(index):
                at = pl.ds(aligned(index * tile, tile), tile)
                take_at = pl.ds(aligned(way * side + index * tile, tile), tile)
                total[way, :, at] = jnp.dot(
                    left.turned[...], grads[:, take_at], preferred_element_type=WIDE
                )

        ring = RingScatter(
            product, total, summed, land, ring_send, ring_recv, credit, slots, parts
        )
        left.copy(ring.owner(0, 0)).start()
        chip_columns = pl.ds(aligned(chip_here() * width, width), width)
        gain_mine[...] = jnp.zeros_like(gain_mine)
        for which, part in enumerate(gain_parts):
            gain_mine[which : which + 1] = part[...] if which < 2 else part[:, chip_columns]
        greet("all", False, True)
        total_sum.start(projections)
        gain_copies = [
            remote(
                gain_mine,
                gain_land.at[shift - 1],
                gain_sems.at[shift - 1, 0],
                gain_sems.at[shift - 1, 1],
                {"gy": block_at(shift)},
            )
            for shift in range(1, count)
        ]
        for item in gain_copies:
            item.start()
        grads[:, 2 * width :] = value_grad[...]
        sums_here = total_sum.finish(projections)
        projected[...] = jnp.concatenate([sums_here] * (STATS // 8), axis=0).T
        pairs = ((query_back, query_raw, query_gain), (key_back, key_raw, key_gain))

        @pl.loop(0, length // 32)
        def _(index):
            at = row_slice(index, 32)
            for which, (back, raw, gain) in enumerate(pairs):
                factor = factors[at, which : which + 1]
                pull = factor * factor * factor * projected[at, which : which + 1] / D
                grads[at, which * width : (which + 1) * width] = (
                    factor * gain[...] * back[at] - raw[at] * pull
                ).astype(LOW)

        def multiply(chunk, place):
            at = row_slice(chunk, rows)
            return nt(grads[at, :side], stack[0, pl.ds(place, width)]) + nt(
                grads[at, side:], stack[1, pl.ds(place, width)]
            )

        def mixed_copy(chunk):
            return pltpu.make_async_copy(
                mixed_grad.at[row_slice(chunk, rows)], mixed_buf, mixed_sems.at[0]
            )

        def token_copy(chunk):
            slot = lax.rem(chunk, 2)
            return pltpu.make_async_copy(
                token_buf.at[slot], token_grad.at[row_slice(chunk, rows)], token_sems.at[slot]
            )

        def fetch(chunk):
            @pl.when(chunk >= 1)
            def _():
                mixed_copy(chunk - 1).start()

        def sums(chunk):
            pass

        def finish(chunk):
            slot = lax.rem(chunk, 2)
            mixed_copy(chunk).wait()

            @pl.when(chunk >= 2)
            def _():
                token_copy(chunk - 2).wait()

            def some(at):
                token_buf[slot, at] = mixed_buf[at] + reduce.raw[at]

            tiles(rows, some)
            token_copy(chunk).start()

        schedule(chunks, reduce, multiply, fetch, sums, finish, ring.event, ring.events)
        writes = [
            pltpu.make_async_copy(
                total.at[way], weight_grad.at[:, way * side : (way + 1) * side], out_sems.at[way]
            )
            for way in range(2)
        ]
        for item in writes:
            item.start()
        gain_total = gain_mine[...]
        for shift in range(1, count):
            gain_copies[shift - 1].wait()
            gain_total = gain_total + gain_land[shift - 1]
        gain_grads[...] = gain_total
        ring.end()
        reduce.end(chunks)
        for chunk in (chunks - 2, chunks - 1):
            token_copy(chunk).wait()
        for item in writes:
            item.wait()

    shape = jax.ShapeDtypeStruct
    out = pl.pallas_call(
        kernel,
        out_shape=[
            shape((length, width), WIDE),
            shape((shard, columns), WIDE),
            shape((8, width), WIDE),
        ]
        + Reduce.landing(rows, chunks, width, True),
        in_specs=[VMEM] * 10 + [HBM, HBM] + [VMEM] * 4,
        out_specs=[HBM, HBM, VMEM, HBM, HBM],
        scratch_shapes=[item for group in groups for item in group],
        compiler_params=pltpu.CompilerParams(
            collective_id=collective, has_side_effects=True, vmem_limit_bytes=60 * MIB
        ),
        cost_estimate=pl.CostEstimate(
            flops=4 * length * columns * D, bytes_accessed=8 * length * D, transcendentals=0
        ),
    )(
        query_back,
        key_back,
        value_grad,
        query_raw,
        key_raw,
        factors,
        projections,
        query_gain,
        key_gain,
        stack,
        inputs,
        mixed_grad,
        *gain_parts,
    )
    return out[:3]


def token_positions(segment):
    length = segment.shape[0]
    labels = jnp.arange(SEGS, dtype=jnp.int32)
    member = (segment[:, None] == labels[None, :]).astype(jnp.int32)
    totals = jnp.sum(member, axis=0)
    starts = jnp.cumsum(totals) - totals
    opening = jnp.sum(member * starts[None, :], axis=1)
    return jnp.arange(length, dtype=jnp.int32) - opening


def rotary_tables(segment):
    place = token_positions(segment).astype(jnp.float32)
    halves = HEAD // 2
    inverse = jnp.exp(jnp.arange(halves, dtype=jnp.float32) * (-2.0 * math.log(THETA) / HEAD))
    angle = place[:, None] * inverse[None, :]
    return (jnp.cos(angle), jnp.sin(angle))


BLOCK = 256
LANES = 128
SCALE = 1.0 / math.sqrt(HEAD)
SCALE_TWO = SCALE * math.log2(math.e)


def turn(values, cosine, sine):
    return values * cosine + pltpu.roll(values, HEAD // 2, 1) * sine


def head_columns(head):
    return slice(head * HEAD, (head + 1) * HEAD)


def nt(left, right):
    return lax.dot_general(left, right, (((1,), (1,)), ((), ())), preferred_element_type=WIDE)


def attend(first_block, query_raw, key_raw, values, factors, query_gain, key_gain, tables, starts):
    length, width = query_raw.shape
    heads = width // HEAD

    def kernel(
        first_block,
        query_raw,
        key_raw,
        values,
        factors,
        query_gain,
        key_gain,
        cosine,
        sine,
        starts,
        queries,
        keys,
        attended,
        peaks,
        peak_columns,
    ):
        @pl.loop(0, length // BLOCK)
        def _(index):
            at = row_slice(index, BLOCK)
            cos, sin = cosine[at], sine[at]
            pairs = ((query_raw, query_gain, queries), (key_raw, key_gain, keys))
            for which, (raw, gain, out) in enumerate(pairs):
                factor = factors[at, which : which + 1]
                for head in range(heads):
                    columns = head_columns(head)
                    normed = raw[at, columns] * factor * gain[:, columns]
                    out[at, columns] = turn(normed, cos, sin).astype(LOW)

        lane = lax.broadcasted_iota(jnp.int32, (BLOCK, LANES), 1)
        row_index = lax.broadcasted_iota(jnp.int32, (BLOCK, BLOCK), 0)
        column_index = lax.broadcasted_iota(jnp.int32, (BLOCK, BLOCK), 1)

        def query_block(index):
            at = row_slice(index, BLOCK)
            start = starts[at]

            def key_block(other, carry):
                there = row_slice(other, BLOCK)
                key_place = column_index + other * BLOCK
                allowed = (key_place >= start) & (key_place <= row_index + index * BLOCK)
                made = []
                for head in range(heads):
                    columns = head_columns(head)
                    peak, total, rows = carry[head]
                    scores = nt(queries[at, columns], keys[there, columns]) * SCALE_TWO
                    scores = jnp.where(allowed, scores, NEGATIVE)
                    higher = jnp.maximum(peak, jnp.max(scores, axis=1, keepdims=True))
                    raised = jnp.exp2(scores - higher)
                    shrink = jnp.exp2(peak - higher)
                    total = total * shrink + jnp.sum(raised, axis=1, keepdims=True)
                    rows = rows * shrink + jnp.dot(
                        raised.astype(LOW), values[there, columns], preferred_element_type=WIDE
                    )
                    made.append((higher, total, rows))
                return tuple(made)

            empty = (
                jnp.full((BLOCK, 1), NEGATIVE, WIDE),
                jnp.zeros((BLOCK, 1), WIDE),
                jnp.zeros((BLOCK, HEAD), WIDE),
            )
            done = lax.fori_loop(first_block[index], index + 1, key_block, (empty,) * heads)
            column = jnp.zeros((BLOCK, LANES), WIDE)
            for head in range(heads):
                peak, total, rows = done[head]
                attended[at, head_columns(head)] = (rows / total).astype(LOW)
                column = jnp.where(lane == head, peak + jnp.log2(total), column)
            peak_columns[at] = column

        loop(length // BLOCK, query_block)
        peaks[...] = peak_columns[...].T[:8]

    shape = jax.ShapeDtypeStruct
    smem = pl.BlockSpec(memory_space=pltpu.SMEM)
    return pl.pallas_call(
        kernel,
        out_shape=[
            shape((length, width), LOW),
            shape((length, width), LOW),
            shape((length, width), LOW),
            shape((8, length), WIDE),
        ],
        in_specs=[smem] + [VMEM] * 9,
        out_specs=[VMEM] * 4,
        scratch_shapes=[pltpu.VMEM((length, LANES), WIDE)],
        compiler_params=pltpu.CompilerParams(vmem_limit_bytes=48 * MIB),
        cost_estimate=pl.CostEstimate(
            flops=2 * length * MAX_LEN * width,
            bytes_accessed=16 * length * width,
            transcendentals=length * MAX_LEN * heads // 2,
        ),
    )(first_block, query_raw, key_raw, values, factors, query_gain, key_gain, *tables, starts)


def attend_back(
    last_block,
    queries,
    keys,
    values,
    attended,
    upstream,
    peaks,
    query_raw,
    key_raw,
    factors,
    query_gain,
    key_gain,
    tables,
    start_row,
):
    length, width = query_raw.shape
    heads = width // HEAD

    def kernel(
        last_block,
        queries,
        keys,
        values,
        attended,
        upstream,
        peaks,
        query_raw,
        key_raw,
        factors,
        query_gain,
        key_gain,
        cosine,
        sine,
        start_row,
        query_out,
        key_out,
        value_out,
        projections,
        query_gain_grad,
        key_gain_grad,
        query_sum,
        key_sum,
        value_sum,
        columns_scratch,
        deltas,
    ):
        lane = lax.broadcasted_iota(jnp.int32, (BLOCK, LANES), 1)
        query_gain_grad[...] = jnp.zeros_like(query_gain_grad)
        key_gain_grad[...] = jnp.zeros_like(key_gain_grad)

        def prepare(index):
            at = row_slice(index, BLOCK)
            column = jnp.zeros((BLOCK, LANES), WIDE)
            for head in range(heads):
                columns = head_columns(head)
                delta = jnp.sum(
                    attended[at, columns].astype(WIDE) * upstream[at, columns].astype(WIDE),
                    axis=1,
                    keepdims=True,
                )
                column = jnp.where(lane == head, delta, column)
            columns_scratch[at] = column
            query_sum[at] = jnp.zeros((BLOCK, width), WIDE)

        loop(length // BLOCK, prepare)
        deltas[...] = columns_scratch[...].T[:8]
        row_index = lax.broadcasted_iota(jnp.int32, (BLOCK, BLOCK), 0)
        column_index = lax.broadcasted_iota(jnp.int32, (BLOCK, BLOCK), 1)

        def turn_back(at, summed, raw, gain, factor, out, gain_grad):
            cos, sin = cosine[at], sine[at]
            share = jnp.zeros((BLOCK, 1), WIDE)
            for head in range(heads):
                columns = head_columns(head)
                normed = turn(summed(head) * SCALE, cos, -sin)
                out[at, columns] = normed
                weighed = normed * raw[at, columns]
                share += jnp.sum(gain[:, columns] * weighed, axis=1, keepdims=True)
                gain_grad[:, columns] += jnp.sum(weighed * factor, axis=0, keepdims=True)
            return share

        def key_block(index):
            at = row_slice(index, BLOCK)
            key_sum[...] = jnp.zeros_like(key_sum)
            value_sum[...] = jnp.zeros_like(value_sum)

            def query_block(other, carry):
                there = row_slice(other, BLOCK)
                key_place = row_index + index * BLOCK
                allowed = (key_place >= start_row[:, there]) & (
                    key_place <= column_index + other * BLOCK
                )
                for head in range(heads):
                    columns = head_columns(head)
                    scores = nt(keys[at, columns], queries[there, columns]) * SCALE_TWO
                    scores = jnp.where(allowed, scores, NEGATIVE)
                    chance = jnp.exp2(scores - peaks[head : head + 1, there])
                    value_sum[:, columns] += jnp.dot(
                        chance.astype(LOW), upstream[there, columns], preferred_element_type=WIDE
                    )
                    chance_grad = nt(values[at, columns], upstream[there, columns])
                    score_grad = (chance * (chance_grad - deltas[head : head + 1, there])).astype(LOW)
                    key_sum[:, columns] += jnp.dot(
                        score_grad, queries[there, columns], preferred_element_type=WIDE
                    )
                    query_sum[there, columns] += lax.dot_general(
                        score_grad,
                        keys[at, columns],
                        (((0,), (0,)), ((), ())),
                        preferred_element_type=WIDE,
                    )
                return carry

            lax.fori_loop(index, last_block[index] + 1, query_block, 0)
            value_out[at] = value_sum[...].astype(LOW)
            share = turn_back(
                at,
                lambda head: key_sum[:, head_columns(head)],
                key_raw,
                key_gain,
                factors[at, 1:2],
                key_out,
                key_gain_grad,
            )
            columns_scratch[at] = jnp.where(lane == 1, share, 0.0)

        loop(length // BLOCK, key_block)

        def finish(index):
            at = row_slice(index, BLOCK)
            share = turn_back(
                at,
                lambda head: query_sum[at, head_columns(head)],
                query_raw,
                query_gain,
                factors[at, 0:1],
                query_out,
                query_gain_grad,
            )
            columns_scratch[at] += jnp.where(lane == 0, share, 0.0)

        loop(length // BLOCK, finish)
        projections[...] = columns_scratch[...].T[:8]

    shape = jax.ShapeDtypeStruct
    smem = pl.BlockSpec(memory_space=pltpu.SMEM)
    return pl.pallas_call(
        kernel,
        out_shape=[
            shape((length, width), WIDE),
            shape((length, width), WIDE),
            shape((length, width), LOW),
            shape((8, length), WIDE),
            shape((1, width), WIDE),
            shape((1, width), WIDE),
        ],
        in_specs=[smem] + [VMEM] * 14,
        out_specs=[VMEM] * 6,
        scratch_shapes=[
            pltpu.VMEM((length, width), WIDE),
            pltpu.VMEM((BLOCK, width), WIDE),
            pltpu.VMEM((BLOCK, width), WIDE),
            pltpu.VMEM((length, LANES), WIDE),
            pltpu.VMEM((8, length), WIDE),
        ],
        compiler_params=pltpu.CompilerParams(vmem_limit_bytes=52 * MIB),
        cost_estimate=pl.CostEstimate(
            flops=5 * length * MAX_LEN * width,
            bytes_accessed=32 * length * width,
            transcendentals=length * MAX_LEN * heads // 2,
        ),
    )(
        last_block,
        queries,
        keys,
        values,
        attended,
        upstream,
        peaks,
        query_raw,
        key_raw,
        factors,
        query_gain,
        key_gain,
        *tables,
        start_row,
    )


def shards(
    tokens,
    query_weight,
    key_weight,
    value_weight,
    output_weight,
    gate_weight,
    up_weight,
    down_weight,
    query_gain,
    key_gain,
    attn_gain,
    mlp_gain,
    seq_ids,
    out_grad,
):
    segment = seq_ids[0]
    length = tokens.shape[0]
    local_width = tokens.shape[1]
    cosine, sine = rotary_tables(segment)
    tables = (
        jnp.concatenate([cosine, cosine], axis=1),
        jnp.concatenate([-sine, sine], axis=1),
    )
    order = jnp.arange(length, dtype=jnp.int32)
    starts = order - token_positions(segment)
    blocks = length // BLOCK
    first_block = starts.reshape(blocks, BLOCK)[:, 0] // BLOCK
    closing = segment.reshape(blocks, BLOCK)[:, -1]
    ends = jnp.sum((segment[None, :] <= closing[:, None]).astype(jnp.int32), axis=1) - 1
    last_block = ends // BLOCK
    gains = jnp.concatenate([attn_gain[None], mlp_gain[None], jnp.zeros((6, local_width))], axis=0)
    query_gain, key_gain = query_gain.reshape(1, -1), key_gain.reshape(1, -1)
    middle = local_width // 2
    pairs = (
        (query_weight, key_weight[:, :middle]),
        (key_weight[:, middle:], value_weight),
    )
    inputs, attn_stack, query_raw, key_raw, values, squares, halves = gather_in(
        tokens, jnp.stack([jnp.concatenate(pair, axis=1) for pair in pairs]), gains, 1
    )
    attn_half, mlp_half = halves[:1], halves[1:2]
    squares, output_weight = lax.optimization_barrier((squares, output_weight))
    output_full = lax.all_gather(output_weight, "gy", axis=1, tiled=True)
    factors = lax.rsqrt(squares[:2].T / D + EPS)
    queries, keys, attended, peaks = attend(
        first_block,
        query_raw,
        key_raw,
        values,
        factors,
        query_gain,
        key_gain,
        tables,
        starts[:, None],
    )
    attn_raw, mixed, mlp_inputs, gate_full, up_full, down_full, upstream = attn_out(
        attended, output_full, attn_half, inputs, out_grad, gate_weight, up_weight, down_weight, 2
    )
    result, mlp_full, mlp_gain_part, hidden, gate, up = mlp_forward(
        mlp_inputs, gate_full, up_full, down_full, mlp_half, mixed, upstream, 3
    )
    gate_grad, up_grad, down_turned = hidden_back(mlp_full, down_full, hidden, gate, up, 4)
    down_weight_grad = down_turned.T
    mixed_grad, attn_full, attn_gain_part, gate_weight_grad, up_weight_grad = mlp_back(
        gate_grad, up_grad, gate_full, up_full, mlp_inputs, attn_half, upstream, attn_raw, 5
    )
    output_product = lax.dot_general(
        attended, attn_full, (((0,), (0,)), ((), ())), preferred_element_type=jnp.float32
    )
    output_weight_grad = lax.psum_scatter(
        output_product.astype(jnp.bfloat16), "gy", scatter_dimension=1, tiled=True
    ).astype(jnp.float32)
    attended_grad = lax.dot_general(
        attn_full, output_full, (((1,), (1,)), ((), ())), preferred_element_type=jnp.float32
    ).astype(jnp.bfloat16)
    query_back, key_back, value_grad, projections, query_gain_part, key_gain_part = attend_back(
        last_block,
        queries,
        keys,
        values,
        attended,
        attended_grad,
        peaks,
        query_raw,
        key_raw,
        factors,
        query_gain,
        key_gain,
        tables,
        starts[None, :],
    )
    token_grad, attn_weight_grads, gain_grads = attn_in_back(
        query_back,
        key_back,
        value_grad,
        query_raw,
        key_raw,
        factors,
        projections,
        query_gain,
        key_gain,
        attn_stack,
        inputs,
        mixed_grad,
        (query_gain_part, key_gain_part, attn_gain_part, mlp_gain_part),
        6,
    )
    query_weight_grad = attn_weight_grads[:, :local_width]
    key_weight_grad = attn_weight_grads[:, local_width : 2 * local_width]
    value_weight_grad = attn_weight_grads[:, 2 * local_width :]
    query_gain_grad, key_gain_grad, attn_gain_grad, mlp_gain_grad = (gain_grads[i] for i in range(4))
    return (
        result,
        token_grad,
        query_weight_grad,
        key_weight_grad,
        value_weight_grad,
        output_weight_grad,
        gate_weight_grad,
        up_weight_grad,
        down_weight_grad,
        query_gain_grad,
        key_gain_grad,
        attn_gain_grad,
        mlp_gain_grad,
    )


def solution(mesh):
    return jax.shard_map(
        shards,
        mesh=mesh,
        in_specs=(
            P("gy", "gx"),
            P("gy", "gx"),
            P("gy", "gx"),
            P("gy", "gx"),
            P("gx", "gy"),
            P("gy", "gx"),
            P("gy", "gx"),
            P("gx", "gy"),
            P("gx"),
            P("gx"),
            P("gx"),
            P("gx"),
            P("gy", None),
            P("gy", "gx"),
        ),
        out_specs=(
            P("gy", "gx"),
            P("gy", "gx"),
            P("gy", "gx"),
            P("gy", "gx"),
            P("gy", "gx"),
            P("gx", "gy"),
            P("gy", "gx"),
            P("gy", "gx"),
            P("gx", "gy"),
            P("gx"),
            P("gx"),
            P("gx"),
            P("gx"),
        ),
        check_vma=False,
    )
```

```python
import math

import jax
import jax.numpy as jnp
from jax import lax
from jax.experimental import pallas as pl
from jax.experimental.pallas import tpu as pltpu
from jax.sharding import PartitionSpec as P

D = 2048
HEAD = 128
MAX_LEN = 1024
SEGS = 4


EPS = 1e-06
THETA = 500000.0
NEGATIVE = -1e30


MESH = pl.DeviceIdType.MESH
HBM = pl.BlockSpec(memory_space=pltpu.HBM)
VMEM = pl.BlockSpec(memory_space=pltpu.VMEM)
LOW = jnp.bfloat16
WIDE = jnp.float32
MIB = 1 << 20
LAG = 2
STATS = 128


def core_here():
    return lax.rem(lax.axis_index("gx"), 2)


def chip_here():
    return lax.div(lax.axis_index("gx"), 2)


def other_core():
    return lax.axis_index("gx") + 1 - 2 * core_here()


def peer_at(shift):
    return lax.rem(lax.axis_index("gx") + 2 * shift, lax.axis_size("gx"))


def rank_at(shift):
    return lax.rem(lax.axis_index("gx") + shift, lax.axis_size("gx"))


def block_at(shift):
    return lax.rem(lax.axis_index("gy") + shift, lax.axis_size("gy"))


def ring_place():
    count = lax.axis_size("gy")
    index = lax.axis_index("gy")
    row, side = lax.div(index, 2), lax.rem(index, 2)
    return side * row + (1 - side) * (count - 1 - row)


def ring_device(place):
    count = lax.axis_size("gy")
    place = lax.rem(place + 2 * count, count)
    back = lax.div(place, count // 2)
    row = (1 - back) * place + back * (count - 1 - place)
    return 2 * row + 1 - back


def greet(gx, ring, all_blocks=False):
    barrier = pltpu.get_barrier_semaphore()
    partners = []
    if all_blocks:
        partners += [{"gy": block_at(k)} for k in range(1, lax.axis_size("gy"))]
    if gx == "all":
        partners += [{"gx": rank_at(k)} for k in range(1, lax.axis_size("gx"))]
    elif gx:
        partners.append({"gx": other_core()})
        partners += [{"gx": peer_at(k)} for k in range(1, lax.axis_size("gx") // 2)]
    if ring:
        place = ring_place()
        partners += [{"gy": ring_device(place + 1)}, {"gy": ring_device(place - 1)}]
    for partner in partners:
        pl.semaphore_signal(barrier, inc=1, device_id=partner, device_id_type=MESH)
    pl.semaphore_wait(barrier, len(partners))


def remote(source, target, send, recv, device):
    return pltpu.make_async_remote_copy(
        src_ref=source,
        dst_ref=target,
        send_sem=send,
        recv_sem=recv,
        device_id=device,
        device_id_type=MESH,
    )


def loop(count, body):
    def step(index, carry):
        body(index)
        return carry

    lax.fori_loop(0, count, step, 0)


def aligned(value, factor):
    return pl.multiple_of(value, factor)


class RingGather:
    def __init__(self, sources, slot, spill, parts, send, recv, local, spilled):
        self.sources, self.slot, self.spill, self.parts = sources, slot, spill, parts
        self.send, self.recv, self.local, self.spilled = send, recv, local, spilled
        self.count = lax.axis_size("gy")

    @staticmethod
    def scratch(parts):
        count = lax.axis_size("gy")
        return [
            pltpu.SemaphoreType.DMA((count - 1, 2, parts)),
            pltpu.SemaphoreType.DMA((count - 1, 2, parts)),
            pltpu.SemaphoreType.DMA((2, parts)),
            pltpu.SemaphoreType.DMA((count, 2, parts)),
        ]

    def spill_copy(self, way, step, part):
        place = ring_place()
        owner = ring_device(place - (1 - 2 * way) * step)
        return pltpu.make_async_copy(
            self.slot(way, owner, part),
            self.spill(way, owner, part),
            self.spilled.at[step, way, part],
        )

    def copy(self, way, step, part, behind):
        place = ring_place()
        sign = 1 - 2 * way
        spot = self.slot(way, ring_device(place - sign * (step + behind)), part)
        return remote(
            spot,
            spot,
            self.send.at[step, way, part],
            self.recv.at[step, way, part],
            {"gy": ring_device(place + sign)},
        )

    def begin(self):
        place = [
            pltpu.make_async_copy(
                self.sources(way, part),
                self.slot(way, lax.axis_index("gy"), part),
                self.local.at[way, part],
            )
            for way in range(2)
            for part in range(self.parts)
        ]
        for item in place:
            item.start()
        for item in place:
            item.wait()
        for part in range(self.parts):
            for way in range(2):
                self.copy(way, 0, part, 0).start()
                self.spill_copy(way, 0, part).start()

    @property
    def events(self):
        return (self.count - 2) * self.parts

    def event(self, index):
        step = 1 + lax.div(index, self.parts)
        for part in range(self.parts):

            @pl.when(lax.rem(index, self.parts) == part)
            def _():
                for way in range(2):
                    self.copy(way, step - 1, part, 1).wait_recv()
                    self.copy(way, step, part, 0).start()
                    self.spill_copy(way, step, part).start()

    def end(self):
        for part in range(self.parts):
            for way in range(2):
                self.copy(way, self.count - 2, part, 1).wait_recv()
                self.spill_copy(way, self.count - 1, part).start()

        def drain(step):
            for part in range(self.parts):
                for way in range(2):
                    self.copy(way, step, part, 0).wait_send()

        loop(self.count - 1, drain)

    def settle(self):
        def drain(step):
            for part in range(self.parts):
                for way in range(2):
                    self.spill_copy(way, step, part).wait()

        loop(self.count, drain)


class RingScatter:
    def __init__(self, product, total, sums, land, send, recv, credit, slots, parts):
        self.product, self.total, self.sums, self.land = product, total, sums, land
        self.send, self.recv, self.credit = send, recv, credit
        self.slots, self.parts = slots, parts
        self.count = lax.axis_size("gy")
        self.rows = total.shape[1] // parts

    @staticmethod
    def scratch(rows, columns, slots, parts):
        count = lax.axis_size("gy")
        return [
            pltpu.VMEM((2, rows, columns), WIDE),
            pltpu.VMEM((2, rows, columns), LOW),
            pltpu.VMEM((slots, 2, rows, columns), LOW),
            pltpu.SemaphoreType.DMA((count - 1, 2, parts)),
            pltpu.SemaphoreType.DMA((count - 1, 2, parts)),
            pltpu.SemaphoreType.REGULAR((2, parts)),
        ]

    def copy(self, way, step, part):
        place = ring_place()
        rows = pl.ds(aligned(part * self.rows, self.rows), self.rows)
        return remote(
            self.sums.at[way, rows],
            self.land.at[lax.rem(step, self.slots), way, rows],
            self.send.at[step, way, part],
            self.recv.at[step, way, part],
            {"gy": ring_device(place + 1 - 2 * way)},
        )

    def owner(self, way, step):
        sign = 1 - 2 * way
        return ring_device(ring_place() - sign * (1 + step))

    @property
    def events(self):
        return self.count * self.parts

    def event(self, index):
        step, part = lax.div(index, self.parts), lax.rem(index, self.parts)
        last = self.count - 1
        tile = min(self.rows, 32)

        @pl.when(part == 0)
        def _():
            for way in range(2):
                self.product(way, step)

        for way in range(2):
            base = part * self.rows

            @pl.when(step >= 1)
            def _():
                self.copy(way, step - 1, part).wait_recv()
                slot = lax.rem(step - 1, self.slots)

                @pl.loop(0, self.rows // tile)
                def _(index):
                    rows = pl.ds(aligned(base + index * tile, tile), tile)
                    self.total[way, rows] += self.land[slot, way, rows].astype(WIDE)

                @pl.when(step - 1 + self.slots < last)
                def _():
                    upstream = ring_device(ring_place() - (1 - 2 * way))
                    pl.semaphore_signal(
                        self.credit.at[way, part],
                        inc=1,
                        device_id={"gy": upstream},
                        device_id_type=MESH,
                    )

            @pl.when(step < last)
            def _():
                @pl.when(step >= 1)
                def _():
                    self.copy(way, step - 1, part).wait_send()

                @pl.loop(0, self.rows // tile)
                def _(index):
                    rows = pl.ds(aligned(base + index * tile, tile), tile)
                    self.sums[way, rows] = self.total[way, rows].astype(LOW)

                @pl.when(step >= self.slots)
                def _():
                    pl.semaphore_wait(self.credit.at[way, part], 1)

                self.copy(way, step, part).start()

    def end(self):
        for part in range(self.parts):
            for way in range(2):
                self.copy(way, self.count - 2, part).wait_send()


class Reduce:
    def __init__(self, refs, cross_land, rows, width, scatter):
        (
            self.keep,
            self.core_send,
            self.core_land,
            self.cross,
            self.cross_stage,
            self.raw,
            self.core_sems,
            self.cross_send_sems,
            self.cross_recv_sems,
            self.stage_sems,
        ) = refs
        self.cross_land = cross_land
        self.rows, self.width, self.scatter = rows, width, scatter
        self.chips = lax.axis_size("gx") // 2

    @staticmethod
    def scratch(rows, chunks, width, scatter):
        chips = lax.axis_size("gx") // 2
        half = chips * width
        part = width if scatter else half
        return [
            pltpu.VMEM((1, rows, half), LOW),
            pltpu.VMEM((2, rows, half), LOW),
            pltpu.VMEM((2, rows, half), LOW),
            pltpu.VMEM((LAG + 2, chips, rows, width) if scatter else (LAG + 2, rows, half), LOW),
            pltpu.VMEM((chips - 1, rows, part), LOW),
            pltpu.VMEM((rows, part), WIDE),
            pltpu.SemaphoreType.DMA((2, chunks)),
            pltpu.SemaphoreType.DMA((chips - 1, chunks)),
            pltpu.SemaphoreType.DMA((chips - 1, chunks)),
            pltpu.SemaphoreType.DMA((chips,)),
        ]

    @staticmethod
    def landing(rows, chunks, width, scatter):
        chips = lax.axis_size("gx") // 2
        half = chips * width
        part = width if scatter else half
        return [jax.ShapeDtypeStruct((chips - 1, chunks, rows, part), LOW)]

    def core_copy(self, chunk):
        return remote(
            self.core_send.at[lax.rem(chunk, 2)],
            self.core_land.at[lax.rem(chunk, 2)],
            self.core_sems.at[0, chunk],
            self.core_sems.at[1, chunk],
            {"gx": other_core()},
        )

    def cross_copy(self, shift, chunk):
        source = self.cross.at[lax.rem(chunk, LAG + 2)]
        if self.scatter:
            block = lax.rem(chip_here() + shift, self.chips)
            source = source.at[block]
        return remote(
            source,
            self.cross_land.at[shift - 1, chunk],
            self.cross_send_sems.at[shift - 1, chunk],
            self.cross_recv_sems.at[shift - 1, chunk],
            {"gx": peer_at(shift)},
        )

    def produce(self, chunk, dot):
        @pl.when(chunk >= 2)
        def _():
            self.core_copy(chunk - 2).wait_send()

        slot = lax.rem(chunk, 2)
        core = core_here()
        for chip in range(self.chips):
            place = aligned((2 * chip + 1 - core) * self.width, self.width)
            self.core_send[slot, :, chip * self.width : (chip + 1) * self.width] = dot(
                place
            ).astype(LOW)
        self.core_copy(chunk).start()
        for chip in range(self.chips):
            place = aligned((2 * chip + core) * self.width, self.width)
            self.keep[0, :, chip * self.width : (chip + 1) * self.width] = dot(
                place
            ).astype(LOW)

    def core_sum(self, chunk):
        slot, place = lax.rem(chunk, 2), lax.rem(chunk, LAG + 2)
        self.core_copy(chunk).wait_recv()

        @pl.when(chunk >= LAG + 2)
        def _():
            for shift in range(1, self.chips):
                self.cross_copy(shift, chunk - LAG - 2).wait_send()

        @pl.loop(0, self.rows // 32)
        def _(index):
            rows = pl.ds(aligned(index * 32, 32), 32)
            total = self.keep[0, rows].astype(WIDE) + self.core_land[slot, rows].astype(WIDE)
            if self.scatter:
                for chip in range(self.chips):
                    columns = slice(chip * self.width, (chip + 1) * self.width)
                    self.cross[place, chip, rows] = total[:, columns].astype(LOW)
            else:
                self.cross[place, rows] = total.astype(LOW)

        for shift in range(1, self.chips):
            self.cross_copy(shift, chunk).start()

    def cross_stage_copy(self, shift, chunk):
        return pltpu.make_async_copy(
            self.cross_land.at[shift - 1, chunk],
            self.cross_stage.at[shift - 1],
            self.stage_sems.at[shift],
        )

    def cross_fetch(self, chunk):
        for shift in range(1, self.chips):
            self.cross_copy(shift, chunk).wait_recv()
            self.cross_stage_copy(shift, chunk).start()

    def cross_sum(self, chunk):
        place = lax.rem(chunk, LAG + 2)
        for shift in range(1, self.chips):
            self.cross_stage_copy(shift, chunk).wait()

        @pl.loop(0, self.rows // 32)
        def _(index):
            rows = pl.ds(aligned(index * 32, 32), 32)
            if self.scatter:
                total = self.cross[place, chip_here(), rows].astype(WIDE)
            else:
                total = self.cross[place, rows].astype(WIDE)
            for shift in range(1, self.chips):
                total = total + self.cross_stage[shift - 1, rows].astype(WIDE)
            self.raw[rows] = total

    def end(self, chunks):
        for chunk in (chunks - 2, chunks - 1):
            self.core_copy(chunk).wait_send()
        for chunk in range(chunks - LAG - 2, chunks):
            for shift in range(1, self.chips):
                self.cross_copy(shift, chunk).wait_send()


class Stats:
    def __init__(self, mine, land, sems):
        self.mine, self.land, self.sems = mine, land, sems

    @staticmethod
    def scratch(rows, chunks):
        return [
            pltpu.VMEM((2, rows, STATS), WIDE),
            pltpu.VMEM((chunks, rows, STATS), WIDE),
            pltpu.SemaphoreType.DMA((2, chunks)),
        ]

    def copy(self, chunk):
        return remote(
            self.mine.at[lax.rem(chunk, 2)],
            self.land.at[chunk],
            self.sems.at[0, chunk],
            self.sems.at[1, chunk],
            {"gx": other_core()},
        )

    def clear(self, chunk):
        @pl.when(chunk >= 2)
        def _():
            self.copy(chunk - 2).wait_send()

    def put(self, chunk, rows, first, second):
        lane = lax.broadcasted_iota(jnp.int32, (first.shape[0], STATS), 1)
        self.mine[lax.rem(chunk, 2), rows] = jnp.where(lane < STATS // 2, first, second)

    def get(self, chunk, rows):
        total = self.mine[lax.rem(chunk, 2), rows] + self.land[chunk, rows]
        return (total[:, :1], total[:, STATS // 2 : STATS // 2 + 1])

    def end(self, chunks):
        for chunk in (chunks - 2, chunks - 1):
            self.copy(chunk).wait_send()


class Spread:
    def __init__(self, buffer, whole, local, send, recv, rows, width):
        self.buffer, self.whole = buffer, whole
        self.local, self.send, self.recv = local, send, recv
        self.rows, self.width = rows, width
        self.chips = lax.axis_size("gx") // 2

    @staticmethod
    def scratch(rows, chunks, width):
        chips = lax.axis_size("gx") // 2
        return [
            pltpu.VMEM((2, chips, rows, width), LOW),
            pltpu.SemaphoreType.DMA((2, chips)),
            pltpu.SemaphoreType.DMA((chunks, chips)),
            pltpu.SemaphoreType.DMA((chunks, chips)),
        ]

    def pair(self, chunk, chip, core):
        slot = lax.rem(chunk, 2)
        source = self.buffer.at[slot, chip]
        rows = pl.ds(aligned(chunk * self.rows, self.rows), self.rows)
        rank = 2 * chip + core
        if len(self.whole.shape) == 3:
            target = self.whole.at[rank, rows]
        else:
            columns = pl.ds(aligned(rank * self.width, self.width), self.width)
            target = self.whole.at[rows, columns]
        here = pltpu.make_async_copy(source, target, self.local.at[slot, chip])
        away = remote(
            source,
            target,
            self.send.at[chunk, chip],
            self.recv.at[chunk, chip],
            {"gx": other_core()},
        )
        return (here, away)

    def put(self, chunk, rows, values):
        for chip in range(self.chips):
            columns = slice(chip * self.width, (chip + 1) * self.width)
            self.buffer[lax.rem(chunk, 2), chip, rows] = values[:, columns].astype(LOW)

    def clear(self, chunk):
        @pl.when(chunk >= 2)
        def _():
            self.settle(chunk - 2)

    def settle(self, chunk):
        for chip in range(self.chips):
            here, away = self.pair(chunk, chip, core_here())
            here.wait()
            away.wait_send()

    def go(self, chunk):
        for chip in range(self.chips):
            here, away = self.pair(chunk, chip, core_here())
            here.start()
            away.start()

    def end(self, chunks):
        for chunk in (chunks - 2, chunks - 1):
            self.settle(chunk)

        def arrive(chunk):
            for chip in range(self.chips):
                self.pair(chunk, chip, 1 - core_here())[1].wait_recv()

        loop(chunks, arrive)


def row_slice(chunk, rows):
    return pl.ds(aligned(chunk * rows, rows), rows)


def core_blocks(source, chunk, rows, width, buffer, sems):
    return [
        pltpu.make_async_copy(
            source.at[2 * chip + core_here(), row_slice(chunk, rows)],
            buffer.at[:, chip * width : (chip + 1) * width],
            sems.at[chip],
        )
        for chip in range(lax.axis_size("gx") // 2)
    ]


def all_blocks(source, rows, width, buffer, sems):
    return [
        pltpu.make_async_copy(
            source.at[rank] if rows is None else source.at[rank, rows],
            buffer.at[:, rank * width : (rank + 1) * width],
            sems.at[rank],
        )
        for rank in range(source.shape[0])
    ]


def tiles(rows, body):
    @pl.loop(0, rows // 32)
    def _(index):
        body(pl.ds(aligned(index * 32, 32), 32))


def schedule(chunks, reduce, multiply, fetch, sums, finish, event=None, events=0, prepare=None):
    steps = chunks + 1 + LAG

    def iteration(step):
        if event is not None:
            low = lax.div(step * events, steps)
            high = lax.div((step + 1) * events, steps)

            def some(index, carry):
                event(index)
                return carry

            lax.fori_loop(low, high, some, 0)

        @pl.when((step >= LAG) & (step < chunks + LAG))
        def _():
            reduce.cross_fetch(step - LAG)

        @pl.when(step >= LAG)
        def _():
            fetch(step - LAG)

        @pl.when(step < chunks)
        def _():
            if prepare is not None:
                prepare(step)
            reduce.produce(step, lambda place: multiply(step, place))
            reduce.core_sum(step)

        @pl.when(step >= 1 + LAG)
        def _():
            finish(step - 1 - LAG)

        @pl.when((step >= LAG) & (step < chunks + LAG))
        def _():
            reduce.cross_sum(step - LAG)
            sums(step - LAG)

    loop(steps, iteration)


def take(refs, counts):
    groups, start = [], 0
    for count in counts:
        groups.append(refs[start : start + count])
        start += count
    return groups


class Columns:
    def __init__(self, source, shard, left, turned, sem):
        self.source, self.shard = source, shard
        self.left, self.turned, self.sem = left, turned, sem

    @staticmethod
    def scratch(length, shard):
        return [
            pltpu.VMEM((length, shard), LOW),
            pltpu.VMEM((shard, length), LOW),
            pltpu.SemaphoreType.DMA((1,)),
        ]

    def copy(self, owner):
        each = self.source.shape[2] // self.shard
        at = pl.ds(aligned(lax.rem(owner, each) * self.shard, self.shard), self.shard)
        source = self.source.at[lax.div(owner, each), :, at]
        return pltpu.make_async_copy(source, self.left, self.sem.at[0])

    def take(self, ring, way, step):
        self.copy(ring.owner(way, step)).wait()
        self.turned[...] = self.left[...].T
        if way == 0:
            self.copy(ring.owner(1, step)).start()
        else:

            @pl.when(step + 1 < ring.count)
            def _():
                self.copy(ring.owner(0, step + 1)).start()


def attn_out(
    attended, weight, gain, tokens, out_grad, gate_shard, up_shard, down_shard, collective
):
    length, width = attended.shape
    chips = lax.axis_size("gx") // 2
    half = chips * width
    count = lax.axis_size("gy")
    chunks = count
    rows = length // chunks
    hidden = gate_shard.shape[1]
    inner = down_shard.shape[0]
    shard = gate_shard.shape[0]
    part_rows = shard // 2
    side = inner // 2
    down_columns = down_shard.shape[1]

    groups = [
        Reduce.scratch(rows, chunks, width, False),
        Stats.scratch(rows, chunks),
        Spread.scratch(rows, chunks, width),
        RingGather.scratch(3),
        [
            pltpu.VMEM((rows, half), LOW),
            pltpu.VMEM((2, rows, half), WIDE),
            pltpu.VMEM((2, rows, half), LOW),
            pltpu.SemaphoreType.DMA((chips,)),
            pltpu.SemaphoreType.DMA((2,)),
            pltpu.SemaphoreType.DMA((2,)),
            pltpu.SemaphoreType.DMA((2,)),
            pltpu.SemaphoreType.DMA((chips - 1, chunks, 2)),
        ],
        [
            pltpu.VMEM((2, D, hidden), LOW),
            pltpu.VMEM((count, inner, down_columns), LOW),
            pltpu.VMEM((chips, length, width), LOW),
        ],
    ]

    def kernel(*refs):
        ins, outs, *scratch = take(refs, [8, 8] + [len(g) for g in groups])
        attended, weight, gain, tokens, out_grad, gate_shard, up_shard, down_shard = ins
        raw_out, mixed_out, low_out, gate_full, up_full, down_full, upstream = outs[:7]
        cross_land = outs[7]
        reduce = Reduce(scratch[0], cross_land, rows, width, False)
        stats = Stats(*scratch[1])
        buffer, local, send, recv = scratch[2]
        spread = Spread(buffer, low_out, local, send, recv, rows, width)
        token_buf, mixed_buf, raw_buf = scratch[4][:3]
        token_sems, mixed_sems, raw_sems, own_sem, up_sems = scratch[4][3:]
        held, held_down, up_land = scratch[5]
        shards_here = (gate_shard, up_shard)

        def place_in(full, down):
            def slot(way, owner, part):
                if part == 2:
                    return down.at[owner, way * side : (way + 1) * side]
                base = owner * shard + part * part_rows
                return full[way].at[pl.ds(aligned(base, part_rows), part_rows)]

            return slot

        slot = place_in((held.at[0], held.at[1]), held_down)
        spill = place_in((gate_full, up_full), down_full)

        def source(way, part):
            if part == 2:
                return down_shard.at[way * side : (way + 1) * side]
            return shards_here[way].at[part * part_rows : (part + 1) * part_rows]

        ring = RingGather(source, slot, spill, 3, *scratch[3])
        own = pltpu.make_async_copy(out_grad, up_land.at[chip_here()], own_sem.at[0])
        up_spill = pltpu.make_async_copy(up_land, upstream, own_sem.at[1])

        def crossings(chunk):
            at = row_slice(chunk, rows)
            return [
                remote(
                    up_land.at[chip_here(), at],
                    up_land.at[chip_here(), at],
                    up_sems.at[shift - 1, chunk, 0],
                    up_sems.at[shift - 1, chunk, 1],
                    {"gx": peer_at(shift)},
                )
                for shift in range(1, chips)
            ]

        own.start()
        greet(True, True)
        ring.begin()
        own.wait()

        def multiply(chunk, place):
            return jnp.dot(
                attended[row_slice(chunk, rows)],
                weight[:, pl.ds(place, width)],
                preferred_element_type=WIDE,
            )

        def prepare(chunk):
            for item in crossings(chunk):
                item.start()

        def token_copies(chunk):
            return core_blocks(tokens, chunk, rows, width, token_buf, token_sems)

        def fetch(chunk):
            @pl.when(chunk >= 1)
            def _():
                for item in token_copies(chunk - 1):
                    item.start()

        def mixed_copy(chunk):
            slot = lax.rem(chunk, 2)
            return pltpu.make_async_copy(
                mixed_buf.at[slot, :, pl.ds(aligned(chip_here() * width, width), width)],
                mixed_out.at[row_slice(chunk, rows)],
                mixed_sems.at[slot],
            )

        def raw_copy(chunk):
            slot = lax.rem(chunk, 2)
            return pltpu.make_async_copy(
                raw_buf.at[slot], raw_out.at[row_slice(chunk, rows)], raw_sems.at[slot]
            )

        def sums(chunk):
            stats.clear(chunk)

            @pl.when(chunk >= 2)
            def _():
                raw_copy(chunk - 2).wait()

            def tile(at):
                raw = reduce.raw[at]
                raw_buf[lax.rem(chunk, 2), at] = raw.astype(LOW)
                squares = jnp.sum(raw * raw, axis=1, keepdims=True)
                stats.put(chunk, at, squares, squares)

            tiles(rows, tile)
            stats.copy(chunk).start()
            raw_copy(chunk).start()

        def finish(chunk):
            slot = lax.rem(chunk, 2)
            for item in token_copies(chunk):
                item.wait()
            stats.copy(chunk).wait_recv()
            spread.clear(chunk)

            @pl.when(chunk >= 2)
            def _():
                mixed_copy(chunk - 2).wait()

            def tile(at):
                squares, _ = stats.get(chunk, at)
                factor = lax.rsqrt(squares / D + EPS)
                mixed = token_buf[at].astype(WIDE) + reduce.raw[at] * factor * gain[...]
                mixed_buf[slot, at] = mixed
                spread.put(chunk, at, mixed)

            tiles(rows, tile)
            spread.go(chunk)
            mixed_copy(chunk).start()

        schedule(chunks, reduce, multiply, fetch, sums, finish, ring.event, ring.events, prepare)
        def drain(chunk):
            for item in crossings(chunk):
                item.wait()

        loop(chunks, drain)
        up_spill.start()
        ring.end()
        up_spill.wait()
        ring.settle()
        reduce.end(chunks)
        stats.end(chunks)
        spread.end(chunks)
        for chunk in (chunks - 2, chunks - 1):
            mixed_copy(chunk).wait()
            raw_copy(chunk).wait()

    shape = jax.ShapeDtypeStruct
    out = pl.pallas_call(
        kernel,
        out_shape=[
            shape((length, half), LOW),
            shape((length, width), WIDE),
            shape((2 * chips, length, width), LOW),
            shape((shard * count, hidden), LOW),
            shape((shard * count, hidden), LOW),
            shape((count, inner, down_columns), LOW),
            shape((chips, length, width), LOW),
        ]
        + Reduce.landing(rows, chunks, width, False),
        in_specs=[VMEM, VMEM, VMEM, HBM, HBM, HBM, HBM, HBM],
        out_specs=[HBM] * 8,
        scratch_shapes=[item for group in groups for item in group],
        compiler_params=pltpu.CompilerParams(
            collective_id=collective, has_side_effects=True, vmem_limit_bytes=60 * MIB
        ),
        cost_estimate=pl.CostEstimate(
            flops=2 * length * width * D, bytes_accessed=8 * length * D, transcendentals=0
        ),
    )(attended, weight, gain, tokens, out_grad, gate_shard, up_shard, down_shard)
    return out[:7]


def mlp_forward(
    inputs, gate_full, up_full, down_first, down_second, gain, mixed, upstream, collective
):
    length, inner = inputs.shape[1], gate_full.shape[1]
    width = mixed.shape[1]
    ranks = inputs.shape[0]
    down_columns = down_first.shape[2]
    down_rows = down_first.shape[1]
    chips = lax.axis_size("gx") // 2
    half = chips * width
    chunks = lax.axis_size("gy")
    rows = length // chunks
    tile = min(512, inner)
    pieces = inner // tile

    groups = [
        Reduce.scratch(rows, chunks, width, False),
        Stats.scratch(rows, chunks),
        Spread.scratch(rows, chunks, width),
        [
            pltpu.VMEM((2, rows, half), LOW),
            pltpu.VMEM((rows, width), WIDE),
            pltpu.VMEM((2, rows, width), LOW),
            pltpu.SemaphoreType.DMA((2, chips)),
            pltpu.SemaphoreType.DMA((1,)),
            pltpu.SemaphoreType.DMA((2,)),
        ],
        [
            pltpu.VMEM((D, inner), LOW),
            pltpu.VMEM((D, inner), LOW),
            pltpu.VMEM((inner, D), LOW),
            pltpu.VMEM((2, rows, D), LOW),
            pltpu.VMEM((2, 3, rows, inner), LOW),
            pltpu.SemaphoreType.DMA((pieces, 2)),
            pltpu.SemaphoreType.DMA((2, chunks)),
            pltpu.SemaphoreType.DMA((2, ranks)),
            pltpu.SemaphoreType.DMA((2, 3)),
        ],
    ]

    def kernel(*refs):
        ins, outs, *scratch = take(refs, [8, 7] + [len(g) for g in groups])
        inputs, gate_full, up_full, down_first, down_second, gain, mixed, upstream = ins
        result, grad_out, gain_grad, hidden_out, gate_out, up_out, cross_land = outs
        gate_weight, up_weight, weight, row_buf, made = scratch[4][:5]
        piece_sems, weight_sem, row_sems, made_sems = scratch[4][5:]
        reduce = Reduce(scratch[0], cross_land, rows, width, False)
        stats = Stats(*scratch[1])
        buffer, local, send, recv = scratch[2]
        spread = Spread(buffer, grad_out, local, send, recv, rows, width)
        up_buf, mixed_buf, result_buf, up_sems, mixed_sems, result_sems = scratch[3]

        def piece_copies(piece):
            at = pl.ds(aligned(piece * tile, tile), tile)
            return [
                pltpu.make_async_copy(gate_full.at[:, at], gate_weight.at[:, at], piece_sems.at[piece, 0]),
                pltpu.make_async_copy(up_full.at[:, at], up_weight.at[:, at], piece_sems.at[piece, 1]),
            ]

        weight_copies = all_blocks(
            down_first, None, down_columns, weight.at[:down_rows], weight_sem.at[0]
        ) + all_blocks(down_second, None, down_columns, weight.at[down_rows:], weight_sem.at[1])

        def row_copy(chunk):
            slot = lax.rem(chunk, 2)
            return all_blocks(
                inputs, row_slice(chunk, rows), width, row_buf.at[slot], row_sems.at[slot]
            )

        def stores(chunk):
            slot, at = lax.rem(chunk, 2), row_slice(chunk, rows)
            return [
                pltpu.make_async_copy(made.at[slot, which], out.at[at], made_sems.at[slot, which])
                for which, out in enumerate((hidden_out, gate_out, up_out))
            ]

        for item in row_copy(0):
            item.start()
        for piece in range(pieces):
            for item in piece_copies(piece):
                item.start()
        for item in weight_copies:
            item.start()
        greet(True, False)
        gain_grad[...] = jnp.zeros_like(gain_grad)

        def prepare(chunk):
            slot = lax.rem(chunk, 2)
            for item in row_copy(chunk):
                item.wait()

            @pl.when(chunk + 1 < chunks)
            def _():
                for item in row_copy(chunk + 1):
                    item.start()

            @pl.when(chunk >= 2)
            def _():
                for item in stores(chunk - 2):
                    item.wait()

            @pl.loop(0, pieces)
            def _(piece):
                @pl.when(chunk == 0)
                def _():
                    for item in piece_copies(piece):
                        item.wait()

                at = pl.ds(aligned(piece * tile, tile), tile)
                gate = jnp.dot(row_buf[slot], gate_weight[:, at], preferred_element_type=WIDE)
                up = jnp.dot(row_buf[slot], up_weight[:, at], preferred_element_type=WIDE)
                made[slot, 0, :, at] = (gate * jax.nn.sigmoid(gate) * up).astype(LOW)
                made[slot, 1, :, at] = gate.astype(LOW)
                made[slot, 2, :, at] = up.astype(LOW)

            @pl.when(chunk == 0)
            def _():
                for item in weight_copies:
                    item.wait()

            for item in stores(chunk):
                item.start()

        def multiply(chunk, place):
            return jnp.dot(
                made[lax.rem(chunk, 2), 0],
                weight[:, pl.ds(place, width)],
                preferred_element_type=WIDE,
            )

        def up_copy(chunk):
            slot = lax.rem(chunk, 2)
            return all_blocks(
                upstream, row_slice(chunk, rows), width, up_buf.at[slot], up_sems.at[slot]
            )

        def mixed_copy(chunk):
            return pltpu.make_async_copy(
                mixed.at[row_slice(chunk, rows)], mixed_buf, mixed_sems.at[0]
            )

        def result_copy(chunk):
            slot = lax.rem(chunk, 2)
            return pltpu.make_async_copy(
                result_buf.at[slot], result.at[row_slice(chunk, rows)], result_sems.at[slot]
            )

        def fetch(chunk):
            @pl.when(chunk < chunks)
            def _():
                for item in up_copy(chunk):
                    item.start()

            @pl.when(chunk >= 1)
            def _():
                mixed_copy(chunk - 1).start()

        def sums(chunk):
            slot = lax.rem(chunk, 2)
            stats.clear(chunk)
            for item in up_copy(chunk):
                item.wait()

            def tile(at):
                raw = reduce.raw[at]
                up = up_buf[slot, at].astype(WIDE)
                squares = jnp.sum(raw * raw, axis=1, keepdims=True)
                projected = jnp.sum(gain[...] * up * raw, axis=1, keepdims=True)
                stats.put(chunk, at, squares, projected)

            tiles(rows, tile)
            stats.copy(chunk).start()

        def finish(chunk):
            slot = lax.rem(chunk, 2)
            mixed_copy(chunk).wait()
            stats.copy(chunk).wait_recv()
            spread.clear(chunk)

            @pl.when(chunk >= 2)
            def _():
                result_copy(chunk - 2).wait()

            block = pl.ds(aligned(chip_here() * width, width), width)

            def tile(at):
                squares, projected = stats.get(chunk, at)
                factor = lax.rsqrt(squares / D + EPS)
                raw = reduce.raw[at]
                up = up_buf[slot, at].astype(WIDE)
                pull = factor * factor * factor * projected / D
                spread.put(chunk, at, factor * gain[...] * up - raw * pull)
                gain_grad[...] += jnp.sum(up * raw * factor, axis=0, keepdims=True)
                result_buf[slot, at] = (
                    mixed_buf[at] + reduce.raw[at, block] * factor * gain[:, block]
                ).astype(LOW)

            tiles(rows, tile)
            spread.go(chunk)
            result_copy(chunk).start()

        schedule(chunks, reduce, multiply, fetch, sums, finish, prepare=prepare)
        reduce.end(chunks)
        stats.end(chunks)
        spread.end(chunks)
        for chunk in (chunks - 2, chunks - 1):
            result_copy(chunk).wait()
            for item in stores(chunk):
                item.wait()

    shape = jax.ShapeDtypeStruct
    out = pl.pallas_call(
        kernel,
        out_shape=[
            shape((length, width), LOW),
            shape((2 * chips, length, width), LOW),
            shape((1, half), WIDE),
            shape((length, inner), LOW),
            shape((length, inner), LOW),
            shape((length, inner), LOW),
        ]
        + Reduce.landing(rows, chunks, width, False),
        in_specs=[HBM] * 5 + [VMEM, HBM, HBM],
        out_specs=[HBM, HBM, VMEM] + [HBM] * 4,
        scratch_shapes=[item for group in groups for item in group],
        compiler_params=pltpu.CompilerParams(
            collective_id=collective, has_side_effects=True, vmem_limit_bytes=60 * MIB
        ),
        cost_estimate=pl.CostEstimate(
            flops=6 * length * inner * D, bytes_accessed=16 * length * D, transcendentals=0
        ),
    )(inputs, gate_full, up_full, down_first, down_second, gain, mixed, upstream)
    return out[:6]


def mlp_back(gate_grad, up_grad, gate_full, up_full, inputs, gain, upstream, attn_raw, collective):
    length, inner = gate_grad.shape
    half = attn_raw.shape[1]
    chips = lax.axis_size("gx") // 2
    width = half // chips
    count = lax.axis_size("gy")
    chunks = count
    rows = length // chunks
    shard = D // count
    slots, parts = 2, 2

    groups = [
        Reduce.scratch(rows, chunks, width, False),
        Stats.scratch(rows, chunks),
        Spread.scratch(rows, chunks, width),
        RingScatter.scratch(shard, inner, slots, parts),
        [
            pltpu.VMEM((rows, half), LOW),
            pltpu.VMEM((2, rows, half), LOW),
            pltpu.SemaphoreType.DMA((chips,)),
            pltpu.SemaphoreType.DMA((2,)),
            pltpu.SemaphoreType.DMA((1,)),
            pltpu.SemaphoreType.DMA((2,)),
        ],
        Columns.scratch(length, shard),
    ]

    def kernel(*refs):
        ins, outs, *scratch = take(refs, [8, 6] + [len(g) for g in groups])
        gate_grad, up_grad, gate_full, up_full, inputs, gain, upstream, attn_raw = ins
        mixed_out, grad_out, gain_grad, gate_out, up_out, cross_land = outs
        reduce = Reduce(scratch[0], cross_land, rows, width, False)
        stats = Stats(*scratch[1])
        buffer, local, send, recv = scratch[2]
        spread = Spread(buffer, grad_out, local, send, recv, rows, width)
        total, summed, land, ring_send, ring_recv, credit = scratch[3]
        up_buf, raw_buf, up_sems, raw_sems, mixed_sems, out_sems = scratch[4]
        left = Columns(inputs, shard, *scratch[5])
        grads = (gate_grad, up_grad)

        def product(way, step):
            left.take(ring, way, step)
            tile = 512

            @pl.loop(0, inner // tile)
            def _(index):
                columns = pl.ds(aligned(index * tile, tile), tile)
                total[way, :, columns] = jnp.dot(
                    left.turned[...], grads[way][:, columns], preferred_element_type=WIDE
                )

        ring = RingScatter(
            product, total, summed, land, ring_send, ring_recv, credit, slots, parts
        )
        left.copy(ring.owner(0, 0)).start()
        greet(True, True)
        gain_grad[...] = jnp.zeros_like(gain_grad)

        def multiply(chunk, place):
            at = row_slice(chunk, rows)
            return lax.dot_general(
                gate_grad[at],
                gate_full[pl.ds(place, width)],
                (((1,), (1,)), ((), ())),
                preferred_element_type=WIDE,
            ) + lax.dot_general(
                up_grad[at],
                up_full[pl.ds(place, width)],
                (((1,), (1,)), ((), ())),
                preferred_element_type=WIDE,
            )

        def up_copy(chunk):
            return all_blocks(upstream, row_slice(chunk, rows), width, up_buf, up_sems)

        def raw_copy(chunk):
            slot = lax.rem(chunk, 2)
            return pltpu.make_async_copy(
                attn_raw.at[row_slice(chunk, rows)], raw_buf.at[slot], raw_sems.at[slot]
            )

        def mixed_copy(chunk):
            return pltpu.make_async_copy(
                reduce.raw.at[:, pl.ds(aligned(chip_here() * width, width), width)],
                mixed_out.at[row_slice(chunk, rows)],
                mixed_sems.at[0],
            )

        def fetch(chunk):
            @pl.when(chunk < chunks)
            def _():
                for item in up_copy(chunk):
                    item.start()
                raw_copy(chunk).start()

        def sums(chunk):
            slot = lax.rem(chunk, 2)
            stats.clear(chunk)
            for item in up_copy(chunk):
                item.wait()
            raw_copy(chunk).wait()

            def tile(at):
                upward = reduce.raw[at] + up_buf[at].astype(WIDE)
                reduce.raw[at] = upward
                raw = raw_buf[slot, at].astype(WIDE)
                squares = jnp.sum(raw * raw, axis=1, keepdims=True)
                projected = jnp.sum(gain[...] * upward * raw, axis=1, keepdims=True)
                stats.put(chunk, at, squares, projected)

            tiles(rows, tile)
            stats.copy(chunk).start()
            mixed_copy(chunk).start()

        def finish(chunk):
            slot = lax.rem(chunk, 2)
            stats.copy(chunk).wait_recv()
            spread.clear(chunk)

            def tile(at):
                squares, projected = stats.get(chunk, at)
                factor = lax.rsqrt(squares / D + EPS)
                upward = reduce.raw[at]
                raw = raw_buf[slot, at].astype(WIDE)
                pull = factor * factor * factor * projected / D
                spread.put(chunk, at, factor * gain[...] * upward - raw * pull)
                gain_grad[...] += jnp.sum(upward * raw * factor, axis=0, keepdims=True)

            tiles(rows, tile)
            spread.go(chunk)
            mixed_copy(chunk).wait()

        schedule(chunks, reduce, multiply, fetch, sums, finish, ring.event, ring.events)
        writes = [
            pltpu.make_async_copy(total.at[way], (gate_out, up_out)[way], out_sems.at[way])
            for way in range(2)
        ]
        for item in writes:
            item.start()
        ring.end()
        reduce.end(chunks)
        stats.end(chunks)
        spread.end(chunks)
        for item in writes:
            item.wait()

    shape = jax.ShapeDtypeStruct
    out = pl.pallas_call(
        kernel,
        out_shape=[
            shape((length, width), WIDE),
            shape((length, D), LOW),
            shape((1, half), WIDE),
            shape((shard, inner), WIDE),
            shape((shard, inner), WIDE),
        ]
        + Reduce.landing(rows, chunks, width, False),
        in_specs=[VMEM, VMEM, VMEM, VMEM, HBM, VMEM, HBM, HBM],
        out_specs=[HBM, HBM, VMEM, HBM, HBM, HBM],
        scratch_shapes=[item for group in groups for item in group],
        compiler_params=pltpu.CompilerParams(
            collective_id=collective, has_side_effects=True, vmem_limit_bytes=60 * MIB
        ),
        cost_estimate=pl.CostEstimate(
            flops=8 * length * inner * D, bytes_accessed=16 * length * D, transcendentals=0
        ),
    )(gate_grad, up_grad, gate_full, up_full, inputs, gain, upstream, attn_raw)
    return out[:5]


class Total:
    def __init__(self, land, send, recv):
        self.land, self.send, self.recv = land, send, recv
        self.count = lax.axis_size("gx")

    @staticmethod
    def scratch(length):
        others = lax.axis_size("gx") - 1
        return [
            pltpu.VMEM((others, 8, length), WIDE),
            pltpu.SemaphoreType.DMA((others,)),
            pltpu.SemaphoreType.DMA((others,)),
        ]

    def copies(self, mine):
        return [
            remote(
                mine,
                self.land.at[shift - 1],
                self.send.at[shift - 1],
                self.recv.at[shift - 1],
                {"gx": rank_at(shift)},
            )
            for shift in range(1, self.count)
        ]

    def start(self, mine):
        for item in self.copies(mine):
            item.start()

    def finish(self, mine):
        for item in self.copies(mine):
            item.wait()
        total = mine[...]
        for shift in range(1, self.count):
            total = total + self.land[shift - 1]
        return total


def gather_in(tokens, stack, output_shard, gains, collective):
    length, width = tokens.shape
    _, shard, side = stack.shape
    columns = 2 * side
    count = lax.axis_size("gy")
    chunks = count
    rows = length // chunks
    chips = lax.axis_size("gx") // 2
    parts = 1
    out_columns = output_shard.shape[1]
    out_rows = width // 2

    groups = [
        RingGather.scratch(parts),
        [
            pltpu.SemaphoreType.DMA((1,)),
            pltpu.SemaphoreType.DMA((2,)),
            pltpu.SemaphoreType.DMA((chips - 1, chunks, 2)),
            pltpu.SemaphoreType.DMA((chips - 1, chunks, 2)),
        ],
        [
            pltpu.VMEM((2, D, side), LOW),
            pltpu.VMEM((2 * chips, length, width), LOW),
            pltpu.VMEM((2, 2, rows, width), WIDE),
            pltpu.VMEM((2, rows, width), LOW),
            pltpu.VMEM((length, STATS), WIDE),
            pltpu.VMEM((8, length), WIDE),
            pltpu.SemaphoreType.DMA((2,)),
            pltpu.SemaphoreType.DMA((2, 3)),
        ],
        Total.scratch(length),
        [
            pltpu.VMEM((chips - 1, 8, width), WIDE),
            pltpu.SemaphoreType.DMA((chips - 1, 2)),
        ],
        RingGather.scratch(1),
        [pltpu.VMEM((count, width, out_columns), LOW)],
    ]

    def kernel(*refs):
        ins, outs, *scratch = take(refs, [4, 8] + [len(g) for g in groups])
        tokens, stack, output_shard, gains = ins
        whole, full, output_full, query_raw, key_raw, values, squares, halves = outs
        out_held = scratch[6][0]
        gain_land, gain_sems = scratch[4]
        own_sem, core_sems, cross_sems, pass_sems = scratch[1]
        weight, held, raw_buf, value_buf, stats, mine = scratch[2][:6]
        copy_sems, out_sems = scratch[2][6:]
        total = Total(*scratch[3])

        def slot(way, owner, part):
            return weight.at[way, pl.ds(aligned(owner * shard, shard), shard)]

        def spill(way, owner, part):
            return full.at[way, pl.ds(aligned(owner * shard, shard), shard)]

        def source(way, part):
            return stack.at[way]

        ring = RingGather(source, slot, spill, parts, *scratch[0])

        def out_slot(way, owner, part):
            return out_held.at[owner, way * out_rows : (way + 1) * out_rows]

        def out_spill(way, owner, part):
            at = pl.ds(aligned(owner * out_columns, out_columns), out_columns)
            return output_full.at[way * out_rows : (way + 1) * out_rows, at]

        def out_source(way, part):
            return output_shard.at[way * out_rows : (way + 1) * out_rows]

        out_ring = RingGather(out_source, out_slot, out_spill, 1, *scratch[5])

        def block(rank, chunk):
            if chunk is None:
                return held.at[rank]
            return held.at[rank, row_slice(chunk, rows)]

        here = lax.axis_index("gx")
        own = pltpu.make_async_copy(tokens, block(here, None), own_sem.at[0])
        core = remote(
            block(here, None), block(here, None), core_sems.at[0], core_sems.at[1], {"gx": other_core()}
        )

        def cross(shift, chunk):
            return remote(
                block(here, chunk),
                block(here, chunk),
                cross_sems.at[shift - 1, chunk, 0],
                cross_sems.at[shift - 1, chunk, 1],
                {"gx": peer_at(shift)},
            )

        def onward(shift, chunk):
            spot = block(peer_at(chips - shift), chunk)
            return remote(
                spot,
                spot,
                pass_sems.at[shift - 1, chunk, 0],
                pass_sems.at[shift - 1, chunk, 1],
                {"gx": other_core()},
            )

        gain_copies = [
            remote(
                gains,
                gain_land.at[shift - 1],
                gain_sems.at[shift - 1, 0],
                gain_sems.at[shift - 1, 1],
                {"gx": peer_at(shift)},
            )
            for shift in range(1, chips)
        ]
        own.start()
        greet("all", True)
        for item in gain_copies:
            item.start()
        ring.begin()
        own.wait()

        def send(chunk):
            for shift in range(1, chips):
                cross(shift, chunk).start()

        loop(chunks, send)
        core.start()

        def step(chunk):
            for shift in range(1, chips):
                cross(shift, chunk).wait_recv()
                onward(shift, chunk).start()

            @pl.when(chunk < ring.events)
            def _():
                ring.event(chunk)

        loop(chunks, step)
        out_ring.begin()
        ring.end()

        def drain(chunk):
            for shift in range(1, chips):
                cross(shift, chunk).wait_send()
                onward(shift, chunk).wait()

        loop(chunks, drain)
        core.wait()
        whole_copy = pltpu.make_async_copy(held, whole, copy_sems.at[0])
        whole_copy.start()

        def stores(chunk):
            slot, at = lax.rem(chunk, 2), row_slice(chunk, rows)
            return [
                pltpu.make_async_copy(raw_buf.at[slot, 0], query_raw.at[at], out_sems.at[slot, 0]),
                pltpu.make_async_copy(raw_buf.at[slot, 1], key_raw.at[at], out_sems.at[slot, 1]),
                pltpu.make_async_copy(value_buf.at[slot], values.at[at], out_sems.at[slot, 2]),
            ]

        lane = lax.broadcasted_iota(jnp.int32, (rows, STATS), 1)

        def project(chunk):
            slot = lax.rem(chunk, 2)
            @pl.when(chunk >= 2)
            def _():
                for item in stores(chunk - 2):
                    item.wait()

            at = row_slice(chunk, rows)
            middle = side - width

            def against(way, columns):
                raw = jnp.zeros((rows, columns.stop - columns.start), WIDE)
                for rank in range(2 * chips):
                    raw = raw + jnp.dot(
                        held[rank, at],
                        weight[way, rank * width : (rank + 1) * width, columns],
                        preferred_element_type=WIDE,
                    )
                return raw

            some = []
            raw_buf[slot, 0] = against(0, slice(0, width))
            raw_buf[slot, 1, :, :middle] = against(0, slice(width, side))
            raw_buf[slot, 1, :, middle:] = against(1, slice(0, middle))
            value_buf[slot] = against(1, slice(middle, side)).astype(LOW)
            for which in range(2):
                raw = raw_buf[slot, which]
                some.append(jnp.sum(raw * raw, axis=1, keepdims=True))
            stats[row_slice(chunk, rows)] = jnp.where(lane == 0, some[0], some[1])
            for item in stores(chunk):
                item.start()

            @pl.when(chunk < out_ring.events)
            def _():
                out_ring.event(chunk)

        loop(chunks, project)
        mine[...] = stats[...].T[:8]
        total.start(mine)
        for chunk in (chunks - 2, chunks - 1):
            for item in stores(chunk):
                item.wait()
        squares[...] = total.finish(mine)
        whole_copy.wait()
        ring.settle()
        out_ring.end()
        out_ring.settle()
        halves[:, pl.ds(aligned(chip_here() * width, width), width)] = gains[...]
        for shift in range(1, chips):
            gain_copies[shift - 1].wait()
            chip = lax.rem(chip_here() + chips - shift, chips)
            halves[:, pl.ds(aligned(chip * width, width), width)] = gain_land[shift - 1]

    shape = jax.ShapeDtypeStruct
    return pl.pallas_call(
        kernel,
        out_shape=[
            shape((2 * chips, length, width), LOW),
            shape((2, shard * count, side), LOW),
            shape((width, D), LOW),
            shape((length, width), WIDE),
            shape((length, width), WIDE),
            shape((length, width), LOW),
            shape((8, length), WIDE),
            shape((8, chips * width), WIDE),
        ],
        in_specs=[HBM, HBM, HBM, VMEM],
        out_specs=[HBM] * 6 + [VMEM, VMEM],
        scratch_shapes=[item for group in groups for item in group],
        compiler_params=pltpu.CompilerParams(
            collective_id=collective, has_side_effects=True, vmem_limit_bytes=40 * MIB
        ),
        cost_estimate=pl.CostEstimate(
            flops=2 * length * columns * D, bytes_accessed=8 * length * D, transcendentals=0
        ),
    )(tokens, stack, output_shard, gains)


def hidden_back(blocks, down_first, down_second, hidden, gate, up, collective):
    length, inner = hidden.shape
    count = lax.axis_size("gy")
    chunks = count
    rows = length // chunks
    shard = D // count
    side = inner // 2
    slots, parts = 3, 2
    down_rows = down_first.shape[1]
    tile = min(512, inner)

    groups = [
        RingScatter.scratch(shard, side, slots, parts),
        [
            pltpu.VMEM((2, 2, rows, inner), LOW),
            pltpu.VMEM((2, 2, rows, inner), LOW),
            pltpu.SemaphoreType.DMA((2, 2)),
            pltpu.SemaphoreType.DMA((2, 2)),
            pltpu.SemaphoreType.DMA((2,)),
            pltpu.VMEM((count, shard, length), LOW),
        ],
        [
            pltpu.VMEM((length, D), LOW),
            pltpu.VMEM((inner, D), LOW),
            pltpu.SemaphoreType.DMA((blocks.shape[0],)),
            pltpu.SemaphoreType.DMA((2, count)),
        ],
    ]

    def kernel(*refs):
        ins, outs, *scratch = take(refs, [6, 3] + [len(g) for g in groups])
        blocks, down_first, down_second, hidden, gate, up = ins
        grad, weight, grad_sems, weight_sems = scratch[2]
        gate_grad, up_grad, weight_grad = outs
        total, summed, land, ring_send, ring_recv, credit = scratch[0]
        given, made, given_sems, made_sems, out_sems, turned = scratch[1]

        def product(way, step):
            owner = ring.owner(way, step)

            @pl.when((step < count // 2) | (step == count - 1))
            def _():
                turned[owner] = grad[:, pl.ds(aligned(owner * shard, shard), shard)].T

            size = min(512, side)

            @pl.loop(0, side // size)
            def _(index):
                at = pl.ds(aligned(index * size, size), size)
                take_at = pl.ds(aligned(way * side + index * size, size), size)
                total[way, :, at] = jnp.dot(
                    turned[owner], hidden[:, take_at], preferred_element_type=WIDE
                )

        ring = RingScatter(
            product, total, summed, land, ring_send, ring_recv, credit, slots, parts
        )

        def load(chunk):
            slot = lax.rem(chunk, 2)
            return [
                pltpu.make_async_copy(
                    (gate, up)[which].at[row_slice(chunk, rows)],
                    given.at[slot, which],
                    given_sems.at[slot, which],
                )
                for which in range(2)
            ]

        def store(chunk):
            slot = lax.rem(chunk, 2)
            return [
                pltpu.make_async_copy(
                    made.at[slot, which],
                    (gate_grad, up_grad)[which].at[row_slice(chunk, rows)],
                    made_sems.at[slot, which],
                )
                for which in range(2)
            ]

        grad_copies = all_blocks(blocks, None, blocks.shape[2], grad, grad_sems)
        weight_copies = all_blocks(
            down_first, None, shard, weight.at[:down_rows], weight_sems.at[0]
        ) + all_blocks(down_second, None, shard, weight.at[down_rows:], weight_sems.at[1])
        for item in grad_copies + weight_copies + load(0):
            item.start()
        greet(False, True)
        for item in grad_copies:
            item.wait()

        def iteration(step):
            slot = lax.rem(step, 2)
            for part in range(parts):
                ring.event(step * parts + part)

            @pl.when(step + 1 < chunks)
            def _():
                for item in load(step + 1):
                    item.start()

            @pl.when(step >= 2)
            def _():
                for item in store(step - 2):
                    item.wait()

            for item in load(step):
                item.wait()

            @pl.when(step == 0)
            def _():
                for item in weight_copies:
                    item.wait()

            @pl.loop(0, inner // tile)
            def _(index):
                at = pl.ds(aligned(index * tile, tile), tile)
                hidden_grad = lax.dot_general(
                    grad[row_slice(step, rows)],
                    weight[at],
                    (((1,), (1,)), ((), ())),
                    preferred_element_type=WIDE,
                )
                gate = given[slot, 0, :, at].astype(WIDE)
                up = given[slot, 1, :, at].astype(WIDE)
                sigma = jax.nn.sigmoid(gate)
                made[slot, 0, :, at] = (
                    hidden_grad * up * sigma * (1.0 + gate * (1.0 - sigma))
                ).astype(LOW)
                made[slot, 1, :, at] = (hidden_grad * gate * sigma).astype(LOW)

            for item in store(step):
                item.start()

        loop(chunks, iteration)
        writes = [
            pltpu.make_async_copy(
                total.at[way], weight_grad.at[:, way * side : (way + 1) * side], out_sems.at[way]
            )
            for way in range(2)
        ]
        for item in writes:
            item.start()
        for chunk in (chunks - 2, chunks - 1):
            for item in store(chunk):
                item.wait()
        ring.end()
        for item in writes:
            item.wait()

    shape = jax.ShapeDtypeStruct
    return pl.pallas_call(
        kernel,
        out_shape=[
            shape((length, inner), LOW),
            shape((length, inner), LOW),
            shape((shard, inner), WIDE),
        ],
        in_specs=[HBM, HBM, HBM, VMEM, HBM, HBM],
        out_specs=[HBM, HBM, HBM],
        scratch_shapes=[item for group in groups for item in group],
        compiler_params=pltpu.CompilerParams(
            collective_id=collective, has_side_effects=True, vmem_limit_bytes=60 * MIB
        ),
        cost_estimate=pl.CostEstimate(
            flops=4 * length * inner * D, bytes_accessed=16 * length * D, transcendentals=0
        ),
    )(blocks, down_first, down_second, hidden, gate, up)


def attn_in_back(
    query_back,
    key_back,
    value_grad,
    query_raw,
    key_raw,
    factors,
    projections,
    query_gain,
    key_gain,
    stack,
    inputs,
    mixed_grad,
    gain_parts,
    collective,
):
    length, columns = value_grad.shape[0], 2 * stack.shape[2]
    width = mixed_grad.shape[1]
    count = lax.axis_size("gy")
    chunks = count
    rows = length // chunks
    shard = D // count
    side = columns // 2
    slots, parts = count - 1, 2
    tile = 256 if side % 256 == 0 else 128

    groups = [
        Reduce.scratch(rows, chunks, width, True),
        RingScatter.scratch(shard, side, slots, parts),
        [
            pltpu.VMEM((rows, width), WIDE),
            pltpu.VMEM((2, rows, width), WIDE),
            pltpu.VMEM((length, columns), LOW),
            pltpu.VMEM((length, STATS), WIDE),
            pltpu.SemaphoreType.DMA((1,)),
            pltpu.SemaphoreType.DMA((2,)),
            pltpu.SemaphoreType.DMA((2,)),
        ],
        Columns.scratch(length, shard),
        Total.scratch(length),
        [
            pltpu.VMEM((8, width), WIDE),
            pltpu.VMEM((count - 1, 8, width), WIDE),
            pltpu.SemaphoreType.DMA((count - 1, 2)),
        ],
    ]

    def kernel(*refs):
        ins, outs, *scratch = take(refs, [16, 4] + [len(g) for g in groups])
        query_back, key_back, value_grad, query_raw, key_raw, factors = ins[:6]
        projections, query_gain, key_gain, stack, inputs, mixed_grad = ins[6:12]
        gain_parts = ins[12:]
        token_grad, weight_grad, gain_grads, cross_land = outs
        gain_mine, gain_land, gain_sems = scratch[5]
        reduce = Reduce(scratch[0], cross_land, rows, width, True)
        total, summed, land, ring_send, ring_recv, credit = scratch[1]
        mixed_buf, token_buf, grads, projected, mixed_sems, token_sems, out_sems = scratch[2]
        left = Columns(inputs, shard, *scratch[3])
        total_sum = Total(*scratch[4])

        def product(way, step):
            left.take(ring, way, step)

            @pl.loop(0, side // tile)
            def _(index):
                at = pl.ds(aligned(index * tile, tile), tile)
                take_at = pl.ds(aligned(way * side + index * tile, tile), tile)
                total[way, :, at] = jnp.dot(
                    left.turned[...], grads[:, take_at], preferred_element_type=WIDE
                )

        ring = RingScatter(
            product, total, summed, land, ring_send, ring_recv, credit, slots, parts
        )
        left.copy(ring.owner(0, 0)).start()
        chip_columns = pl.ds(aligned(chip_here() * width, width), width)
        gain_mine[...] = jnp.zeros_like(gain_mine)
        for which, part in enumerate(gain_parts):
            gain_mine[which : which + 1] = part[...] if which < 2 else part[:, chip_columns]
        greet("all", False, True)
        total_sum.start(projections)
        gain_copies = [
            remote(
                gain_mine,
                gain_land.at[shift - 1],
                gain_sems.at[shift - 1, 0],
                gain_sems.at[shift - 1, 1],
                {"gy": block_at(shift)},
            )
            for shift in range(1, count)
        ]
        for item in gain_copies:
            item.start()
        grads[:, 2 * width :] = value_grad[...]
        sums_here = total_sum.finish(projections)
        projected[...] = jnp.concatenate([sums_here] * (STATS // 8), axis=0).T
        pairs = ((query_back, query_raw, query_gain), (key_back, key_raw, key_gain))

        @pl.loop(0, length // 32)
        def _(index):
            at = row_slice(index, 32)
            for which, (back, raw, gain) in enumerate(pairs):
                factor = factors[at, which : which + 1]
                pull = factor * factor * factor * projected[at, which : which + 1] / D
                grads[at, which * width : (which + 1) * width] = (
                    factor * gain[...] * back[at] - raw[at] * pull
                ).astype(LOW)

        def multiply(chunk, place):
            at = row_slice(chunk, rows)
            return nt(grads[at, :side], stack[0, pl.ds(place, width)]) + nt(
                grads[at, side:], stack[1, pl.ds(place, width)]
            )

        def mixed_copy(chunk):
            return pltpu.make_async_copy(
                mixed_grad.at[row_slice(chunk, rows)], mixed_buf, mixed_sems.at[0]
            )

        def token_copy(chunk):
            slot = lax.rem(chunk, 2)
            return pltpu.make_async_copy(
                token_buf.at[slot], token_grad.at[row_slice(chunk, rows)], token_sems.at[slot]
            )

        def fetch(chunk):
            @pl.when(chunk >= 1)
            def _():
                mixed_copy(chunk - 1).start()

        def sums(chunk):
            pass

        def finish(chunk):
            slot = lax.rem(chunk, 2)
            mixed_copy(chunk).wait()

            @pl.when(chunk >= 2)
            def _():
                token_copy(chunk - 2).wait()

            def some(at):
                token_buf[slot, at] = mixed_buf[at] + reduce.raw[at]

            tiles(rows, some)
            token_copy(chunk).start()

        schedule(chunks, reduce, multiply, fetch, sums, finish, ring.event, ring.events)
        writes = [
            pltpu.make_async_copy(
                total.at[way], weight_grad.at[:, way * side : (way + 1) * side], out_sems.at[way]
            )
            for way in range(2)
        ]
        for item in writes:
            item.start()
        gain_total = gain_mine[...]
        for shift in range(1, count):
            gain_copies[shift - 1].wait()
            gain_total = gain_total + gain_land[shift - 1]
        gain_grads[...] = gain_total
        ring.end()
        reduce.end(chunks)
        for chunk in (chunks - 2, chunks - 1):
            token_copy(chunk).wait()
        for item in writes:
            item.wait()

    shape = jax.ShapeDtypeStruct
    out = pl.pallas_call(
        kernel,
        out_shape=[
            shape((length, width), WIDE),
            shape((shard, columns), WIDE),
            shape((8, width), WIDE),
        ]
        + Reduce.landing(rows, chunks, width, True),
        in_specs=[VMEM] * 10 + [HBM, HBM] + [VMEM] * 4,
        out_specs=[HBM, HBM, VMEM, HBM],
        scratch_shapes=[item for group in groups for item in group],
        compiler_params=pltpu.CompilerParams(
            collective_id=collective, has_side_effects=True, vmem_limit_bytes=60 * MIB
        ),
        cost_estimate=pl.CostEstimate(
            flops=4 * length * columns * D, bytes_accessed=8 * length * D, transcendentals=0
        ),
    )(
        query_back,
        key_back,
        value_grad,
        query_raw,
        key_raw,
        factors,
        projections,
        query_gain,
        key_gain,
        stack,
        inputs,
        mixed_grad,
        *gain_parts,
    )
    return out[:3]


def token_positions(segment):
    length = segment.shape[0]
    labels = jnp.arange(SEGS, dtype=jnp.int32)
    member = (segment[:, None] == labels[None, :]).astype(jnp.int32)
    totals = jnp.sum(member, axis=0)
    starts = jnp.cumsum(totals) - totals
    opening = jnp.sum(member * starts[None, :], axis=1)
    return jnp.arange(length, dtype=jnp.int32) - opening


def rotary_tables(segment):
    place = token_positions(segment).astype(jnp.float32)
    halves = HEAD // 2
    inverse = jnp.exp(jnp.arange(halves, dtype=jnp.float32) * (-2.0 * math.log(THETA) / HEAD))
    angle = place[:, None] * inverse[None, :]
    return (jnp.cos(angle), jnp.sin(angle))


BLOCK = 256
LANES = 128
SCALE = 1.0 / math.sqrt(HEAD)
SCALE_TWO = SCALE * math.log2(math.e)


def turn(values, cosine, sine):
    return values * cosine + pltpu.roll(values, HEAD // 2, 1) * sine


def head_columns(head):
    return slice(head * HEAD, (head + 1) * HEAD)


def nt(left, right):
    return lax.dot_general(left, right, (((1,), (1,)), ((), ())), preferred_element_type=WIDE)


def attend(first_block, query_raw, key_raw, values, factors, query_gain, key_gain, tables, starts):
    length, width = query_raw.shape
    heads = width // HEAD

    def kernel(
        first_block,
        query_raw,
        key_raw,
        values,
        factors,
        query_gain,
        key_gain,
        cosine,
        sine,
        starts,
        queries,
        keys,
        attended,
        peaks,
        peak_columns,
    ):
        @pl.loop(0, length // BLOCK)
        def _(index):
            at = row_slice(index, BLOCK)
            cos, sin = cosine[at], sine[at]
            pairs = ((query_raw, query_gain, queries), (key_raw, key_gain, keys))
            for which, (raw, gain, out) in enumerate(pairs):
                factor = factors[at, which : which + 1]
                for head in range(heads):
                    columns = head_columns(head)
                    normed = raw[at, columns] * factor * gain[:, columns]
                    out[at, columns] = turn(normed, cos, sin).astype(LOW)

        lane = lax.broadcasted_iota(jnp.int32, (BLOCK, LANES), 1)
        row_index = lax.broadcasted_iota(jnp.int32, (BLOCK, BLOCK), 0)
        column_index = lax.broadcasted_iota(jnp.int32, (BLOCK, BLOCK), 1)

        def query_block(index):
            at = row_slice(index, BLOCK)
            start = starts[at]

            def key_block(other, carry):
                there = row_slice(other, BLOCK)
                key_place = column_index + other * BLOCK
                allowed = (key_place >= start) & (key_place <= row_index + index * BLOCK)
                made = []
                for head in range(heads):
                    columns = head_columns(head)
                    peak, total, rows = carry[head]
                    scores = nt(queries[at, columns], keys[there, columns]) * SCALE_TWO
                    scores = jnp.where(allowed, scores, NEGATIVE)
                    higher = jnp.maximum(peak, jnp.max(scores, axis=1, keepdims=True))
                    raised = jnp.exp2(scores - higher)
                    shrink = jnp.exp2(peak - higher)
                    total = total * shrink + jnp.sum(raised, axis=1, keepdims=True)
                    rows = rows * shrink + jnp.dot(
                        raised.astype(LOW), values[there, columns], preferred_element_type=WIDE
                    )
                    made.append((higher, total, rows))
                return tuple(made)

            empty = (
                jnp.full((BLOCK, 1), NEGATIVE, WIDE),
                jnp.zeros((BLOCK, 1), WIDE),
                jnp.zeros((BLOCK, HEAD), WIDE),
            )
            done = lax.fori_loop(first_block[index], index + 1, key_block, (empty,) * heads)
            column = jnp.zeros((BLOCK, LANES), WIDE)
            for head in range(heads):
                peak, total, rows = done[head]
                attended[at, head_columns(head)] = (rows / total).astype(LOW)
                column = jnp.where(lane == head, peak + jnp.log2(total), column)
            peak_columns[at] = column

        loop(length // BLOCK, query_block)
        peaks[...] = peak_columns[...].T[:8]

    shape = jax.ShapeDtypeStruct
    smem = pl.BlockSpec(memory_space=pltpu.SMEM)
    return pl.pallas_call(
        kernel,
        out_shape=[
            shape((length, width), LOW),
            shape((length, width), LOW),
            shape((length, width), LOW),
            shape((8, length), WIDE),
        ],
        in_specs=[smem] + [VMEM] * 9,
        out_specs=[VMEM] * 4,
        scratch_shapes=[pltpu.VMEM((length, LANES), WIDE)],
        compiler_params=pltpu.CompilerParams(vmem_limit_bytes=48 * MIB),
        cost_estimate=pl.CostEstimate(
            flops=2 * length * MAX_LEN * width,
            bytes_accessed=16 * length * width,
            transcendentals=length * MAX_LEN * heads // 2,
        ),
    )(first_block, query_raw, key_raw, values, factors, query_gain, key_gain, *tables, starts)


def attend_back(
    last_block,
    queries,
    keys,
    values,
    attended,
    upstream,
    peaks,
    query_raw,
    key_raw,
    factors,
    query_gain,
    key_gain,
    tables,
    start_row,
):
    length, width = query_raw.shape
    heads = width // HEAD

    def kernel(
        last_block,
        queries,
        keys,
        values,
        attended,
        upstream,
        peaks,
        query_raw,
        key_raw,
        factors,
        query_gain,
        key_gain,
        cosine,
        sine,
        start_row,
        query_out,
        key_out,
        value_out,
        projections,
        query_gain_grad,
        key_gain_grad,
        query_sum,
        key_sum,
        value_sum,
        columns_scratch,
        deltas,
    ):
        lane = lax.broadcasted_iota(jnp.int32, (BLOCK, LANES), 1)
        query_gain_grad[...] = jnp.zeros_like(query_gain_grad)
        key_gain_grad[...] = jnp.zeros_like(key_gain_grad)

        def prepare(index):
            at = row_slice(index, BLOCK)
            column = jnp.zeros((BLOCK, LANES), WIDE)
            for head in range(heads):
                columns = head_columns(head)
                delta = jnp.sum(
                    attended[at, columns].astype(WIDE) * upstream[at, columns].astype(WIDE),
                    axis=1,
                    keepdims=True,
                )
                column = jnp.where(lane == head, delta, column)
            columns_scratch[at] = column
            query_sum[at] = jnp.zeros((BLOCK, width), WIDE)

        loop(length // BLOCK, prepare)
        deltas[...] = columns_scratch[...].T[:8]
        row_index = lax.broadcasted_iota(jnp.int32, (BLOCK, BLOCK), 0)
        column_index = lax.broadcasted_iota(jnp.int32, (BLOCK, BLOCK), 1)

        def turn_back(at, summed, raw, gain, factor, out, gain_grad):
            cos, sin = cosine[at], sine[at]
            share = jnp.zeros((BLOCK, 1), WIDE)
            for head in range(heads):
                columns = head_columns(head)
                normed = turn(summed(head) * SCALE, cos, -sin)
                out[at, columns] = normed
                weighed = normed * raw[at, columns]
                share += jnp.sum(gain[:, columns] * weighed, axis=1, keepdims=True)
                gain_grad[:, columns] += jnp.sum(weighed * factor, axis=0, keepdims=True)
            return share

        def key_block(index):
            at = row_slice(index, BLOCK)
            key_sum[...] = jnp.zeros_like(key_sum)
            value_sum[...] = jnp.zeros_like(value_sum)

            def query_block(other, carry):
                there = row_slice(other, BLOCK)
                key_place = row_index + index * BLOCK
                allowed = (key_place >= start_row[:, there]) & (
                    key_place <= column_index + other * BLOCK
                )
                for head in range(heads):
                    columns = head_columns(head)
                    scores = nt(keys[at, columns], queries[there, columns]) * SCALE_TWO
                    scores = jnp.where(allowed, scores, NEGATIVE)
                    chance = jnp.exp2(scores - peaks[head : head + 1, there])
                    value_sum[:, columns] += jnp.dot(
                        chance.astype(LOW), upstream[there, columns], preferred_element_type=WIDE
                    )
                    chance_grad = nt(values[at, columns], upstream[there, columns])
                    score_grad = (chance * (chance_grad - deltas[head : head + 1, there])).astype(LOW)
                    key_sum[:, columns] += jnp.dot(
                        score_grad, queries[there, columns], preferred_element_type=WIDE
                    )
                    query_sum[there, columns] += lax.dot_general(
                        score_grad,
                        keys[at, columns],
                        (((0,), (0,)), ((), ())),
                        preferred_element_type=WIDE,
                    )
                return carry

            lax.fori_loop(index, last_block[index] + 1, query_block, 0)
            value_out[at] = value_sum[...].astype(LOW)
            share = turn_back(
                at,
                lambda head: key_sum[:, head_columns(head)],
                key_raw,
                key_gain,
                factors[at, 1:2],
                key_out,
                key_gain_grad,
            )
            columns_scratch[at] = jnp.where(lane == 1, share, 0.0)

        loop(length // BLOCK, key_block)

        def finish(index):
            at = row_slice(index, BLOCK)
            share = turn_back(
                at,
                lambda head: query_sum[at, head_columns(head)],
                query_raw,
                query_gain,
                factors[at, 0:1],
                query_out,
                query_gain_grad,
            )
            columns_scratch[at] += jnp.where(lane == 0, share, 0.0)

        loop(length // BLOCK, finish)
        projections[...] = columns_scratch[...].T[:8]

    shape = jax.ShapeDtypeStruct
    smem = pl.BlockSpec(memory_space=pltpu.SMEM)
    return pl.pallas_call(
        kernel,
        out_shape=[
            shape((length, width), WIDE),
            shape((length, width), WIDE),
            shape((length, width), LOW),
            shape((8, length), WIDE),
            shape((1, width), WIDE),
            shape((1, width), WIDE),
        ],
        in_specs=[smem] + [VMEM] * 14,
        out_specs=[VMEM] * 6,
        scratch_shapes=[
            pltpu.VMEM((length, width), WIDE),
            pltpu.VMEM((BLOCK, width), WIDE),
            pltpu.VMEM((BLOCK, width), WIDE),
            pltpu.VMEM((length, LANES), WIDE),
            pltpu.VMEM((8, length), WIDE),
        ],
        compiler_params=pltpu.CompilerParams(vmem_limit_bytes=52 * MIB),
        cost_estimate=pl.CostEstimate(
            flops=5 * length * MAX_LEN * width,
            bytes_accessed=32 * length * width,
            transcendentals=length * MAX_LEN * heads // 2,
        ),
    )(
        last_block,
        queries,
        keys,
        values,
        attended,
        upstream,
        peaks,
        query_raw,
        key_raw,
        factors,
        query_gain,
        key_gain,
        *tables,
        start_row,
    )


def shards(
    tokens,
    query_weight,
    key_weight,
    value_weight,
    output_weight,
    gate_weight,
    up_weight,
    down_weight,
    query_gain,
    key_gain,
    attn_gain,
    mlp_gain,
    seq_ids,
    out_grad,
):
    segment = seq_ids[0]
    length = tokens.shape[0]
    local_width = tokens.shape[1]
    cosine, sine = rotary_tables(segment)
    tables = (
        jnp.concatenate([cosine, cosine], axis=1),
        jnp.concatenate([-sine, sine], axis=1),
    )
    order = jnp.arange(length, dtype=jnp.int32)
    starts = order - token_positions(segment)
    blocks = length // BLOCK
    first_block = starts.reshape(blocks, BLOCK)[:, 0] // BLOCK
    closing = segment.reshape(blocks, BLOCK)[:, -1]
    ends = jnp.sum((segment[None, :] <= closing[:, None]).astype(jnp.int32), axis=1) - 1
    last_block = ends // BLOCK
    gains = jnp.concatenate([attn_gain[None], mlp_gain[None], jnp.zeros((6, local_width))], axis=0)
    query_gain, key_gain = query_gain.reshape(1, -1), key_gain.reshape(1, -1)
    middle = local_width // 2
    pairs = (
        (query_weight, key_weight[:, :middle]),
        (key_weight[:, middle:], value_weight),
    )
    stack = jnp.stack([jnp.concatenate(pair, axis=1) for pair in pairs])
    inputs, attn_stack, output_full, query_raw, key_raw, values, squares, halves = gather_in(
        tokens, stack, output_weight, gains, 1
    )
    attn_half, mlp_half = halves[:1], halves[1:2]
    middle = down_weight.shape[0] // 2
    squares, down_rows = lax.optimization_barrier((squares, down_weight[middle:]))
    down_second = lax.all_gather(down_rows, "gy", axis=0)
    factors = lax.rsqrt(squares[:2].T / D + EPS)
    queries, keys, attended, peaks = attend(
        first_block,
        query_raw,
        key_raw,
        values,
        factors,
        query_gain,
        key_gain,
        tables,
        starts[:, None],
    )
    attn_raw, mixed, mlp_inputs, gate_full, up_full, down_first, upstream = attn_out(
        attended, output_full, attn_half, inputs, out_grad, gate_weight, up_weight, down_weight[:middle], 2
    )
    result, mlp_full, mlp_gain_part, hidden, gate, up = mlp_forward(
        mlp_inputs, gate_full, up_full, down_first, down_second, mlp_half, mixed, upstream, 3
    )
    gate_grad, up_grad, down_turned = hidden_back(
        mlp_full, down_first, down_second, hidden, gate, up, 4
    )
    down_weight_grad = down_turned.T
    mixed_grad, attn_full, attn_gain_part, gate_weight_grad, up_weight_grad = mlp_back(
        gate_grad, up_grad, gate_full, up_full, mlp_inputs, attn_half, upstream, attn_raw, 5
    )
    output_product = lax.dot_general(
        attended, attn_full, (((0,), (0,)), ((), ())), preferred_element_type=jnp.float32
    )
    output_weight_grad = lax.psum_scatter(
        output_product.astype(jnp.bfloat16), "gy", scatter_dimension=1, tiled=True
    ).astype(jnp.float32)
    attended_grad = lax.dot_general(
        attn_full, output_full, (((1,), (1,)), ((), ())), preferred_element_type=jnp.float32
    ).astype(jnp.bfloat16)
    query_back, key_back, value_grad, projections, query_gain_part, key_gain_part = attend_back(
        last_block,
        queries,
        keys,
        values,
        attended,
        attended_grad,
        peaks,
        query_raw,
        key_raw,
        factors,
        query_gain,
        key_gain,
        tables,
        starts[None, :],
    )
    token_grad, attn_weight_grads, gain_grads = attn_in_back(
        query_back,
        key_back,
        value_grad,
        query_raw,
        key_raw,
        factors,
        projections,
        query_gain,
        key_gain,
        attn_stack,
        inputs,
        mixed_grad,
        (query_gain_part, key_gain_part, attn_gain_part, mlp_gain_part),
        6,
    )
    query_weight_grad = attn_weight_grads[:, :local_width]
    key_weight_grad = attn_weight_grads[:, local_width : 2 * local_width]
    value_weight_grad = attn_weight_grads[:, 2 * local_width :]
    query_gain_grad, key_gain_grad, attn_gain_grad, mlp_gain_grad = (gain_grads[i] for i in range(4))
    return (
        result,
        token_grad,
        query_weight_grad,
        key_weight_grad,
        value_weight_grad,
        output_weight_grad,
        gate_weight_grad,
        up_weight_grad,
        down_weight_grad,
        query_gain_grad,
        key_gain_grad,
        attn_gain_grad,
        mlp_gain_grad,
    )


def solution(mesh):
    return jax.shard_map(
        shards,
        mesh=mesh,
        in_specs=(
            P("gy", "gx"),
            P("gy", "gx"),
            P("gy", "gx"),
            P("gy", "gx"),
            P("gx", "gy"),
            P("gy", "gx"),
            P("gy", "gx"),
            P("gx", "gy"),
            P("gx"),
            P("gx"),
            P("gx"),
            P("gx"),
            P("gy", None),
            P("gy", "gx"),
        ),
        out_specs=(
            P("gy", "gx"),
            P("gy", "gx"),
            P("gy", "gx"),
            P("gy", "gx"),
            P("gy", "gx"),
            P("gx", "gy"),
            P("gy", "gx"),
            P("gy", "gx"),
            P("gx", "gy"),
            P("gx"),
            P("gx"),
            P("gx"),
            P("gx"),
        ),
        check_vma=False,
    )
```

```python
import math

import jax
import jax.numpy as jnp
from jax import lax
from jax.experimental import pallas as pl
from jax.experimental.pallas import tpu as pltpu
from jax.sharding import PartitionSpec as P

D = 2048
HEAD = 128
MAX_LEN = 1024
SEGS = 4


EPS = 1e-06
THETA = 500000.0
NEGATIVE = -1e30


MESH = pl.DeviceIdType.MESH
HBM = pl.BlockSpec(memory_space=pltpu.HBM)
VMEM = pl.BlockSpec(memory_space=pltpu.VMEM)
LOW = jnp.bfloat16
WIDE = jnp.float32
MIB = 1 << 20
LAG = 2
STATS = 128


def core_here():
    return lax.rem(lax.axis_index("gx"), 2)


def chip_here():
    return lax.div(lax.axis_index("gx"), 2)


def other_core():
    return lax.axis_index("gx") + 1 - 2 * core_here()


def peer_at(shift):
    return lax.rem(lax.axis_index("gx") + 2 * shift, lax.axis_size("gx"))


def rank_at(shift):
    return lax.rem(lax.axis_index("gx") + shift, lax.axis_size("gx"))


def block_at(shift):
    return lax.rem(lax.axis_index("gy") + shift, lax.axis_size("gy"))


def ring_place():
    count = lax.axis_size("gy")
    index = lax.axis_index("gy")
    row, side = lax.div(index, 2), lax.rem(index, 2)
    return side * row + (1 - side) * (count - 1 - row)


def ring_device(place):
    count = lax.axis_size("gy")
    place = lax.rem(place + 2 * count, count)
    back = lax.div(place, count // 2)
    row = (1 - back) * place + back * (count - 1 - place)
    return 2 * row + 1 - back


def greet(gx, ring, all_blocks=False):
    barrier = pltpu.get_barrier_semaphore()
    partners = []
    if all_blocks:
        partners += [{"gy": block_at(k)} for k in range(1, lax.axis_size("gy"))]
    if gx == "all":
        partners += [{"gx": rank_at(k)} for k in range(1, lax.axis_size("gx"))]
    elif gx:
        partners.append({"gx": other_core()})
        partners += [{"gx": peer_at(k)} for k in range(1, lax.axis_size("gx") // 2)]
    if ring:
        place = ring_place()
        partners += [{"gy": ring_device(place + 1)}, {"gy": ring_device(place - 1)}]
    for partner in partners:
        pl.semaphore_signal(barrier, inc=1, device_id=partner, device_id_type=MESH)
    pl.semaphore_wait(barrier, len(partners))


def remote(source, target, send, recv, device):
    return pltpu.make_async_remote_copy(
        src_ref=source,
        dst_ref=target,
        send_sem=send,
        recv_sem=recv,
        device_id=device,
        device_id_type=MESH,
    )


def loop(count, body):
    def step(index, carry):
        body(index)
        return carry

    lax.fori_loop(0, count, step, 0)


def aligned(value, factor):
    return pl.multiple_of(value, factor)


class RingGather:
    def __init__(self, sources, slot, spill, parts, send, recv, local, spilled):
        self.sources, self.slot, self.spill, self.parts = sources, slot, spill, parts
        self.send, self.recv, self.local, self.spilled = send, recv, local, spilled
        self.count = lax.axis_size("gy")

    @staticmethod
    def scratch(parts):
        count = lax.axis_size("gy")
        return [
            pltpu.SemaphoreType.DMA((count - 1, 2, parts)),
            pltpu.SemaphoreType.DMA((count - 1, 2, parts)),
            pltpu.SemaphoreType.DMA((2, parts)),
            pltpu.SemaphoreType.DMA((count, 2, parts)),
        ]

    def spill_copy(self, way, step, part):
        place = ring_place()
        owner = ring_device(place - (1 - 2 * way) * step)
        return pltpu.make_async_copy(
            self.slot(way, owner, part),
            self.spill(way, owner, part),
            self.spilled.at[step, way, part],
        )

    def copy(self, way, step, part, behind):
        place = ring_place()
        sign = 1 - 2 * way
        spot = self.slot(way, ring_device(place - sign * (step + behind)), part)
        return remote(
            spot,
            spot,
            self.send.at[step, way, part],
            self.recv.at[step, way, part],
            {"gy": ring_device(place + sign)},
        )

    def begin(self):
        place = [
            pltpu.make_async_copy(
                self.sources(way, part),
                self.slot(way, lax.axis_index("gy"), part),
                self.local.at[way, part],
            )
            for way in range(2)
            for part in range(self.parts)
        ]
        for item in place:
            item.start()
        for item in place:
            item.wait()
        for part in range(self.parts):
            for way in range(2):
                self.copy(way, 0, part, 0).start()
                self.spill_copy(way, 0, part).start()

    @property
    def events(self):
        return (self.count - 2) * self.parts

    def event(self, index):
        step = 1 + lax.div(index, self.parts)
        for part in range(self.parts):

            @pl.when(lax.rem(index, self.parts) == part)
            def _():
                for way in range(2):
                    self.copy(way, step - 1, part, 1).wait_recv()
                    self.copy(way, step, part, 0).start()
                    self.spill_copy(way, step, part).start()

    def end(self):
        for part in range(self.parts):
            for way in range(2):
                self.copy(way, self.count - 2, part, 1).wait_recv()
                self.spill_copy(way, self.count - 1, part).start()

        def drain(step):
            for part in range(self.parts):
                for way in range(2):
                    self.copy(way, step, part, 0).wait_send()

        loop(self.count - 1, drain)

    def settle(self):
        def drain(step):
            for part in range(self.parts):
                for way in range(2):
                    self.spill_copy(way, step, part).wait()

        loop(self.count, drain)


class RingScatter:
    def __init__(self, product, total, sums, land, send, recv, credit, slots, parts):
        self.product, self.total, self.sums, self.land = product, total, sums, land
        self.send, self.recv, self.credit = send, recv, credit
        self.slots, self.parts = slots, parts
        self.count = lax.axis_size("gy")
        self.rows = total.shape[1] // parts

    @staticmethod
    def scratch(rows, columns, slots, parts):
        count = lax.axis_size("gy")
        return [
            pltpu.VMEM((2, rows, columns), WIDE),
            pltpu.VMEM((2, rows, columns), LOW),
            pltpu.VMEM((slots, 2, rows, columns), LOW),
            pltpu.SemaphoreType.DMA((count - 1, 2, parts)),
            pltpu.SemaphoreType.DMA((count - 1, 2, parts)),
            pltpu.SemaphoreType.REGULAR((2, parts)),
        ]

    def copy(self, way, step, part):
        place = ring_place()
        rows = pl.ds(aligned(part * self.rows, self.rows), self.rows)
        return remote(
            self.sums.at[way, rows],
            self.land.at[lax.rem(step, self.slots), way, rows],
            self.send.at[step, way, part],
            self.recv.at[step, way, part],
            {"gy": ring_device(place + 1 - 2 * way)},
        )

    def owner(self, way, step):
        sign = 1 - 2 * way
        return ring_device(ring_place() - sign * (1 + step))

    @property
    def events(self):
        return self.count * self.parts

    def event(self, index):
        step, part = lax.div(index, self.parts), lax.rem(index, self.parts)
        last = self.count - 1
        tile = min(self.rows, 32)

        @pl.when(part == 0)
        def _():
            for way in range(2):
                self.product(way, step)

        for way in range(2):
            base = part * self.rows

            slot = lax.rem(step - 1 + self.slots, self.slots)

            def over(body):
                @pl.loop(0, self.rows // tile)
                def _(index):
                    body(pl.ds(aligned(base + index * tile, tile), tile))

            @pl.when(step >= 1)
            def _():
                self.copy(way, step - 1, part).wait_recv()

            @pl.when((step >= 1) & (step < last))
            def _():
                self.copy(way, step - 1, part).wait_send()

            @pl.when(step == 0)
            def _():
                def first(rows):
                    self.sums[way, rows] = self.total[way, rows].astype(LOW)

                over(first)

            @pl.when((step >= 1) & (step < last))
            def _():
                def more(rows):
                    summed = self.total[way, rows] + self.land[slot, way, rows].astype(WIDE)
                    self.sums[way, rows] = summed.astype(LOW)

                over(more)

            @pl.when(step == last)
            def _():
                def final(rows):
                    self.total[way, rows] += self.land[slot, way, rows].astype(WIDE)

                over(final)

            @pl.when((step >= 1) & (step - 1 + self.slots < last))
            def _():
                upstream = ring_device(ring_place() - (1 - 2 * way))
                pl.semaphore_signal(
                    self.credit.at[way, part],
                    inc=1,
                    device_id={"gy": upstream},
                    device_id_type=MESH,
                )

            @pl.when(step < last)
            def _():
                @pl.when(step >= self.slots)
                def _():
                    pl.semaphore_wait(self.credit.at[way, part], 1)

                self.copy(way, step, part).start()

    def end(self):
        for part in range(self.parts):
            for way in range(2):
                self.copy(way, self.count - 2, part).wait_send()


class Reduce:
    def __init__(self, refs, cross_land, rows, width, scatter):
        (
            self.keep,
            self.core_send,
            self.core_land,
            self.cross,
            self.cross_stage,
            self.raw,
            self.core_sems,
            self.cross_send_sems,
            self.cross_recv_sems,
            self.stage_sems,
        ) = refs
        self.cross_land = cross_land
        self.rows, self.width, self.scatter = rows, width, scatter
        self.chips = lax.axis_size("gx") // 2

    @staticmethod
    def scratch(rows, chunks, width, scatter):
        chips = lax.axis_size("gx") // 2
        half = chips * width
        part = width if scatter else half
        return [
            pltpu.VMEM((1, rows, half), LOW),
            pltpu.VMEM((2, rows, half), LOW),
            pltpu.VMEM((2, rows, half), LOW),
            pltpu.VMEM((LAG + 2, chips, rows, width) if scatter else (LAG + 2, rows, half), LOW),
            pltpu.VMEM((chips - 1, rows, part), LOW),
            pltpu.VMEM((rows, part), WIDE),
            pltpu.SemaphoreType.DMA((2, chunks)),
            pltpu.SemaphoreType.DMA((chips - 1, chunks)),
            pltpu.SemaphoreType.DMA((chips - 1, chunks)),
            pltpu.SemaphoreType.DMA((chips,)),
        ]

    @staticmethod
    def landing(rows, chunks, width, scatter):
        chips = lax.axis_size("gx") // 2
        half = chips * width
        part = width if scatter else half
        return [jax.ShapeDtypeStruct((chips - 1, chunks, rows, part), LOW)]

    def core_copy(self, chunk):
        return remote(
            self.core_send.at[lax.rem(chunk, 2)],
            self.core_land.at[lax.rem(chunk, 2)],
            self.core_sems.at[0, chunk],
            self.core_sems.at[1, chunk],
            {"gx": other_core()},
        )

    def cross_copy(self, shift, chunk):
        source = self.cross.at[lax.rem(chunk, LAG + 2)]
        if self.scatter:
            block = lax.rem(chip_here() + shift, self.chips)
            source = source.at[block]
        return remote(
            source,
            self.cross_land.at[shift - 1, chunk],
            self.cross_send_sems.at[shift - 1, chunk],
            self.cross_recv_sems.at[shift - 1, chunk],
            {"gx": peer_at(shift)},
        )

    def produce(self, chunk, dot):
        @pl.when(chunk >= 2)
        def _():
            self.core_copy(chunk - 2).wait_send()

        slot = lax.rem(chunk, 2)
        core = core_here()
        for chip in range(self.chips):
            place = aligned((2 * chip + 1 - core) * self.width, self.width)
            self.core_send[slot, :, chip * self.width : (chip + 1) * self.width] = dot(
                place
            ).astype(LOW)
        self.core_copy(chunk).start()
        for chip in range(self.chips):
            place = aligned((2 * chip + core) * self.width, self.width)
            self.keep[0, :, chip * self.width : (chip + 1) * self.width] = dot(
                place
            ).astype(LOW)

    def core_sum(self, chunk):
        slot, place = lax.rem(chunk, 2), lax.rem(chunk, LAG + 2)
        self.core_copy(chunk).wait_recv()

        @pl.when(chunk >= LAG + 2)
        def _():
            for shift in range(1, self.chips):
                self.cross_copy(shift, chunk - LAG - 2).wait_send()

        @pl.loop(0, self.rows // 32)
        def _(index):
            rows = pl.ds(aligned(index * 32, 32), 32)
            total = self.keep[0, rows].astype(WIDE) + self.core_land[slot, rows].astype(WIDE)
            if self.scatter:
                for chip in range(self.chips):
                    columns = slice(chip * self.width, (chip + 1) * self.width)
                    self.cross[place, chip, rows] = total[:, columns].astype(LOW)
            else:
                self.cross[place, rows] = total.astype(LOW)

        for shift in range(1, self.chips):
            self.cross_copy(shift, chunk).start()

    def cross_stage_copy(self, shift, chunk):
        return pltpu.make_async_copy(
            self.cross_land.at[shift - 1, chunk],
            self.cross_stage.at[shift - 1],
            self.stage_sems.at[shift],
        )

    def cross_fetch(self, chunk):
        for shift in range(1, self.chips):
            self.cross_copy(shift, chunk).wait_recv()
            self.cross_stage_copy(shift, chunk).start()

    def cross_sum(self, chunk):
        place = lax.rem(chunk, LAG + 2)
        for shift in range(1, self.chips):
            self.cross_stage_copy(shift, chunk).wait()

        @pl.loop(0, self.rows // 32)
        def _(index):
            rows = pl.ds(aligned(index * 32, 32), 32)
            if self.scatter:
                total = self.cross[place, chip_here(), rows].astype(WIDE)
            else:
                total = self.cross[place, rows].astype(WIDE)
            for shift in range(1, self.chips):
                total = total + self.cross_stage[shift - 1, rows].astype(WIDE)
            self.raw[rows] = total

    def end(self, chunks):
        for chunk in (chunks - 2, chunks - 1):
            self.core_copy(chunk).wait_send()
        for chunk in range(chunks - LAG - 2, chunks):
            for shift in range(1, self.chips):
                self.cross_copy(shift, chunk).wait_send()


class Stats:
    def __init__(self, mine, land, sems):
        self.mine, self.land, self.sems = mine, land, sems

    @staticmethod
    def scratch(rows, chunks):
        return [
            pltpu.VMEM((2, rows, STATS), WIDE),
            pltpu.VMEM((chunks, rows, STATS), WIDE),
            pltpu.SemaphoreType.DMA((2, chunks)),
        ]

    def copy(self, chunk):
        return remote(
            self.mine.at[lax.rem(chunk, 2)],
            self.land.at[chunk],
            self.sems.at[0, chunk],
            self.sems.at[1, chunk],
            {"gx": other_core()},
        )

    def clear(self, chunk):
        @pl.when(chunk >= 2)
        def _():
            self.copy(chunk - 2).wait_send()

    def put(self, chunk, rows, first, second):
        lane = lax.broadcasted_iota(jnp.int32, (first.shape[0], STATS), 1)
        self.mine[lax.rem(chunk, 2), rows] = jnp.where(lane < STATS // 2, first, second)

    def get(self, chunk, rows):
        total = self.mine[lax.rem(chunk, 2), rows] + self.land[chunk, rows]
        return (total[:, :1], total[:, STATS // 2 : STATS // 2 + 1])

    def end(self, chunks):
        for chunk in (chunks - 2, chunks - 1):
            self.copy(chunk).wait_send()


class Spread:
    def __init__(self, buffer, whole, local, send, recv, rows, width):
        self.buffer, self.whole = buffer, whole
        self.local, self.send, self.recv = local, send, recv
        self.rows, self.width = rows, width
        self.chips = lax.axis_size("gx") // 2

    @staticmethod
    def scratch(rows, chunks, width):
        chips = lax.axis_size("gx") // 2
        return [
            pltpu.VMEM((2, chips, rows, width), LOW),
            pltpu.SemaphoreType.DMA((2, chips)),
            pltpu.SemaphoreType.DMA((chunks, chips)),
            pltpu.SemaphoreType.DMA((chunks, chips)),
        ]

    def pair(self, chunk, chip, core):
        slot = lax.rem(chunk, 2)
        source = self.buffer.at[slot, chip]
        rows = pl.ds(aligned(chunk * self.rows, self.rows), self.rows)
        rank = 2 * chip + core
        if len(self.whole.shape) == 3:
            target = self.whole.at[rank, rows]
        else:
            columns = pl.ds(aligned(rank * self.width, self.width), self.width)
            target = self.whole.at[rows, columns]
        here = pltpu.make_async_copy(source, target, self.local.at[slot, chip])
        away = remote(
            source,
            target,
            self.send.at[chunk, chip],
            self.recv.at[chunk, chip],
            {"gx": other_core()},
        )
        return (here, away)

    def put(self, chunk, rows, values):
        for chip in range(self.chips):
            columns = slice(chip * self.width, (chip + 1) * self.width)
            self.buffer[lax.rem(chunk, 2), chip, rows] = values[:, columns].astype(LOW)

    def clear(self, chunk):
        @pl.when(chunk >= 2)
        def _():
            self.settle(chunk - 2)

    def settle(self, chunk):
        for chip in range(self.chips):
            here, away = self.pair(chunk, chip, core_here())
            here.wait()
            away.wait_send()

    def go(self, chunk):
        for chip in range(self.chips):
            here, away = self.pair(chunk, chip, core_here())
            here.start()
            away.start()

    def end(self, chunks):
        for chunk in (chunks - 2, chunks - 1):
            self.settle(chunk)

        def arrive(chunk):
            for chip in range(self.chips):
                self.pair(chunk, chip, 1 - core_here())[1].wait_recv()

        loop(chunks, arrive)


def row_slice(chunk, rows):
    return pl.ds(aligned(chunk * rows, rows), rows)


def core_blocks(source, chunk, rows, width, buffer, sems):
    return [
        pltpu.make_async_copy(
            source.at[2 * chip + core_here(), row_slice(chunk, rows)],
            buffer.at[:, chip * width : (chip + 1) * width],
            sems.at[chip],
        )
        for chip in range(lax.axis_size("gx") // 2)
    ]


def all_blocks(source, rows, width, buffer, sems):
    return [
        pltpu.make_async_copy(
            source.at[rank] if rows is None else source.at[rank, rows],
            buffer.at[:, rank * width : (rank + 1) * width],
            sems.at[rank],
        )
        for rank in range(source.shape[0])
    ]


def tiles(rows, body):
    @pl.loop(0, rows // 32)
    def _(index):
        body(pl.ds(aligned(index * 32, 32), 32))


def schedule(chunks, reduce, multiply, fetch, sums, finish, event=None, events=0, prepare=None):
    steps = chunks + 1 + LAG

    def iteration(step):
        if event is not None:
            low = lax.div(step * events, steps)
            high = lax.div((step + 1) * events, steps)

            def some(index, carry):
                event(index)
                return carry

            lax.fori_loop(low, high, some, 0)

        @pl.when((step >= LAG) & (step < chunks + LAG))
        def _():
            reduce.cross_fetch(step - LAG)

        @pl.when(step >= LAG)
        def _():
            fetch(step - LAG)

        @pl.when(step < chunks)
        def _():
            if prepare is not None:
                prepare(step)
            reduce.produce(step, lambda place: multiply(step, place))
            reduce.core_sum(step)

        @pl.when(step >= 1 + LAG)
        def _():
            finish(step - 1 - LAG)

        @pl.when((step >= LAG) & (step < chunks + LAG))
        def _():
            reduce.cross_sum(step - LAG)
            sums(step - LAG)

    loop(steps, iteration)


def take(refs, counts):
    groups, start = [], 0
    for count in counts:
        groups.append(refs[start : start + count])
        start += count
    return groups


class Columns:
    def __init__(self, source, shard, left, turned, sem):
        self.source, self.shard = source, shard
        self.left, self.turned, self.sem = left, turned, sem

    @staticmethod
    def scratch(length, shard):
        return [
            pltpu.VMEM((length, shard), LOW),
            pltpu.VMEM((shard, length), LOW),
            pltpu.SemaphoreType.DMA((1,)),
        ]

    def copy(self, owner):
        each = self.source.shape[2] // self.shard
        at = pl.ds(aligned(lax.rem(owner, each) * self.shard, self.shard), self.shard)
        source = self.source.at[lax.div(owner, each), :, at]
        return pltpu.make_async_copy(source, self.left, self.sem.at[0])

    def take(self, ring, way, step):
        self.copy(ring.owner(way, step)).wait()
        self.turned[...] = self.left[...].T
        if way == 0:
            self.copy(ring.owner(1, step)).start()
        else:

            @pl.when(step + 1 < ring.count)
            def _():
                self.copy(ring.owner(0, step + 1)).start()


def attn_out(
    attended, weight, gain, tokens, out_grad, gate_shard, up_shard, down_shard, collective
):
    length, width = attended.shape
    chips = lax.axis_size("gx") // 2
    half = chips * width
    count = lax.axis_size("gy")
    chunks = count
    rows = length // chunks
    hidden = gate_shard.shape[1]
    inner = down_shard.shape[0]
    shard = gate_shard.shape[0]
    part_rows = shard // 2
    side = inner // 2
    down_columns = down_shard.shape[1]

    groups = [
        Reduce.scratch(rows, chunks, width, False),
        Stats.scratch(rows, chunks),
        Spread.scratch(rows, chunks, width),
        RingGather.scratch(3),
        [
            pltpu.VMEM((rows, half), LOW),
            pltpu.VMEM((2, rows, half), WIDE),
            pltpu.VMEM((2, rows, half), LOW),
            pltpu.SemaphoreType.DMA((chips,)),
            pltpu.SemaphoreType.DMA((2,)),
            pltpu.SemaphoreType.DMA((2,)),
            pltpu.SemaphoreType.DMA((2,)),
            pltpu.SemaphoreType.DMA((chips - 1, chunks, 2)),
        ],
        [
            pltpu.VMEM((2, D, hidden), LOW),
            pltpu.VMEM((count, inner, down_columns), LOW),
            pltpu.VMEM((chips, length, width), LOW),
        ],
    ]

    def kernel(*refs):
        ins, outs, *scratch = take(refs, [8, 8] + [len(g) for g in groups])
        attended, weight, gain, tokens, out_grad, gate_shard, up_shard, down_shard = ins
        raw_out, mixed_out, low_out, gate_full, up_full, down_full, upstream = outs[:7]
        cross_land = outs[7]
        reduce = Reduce(scratch[0], cross_land, rows, width, False)
        stats = Stats(*scratch[1])
        buffer, local, send, recv = scratch[2]
        spread = Spread(buffer, low_out, local, send, recv, rows, width)
        token_buf, mixed_buf, raw_buf = scratch[4][:3]
        token_sems, mixed_sems, raw_sems, own_sem, up_sems = scratch[4][3:]
        held, held_down, up_land = scratch[5]
        shards_here = (gate_shard, up_shard)

        def place_in(full, down):
            def slot(way, owner, part):
                if part == 2:
                    return down.at[owner, way * side : (way + 1) * side]
                base = owner * shard + part * part_rows
                return full[way].at[pl.ds(aligned(base, part_rows), part_rows)]

            return slot

        slot = place_in((held.at[0], held.at[1]), held_down)
        spill = place_in((gate_full, up_full), down_full)

        def source(way, part):
            if part == 2:
                return down_shard.at[way * side : (way + 1) * side]
            return shards_here[way].at[part * part_rows : (part + 1) * part_rows]

        ring = RingGather(source, slot, spill, 3, *scratch[3])
        own = pltpu.make_async_copy(out_grad, up_land.at[chip_here()], own_sem.at[0])
        up_spill = pltpu.make_async_copy(up_land, upstream, own_sem.at[1])

        def crossings(chunk):
            at = row_slice(chunk, rows)
            return [
                remote(
                    up_land.at[chip_here(), at],
                    up_land.at[chip_here(), at],
                    up_sems.at[shift - 1, chunk, 0],
                    up_sems.at[shift - 1, chunk, 1],
                    {"gx": peer_at(shift)},
                )
                for shift in range(1, chips)
            ]

        own.start()
        greet(True, True)
        ring.begin()
        own.wait()

        def multiply(chunk, place):
            return jnp.dot(
                attended[row_slice(chunk, rows)],
                weight[:, pl.ds(place, width)],
                preferred_element_type=WIDE,
            )

        def prepare(chunk):
            for item in crossings(chunk):
                item.start()

        def token_copies(chunk):
            return core_blocks(tokens, chunk, rows, width, token_buf, token_sems)

        def fetch(chunk):
            @pl.when(chunk >= 1)
            def _():
                for item in token_copies(chunk - 1):
                    item.start()

        def mixed_copy(chunk):
            slot = lax.rem(chunk, 2)
            return pltpu.make_async_copy(
                mixed_buf.at[slot, :, pl.ds(aligned(chip_here() * width, width), width)],
                mixed_out.at[row_slice(chunk, rows)],
                mixed_sems.at[slot],
            )

        def raw_copy(chunk):
            slot = lax.rem(chunk, 2)
            return pltpu.make_async_copy(
                raw_buf.at[slot], raw_out.at[row_slice(chunk, rows)], raw_sems.at[slot]
            )

        def sums(chunk):
            stats.clear(chunk)

            @pl.when(chunk >= 2)
            def _():
                raw_copy(chunk - 2).wait()

            def tile(at):
                raw = reduce.raw[at]
                raw_buf[lax.rem(chunk, 2), at] = raw.astype(LOW)
                squares = jnp.sum(raw * raw, axis=1, keepdims=True)
                stats.put(chunk, at, squares, squares)

            tiles(rows, tile)
            stats.copy(chunk).start()
            raw_copy(chunk).start()

        def finish(chunk):
            slot = lax.rem(chunk, 2)
            for item in token_copies(chunk):
                item.wait()
            stats.copy(chunk).wait_recv()
            spread.clear(chunk)

            @pl.when(chunk >= 2)
            def _():
                mixed_copy(chunk - 2).wait()

            def tile(at):
                squares, _ = stats.get(chunk, at)
                factor = lax.rsqrt(squares / D + EPS)
                mixed = token_buf[at].astype(WIDE) + reduce.raw[at] * factor * gain[...]
                mixed_buf[slot, at] = mixed
                spread.put(chunk, at, mixed)

            tiles(rows, tile)
            spread.go(chunk)
            mixed_copy(chunk).start()

        schedule(chunks, reduce, multiply, fetch, sums, finish, ring.event, ring.events, prepare)
        def drain(chunk):
            for item in crossings(chunk):
                item.wait()

        loop(chunks, drain)
        up_spill.start()
        ring.end()
        up_spill.wait()
        ring.settle()
        reduce.end(chunks)
        stats.end(chunks)
        spread.end(chunks)
        for chunk in (chunks - 2, chunks - 1):
            mixed_copy(chunk).wait()
            raw_copy(chunk).wait()

    shape = jax.ShapeDtypeStruct
    out = pl.pallas_call(
        kernel,
        out_shape=[
            shape((length, half), LOW),
            shape((length, width), WIDE),
            shape((2 * chips, length, width), LOW),
            shape((shard * count, hidden), LOW),
            shape((shard * count, hidden), LOW),
            shape((count, inner, down_columns), LOW),
            shape((chips, length, width), LOW),
        ]
        + Reduce.landing(rows, chunks, width, False),
        in_specs=[VMEM, VMEM, VMEM, HBM, HBM, HBM, HBM, HBM],
        out_specs=[HBM] * 8,
        scratch_shapes=[item for group in groups for item in group],
        compiler_params=pltpu.CompilerParams(
            collective_id=collective, has_side_effects=True, vmem_limit_bytes=60 * MIB
        ),
        cost_estimate=pl.CostEstimate(
            flops=2 * length * width * D, bytes_accessed=8 * length * D, transcendentals=0
        ),
    )(attended, weight, gain, tokens, out_grad, gate_shard, up_shard, down_shard)
    return out[:7]


def mlp_forward(
    inputs, gate_full, up_full, down_first, down_second, gain, mixed, upstream, collective
):
    length, inner = inputs.shape[1], gate_full.shape[1]
    width = mixed.shape[1]
    ranks = inputs.shape[0]
    down_columns = down_first.shape[2]
    down_rows = down_first.shape[1]
    chips = lax.axis_size("gx") // 2
    half = chips * width
    chunks = lax.axis_size("gy")
    rows = length // chunks
    tile = min(512, inner)
    pieces = inner // tile

    groups = [
        Reduce.scratch(rows, chunks, width, False),
        Stats.scratch(rows, chunks),
        Spread.scratch(rows, chunks, width),
        [
            pltpu.VMEM((2, rows, half), LOW),
            pltpu.VMEM((rows, width), WIDE),
            pltpu.VMEM((2, rows, width), LOW),
            pltpu.SemaphoreType.DMA((2, chips)),
            pltpu.SemaphoreType.DMA((1,)),
            pltpu.SemaphoreType.DMA((2,)),
        ],
        [
            pltpu.VMEM((D, inner), LOW),
            pltpu.VMEM((D, inner), LOW),
            pltpu.VMEM((inner, D), LOW),
            pltpu.VMEM((2, rows, D), LOW),
            pltpu.VMEM((2, 3, rows, inner), LOW),
            pltpu.SemaphoreType.DMA((pieces, 2)),
            pltpu.SemaphoreType.DMA((2, chunks)),
            pltpu.SemaphoreType.DMA((2, ranks)),
            pltpu.SemaphoreType.DMA((2, 3)),
        ],
    ]

    def kernel(*refs):
        ins, outs, *scratch = take(refs, [8, 7] + [len(g) for g in groups])
        inputs, gate_full, up_full, down_first, down_second, gain, mixed, upstream = ins
        result, grad_out, gain_grad, hidden_out, silu_out, slope_out, cross_land = outs
        gate_weight, up_weight, weight, row_buf, made = scratch[4][:5]
        piece_sems, weight_sem, row_sems, made_sems = scratch[4][5:]
        reduce = Reduce(scratch[0], cross_land, rows, width, False)
        stats = Stats(*scratch[1])
        buffer, local, send, recv = scratch[2]
        spread = Spread(buffer, grad_out, local, send, recv, rows, width)
        up_buf, mixed_buf, result_buf, up_sems, mixed_sems, result_sems = scratch[3]

        def piece_copies(piece):
            at = pl.ds(aligned(piece * tile, tile), tile)
            return [
                pltpu.make_async_copy(gate_full.at[:, at], gate_weight.at[:, at], piece_sems.at[piece, 0]),
                pltpu.make_async_copy(up_full.at[:, at], up_weight.at[:, at], piece_sems.at[piece, 1]),
            ]

        weight_copies = all_blocks(
            down_first, None, down_columns, weight.at[:down_rows], weight_sem.at[0]
        ) + all_blocks(down_second, None, down_columns, weight.at[down_rows:], weight_sem.at[1])

        def row_copy(chunk):
            slot = lax.rem(chunk, 2)
            return all_blocks(
                inputs, row_slice(chunk, rows), width, row_buf.at[slot], row_sems.at[slot]
            )

        def stores(chunk):
            slot, at = lax.rem(chunk, 2), row_slice(chunk, rows)
            return [
                pltpu.make_async_copy(made.at[slot, which], out.at[at], made_sems.at[slot, which])
                for which, out in enumerate((hidden_out, silu_out, slope_out))
            ]

        for item in row_copy(0):
            item.start()
        for piece in range(pieces):
            for item in piece_copies(piece):
                item.start()
        for item in weight_copies:
            item.start()
        greet(True, False)
        gain_grad[...] = jnp.zeros_like(gain_grad)

        def prepare(chunk):
            slot = lax.rem(chunk, 2)
            for item in row_copy(chunk):
                item.wait()

            @pl.when(chunk + 1 < chunks)
            def _():
                for item in row_copy(chunk + 1):
                    item.start()

            @pl.when(chunk >= 2)
            def _():
                for item in stores(chunk - 2):
                    item.wait()

            @pl.loop(0, pieces)
            def _(piece):
                @pl.when(chunk == 0)
                def _():
                    for item in piece_copies(piece):
                        item.wait()

                at = pl.ds(aligned(piece * tile, tile), tile)
                gate = jnp.dot(row_buf[slot], gate_weight[:, at], preferred_element_type=WIDE)
                up = jnp.dot(row_buf[slot], up_weight[:, at], preferred_element_type=WIDE)
                sigma = jax.nn.sigmoid(gate)
                silu = gate * sigma
                made[slot, 0, :, at] = (silu * up).astype(LOW)
                made[slot, 1, :, at] = silu.astype(LOW)
                made[slot, 2, :, at] = (up * (sigma + silu * (1.0 - sigma))).astype(LOW)

            @pl.when(chunk == 0)
            def _():
                for item in weight_copies:
                    item.wait()

            for item in stores(chunk):
                item.start()

        def multiply(chunk, place):
            return jnp.dot(
                made[lax.rem(chunk, 2), 0],
                weight[:, pl.ds(place, width)],
                preferred_element_type=WIDE,
            )

        def up_copy(chunk):
            slot = lax.rem(chunk, 2)
            return all_blocks(
                upstream, row_slice(chunk, rows), width, up_buf.at[slot], up_sems.at[slot]
            )

        def mixed_copy(chunk):
            return pltpu.make_async_copy(
                mixed.at[row_slice(chunk, rows)], mixed_buf, mixed_sems.at[0]
            )

        def result_copy(chunk):
            slot = lax.rem(chunk, 2)
            return pltpu.make_async_copy(
                result_buf.at[slot], result.at[row_slice(chunk, rows)], result_sems.at[slot]
            )

        def fetch(chunk):
            @pl.when(chunk < chunks)
            def _():
                for item in up_copy(chunk):
                    item.start()

            @pl.when(chunk >= 1)
            def _():
                mixed_copy(chunk - 1).start()

        def sums(chunk):
            slot = lax.rem(chunk, 2)
            stats.clear(chunk)
            for item in up_copy(chunk):
                item.wait()

            def tile(at):
                raw = reduce.raw[at]
                up = up_buf[slot, at].astype(WIDE)
                squares = jnp.sum(raw * raw, axis=1, keepdims=True)
                projected = jnp.sum(gain[...] * up * raw, axis=1, keepdims=True)
                stats.put(chunk, at, squares, projected)

            tiles(rows, tile)
            stats.copy(chunk).start()

        def finish(chunk):
            slot = lax.rem(chunk, 2)
            mixed_copy(chunk).wait()
            stats.copy(chunk).wait_recv()
            spread.clear(chunk)

            @pl.when(chunk >= 2)
            def _():
                result_copy(chunk - 2).wait()

            block = pl.ds(aligned(chip_here() * width, width), width)

            def tile(at):
                squares, projected = stats.get(chunk, at)
                factor = lax.rsqrt(squares / D + EPS)
                raw = reduce.raw[at]
                up = up_buf[slot, at].astype(WIDE)
                pull = factor * factor * factor * projected / D
                spread.put(chunk, at, factor * gain[...] * up - raw * pull)
                gain_grad[...] += jnp.sum(up * raw * factor, axis=0, keepdims=True)
                result_buf[slot, at] = (
                    mixed_buf[at] + reduce.raw[at, block] * factor * gain[:, block]
                ).astype(LOW)

            tiles(rows, tile)
            spread.go(chunk)
            result_copy(chunk).start()

        schedule(chunks, reduce, multiply, fetch, sums, finish, prepare=prepare)
        reduce.end(chunks)
        stats.end(chunks)
        spread.end(chunks)
        for chunk in (chunks - 2, chunks - 1):
            result_copy(chunk).wait()
            for item in stores(chunk):
                item.wait()

    shape = jax.ShapeDtypeStruct
    out = pl.pallas_call(
        kernel,
        out_shape=[
            shape((length, width), LOW),
            shape((2 * chips, length, width), LOW),
            shape((1, half), WIDE),
            shape((length, inner), LOW),
            shape((length, inner), LOW),
            shape((length, inner), LOW),
        ]
        + Reduce.landing(rows, chunks, width, False),
        in_specs=[HBM] * 5 + [VMEM, HBM, HBM],
        out_specs=[HBM, HBM, VMEM] + [HBM] * 4,
        scratch_shapes=[item for group in groups for item in group],
        compiler_params=pltpu.CompilerParams(
            collective_id=collective, has_side_effects=True, vmem_limit_bytes=60 * MIB
        ),
        cost_estimate=pl.CostEstimate(
            flops=6 * length * inner * D, bytes_accessed=16 * length * D, transcendentals=0
        ),
    )(inputs, gate_full, up_full, down_first, down_second, gain, mixed, upstream)
    return out[:6]


def mlp_back(gate_grad, up_grad, gate_full, up_full, inputs, gain, upstream, attn_raw, collective):
    length, inner = gate_grad.shape
    half = attn_raw.shape[1]
    chips = lax.axis_size("gx") // 2
    width = half // chips
    count = lax.axis_size("gy")
    chunks = count
    rows = length // chunks
    shard = D // count
    slots, parts = 2, 2

    groups = [
        Reduce.scratch(rows, chunks, width, False),
        Stats.scratch(rows, chunks),
        Spread.scratch(rows, chunks, width),
        RingScatter.scratch(shard, inner, slots, parts),
        [
            pltpu.VMEM((rows, half), LOW),
            pltpu.VMEM((2, rows, half), LOW),
            pltpu.SemaphoreType.DMA((chips,)),
            pltpu.SemaphoreType.DMA((2,)),
            pltpu.SemaphoreType.DMA((1,)),
            pltpu.SemaphoreType.DMA((2,)),
        ],
        Columns.scratch(length, shard),
        [
            pltpu.VMEM((2, length, inner), LOW),
            pltpu.VMEM((2, D, inner), LOW),
            pltpu.SemaphoreType.DMA((2, 2)),
        ],
    ]

    def kernel(*refs):
        ins, outs, *scratch = take(refs, [8, 6] + [len(g) for g in groups])
        gate_grad, up_grad, gate_full, up_full, inputs, gain, upstream, attn_raw = ins
        grads, weights, load_sems = scratch[6]
        grad_copies = [
            pltpu.make_async_copy((gate_grad, up_grad)[way], grads.at[way], load_sems.at[0, way])
            for way in range(2)
        ]
        weight_copies = [
            pltpu.make_async_copy((gate_full, up_full)[way], weights.at[way], load_sems.at[1, way])
            for way in range(2)
        ]
        mixed_out, grad_out, gain_grad, gate_out, up_out, cross_land = outs
        reduce = Reduce(scratch[0], cross_land, rows, width, False)
        stats = Stats(*scratch[1])
        buffer, local, send, recv = scratch[2]
        spread = Spread(buffer, grad_out, local, send, recv, rows, width)
        total, summed, land, ring_send, ring_recv, credit = scratch[3]
        up_buf, raw_buf, up_sems, raw_sems, mixed_sems, out_sems = scratch[4]
        left = Columns(inputs, shard, *scratch[5])

        def product(way, step):
            left.take(ring, way, step)
            tile = 512

            @pl.when(step == 0)
            def _():
                grad_copies[way].wait()

            @pl.loop(0, inner // tile)
            def _(index):
                columns = pl.ds(aligned(index * tile, tile), tile)
                total[way, :, columns] = jnp.dot(
                    left.turned[...], grads[way, :, columns], preferred_element_type=WIDE
                )

        ring = RingScatter(
            product, total, summed, land, ring_send, ring_recv, credit, slots, parts
        )
        left.copy(ring.owner(0, 0)).start()
        for item in grad_copies + weight_copies:
            item.start()
        greet(True, True)
        gain_grad[...] = jnp.zeros_like(gain_grad)

        def prepare(chunk):
            @pl.when(chunk == 0)
            def _():
                for item in weight_copies:
                    item.wait()

        def multiply(chunk, place):
            at = row_slice(chunk, rows)
            return nt(grads[0, at], weights[0, pl.ds(place, width)]) + nt(
                grads[1, at], weights[1, pl.ds(place, width)]
            )

        def up_copy(chunk):
            return all_blocks(upstream, row_slice(chunk, rows), width, up_buf, up_sems)

        def raw_copy(chunk):
            slot = lax.rem(chunk, 2)
            return pltpu.make_async_copy(
                attn_raw.at[row_slice(chunk, rows)], raw_buf.at[slot], raw_sems.at[slot]
            )

        def mixed_copy(chunk):
            return pltpu.make_async_copy(
                reduce.raw.at[:, pl.ds(aligned(chip_here() * width, width), width)],
                mixed_out.at[row_slice(chunk, rows)],
                mixed_sems.at[0],
            )

        def fetch(chunk):
            @pl.when(chunk < chunks)
            def _():
                for item in up_copy(chunk):
                    item.start()
                raw_copy(chunk).start()

        def sums(chunk):
            slot = lax.rem(chunk, 2)
            stats.clear(chunk)
            for item in up_copy(chunk):
                item.wait()
            raw_copy(chunk).wait()

            def tile(at):
                upward = reduce.raw[at] + up_buf[at].astype(WIDE)
                reduce.raw[at] = upward
                raw = raw_buf[slot, at].astype(WIDE)
                squares = jnp.sum(raw * raw, axis=1, keepdims=True)
                projected = jnp.sum(gain[...] * upward * raw, axis=1, keepdims=True)
                stats.put(chunk, at, squares, projected)

            tiles(rows, tile)
            stats.copy(chunk).start()
            mixed_copy(chunk).start()

        def finish(chunk):
            slot = lax.rem(chunk, 2)
            stats.copy(chunk).wait_recv()
            spread.clear(chunk)

            def tile(at):
                squares, projected = stats.get(chunk, at)
                factor = lax.rsqrt(squares / D + EPS)
                upward = reduce.raw[at]
                raw = raw_buf[slot, at].astype(WIDE)
                pull = factor * factor * factor * projected / D
                spread.put(chunk, at, factor * gain[...] * upward - raw * pull)
                gain_grad[...] += jnp.sum(upward * raw * factor, axis=0, keepdims=True)

            tiles(rows, tile)
            spread.go(chunk)
            mixed_copy(chunk).wait()

        schedule(chunks, reduce, multiply, fetch, sums, finish, ring.event, ring.events, prepare)
        writes = [
            pltpu.make_async_copy(total.at[way], (gate_out, up_out)[way], out_sems.at[way])
            for way in range(2)
        ]
        for item in writes:
            item.start()
        ring.end()
        reduce.end(chunks)
        stats.end(chunks)
        spread.end(chunks)
        for item in writes:
            item.wait()

    shape = jax.ShapeDtypeStruct
    out = pl.pallas_call(
        kernel,
        out_shape=[
            shape((length, width), WIDE),
            shape((length, D), LOW),
            shape((1, half), WIDE),
            shape((shard, inner), WIDE),
            shape((shard, inner), WIDE),
        ]
        + Reduce.landing(rows, chunks, width, False),
        in_specs=[HBM, HBM, HBM, HBM, HBM, VMEM, HBM, HBM],
        out_specs=[HBM, HBM, VMEM, HBM, HBM, HBM],
        scratch_shapes=[item for group in groups for item in group],
        compiler_params=pltpu.CompilerParams(
            collective_id=collective, has_side_effects=True, vmem_limit_bytes=60 * MIB
        ),
        cost_estimate=pl.CostEstimate(
            flops=8 * length * inner * D, bytes_accessed=16 * length * D, transcendentals=0
        ),
    )(gate_grad, up_grad, gate_full, up_full, inputs, gain, upstream, attn_raw)
    return out[:5]


class Total:
    def __init__(self, land, send, recv):
        self.land, self.send, self.recv = land, send, recv
        self.count = lax.axis_size("gx")

    @staticmethod
    def scratch(length):
        others = lax.axis_size("gx") - 1
        return [
            pltpu.VMEM((others, 8, length), WIDE),
            pltpu.SemaphoreType.DMA((others,)),
            pltpu.SemaphoreType.DMA((others,)),
        ]

    def copies(self, mine):
        return [
            remote(
                mine,
                self.land.at[shift - 1],
                self.send.at[shift - 1],
                self.recv.at[shift - 1],
                {"gx": rank_at(shift)},
            )
            for shift in range(1, self.count)
        ]

    def start(self, mine):
        for item in self.copies(mine):
            item.start()

    def finish(self, mine):
        for item in self.copies(mine):
            item.wait()
        total = mine[...]
        for shift in range(1, self.count):
            total = total + self.land[shift - 1]
        return total


def gather_in(tokens, stack, output_shard, gains, collective):
    length, width = tokens.shape
    _, shard, side = stack.shape
    columns = 2 * side
    count = lax.axis_size("gy")
    chunks = count
    rows = length // chunks
    chips = lax.axis_size("gx") // 2
    parts = 1
    out_columns = output_shard.shape[1]
    out_rows = width // 2

    groups = [
        RingGather.scratch(parts),
        [
            pltpu.SemaphoreType.DMA((1,)),
            pltpu.SemaphoreType.DMA((2,)),
            pltpu.SemaphoreType.DMA((chips - 1, chunks, 2)),
            pltpu.SemaphoreType.DMA((chips - 1, chunks, 2)),
        ],
        [
            pltpu.VMEM((2, D, side), LOW),
            pltpu.VMEM((2 * chips, length, width), LOW),
            pltpu.VMEM((2, 2, rows, width), WIDE),
            pltpu.VMEM((2, rows, width), LOW),
            pltpu.VMEM((length, STATS), WIDE),
            pltpu.VMEM((8, length), WIDE),
            pltpu.SemaphoreType.DMA((2,)),
            pltpu.SemaphoreType.DMA((2, 3)),
        ],
        Total.scratch(length),
        [
            pltpu.VMEM((chips - 1, 8, width), WIDE),
            pltpu.SemaphoreType.DMA((chips - 1, 2)),
        ],
        RingGather.scratch(1),
        [pltpu.VMEM((count, width, out_columns), LOW)],
    ]

    def kernel(*refs):
        ins, outs, *scratch = take(refs, [4, 8] + [len(g) for g in groups])
        tokens, stack, output_shard, gains = ins
        whole, full, output_full, query_raw, key_raw, values, squares, halves = outs
        out_held = scratch[6][0]
        gain_land, gain_sems = scratch[4]
        own_sem, core_sems, cross_sems, pass_sems = scratch[1]
        weight, held, raw_buf, value_buf, stats, mine = scratch[2][:6]
        copy_sems, out_sems = scratch[2][6:]
        total = Total(*scratch[3])

        def slot(way, owner, part):
            return weight.at[way, pl.ds(aligned(owner * shard, shard), shard)]

        def spill(way, owner, part):
            return full.at[way, pl.ds(aligned(owner * shard, shard), shard)]

        def source(way, part):
            return stack.at[way]

        ring = RingGather(source, slot, spill, parts, *scratch[0])

        def out_slot(way, owner, part):
            return out_held.at[owner, way * out_rows : (way + 1) * out_rows]

        def out_spill(way, owner, part):
            at = pl.ds(aligned(owner * out_columns, out_columns), out_columns)
            return output_full.at[way * out_rows : (way + 1) * out_rows, at]

        def out_source(way, part):
            return output_shard.at[way * out_rows : (way + 1) * out_rows]

        out_ring = RingGather(out_source, out_slot, out_spill, 1, *scratch[5])

        def block(rank, chunk):
            if chunk is None:
                return held.at[rank]
            return held.at[rank, row_slice(chunk, rows)]

        here = lax.axis_index("gx")
        own = pltpu.make_async_copy(tokens, block(here, None), own_sem.at[0])
        core = remote(
            block(here, None), block(here, None), core_sems.at[0], core_sems.at[1], {"gx": other_core()}
        )

        def cross(shift, chunk):
            return remote(
                block(here, chunk),
                block(here, chunk),
                cross_sems.at[shift - 1, chunk, 0],
                cross_sems.at[shift - 1, chunk, 1],
                {"gx": peer_at(shift)},
            )

        def onward(shift, chunk):
            spot = block(peer_at(chips - shift), chunk)
            return remote(
                spot,
                spot,
                pass_sems.at[shift - 1, chunk, 0],
                pass_sems.at[shift - 1, chunk, 1],
                {"gx": other_core()},
            )

        gain_copies = [
            remote(
                gains,
                gain_land.at[shift - 1],
                gain_sems.at[shift - 1, 0],
                gain_sems.at[shift - 1, 1],
                {"gx": peer_at(shift)},
            )
            for shift in range(1, chips)
        ]
        own.start()
        greet("all", True)
        for item in gain_copies:
            item.start()
        ring.begin()
        own.wait()

        def send(chunk):
            for shift in range(1, chips):
                cross(shift, chunk).start()

        loop(chunks, send)
        core.start()

        def step(chunk):
            for shift in range(1, chips):
                cross(shift, chunk).wait_recv()
                onward(shift, chunk).start()

            @pl.when(chunk < ring.events)
            def _():
                ring.event(chunk)

        loop(chunks, step)
        out_ring.begin()
        ring.end()

        def drain(chunk):
            for shift in range(1, chips):
                cross(shift, chunk).wait_send()
                onward(shift, chunk).wait()

        loop(chunks, drain)
        core.wait()
        whole_copy = pltpu.make_async_copy(held, whole, copy_sems.at[0])
        whole_copy.start()

        def stores(chunk):
            slot, at = lax.rem(chunk, 2), row_slice(chunk, rows)
            return [
                pltpu.make_async_copy(raw_buf.at[slot, 0], query_raw.at[at], out_sems.at[slot, 0]),
                pltpu.make_async_copy(raw_buf.at[slot, 1], key_raw.at[at], out_sems.at[slot, 1]),
                pltpu.make_async_copy(value_buf.at[slot], values.at[at], out_sems.at[slot, 2]),
            ]

        lane = lax.broadcasted_iota(jnp.int32, (rows, STATS), 1)

        def project(chunk):
            slot = lax.rem(chunk, 2)
            @pl.when(chunk >= 2)
            def _():
                for item in stores(chunk - 2):
                    item.wait()

            at = row_slice(chunk, rows)
            middle = side - width

            def against(way, columns):
                raw = jnp.zeros((rows, columns.stop - columns.start), WIDE)
                for rank in range(2 * chips):
                    raw = raw + jnp.dot(
                        held[rank, at],
                        weight[way, rank * width : (rank + 1) * width, columns],
                        preferred_element_type=WIDE,
                    )
                return raw

            some = []
            raw_buf[slot, 0] = against(0, slice(0, width))
            raw_buf[slot, 1, :, :middle] = against(0, slice(width, side))
            raw_buf[slot, 1, :, middle:] = against(1, slice(0, middle))
            value_buf[slot] = against(1, slice(middle, side)).astype(LOW)
            for which in range(2):
                raw = raw_buf[slot, which]
                some.append(jnp.sum(raw * raw, axis=1, keepdims=True))
            stats[row_slice(chunk, rows)] = jnp.where(lane == 0, some[0], some[1])
            for item in stores(chunk):
                item.start()

            @pl.when(chunk < out_ring.events)
            def _():
                out_ring.event(chunk)

        loop(chunks, project)
        mine[...] = stats[...].T[:8]
        total.start(mine)
        for chunk in (chunks - 2, chunks - 1):
            for item in stores(chunk):
                item.wait()
        squares[...] = total.finish(mine)
        whole_copy.wait()
        ring.settle()
        out_ring.end()
        out_ring.settle()
        halves[:, pl.ds(aligned(chip_here() * width, width), width)] = gains[...]
        for shift in range(1, chips):
            gain_copies[shift - 1].wait()
            chip = lax.rem(chip_here() + chips - shift, chips)
            halves[:, pl.ds(aligned(chip * width, width), width)] = gain_land[shift - 1]

    shape = jax.ShapeDtypeStruct
    return pl.pallas_call(
        kernel,
        out_shape=[
            shape((2 * chips, length, width), LOW),
            shape((2, shard * count, side), LOW),
            shape((width, D), LOW),
            shape((length, width), WIDE),
            shape((length, width), WIDE),
            shape((length, width), LOW),
            shape((8, length), WIDE),
            shape((8, chips * width), WIDE),
        ],
        in_specs=[HBM, HBM, HBM, VMEM],
        out_specs=[HBM] * 6 + [VMEM, VMEM],
        scratch_shapes=[item for group in groups for item in group],
        compiler_params=pltpu.CompilerParams(
            collective_id=collective, has_side_effects=True, vmem_limit_bytes=40 * MIB
        ),
        cost_estimate=pl.CostEstimate(
            flops=2 * length * columns * D, bytes_accessed=8 * length * D, transcendentals=0
        ),
    )(tokens, stack, output_shard, gains)


def hidden_back(blocks, down_first, down_second, hidden, silu, slope, collective):
    length, inner = hidden.shape
    count = lax.axis_size("gy")
    chunks = count
    rows = length // chunks
    shard = D // count
    side = inner // 2
    slots, parts = 3, 2
    down_rows = down_first.shape[1]
    tile = min(512, inner)

    groups = [
        RingScatter.scratch(shard, side, slots, parts),
        [
            pltpu.VMEM((2, 2, rows, inner), LOW),
            pltpu.VMEM((2, 2, rows, inner), LOW),
            pltpu.SemaphoreType.DMA((2, 2)),
            pltpu.SemaphoreType.DMA((2, 2)),
            pltpu.SemaphoreType.DMA((2,)),
            pltpu.VMEM((count, shard, length), LOW),
        ],
        [
            pltpu.VMEM((length, D), LOW),
            pltpu.VMEM((inner, D), LOW),
            pltpu.SemaphoreType.DMA((blocks.shape[0],)),
            pltpu.SemaphoreType.DMA((2, count)),
        ],
    ]

    def kernel(*refs):
        ins, outs, *scratch = take(refs, [6, 3] + [len(g) for g in groups])
        blocks, down_first, down_second, hidden, silu, slope = ins
        grad, weight, grad_sems, weight_sems = scratch[2]
        gate_grad, up_grad, weight_grad = outs
        total, summed, land, ring_send, ring_recv, credit = scratch[0]
        given, made, given_sems, made_sems, out_sems, turned = scratch[1]

        def product(way, step):
            owner = ring.owner(way, step)

            @pl.when((step < count // 2) | (step == count - 1))
            def _():
                turned[owner] = grad[:, pl.ds(aligned(owner * shard, shard), shard)].T

            size = min(512, side)

            @pl.loop(0, side // size)
            def _(index):
                at = pl.ds(aligned(index * size, size), size)
                take_at = pl.ds(aligned(way * side + index * size, size), size)
                total[way, :, at] = jnp.dot(
                    turned[owner], hidden[:, take_at], preferred_element_type=WIDE
                )

        ring = RingScatter(
            product, total, summed, land, ring_send, ring_recv, credit, slots, parts
        )

        def load(chunk):
            slot = lax.rem(chunk, 2)
            return [
                pltpu.make_async_copy(
                    (slope, silu)[which].at[row_slice(chunk, rows)],
                    given.at[slot, which],
                    given_sems.at[slot, which],
                )
                for which in range(2)
            ]

        def store(chunk):
            slot = lax.rem(chunk, 2)
            return [
                pltpu.make_async_copy(
                    made.at[slot, which],
                    (gate_grad, up_grad)[which].at[row_slice(chunk, rows)],
                    made_sems.at[slot, which],
                )
                for which in range(2)
            ]

        grad_copies = all_blocks(blocks, None, blocks.shape[2], grad, grad_sems)
        weight_copies = all_blocks(
            down_first, None, shard, weight.at[:down_rows], weight_sems.at[0]
        ) + all_blocks(down_second, None, shard, weight.at[down_rows:], weight_sems.at[1])
        for item in grad_copies + weight_copies + load(0):
            item.start()
        greet(False, True)
        for item in grad_copies:
            item.wait()

        def iteration(step):
            slot = lax.rem(step, 2)
            for part in range(parts):
                ring.event(step * parts + part)

            @pl.when(step + 1 < chunks)
            def _():
                for item in load(step + 1):
                    item.start()

            @pl.when(step >= 2)
            def _():
                for item in store(step - 2):
                    item.wait()

            for item in load(step):
                item.wait()

            @pl.when(step == 0)
            def _():
                for item in weight_copies:
                    item.wait()

            @pl.loop(0, inner // tile)
            def _(index):
                at = pl.ds(aligned(index * tile, tile), tile)
                hidden_grad = lax.dot_general(
                    grad[row_slice(step, rows)],
                    weight[at],
                    (((1,), (1,)), ((), ())),
                    preferred_element_type=WIDE,
                )
                for which in range(2):
                    made[slot, which, :, at] = (
                        hidden_grad * given[slot, which, :, at].astype(WIDE)
                    ).astype(LOW)

            for item in store(step):
                item.start()

        loop(chunks, iteration)
        writes = [
            pltpu.make_async_copy(
                total.at[way], weight_grad.at[:, way * side : (way + 1) * side], out_sems.at[way]
            )
            for way in range(2)
        ]
        for item in writes:
            item.start()
        for chunk in (chunks - 2, chunks - 1):
            for item in store(chunk):
                item.wait()
        ring.end()
        for item in writes:
            item.wait()

    shape = jax.ShapeDtypeStruct
    return pl.pallas_call(
        kernel,
        out_shape=[
            shape((length, inner), LOW),
            shape((length, inner), LOW),
            shape((shard, inner), WIDE),
        ],
        in_specs=[HBM, HBM, HBM, VMEM, HBM, HBM],
        out_specs=[HBM, HBM, HBM],
        scratch_shapes=[item for group in groups for item in group],
        compiler_params=pltpu.CompilerParams(
            collective_id=collective, has_side_effects=True, vmem_limit_bytes=60 * MIB
        ),
        cost_estimate=pl.CostEstimate(
            flops=4 * length * inner * D, bytes_accessed=16 * length * D, transcendentals=0
        ),
    )(blocks, down_first, down_second, hidden, silu, slope)


def attn_in_back(
    query_back,
    key_back,
    value_grad,
    query_raw,
    key_raw,
    factors,
    projections,
    query_gain,
    key_gain,
    stack,
    inputs,
    mixed_grad,
    gain_parts,
    collective,
):
    length, columns = value_grad.shape[0], 2 * stack.shape[2]
    width = mixed_grad.shape[1]
    count = lax.axis_size("gy")
    chunks = count
    rows = length // chunks
    shard = D // count
    side = columns // 2
    slots, parts = count - 1, 2
    tile = 256 if side % 256 == 0 else 128

    groups = [
        Reduce.scratch(rows, chunks, width, True),
        RingScatter.scratch(shard, side, slots, parts),
        [
            pltpu.VMEM((rows, width), WIDE),
            pltpu.VMEM((2, rows, width), WIDE),
            pltpu.VMEM((length, columns), LOW),
            pltpu.VMEM((length, STATS), WIDE),
            pltpu.VMEM((2, 4, rows, width), WIDE),
            pltpu.VMEM((2, D, side), LOW),
            pltpu.SemaphoreType.DMA((2, 4)),
            pltpu.SemaphoreType.DMA((2,)),
            pltpu.SemaphoreType.DMA((1,)),
            pltpu.SemaphoreType.DMA((2,)),
            pltpu.SemaphoreType.DMA((2,)),
        ],
        Columns.scratch(length, shard),
        Total.scratch(length),
        [
            pltpu.VMEM((8, width), WIDE),
            pltpu.VMEM((count - 1, 8, width), WIDE),
            pltpu.SemaphoreType.DMA((count - 1, 2)),
        ],
    ]

    def kernel(*refs):
        ins, outs, *scratch = take(refs, [16, 4] + [len(g) for g in groups])
        query_back, key_back, value_grad, query_raw, key_raw, factors = ins[:6]
        projections, query_gain, key_gain, full, inputs, mixed_grad = ins[6:12]
        gain_parts = ins[12:]
        token_grad, weight_grad, gain_grads, cross_land = outs
        gain_mine, gain_land, gain_sems = scratch[5]
        reduce = Reduce(scratch[0], cross_land, rows, width, True)
        total, summed, land, ring_send, ring_recv, credit = scratch[1]
        mixed_buf, token_buf, grads, projected, given, stack = scratch[2][:6]
        given_sems, whole_sems, mixed_sems, token_sems, out_sems = scratch[2][6:]
        left = Columns(inputs, shard, *scratch[3])
        total_sum = Total(*scratch[4])

        def product(way, step):
            left.take(ring, way, step)

            @pl.loop(0, side // tile)
            def _(index):
                at = pl.ds(aligned(index * tile, tile), tile)
                take_at = pl.ds(aligned(way * side + index * tile, tile), tile)
                total[way, :, at] = jnp.dot(
                    left.turned[...], grads[:, take_at], preferred_element_type=WIDE
                )

        ring = RingScatter(
            product, total, summed, land, ring_send, ring_recv, credit, slots, parts
        )
        def load(chunk):
            slot, at = lax.rem(chunk, 2), row_slice(chunk, rows)
            return [
                pltpu.make_async_copy(
                    source.at[at], given.at[slot, which], given_sems.at[slot, which]
                )
                for which, source in enumerate((query_back, key_back, query_raw, key_raw))
            ]

        value_copy = pltpu.make_async_copy(value_grad, grads.at[:, 2 * width :], whole_sems.at[0])
        stack_copy = pltpu.make_async_copy(full, stack, whole_sems.at[1])
        left.copy(ring.owner(0, 0)).start()
        for item in load(0):
            item.start()
        value_copy.start()
        stack_copy.start()
        chip_columns = pl.ds(aligned(chip_here() * width, width), width)
        gain_mine[...] = jnp.zeros_like(gain_mine)
        for which, part in enumerate(gain_parts):
            gain_mine[which : which + 1] = part[...] if which < 2 else part[:, chip_columns]
        greet("all", False, True)
        total_sum.start(projections)
        gain_copies = [
            remote(
                gain_mine,
                gain_land.at[shift - 1],
                gain_sems.at[shift - 1, 0],
                gain_sems.at[shift - 1, 1],
                {"gy": block_at(shift)},
            )
            for shift in range(1, count)
        ]
        for item in gain_copies:
            item.start()
        sums_here = total_sum.finish(projections)
        projected[...] = jnp.concatenate([sums_here] * (STATS // 8), axis=0).T

        def form(chunk):
            slot = lax.rem(chunk, 2)

            @pl.when(chunk + 1 < chunks)
            def _():
                for item in load(chunk + 1):
                    item.start()

            for item in load(chunk):
                item.wait()

            def some(part):
                at = pl.ds(aligned(chunk * rows + part.start, 32), 32)
                for which, gain in enumerate((query_gain, key_gain)):
                    factor = factors[at, which : which + 1]
                    pull = factor * factor * factor * projected[at, which : which + 1] / D
                    back, raw = given[slot, which, part], given[slot, which + 2, part]
                    grads[at, which * width : (which + 1) * width] = (
                        factor * gain[...] * back - raw * pull
                    ).astype(LOW)

            tiles(rows, some)

        loop(chunks, form)
        value_copy.wait()

        def prepare(chunk):
            @pl.when(chunk == 0)
            def _():
                stack_copy.wait()

        def multiply(chunk, place):
            at = row_slice(chunk, rows)
            return nt(grads[at, :side], stack[0, pl.ds(place, width)]) + nt(
                grads[at, side:], stack[1, pl.ds(place, width)]
            )

        def mixed_copy(chunk):
            return pltpu.make_async_copy(
                mixed_grad.at[row_slice(chunk, rows)], mixed_buf, mixed_sems.at[0]
            )

        def token_copy(chunk):
            slot = lax.rem(chunk, 2)
            return pltpu.make_async_copy(
                token_buf.at[slot], token_grad.at[row_slice(chunk, rows)], token_sems.at[slot]
            )

        def fetch(chunk):
            @pl.when(chunk >= 1)
            def _():
                mixed_copy(chunk - 1).start()

        def sums(chunk):
            pass

        def finish(chunk):
            slot = lax.rem(chunk, 2)
            mixed_copy(chunk).wait()

            @pl.when(chunk >= 2)
            def _():
                token_copy(chunk - 2).wait()

            def some(at):
                token_buf[slot, at] = mixed_buf[at] + reduce.raw[at]

            tiles(rows, some)
            token_copy(chunk).start()

        schedule(chunks, reduce, multiply, fetch, sums, finish, ring.event, ring.events, prepare)
        writes = [
            pltpu.make_async_copy(
                total.at[way], weight_grad.at[:, way * side : (way + 1) * side], out_sems.at[way]
            )
            for way in range(2)
        ]
        for item in writes:
            item.start()
        gain_total = gain_mine[...]
        for shift in range(1, count):
            gain_copies[shift - 1].wait()
            gain_total = gain_total + gain_land[shift - 1]
        gain_grads[...] = gain_total
        ring.end()
        reduce.end(chunks)
        for chunk in (chunks - 2, chunks - 1):
            token_copy(chunk).wait()
        for item in writes:
            item.wait()

    shape = jax.ShapeDtypeStruct
    out = pl.pallas_call(
        kernel,
        out_shape=[
            shape((length, width), WIDE),
            shape((shard, columns), WIDE),
            shape((8, width), WIDE),
        ]
        + Reduce.landing(rows, chunks, width, True),
        in_specs=[HBM] * 5 + [VMEM] * 4 + [HBM] * 3 + [VMEM] * 4,
        out_specs=[HBM, HBM, VMEM, HBM],
        scratch_shapes=[item for group in groups for item in group],
        compiler_params=pltpu.CompilerParams(
            collective_id=collective, has_side_effects=True, vmem_limit_bytes=60 * MIB
        ),
        cost_estimate=pl.CostEstimate(
            flops=4 * length * columns * D, bytes_accessed=8 * length * D, transcendentals=0
        ),
    )(
        query_back,
        key_back,
        value_grad,
        query_raw,
        key_raw,
        factors,
        projections,
        query_gain,
        key_gain,
        stack,
        inputs,
        mixed_grad,
        *gain_parts,
    )
    return out[:3]


def token_positions(segment):
    length = segment.shape[0]
    labels = jnp.arange(SEGS, dtype=jnp.int32)
    member = (segment[:, None] == labels[None, :]).astype(jnp.int32)
    totals = jnp.sum(member, axis=0)
    starts = jnp.cumsum(totals) - totals
    opening = jnp.sum(member * starts[None, :], axis=1)
    return jnp.arange(length, dtype=jnp.int32) - opening


def rotary_tables(segment):
    place = token_positions(segment).astype(jnp.float32)
    halves = HEAD // 2
    inverse = jnp.exp(jnp.arange(halves, dtype=jnp.float32) * (-2.0 * math.log(THETA) / HEAD))
    angle = place[:, None] * inverse[None, :]
    return (jnp.cos(angle), jnp.sin(angle))


BLOCK = 256
LANES = 128
SCALE = 1.0 / math.sqrt(HEAD)
SCALE_TWO = SCALE * math.log2(math.e)


def turn(values, cosine, sine):
    return values * cosine + pltpu.roll(values, HEAD // 2, 1) * sine


def head_columns(head):
    return slice(head * HEAD, (head + 1) * HEAD)


def nt(left, right):
    return lax.dot_general(left, right, (((1,), (1,)), ((), ())), preferred_element_type=WIDE)


def attend(first_block, query_raw, key_raw, values, factors, query_gain, key_gain, tables, starts):
    length, width = query_raw.shape
    heads = width // HEAD

    def kernel(
        first_block,
        query_raw,
        key_raw,
        values,
        factors,
        query_gain,
        key_gain,
        cosine,
        sine,
        starts,
        queries,
        keys,
        attended,
        peaks,
        peak_columns,
        given,
        held_values,
        given_sems,
        value_sem,
    ):
        def load(index):
            slot, at = lax.rem(index, 2), row_slice(index, BLOCK)
            return [
                pltpu.make_async_copy(
                    source.at[at], given.at[slot, which], given_sems.at[slot, which]
                )
                for which, source in enumerate((query_raw, key_raw))
            ]

        value_copy = pltpu.make_async_copy(values, held_values, value_sem.at[0])
        for item in load(0):
            item.start()
        value_copy.start()

        def norm_block(index):
            at = row_slice(index, BLOCK)
            slot = lax.rem(index, 2)

            @pl.when(index + 1 < length // BLOCK)
            def _():
                for item in load(index + 1):
                    item.start()

            for item in load(index):
                item.wait()
            cos, sin = cosine[at], sine[at]
            for which, (gain, out) in enumerate(((query_gain, queries), (key_gain, keys))):
                factor = factors[at, which : which + 1]
                for head in range(heads):
                    columns = head_columns(head)
                    normed = given[slot, which, :, columns] * factor * gain[:, columns]
                    out[at, columns] = turn(normed, cos, sin).astype(LOW)

        loop(length // BLOCK, norm_block)
        value_copy.wait()

        lane = lax.broadcasted_iota(jnp.int32, (BLOCK, LANES), 1)
        row_index = lax.broadcasted_iota(jnp.int32, (BLOCK, BLOCK), 0)
        column_index = lax.broadcasted_iota(jnp.int32, (BLOCK, BLOCK), 1)

        def query_block(index):
            at = row_slice(index, BLOCK)
            start = starts[at]

            def key_block(other, carry):
                there = row_slice(other, BLOCK)
                key_place = column_index + other * BLOCK
                allowed = (key_place >= start) & (key_place <= row_index + index * BLOCK)
                made = []
                for head in range(heads):
                    columns = head_columns(head)
                    peak, total, rows = carry[head]
                    scores = nt(queries[at, columns], keys[there, columns]) * SCALE_TWO
                    scores = jnp.where(allowed, scores, NEGATIVE)
                    higher = jnp.maximum(peak, jnp.max(scores, axis=1, keepdims=True))
                    raised = jnp.exp2(scores - higher)
                    shrink = jnp.exp2(peak - higher)
                    total = total * shrink + jnp.sum(raised, axis=1, keepdims=True)
                    rows = rows * shrink + jnp.dot(
                        raised.astype(LOW), held_values[there, columns], preferred_element_type=WIDE
                    )
                    made.append((higher, total, rows))
                return tuple(made)

            empty = (
                jnp.full((BLOCK, 1), NEGATIVE, WIDE),
                jnp.zeros((BLOCK, 1), WIDE),
                jnp.zeros((BLOCK, HEAD), WIDE),
            )
            done = lax.fori_loop(first_block[index], index + 1, key_block, (empty,) * heads)
            column = jnp.zeros((BLOCK, LANES), WIDE)
            for head in range(heads):
                peak, total, rows = done[head]
                attended[at, head_columns(head)] = (rows / total).astype(LOW)
                column = jnp.where(lane == head, peak + jnp.log2(total), column)
            peak_columns[at] = column

        loop(length // BLOCK, query_block)
        peaks[...] = peak_columns[...].T[:8]

    shape = jax.ShapeDtypeStruct
    smem = pl.BlockSpec(memory_space=pltpu.SMEM)
    return pl.pallas_call(
        kernel,
        out_shape=[
            shape((length, width), LOW),
            shape((length, width), LOW),
            shape((length, width), LOW),
            shape((8, length), WIDE),
        ],
        in_specs=[smem] + [HBM] * 3 + [VMEM] * 6,
        out_specs=[VMEM] * 4,
        scratch_shapes=[
            pltpu.VMEM((length, LANES), WIDE),
            pltpu.VMEM((2, 2, BLOCK, width), WIDE),
            pltpu.VMEM((length, width), LOW),
            pltpu.SemaphoreType.DMA((2, 2)),
            pltpu.SemaphoreType.DMA((1,)),
        ],
        compiler_params=pltpu.CompilerParams(vmem_limit_bytes=48 * MIB),
        cost_estimate=pl.CostEstimate(
            flops=2 * length * MAX_LEN * width,
            bytes_accessed=16 * length * width,
            transcendentals=length * MAX_LEN * heads // 2,
        ),
    )(first_block, query_raw, key_raw, values, factors, query_gain, key_gain, *tables, starts)


def attend_back(
    last_block,
    queries,
    keys,
    values,
    attended,
    upstream,
    peaks,
    query_raw,
    key_raw,
    factors,
    query_gain,
    key_gain,
    tables,
    start_row,
):
    length, width = query_raw.shape
    heads = width // HEAD

    def kernel(
        last_block,
        queries,
        keys,
        values,
        attended,
        upstream,
        peaks,
        query_raw,
        key_raw,
        factors,
        query_gain,
        key_gain,
        cosine,
        sine,
        start_row,
        query_out,
        key_out,
        value_out,
        projections,
        query_gain_grad,
        key_gain_grad,
        query_sum,
        key_sum,
        value_sum,
        columns_scratch,
        deltas,
        held_query,
        held_key,
        made,
        load_sems,
        made_sems,
    ):
        loads = [
            pltpu.make_async_copy(query_raw, held_query, load_sems.at[0]),
            pltpu.make_async_copy(key_raw, held_key, load_sems.at[1]),
        ]
        for item in loads:
            item.start()

        def store(index, out):
            slot = lax.rem(index, 2)
            return pltpu.make_async_copy(
                made.at[slot], out.at[row_slice(index, BLOCK)], made_sems.at[slot]
            )

        lane = lax.broadcasted_iota(jnp.int32, (BLOCK, LANES), 1)
        query_gain_grad[...] = jnp.zeros_like(query_gain_grad)
        key_gain_grad[...] = jnp.zeros_like(key_gain_grad)

        def prepare(index):
            at = row_slice(index, BLOCK)
            column = jnp.zeros((BLOCK, LANES), WIDE)
            for head in range(heads):
                columns = head_columns(head)
                delta = jnp.sum(
                    attended[at, columns].astype(WIDE) * upstream[at, columns].astype(WIDE),
                    axis=1,
                    keepdims=True,
                )
                column = jnp.where(lane == head, delta, column)
            columns_scratch[at] = column
            query_sum[at] = jnp.zeros((BLOCK, width), WIDE)

        loop(length // BLOCK, prepare)
        deltas[...] = columns_scratch[...].T[:8]
        row_index = lax.broadcasted_iota(jnp.int32, (BLOCK, BLOCK), 0)
        column_index = lax.broadcasted_iota(jnp.int32, (BLOCK, BLOCK), 1)

        def turn_back(index, summed, raw, gain, factor, out, gain_grad):
            at, slot = row_slice(index, BLOCK), lax.rem(index, 2)

            @pl.when(index >= 2)
            def _():
                store(index - 2, out).wait()

            cos, sin = cosine[at], sine[at]
            share = jnp.zeros((BLOCK, 1), WIDE)
            for head in range(heads):
                columns = head_columns(head)
                normed = turn(summed(head) * SCALE, cos, -sin)
                made[slot, :, columns] = normed
                weighed = normed * raw[at, columns]
                share += jnp.sum(gain[:, columns] * weighed, axis=1, keepdims=True)
                gain_grad[:, columns] += jnp.sum(weighed * factor, axis=0, keepdims=True)
            store(index, out).start()
            return share

        def key_block(index):
            at = row_slice(index, BLOCK)
            key_sum[...] = jnp.zeros_like(key_sum)
            value_sum[...] = jnp.zeros_like(value_sum)

            def query_block(other, carry):
                there = row_slice(other, BLOCK)
                key_place = row_index + index * BLOCK
                allowed = (key_place >= start_row[:, there]) & (
                    key_place <= column_index + other * BLOCK
                )
                for head in range(heads):
                    columns = head_columns(head)
                    scores = nt(keys[at, columns], queries[there, columns]) * SCALE_TWO
                    scores = jnp.where(allowed, scores, NEGATIVE)
                    chance = jnp.exp2(scores - peaks[head : head + 1, there])
                    value_sum[:, columns] += jnp.dot(
                        chance.astype(LOW), upstream[there, columns], preferred_element_type=WIDE
                    )
                    chance_grad = nt(values[at, columns], upstream[there, columns])
                    score_grad = (chance * (chance_grad - deltas[head : head + 1, there])).astype(LOW)
                    key_sum[:, columns] += jnp.dot(
                        score_grad, queries[there, columns], preferred_element_type=WIDE
                    )
                    query_sum[there, columns] += lax.dot_general(
                        score_grad,
                        keys[at, columns],
                        (((0,), (0,)), ((), ())),
                        preferred_element_type=WIDE,
                    )
                return carry

            lax.fori_loop(index, last_block[index] + 1, query_block, 0)
            value_out[at] = value_sum[...].astype(LOW)

            @pl.when(index == 0)
            def _():
                loads[1].wait()

            share = turn_back(
                index,
                lambda head: key_sum[:, head_columns(head)],
                held_key,
                key_gain,
                factors[at, 1:2],
                key_out,
                key_gain_grad,
            )
            columns_scratch[at] = jnp.where(lane == 1, share, 0.0)

        loop(length // BLOCK, key_block)
        for index in (length // BLOCK - 2, length // BLOCK - 1):
            store(index, key_out).wait()
        loads[0].wait()

        def finish(index):
            at = row_slice(index, BLOCK)
            share = turn_back(
                index,
                lambda head: query_sum[at, head_columns(head)],
                held_query,
                query_gain,
                factors[at, 0:1],
                query_out,
                query_gain_grad,
            )
            columns_scratch[at] += jnp.where(lane == 0, share, 0.0)

        loop(length // BLOCK, finish)
        for index in (length // BLOCK - 2, length // BLOCK - 1):
            store(index, query_out).wait()
        projections[...] = columns_scratch[...].T[:8]

    shape = jax.ShapeDtypeStruct
    smem = pl.BlockSpec(memory_space=pltpu.SMEM)
    return pl.pallas_call(
        kernel,
        out_shape=[
            shape((length, width), WIDE),
            shape((length, width), WIDE),
            shape((length, width), LOW),
            shape((8, length), WIDE),
            shape((1, width), WIDE),
            shape((1, width), WIDE),
        ],
        in_specs=[smem] + [VMEM] * 6 + [HBM] * 2 + [VMEM] * 6,
        out_specs=[HBM] * 2 + [VMEM] * 4,
        scratch_shapes=[
            pltpu.VMEM((length, width), WIDE),
            pltpu.VMEM((BLOCK, width), WIDE),
            pltpu.VMEM((BLOCK, width), WIDE),
            pltpu.VMEM((length, LANES), WIDE),
            pltpu.VMEM((8, length), WIDE),
            pltpu.VMEM((length, width), WIDE),
            pltpu.VMEM((length, width), WIDE),
            pltpu.VMEM((2, BLOCK, width), WIDE),
            pltpu.SemaphoreType.DMA((2,)),
            pltpu.SemaphoreType.DMA((2,)),
        ],
        compiler_params=pltpu.CompilerParams(vmem_limit_bytes=52 * MIB),
        cost_estimate=pl.CostEstimate(
            flops=5 * length * MAX_LEN * width,
            bytes_accessed=32 * length * width,
            transcendentals=length * MAX_LEN * heads // 2,
        ),
    )(
        last_block,
        queries,
        keys,
        values,
        attended,
        upstream,
        peaks,
        query_raw,
        key_raw,
        factors,
        query_gain,
        key_gain,
        *tables,
        start_row,
    )


def shards(
    tokens,
    query_weight,
    key_weight,
    value_weight,
    output_weight,
    gate_weight,
    up_weight,
    down_weight,
    query_gain,
    key_gain,
    attn_gain,
    mlp_gain,
    seq_ids,
    out_grad,
):
    segment = seq_ids[0]
    length = tokens.shape[0]
    local_width = tokens.shape[1]
    cosine, sine = rotary_tables(segment)
    tables = (
        jnp.concatenate([cosine, cosine], axis=1),
        jnp.concatenate([-sine, sine], axis=1),
    )
    order = jnp.arange(length, dtype=jnp.int32)
    starts = order - token_positions(segment)
    blocks = length // BLOCK
    first_block = starts.reshape(blocks, BLOCK)[:, 0] // BLOCK
    closing = segment.reshape(blocks, BLOCK)[:, -1]
    ends = jnp.sum((segment[None, :] <= closing[:, None]).astype(jnp.int32), axis=1) - 1
    last_block = ends // BLOCK
    gains = jnp.concatenate([attn_gain[None], mlp_gain[None], jnp.zeros((6, local_width))], axis=0)
    query_gain, key_gain = query_gain.reshape(1, -1), key_gain.reshape(1, -1)
    middle = local_width // 2
    pairs = (
        (query_weight, key_weight[:, :middle]),
        (key_weight[:, middle:], value_weight),
    )
    stack = jnp.stack([jnp.concatenate(pair, axis=1) for pair in pairs])
    inputs, attn_stack, output_full, query_raw, key_raw, values, squares, halves = gather_in(
        tokens, stack, output_weight, gains, 1
    )
    attn_half, mlp_half = halves[:1], halves[1:2]
    middle = down_weight.shape[0] // 2
    squares, down_rows = lax.optimization_barrier((squares, down_weight[middle:]))
    down_second = lax.all_gather(down_rows, "gy", axis=0)
    factors = lax.rsqrt(squares[:2].T / D + EPS)
    queries, keys, attended, peaks = attend(
        first_block,
        query_raw,
        key_raw,
        values,
        factors,
        query_gain,
        key_gain,
        tables,
        starts[:, None],
    )
    attn_raw, mixed, mlp_inputs, gate_full, up_full, down_first, upstream = attn_out(
        attended, output_full, attn_half, inputs, out_grad, gate_weight, up_weight, down_weight[:middle], 2
    )
    result, mlp_full, mlp_gain_part, hidden, silu, slope = mlp_forward(
        mlp_inputs, gate_full, up_full, down_first, down_second, mlp_half, mixed, upstream, 3
    )
    gate_grad, up_grad, down_turned = hidden_back(
        mlp_full, down_first, down_second, hidden, silu, slope, 4
    )
    down_weight_grad = down_turned.T
    mixed_grad, attn_full, attn_gain_part, gate_weight_grad, up_weight_grad = mlp_back(
        gate_grad, up_grad, gate_full, up_full, mlp_inputs, attn_half, upstream, attn_raw, 5
    )
    output_product = lax.dot_general(
        attended, attn_full, (((0,), (0,)), ((), ())), preferred_element_type=jnp.float32
    )
    output_weight_grad = lax.psum_scatter(
        output_product.astype(jnp.bfloat16), "gy", scatter_dimension=1, tiled=True
    ).astype(jnp.float32)
    attended_grad = lax.dot_general(
        attn_full, output_full, (((1,), (1,)), ((), ())), preferred_element_type=jnp.float32
    ).astype(jnp.bfloat16)
    query_back, key_back, value_grad, projections, query_gain_part, key_gain_part = attend_back(
        last_block,
        queries,
        keys,
        values,
        attended,
        attended_grad,
        peaks,
        query_raw,
        key_raw,
        factors,
        query_gain,
        key_gain,
        tables,
        starts[None, :],
    )
    token_grad, attn_weight_grads, gain_grads = attn_in_back(
        query_back,
        key_back,
        value_grad,
        query_raw,
        key_raw,
        factors,
        projections,
        query_gain,
        key_gain,
        attn_stack,
        inputs,
        mixed_grad,
        (query_gain_part, key_gain_part, attn_gain_part, mlp_gain_part),
        6,
    )
    query_weight_grad = attn_weight_grads[:, :local_width]
    key_weight_grad = attn_weight_grads[:, local_width : 2 * local_width]
    value_weight_grad = attn_weight_grads[:, 2 * local_width :]
    query_gain_grad, key_gain_grad, attn_gain_grad, mlp_gain_grad = (gain_grads[i] for i in range(4))
    return (
        result,
        token_grad,
        query_weight_grad,
        key_weight_grad,
        value_weight_grad,
        output_weight_grad,
        gate_weight_grad,
        up_weight_grad,
        down_weight_grad,
        query_gain_grad,
        key_gain_grad,
        attn_gain_grad,
        mlp_gain_grad,
    )


def solution(mesh):
    return jax.shard_map(
        shards,
        mesh=mesh,
        in_specs=(
            P("gy", "gx"),
            P("gy", "gx"),
            P("gy", "gx"),
            P("gy", "gx"),
            P("gx", "gy"),
            P("gy", "gx"),
            P("gy", "gx"),
            P("gx", "gy"),
            P("gx"),
            P("gx"),
            P("gx"),
            P("gx"),
            P("gy", None),
            P("gy", "gx"),
        ),
        out_specs=(
            P("gy", "gx"),
            P("gy", "gx"),
            P("gy", "gx"),
            P("gy", "gx"),
            P("gy", "gx"),
            P("gx", "gy"),
            P("gy", "gx"),
            P("gy", "gx"),
            P("gx", "gy"),
            P("gx"),
            P("gx"),
            P("gx"),
            P("gx"),
        ),
        check_vma=False,
    )
```

```python
import math

import jax
import jax.numpy as jnp
from jax import lax
from jax.experimental import pallas as pl
from jax.experimental.pallas import tpu as pltpu
from jax.sharding import PartitionSpec as P

D = 2048
HEAD = 128
MAX_LEN = 1024
SEGS = 4


EPS = 1e-06
THETA = 500000.0
NEGATIVE = -1e30


MESH = pl.DeviceIdType.MESH
HBM = pl.BlockSpec(memory_space=pltpu.HBM)
VMEM = pl.BlockSpec(memory_space=pltpu.VMEM)
LOW = jnp.bfloat16
WIDE = jnp.float32
MIB = 1 << 20
LAG = 2
STATS = 128


def core_here():
    return lax.rem(lax.axis_index("gx"), 2)


def chip_here():
    return lax.div(lax.axis_index("gx"), 2)


def other_core():
    return lax.axis_index("gx") + 1 - 2 * core_here()


def peer_at(shift):
    return lax.rem(lax.axis_index("gx") + 2 * shift, lax.axis_size("gx"))


def rank_at(shift):
    return lax.rem(lax.axis_index("gx") + shift, lax.axis_size("gx"))


def block_at(shift):
    return lax.rem(lax.axis_index("gy") + shift, lax.axis_size("gy"))


def ring_place():
    count = lax.axis_size("gy")
    index = lax.axis_index("gy")
    row, side = lax.div(index, 2), lax.rem(index, 2)
    return side * row + (1 - side) * (count - 1 - row)


def ring_device(place):
    count = lax.axis_size("gy")
    place = lax.rem(place + 2 * count, count)
    back = lax.div(place, count // 2)
    row = (1 - back) * place + back * (count - 1 - place)
    return 2 * row + 1 - back


def greet(gx, ring, all_blocks=False):
    barrier = pltpu.get_barrier_semaphore()
    partners = []
    if all_blocks:
        partners += [{"gy": block_at(k)} for k in range(1, lax.axis_size("gy"))]
    if gx == "all":
        partners += [{"gx": rank_at(k)} for k in range(1, lax.axis_size("gx"))]
    elif gx:
        partners.append({"gx": other_core()})
        partners += [{"gx": peer_at(k)} for k in range(1, lax.axis_size("gx") // 2)]
    if ring:
        place = ring_place()
        partners += [{"gy": ring_device(place + 1)}, {"gy": ring_device(place - 1)}]
    for partner in partners:
        pl.semaphore_signal(barrier, inc=1, device_id=partner, device_id_type=MESH)
    pl.semaphore_wait(barrier, len(partners))


def remote(source, target, send, recv, device):
    return pltpu.make_async_remote_copy(
        src_ref=source,
        dst_ref=target,
        send_sem=send,
        recv_sem=recv,
        device_id=device,
        device_id_type=MESH,
    )


def loop(count, body):
    def step(index, carry):
        body(index)
        return carry

    lax.fori_loop(0, count, step, 0)


def aligned(value, factor):
    return pl.multiple_of(value, factor)


class RingGather:
    def __init__(self, sources, slot, spill, parts, send, recv, local, spilled):
        self.sources, self.slot, self.spill, self.parts = sources, slot, spill, parts
        self.send, self.recv, self.local, self.spilled = send, recv, local, spilled
        self.count = lax.axis_size("gy")

    @staticmethod
    def scratch(parts):
        count = lax.axis_size("gy")
        return [
            pltpu.SemaphoreType.DMA((count - 1, 2, parts)),
            pltpu.SemaphoreType.DMA((count - 1, 2, parts)),
            pltpu.SemaphoreType.DMA((2, parts)),
            pltpu.SemaphoreType.DMA((count, 2, parts)),
        ]

    def spill_copy(self, way, step, part):
        place = ring_place()
        owner = ring_device(place - (1 - 2 * way) * step)
        return pltpu.make_async_copy(
            self.slot(way, owner, part),
            self.spill(way, owner, part),
            self.spilled.at[step, way, part],
        )

    def copy(self, way, step, part, behind):
        place = ring_place()
        sign = 1 - 2 * way
        spot = self.slot(way, ring_device(place - sign * (step + behind)), part)
        return remote(
            spot,
            spot,
            self.send.at[step, way, part],
            self.recv.at[step, way, part],
            {"gy": ring_device(place + sign)},
        )

    def begin(self):
        place = [
            pltpu.make_async_copy(
                self.sources(way, part),
                self.slot(way, lax.axis_index("gy"), part),
                self.local.at[way, part],
            )
            for way in range(2)
            for part in range(self.parts)
        ]
        for item in place:
            item.start()
        for item in place:
            item.wait()
        for part in range(self.parts):
            for way in range(2):
                self.copy(way, 0, part, 0).start()
                self.spill_copy(way, 0, part).start()

    @property
    def events(self):
        return (self.count - 2) * self.parts

    def event(self, index):
        step = 1 + lax.div(index, self.parts)
        for part in range(self.parts):

            @pl.when(lax.rem(index, self.parts) == part)
            def _():
                for way in range(2):
                    self.copy(way, step - 1, part, 1).wait_recv()
                    self.copy(way, step, part, 0).start()
                    self.spill_copy(way, step, part).start()

    def end(self):
        for part in range(self.parts):
            for way in range(2):
                self.copy(way, self.count - 2, part, 1).wait_recv()
                self.spill_copy(way, self.count - 1, part).start()

        def drain(step):
            for part in range(self.parts):
                for way in range(2):
                    self.copy(way, step, part, 0).wait_send()

        loop(self.count - 1, drain)

    def settle(self):
        def drain(step):
            for part in range(self.parts):
                for way in range(2):
                    self.spill_copy(way, step, part).wait()

        loop(self.count, drain)


class RingScatter:
    def __init__(self, product, total, sums, land, send, recv, credit, slots, parts):
        self.product, self.total, self.sums, self.land = product, total, sums, land
        self.send, self.recv, self.credit = send, recv, credit
        self.slots, self.parts = slots, parts
        self.count = lax.axis_size("gy")
        self.rows = total.shape[1] // parts

    @staticmethod
    def scratch(rows, columns, slots, parts):
        count = lax.axis_size("gy")
        return [
            pltpu.VMEM((2, rows, columns), WIDE),
            pltpu.VMEM((2, rows, columns), LOW),
            pltpu.VMEM((slots, 2, rows, columns), LOW),
            pltpu.SemaphoreType.DMA((count - 1, 2, parts)),
            pltpu.SemaphoreType.DMA((count - 1, 2, parts)),
            pltpu.SemaphoreType.REGULAR((2, parts)),
        ]

    def copy(self, way, step, part):
        place = ring_place()
        rows = pl.ds(aligned(part * self.rows, self.rows), self.rows)
        return remote(
            self.sums.at[way, rows],
            self.land.at[lax.rem(step, self.slots), way, rows],
            self.send.at[step, way, part],
            self.recv.at[step, way, part],
            {"gy": ring_device(place + 1 - 2 * way)},
        )

    def owner(self, way, step):
        sign = 1 - 2 * way
        return ring_device(ring_place() - sign * (1 + step))

    @property
    def events(self):
        return self.count * self.parts

    def event(self, index):
        step, part = lax.div(index, self.parts), lax.rem(index, self.parts)
        last = self.count - 1
        tile = min(self.rows, 32)

        @pl.when(part == 0)
        def _():
            for way in range(2):
                self.product(way, step)

        for way in range(2):
            base = part * self.rows

            slot = lax.rem(step - 1 + self.slots, self.slots)

            def over(body):
                @pl.loop(0, self.rows // tile)
                def _(index):
                    body(pl.ds(aligned(base + index * tile, tile), tile))

            @pl.when(step >= 1)
            def _():
                self.copy(way, step - 1, part).wait_recv()

            @pl.when((step >= 1) & (step < last))
            def _():
                self.copy(way, step - 1, part).wait_send()

            @pl.when(step == 0)
            def _():
                def first(rows):
                    self.sums[way, rows] = self.total[way, rows].astype(LOW)

                over(first)

            @pl.when((step >= 1) & (step < last))
            def _():
                def more(rows):
                    summed = self.total[way, rows] + self.land[slot, way, rows].astype(WIDE)
                    self.sums[way, rows] = summed.astype(LOW)

                over(more)

            @pl.when(step == last)
            def _():
                def final(rows):
                    self.total[way, rows] += self.land[slot, way, rows].astype(WIDE)

                over(final)

            @pl.when((step >= 1) & (step - 1 + self.slots < last))
            def _():
                upstream = ring_device(ring_place() - (1 - 2 * way))
                pl.semaphore_signal(
                    self.credit.at[way, part],
                    inc=1,
                    device_id={"gy": upstream},
                    device_id_type=MESH,
                )

            @pl.when(step < last)
            def _():
                @pl.when(step >= self.slots)
                def _():
                    pl.semaphore_wait(self.credit.at[way, part], 1)

                self.copy(way, step, part).start()

    def end(self):
        for part in range(self.parts):
            for way in range(2):
                self.copy(way, self.count - 2, part).wait_send()


class Reduce:
    def __init__(self, refs, cross_land, rows, width, scatter):
        (
            self.keep,
            self.core_send,
            self.core_land,
            self.cross,
            self.cross_stage,
            self.raw,
            self.core_sems,
            self.cross_send_sems,
            self.cross_recv_sems,
            self.stage_sems,
        ) = refs
        self.cross_land = cross_land
        self.rows, self.width, self.scatter = rows, width, scatter
        self.chips = lax.axis_size("gx") // 2

    @staticmethod
    def scratch(rows, chunks, width, scatter):
        chips = lax.axis_size("gx") // 2
        half = chips * width
        part = width if scatter else half
        return [
            pltpu.VMEM((1, rows, half), LOW),
            pltpu.VMEM((2, rows, half), LOW),
            pltpu.VMEM((2, rows, half), LOW),
            pltpu.VMEM((LAG + 2, chips, rows, width) if scatter else (LAG + 2, rows, half), LOW),
            pltpu.VMEM((chips - 1, rows, part), LOW),
            pltpu.VMEM((rows, part), WIDE),
            pltpu.SemaphoreType.DMA((2, chunks)),
            pltpu.SemaphoreType.DMA((chips - 1, chunks)),
            pltpu.SemaphoreType.DMA((chips - 1, chunks)),
            pltpu.SemaphoreType.DMA((chips,)),
        ]

    @staticmethod
    def landing(rows, chunks, width, scatter):
        chips = lax.axis_size("gx") // 2
        half = chips * width
        part = width if scatter else half
        return [jax.ShapeDtypeStruct((chips - 1, chunks, rows, part), LOW)]

    def core_copy(self, chunk):
        return remote(
            self.core_send.at[lax.rem(chunk, 2)],
            self.core_land.at[lax.rem(chunk, 2)],
            self.core_sems.at[0, chunk],
            self.core_sems.at[1, chunk],
            {"gx": other_core()},
        )

    def cross_copy(self, shift, chunk):
        source = self.cross.at[lax.rem(chunk, LAG + 2)]
        if self.scatter:
            block = lax.rem(chip_here() + shift, self.chips)
            source = source.at[block]
        return remote(
            source,
            self.cross_land.at[shift - 1, chunk],
            self.cross_send_sems.at[shift - 1, chunk],
            self.cross_recv_sems.at[shift - 1, chunk],
            {"gx": peer_at(shift)},
        )

    def produce(self, chunk, dot):
        @pl.when(chunk >= 2)
        def _():
            self.core_copy(chunk - 2).wait_send()

        slot = lax.rem(chunk, 2)
        core = core_here()
        for chip in range(self.chips):
            place = aligned((2 * chip + 1 - core) * self.width, self.width)
            self.core_send[slot, :, chip * self.width : (chip + 1) * self.width] = dot(
                place
            ).astype(LOW)
        self.core_copy(chunk).start()
        for chip in range(self.chips):
            place = aligned((2 * chip + core) * self.width, self.width)
            self.keep[0, :, chip * self.width : (chip + 1) * self.width] = dot(
                place
            ).astype(LOW)

    def core_sum(self, chunk):
        slot, place = lax.rem(chunk, 2), lax.rem(chunk, LAG + 2)
        self.core_copy(chunk).wait_recv()

        @pl.when(chunk >= LAG + 2)
        def _():
            for shift in range(1, self.chips):
                self.cross_copy(shift, chunk - LAG - 2).wait_send()

        @pl.loop(0, self.rows // 32)
        def _(index):
            rows = pl.ds(aligned(index * 32, 32), 32)
            total = self.keep[0, rows].astype(WIDE) + self.core_land[slot, rows].astype(WIDE)
            if self.scatter:
                for chip in range(self.chips):
                    columns = slice(chip * self.width, (chip + 1) * self.width)
                    self.cross[place, chip, rows] = total[:, columns].astype(LOW)
            else:
                self.cross[place, rows] = total.astype(LOW)

        for shift in range(1, self.chips):
            self.cross_copy(shift, chunk).start()

    def cross_stage_copy(self, shift, chunk):
        return pltpu.make_async_copy(
            self.cross_land.at[shift - 1, chunk],
            self.cross_stage.at[shift - 1],
            self.stage_sems.at[shift],
        )

    def cross_fetch(self, chunk):
        for shift in range(1, self.chips):
            self.cross_copy(shift, chunk).wait_recv()
            self.cross_stage_copy(shift, chunk).start()

    def cross_sum(self, chunk):
        place = lax.rem(chunk, LAG + 2)
        for shift in range(1, self.chips):
            self.cross_stage_copy(shift, chunk).wait()

        @pl.loop(0, self.rows // 32)
        def _(index):
            rows = pl.ds(aligned(index * 32, 32), 32)
            if self.scatter:
                total = self.cross[place, chip_here(), rows].astype(WIDE)
            else:
                total = self.cross[place, rows].astype(WIDE)
            for shift in range(1, self.chips):
                total = total + self.cross_stage[shift - 1, rows].astype(WIDE)
            self.raw[rows] = total

    def end(self, chunks):
        for chunk in (chunks - 2, chunks - 1):
            self.core_copy(chunk).wait_send()
        for chunk in range(chunks - LAG - 2, chunks):
            for shift in range(1, self.chips):
                self.cross_copy(shift, chunk).wait_send()


class Stats:
    def __init__(self, mine, land, sems):
        self.mine, self.land, self.sems = mine, land, sems

    @staticmethod
    def scratch(rows, chunks):
        return [
            pltpu.VMEM((2, rows, STATS), WIDE),
            pltpu.VMEM((chunks, rows, STATS), WIDE),
            pltpu.SemaphoreType.DMA((2, chunks)),
        ]

    def copy(self, chunk):
        return remote(
            self.mine.at[lax.rem(chunk, 2)],
            self.land.at[chunk],
            self.sems.at[0, chunk],
            self.sems.at[1, chunk],
            {"gx": other_core()},
        )

    def clear(self, chunk):
        @pl.when(chunk >= 2)
        def _():
            self.copy(chunk - 2).wait_send()

    def put(self, chunk, rows, first, second):
        lane = lax.broadcasted_iota(jnp.int32, (first.shape[0], STATS), 1)
        self.mine[lax.rem(chunk, 2), rows] = jnp.where(lane < STATS // 2, first, second)

    def get(self, chunk, rows):
        total = self.mine[lax.rem(chunk, 2), rows] + self.land[chunk, rows]
        return (total[:, :1], total[:, STATS // 2 : STATS // 2 + 1])

    def end(self, chunks):
        for chunk in (chunks - 2, chunks - 1):
            self.copy(chunk).wait_send()


class Spread:
    def __init__(self, buffer, whole, local, send, recv, rows, width):
        self.buffer, self.whole = buffer, whole
        self.local, self.send, self.recv = local, send, recv
        self.rows, self.width = rows, width
        self.chips = lax.axis_size("gx") // 2

    @staticmethod
    def scratch(rows, chunks, width):
        chips = lax.axis_size("gx") // 2
        return [
            pltpu.VMEM((2, chips, rows, width), LOW),
            pltpu.SemaphoreType.DMA((2, chips)),
            pltpu.SemaphoreType.DMA((chunks, chips)),
            pltpu.SemaphoreType.DMA((chunks, chips)),
        ]

    def pair(self, chunk, chip, core):
        slot = lax.rem(chunk, 2)
        source = self.buffer.at[slot, chip]
        rows = pl.ds(aligned(chunk * self.rows, self.rows), self.rows)
        rank = 2 * chip + core
        if len(self.whole.shape) == 3:
            target = self.whole.at[rank, rows]
        else:
            columns = pl.ds(aligned(rank * self.width, self.width), self.width)
            target = self.whole.at[rows, columns]
        here = pltpu.make_async_copy(source, target, self.local.at[slot, chip])
        away = remote(
            source,
            target,
            self.send.at[chunk, chip],
            self.recv.at[chunk, chip],
            {"gx": other_core()},
        )
        return (here, away)

    def put(self, chunk, rows, values):
        for chip in range(self.chips):
            columns = slice(chip * self.width, (chip + 1) * self.width)
            self.buffer[lax.rem(chunk, 2), chip, rows] = values[:, columns].astype(LOW)

    def clear(self, chunk):
        @pl.when(chunk >= 2)
        def _():
            self.settle(chunk - 2)

    def settle(self, chunk):
        for chip in range(self.chips):
            here, away = self.pair(chunk, chip, core_here())
            here.wait()
            away.wait_send()

    def go(self, chunk):
        for chip in range(self.chips):
            here, away = self.pair(chunk, chip, core_here())
            here.start()
            away.start()

    def end(self, chunks):
        for chunk in (chunks - 2, chunks - 1):
            self.settle(chunk)

        def arrive(chunk):
            for chip in range(self.chips):
                self.pair(chunk, chip, 1 - core_here())[1].wait_recv()

        loop(chunks, arrive)


def row_slice(chunk, rows):
    return pl.ds(aligned(chunk * rows, rows), rows)


def core_blocks(source, chunk, rows, width, buffer, sems):
    return [
        pltpu.make_async_copy(
            source.at[2 * chip + core_here(), row_slice(chunk, rows)],
            buffer.at[:, chip * width : (chip + 1) * width],
            sems.at[chip],
        )
        for chip in range(lax.axis_size("gx") // 2)
    ]


def all_blocks(source, rows, width, buffer, sems):
    return [
        pltpu.make_async_copy(
            source.at[rank] if rows is None else source.at[rank, rows],
            buffer.at[:, rank * width : (rank + 1) * width],
            sems.at[rank],
        )
        for rank in range(source.shape[0])
    ]


def tiles(rows, body):
    @pl.loop(0, rows // 32)
    def _(index):
        body(pl.ds(aligned(index * 32, 32), 32))


def schedule(chunks, reduce, multiply, fetch, sums, finish, event=None, events=0, prepare=None):
    steps = chunks + 1 + LAG

    def iteration(step):
        if event is not None:
            low = lax.div(step * events, steps)
            high = lax.div((step + 1) * events, steps)

            def some(index, carry):
                event(index)
                return carry

            lax.fori_loop(low, high, some, 0)

        @pl.when((step >= LAG) & (step < chunks + LAG))
        def _():
            reduce.cross_fetch(step - LAG)

        @pl.when(step >= LAG)
        def _():
            fetch(step - LAG)

        @pl.when(step < chunks)
        def _():
            if prepare is not None:
                prepare(step)
            reduce.produce(step, lambda place: multiply(step, place))
            reduce.core_sum(step)

        @pl.when(step >= 1 + LAG)
        def _():
            finish(step - 1 - LAG)

        @pl.when((step >= LAG) & (step < chunks + LAG))
        def _():
            reduce.cross_sum(step - LAG)
            sums(step - LAG)

    loop(steps, iteration)


def take(refs, counts):
    groups, start = [], 0
    for count in counts:
        groups.append(refs[start : start + count])
        start += count
    return groups


class Columns:
    def __init__(self, source, shard, left, turned, sem):
        self.source, self.shard = source, shard
        self.left, self.turned, self.sem = left, turned, sem

    @staticmethod
    def scratch(length, shard):
        return [
            pltpu.VMEM((length, shard), LOW),
            pltpu.VMEM((shard, length), LOW),
            pltpu.SemaphoreType.DMA((1,)),
        ]

    def copy(self, owner):
        each = self.source.shape[2] // self.shard
        at = pl.ds(aligned(lax.rem(owner, each) * self.shard, self.shard), self.shard)
        source = self.source.at[lax.div(owner, each), :, at]
        return pltpu.make_async_copy(source, self.left, self.sem.at[0])

    def take(self, ring, way, step):
        self.copy(ring.owner(way, step)).wait()
        self.turned[...] = self.left[...].T
        if way == 0:
            self.copy(ring.owner(1, step)).start()
        else:

            @pl.when(step + 1 < ring.count)
            def _():
                self.copy(ring.owner(0, step + 1)).start()


def turn_blocks(count, copy, target, stage, depth):
    for index in range(min(depth, count)):
        copy(index).start()

    def each(index):
        copy(index).wait()
        target(index, stage[lax.rem(index, depth)].T)

        @pl.when(index + depth < count)
        def _():
            copy(index + depth).start()

    loop(count, each)


def attn_out(
    attended, weight, gain, tokens, out_grad, gate_shard, up_shard, down_shard, collective
):
    length, width = attended.shape
    chips = lax.axis_size("gx") // 2
    half = chips * width
    count = lax.axis_size("gy")
    chunks = count
    rows = length // chunks
    hidden = gate_shard.shape[1]
    inner = down_shard.shape[0]
    shard = gate_shard.shape[0]
    part_rows = shard // 2
    side = inner // 2
    down_columns = down_shard.shape[1]

    groups = [
        Reduce.scratch(rows, chunks, width, False),
        Stats.scratch(rows, chunks),
        Spread.scratch(rows, chunks, width),
        RingGather.scratch(3),
        [
            pltpu.VMEM((rows, half), LOW),
            pltpu.VMEM((2, rows, half), WIDE),
            pltpu.VMEM((2, rows, half), LOW),
            pltpu.SemaphoreType.DMA((chips,)),
            pltpu.SemaphoreType.DMA((2,)),
            pltpu.SemaphoreType.DMA((2,)),
            pltpu.SemaphoreType.DMA((2,)),
            pltpu.SemaphoreType.DMA((chips - 1, chunks, 2)),
        ],
        [
            pltpu.VMEM((2, D, hidden), LOW),
            pltpu.VMEM((count, inner, down_columns), LOW),
            pltpu.VMEM((chips, length, width), LOW),
        ],
    ]

    def kernel(*refs):
        ins, outs, *scratch = take(refs, [8, 8] + [len(g) for g in groups])
        attended, weight, gain, tokens, out_grad, gate_shard, up_shard, down_shard = ins
        raw_out, mixed_out, low_out, gate_full, up_full, down_full, upstream = outs[:7]
        cross_land = outs[7]
        reduce = Reduce(scratch[0], cross_land, rows, width, False)
        stats = Stats(*scratch[1])
        buffer, local, send, recv = scratch[2]
        spread = Spread(buffer, low_out, local, send, recv, rows, width)
        token_buf, mixed_buf, raw_buf = scratch[4][:3]
        token_sems, mixed_sems, raw_sems, own_sem, up_sems = scratch[4][3:]
        held, held_down, up_land = scratch[5]
        shards_here = (gate_shard, up_shard)

        def place_in(full, down):
            def slot(way, owner, part):
                if part == 2:
                    return down.at[owner, way * side : (way + 1) * side]
                base = owner * shard + part * part_rows
                return full[way].at[pl.ds(aligned(base, part_rows), part_rows)]

            return slot

        slot = place_in((held.at[0], held.at[1]), held_down)
        spill = place_in((gate_full, up_full), down_full)

        def source(way, part):
            if part == 2:
                return down_shard.at[way * side : (way + 1) * side]
            return shards_here[way].at[part * part_rows : (part + 1) * part_rows]

        ring = RingGather(source, slot, spill, 3, *scratch[3])
        own = pltpu.make_async_copy(out_grad, up_land.at[chip_here()], own_sem.at[0])
        up_spill = pltpu.make_async_copy(up_land, upstream, own_sem.at[1])

        def crossings(chunk):
            at = row_slice(chunk, rows)
            return [
                remote(
                    up_land.at[chip_here(), at],
                    up_land.at[chip_here(), at],
                    up_sems.at[shift - 1, chunk, 0],
                    up_sems.at[shift - 1, chunk, 1],
                    {"gx": peer_at(shift)},
                )
                for shift in range(1, chips)
            ]

        own.start()
        greet(True, True)
        ring.begin()
        own.wait()

        def multiply(chunk, place):
            return jnp.dot(
                attended[row_slice(chunk, rows)],
                weight[:, pl.ds(place, width)],
                preferred_element_type=WIDE,
            )

        def prepare(chunk):
            for item in crossings(chunk):
                item.start()

        def token_copies(chunk):
            return core_blocks(tokens, chunk, rows, width, token_buf, token_sems)

        def fetch(chunk):
            @pl.when(chunk >= 1)
            def _():
                for item in token_copies(chunk - 1):
                    item.start()

        def mixed_copy(chunk):
            slot = lax.rem(chunk, 2)
            return pltpu.make_async_copy(
                mixed_buf.at[slot, :, pl.ds(aligned(chip_here() * width, width), width)],
                mixed_out.at[row_slice(chunk, rows)],
                mixed_sems.at[slot],
            )

        def raw_copy(chunk):
            slot = lax.rem(chunk, 2)
            return pltpu.make_async_copy(
                raw_buf.at[slot], raw_out.at[row_slice(chunk, rows)], raw_sems.at[slot]
            )

        def sums(chunk):
            stats.clear(chunk)

            @pl.when(chunk >= 2)
            def _():
                raw_copy(chunk - 2).wait()

            def tile(at):
                raw = reduce.raw[at]
                raw_buf[lax.rem(chunk, 2), at] = raw.astype(LOW)
                squares = jnp.sum(raw * raw, axis=1, keepdims=True)
                stats.put(chunk, at, squares, squares)

            tiles(rows, tile)
            stats.copy(chunk).start()
            raw_copy(chunk).start()

        def finish(chunk):
            slot = lax.rem(chunk, 2)
            for item in token_copies(chunk):
                item.wait()
            stats.copy(chunk).wait_recv()
            spread.clear(chunk)

            @pl.when(chunk >= 2)
            def _():
                mixed_copy(chunk - 2).wait()

            def tile(at):
                squares, _ = stats.get(chunk, at)
                factor = lax.rsqrt(squares / D + EPS)
                mixed = token_buf[at].astype(WIDE) + reduce.raw[at] * factor * gain[...]
                mixed_buf[slot, at] = mixed
                spread.put(chunk, at, mixed)

            tiles(rows, tile)
            spread.go(chunk)
            mixed_copy(chunk).start()

        schedule(chunks, reduce, multiply, fetch, sums, finish, ring.event, ring.events, prepare)
        def drain(chunk):
            for item in crossings(chunk):
                item.wait()

        loop(chunks, drain)
        up_spill.start()
        ring.end()
        up_spill.wait()
        ring.settle()
        reduce.end(chunks)
        stats.end(chunks)
        spread.end(chunks)
        for chunk in (chunks - 2, chunks - 1):
            mixed_copy(chunk).wait()
            raw_copy(chunk).wait()

    shape = jax.ShapeDtypeStruct
    out = pl.pallas_call(
        kernel,
        out_shape=[
            shape((length, half), LOW),
            shape((length, width), WIDE),
            shape((2 * chips, length, width), LOW),
            shape((shard * count, hidden), LOW),
            shape((shard * count, hidden), LOW),
            shape((count, inner, down_columns), LOW),
            shape((chips, length, width), LOW),
        ]
        + Reduce.landing(rows, chunks, width, False),
        in_specs=[VMEM, VMEM, VMEM, HBM, HBM, HBM, HBM, HBM],
        out_specs=[HBM] * 8,
        scratch_shapes=[item for group in groups for item in group],
        compiler_params=pltpu.CompilerParams(
            collective_id=collective, has_side_effects=True, vmem_limit_bytes=60 * MIB
        ),
        cost_estimate=pl.CostEstimate(
            flops=2 * length * width * D, bytes_accessed=8 * length * D, transcendentals=0
        ),
    )(attended, weight, gain, tokens, out_grad, gate_shard, up_shard, down_shard)
    return out[:7]


def mlp_forward(
    inputs, gate_full, up_full, down_first, down_second, gain, mixed, upstream, collective
):
    length, inner = inputs.shape[1], gate_full.shape[1]
    width = mixed.shape[1]
    ranks = inputs.shape[0]
    down_columns = down_first.shape[2]
    down_rows = down_first.shape[1]
    chips = lax.axis_size("gx") // 2
    half = chips * width
    chunks = lax.axis_size("gy")
    rows = length // chunks
    tile = min(512, inner)
    pieces = inner // tile

    groups = [
        Reduce.scratch(rows, chunks, width, False),
        Stats.scratch(rows, chunks),
        Spread.scratch(rows, chunks, width),
        [
            pltpu.VMEM((2, rows, half), LOW),
            pltpu.VMEM((rows, width), WIDE),
            pltpu.VMEM((2, rows, width), LOW),
            pltpu.SemaphoreType.DMA((2, chips)),
            pltpu.SemaphoreType.DMA((1,)),
            pltpu.SemaphoreType.DMA((2,)),
        ],
        [
            pltpu.VMEM((D, inner), LOW),
            pltpu.VMEM((D, inner), LOW),
            pltpu.VMEM((inner, D), LOW),
            pltpu.VMEM((2, rows, D), LOW),
            pltpu.VMEM((2, 3, rows, inner), LOW),
            pltpu.SemaphoreType.DMA((pieces, 2)),
            pltpu.SemaphoreType.DMA((2, chunks)),
            pltpu.SemaphoreType.DMA((2, ranks)),
            pltpu.SemaphoreType.DMA((2, 3)),
        ],
    ]

    def kernel(*refs):
        ins, outs, *scratch = take(refs, [8, 7] + [len(g) for g in groups])
        inputs, gate_full, up_full, down_first, down_second, gain, mixed, upstream = ins
        result, grad_out, gain_grad, hidden_out, silu_out, slope_out, cross_land = outs
        gate_weight, up_weight, weight, row_buf, made = scratch[4][:5]
        piece_sems, weight_sem, row_sems, made_sems = scratch[4][5:]
        reduce = Reduce(scratch[0], cross_land, rows, width, False)
        stats = Stats(*scratch[1])
        buffer, local, send, recv = scratch[2]
        spread = Spread(buffer, grad_out, local, send, recv, rows, width)
        up_buf, mixed_buf, result_buf, up_sems, mixed_sems, result_sems = scratch[3]

        def piece_copies(piece):
            at = pl.ds(aligned(piece * tile, tile), tile)
            return [
                pltpu.make_async_copy(gate_full.at[:, at], gate_weight.at[:, at], piece_sems.at[piece, 0]),
                pltpu.make_async_copy(up_full.at[:, at], up_weight.at[:, at], piece_sems.at[piece, 1]),
            ]

        weight_copies = all_blocks(
            down_first, None, down_columns, weight.at[:down_rows], weight_sem.at[0]
        ) + all_blocks(down_second, None, down_columns, weight.at[down_rows:], weight_sem.at[1])

        def row_copy(chunk):
            slot = lax.rem(chunk, 2)
            return all_blocks(
                inputs, row_slice(chunk, rows), width, row_buf.at[slot], row_sems.at[slot]
            )

        def stores(chunk):
            slot, at = lax.rem(chunk, 2), row_slice(chunk, rows)
            return [
                pltpu.make_async_copy(made.at[slot, which], out.at[at], made_sems.at[slot, which])
                for which, out in enumerate((hidden_out, silu_out, slope_out))
            ]

        for item in row_copy(0):
            item.start()
        for piece in range(pieces):
            for item in piece_copies(piece):
                item.start()
        for item in weight_copies:
            item.start()
        greet(True, False)
        gain_grad[...] = jnp.zeros_like(gain_grad)

        def prepare(chunk):
            slot = lax.rem(chunk, 2)
            for item in row_copy(chunk):
                item.wait()

            @pl.when(chunk + 1 < chunks)
            def _():
                for item in row_copy(chunk + 1):
                    item.start()

            @pl.when(chunk >= 2)
            def _():
                for item in stores(chunk - 2):
                    item.wait()

            @pl.loop(0, pieces)
            def _(piece):
                @pl.when(chunk == 0)
                def _():
                    for item in piece_copies(piece):
                        item.wait()

                at = pl.ds(aligned(piece * tile, tile), tile)
                gate = jnp.dot(row_buf[slot], gate_weight[:, at], preferred_element_type=WIDE)
                up = jnp.dot(row_buf[slot], up_weight[:, at], preferred_element_type=WIDE)
                sigma = jax.nn.sigmoid(gate)
                silu = gate * sigma
                made[slot, 0, :, at] = (silu * up).astype(LOW)
                made[slot, 1, :, at] = silu.astype(LOW)
                made[slot, 2, :, at] = (up * (sigma + silu * (1.0 - sigma))).astype(LOW)

            @pl.when(chunk == 0)
            def _():
                for item in weight_copies:
                    item.wait()

            for item in stores(chunk):
                item.start()

        def multiply(chunk, place):
            return jnp.dot(
                made[lax.rem(chunk, 2), 0],
                weight[:, pl.ds(place, width)],
                preferred_element_type=WIDE,
            )

        def up_copy(chunk):
            slot = lax.rem(chunk, 2)
            return all_blocks(
                upstream, row_slice(chunk, rows), width, up_buf.at[slot], up_sems.at[slot]
            )

        def mixed_copy(chunk):
            return pltpu.make_async_copy(
                mixed.at[row_slice(chunk, rows)], mixed_buf, mixed_sems.at[0]
            )

        def result_copy(chunk):
            slot = lax.rem(chunk, 2)
            return pltpu.make_async_copy(
                result_buf.at[slot], result.at[row_slice(chunk, rows)], result_sems.at[slot]
            )

        def fetch(chunk):
            @pl.when(chunk < chunks)
            def _():
                for item in up_copy(chunk):
                    item.start()

            @pl.when(chunk >= 1)
            def _():
                mixed_copy(chunk - 1).start()

        def sums(chunk):
            slot = lax.rem(chunk, 2)
            stats.clear(chunk)
            for item in up_copy(chunk):
                item.wait()

            def tile(at):
                raw = reduce.raw[at]
                up = up_buf[slot, at].astype(WIDE)
                squares = jnp.sum(raw * raw, axis=1, keepdims=True)
                projected = jnp.sum(gain[...] * up * raw, axis=1, keepdims=True)
                stats.put(chunk, at, squares, projected)

            tiles(rows, tile)
            stats.copy(chunk).start()

        def finish(chunk):
            slot = lax.rem(chunk, 2)
            mixed_copy(chunk).wait()
            stats.copy(chunk).wait_recv()
            spread.clear(chunk)

            @pl.when(chunk >= 2)
            def _():
                result_copy(chunk - 2).wait()

            block = pl.ds(aligned(chip_here() * width, width), width)

            def tile(at):
                squares, projected = stats.get(chunk, at)
                factor = lax.rsqrt(squares / D + EPS)
                raw = reduce.raw[at]
                up = up_buf[slot, at].astype(WIDE)
                pull = factor * factor * factor * projected / D
                spread.put(chunk, at, factor * gain[...] * up - raw * pull)
                gain_grad[...] += jnp.sum(up * raw * factor, axis=0, keepdims=True)
                result_buf[slot, at] = (
                    mixed_buf[at] + reduce.raw[at, block] * factor * gain[:, block]
                ).astype(LOW)

            tiles(rows, tile)
            spread.go(chunk)
            result_copy(chunk).start()

        schedule(chunks, reduce, multiply, fetch, sums, finish, prepare=prepare)
        reduce.end(chunks)
        stats.end(chunks)
        spread.end(chunks)
        for chunk in (chunks - 2, chunks - 1):
            result_copy(chunk).wait()
            for item in stores(chunk):
                item.wait()

    shape = jax.ShapeDtypeStruct
    out = pl.pallas_call(
        kernel,
        out_shape=[
            shape((length, width), LOW),
            shape((2 * chips, length, width), LOW),
            shape((1, half), WIDE),
            shape((length, inner), LOW),
            shape((length, inner), LOW),
            shape((length, inner), LOW),
        ]
        + Reduce.landing(rows, chunks, width, False),
        in_specs=[HBM] * 5 + [VMEM, HBM, HBM],
        out_specs=[HBM, HBM, VMEM] + [HBM] * 4,
        scratch_shapes=[item for group in groups for item in group],
        compiler_params=pltpu.CompilerParams(
            collective_id=collective, has_side_effects=True, vmem_limit_bytes=60 * MIB
        ),
        cost_estimate=pl.CostEstimate(
            flops=6 * length * inner * D, bytes_accessed=16 * length * D, transcendentals=0
        ),
    )(inputs, gate_full, up_full, down_first, down_second, gain, mixed, upstream)
    return out[:6]


def mlp_back(gate_grad, up_grad, gate_full, up_full, inputs, gain, upstream, attn_raw, collective):
    length, inner = gate_grad.shape
    half = attn_raw.shape[1]
    chips = lax.axis_size("gx") // 2
    width = half // chips
    count = lax.axis_size("gy")
    chunks = count
    rows = length // chunks
    shard = D // count
    slots, parts = 2, 2

    groups = [
        Reduce.scratch(rows, chunks, width, False),
        Stats.scratch(rows, chunks),
        Spread.scratch(rows, chunks, width),
        RingScatter.scratch(shard, inner, slots, parts),
        [
            pltpu.VMEM((rows, half), LOW),
            pltpu.VMEM((2, rows, half), LOW),
            pltpu.SemaphoreType.DMA((chips,)),
            pltpu.SemaphoreType.DMA((2,)),
            pltpu.SemaphoreType.DMA((1,)),
            pltpu.SemaphoreType.DMA((2,)),
        ],
        Columns.scratch(length, shard),
        [
            pltpu.VMEM((2, length, inner), LOW),
            pltpu.VMEM((2, inner, D), LOW),
            pltpu.SemaphoreType.DMA((2,)),
            pltpu.SemaphoreType.DMA((LAG + 2,)),
        ],
    ]

    def kernel(*refs):
        ins, outs, *scratch = take(refs, [8, 6] + [len(g) for g in groups])
        gate_grad, up_grad, gate_full, up_full, inputs, gain, upstream, attn_raw = ins
        grads, weights, load_sems, turn_sems = scratch[6]
        grad_copies = [
            pltpu.make_async_copy((gate_grad, up_grad)[way], grads.at[way], load_sems.at[way])
            for way in range(2)
        ]
        mixed_out, grad_out, gain_grad, gate_out, up_out, cross_land = outs
        reduce = Reduce(scratch[0], cross_land, rows, width, False)
        stats = Stats(*scratch[1])
        buffer, local, send, recv = scratch[2]
        spread = Spread(buffer, grad_out, local, send, recv, rows, width)
        total, summed, land, ring_send, ring_recv, credit = scratch[3]
        up_buf, raw_buf, up_sems, raw_sems, mixed_sems, out_sems = scratch[4]
        left = Columns(inputs, shard, *scratch[5])

        def product(way, step):
            left.take(ring, way, step)
            tile = 512

            @pl.when(step == 0)
            def _():
                grad_copies[way].wait()

            @pl.loop(0, inner // tile)
            def _(index):
                columns = pl.ds(aligned(index * tile, tile), tile)
                total[way, :, columns] = jnp.dot(
                    left.turned[...], grads[way, :, columns], preferred_element_type=WIDE
                )

        ring = RingScatter(
            product, total, summed, land, ring_send, ring_recv, credit, slots, parts
        )
        left.copy(ring.owner(0, 0)).start()
        for item in grad_copies:
            item.start()
        greet(True, True)
        gain_grad[...] = jnp.zeros_like(gain_grad)

        def turn_weights():
            across, depth = inner // half, LAG + 2
            for way, source in enumerate((gate_full, up_full)):

                def spot(index):
                    return (lax.div(index, across) * rows, lax.rem(index, across) * half)

                def copy(index):
                    down, right = spot(index)
                    block = source.at[
                        pl.ds(aligned(down, rows), rows), pl.ds(aligned(right, half), half)
                    ]
                    slot = lax.rem(index, depth)
                    return pltpu.make_async_copy(block, reduce.cross.at[slot], turn_sems.at[slot])

                def target(index, values):
                    down, right = spot(index)
                    weights[way, pl.ds(aligned(right, half), half), pl.ds(aligned(down, rows), rows)] = (
                        values
                    )

                turn_blocks(D // rows * across, copy, target, reduce.cross, depth)

        def multiply(chunk, place):
            at, columns = row_slice(chunk, rows), pl.ds(place, width)
            return jnp.dot(
                grads[0, at], weights[0, :, columns], preferred_element_type=WIDE
            ) + jnp.dot(grads[1, at], weights[1, :, columns], preferred_element_type=WIDE)

        def up_copy(chunk):
            return all_blocks(upstream, row_slice(chunk, rows), width, up_buf, up_sems)

        def raw_copy(chunk):
            slot = lax.rem(chunk, 2)
            return pltpu.make_async_copy(
                attn_raw.at[row_slice(chunk, rows)], raw_buf.at[slot], raw_sems.at[slot]
            )

        def mixed_copy(chunk):
            return pltpu.make_async_copy(
                reduce.raw.at[:, pl.ds(aligned(chip_here() * width, width), width)],
                mixed_out.at[row_slice(chunk, rows)],
                mixed_sems.at[0],
            )

        def fetch(chunk):
            @pl.when(chunk < chunks)
            def _():
                for item in up_copy(chunk):
                    item.start()
                raw_copy(chunk).start()

        def sums(chunk):
            slot = lax.rem(chunk, 2)
            stats.clear(chunk)
            for item in up_copy(chunk):
                item.wait()
            raw_copy(chunk).wait()

            def tile(at):
                upward = reduce.raw[at] + up_buf[at].astype(WIDE)
                reduce.raw[at] = upward
                raw = raw_buf[slot, at].astype(WIDE)
                squares = jnp.sum(raw * raw, axis=1, keepdims=True)
                projected = jnp.sum(gain[...] * upward * raw, axis=1, keepdims=True)
                stats.put(chunk, at, squares, projected)

            tiles(rows, tile)
            stats.copy(chunk).start()
            mixed_copy(chunk).start()

        def finish(chunk):
            slot = lax.rem(chunk, 2)
            stats.copy(chunk).wait_recv()
            spread.clear(chunk)

            def tile(at):
                squares, projected = stats.get(chunk, at)
                factor = lax.rsqrt(squares / D + EPS)
                upward = reduce.raw[at]
                raw = raw_buf[slot, at].astype(WIDE)
                pull = factor * factor * factor * projected / D
                spread.put(chunk, at, factor * gain[...] * upward - raw * pull)
                gain_grad[...] += jnp.sum(upward * raw * factor, axis=0, keepdims=True)

            tiles(rows, tile)
            spread.go(chunk)
            mixed_copy(chunk).wait()

        for index in range(parts):
            ring.event(jnp.int32(index))
        turn_weights()

        def later(index):
            ring.event(index + parts)

        schedule(chunks, reduce, multiply, fetch, sums, finish, later, ring.events - parts)
        writes = [
            pltpu.make_async_copy(total.at[way], (gate_out, up_out)[way], out_sems.at[way])
            for way in range(2)
        ]
        for item in writes:
            item.start()
        ring.end()
        reduce.end(chunks)
        stats.end(chunks)
        spread.end(chunks)
        for item in writes:
            item.wait()

    shape = jax.ShapeDtypeStruct
    out = pl.pallas_call(
        kernel,
        out_shape=[
            shape((length, width), WIDE),
            shape((length, D), LOW),
            shape((1, half), WIDE),
            shape((shard, inner), WIDE),
            shape((shard, inner), WIDE),
        ]
        + Reduce.landing(rows, chunks, width, False),
        in_specs=[HBM, HBM, HBM, HBM, HBM, VMEM, HBM, HBM],
        out_specs=[HBM, HBM, VMEM, HBM, HBM, HBM],
        scratch_shapes=[item for group in groups for item in group],
        compiler_params=pltpu.CompilerParams(
            collective_id=collective, has_side_effects=True, vmem_limit_bytes=60 * MIB
        ),
        cost_estimate=pl.CostEstimate(
            flops=8 * length * inner * D, bytes_accessed=16 * length * D, transcendentals=0
        ),
    )(gate_grad, up_grad, gate_full, up_full, inputs, gain, upstream, attn_raw)
    return out[:5]


class Total:
    def __init__(self, land, send, recv):
        self.land, self.send, self.recv = land, send, recv
        self.count = lax.axis_size("gx")

    @staticmethod
    def scratch(length):
        others = lax.axis_size("gx") - 1
        return [
            pltpu.VMEM((others, 8, length), WIDE),
            pltpu.SemaphoreType.DMA((others,)),
            pltpu.SemaphoreType.DMA((others,)),
        ]

    def copies(self, mine):
        return [
            remote(
                mine,
                self.land.at[shift - 1],
                self.send.at[shift - 1],
                self.recv.at[shift - 1],
                {"gx": rank_at(shift)},
            )
            for shift in range(1, self.count)
        ]

    def start(self, mine):
        for item in self.copies(mine):
            item.start()

    def finish(self, mine):
        for item in self.copies(mine):
            item.wait()
        total = mine[...]
        for shift in range(1, self.count):
            total = total + self.land[shift - 1]
        return total


def gather_in(tokens, stack, output_shard, gains, collective):
    length, width = tokens.shape
    _, shard, side = stack.shape
    columns = 2 * side
    count = lax.axis_size("gy")
    chunks = count
    rows = length // chunks
    chips = lax.axis_size("gx") // 2
    parts = 1
    out_columns = output_shard.shape[1]
    out_rows = width // 2

    groups = [
        RingGather.scratch(parts),
        [
            pltpu.SemaphoreType.DMA((1,)),
            pltpu.SemaphoreType.DMA((2,)),
            pltpu.SemaphoreType.DMA((chips - 1, chunks, 2)),
            pltpu.SemaphoreType.DMA((chips - 1, chunks, 2)),
        ],
        [
            pltpu.VMEM((2, D, side), LOW),
            pltpu.VMEM((2 * chips, length, width), LOW),
            pltpu.VMEM((2, 2, rows, width), WIDE),
            pltpu.VMEM((2, rows, width), LOW),
            pltpu.VMEM((length, STATS), WIDE),
            pltpu.VMEM((8, length), WIDE),
            pltpu.SemaphoreType.DMA((2,)),
            pltpu.SemaphoreType.DMA((2, 3)),
        ],
        Total.scratch(length),
        [
            pltpu.VMEM((chips - 1, 8, width), WIDE),
            pltpu.SemaphoreType.DMA((chips - 1, 2)),
        ],
        RingGather.scratch(1),
        [pltpu.VMEM((count, width, out_columns), LOW)],
    ]

    def kernel(*refs):
        ins, outs, *scratch = take(refs, [4, 8] + [len(g) for g in groups])
        tokens, stack, output_shard, gains = ins
        whole, full, output_full, query_raw, key_raw, values, squares, halves = outs
        out_held = scratch[6][0]
        gain_land, gain_sems = scratch[4]
        own_sem, core_sems, cross_sems, pass_sems = scratch[1]
        weight, held, raw_buf, value_buf, stats, mine = scratch[2][:6]
        copy_sems, out_sems = scratch[2][6:]
        total = Total(*scratch[3])

        def slot(way, owner, part):
            return weight.at[way, pl.ds(aligned(owner * shard, shard), shard)]

        def spill(way, owner, part):
            return full.at[way, pl.ds(aligned(owner * shard, shard), shard)]

        def source(way, part):
            return stack.at[way]

        ring = RingGather(source, slot, spill, parts, *scratch[0])

        def out_slot(way, owner, part):
            return out_held.at[owner, way * out_rows : (way + 1) * out_rows]

        def out_spill(way, owner, part):
            at = pl.ds(aligned(owner * out_columns, out_columns), out_columns)
            return output_full.at[way * out_rows : (way + 1) * out_rows, at]

        def out_source(way, part):
            return output_shard.at[way * out_rows : (way + 1) * out_rows]

        out_ring = RingGather(out_source, out_slot, out_spill, 1, *scratch[5])

        def block(rank, chunk):
            if chunk is None:
                return held.at[rank]
            return held.at[rank, row_slice(chunk, rows)]

        here = lax.axis_index("gx")
        own = pltpu.make_async_copy(tokens, block(here, None), own_sem.at[0])
        core = remote(
            block(here, None), block(here, None), core_sems.at[0], core_sems.at[1], {"gx": other_core()}
        )

        def cross(shift, chunk):
            return remote(
                block(here, chunk),
                block(here, chunk),
                cross_sems.at[shift - 1, chunk, 0],
                cross_sems.at[shift - 1, chunk, 1],
                {"gx": peer_at(shift)},
            )

        def onward(shift, chunk):
            spot = block(peer_at(chips - shift), chunk)
            return remote(
                spot,
                spot,
                pass_sems.at[shift - 1, chunk, 0],
                pass_sems.at[shift - 1, chunk, 1],
                {"gx": other_core()},
            )

        gain_copies = [
            remote(
                gains,
                gain_land.at[shift - 1],
                gain_sems.at[shift - 1, 0],
                gain_sems.at[shift - 1, 1],
                {"gx": peer_at(shift)},
            )
            for shift in range(1, chips)
        ]
        own.start()
        greet("all", True)
        for item in gain_copies:
            item.start()
        ring.begin()
        own.wait()

        def send(chunk):
            for shift in range(1, chips):
                cross(shift, chunk).start()

        loop(chunks, send)
        core.start()

        def step(chunk):
            for shift in range(1, chips):
                cross(shift, chunk).wait_recv()
                onward(shift, chunk).start()

            @pl.when(chunk < ring.events)
            def _():
                ring.event(chunk)

        loop(chunks, step)
        out_ring.begin()
        ring.end()

        def drain(chunk):
            for shift in range(1, chips):
                cross(shift, chunk).wait_send()
                onward(shift, chunk).wait()

        loop(chunks, drain)
        core.wait()
        whole_copy = pltpu.make_async_copy(held, whole, copy_sems.at[0])
        whole_copy.start()

        def stores(chunk):
            slot, at = lax.rem(chunk, 2), row_slice(chunk, rows)
            return [
                pltpu.make_async_copy(raw_buf.at[slot, 0], query_raw.at[at], out_sems.at[slot, 0]),
                pltpu.make_async_copy(raw_buf.at[slot, 1], key_raw.at[at], out_sems.at[slot, 1]),
                pltpu.make_async_copy(value_buf.at[slot], values.at[at], out_sems.at[slot, 2]),
            ]

        lane = lax.broadcasted_iota(jnp.int32, (rows, STATS), 1)

        def project(chunk):
            slot = lax.rem(chunk, 2)
            @pl.when(chunk >= 2)
            def _():
                for item in stores(chunk - 2):
                    item.wait()

            at = row_slice(chunk, rows)
            middle = side - width

            def against(way, columns):
                raw = jnp.zeros((rows, columns.stop - columns.start), WIDE)
                for rank in range(2 * chips):
                    raw = raw + jnp.dot(
                        held[rank, at],
                        weight[way, rank * width : (rank + 1) * width, columns],
                        preferred_element_type=WIDE,
                    )
                return raw

            some = []
            raw_buf[slot, 0] = against(0, slice(0, width))
            raw_buf[slot, 1, :, :middle] = against(0, slice(width, side))
            raw_buf[slot, 1, :, middle:] = against(1, slice(0, middle))
            value_buf[slot] = against(1, slice(middle, side)).astype(LOW)
            for which in range(2):
                raw = raw_buf[slot, which]
                some.append(jnp.sum(raw * raw, axis=1, keepdims=True))
            stats[row_slice(chunk, rows)] = jnp.where(lane == 0, some[0], some[1])
            for item in stores(chunk):
                item.start()

            @pl.when(chunk < out_ring.events)
            def _():
                out_ring.event(chunk)

        loop(chunks, project)
        mine[...] = stats[...].T[:8]
        total.start(mine)
        for chunk in (chunks - 2, chunks - 1):
            for item in stores(chunk):
                item.wait()
        squares[...] = total.finish(mine)
        whole_copy.wait()
        ring.settle()
        out_ring.end()
        out_ring.settle()
        halves[:, pl.ds(aligned(chip_here() * width, width), width)] = gains[...]
        for shift in range(1, chips):
            gain_copies[shift - 1].wait()
            chip = lax.rem(chip_here() + chips - shift, chips)
            halves[:, pl.ds(aligned(chip * width, width), width)] = gain_land[shift - 1]

    shape = jax.ShapeDtypeStruct
    return pl.pallas_call(
        kernel,
        out_shape=[
            shape((2 * chips, length, width), LOW),
            shape((2, shard * count, side), LOW),
            shape((width, D), LOW),
            shape((length, width), WIDE),
            shape((length, width), WIDE),
            shape((length, width), LOW),
            shape((8, length), WIDE),
            shape((8, chips * width), WIDE),
        ],
        in_specs=[HBM, HBM, HBM, VMEM],
        out_specs=[HBM] * 6 + [VMEM, VMEM],
        scratch_shapes=[item for group in groups for item in group],
        compiler_params=pltpu.CompilerParams(
            collective_id=collective, has_side_effects=True, vmem_limit_bytes=40 * MIB
        ),
        cost_estimate=pl.CostEstimate(
            flops=2 * length * columns * D, bytes_accessed=8 * length * D, transcendentals=0
        ),
    )(tokens, stack, output_shard, gains)


def hidden_back(blocks, down_first, down_second, hidden, silu, slope, collective):
    length, inner = hidden.shape
    count = lax.axis_size("gy")
    chunks = count
    rows = length // chunks
    shard = D // count
    side = inner // 2
    slots, parts = 3, 2
    down_rows = down_first.shape[1]
    tile = min(512, inner)

    groups = [
        RingScatter.scratch(shard, side, slots, parts),
        [
            pltpu.VMEM((2, 2, rows, inner), LOW),
            pltpu.VMEM((2, 2, rows, inner), LOW),
            pltpu.SemaphoreType.DMA((2, 2)),
            pltpu.SemaphoreType.DMA((2, 2)),
            pltpu.SemaphoreType.DMA((2,)),
            pltpu.VMEM((count, shard, length), LOW),
        ],
        [
            pltpu.VMEM((length, D), LOW),
            pltpu.VMEM((D, inner), LOW),
            pltpu.VMEM((2, down_rows, shard), LOW),
            pltpu.SemaphoreType.DMA((blocks.shape[0],)),
            pltpu.SemaphoreType.DMA((2,)),
        ],
    ]

    def kernel(*refs):
        ins, outs, *scratch = take(refs, [6, 3] + [len(g) for g in groups])
        blocks, down_first, down_second, hidden, silu, slope = ins
        grad, weight, stage, grad_sems, stage_sems = scratch[2]
        gate_grad, up_grad, weight_grad = outs
        total, summed, land, ring_send, ring_recv, credit = scratch[0]
        given, made, given_sems, made_sems, out_sems, turned = scratch[1]

        def product(way, step):
            owner = ring.owner(way, step)

            @pl.when((step < count // 2) | (step == count - 1))
            def _():
                turned[owner] = grad[:, pl.ds(aligned(owner * shard, shard), shard)].T

            size = min(512, side)

            @pl.loop(0, side // size)
            def _(index):
                at = pl.ds(aligned(index * size, size), size)
                take_at = pl.ds(aligned(way * side + index * size, size), size)
                total[way, :, at] = jnp.dot(
                    turned[owner], hidden[:, take_at], preferred_element_type=WIDE
                )

        ring = RingScatter(
            product, total, summed, land, ring_send, ring_recv, credit, slots, parts
        )

        def load(chunk):
            slot = lax.rem(chunk, 2)
            return [
                pltpu.make_async_copy(
                    (slope, silu)[which].at[row_slice(chunk, rows)],
                    given.at[slot, which],
                    given_sems.at[slot, which],
                )
                for which in range(2)
            ]

        def store(chunk):
            slot = lax.rem(chunk, 2)
            return [
                pltpu.make_async_copy(
                    made.at[slot, which],
                    (gate_grad, up_grad)[which].at[row_slice(chunk, rows)],
                    made_sems.at[slot, which],
                )
                for which in range(2)
            ]

        grad_copies = all_blocks(blocks, None, blocks.shape[2], grad, grad_sems)
        for item in grad_copies + load(0):
            item.start()
        greet(False, True)
        for item in grad_copies:
            item.wait()

        def turn_weight():
            for which, source in enumerate((down_first, down_second)):

                def copy(index):
                    slot = lax.rem(index, 2)
                    return pltpu.make_async_copy(
                        source.at[index], stage.at[slot], stage_sems.at[slot]
                    )

                def target(index, values):
                    at = pl.ds(aligned(index * shard, shard), shard)
                    weight[at, which * down_rows : (which + 1) * down_rows] = values

                turn_blocks(count, copy, target, stage, 2)

        def iteration(step):
            slot = lax.rem(step, 2)
            for part in range(parts):
                ring.event(step * parts + part)

            @pl.when(step + 1 < chunks)
            def _():
                for item in load(step + 1):
                    item.start()

            @pl.when(step >= 2)
            def _():
                for item in store(step - 2):
                    item.wait()

            for item in load(step):
                item.wait()

            @pl.when(step == 0)
            def _():
                turn_weight()

            @pl.loop(0, inner // tile)
            def _(index):
                at = pl.ds(aligned(index * tile, tile), tile)
                hidden_grad = jnp.dot(
                    grad[row_slice(step, rows)], weight[:, at], preferred_element_type=WIDE
                )
                for which in range(2):
                    made[slot, which, :, at] = (
                        hidden_grad * given[slot, which, :, at].astype(WIDE)
                    ).astype(LOW)

            for item in store(step):
                item.start()

        loop(chunks, iteration)
        writes = [
            pltpu.make_async_copy(
                total.at[way], weight_grad.at[:, way * side : (way + 1) * side], out_sems.at[way]
            )
            for way in range(2)
        ]
        for item in writes:
            item.start()
        for chunk in (chunks - 2, chunks - 1):
            for item in store(chunk):
                item.wait()
        ring.end()
        for item in writes:
            item.wait()

    shape = jax.ShapeDtypeStruct
    return pl.pallas_call(
        kernel,
        out_shape=[
            shape((length, inner), LOW),
            shape((length, inner), LOW),
            shape((shard, inner), WIDE),
        ],
        in_specs=[HBM, HBM, HBM, VMEM, HBM, HBM],
        out_specs=[HBM, HBM, HBM],
        scratch_shapes=[item for group in groups for item in group],
        compiler_params=pltpu.CompilerParams(
            collective_id=collective, has_side_effects=True, vmem_limit_bytes=60 * MIB
        ),
        cost_estimate=pl.CostEstimate(
            flops=4 * length * inner * D, bytes_accessed=16 * length * D, transcendentals=0
        ),
    )(blocks, down_first, down_second, hidden, silu, slope)


def attn_in_back(
    query_back,
    key_back,
    value_grad,
    query_raw,
    key_raw,
    factors,
    projections,
    query_gain,
    key_gain,
    stack,
    inputs,
    mixed_grad,
    gain_parts,
    collective,
):
    length, columns = value_grad.shape[0], 2 * stack.shape[2]
    width = mixed_grad.shape[1]
    count = lax.axis_size("gy")
    chunks = count
    rows = length // chunks
    shard = D // count
    side = columns // 2
    slots, parts = count - 1, 2
    tile = 256 if side % 256 == 0 else 128

    groups = [
        Reduce.scratch(rows, chunks, width, True),
        RingScatter.scratch(shard, side, slots, parts),
        [
            pltpu.VMEM((rows, width), WIDE),
            pltpu.VMEM((2, rows, width), WIDE),
            pltpu.VMEM((length, columns), LOW),
            pltpu.VMEM((length, STATS), WIDE),
            pltpu.VMEM((2, 4, rows, width), WIDE),
            pltpu.VMEM((2, side, D), LOW),
            pltpu.VMEM((2, shard, side), LOW),
            pltpu.SemaphoreType.DMA((2, 4)),
            pltpu.SemaphoreType.DMA((1,)),
            pltpu.SemaphoreType.DMA((2,)),
            pltpu.SemaphoreType.DMA((1,)),
            pltpu.SemaphoreType.DMA((2,)),
            pltpu.SemaphoreType.DMA((2,)),
        ],
        Columns.scratch(length, shard),
        Total.scratch(length),
        [
            pltpu.VMEM((8, width), WIDE),
            pltpu.VMEM((count - 1, 8, width), WIDE),
            pltpu.SemaphoreType.DMA((count - 1, 2)),
        ],
    ]

    def kernel(*refs):
        ins, outs, *scratch = take(refs, [16, 4] + [len(g) for g in groups])
        query_back, key_back, value_grad, query_raw, key_raw, factors = ins[:6]
        projections, query_gain, key_gain, full, inputs, mixed_grad = ins[6:12]
        gain_parts = ins[12:]
        token_grad, weight_grad, gain_grads, cross_land = outs
        gain_mine, gain_land, gain_sems = scratch[5]
        reduce = Reduce(scratch[0], cross_land, rows, width, True)
        total, summed, land, ring_send, ring_recv, credit = scratch[1]
        mixed_buf, token_buf, grads, projected, given, stack, stage = scratch[2][:7]
        given_sems, whole_sems, stage_sems, mixed_sems, token_sems, out_sems = scratch[2][7:]
        left = Columns(inputs, shard, *scratch[3])
        total_sum = Total(*scratch[4])

        def product(way, step):
            left.take(ring, way, step)

            @pl.loop(0, side // tile)
            def _(index):
                at = pl.ds(aligned(index * tile, tile), tile)
                take_at = pl.ds(aligned(way * side + index * tile, tile), tile)
                total[way, :, at] = jnp.dot(
                    left.turned[...], grads[:, take_at], preferred_element_type=WIDE
                )

        ring = RingScatter(
            product, total, summed, land, ring_send, ring_recv, credit, slots, parts
        )
        def load(chunk):
            slot, at = lax.rem(chunk, 2), row_slice(chunk, rows)
            return [
                pltpu.make_async_copy(
                    source.at[at], given.at[slot, which], given_sems.at[slot, which]
                )
                for which, source in enumerate((query_back, key_back, query_raw, key_raw))
            ]

        value_copy = pltpu.make_async_copy(value_grad, grads.at[:, 2 * width :], whole_sems.at[0])
        left.copy(ring.owner(0, 0)).start()
        for item in load(0):
            item.start()
        value_copy.start()
        chip_columns = pl.ds(aligned(chip_here() * width, width), width)
        gain_mine[...] = jnp.zeros_like(gain_mine)
        for which, part in enumerate(gain_parts):
            gain_mine[which : which + 1] = part[...] if which < 2 else part[:, chip_columns]
        greet("all", False, True)
        total_sum.start(projections)
        gain_copies = [
            remote(
                gain_mine,
                gain_land.at[shift - 1],
                gain_sems.at[shift - 1, 0],
                gain_sems.at[shift - 1, 1],
                {"gy": block_at(shift)},
            )
            for shift in range(1, count)
        ]
        for item in gain_copies:
            item.start()
        sums_here = total_sum.finish(projections)
        projected[...] = jnp.concatenate([sums_here] * (STATS // 8), axis=0).T

        def form(chunk):
            slot = lax.rem(chunk, 2)

            @pl.when(chunk + 1 < chunks)
            def _():
                for item in load(chunk + 1):
                    item.start()

            for item in load(chunk):
                item.wait()

            def some(part):
                at = pl.ds(aligned(chunk * rows + part.start, 32), 32)
                for which, gain in enumerate((query_gain, key_gain)):
                    factor = factors[at, which : which + 1]
                    pull = factor * factor * factor * projected[at, which : which + 1] / D
                    back, raw = given[slot, which, part], given[slot, which + 2, part]
                    grads[at, which * width : (which + 1) * width] = (
                        factor * gain[...] * back - raw * pull
                    ).astype(LOW)

            tiles(rows, some)

        loop(chunks, form)
        value_copy.wait()

        def turn_stack():
            for way in range(2):

                def spot(index):
                    return pl.ds(aligned(index * shard, shard), shard)

                def copy(index):
                    slot = lax.rem(index, 2)
                    return pltpu.make_async_copy(
                        full.at[way, spot(index)], stage.at[slot], stage_sems.at[slot]
                    )

                def target(index, values):
                    stack[way, :, spot(index)] = values

                turn_blocks(count, copy, target, stage, 2)

        def multiply(chunk, place):
            at, columns = row_slice(chunk, rows), pl.ds(place, width)
            return jnp.dot(
                grads[at, :side], stack[0, :, columns], preferred_element_type=WIDE
            ) + jnp.dot(grads[at, side:], stack[1, :, columns], preferred_element_type=WIDE)

        def mixed_copy(chunk):
            return pltpu.make_async_copy(
                mixed_grad.at[row_slice(chunk, rows)], mixed_buf, mixed_sems.at[0]
            )

        def token_copy(chunk):
            slot = lax.rem(chunk, 2)
            return pltpu.make_async_copy(
                token_buf.at[slot], token_grad.at[row_slice(chunk, rows)], token_sems.at[slot]
            )

        def fetch(chunk):
            @pl.when(chunk >= 1)
            def _():
                mixed_copy(chunk - 1).start()

        def sums(chunk):
            pass

        def finish(chunk):
            slot = lax.rem(chunk, 2)
            mixed_copy(chunk).wait()

            @pl.when(chunk >= 2)
            def _():
                token_copy(chunk - 2).wait()

            def some(at):
                token_buf[slot, at] = mixed_buf[at] + reduce.raw[at]

            tiles(rows, some)
            token_copy(chunk).start()

        for index in range(parts):
            ring.event(jnp.int32(index))
        turn_stack()

        def later(index):
            ring.event(index + parts)

        schedule(chunks, reduce, multiply, fetch, sums, finish, later, ring.events - parts)
        writes = [
            pltpu.make_async_copy(
                total.at[way], weight_grad.at[:, way * side : (way + 1) * side], out_sems.at[way]
            )
            for way in range(2)
        ]
        for item in writes:
            item.start()
        gain_total = gain_mine[...]
        for shift in range(1, count):
            gain_copies[shift - 1].wait()
            gain_total = gain_total + gain_land[shift - 1]
        gain_grads[...] = gain_total
        ring.end()
        reduce.end(chunks)
        for chunk in (chunks - 2, chunks - 1):
            token_copy(chunk).wait()
        for item in writes:
            item.wait()

    shape = jax.ShapeDtypeStruct
    out = pl.pallas_call(
        kernel,
        out_shape=[
            shape((length, width), WIDE),
            shape((shard, columns), WIDE),
            shape((8, width), WIDE),
        ]
        + Reduce.landing(rows, chunks, width, True),
        in_specs=[HBM] * 5 + [VMEM] * 4 + [HBM] * 3 + [VMEM] * 4,
        out_specs=[HBM, HBM, VMEM, HBM],
        scratch_shapes=[item for group in groups for item in group],
        compiler_params=pltpu.CompilerParams(
            collective_id=collective, has_side_effects=True, vmem_limit_bytes=60 * MIB
        ),
        cost_estimate=pl.CostEstimate(
            flops=4 * length * columns * D, bytes_accessed=8 * length * D, transcendentals=0
        ),
    )(
        query_back,
        key_back,
        value_grad,
        query_raw,
        key_raw,
        factors,
        projections,
        query_gain,
        key_gain,
        stack,
        inputs,
        mixed_grad,
        *gain_parts,
    )
    return out[:3]


def token_positions(segment):
    length = segment.shape[0]
    labels = jnp.arange(SEGS, dtype=jnp.int32)
    member = (segment[:, None] == labels[None, :]).astype(jnp.int32)
    totals = jnp.sum(member, axis=0)
    starts = jnp.cumsum(totals) - totals
    opening = jnp.sum(member * starts[None, :], axis=1)
    return jnp.arange(length, dtype=jnp.int32) - opening


def rotary_tables(segment):
    place = token_positions(segment).astype(jnp.float32)
    halves = HEAD // 2
    inverse = jnp.exp(jnp.arange(halves, dtype=jnp.float32) * (-2.0 * math.log(THETA) / HEAD))
    angle = place[:, None] * inverse[None, :]
    return (jnp.cos(angle), jnp.sin(angle))


BLOCK = 256
LANES = 128
SCALE = 1.0 / math.sqrt(HEAD)
SCALE_TWO = SCALE * math.log2(math.e)


def turn(values, cosine, sine):
    return values * cosine + pltpu.roll(values, HEAD // 2, 1) * sine


def head_columns(head):
    return slice(head * HEAD, (head + 1) * HEAD)


def nt(left, right):
    return lax.dot_general(left, right, (((1,), (1,)), ((), ())), preferred_element_type=WIDE)


def attend(first_block, query_raw, key_raw, values, factors, query_gain, key_gain, tables, starts):
    length, width = query_raw.shape
    heads = width // HEAD

    def kernel(
        first_block,
        query_raw,
        key_raw,
        values,
        factors,
        query_gain,
        key_gain,
        cosine,
        sine,
        starts,
        queries,
        keys,
        attended,
        peaks,
        peak_columns,
    ):
        @pl.loop(0, length // BLOCK)
        def _(index):
            at = row_slice(index, BLOCK)
            cos, sin = cosine[at], sine[at]
            pairs = ((query_raw, query_gain, queries), (key_raw, key_gain, keys))
            for which, (raw, gain, out) in enumerate(pairs):
                factor = factors[at, which : which + 1]
                for head in range(heads):
                    columns = head_columns(head)
                    normed = raw[at, columns] * factor * gain[:, columns]
                    out[at, columns] = turn(normed, cos, sin).astype(LOW)

        lane = lax.broadcasted_iota(jnp.int32, (BLOCK, LANES), 1)
        row_index = lax.broadcasted_iota(jnp.int32, (BLOCK, BLOCK), 0)
        column_index = lax.broadcasted_iota(jnp.int32, (BLOCK, BLOCK), 1)

        def query_block(index):
            at = row_slice(index, BLOCK)
            start = starts[at]

            def key_block(other, carry):
                there = row_slice(other, BLOCK)
                key_place = column_index + other * BLOCK
                allowed = (key_place >= start) & (key_place <= row_index + index * BLOCK)
                made = []
                for head in range(heads):
                    columns = head_columns(head)
                    peak, total, rows = carry[head]
                    scores = nt(queries[at, columns], keys[there, columns]) * SCALE_TWO
                    scores = jnp.where(allowed, scores, NEGATIVE)
                    higher = jnp.maximum(peak, jnp.max(scores, axis=1, keepdims=True))
                    raised = jnp.exp2(scores - higher)
                    shrink = jnp.exp2(peak - higher)
                    total = total * shrink + jnp.sum(raised, axis=1, keepdims=True)
                    rows = rows * shrink + jnp.dot(
                        raised.astype(LOW), values[there, columns], preferred_element_type=WIDE
                    )
                    made.append((higher, total, rows))
                return tuple(made)

            empty = (
                jnp.full((BLOCK, 1), NEGATIVE, WIDE),
                jnp.zeros((BLOCK, 1), WIDE),
                jnp.zeros((BLOCK, HEAD), WIDE),
            )
            done = lax.fori_loop(first_block[index], index + 1, key_block, (empty,) * heads)
            column = jnp.zeros((BLOCK, LANES), WIDE)
            for head in range(heads):
                peak, total, rows = done[head]
                attended[at, head_columns(head)] = (rows / total).astype(LOW)
                column = jnp.where(lane == head, peak + jnp.log2(total), column)
            peak_columns[at] = column

        loop(length // BLOCK, query_block)
        peaks[...] = peak_columns[...].T[:8]

    shape = jax.ShapeDtypeStruct
    smem = pl.BlockSpec(memory_space=pltpu.SMEM)
    return pl.pallas_call(
        kernel,
        out_shape=[
            shape((length, width), LOW),
            shape((length, width), LOW),
            shape((length, width), LOW),
            shape((8, length), WIDE),
        ],
        in_specs=[smem] + [VMEM] * 9,
        out_specs=[VMEM] * 4,
        scratch_shapes=[pltpu.VMEM((length, LANES), WIDE)],
        compiler_params=pltpu.CompilerParams(vmem_limit_bytes=48 * MIB),
        cost_estimate=pl.CostEstimate(
            flops=2 * length * MAX_LEN * width,
            bytes_accessed=16 * length * width,
            transcendentals=length * MAX_LEN * heads // 2,
        ),
    )(first_block, query_raw, key_raw, values, factors, query_gain, key_gain, *tables, starts)


def attend_back(
    last_block,
    queries,
    keys,
    values,
    attended,
    upstream,
    peaks,
    query_raw,
    key_raw,
    factors,
    query_gain,
    key_gain,
    tables,
    start_row,
):
    length, width = query_raw.shape
    heads = width // HEAD

    def kernel(
        last_block,
        queries,
        keys,
        values,
        attended,
        upstream,
        peaks,
        query_raw,
        key_raw,
        factors,
        query_gain,
        key_gain,
        cosine,
        sine,
        start_row,
        query_out,
        key_out,
        value_out,
        projections,
        query_gain_grad,
        key_gain_grad,
        query_sum,
        key_sum,
        value_sum,
        columns_scratch,
        deltas,
    ):
        lane = lax.broadcasted_iota(jnp.int32, (BLOCK, LANES), 1)
        query_gain_grad[...] = jnp.zeros_like(query_gain_grad)
        key_gain_grad[...] = jnp.zeros_like(key_gain_grad)

        def prepare(index):
            at = row_slice(index, BLOCK)
            column = jnp.zeros((BLOCK, LANES), WIDE)
            for head in range(heads):
                columns = head_columns(head)
                delta = jnp.sum(
                    attended[at, columns].astype(WIDE) * upstream[at, columns].astype(WIDE),
                    axis=1,
                    keepdims=True,
                )
                column = jnp.where(lane == head, delta, column)
            columns_scratch[at] = column
            query_sum[at] = jnp.zeros((BLOCK, width), WIDE)

        loop(length // BLOCK, prepare)
        deltas[...] = columns_scratch[...].T[:8]
        row_index = lax.broadcasted_iota(jnp.int32, (BLOCK, BLOCK), 0)
        column_index = lax.broadcasted_iota(jnp.int32, (BLOCK, BLOCK), 1)

        def turn_back(at, summed, raw, gain, factor, out, gain_grad):
            cos, sin = cosine[at], sine[at]
            share = jnp.zeros((BLOCK, 1), WIDE)
            for head in range(heads):
                columns = head_columns(head)
                normed = turn(summed(head) * SCALE, cos, -sin)
                out[at, columns] = normed
                weighed = normed * raw[at, columns]
                share += jnp.sum(gain[:, columns] * weighed, axis=1, keepdims=True)
                gain_grad[:, columns] += jnp.sum(weighed * factor, axis=0, keepdims=True)
            return share

        def key_block(index):
            at = row_slice(index, BLOCK)
            key_sum[...] = jnp.zeros_like(key_sum)
            value_sum[...] = jnp.zeros_like(value_sum)

            def query_block(other, carry):
                there = row_slice(other, BLOCK)
                key_place = row_index + index * BLOCK
                allowed = (key_place >= start_row[:, there]) & (
                    key_place <= column_index + other * BLOCK
                )
                for head in range(heads):
                    columns = head_columns(head)
                    scores = nt(keys[at, columns], queries[there, columns]) * SCALE_TWO
                    scores = jnp.where(allowed, scores, NEGATIVE)
                    chance = jnp.exp2(scores - peaks[head : head + 1, there])
                    value_sum[:, columns] += jnp.dot(
                        chance.astype(LOW), upstream[there, columns], preferred_element_type=WIDE
                    )
                    chance_grad = nt(values[at, columns], upstream[there, columns])
                    score_grad = (chance * (chance_grad - deltas[head : head + 1, there])).astype(LOW)
                    key_sum[:, columns] += jnp.dot(
                        score_grad, queries[there, columns], preferred_element_type=WIDE
                    )
                    query_sum[there, columns] += lax.dot_general(
                        score_grad,
                        keys[at, columns],
                        (((0,), (0,)), ((), ())),
                        preferred_element_type=WIDE,
                    )
                return carry

            lax.fori_loop(index, last_block[index] + 1, query_block, 0)
            value_out[at] = value_sum[...].astype(LOW)
            share = turn_back(
                at,
                lambda head: key_sum[:, head_columns(head)],
                key_raw,
                key_gain,
                factors[at, 1:2],
                key_out,
                key_gain_grad,
            )
            columns_scratch[at] = jnp.where(lane == 1, share, 0.0)

        loop(length // BLOCK, key_block)

        def finish(index):
            at = row_slice(index, BLOCK)
            share = turn_back(
                at,
                lambda head: query_sum[at, head_columns(head)],
                query_raw,
                query_gain,
                factors[at, 0:1],
                query_out,
                query_gain_grad,
            )
            columns_scratch[at] += jnp.where(lane == 0, share, 0.0)

        loop(length // BLOCK, finish)
        projections[...] = columns_scratch[...].T[:8]

    shape = jax.ShapeDtypeStruct
    smem = pl.BlockSpec(memory_space=pltpu.SMEM)
    return pl.pallas_call(
        kernel,
        out_shape=[
            shape((length, width), WIDE),
            shape((length, width), WIDE),
            shape((length, width), LOW),
            shape((8, length), WIDE),
            shape((1, width), WIDE),
            shape((1, width), WIDE),
        ],
        in_specs=[smem] + [VMEM] * 14,
        out_specs=[VMEM] * 6,
        scratch_shapes=[
            pltpu.VMEM((length, width), WIDE),
            pltpu.VMEM((BLOCK, width), WIDE),
            pltpu.VMEM((BLOCK, width), WIDE),
            pltpu.VMEM((length, LANES), WIDE),
            pltpu.VMEM((8, length), WIDE),
        ],
        compiler_params=pltpu.CompilerParams(vmem_limit_bytes=52 * MIB),
        cost_estimate=pl.CostEstimate(
            flops=5 * length * MAX_LEN * width,
            bytes_accessed=32 * length * width,
            transcendentals=length * MAX_LEN * heads // 2,
        ),
    )(
        last_block,
        queries,
        keys,
        values,
        attended,
        upstream,
        peaks,
        query_raw,
        key_raw,
        factors,
        query_gain,
        key_gain,
        *tables,
        start_row,
    )


def shards(
    tokens,
    query_weight,
    key_weight,
    value_weight,
    output_weight,
    gate_weight,
    up_weight,
    down_weight,
    query_gain,
    key_gain,
    attn_gain,
    mlp_gain,
    seq_ids,
    out_grad,
):
    segment = seq_ids[0]
    length = tokens.shape[0]
    local_width = tokens.shape[1]
    cosine, sine = rotary_tables(segment)
    tables = (
        jnp.concatenate([cosine, cosine], axis=1),
        jnp.concatenate([-sine, sine], axis=1),
    )
    order = jnp.arange(length, dtype=jnp.int32)
    starts = order - token_positions(segment)
    blocks = length // BLOCK
    first_block = starts.reshape(blocks, BLOCK)[:, 0] // BLOCK
    closing = segment.reshape(blocks, BLOCK)[:, -1]
    ends = jnp.sum((segment[None, :] <= closing[:, None]).astype(jnp.int32), axis=1) - 1
    last_block = ends // BLOCK
    gains = jnp.concatenate([attn_gain[None], mlp_gain[None], jnp.zeros((6, local_width))], axis=0)
    query_gain, key_gain = query_gain.reshape(1, -1), key_gain.reshape(1, -1)
    middle = local_width // 2
    pairs = (
        (query_weight, key_weight[:, :middle]),
        (key_weight[:, middle:], value_weight),
    )
    stack = jnp.stack([jnp.concatenate(pair, axis=1) for pair in pairs])
    inputs, attn_stack, output_full, query_raw, key_raw, values, squares, halves = gather_in(
        tokens, stack, output_weight, gains, 1
    )
    attn_half, mlp_half = halves[:1], halves[1:2]
    middle = down_weight.shape[0] // 2
    squares, down_rows = lax.optimization_barrier((squares, down_weight[middle:]))
    down_second = lax.all_gather(down_rows, "gy", axis=0)
    factors = lax.rsqrt(squares[:2].T / D + EPS)
    queries, keys, attended, peaks = attend(
        first_block,
        query_raw,
        key_raw,
        values,
        factors,
        query_gain,
        key_gain,
        tables,
        starts[:, None],
    )
    attn_raw, mixed, mlp_inputs, gate_full, up_full, down_first, upstream = attn_out(
        attended, output_full, attn_half, inputs, out_grad, gate_weight, up_weight, down_weight[:middle], 2
    )
    result, mlp_full, mlp_gain_part, hidden, silu, slope = mlp_forward(
        mlp_inputs, gate_full, up_full, down_first, down_second, mlp_half, mixed, upstream, 3
    )
    gate_grad, up_grad, down_turned = hidden_back(
        mlp_full, down_first, down_second, hidden, silu, slope, 4
    )
    down_weight_grad = down_turned.T
    mixed_grad, attn_full, attn_gain_part, gate_weight_grad, up_weight_grad = mlp_back(
        gate_grad, up_grad, gate_full, up_full, mlp_inputs, attn_half, upstream, attn_raw, 5
    )
    output_product = lax.dot_general(
        attended, attn_full, (((0,), (0,)), ((), ())), preferred_element_type=jnp.float32
    )
    output_weight_grad = lax.psum_scatter(
        output_product.astype(jnp.bfloat16), "gy", scatter_dimension=1, tiled=True
    ).astype(jnp.float32)
    attended_grad = lax.dot_general(
        attn_full, output_full, (((1,), (1,)), ((), ())), preferred_element_type=jnp.float32
    ).astype(jnp.bfloat16)
    query_back, key_back, value_grad, projections, query_gain_part, key_gain_part = attend_back(
        last_block,
        queries,
        keys,
        values,
        attended,
        attended_grad,
        peaks,
        query_raw,
        key_raw,
        factors,
        query_gain,
        key_gain,
        tables,
        starts[None, :],
    )
    token_grad, attn_weight_grads, gain_grads = attn_in_back(
        query_back,
        key_back,
        value_grad,
        query_raw,
        key_raw,
        factors,
        projections,
        query_gain,
        key_gain,
        attn_stack,
        inputs,
        mixed_grad,
        (query_gain_part, key_gain_part, attn_gain_part, mlp_gain_part),
        6,
    )
    query_weight_grad = attn_weight_grads[:, :local_width]
    key_weight_grad = attn_weight_grads[:, local_width : 2 * local_width]
    value_weight_grad = attn_weight_grads[:, 2 * local_width :]
    query_gain_grad, key_gain_grad, attn_gain_grad, mlp_gain_grad = (gain_grads[i] for i in range(4))
    return (
        result,
        token_grad,
        query_weight_grad,
        key_weight_grad,
        value_weight_grad,
        output_weight_grad,
        gate_weight_grad,
        up_weight_grad,
        down_weight_grad,
        query_gain_grad,
        key_gain_grad,
        attn_gain_grad,
        mlp_gain_grad,
    )


def solution(mesh):
    return jax.shard_map(
        shards,
        mesh=mesh,
        in_specs=(
            P("gy", "gx"),
            P("gy", "gx"),
            P("gy", "gx"),
            P("gy", "gx"),
            P("gx", "gy"),
            P("gy", "gx"),
            P("gy", "gx"),
            P("gx", "gy"),
            P("gx"),
            P("gx"),
            P("gx"),
            P("gx"),
            P("gy", None),
            P("gy", "gx"),
        ),
        out_specs=(
            P("gy", "gx"),
            P("gy", "gx"),
            P("gy", "gx"),
            P("gy", "gx"),
            P("gy", "gx"),
            P("gx", "gy"),
            P("gy", "gx"),
            P("gy", "gx"),
            P("gx", "gy"),
            P("gx"),
            P("gx"),
            P("gx"),
            P("gx"),
        ),
        check_vma=False,
    )
```

```python
import math

import jax
import jax.numpy as jnp
from jax import lax
from jax.experimental import pallas as pl
from jax.experimental.pallas import tpu as pltpu
from jax.sharding import PartitionSpec as P

D = 2048
HEAD = 128
MAX_LEN = 1024
SEGS = 4


EPS = 1e-06
THETA = 500000.0
NEGATIVE = -1e30


MESH = pl.DeviceIdType.MESH
HBM = pl.BlockSpec(memory_space=pltpu.HBM)
VMEM = pl.BlockSpec(memory_space=pltpu.VMEM)
LOW = jnp.bfloat16
WIDE = jnp.float32
MIB = 1 << 20
LAG = 2
STATS = 128


def core_here():
    return lax.rem(lax.axis_index("gx"), 2)


def chip_here():
    return lax.div(lax.axis_index("gx"), 2)


def other_core():
    return lax.axis_index("gx") + 1 - 2 * core_here()


def peer_at(shift):
    return lax.rem(lax.axis_index("gx") + 2 * shift, lax.axis_size("gx"))


def rank_at(shift):
    return lax.rem(lax.axis_index("gx") + shift, lax.axis_size("gx"))


def block_at(shift):
    return lax.rem(lax.axis_index("gy") + shift, lax.axis_size("gy"))


def ring_place():
    count = lax.axis_size("gy")
    index = lax.axis_index("gy")
    row, side = lax.div(index, 2), lax.rem(index, 2)
    return side * row + (1 - side) * (count - 1 - row)


def ring_device(place):
    count = lax.axis_size("gy")
    place = lax.rem(place + 2 * count, count)
    back = lax.div(place, count // 2)
    row = (1 - back) * place + back * (count - 1 - place)
    return 2 * row + 1 - back


def greet(gx, ring, all_blocks=False):
    barrier = pltpu.get_barrier_semaphore()
    partners = []
    if all_blocks:
        partners += [{"gy": block_at(k)} for k in range(1, lax.axis_size("gy"))]
    if gx == "all":
        partners += [{"gx": rank_at(k)} for k in range(1, lax.axis_size("gx"))]
    elif gx:
        partners.append({"gx": other_core()})
        partners += [{"gx": peer_at(k)} for k in range(1, lax.axis_size("gx") // 2)]
    if ring:
        place = ring_place()
        partners += [{"gy": ring_device(place + 1)}, {"gy": ring_device(place - 1)}]
    for partner in partners:
        pl.semaphore_signal(barrier, inc=1, device_id=partner, device_id_type=MESH)
    pl.semaphore_wait(barrier, len(partners))


def remote(source, target, send, recv, device):
    return pltpu.make_async_remote_copy(
        src_ref=source,
        dst_ref=target,
        send_sem=send,
        recv_sem=recv,
        device_id=device,
        device_id_type=MESH,
    )


def loop(count, body):
    def step(index, carry):
        body(index)
        return carry

    lax.fori_loop(0, count, step, 0)


def aligned(value, factor):
    return pl.multiple_of(value, factor)


class RingGather:
    def __init__(self, sources, slot, spill, parts, send, recv, local, spilled):
        self.sources, self.slot, self.spill, self.parts = sources, slot, spill, parts
        self.send, self.recv, self.local, self.spilled = send, recv, local, spilled
        self.count = lax.axis_size("gy")

    @staticmethod
    def scratch(parts):
        count = lax.axis_size("gy")
        return [
            pltpu.SemaphoreType.DMA((count - 1, 2, parts)),
            pltpu.SemaphoreType.DMA((count - 1, 2, parts)),
            pltpu.SemaphoreType.DMA((2, parts)),
            pltpu.SemaphoreType.DMA((count, 2, parts)),
        ]

    def spill_copy(self, way, step, part):
        place = ring_place()
        owner = ring_device(place - (1 - 2 * way) * step)
        return pltpu.make_async_copy(
            self.slot(way, owner, part),
            self.spill(way, owner, part),
            self.spilled.at[step, way, part],
        )

    def copy(self, way, step, part, behind):
        place = ring_place()
        sign = 1 - 2 * way
        spot = self.slot(way, ring_device(place - sign * (step + behind)), part)
        return remote(
            spot,
            spot,
            self.send.at[step, way, part],
            self.recv.at[step, way, part],
            {"gy": ring_device(place + sign)},
        )

    def begin(self):
        place = [
            pltpu.make_async_copy(
                self.sources(way, part),
                self.slot(way, lax.axis_index("gy"), part),
                self.local.at[way, part],
            )
            for way in range(2)
            for part in range(self.parts)
        ]
        for item in place:
            item.start()
        for item in place:
            item.wait()
        for part in range(self.parts):
            for way in range(2):
                self.copy(way, 0, part, 0).start()
                self.spill_copy(way, 0, part).start()

    @property
    def events(self):
        return (self.count - 2) * self.parts

    def event(self, index):
        step = 1 + lax.div(index, self.parts)
        for part in range(self.parts):

            @pl.when(lax.rem(index, self.parts) == part)
            def _():
                for way in range(2):
                    self.copy(way, step - 1, part, 1).wait_recv()
                    self.copy(way, step, part, 0).start()
                    self.spill_copy(way, step, part).start()

    def end(self):
        for part in range(self.parts):
            for way in range(2):
                self.copy(way, self.count - 2, part, 1).wait_recv()
                self.spill_copy(way, self.count - 1, part).start()

        def drain(step):
            for part in range(self.parts):
                for way in range(2):
                    self.copy(way, step, part, 0).wait_send()

        loop(self.count - 1, drain)

    def settle(self):
        def drain(step):
            for part in range(self.parts):
                for way in range(2):
                    self.spill_copy(way, step, part).wait()

        loop(self.count, drain)


class RingScatter:
    def __init__(self, product, total, sums, land, send, recv, credit, slots, parts):
        self.product, self.total, self.sums, self.land = product, total, sums, land
        self.send, self.recv, self.credit = send, recv, credit
        self.slots, self.parts = slots, parts
        self.count = lax.axis_size("gy")
        self.rows = total.shape[2]

    @staticmethod
    def scratch(rows, columns, slots, parts):
        count = lax.axis_size("gy")
        return [
            pltpu.VMEM((2, parts, rows, columns // parts), WIDE),
            pltpu.VMEM((2, parts, rows, columns // parts), LOW),
            pltpu.VMEM((slots, 2, parts, rows, columns // parts), LOW),
            pltpu.SemaphoreType.DMA((count - 1, 2, parts)),
            pltpu.SemaphoreType.DMA((count - 1, 2, parts)),
            pltpu.SemaphoreType.REGULAR((2, parts)),
        ]

    def copy(self, way, step, part):
        place = ring_place()
        return remote(
            self.sums.at[way, part],
            self.land.at[lax.rem(step, self.slots), way, part],
            self.send.at[step, way, part],
            self.recv.at[step, way, part],
            {"gy": ring_device(place + 1 - 2 * way)},
        )

    def owner(self, way, step):
        sign = 1 - 2 * way
        return ring_device(ring_place() - sign * (1 + step))

    @property
    def events(self):
        return self.count * self.parts

    def event(self, index):
        step, part = lax.div(index, self.parts), lax.rem(index, self.parts)
        last = self.count - 1
        tile = min(self.rows, 32)

        for way in range(2):
            self.product(way, step, part)

        for way in range(2):

            slot = lax.rem(step - 1 + self.slots, self.slots)

            def over(body):
                @pl.loop(0, self.rows // tile)
                def _(index):
                    body(pl.ds(aligned(index * tile, tile), tile))

            @pl.when(step >= 1)
            def _():
                self.copy(way, step - 1, part).wait_recv()

            @pl.when((step >= 1) & (step < last))
            def _():
                self.copy(way, step - 1, part).wait_send()

            @pl.when(step == 0)
            def _():
                def first(rows):
                    self.sums[way, part, rows] = self.total[way, part, rows].astype(LOW)

                over(first)

            @pl.when((step >= 1) & (step < last))
            def _():
                def more(rows):
                    arrived = self.land[slot, way, part, rows].astype(WIDE)
                    self.sums[way, part, rows] = (self.total[way, part, rows] + arrived).astype(LOW)

                over(more)

            @pl.when(step == last)
            def _():
                def final(rows):
                    self.total[way, part, rows] += self.land[slot, way, part, rows].astype(WIDE)

                over(final)

            @pl.when((step >= 1) & (step - 1 + self.slots < last))
            def _():
                upstream = ring_device(ring_place() - (1 - 2 * way))
                pl.semaphore_signal(
                    self.credit.at[way, part],
                    inc=1,
                    device_id={"gy": upstream},
                    device_id_type=MESH,
                )

            @pl.when(step < last)
            def _():
                @pl.when(step >= self.slots)
                def _():
                    pl.semaphore_wait(self.credit.at[way, part], 1)

                self.copy(way, step, part).start()

    def end(self):
        for part in range(self.parts):
            for way in range(2):
                self.copy(way, self.count - 2, part).wait_send()


class Reduce:
    def __init__(self, refs, cross_land, rows, width, scatter):
        (
            self.keep,
            self.core_send,
            self.core_land,
            self.cross,
            self.cross_stage,
            self.raw,
            self.core_sems,
            self.cross_send_sems,
            self.cross_recv_sems,
            self.stage_sems,
        ) = refs
        self.cross_land = cross_land
        self.rows, self.width, self.scatter = rows, width, scatter
        self.chips = lax.axis_size("gx") // 2

    @staticmethod
    def scratch(rows, chunks, width, scatter):
        chips = lax.axis_size("gx") // 2
        half = chips * width
        part = width if scatter else half
        return [
            pltpu.VMEM((1, rows, half), LOW),
            pltpu.VMEM((2, rows, half), LOW),
            pltpu.VMEM((2, rows, half), LOW),
            pltpu.VMEM((LAG + 1, chips, rows, width) if scatter else (LAG + 1, rows, half), LOW),
            pltpu.VMEM((chips - 1, rows, part), LOW),
            pltpu.VMEM((rows, part), WIDE),
            pltpu.SemaphoreType.DMA((2, chunks)),
            pltpu.SemaphoreType.DMA((chips - 1, chunks)),
            pltpu.SemaphoreType.DMA((chips - 1, chunks)),
            pltpu.SemaphoreType.DMA((chips,)),
        ]

    @staticmethod
    def landing(rows, chunks, width, scatter):
        chips = lax.axis_size("gx") // 2
        half = chips * width
        part = width if scatter else half
        return [jax.ShapeDtypeStruct((chips - 1, chunks, rows, part), LOW)]

    def core_copy(self, chunk):
        return remote(
            self.core_send.at[lax.rem(chunk, 2)],
            self.core_land.at[lax.rem(chunk, 2)],
            self.core_sems.at[0, chunk],
            self.core_sems.at[1, chunk],
            {"gx": other_core()},
        )

    def cross_copy(self, shift, chunk):
        source = self.cross.at[lax.rem(chunk, LAG + 1)]
        if self.scatter:
            block = lax.rem(chip_here() + shift, self.chips)
            source = source.at[block]
        return remote(
            source,
            self.cross_land.at[shift - 1, chunk],
            self.cross_send_sems.at[shift - 1, chunk],
            self.cross_recv_sems.at[shift - 1, chunk],
            {"gx": peer_at(shift)},
        )

    def produce(self, chunk, dot):
        @pl.when(chunk >= 2)
        def _():
            self.core_copy(chunk - 2).wait_send()

        slot = lax.rem(chunk, 2)
        core = core_here()
        for chip in range(self.chips):
            place = aligned((2 * chip + 1 - core) * self.width, self.width)
            self.core_send[slot, :, chip * self.width : (chip + 1) * self.width] = dot(
                place
            ).astype(LOW)
        self.core_copy(chunk).start()
        for chip in range(self.chips):
            place = aligned((2 * chip + core) * self.width, self.width)
            self.keep[0, :, chip * self.width : (chip + 1) * self.width] = dot(
                place
            ).astype(LOW)

    def core_sum(self, chunk):
        slot, place = lax.rem(chunk, 2), lax.rem(chunk, LAG + 1)
        self.core_copy(chunk).wait_recv()

        @pl.when(chunk >= LAG + 1)
        def _():
            for shift in range(1, self.chips):
                self.cross_copy(shift, chunk - LAG - 1).wait_send()

        @pl.loop(0, self.rows // 32)
        def _(index):
            rows = pl.ds(aligned(index * 32, 32), 32)
            total = self.keep[0, rows].astype(WIDE) + self.core_land[slot, rows].astype(WIDE)
            if self.scatter:
                for chip in range(self.chips):
                    columns = slice(chip * self.width, (chip + 1) * self.width)
                    self.cross[place, chip, rows] = total[:, columns].astype(LOW)
            else:
                self.cross[place, rows] = total.astype(LOW)

        for shift in range(1, self.chips):
            self.cross_copy(shift, chunk).start()

    def cross_stage_copy(self, shift, chunk):
        return pltpu.make_async_copy(
            self.cross_land.at[shift - 1, chunk],
            self.cross_stage.at[shift - 1],
            self.stage_sems.at[shift],
        )

    def cross_fetch(self, chunk):
        for shift in range(1, self.chips):
            self.cross_copy(shift, chunk).wait_recv()
            self.cross_stage_copy(shift, chunk).start()

    def cross_sum(self, chunk):
        place = lax.rem(chunk, LAG + 1)
        for shift in range(1, self.chips):
            self.cross_stage_copy(shift, chunk).wait()

        @pl.loop(0, self.rows // 32)
        def _(index):
            rows = pl.ds(aligned(index * 32, 32), 32)
            if self.scatter:
                total = self.cross[place, chip_here(), rows].astype(WIDE)
            else:
                total = self.cross[place, rows].astype(WIDE)
            for shift in range(1, self.chips):
                total = total + self.cross_stage[shift - 1, rows].astype(WIDE)
            self.raw[rows] = total

    def end(self, chunks):
        for chunk in (chunks - 2, chunks - 1):
            self.core_copy(chunk).wait_send()
        for chunk in range(chunks - LAG - 1, chunks):
            for shift in range(1, self.chips):
                self.cross_copy(shift, chunk).wait_send()


class Stats:
    def __init__(self, mine, land, sems):
        self.mine, self.land, self.sems = mine, land, sems

    @staticmethod
    def scratch(rows, chunks):
        return [
            pltpu.VMEM((2, rows, STATS), WIDE),
            pltpu.VMEM((2, rows, STATS), WIDE),
            pltpu.SemaphoreType.DMA((2, chunks)),
        ]

    def copy(self, chunk):
        return remote(
            self.mine.at[lax.rem(chunk, 2)],
            self.land.at[lax.rem(chunk, 2)],
            self.sems.at[0, chunk],
            self.sems.at[1, chunk],
            {"gx": other_core()},
        )

    def clear(self, chunk):
        @pl.when(chunk >= 2)
        def _():
            self.copy(chunk - 2).wait_send()

    def put(self, chunk, rows, first, second):
        lane = lax.broadcasted_iota(jnp.int32, (first.shape[0], STATS), 1)
        self.mine[lax.rem(chunk, 2), rows] = jnp.where(lane < STATS // 2, first, second)

    def get(self, chunk, rows):
        total = self.mine[lax.rem(chunk, 2), rows] + self.land[lax.rem(chunk, 2), rows]
        return (total[:, :1], total[:, STATS // 2 : STATS // 2 + 1])

    def end(self, chunks):
        for chunk in (chunks - 2, chunks - 1):
            self.copy(chunk).wait_send()


class Spread:
    def __init__(self, buffer, whole, local, send, recv, rows, width):
        self.buffer, self.whole = buffer, whole
        self.local, self.send, self.recv = local, send, recv
        self.rows, self.width = rows, width
        self.chips = lax.axis_size("gx") // 2

    @staticmethod
    def scratch(rows, chunks, width):
        chips = lax.axis_size("gx") // 2
        return [
            pltpu.VMEM((2, chips, rows, width), LOW),
            pltpu.SemaphoreType.DMA((2, chips)),
            pltpu.SemaphoreType.DMA((chunks, chips)),
            pltpu.SemaphoreType.DMA((chunks, chips)),
        ]

    def pair(self, chunk, chip, core):
        slot = lax.rem(chunk, 2)
        source = self.buffer.at[slot, chip]
        rows = pl.ds(aligned(chunk * self.rows, self.rows), self.rows)
        rank = 2 * chip + core
        if len(self.whole.shape) == 3:
            target = self.whole.at[rank, rows]
        else:
            columns = pl.ds(aligned(rank * self.width, self.width), self.width)
            target = self.whole.at[rows, columns]
        here = pltpu.make_async_copy(source, target, self.local.at[slot, chip])
        away = remote(
            source,
            target,
            self.send.at[chunk, chip],
            self.recv.at[chunk, chip],
            {"gx": other_core()},
        )
        return (here, away)

    def put(self, chunk, rows, values):
        for chip in range(self.chips):
            columns = slice(chip * self.width, (chip + 1) * self.width)
            self.buffer[lax.rem(chunk, 2), chip, rows] = values[:, columns].astype(LOW)

    def clear(self, chunk):
        @pl.when(chunk >= 2)
        def _():
            self.settle(chunk - 2)

    def settle(self, chunk):
        for chip in range(self.chips):
            here, away = self.pair(chunk, chip, core_here())
            here.wait()
            away.wait_send()

    def go(self, chunk):
        for chip in range(self.chips):
            here, away = self.pair(chunk, chip, core_here())
            here.start()
            away.start()

    def end(self, chunks):
        for chunk in (chunks - 2, chunks - 1):
            self.settle(chunk)

        def arrive(chunk):
            for chip in range(self.chips):
                self.pair(chunk, chip, 1 - core_here())[1].wait_recv()

        loop(chunks, arrive)


def row_slice(chunk, rows):
    return pl.ds(aligned(chunk * rows, rows), rows)


def core_blocks(source, chunk, rows, width, buffer, sems):
    return [
        pltpu.make_async_copy(
            source.at[2 * chip + core_here(), row_slice(chunk, rows)],
            buffer.at[:, chip * width : (chip + 1) * width],
            sems.at[chip],
        )
        for chip in range(lax.axis_size("gx") // 2)
    ]


def all_blocks(source, rows, width, buffer, sems):
    return [
        pltpu.make_async_copy(
            source.at[rank] if rows is None else source.at[rank, rows],
            buffer.at[:, rank * width : (rank + 1) * width],
            sems.at[rank],
        )
        for rank in range(source.shape[0])
    ]


def tiles(rows, body):
    @pl.loop(0, rows // 32)
    def _(index):
        body(pl.ds(aligned(index * 32, 32), 32))


def schedule(chunks, reduce, multiply, fetch, sums, finish, event=None, events=0, prepare=None):
    steps = chunks + 1 + LAG

    def ring_events(place):
        if event is not None:
            low = lax.div(place * events, 2 * steps)
            high = lax.div((place + 1) * events, 2 * steps)

            def some(index, carry):
                event(index)
                return carry

            lax.fori_loop(low, high, some, 0)

    def iteration(step):
        ring_events(2 * step)

        @pl.when((step >= LAG) & (step < chunks + LAG))
        def _():
            reduce.cross_fetch(step - LAG)

        @pl.when(step >= LAG)
        def _():
            fetch(step - LAG)

        @pl.when(step < chunks)
        def _():
            if prepare is not None:
                prepare(step)
            reduce.produce(step, lambda place: multiply(step, place))
            reduce.core_sum(step)

        ring_events(2 * step + 1)

        @pl.when(step >= 1 + LAG)
        def _():
            finish(step - 1 - LAG)

        @pl.when((step >= LAG) & (step < chunks + LAG))
        def _():
            reduce.cross_sum(step - LAG)
            sums(step - LAG)

    loop(steps, iteration)


def take(refs, counts):
    groups, start = [], 0
    for count in counts:
        groups.append(refs[start : start + count])
        start += count
    return groups


class Columns:
    def __init__(self, source, shard, left, turned, sem):
        self.source, self.shard = source, shard
        self.left, self.turned, self.sem = left, turned, sem

    @staticmethod
    def scratch(length, shard):
        return [
            pltpu.VMEM((length, shard), LOW),
            pltpu.VMEM((2, shard, length), LOW),
            pltpu.SemaphoreType.DMA((1,)),
        ]

    def copy(self, owner):
        each = self.source.shape[2] // self.shard
        at = pl.ds(aligned(lax.rem(owner, each) * self.shard, self.shard), self.shard)
        source = self.source.at[lax.div(owner, each), :, at]
        return pltpu.make_async_copy(source, self.left, self.sem.at[0])

    def take(self, ring, way, step):
        self.copy(ring.owner(way, step)).wait()
        self.turned[way] = self.left[...].T
        if way == 0:
            self.copy(ring.owner(1, step)).start()
        else:

            @pl.when(step + 1 < ring.count)
            def _():
                self.copy(ring.owner(0, step + 1)).start()


def attn_out(
    attended, weight, gain, tokens, out_grad, gate_shard, up_shard, down_shard, collective
):
    length, width = attended.shape
    chips = lax.axis_size("gx") // 2
    half = chips * width
    count = lax.axis_size("gy")
    chunks = count
    rows = length // chunks
    hidden = gate_shard.shape[1]
    inner = down_shard.shape[0]
    shard = gate_shard.shape[0]
    part_rows = shard // 2
    side = inner // 2
    down_columns = down_shard.shape[1]

    groups = [
        Reduce.scratch(rows, chunks, width, False),
        Stats.scratch(rows, chunks),
        Spread.scratch(rows, chunks, width),
        RingGather.scratch(3),
        [
            pltpu.VMEM((rows, half), LOW),
            pltpu.VMEM((2, rows, half), WIDE),
            pltpu.VMEM((2, rows, half), LOW),
            pltpu.SemaphoreType.DMA((chips,)),
            pltpu.SemaphoreType.DMA((2,)),
            pltpu.SemaphoreType.DMA((2,)),
            pltpu.SemaphoreType.DMA((2,)),
            pltpu.SemaphoreType.DMA((chips - 1, chunks, 2)),
        ],
        [
            pltpu.VMEM((2, D, hidden), LOW),
            pltpu.VMEM((count, inner, down_columns), LOW),
            pltpu.VMEM((chips, length, width), LOW),
        ],
    ]

    def kernel(*refs):
        ins, outs, *scratch = take(refs, [8, 8] + [len(g) for g in groups])
        attended, weight, gain, tokens, out_grad, gate_shard, up_shard, down_shard = ins
        raw_out, mixed_out, low_out, gate_full, up_full, down_full, upstream = outs[:7]
        cross_land = outs[7]
        reduce = Reduce(scratch[0], cross_land, rows, width, False)
        stats = Stats(*scratch[1])
        buffer, local, send, recv = scratch[2]
        spread = Spread(buffer, low_out, local, send, recv, rows, width)
        token_buf, mixed_buf, raw_buf = scratch[4][:3]
        token_sems, mixed_sems, raw_sems, own_sem, up_sems = scratch[4][3:]
        held, held_down, up_land = scratch[5]
        shards_here = (gate_shard, up_shard)

        def place_in(full, down):
            def slot(way, owner, part):
                if part == 2:
                    return down.at[owner, way * side : (way + 1) * side]
                base = owner * shard + part * part_rows
                return full[way].at[pl.ds(aligned(base, part_rows), part_rows)]

            return slot

        slot = place_in((held.at[0], held.at[1]), held_down)
        spill = place_in((gate_full, up_full), down_full)

        def source(way, part):
            if part == 2:
                return down_shard.at[way * side : (way + 1) * side]
            return shards_here[way].at[part * part_rows : (part + 1) * part_rows]

        ring = RingGather(source, slot, spill, 3, *scratch[3])
        own = pltpu.make_async_copy(out_grad, up_land.at[chip_here()], own_sem.at[0])
        up_spill = pltpu.make_async_copy(up_land, upstream, own_sem.at[1])

        def crossings(chunk):
            at = row_slice(chunk, rows)
            return [
                remote(
                    up_land.at[chip_here(), at],
                    up_land.at[chip_here(), at],
                    up_sems.at[shift - 1, chunk, 0],
                    up_sems.at[shift - 1, chunk, 1],
                    {"gx": peer_at(shift)},
                )
                for shift in range(1, chips)
            ]

        own.start()
        greet(True, True)
        ring.begin()
        own.wait()

        def multiply(chunk, place):
            return jnp.dot(
                attended[row_slice(chunk, rows)],
                weight[:, pl.ds(place, width)],
                preferred_element_type=WIDE,
            )

        def prepare(chunk):
            for item in crossings(chunk):
                item.start()

        def token_copies(chunk):
            return core_blocks(tokens, chunk, rows, width, token_buf, token_sems)

        def fetch(chunk):
            @pl.when(chunk >= 1)
            def _():
                for item in token_copies(chunk - 1):
                    item.start()

        def mixed_copy(chunk):
            slot = lax.rem(chunk, 2)
            return pltpu.make_async_copy(
                mixed_buf.at[slot, :, pl.ds(aligned(chip_here() * width, width), width)],
                mixed_out.at[row_slice(chunk, rows)],
                mixed_sems.at[slot],
            )

        def raw_copy(chunk):
            slot = lax.rem(chunk, 2)
            return pltpu.make_async_copy(
                raw_buf.at[slot], raw_out.at[row_slice(chunk, rows)], raw_sems.at[slot]
            )

        def sums(chunk):
            stats.clear(chunk)

            @pl.when(chunk >= 2)
            def _():
                raw_copy(chunk - 2).wait()

            def tile(at):
                raw = reduce.raw[at]
                raw_buf[lax.rem(chunk, 2), at] = raw.astype(LOW)
                squares = jnp.sum(raw * raw, axis=1, keepdims=True)
                stats.put(chunk, at, squares, squares)

            tiles(rows, tile)
            stats.copy(chunk).start()
            raw_copy(chunk).start()

        def finish(chunk):
            slot = lax.rem(chunk, 2)
            for item in token_copies(chunk):
                item.wait()
            stats.copy(chunk).wait_recv()
            spread.clear(chunk)

            @pl.when(chunk >= 2)
            def _():
                mixed_copy(chunk - 2).wait()

            def tile(at):
                squares, _ = stats.get(chunk, at)
                factor = lax.rsqrt(squares / D + EPS)
                mixed = token_buf[at].astype(WIDE) + reduce.raw[at] * factor * gain[...]
                mixed_buf[slot, at] = mixed
                spread.put(chunk, at, mixed)

            tiles(rows, tile)
            spread.go(chunk)
            mixed_copy(chunk).start()

        schedule(chunks, reduce, multiply, fetch, sums, finish, ring.event, ring.events, prepare)
        def drain(chunk):
            for item in crossings(chunk):
                item.wait()

        loop(chunks, drain)
        up_spill.start()
        ring.end()
        up_spill.wait()
        ring.settle()
        reduce.end(chunks)
        stats.end(chunks)
        spread.end(chunks)
        for chunk in (chunks - 2, chunks - 1):
            mixed_copy(chunk).wait()
            raw_copy(chunk).wait()

    shape = jax.ShapeDtypeStruct
    out = pl.pallas_call(
        kernel,
        out_shape=[
            shape((length, half), LOW),
            shape((length, width), WIDE),
            shape((2 * chips, length, width), LOW),
            shape((shard * count, hidden), LOW),
            shape((shard * count, hidden), LOW),
            shape((count, inner, down_columns), LOW),
            shape((chips, length, width), LOW),
        ]
        + Reduce.landing(rows, chunks, width, False),
        in_specs=[VMEM, VMEM, VMEM, HBM, HBM, HBM, HBM, HBM],
        out_specs=[HBM] * 8,
        scratch_shapes=[item for group in groups for item in group],
        compiler_params=pltpu.CompilerParams(
            collective_id=collective, has_side_effects=True, vmem_limit_bytes=60 * MIB
        ),
        cost_estimate=pl.CostEstimate(
            flops=2 * length * width * D, bytes_accessed=8 * length * D, transcendentals=0
        ),
    )(attended, weight, gain, tokens, out_grad, gate_shard, up_shard, down_shard)
    return out[:7]


def mlp_forward(
    inputs, gate_full, up_full, down_first, down_second, gain, mixed, upstream, collective
):
    length, inner = inputs.shape[1], gate_full.shape[1]
    width = mixed.shape[1]
    ranks = inputs.shape[0]
    down_columns = down_first.shape[2]
    down_rows = down_first.shape[1]
    chips = lax.axis_size("gx") // 2
    half = chips * width
    chunks = lax.axis_size("gy")
    rows = length // chunks
    tile = min(512, inner)
    pieces = inner // tile

    groups = [
        Reduce.scratch(rows, chunks, width, False),
        Stats.scratch(rows, chunks),
        Spread.scratch(rows, chunks, width),
        [
            pltpu.VMEM((2, rows, half), LOW),
            pltpu.VMEM((rows, width), WIDE),
            pltpu.VMEM((2, rows, width), LOW),
            pltpu.SemaphoreType.DMA((2, chips)),
            pltpu.SemaphoreType.DMA((1,)),
            pltpu.SemaphoreType.DMA((2,)),
        ],
        [
            pltpu.VMEM((D, inner), LOW),
            pltpu.VMEM((D, inner), LOW),
            pltpu.VMEM((inner, D), LOW),
            pltpu.VMEM((2, rows, D), LOW),
            pltpu.VMEM((2, 3, rows, inner), LOW),
            pltpu.SemaphoreType.DMA((pieces, 2)),
            pltpu.SemaphoreType.DMA((2, chunks)),
            pltpu.SemaphoreType.DMA((2, ranks)),
            pltpu.SemaphoreType.DMA((2, 3)),
        ],
    ]

    def kernel(*refs):
        ins, outs, *scratch = take(refs, [8, 7] + [len(g) for g in groups])
        inputs, gate_full, up_full, down_first, down_second, gain, mixed, upstream = ins
        result, grad_out, gain_grad, hidden_out, silu_out, slope_out, cross_land = outs
        gate_weight, up_weight, weight, row_buf, made = scratch[4][:5]
        piece_sems, weight_sem, row_sems, made_sems = scratch[4][5:]
        reduce = Reduce(scratch[0], cross_land, rows, width, False)
        stats = Stats(*scratch[1])
        buffer, local, send, recv = scratch[2]
        spread = Spread(buffer, grad_out, local, send, recv, rows, width)
        up_buf, mixed_buf, result_buf, up_sems, mixed_sems, result_sems = scratch[3]

        def piece_copies(piece):
            at = pl.ds(aligned(piece * tile, tile), tile)
            return [
                pltpu.make_async_copy(gate_full.at[:, at], gate_weight.at[:, at], piece_sems.at[piece, 0]),
                pltpu.make_async_copy(up_full.at[:, at], up_weight.at[:, at], piece_sems.at[piece, 1]),
            ]

        weight_copies = all_blocks(
            down_first, None, down_columns, weight.at[:down_rows], weight_sem.at[0]
        ) + all_blocks(down_second, None, down_columns, weight.at[down_rows:], weight_sem.at[1])

        def row_copy(chunk):
            slot = lax.rem(chunk, 2)
            return all_blocks(
                inputs, row_slice(chunk, rows), width, row_buf.at[slot], row_sems.at[slot]
            )

        def stores(chunk):
            slot, at = lax.rem(chunk, 2), row_slice(chunk, rows)
            return [
                pltpu.make_async_copy(made.at[slot, which], out.at[at], made_sems.at[slot, which])
                for which, out in enumerate((hidden_out, silu_out, slope_out))
            ]

        for item in row_copy(0):
            item.start()
        for piece in range(pieces):
            for item in piece_copies(piece):
                item.start()
        for item in weight_copies:
            item.start()
        greet(True, False)
        gain_grad[...] = jnp.zeros_like(gain_grad)

        def prepare(chunk):
            slot = lax.rem(chunk, 2)
            for item in row_copy(chunk):
                item.wait()

            @pl.when(chunk + 1 < chunks)
            def _():
                for item in row_copy(chunk + 1):
                    item.start()

            @pl.when(chunk >= 2)
            def _():
                for item in stores(chunk - 2):
                    item.wait()

            @pl.loop(0, pieces)
            def _(piece):
                @pl.when(chunk == 0)
                def _():
                    for item in piece_copies(piece):
                        item.wait()

                at = pl.ds(aligned(piece * tile, tile), tile)
                gate = jnp.dot(row_buf[slot], gate_weight[:, at], preferred_element_type=WIDE)
                up = jnp.dot(row_buf[slot], up_weight[:, at], preferred_element_type=WIDE)
                sigma = jax.nn.sigmoid(gate)
                silu = gate * sigma
                made[slot, 0, :, at] = (silu * up).astype(LOW)
                made[slot, 1, :, at] = silu.astype(LOW)
                made[slot, 2, :, at] = (up * (sigma + silu * (1.0 - sigma))).astype(LOW)

            @pl.when(chunk == 0)
            def _():
                for item in weight_copies:
                    item.wait()

            for item in stores(chunk):
                item.start()

        def multiply(chunk, place):
            return jnp.dot(
                made[lax.rem(chunk, 2), 0],
                weight[:, pl.ds(place, width)],
                preferred_element_type=WIDE,
            )

        def up_copy(chunk):
            slot = lax.rem(chunk, 2)
            return all_blocks(
                upstream, row_slice(chunk, rows), width, up_buf.at[slot], up_sems.at[slot]
            )

        def mixed_copy(chunk):
            return pltpu.make_async_copy(
                mixed.at[row_slice(chunk, rows)], mixed_buf, mixed_sems.at[0]
            )

        def result_copy(chunk):
            slot = lax.rem(chunk, 2)
            return pltpu.make_async_copy(
                result_buf.at[slot], result.at[row_slice(chunk, rows)], result_sems.at[slot]
            )

        def fetch(chunk):
            @pl.when(chunk < chunks)
            def _():
                for item in up_copy(chunk):
                    item.start()

            @pl.when(chunk >= 1)
            def _():
                mixed_copy(chunk - 1).start()

        def sums(chunk):
            slot = lax.rem(chunk, 2)
            stats.clear(chunk)
            for item in up_copy(chunk):
                item.wait()

            def tile(at):
                raw = reduce.raw[at]
                up = up_buf[slot, at].astype(WIDE)
                squares = jnp.sum(raw * raw, axis=1, keepdims=True)
                projected = jnp.sum(gain[...] * up * raw, axis=1, keepdims=True)
                stats.put(chunk, at, squares, projected)

            tiles(rows, tile)
            stats.copy(chunk).start()

        def finish(chunk):
            slot = lax.rem(chunk, 2)
            mixed_copy(chunk).wait()
            stats.copy(chunk).wait_recv()
            spread.clear(chunk)

            @pl.when(chunk >= 2)
            def _():
                result_copy(chunk - 2).wait()

            block = pl.ds(aligned(chip_here() * width, width), width)

            def tile(at):
                squares, projected = stats.get(chunk, at)
                factor = lax.rsqrt(squares / D + EPS)
                raw = reduce.raw[at]
                up = up_buf[slot, at].astype(WIDE)
                pull = factor * factor * factor * projected / D
                spread.put(chunk, at, factor * gain[...] * up - raw * pull)
                gain_grad[...] += jnp.sum(up * raw * factor, axis=0, keepdims=True)
                result_buf[slot, at] = (
                    mixed_buf[at] + reduce.raw[at, block] * factor * gain[:, block]
                ).astype(LOW)

            tiles(rows, tile)
            spread.go(chunk)
            result_copy(chunk).start()

        schedule(chunks, reduce, multiply, fetch, sums, finish, prepare=prepare)
        reduce.end(chunks)
        stats.end(chunks)
        spread.end(chunks)
        for chunk in (chunks - 2, chunks - 1):
            result_copy(chunk).wait()
            for item in stores(chunk):
                item.wait()

    shape = jax.ShapeDtypeStruct
    out = pl.pallas_call(
        kernel,
        out_shape=[
            shape((length, width), LOW),
            shape((2 * chips, length, width), LOW),
            shape((1, half), WIDE),
            shape((length, inner), LOW),
            shape((length, inner), LOW),
            shape((length, inner), LOW),
        ]
        + Reduce.landing(rows, chunks, width, False),
        in_specs=[HBM] * 5 + [VMEM, HBM, HBM],
        out_specs=[HBM, HBM, VMEM] + [HBM] * 4,
        scratch_shapes=[item for group in groups for item in group],
        compiler_params=pltpu.CompilerParams(
            collective_id=collective, has_side_effects=True, vmem_limit_bytes=60 * MIB
        ),
        cost_estimate=pl.CostEstimate(
            flops=6 * length * inner * D, bytes_accessed=16 * length * D, transcendentals=0
        ),
    )(inputs, gate_full, up_full, down_first, down_second, gain, mixed, upstream)
    return out[:6]


def mlp_back(gate_grad, up_grad, gate_full, up_full, inputs, gain, upstream, attn_raw, collective):
    length, inner = gate_grad.shape
    half = attn_raw.shape[1]
    chips = lax.axis_size("gx") // 2
    width = half // chips
    count = lax.axis_size("gy")
    chunks = count
    rows = length // chunks
    shard = D // count
    slots, parts = 2, 4
    piece = inner // parts

    groups = [
        Reduce.scratch(rows, chunks, width, False),
        Stats.scratch(rows, chunks),
        Spread.scratch(rows, chunks, width),
        RingScatter.scratch(shard, inner, slots, parts),
        [
            pltpu.VMEM((rows, half), LOW),
            pltpu.VMEM((2, rows, half), LOW),
            pltpu.SemaphoreType.DMA((chips,)),
            pltpu.SemaphoreType.DMA((2,)),
            pltpu.SemaphoreType.DMA((1,)),
            pltpu.SemaphoreType.DMA((2, parts)),
        ],
        Columns.scratch(length, shard),
        [
            pltpu.VMEM((2, length, inner), LOW),
            pltpu.VMEM((2, D, inner), LOW),
            pltpu.SemaphoreType.DMA((2, 2)),
        ],
    ]

    def kernel(*refs):
        ins, outs, *scratch = take(refs, [8, 6] + [len(g) for g in groups])
        gate_grad, up_grad, gate_full, up_full, inputs, gain, upstream, attn_raw = ins
        grads, weights, load_sems = scratch[6]
        grad_copies = [
            pltpu.make_async_copy((gate_grad, up_grad)[way], grads.at[way], load_sems.at[0, way])
            for way in range(2)
        ]
        weight_copies = [
            pltpu.make_async_copy((gate_full, up_full)[way], weights.at[way], load_sems.at[1, way])
            for way in range(2)
        ]
        mixed_out, grad_out, gain_grad, gate_out, up_out, cross_land = outs
        reduce = Reduce(scratch[0], cross_land, rows, width, False)
        stats = Stats(*scratch[1])
        buffer, local, send, recv = scratch[2]
        spread = Spread(buffer, grad_out, local, send, recv, rows, width)
        total, summed, land, ring_send, ring_recv, credit = scratch[3]
        up_buf, raw_buf, up_sems, raw_sems, mixed_sems, out_sems = scratch[4]
        left = Columns(inputs, shard, *scratch[5])

        def product(way, step, part):
            @pl.when(part == 0)
            def _():
                left.take(ring, way, step)

            @pl.when((part == 0) & (step == 0))
            def _():
                grad_copies[way].wait()

            columns = pl.ds(aligned(part * piece, piece), piece)
            total[way, part] = jnp.dot(
                left.turned[way], grads[way, :, columns], preferred_element_type=WIDE
            )

        ring = RingScatter(
            product, total, summed, land, ring_send, ring_recv, credit, slots, parts
        )
        left.copy(ring.owner(0, 0)).start()
        for item in grad_copies + weight_copies:
            item.start()
        greet(True, True)
        gain_grad[...] = jnp.zeros_like(gain_grad)

        def prepare(chunk):
            @pl.when(chunk == 0)
            def _():
                for item in weight_copies:
                    item.wait()

        def multiply(chunk, place):
            at = row_slice(chunk, rows)
            return nt(grads[0, at], weights[0, pl.ds(place, width)]) + nt(
                grads[1, at], weights[1, pl.ds(place, width)]
            )

        def up_copy(chunk):
            return all_blocks(upstream, row_slice(chunk, rows), width, up_buf, up_sems)

        def raw_copy(chunk):
            slot = lax.rem(chunk, 2)
            return pltpu.make_async_copy(
                attn_raw.at[row_slice(chunk, rows)], raw_buf.at[slot], raw_sems.at[slot]
            )

        def mixed_copy(chunk):
            return pltpu.make_async_copy(
                reduce.raw.at[:, pl.ds(aligned(chip_here() * width, width), width)],
                mixed_out.at[row_slice(chunk, rows)],
                mixed_sems.at[0],
            )

        def fetch(chunk):
            @pl.when(chunk < chunks)
            def _():
                for item in up_copy(chunk):
                    item.start()
                raw_copy(chunk).start()

        def sums(chunk):
            slot = lax.rem(chunk, 2)
            stats.clear(chunk)
            for item in up_copy(chunk):
                item.wait()
            raw_copy(chunk).wait()

            def tile(at):
                upward = reduce.raw[at] + up_buf[at].astype(WIDE)
                reduce.raw[at] = upward
                raw = raw_buf[slot, at].astype(WIDE)
                squares = jnp.sum(raw * raw, axis=1, keepdims=True)
                projected = jnp.sum(gain[...] * upward * raw, axis=1, keepdims=True)
                stats.put(chunk, at, squares, projected)

            tiles(rows, tile)
            stats.copy(chunk).start()
            mixed_copy(chunk).start()

        def finish(chunk):
            slot = lax.rem(chunk, 2)
            stats.copy(chunk).wait_recv()
            spread.clear(chunk)

            def tile(at):
                squares, projected = stats.get(chunk, at)
                factor = lax.rsqrt(squares / D + EPS)
                upward = reduce.raw[at]
                raw = raw_buf[slot, at].astype(WIDE)
                pull = factor * factor * factor * projected / D
                spread.put(chunk, at, factor * gain[...] * upward - raw * pull)
                gain_grad[...] += jnp.sum(upward * raw * factor, axis=0, keepdims=True)

            tiles(rows, tile)
            spread.go(chunk)
            mixed_copy(chunk).wait()

        schedule(chunks, reduce, multiply, fetch, sums, finish, ring.event, ring.events, prepare)
        writes = [
            pltpu.make_async_copy(
                total.at[way, part],
                (gate_out, up_out)[way].at[:, part * piece : (part + 1) * piece],
                out_sems.at[way, part],
            )
            for way in range(2)
            for part in range(parts)
        ]
        for item in writes:
            item.start()
        ring.end()
        reduce.end(chunks)
        stats.end(chunks)
        spread.end(chunks)
        for item in writes:
            item.wait()

    shape = jax.ShapeDtypeStruct
    out = pl.pallas_call(
        kernel,
        out_shape=[
            shape((length, width), WIDE),
            shape((length, D), LOW),
            shape((1, half), WIDE),
            shape((shard, inner), WIDE),
            shape((shard, inner), WIDE),
        ]
        + Reduce.landing(rows, chunks, width, False),
        in_specs=[HBM, HBM, HBM, HBM, HBM, VMEM, HBM, HBM],
        out_specs=[HBM, HBM, VMEM, HBM, HBM, HBM],
        scratch_shapes=[item for group in groups for item in group],
        compiler_params=pltpu.CompilerParams(
            collective_id=collective, has_side_effects=True, vmem_limit_bytes=60 * MIB
        ),
        cost_estimate=pl.CostEstimate(
            flops=8 * length * inner * D, bytes_accessed=16 * length * D, transcendentals=0
        ),
    )(gate_grad, up_grad, gate_full, up_full, inputs, gain, upstream, attn_raw)
    return out[:5]


class Total:
    def __init__(self, land, send, recv):
        self.land, self.send, self.recv = land, send, recv
        self.count = lax.axis_size("gx")

    @staticmethod
    def scratch(length):
        others = lax.axis_size("gx") - 1
        return [
            pltpu.VMEM((others, 8, length), WIDE),
            pltpu.SemaphoreType.DMA((others,)),
            pltpu.SemaphoreType.DMA((others,)),
        ]

    def copies(self, mine):
        return [
            remote(
                mine,
                self.land.at[shift - 1],
                self.send.at[shift - 1],
                self.recv.at[shift - 1],
                {"gx": rank_at(shift)},
            )
            for shift in range(1, self.count)
        ]

    def start(self, mine):
        for item in self.copies(mine):
            item.start()

    def finish(self, mine):
        for item in self.copies(mine):
            item.wait()
        total = mine[...]
        for shift in range(1, self.count):
            total = total + self.land[shift - 1]
        return total


def gather_in(tokens, stack, output_shard, gains, collective):
    length, width = tokens.shape
    _, shard, side = stack.shape
    columns = 2 * side
    count = lax.axis_size("gy")
    chunks = count
    rows = length // chunks
    chips = lax.axis_size("gx") // 2
    parts = 1
    out_columns = output_shard.shape[1]
    out_rows = width // 2

    groups = [
        RingGather.scratch(parts),
        [
            pltpu.SemaphoreType.DMA((1,)),
            pltpu.SemaphoreType.DMA((2,)),
            pltpu.SemaphoreType.DMA((chips - 1, chunks, 2)),
            pltpu.SemaphoreType.DMA((chips - 1, chunks, 2)),
        ],
        [
            pltpu.VMEM((2, D, side), LOW),
            pltpu.VMEM((2 * chips, length, width), LOW),
            pltpu.VMEM((2, 2, rows, width), WIDE),
            pltpu.VMEM((2, rows, width), LOW),
            pltpu.VMEM((length, STATS), WIDE),
            pltpu.VMEM((8, length), WIDE),
            pltpu.SemaphoreType.DMA((2,)),
            pltpu.SemaphoreType.DMA((2, 3)),
        ],
        Total.scratch(length),
        [
            pltpu.VMEM((chips - 1, 8, width), WIDE),
            pltpu.SemaphoreType.DMA((chips - 1, 2)),
        ],
        RingGather.scratch(1),
        [pltpu.VMEM((count, width, out_columns), LOW)],
    ]

    def kernel(*refs):
        ins, outs, *scratch = take(refs, [4, 8] + [len(g) for g in groups])
        tokens, stack, output_shard, gains = ins
        whole, full, output_full, query_raw, key_raw, values, squares, halves = outs
        out_held = scratch[6][0]
        gain_land, gain_sems = scratch[4]
        own_sem, core_sems, cross_sems, pass_sems = scratch[1]
        weight, held, raw_buf, value_buf, stats, mine = scratch[2][:6]
        copy_sems, out_sems = scratch[2][6:]
        total = Total(*scratch[3])

        def slot(way, owner, part):
            return weight.at[way, pl.ds(aligned(owner * shard, shard), shard)]

        def spill(way, owner, part):
            return full.at[way, pl.ds(aligned(owner * shard, shard), shard)]

        def source(way, part):
            return stack.at[way]

        ring = RingGather(source, slot, spill, parts, *scratch[0])

        def out_slot(way, owner, part):
            return out_held.at[owner, way * out_rows : (way + 1) * out_rows]

        def out_spill(way, owner, part):
            at = pl.ds(aligned(owner * out_columns, out_columns), out_columns)
            return output_full.at[way * out_rows : (way + 1) * out_rows, at]

        def out_source(way, part):
            return output_shard.at[way * out_rows : (way + 1) * out_rows]

        out_ring = RingGather(out_source, out_slot, out_spill, 1, *scratch[5])

        def block(rank, chunk):
            if chunk is None:
                return held.at[rank]
            return held.at[rank, row_slice(chunk, rows)]

        here = lax.axis_index("gx")
        own = pltpu.make_async_copy(tokens, block(here, None), own_sem.at[0])
        core = remote(
            block(here, None), block(here, None), core_sems.at[0], core_sems.at[1], {"gx": other_core()}
        )

        def cross(shift, chunk):
            return remote(
                block(here, chunk),
                block(here, chunk),
                cross_sems.at[shift - 1, chunk, 0],
                cross_sems.at[shift - 1, chunk, 1],
                {"gx": peer_at(shift)},
            )

        def onward(shift, chunk):
            spot = block(peer_at(chips - shift), chunk)
            return remote(
                spot,
                spot,
                pass_sems.at[shift - 1, chunk, 0],
                pass_sems.at[shift - 1, chunk, 1],
                {"gx": other_core()},
            )

        gain_copies = [
            remote(
                gains,
                gain_land.at[shift - 1],
                gain_sems.at[shift - 1, 0],
                gain_sems.at[shift - 1, 1],
                {"gx": peer_at(shift)},
            )
            for shift in range(1, chips)
        ]
        own.start()
        greet("all", True)
        for item in gain_copies:
            item.start()
        ring.begin()
        own.wait()

        def send(chunk):
            for shift in range(1, chips):
                cross(shift, chunk).start()

        loop(chunks, send)
        core.start()

        def step(chunk):
            for shift in range(1, chips):
                cross(shift, chunk).wait_recv()
                onward(shift, chunk).start()

            @pl.when(chunk < ring.events)
            def _():
                ring.event(chunk)

        loop(chunks, step)
        out_ring.begin()
        ring.end()

        def drain(chunk):
            for shift in range(1, chips):
                cross(shift, chunk).wait_send()
                onward(shift, chunk).wait()

        loop(chunks, drain)
        core.wait()
        whole_copy = pltpu.make_async_copy(held, whole, copy_sems.at[0])
        whole_copy.start()

        def stores(chunk):
            slot, at = lax.rem(chunk, 2), row_slice(chunk, rows)
            return [
                pltpu.make_async_copy(raw_buf.at[slot, 0], query_raw.at[at], out_sems.at[slot, 0]),
                pltpu.make_async_copy(raw_buf.at[slot, 1], key_raw.at[at], out_sems.at[slot, 1]),
                pltpu.make_async_copy(value_buf.at[slot], values.at[at], out_sems.at[slot, 2]),
            ]

        lane = lax.broadcasted_iota(jnp.int32, (rows, STATS), 1)

        def project(chunk):
            slot = lax.rem(chunk, 2)
            @pl.when(chunk >= 2)
            def _():
                for item in stores(chunk - 2):
                    item.wait()

            at = row_slice(chunk, rows)
            middle = side - width

            def against(way, columns):
                raw = jnp.zeros((rows, columns.stop - columns.start), WIDE)
                for rank in range(2 * chips):
                    raw = raw + jnp.dot(
                        held[rank, at],
                        weight[way, rank * width : (rank + 1) * width, columns],
                        preferred_element_type=WIDE,
                    )
                return raw

            some = []
            raw_buf[slot, 0] = against(0, slice(0, width))
            raw_buf[slot, 1, :, :middle] = against(0, slice(width, side))
            raw_buf[slot, 1, :, middle:] = against(1, slice(0, middle))
            value_buf[slot] = against(1, slice(middle, side)).astype(LOW)
            for which in range(2):
                raw = raw_buf[slot, which]
                some.append(jnp.sum(raw * raw, axis=1, keepdims=True))
            stats[row_slice(chunk, rows)] = jnp.where(lane == 0, some[0], some[1])
            for item in stores(chunk):
                item.start()

            @pl.when(chunk < out_ring.events)
            def _():
                out_ring.event(chunk)

        loop(chunks, project)
        mine[...] = stats[...].T[:8]
        total.start(mine)
        for chunk in (chunks - 2, chunks - 1):
            for item in stores(chunk):
                item.wait()
        squares[...] = total.finish(mine)
        whole_copy.wait()
        ring.settle()
        out_ring.end()
        out_ring.settle()
        halves[:, pl.ds(aligned(chip_here() * width, width), width)] = gains[...]
        for shift in range(1, chips):
            gain_copies[shift - 1].wait()
            chip = lax.rem(chip_here() + chips - shift, chips)
            halves[:, pl.ds(aligned(chip * width, width), width)] = gain_land[shift - 1]

    shape = jax.ShapeDtypeStruct
    return pl.pallas_call(
        kernel,
        out_shape=[
            shape((2 * chips, length, width), LOW),
            shape((2, shard * count, side), LOW),
            shape((width, D), LOW),
            shape((length, width), WIDE),
            shape((length, width), WIDE),
            shape((length, width), LOW),
            shape((8, length), WIDE),
            shape((8, chips * width), WIDE),
        ],
        in_specs=[HBM, HBM, HBM, VMEM],
        out_specs=[HBM] * 6 + [VMEM, VMEM],
        scratch_shapes=[item for group in groups for item in group],
        compiler_params=pltpu.CompilerParams(
            collective_id=collective, has_side_effects=True, vmem_limit_bytes=40 * MIB
        ),
        cost_estimate=pl.CostEstimate(
            flops=2 * length * columns * D, bytes_accessed=8 * length * D, transcendentals=0
        ),
    )(tokens, stack, output_shard, gains)


def hidden_back(blocks, down_first, down_second, hidden, silu, slope, collective):
    length, inner = hidden.shape
    count = lax.axis_size("gy")
    chunks = count
    rows = length // chunks
    shard = D // count
    side = inner // 2
    slots, parts = 3, 4
    piece = side // parts
    down_rows = down_first.shape[1]
    tile = min(512, inner)

    groups = [
        RingScatter.scratch(shard, side, slots, parts),
        [
            pltpu.VMEM((2, 2, rows, inner), LOW),
            pltpu.VMEM((2, 2, rows, inner), LOW),
            pltpu.SemaphoreType.DMA((2, 2)),
            pltpu.SemaphoreType.DMA((2, 2)),
            pltpu.SemaphoreType.DMA((2, parts)),
            pltpu.VMEM((count, shard, length), LOW),
        ],
        [
            pltpu.VMEM((length, D), LOW),
            pltpu.VMEM((inner, D), LOW),
            pltpu.SemaphoreType.DMA((blocks.shape[0],)),
            pltpu.SemaphoreType.DMA((2, count)),
        ],
    ]

    def kernel(*refs):
        ins, outs, *scratch = take(refs, [6, 3] + [len(g) for g in groups])
        blocks, down_first, down_second, hidden, silu, slope = ins
        grad, weight, grad_sems, weight_sems = scratch[2]
        gate_grad, up_grad, weight_grad = outs
        total, summed, land, ring_send, ring_recv, credit = scratch[0]
        given, made, given_sems, made_sems, out_sems, turned = scratch[1]

        def product(way, step, part):
            owner = ring.owner(way, step)

            @pl.when((part == 0) & ((step < count // 2) | (step == count - 1)))
            def _():
                turned[owner] = grad[:, pl.ds(aligned(owner * shard, shard), shard)].T

            columns = pl.ds(aligned(way * side + part * piece, piece), piece)
            total[way, part] = jnp.dot(
                turned[owner], hidden[:, columns], preferred_element_type=WIDE
            )

        ring = RingScatter(
            product, total, summed, land, ring_send, ring_recv, credit, slots, parts
        )

        def load(chunk):
            slot = lax.rem(chunk, 2)
            return [
                pltpu.make_async_copy(
                    (slope, silu)[which].at[row_slice(chunk, rows)],
                    given.at[slot, which],
                    given_sems.at[slot, which],
                )
                for which in range(2)
            ]

        def store(chunk):
            slot = lax.rem(chunk, 2)
            return [
                pltpu.make_async_copy(
                    made.at[slot, which],
                    (gate_grad, up_grad)[which].at[row_slice(chunk, rows)],
                    made_sems.at[slot, which],
                )
                for which in range(2)
            ]

        grad_copies = all_blocks(blocks, None, blocks.shape[2], grad, grad_sems)
        weight_copies = all_blocks(
            down_first, None, shard, weight.at[:down_rows], weight_sems.at[0]
        ) + all_blocks(down_second, None, shard, weight.at[down_rows:], weight_sems.at[1])
        for item in grad_copies + weight_copies + load(0):
            item.start()
        greet(False, True)
        for item in grad_copies:
            item.wait()

        def iteration(step):
            slot = lax.rem(step, 2)
            @pl.when(step + 1 < chunks)
            def _():
                for item in load(step + 1):
                    item.start()

            @pl.when(step >= 2)
            def _():
                for item in store(step - 2):
                    item.wait()

            for item in load(step):
                item.wait()

            each = parts // (inner // tile)

            @pl.loop(0, inner // tile)
            def _(index):
                for which in range(each):
                    ring.event(step * parts + index * each + which)

                @pl.when((step == 0) & (index == 0))
                def _():
                    for item in weight_copies:
                        item.wait()

                at = pl.ds(aligned(index * tile, tile), tile)
                hidden_grad = nt(grad[row_slice(step, rows)], weight[at])
                for which in range(2):
                    made[slot, which, :, at] = (
                        hidden_grad * given[slot, which, :, at].astype(WIDE)
                    ).astype(LOW)

            for item in store(step):
                item.start()

        loop(chunks, iteration)
        writes = [
            pltpu.make_async_copy(
                total.at[way, part],
                weight_grad.at[:, way * side + part * piece : way * side + (part + 1) * piece],
                out_sems.at[way, part],
            )
            for way in range(2)
            for part in range(parts)
        ]
        for item in writes:
            item.start()
        for chunk in (chunks - 2, chunks - 1):
            for item in store(chunk):
                item.wait()
        ring.end()
        for item in writes:
            item.wait()

    shape = jax.ShapeDtypeStruct
    return pl.pallas_call(
        kernel,
        out_shape=[
            shape((length, inner), LOW),
            shape((length, inner), LOW),
            shape((shard, inner), WIDE),
        ],
        in_specs=[HBM, HBM, HBM, VMEM, HBM, HBM],
        out_specs=[HBM, HBM, HBM],
        scratch_shapes=[item for group in groups for item in group],
        compiler_params=pltpu.CompilerParams(
            collective_id=collective, has_side_effects=True, vmem_limit_bytes=60 * MIB
        ),
        cost_estimate=pl.CostEstimate(
            flops=4 * length * inner * D, bytes_accessed=16 * length * D, transcendentals=0
        ),
    )(blocks, down_first, down_second, hidden, silu, slope)


def attn_in_back(
    query_back,
    key_back,
    value_grad,
    query_raw,
    key_raw,
    factors,
    projections,
    query_gain,
    key_gain,
    stack,
    inputs,
    mixed_grad,
    gain_parts,
    collective,
):
    length, columns = value_grad.shape[0], 2 * stack.shape[2]
    width = mixed_grad.shape[1]
    count = lax.axis_size("gy")
    chunks = count
    rows = length // chunks
    shard = D // count
    side = columns // 2
    slots, parts = count - 1, 3
    piece = side // parts

    groups = [
        Reduce.scratch(rows, chunks, width, True),
        RingScatter.scratch(shard, side, slots, parts),
        [
            pltpu.VMEM((rows, width), WIDE),
            pltpu.VMEM((2, rows, width), WIDE),
            pltpu.VMEM((length, columns), LOW),
            pltpu.VMEM((length, STATS), WIDE),
            pltpu.VMEM((2, 4, rows, width), WIDE),
            pltpu.VMEM((2, D, side), LOW),
            pltpu.SemaphoreType.DMA((2, 4)),
            pltpu.SemaphoreType.DMA((2,)),
            pltpu.SemaphoreType.DMA((1,)),
            pltpu.SemaphoreType.DMA((2,)),
            pltpu.SemaphoreType.DMA((2, parts)),
        ],
        Columns.scratch(length, shard),
        Total.scratch(length),
        [
            pltpu.VMEM((8, width), WIDE),
            pltpu.VMEM((count - 1, 8, width), WIDE),
            pltpu.SemaphoreType.DMA((count - 1, 2)),
        ],
    ]

    def kernel(*refs):
        ins, outs, *scratch = take(refs, [16, 4] + [len(g) for g in groups])
        query_back, key_back, value_grad, query_raw, key_raw, factors = ins[:6]
        projections, query_gain, key_gain, full, inputs, mixed_grad = ins[6:12]
        gain_parts = ins[12:]
        token_grad, weight_grad, gain_grads, cross_land = outs
        gain_mine, gain_land, gain_sems = scratch[5]
        reduce = Reduce(scratch[0], cross_land, rows, width, True)
        total, summed, land, ring_send, ring_recv, credit = scratch[1]
        mixed_buf, token_buf, grads, projected, given, stack = scratch[2][:6]
        given_sems, whole_sems, mixed_sems, token_sems, out_sems = scratch[2][6:]
        left = Columns(inputs, shard, *scratch[3])
        total_sum = Total(*scratch[4])

        def product(way, step, part):
            @pl.when(part == 0)
            def _():
                left.take(ring, way, step)

            columns = pl.ds(aligned(way * side + part * piece, piece), piece)
            total[way, part] = jnp.dot(
                left.turned[way], grads[:, columns], preferred_element_type=WIDE
            )

        ring = RingScatter(
            product, total, summed, land, ring_send, ring_recv, credit, slots, parts
        )
        def load(chunk):
            slot, at = lax.rem(chunk, 2), row_slice(chunk, rows)
            return [
                pltpu.make_async_copy(
                    source.at[at], given.at[slot, which], given_sems.at[slot, which]
                )
                for which, source in enumerate((query_back, key_back, query_raw, key_raw))
            ]

        value_copy = pltpu.make_async_copy(value_grad, grads.at[:, 2 * width :], whole_sems.at[0])
        stack_copy = pltpu.make_async_copy(full, stack, whole_sems.at[1])
        left.copy(ring.owner(0, 0)).start()
        for item in load(0):
            item.start()
        value_copy.start()
        stack_copy.start()
        chip_columns = pl.ds(aligned(chip_here() * width, width), width)
        gain_mine[...] = jnp.zeros_like(gain_mine)
        for which, part in enumerate(gain_parts):
            gain_mine[which : which + 1] = part[...] if which < 2 else part[:, chip_columns]
        greet("all", False, True)
        total_sum.start(projections)
        gain_copies = [
            remote(
                gain_mine,
                gain_land.at[shift - 1],
                gain_sems.at[shift - 1, 0],
                gain_sems.at[shift - 1, 1],
                {"gy": block_at(shift)},
            )
            for shift in range(1, count)
        ]
        for item in gain_copies:
            item.start()
        sums_here = total_sum.finish(projections)
        projected[...] = jnp.concatenate([sums_here] * (STATS // 8), axis=0).T

        def form(chunk):
            slot = lax.rem(chunk, 2)

            @pl.when(chunk + 1 < chunks)
            def _():
                for item in load(chunk + 1):
                    item.start()

            for item in load(chunk):
                item.wait()

            def some(part):
                at = pl.ds(aligned(chunk * rows + part.start, 32), 32)
                for which, gain in enumerate((query_gain, key_gain)):
                    factor = factors[at, which : which + 1]
                    pull = factor * factor * factor * projected[at, which : which + 1] / D
                    back, raw = given[slot, which, part], given[slot, which + 2, part]
                    grads[at, which * width : (which + 1) * width] = (
                        factor * gain[...] * back - raw * pull
                    ).astype(LOW)

            tiles(rows, some)

        loop(chunks, form)
        value_copy.wait()

        def prepare(chunk):
            @pl.when(chunk == 0)
            def _():
                stack_copy.wait()

        def multiply(chunk, place):
            at = row_slice(chunk, rows)
            return nt(grads[at, :side], stack[0, pl.ds(place, width)]) + nt(
                grads[at, side:], stack[1, pl.ds(place, width)]
            )

        def mixed_copy(chunk):
            return pltpu.make_async_copy(
                mixed_grad.at[row_slice(chunk, rows)], mixed_buf, mixed_sems.at[0]
            )

        def token_copy(chunk):
            slot = lax.rem(chunk, 2)
            return pltpu.make_async_copy(
                token_buf.at[slot], token_grad.at[row_slice(chunk, rows)], token_sems.at[slot]
            )

        def fetch(chunk):
            @pl.when(chunk >= 1)
            def _():
                mixed_copy(chunk - 1).start()

        def sums(chunk):
            pass

        def finish(chunk):
            slot = lax.rem(chunk, 2)
            mixed_copy(chunk).wait()

            @pl.when(chunk >= 2)
            def _():
                token_copy(chunk - 2).wait()

            def some(at):
                token_buf[slot, at] = mixed_buf[at] + reduce.raw[at]

            tiles(rows, some)
            token_copy(chunk).start()

        schedule(chunks, reduce, multiply, fetch, sums, finish, ring.event, ring.events, prepare)
        writes = [
            pltpu.make_async_copy(
                total.at[way, part],
                weight_grad.at[:, way * side + part * piece : way * side + (part + 1) * piece],
                out_sems.at[way, part],
            )
            for way in range(2)
            for part in range(parts)
        ]
        for item in writes:
            item.start()
        gain_total = gain_mine[...]
        for shift in range(1, count):
            gain_copies[shift - 1].wait()
            gain_total = gain_total + gain_land[shift - 1]
        gain_grads[...] = gain_total
        ring.end()
        reduce.end(chunks)
        for chunk in (chunks - 2, chunks - 1):
            token_copy(chunk).wait()
        for item in writes:
            item.wait()

    shape = jax.ShapeDtypeStruct
    out = pl.pallas_call(
        kernel,
        out_shape=[
            shape((length, width), WIDE),
            shape((shard, columns), WIDE),
            shape((8, width), WIDE),
        ]
        + Reduce.landing(rows, chunks, width, True),
        in_specs=[HBM] * 5 + [VMEM] * 4 + [HBM] * 3 + [VMEM] * 4,
        out_specs=[HBM, HBM, VMEM, HBM],
        scratch_shapes=[item for group in groups for item in group],
        compiler_params=pltpu.CompilerParams(
            collective_id=collective, has_side_effects=True, vmem_limit_bytes=60 * MIB
        ),
        cost_estimate=pl.CostEstimate(
            flops=4 * length * columns * D, bytes_accessed=8 * length * D, transcendentals=0
        ),
    )(
        query_back,
        key_back,
        value_grad,
        query_raw,
        key_raw,
        factors,
        projections,
        query_gain,
        key_gain,
        stack,
        inputs,
        mixed_grad,
        *gain_parts,
    )
    return out[:3]


def token_positions(segment):
    length = segment.shape[0]
    labels = jnp.arange(SEGS, dtype=jnp.int32)
    member = (segment[:, None] == labels[None, :]).astype(jnp.int32)
    totals = jnp.sum(member, axis=0)
    starts = jnp.cumsum(totals) - totals
    opening = jnp.sum(member * starts[None, :], axis=1)
    return jnp.arange(length, dtype=jnp.int32) - opening


def rotary_tables(segment):
    place = token_positions(segment).astype(jnp.float32)
    halves = HEAD // 2
    inverse = jnp.exp(jnp.arange(halves, dtype=jnp.float32) * (-2.0 * math.log(THETA) / HEAD))
    angle = place[:, None] * inverse[None, :]
    return (jnp.cos(angle), jnp.sin(angle))


BLOCK = 256
LANES = 128
SCALE = 1.0 / math.sqrt(HEAD)
SCALE_TWO = SCALE * math.log2(math.e)


def turn(values, cosine, sine):
    return values * cosine + pltpu.roll(values, HEAD // 2, 1) * sine


def head_columns(head):
    return slice(head * HEAD, (head + 1) * HEAD)


def nt(left, right):
    return lax.dot_general(left, right, (((1,), (1,)), ((), ())), preferred_element_type=WIDE)


def attend(first_block, query_raw, key_raw, values, factors, query_gain, key_gain, tables, starts):
    length, width = query_raw.shape
    heads = width // HEAD

    def kernel(
        first_block,
        query_raw,
        key_raw,
        values,
        factors,
        query_gain,
        key_gain,
        cosine,
        sine,
        starts,
        queries,
        keys,
        attended,
        peaks,
        peak_columns,
    ):
        @pl.loop(0, length // BLOCK)
        def _(index):
            at = row_slice(index, BLOCK)
            cos, sin = cosine[at], sine[at]
            pairs = ((query_raw, query_gain, queries), (key_raw, key_gain, keys))
            for which, (raw, gain, out) in enumerate(pairs):
                factor = factors[at, which : which + 1]
                for head in range(heads):
                    columns = head_columns(head)
                    normed = raw[at, columns] * factor * gain[:, columns]
                    out[at, columns] = turn(normed, cos, sin).astype(LOW)

        lane = lax.broadcasted_iota(jnp.int32, (BLOCK, LANES), 1)
        row_index = lax.broadcasted_iota(jnp.int32, (BLOCK, BLOCK), 0)
        column_index = lax.broadcasted_iota(jnp.int32, (BLOCK, BLOCK), 1)

        def query_block(index):
            at = row_slice(index, BLOCK)
            start = starts[at]

            def key_block(other, carry):
                there = row_slice(other, BLOCK)
                key_place = column_index + other * BLOCK
                allowed = (key_place >= start) & (key_place <= row_index + index * BLOCK)
                made = []
                for head in range(heads):
                    columns = head_columns(head)
                    peak, total, rows = carry[head]
                    scores = nt(queries[at, columns], keys[there, columns]) * SCALE_TWO
                    scores = jnp.where(allowed, scores, NEGATIVE)
                    higher = jnp.maximum(peak, jnp.max(scores, axis=1, keepdims=True))
                    raised = jnp.exp2(scores - higher)
                    shrink = jnp.exp2(peak - higher)
                    total = total * shrink + jnp.sum(raised, axis=1, keepdims=True)
                    rows = rows * shrink + jnp.dot(
                        raised.astype(LOW), values[there, columns], preferred_element_type=WIDE
                    )
                    made.append((higher, total, rows))
                return tuple(made)

            empty = (
                jnp.full((BLOCK, 1), NEGATIVE, WIDE),
                jnp.zeros((BLOCK, 1), WIDE),
                jnp.zeros((BLOCK, HEAD), WIDE),
            )
            done = lax.fori_loop(first_block[index], index + 1, key_block, (empty,) * heads)
            column = jnp.zeros((BLOCK, LANES), WIDE)
            for head in range(heads):
                peak, total, rows = done[head]
                attended[at, head_columns(head)] = (rows / total).astype(LOW)
                column = jnp.where(lane == head, peak + jnp.log2(total), column)
            peak_columns[at] = column

        loop(length // BLOCK, query_block)
        peaks[...] = peak_columns[...].T[:8]

    shape = jax.ShapeDtypeStruct
    smem = pl.BlockSpec(memory_space=pltpu.SMEM)
    return pl.pallas_call(
        kernel,
        out_shape=[
            shape((length, width), LOW),
            shape((length, width), LOW),
            shape((length, width), LOW),
            shape((8, length), WIDE),
        ],
        in_specs=[smem] + [VMEM] * 9,
        out_specs=[VMEM] * 4,
        scratch_shapes=[pltpu.VMEM((length, LANES), WIDE)],
        compiler_params=pltpu.CompilerParams(vmem_limit_bytes=48 * MIB),
        cost_estimate=pl.CostEstimate(
            flops=2 * length * MAX_LEN * width,
            bytes_accessed=16 * length * width,
            transcendentals=length * MAX_LEN * heads // 2,
        ),
    )(first_block, query_raw, key_raw, values, factors, query_gain, key_gain, *tables, starts)


def attend_back(
    last_block,
    queries,
    keys,
    values,
    attended,
    upstream,
    peaks,
    query_raw,
    key_raw,
    factors,
    query_gain,
    key_gain,
    tables,
    start_row,
):
    length, width = query_raw.shape
    heads = width // HEAD

    def kernel(
        last_block,
        queries,
        keys,
        values,
        attended,
        upstream,
        peaks,
        query_raw,
        key_raw,
        factors,
        query_gain,
        key_gain,
        cosine,
        sine,
        start_row,
        query_out,
        key_out,
        value_out,
        projections,
        query_gain_grad,
        key_gain_grad,
        query_sum,
        key_sum,
        value_sum,
        columns_scratch,
        deltas,
    ):
        lane = lax.broadcasted_iota(jnp.int32, (BLOCK, LANES), 1)
        query_gain_grad[...] = jnp.zeros_like(query_gain_grad)
        key_gain_grad[...] = jnp.zeros_like(key_gain_grad)

        def prepare(index):
            at = row_slice(index, BLOCK)
            column = jnp.zeros((BLOCK, LANES), WIDE)
            for head in range(heads):
                columns = head_columns(head)
                delta = jnp.sum(
                    attended[at, columns].astype(WIDE) * upstream[at, columns].astype(WIDE),
                    axis=1,
                    keepdims=True,
                )
                column = jnp.where(lane == head, delta, column)
            columns_scratch[at] = column
            query_sum[at] = jnp.zeros((BLOCK, width), WIDE)

        loop(length // BLOCK, prepare)
        deltas[...] = columns_scratch[...].T[:8]
        row_index = lax.broadcasted_iota(jnp.int32, (BLOCK, BLOCK), 0)
        column_index = lax.broadcasted_iota(jnp.int32, (BLOCK, BLOCK), 1)

        def turn_back(at, summed, raw, gain, factor, out, gain_grad):
            cos, sin = cosine[at], sine[at]
            share = jnp.zeros((BLOCK, 1), WIDE)
            for head in range(heads):
                columns = head_columns(head)
                normed = turn(summed(head) * SCALE, cos, -sin)
                out[at, columns] = normed
                weighed = normed * raw[at, columns]
                share += jnp.sum(gain[:, columns] * weighed, axis=1, keepdims=True)
                gain_grad[:, columns] += jnp.sum(weighed * factor, axis=0, keepdims=True)
            return share

        def key_block(index):
            at = row_slice(index, BLOCK)
            key_sum[...] = jnp.zeros_like(key_sum)
            value_sum[...] = jnp.zeros_like(value_sum)

            def query_block(other, carry):
                there = row_slice(other, BLOCK)
                key_place = row_index + index * BLOCK
                allowed = (key_place >= start_row[:, there]) & (
                    key_place <= column_index + other * BLOCK
                )
                for head in range(heads):
                    columns = head_columns(head)
                    scores = nt(keys[at, columns], queries[there, columns]) * SCALE_TWO
                    scores = jnp.where(allowed, scores, NEGATIVE)
                    chance = jnp.exp2(scores - peaks[head : head + 1, there])
                    value_sum[:, columns] += jnp.dot(
                        chance.astype(LOW), upstream[there, columns], preferred_element_type=WIDE
                    )
                    chance_grad = nt(values[at, columns], upstream[there, columns])
                    score_grad = (chance * (chance_grad - deltas[head : head + 1, there])).astype(LOW)
                    key_sum[:, columns] += jnp.dot(
                        score_grad, queries[there, columns], preferred_element_type=WIDE
                    )
                    query_sum[there, columns] += lax.dot_general(
                        score_grad,
                        keys[at, columns],
                        (((0,), (0,)), ((), ())),
                        preferred_element_type=WIDE,
                    )
                return carry

            lax.fori_loop(index, last_block[index] + 1, query_block, 0)
            value_out[at] = value_sum[...].astype(LOW)
            share = turn_back(
                at,
                lambda head: key_sum[:, head_columns(head)],
                key_raw,
                key_gain,
                factors[at, 1:2],
                key_out,
                key_gain_grad,
            )
            columns_scratch[at] = jnp.where(lane == 1, share, 0.0)

        loop(length // BLOCK, key_block)

        def finish(index):
            at = row_slice(index, BLOCK)
            share = turn_back(
                at,
                lambda head: query_sum[at, head_columns(head)],
                query_raw,
                query_gain,
                factors[at, 0:1],
                query_out,
                query_gain_grad,
            )
            columns_scratch[at] += jnp.where(lane == 0, share, 0.0)

        loop(length // BLOCK, finish)
        projections[...] = columns_scratch[...].T[:8]

    shape = jax.ShapeDtypeStruct
    smem = pl.BlockSpec(memory_space=pltpu.SMEM)
    return pl.pallas_call(
        kernel,
        out_shape=[
            shape((length, width), WIDE),
            shape((length, width), WIDE),
            shape((length, width), LOW),
            shape((8, length), WIDE),
            shape((1, width), WIDE),
            shape((1, width), WIDE),
        ],
        in_specs=[smem] + [VMEM] * 14,
        out_specs=[VMEM] * 6,
        scratch_shapes=[
            pltpu.VMEM((length, width), WIDE),
            pltpu.VMEM((BLOCK, width), WIDE),
            pltpu.VMEM((BLOCK, width), WIDE),
            pltpu.VMEM((length, LANES), WIDE),
            pltpu.VMEM((8, length), WIDE),
        ],
        compiler_params=pltpu.CompilerParams(vmem_limit_bytes=52 * MIB),
        cost_estimate=pl.CostEstimate(
            flops=5 * length * MAX_LEN * width,
            bytes_accessed=32 * length * width,
            transcendentals=length * MAX_LEN * heads // 2,
        ),
    )(
        last_block,
        queries,
        keys,
        values,
        attended,
        upstream,
        peaks,
        query_raw,
        key_raw,
        factors,
        query_gain,
        key_gain,
        *tables,
        start_row,
    )


def shards(
    tokens,
    query_weight,
    key_weight,
    value_weight,
    output_weight,
    gate_weight,
    up_weight,
    down_weight,
    query_gain,
    key_gain,
    attn_gain,
    mlp_gain,
    seq_ids,
    out_grad,
):
    segment = seq_ids[0]
    length = tokens.shape[0]
    local_width = tokens.shape[1]
    cosine, sine = rotary_tables(segment)
    tables = (
        jnp.concatenate([cosine, cosine], axis=1),
        jnp.concatenate([-sine, sine], axis=1),
    )
    order = jnp.arange(length, dtype=jnp.int32)
    starts = order - token_positions(segment)
    blocks = length // BLOCK
    first_block = starts.reshape(blocks, BLOCK)[:, 0] // BLOCK
    closing = segment.reshape(blocks, BLOCK)[:, -1]
    ends = jnp.sum((segment[None, :] <= closing[:, None]).astype(jnp.int32), axis=1) - 1
    last_block = ends // BLOCK
    gains = jnp.concatenate([attn_gain[None], mlp_gain[None], jnp.zeros((6, local_width))], axis=0)
    query_gain, key_gain = query_gain.reshape(1, -1), key_gain.reshape(1, -1)
    middle = local_width // 2
    pairs = (
        (query_weight, key_weight[:, :middle]),
        (key_weight[:, middle:], value_weight),
    )
    stack = jnp.stack([jnp.concatenate(pair, axis=1) for pair in pairs])
    inputs, attn_stack, output_full, query_raw, key_raw, values, squares, halves = gather_in(
        tokens, stack, output_weight, gains, 1
    )
    attn_half, mlp_half = halves[:1], halves[1:2]
    middle = down_weight.shape[0] // 2
    squares, down_rows = lax.optimization_barrier((squares, down_weight[middle:]))
    down_second = lax.all_gather(down_rows, "gy", axis=0)
    factors = lax.rsqrt(squares[:2].T / D + EPS)
    queries, keys, attended, peaks = attend(
        first_block,
        query_raw,
        key_raw,
        values,
        factors,
        query_gain,
        key_gain,
        tables,
        starts[:, None],
    )
    attn_raw, mixed, mlp_inputs, gate_full, up_full, down_first, upstream = attn_out(
        attended, output_full, attn_half, inputs, out_grad, gate_weight, up_weight, down_weight[:middle], 2
    )
    result, mlp_full, mlp_gain_part, hidden, silu, slope = mlp_forward(
        mlp_inputs, gate_full, up_full, down_first, down_second, mlp_half, mixed, upstream, 3
    )
    gate_grad, up_grad, down_turned = hidden_back(
        mlp_full, down_first, down_second, hidden, silu, slope, 4
    )
    down_weight_grad = down_turned.T
    mixed_grad, attn_full, attn_gain_part, gate_weight_grad, up_weight_grad = mlp_back(
        gate_grad, up_grad, gate_full, up_full, mlp_inputs, attn_half, upstream, attn_raw, 5
    )
    output_product = lax.dot_general(
        attended, attn_full, (((0,), (0,)), ((), ())), preferred_element_type=jnp.float32
    )
    output_weight_grad = lax.psum_scatter(
        output_product.astype(jnp.bfloat16), "gy", scatter_dimension=1, tiled=True
    ).astype(jnp.float32)
    attended_grad = lax.dot_general(
        attn_full, output_full, (((1,), (1,)), ((), ())), preferred_element_type=jnp.float32
    ).astype(jnp.bfloat16)
    query_back, key_back, value_grad, projections, query_gain_part, key_gain_part = attend_back(
        last_block,
        queries,
        keys,
        values,
        attended,
        attended_grad,
        peaks,
        query_raw,
        key_raw,
        factors,
        query_gain,
        key_gain,
        tables,
        starts[None, :],
    )
    token_grad, attn_weight_grads, gain_grads = attn_in_back(
        query_back,
        key_back,
        value_grad,
        query_raw,
        key_raw,
        factors,
        projections,
        query_gain,
        key_gain,
        attn_stack,
        inputs,
        mixed_grad,
        (query_gain_part, key_gain_part, attn_gain_part, mlp_gain_part),
        6,
    )
    query_weight_grad = attn_weight_grads[:, :local_width]
    key_weight_grad = attn_weight_grads[:, local_width : 2 * local_width]
    value_weight_grad = attn_weight_grads[:, 2 * local_width :]
    query_gain_grad, key_gain_grad, attn_gain_grad, mlp_gain_grad = (gain_grads[i] for i in range(4))
    return (
        result,
        token_grad,
        query_weight_grad,
        key_weight_grad,
        value_weight_grad,
        output_weight_grad,
        gate_weight_grad,
        up_weight_grad,
        down_weight_grad,
        query_gain_grad,
        key_gain_grad,
        attn_gain_grad,
        mlp_gain_grad,
    )


def solution(mesh):
    return jax.shard_map(
        shards,
        mesh=mesh,
        in_specs=(
            P("gy", "gx"),
            P("gy", "gx"),
            P("gy", "gx"),
            P("gy", "gx"),
            P("gx", "gy"),
            P("gy", "gx"),
            P("gy", "gx"),
            P("gx", "gy"),
            P("gx"),
            P("gx"),
            P("gx"),
            P("gx"),
            P("gy", None),
            P("gy", "gx"),
        ),
        out_specs=(
            P("gy", "gx"),
            P("gy", "gx"),
            P("gy", "gx"),
            P("gy", "gx"),
            P("gy", "gx"),
            P("gx", "gy"),
            P("gy", "gx"),
            P("gy", "gx"),
            P("gx", "gy"),
            P("gx"),
            P("gx"),
            P("gx"),
            P("gx"),
        ),
        check_vma=False,
    )
```

```python
import math

import jax
import jax.numpy as jnp
from jax import lax
from jax.experimental import pallas as pl
from jax.experimental.pallas import tpu as pltpu
from jax.sharding import PartitionSpec as P

D = 2048
HEAD = 128
MAX_LEN = 1024
SEGS = 4


EPS = 1e-06
THETA = 500000.0
NEGATIVE = -1e30


MESH = pl.DeviceIdType.MESH
HBM = pl.BlockSpec(memory_space=pltpu.HBM)
VMEM = pl.BlockSpec(memory_space=pltpu.VMEM)
LOW = jnp.bfloat16
WIDE = jnp.float32
MIB = 1 << 20
LAG = 2
STATS = 128


def core_here():
    return lax.rem(lax.axis_index("gx"), 2)


def chip_here():
    return lax.div(lax.axis_index("gx"), 2)


def other_core():
    return lax.axis_index("gx") + 1 - 2 * core_here()


def peer_at(shift):
    return lax.rem(lax.axis_index("gx") + 2 * shift, lax.axis_size("gx"))


def rank_at(shift):
    return lax.rem(lax.axis_index("gx") + shift, lax.axis_size("gx"))


def block_at(shift):
    return lax.rem(lax.axis_index("gy") + shift, lax.axis_size("gy"))


def ring_place():
    count = lax.axis_size("gy")
    index = lax.axis_index("gy")
    row, side = lax.div(index, 2), lax.rem(index, 2)
    return side * row + (1 - side) * (count - 1 - row)


def ring_device(place):
    count = lax.axis_size("gy")
    place = lax.rem(place + 2 * count, count)
    back = lax.div(place, count // 2)
    row = (1 - back) * place + back * (count - 1 - place)
    return 2 * row + 1 - back


def greet(gx, ring, all_blocks=False):
    barrier = pltpu.get_barrier_semaphore()
    partners = []
    if all_blocks:
        partners += [{"gy": block_at(k)} for k in range(1, lax.axis_size("gy"))]
    if gx == "all":
        partners += [{"gx": rank_at(k)} for k in range(1, lax.axis_size("gx"))]
    elif gx:
        partners.append({"gx": other_core()})
        partners += [{"gx": peer_at(k)} for k in range(1, lax.axis_size("gx") // 2)]
    if ring:
        place = ring_place()
        partners += [{"gy": ring_device(place + 1)}, {"gy": ring_device(place - 1)}]
    for partner in partners:
        pl.semaphore_signal(barrier, inc=1, device_id=partner, device_id_type=MESH)
    pl.semaphore_wait(barrier, len(partners))


def remote(source, target, send, recv, device):
    return pltpu.make_async_remote_copy(
        src_ref=source,
        dst_ref=target,
        send_sem=send,
        recv_sem=recv,
        device_id=device,
        device_id_type=MESH,
    )


def loop(count, body):
    def step(index, carry):
        body(index)
        return carry

    lax.fori_loop(0, count, step, 0)


def aligned(value, factor):
    return pl.multiple_of(value, factor)


class RingGather:
    def __init__(self, sources, slot, spill, parts, send, recv, local, spilled):
        self.sources, self.slot, self.spill, self.parts = sources, slot, spill, parts
        self.send, self.recv, self.local, self.spilled = send, recv, local, spilled
        self.count = lax.axis_size("gy")

    @staticmethod
    def scratch(parts):
        count = lax.axis_size("gy")
        return [
            pltpu.SemaphoreType.DMA((count - 1, 2, parts)),
            pltpu.SemaphoreType.DMA((count - 1, 2, parts)),
            pltpu.SemaphoreType.DMA((2, parts)),
            pltpu.SemaphoreType.DMA((count, 2, parts)),
        ]

    def spill_copy(self, way, step, part):
        place = ring_place()
        owner = ring_device(place - (1 - 2 * way) * step)
        return pltpu.make_async_copy(
            self.slot(way, owner, part),
            self.spill(way, owner, part),
            self.spilled.at[step, way, part],
        )

    def copy(self, way, step, part, behind):
        place = ring_place()
        sign = 1 - 2 * way
        spot = self.slot(way, ring_device(place - sign * (step + behind)), part)
        return remote(
            spot,
            spot,
            self.send.at[step, way, part],
            self.recv.at[step, way, part],
            {"gy": ring_device(place + sign)},
        )

    def begin(self):
        place = [
            pltpu.make_async_copy(
                self.sources(way, part),
                self.slot(way, lax.axis_index("gy"), part),
                self.local.at[way, part],
            )
            for way in range(2)
            for part in range(self.parts)
        ]
        for item in place:
            item.start()
        for item in place:
            item.wait()
        for part in range(self.parts):
            for way in range(2):
                self.copy(way, 0, part, 0).start()
                self.spill_copy(way, 0, part).start()

    @property
    def events(self):
        return (self.count - 2) * self.parts

    def event(self, index):
        step = 1 + lax.div(index, self.parts)
        for part in range(self.parts):

            @pl.when(lax.rem(index, self.parts) == part)
            def _():
                for way in range(2):
                    self.copy(way, step - 1, part, 1).wait_recv()
                    self.copy(way, step, part, 0).start()
                    self.spill_copy(way, step, part).start()

    def end(self):
        for part in range(self.parts):
            for way in range(2):
                self.copy(way, self.count - 2, part, 1).wait_recv()
                self.spill_copy(way, self.count - 1, part).start()

        def drain(step):
            for part in range(self.parts):
                for way in range(2):
                    self.copy(way, step, part, 0).wait_send()

        loop(self.count - 1, drain)

    def settle(self):
        def drain(step):
            for part in range(self.parts):
                for way in range(2):
                    self.spill_copy(way, step, part).wait()

        loop(self.count, drain)


class RingScatter:
    def __init__(self, product, total, sums, land, send, recv, credit, slots, parts):
        self.product, self.total, self.sums, self.land = product, total, sums, land
        self.send, self.recv, self.credit = send, recv, credit
        self.slots, self.parts = slots, parts
        self.count = lax.axis_size("gy")
        self.rows = total.shape[2]

    @staticmethod
    def scratch(rows, columns, slots, parts):
        count = lax.axis_size("gy")
        return [
            pltpu.VMEM((2, parts, rows, columns // parts), WIDE),
            pltpu.VMEM((2, parts, rows, columns // parts), LOW),
            pltpu.VMEM((slots, 2, parts, rows, columns // parts), LOW),
            pltpu.SemaphoreType.DMA((count - 1, 2, parts)),
            pltpu.SemaphoreType.DMA((count - 1, 2, parts)),
            pltpu.SemaphoreType.REGULAR((2, parts)),
        ]

    def copy(self, way, step, part):
        place = ring_place()
        return remote(
            self.sums.at[way, part],
            self.land.at[lax.rem(step, self.slots), way, part],
            self.send.at[step, way, part],
            self.recv.at[step, way, part],
            {"gy": ring_device(place + 1 - 2 * way)},
        )

    def owner(self, way, step):
        sign = 1 - 2 * way
        return ring_device(ring_place() - sign * (1 + step))

    @property
    def events(self):
        return self.count * self.parts

    def event(self, index):
        step, part = lax.div(index, self.parts), lax.rem(index, self.parts)
        last = self.count - 1
        tile = min(self.rows, 32)

        for way in range(2):
            self.product(way, step, part)

        for way in range(2):

            slot = lax.rem(step - 1 + self.slots, self.slots)

            def over(body):
                @pl.loop(0, self.rows // tile)
                def _(index):
                    body(pl.ds(aligned(index * tile, tile), tile))

            @pl.when(step >= 1)
            def _():
                self.copy(way, step - 1, part).wait_recv()

            @pl.when((step >= 1) & (step < last))
            def _():
                self.copy(way, step - 1, part).wait_send()

            @pl.when(step == 0)
            def _():
                def first(rows):
                    self.sums[way, part, rows] = self.total[way, part, rows].astype(LOW)

                over(first)

            @pl.when((step >= 1) & (step < last))
            def _():
                def more(rows):
                    arrived = self.land[slot, way, part, rows].astype(WIDE)
                    self.sums[way, part, rows] = (self.total[way, part, rows] + arrived).astype(LOW)

                over(more)

            @pl.when(step == last)
            def _():
                def final(rows):
                    self.total[way, part, rows] += self.land[slot, way, part, rows].astype(WIDE)

                over(final)

            @pl.when((step >= 1) & (step - 1 + self.slots < last))
            def _():
                upstream = ring_device(ring_place() - (1 - 2 * way))
                pl.semaphore_signal(
                    self.credit.at[way, part],
                    inc=1,
                    device_id={"gy": upstream},
                    device_id_type=MESH,
                )

            @pl.when(step < last)
            def _():
                @pl.when(step >= self.slots)
                def _():
                    pl.semaphore_wait(self.credit.at[way, part], 1)

                self.copy(way, step, part).start()

    def end(self):
        for part in range(self.parts):
            for way in range(2):
                self.copy(way, self.count - 2, part).wait_send()


class Reduce:
    def __init__(self, refs, cross_land, rows, width, scatter):
        (
            self.keep,
            self.core_send,
            self.core_land,
            self.cross,
            self.cross_stage,
            self.raw,
            self.core_sems,
            self.cross_send_sems,
            self.cross_recv_sems,
            self.stage_sems,
        ) = refs
        self.cross_land = cross_land
        self.rows, self.width, self.scatter = rows, width, scatter
        self.chips = lax.axis_size("gx") // 2

    @staticmethod
    def scratch(rows, chunks, width, scatter):
        chips = lax.axis_size("gx") // 2
        half = chips * width
        part = width if scatter else half
        return [
            pltpu.VMEM((1, rows, half), LOW),
            pltpu.VMEM((2, rows, half), LOW),
            pltpu.VMEM((2, rows, half), LOW),
            pltpu.VMEM((LAG + 1, chips, rows, width) if scatter else (LAG + 1, rows, half), LOW),
            pltpu.VMEM((chips - 1, rows, part), LOW),
            pltpu.VMEM((rows, part), WIDE),
            pltpu.SemaphoreType.DMA((2, chunks)),
            pltpu.SemaphoreType.DMA((chips - 1, chunks)),
            pltpu.SemaphoreType.DMA((chips - 1, chunks)),
            pltpu.SemaphoreType.DMA((chips,)),
        ]

    @staticmethod
    def landing(rows, chunks, width, scatter):
        chips = lax.axis_size("gx") // 2
        half = chips * width
        part = width if scatter else half
        return [jax.ShapeDtypeStruct((chips - 1, chunks, rows, part), LOW)]

    def core_copy(self, chunk):
        return remote(
            self.core_send.at[lax.rem(chunk, 2)],
            self.core_land.at[lax.rem(chunk, 2)],
            self.core_sems.at[0, chunk],
            self.core_sems.at[1, chunk],
            {"gx": other_core()},
        )

    def cross_copy(self, shift, chunk):
        source = self.cross.at[lax.rem(chunk, LAG + 1)]
        if self.scatter:
            block = lax.rem(chip_here() + shift, self.chips)
            source = source.at[block]
        return remote(
            source,
            self.cross_land.at[shift - 1, chunk],
            self.cross_send_sems.at[shift - 1, chunk],
            self.cross_recv_sems.at[shift - 1, chunk],
            {"gx": peer_at(shift)},
        )

    def produce(self, chunk, dot):
        @pl.when(chunk >= 2)
        def _():
            self.core_copy(chunk - 2).wait_send()

        slot = lax.rem(chunk, 2)
        core = core_here()
        for chip in range(self.chips):
            place = aligned((2 * chip + 1 - core) * self.width, self.width)
            self.core_send[slot, :, chip * self.width : (chip + 1) * self.width] = dot(
                place
            ).astype(LOW)
        self.core_copy(chunk).start()
        for chip in range(self.chips):
            place = aligned((2 * chip + core) * self.width, self.width)
            self.keep[0, :, chip * self.width : (chip + 1) * self.width] = dot(
                place
            ).astype(LOW)

    def core_sum(self, chunk):
        slot, place = lax.rem(chunk, 2), lax.rem(chunk, LAG + 1)
        self.core_copy(chunk).wait_recv()

        @pl.when(chunk >= LAG + 1)
        def _():
            for shift in range(1, self.chips):
                self.cross_copy(shift, chunk - LAG - 1).wait_send()

        @pl.loop(0, self.rows // 32)
        def _(index):
            rows = pl.ds(aligned(index * 32, 32), 32)
            total = self.keep[0, rows].astype(WIDE) + self.core_land[slot, rows].astype(WIDE)
            if self.scatter:
                for chip in range(self.chips):
                    columns = slice(chip * self.width, (chip + 1) * self.width)
                    self.cross[place, chip, rows] = total[:, columns].astype(LOW)
            else:
                self.cross[place, rows] = total.astype(LOW)

        for shift in range(1, self.chips):
            self.cross_copy(shift, chunk).start()

    def cross_stage_copy(self, shift, chunk):
        return pltpu.make_async_copy(
            self.cross_land.at[shift - 1, chunk],
            self.cross_stage.at[shift - 1],
            self.stage_sems.at[shift],
        )

    def cross_fetch(self, chunk):
        for shift in range(1, self.chips):
            self.cross_copy(shift, chunk).wait_recv()
            self.cross_stage_copy(shift, chunk).start()

    def cross_sum(self, chunk):
        place = lax.rem(chunk, LAG + 1)
        for shift in range(1, self.chips):
            self.cross_stage_copy(shift, chunk).wait()

        @pl.loop(0, self.rows // 32)
        def _(index):
            rows = pl.ds(aligned(index * 32, 32), 32)
            if self.scatter:
                total = self.cross[place, chip_here(), rows].astype(WIDE)
            else:
                total = self.cross[place, rows].astype(WIDE)
            for shift in range(1, self.chips):
                total = total + self.cross_stage[shift - 1, rows].astype(WIDE)
            self.raw[rows] = total

    def end(self, chunks):
        for chunk in (chunks - 2, chunks - 1):
            self.core_copy(chunk).wait_send()
        for chunk in range(chunks - LAG - 1, chunks):
            for shift in range(1, self.chips):
                self.cross_copy(shift, chunk).wait_send()


class Stats:
    def __init__(self, mine, land, sems):
        self.mine, self.land, self.sems = mine, land, sems

    @staticmethod
    def scratch(rows, chunks):
        return [
            pltpu.VMEM((2, rows, STATS), WIDE),
            pltpu.VMEM((2, rows, STATS), WIDE),
            pltpu.SemaphoreType.DMA((2, chunks)),
        ]

    def copy(self, chunk):
        return remote(
            self.mine.at[lax.rem(chunk, 2)],
            self.land.at[lax.rem(chunk, 2)],
            self.sems.at[0, chunk],
            self.sems.at[1, chunk],
            {"gx": other_core()},
        )

    def clear(self, chunk):
        @pl.when(chunk >= 2)
        def _():
            self.copy(chunk - 2).wait_send()

    def put(self, chunk, rows, first, second):
        lane = lax.broadcasted_iota(jnp.int32, (first.shape[0], STATS), 1)
        self.mine[lax.rem(chunk, 2), rows] = jnp.where(lane < STATS // 2, first, second)

    def get(self, chunk, rows):
        total = self.mine[lax.rem(chunk, 2), rows] + self.land[lax.rem(chunk, 2), rows]
        return (total[:, :1], total[:, STATS // 2 : STATS // 2 + 1])

    def end(self, chunks):
        for chunk in (chunks - 2, chunks - 1):
            self.copy(chunk).wait_send()


class Spread:
    def __init__(self, buffer, whole, local, send, recv, rows, width):
        self.buffer, self.whole = buffer, whole
        self.local, self.send, self.recv = local, send, recv
        self.rows, self.width = rows, width
        self.chips = lax.axis_size("gx") // 2

    @staticmethod
    def scratch(rows, chunks, width):
        chips = lax.axis_size("gx") // 2
        return [
            pltpu.VMEM((2, chips, rows, width), LOW),
            pltpu.SemaphoreType.DMA((2, chips)),
            pltpu.SemaphoreType.DMA((chunks, chips)),
            pltpu.SemaphoreType.DMA((chunks, chips)),
        ]

    def pair(self, chunk, chip, core):
        slot = lax.rem(chunk, 2)
        source = self.buffer.at[slot, chip]
        rows = pl.ds(aligned(chunk * self.rows, self.rows), self.rows)
        rank = 2 * chip + core
        if len(self.whole.shape) == 3:
            target = self.whole.at[rank, rows]
        else:
            columns = pl.ds(aligned(rank * self.width, self.width), self.width)
            target = self.whole.at[rows, columns]
        here = pltpu.make_async_copy(source, target, self.local.at[slot, chip])
        away = remote(
            source,
            target,
            self.send.at[chunk, chip],
            self.recv.at[chunk, chip],
            {"gx": other_core()},
        )
        return (here, away)

    def put(self, chunk, rows, values):
        for chip in range(self.chips):
            columns = slice(chip * self.width, (chip + 1) * self.width)
            self.buffer[lax.rem(chunk, 2), chip, rows] = values[:, columns].astype(LOW)

    def clear(self, chunk):
        @pl.when(chunk >= 2)
        def _():
            self.settle(chunk - 2)

    def settle(self, chunk):
        for chip in range(self.chips):
            here, away = self.pair(chunk, chip, core_here())
            here.wait()
            away.wait_send()

    def go(self, chunk):
        for chip in range(self.chips):
            here, away = self.pair(chunk, chip, core_here())
            here.start()
            away.start()

    def end(self, chunks):
        for chunk in (chunks - 2, chunks - 1):
            self.settle(chunk)

        def arrive(chunk):
            for chip in range(self.chips):
                self.pair(chunk, chip, 1 - core_here())[1].wait_recv()

        loop(chunks, arrive)


def row_slice(chunk, rows):
    return pl.ds(aligned(chunk * rows, rows), rows)


def core_blocks(source, chunk, rows, width, buffer, sems):
    return [
        pltpu.make_async_copy(
            source.at[2 * chip + core_here(), row_slice(chunk, rows)],
            buffer.at[:, chip * width : (chip + 1) * width],
            sems.at[chip],
        )
        for chip in range(lax.axis_size("gx") // 2)
    ]


def all_blocks(source, rows, width, buffer, sems):
    return [
        pltpu.make_async_copy(
            source.at[rank] if rows is None else source.at[rank, rows],
            buffer.at[:, rank * width : (rank + 1) * width],
            sems.at[rank],
        )
        for rank in range(source.shape[0])
    ]


def tiles(rows, body):
    @pl.loop(0, rows // 32)
    def _(index):
        body(pl.ds(aligned(index * 32, 32), 32))


def schedule(chunks, reduce, multiply, fetch, sums, finish, event=None, events=0, prepare=None):
    steps = chunks + 1 + LAG

    def ring_events(place):
        if event is not None:
            low = lax.div(place * events, 2 * steps)
            high = lax.div((place + 1) * events, 2 * steps)

            def some(index, carry):
                event(index)
                return carry

            lax.fori_loop(low, high, some, 0)

    def iteration(step):
        ring_events(2 * step)

        @pl.when((step >= LAG) & (step < chunks + LAG))
        def _():
            reduce.cross_fetch(step - LAG)

        @pl.when(step >= LAG)
        def _():
            fetch(step - LAG)

        @pl.when(step < chunks)
        def _():
            if prepare is not None:
                prepare(step)
            reduce.produce(step, lambda place: multiply(step, place))
            reduce.core_sum(step)

        ring_events(2 * step + 1)

        @pl.when(step >= 1 + LAG)
        def _():
            finish(step - 1 - LAG)

        @pl.when((step >= LAG) & (step < chunks + LAG))
        def _():
            reduce.cross_sum(step - LAG)
            sums(step - LAG)

    loop(steps, iteration)


def take(refs, counts):
    groups, start = [], 0
    for count in counts:
        groups.append(refs[start : start + count])
        start += count
    return groups


class Columns:
    def __init__(self, source, shard, left, turned, sem):
        self.source, self.shard = source, shard
        self.left, self.turned, self.sem = left, turned, sem

    @staticmethod
    def scratch(length, shard):
        return [
            pltpu.VMEM((length, shard), LOW),
            pltpu.VMEM((2, shard, length), LOW),
            pltpu.SemaphoreType.DMA((1,)),
        ]

    def copy(self, owner):
        each = self.source.shape[2] // self.shard
        at = pl.ds(aligned(lax.rem(owner, each) * self.shard, self.shard), self.shard)
        source = self.source.at[lax.div(owner, each), :, at]
        return pltpu.make_async_copy(source, self.left, self.sem.at[0])

    def take(self, ring, way, step):
        self.copy(ring.owner(way, step)).wait()
        self.turned[way] = self.left[...].T
        if way == 0:
            self.copy(ring.owner(1, step)).start()
        else:

            @pl.when(step + 1 < ring.count)
            def _():
                self.copy(ring.owner(0, step + 1)).start()


def attn_out(
    attended, weight, gain, tokens, out_grad, gate_shard, up_shard, down_shard, collective
):
    length, width = attended.shape
    chips = lax.axis_size("gx") // 2
    half = chips * width
    count = lax.axis_size("gy")
    chunks = count
    rows = length // chunks
    hidden = gate_shard.shape[1]
    inner = down_shard.shape[0]
    shard = gate_shard.shape[0]
    part_rows = shard // 2
    side = inner // 2
    down_columns = down_shard.shape[1]

    groups = [
        Reduce.scratch(rows, chunks, width, False),
        Stats.scratch(rows, chunks),
        Spread.scratch(rows, chunks, width),
        RingGather.scratch(3),
        [
            pltpu.VMEM((rows, half), LOW),
            pltpu.VMEM((2, rows, half), WIDE),
            pltpu.VMEM((2, rows, half), LOW),
            pltpu.SemaphoreType.DMA((chips,)),
            pltpu.SemaphoreType.DMA((2,)),
            pltpu.SemaphoreType.DMA((2,)),
            pltpu.SemaphoreType.DMA((2,)),
            pltpu.SemaphoreType.DMA((chips - 1, chunks, 2)),
        ],
        [
            pltpu.VMEM((2, D, hidden), LOW),
            pltpu.VMEM((count, inner, down_columns), LOW),
            pltpu.VMEM((chips, length, width), LOW),
        ],
    ]

    def kernel(*refs):
        ins, outs, *scratch = take(refs, [8, 8] + [len(g) for g in groups])
        attended, weight, gain, tokens, out_grad, gate_shard, up_shard, down_shard = ins
        raw_out, mixed_out, low_out, gate_full, up_full, down_full, upstream = outs[:7]
        cross_land = outs[7]
        reduce = Reduce(scratch[0], cross_land, rows, width, False)
        stats = Stats(*scratch[1])
        buffer, local, send, recv = scratch[2]
        spread = Spread(buffer, low_out, local, send, recv, rows, width)
        token_buf, mixed_buf, raw_buf = scratch[4][:3]
        token_sems, mixed_sems, raw_sems, own_sem, up_sems = scratch[4][3:]
        held, held_down, up_land = scratch[5]
        shards_here = (gate_shard, up_shard)

        def place_in(full, down):
            def slot(way, owner, part):
                if part == 2:
                    return down.at[owner, way * side : (way + 1) * side]
                base = owner * shard + part * part_rows
                return full[way].at[pl.ds(aligned(base, part_rows), part_rows)]

            return slot

        slot = place_in((held.at[0], held.at[1]), held_down)
        spill = place_in((gate_full, up_full), down_full)

        def source(way, part):
            if part == 2:
                return down_shard.at[way * side : (way + 1) * side]
            return shards_here[way].at[part * part_rows : (part + 1) * part_rows]

        ring = RingGather(source, slot, spill, 3, *scratch[3])
        own = pltpu.make_async_copy(out_grad, up_land.at[chip_here()], own_sem.at[0])
        up_spill = pltpu.make_async_copy(up_land, upstream, own_sem.at[1])

        def crossings(chunk):
            at = row_slice(chunk, rows)
            return [
                remote(
                    up_land.at[chip_here(), at],
                    up_land.at[chip_here(), at],
                    up_sems.at[shift - 1, chunk, 0],
                    up_sems.at[shift - 1, chunk, 1],
                    {"gx": peer_at(shift)},
                )
                for shift in range(1, chips)
            ]

        own.start()
        greet(True, True)
        ring.begin()
        own.wait()

        def multiply(chunk, place):
            return jnp.dot(
                attended[row_slice(chunk, rows)],
                weight[:, pl.ds(place, width)],
                preferred_element_type=WIDE,
            )

        def prepare(chunk):
            for item in crossings(chunk):
                item.start()

        def token_copies(chunk):
            return core_blocks(tokens, chunk, rows, width, token_buf, token_sems)

        def fetch(chunk):
            @pl.when(chunk >= 1)
            def _():
                for item in token_copies(chunk - 1):
                    item.start()

        def mixed_copy(chunk):
            slot = lax.rem(chunk, 2)
            return pltpu.make_async_copy(
                mixed_buf.at[slot, :, pl.ds(aligned(chip_here() * width, width), width)],
                mixed_out.at[row_slice(chunk, rows)],
                mixed_sems.at[slot],
            )

        def raw_copy(chunk):
            slot = lax.rem(chunk, 2)
            return pltpu.make_async_copy(
                raw_buf.at[slot], raw_out.at[row_slice(chunk, rows)], raw_sems.at[slot]
            )

        def sums(chunk):
            stats.clear(chunk)

            @pl.when(chunk >= 2)
            def _():
                raw_copy(chunk - 2).wait()

            def tile(at):
                raw = reduce.raw[at]
                raw_buf[lax.rem(chunk, 2), at] = raw.astype(LOW)
                squares = jnp.sum(raw * raw, axis=1, keepdims=True)
                stats.put(chunk, at, squares, squares)

            tiles(rows, tile)
            stats.copy(chunk).start()
            raw_copy(chunk).start()

        def finish(chunk):
            slot = lax.rem(chunk, 2)
            for item in token_copies(chunk):
                item.wait()
            stats.copy(chunk).wait_recv()
            spread.clear(chunk)

            @pl.when(chunk >= 2)
            def _():
                mixed_copy(chunk - 2).wait()

            def tile(at):
                squares, _ = stats.get(chunk, at)
                factor = lax.rsqrt(squares / D + EPS)
                mixed = token_buf[at].astype(WIDE) + reduce.raw[at] * factor * gain[...]
                mixed_buf[slot, at] = mixed
                spread.put(chunk, at, mixed)

            tiles(rows, tile)
            spread.go(chunk)
            mixed_copy(chunk).start()

        schedule(chunks, reduce, multiply, fetch, sums, finish, ring.event, ring.events, prepare)
        def drain(chunk):
            for item in crossings(chunk):
                item.wait()

        loop(chunks, drain)
        up_spill.start()
        ring.end()
        up_spill.wait()
        ring.settle()
        reduce.end(chunks)
        stats.end(chunks)
        spread.end(chunks)
        for chunk in (chunks - 2, chunks - 1):
            mixed_copy(chunk).wait()
            raw_copy(chunk).wait()

    shape = jax.ShapeDtypeStruct
    out = pl.pallas_call(
        kernel,
        out_shape=[
            shape((length, half), LOW),
            shape((length, width), WIDE),
            shape((2 * chips, length, width), LOW),
            shape((shard * count, hidden), LOW),
            shape((shard * count, hidden), LOW),
            shape((count, inner, down_columns), LOW),
            shape((chips, length, width), LOW),
        ]
        + Reduce.landing(rows, chunks, width, False),
        in_specs=[VMEM, VMEM, VMEM, HBM, HBM, HBM, HBM, HBM],
        out_specs=[HBM] * 8,
        scratch_shapes=[item for group in groups for item in group],
        compiler_params=pltpu.CompilerParams(
            collective_id=collective, has_side_effects=True, vmem_limit_bytes=60 * MIB
        ),
        cost_estimate=pl.CostEstimate(
            flops=2 * length * width * D, bytes_accessed=8 * length * D, transcendentals=0
        ),
    )(attended, weight, gain, tokens, out_grad, gate_shard, up_shard, down_shard)
    return out[:7]


def mlp_forward(
    inputs, gate_full, up_full, down_first, down_second, gain, mixed, upstream, collective
):
    length, inner = inputs.shape[1], gate_full.shape[1]
    width = mixed.shape[1]
    ranks = inputs.shape[0]
    down_columns = down_first.shape[2]
    down_rows = down_first.shape[1]
    chips = lax.axis_size("gx") // 2
    half = chips * width
    chunks = lax.axis_size("gy")
    rows = length // chunks
    tile = min(512, inner)
    pieces = inner // tile

    groups = [
        Reduce.scratch(rows, chunks, width, False),
        Stats.scratch(rows, chunks),
        Spread.scratch(rows, chunks, width),
        [
            pltpu.VMEM((2, rows, half), LOW),
            pltpu.VMEM((rows, width), WIDE),
            pltpu.VMEM((2, rows, width), LOW),
            pltpu.SemaphoreType.DMA((2, chips)),
            pltpu.SemaphoreType.DMA((1,)),
            pltpu.SemaphoreType.DMA((2,)),
        ],
        [
            pltpu.VMEM((D, inner), LOW),
            pltpu.VMEM((D, inner), LOW),
            pltpu.VMEM((inner, D), LOW),
            pltpu.VMEM((2, rows, D), LOW),
            pltpu.VMEM((2, 3, rows, inner), LOW),
            pltpu.SemaphoreType.DMA((pieces, 2)),
            pltpu.SemaphoreType.DMA((2, chunks)),
            pltpu.SemaphoreType.DMA((2, ranks)),
            pltpu.SemaphoreType.DMA((2, 3)),
        ],
    ]

    def kernel(*refs):
        ins, outs, *scratch = take(refs, [8, 7] + [len(g) for g in groups])
        inputs, gate_full, up_full, down_first, down_second, gain, mixed, upstream = ins
        result, grad_out, gain_grad, hidden_out, silu_out, slope_out, cross_land = outs
        gate_weight, up_weight, weight, row_buf, made = scratch[4][:5]
        piece_sems, weight_sem, row_sems, made_sems = scratch[4][5:]
        reduce = Reduce(scratch[0], cross_land, rows, width, False)
        stats = Stats(*scratch[1])
        buffer, local, send, recv = scratch[2]
        spread = Spread(buffer, grad_out, local, send, recv, rows, width)
        up_buf, mixed_buf, result_buf, up_sems, mixed_sems, result_sems = scratch[3]

        def piece_copies(piece):
            at = pl.ds(aligned(piece * tile, tile), tile)
            return [
                pltpu.make_async_copy(gate_full.at[:, at], gate_weight.at[:, at], piece_sems.at[piece, 0]),
                pltpu.make_async_copy(up_full.at[:, at], up_weight.at[:, at], piece_sems.at[piece, 1]),
            ]

        weight_copies = all_blocks(
            down_first, None, down_columns, weight.at[:down_rows], weight_sem.at[0]
        ) + all_blocks(down_second, None, down_columns, weight.at[down_rows:], weight_sem.at[1])

        def row_copy(chunk):
            slot = lax.rem(chunk, 2)
            return all_blocks(
                inputs, row_slice(chunk, rows), width, row_buf.at[slot], row_sems.at[slot]
            )

        def stores(chunk):
            slot, at = lax.rem(chunk, 2), row_slice(chunk, rows)
            return [
                pltpu.make_async_copy(made.at[slot, which], out.at[at], made_sems.at[slot, which])
                for which, out in enumerate((hidden_out, silu_out, slope_out))
            ]

        for item in row_copy(0):
            item.start()
        for piece in range(pieces):
            for item in piece_copies(piece):
                item.start()
        for item in weight_copies:
            item.start()
        greet(True, False)
        gain_grad[...] = jnp.zeros_like(gain_grad)

        def prepare(chunk):
            slot = lax.rem(chunk, 2)
            for item in row_copy(chunk):
                item.wait()

            @pl.when(chunk + 1 < chunks)
            def _():
                for item in row_copy(chunk + 1):
                    item.start()

            @pl.when(chunk >= 2)
            def _():
                for item in stores(chunk - 2):
                    item.wait()

            @pl.loop(0, pieces)
            def _(piece):
                @pl.when(chunk == 0)
                def _():
                    for item in piece_copies(piece):
                        item.wait()

                at = pl.ds(aligned(piece * tile, tile), tile)
                gate = jnp.dot(row_buf[slot], gate_weight[:, at], preferred_element_type=WIDE)
                up = jnp.dot(row_buf[slot], up_weight[:, at], preferred_element_type=WIDE)
                sigma = jax.nn.sigmoid(gate)
                silu = gate * sigma
                made[slot, 0, :, at] = (silu * up).astype(LOW)
                made[slot, 1, :, at] = silu.astype(LOW)
                made[slot, 2, :, at] = (up * (sigma + silu * (1.0 - sigma))).astype(LOW)

            @pl.when(chunk == 0)
            def _():
                for item in weight_copies:
                    item.wait()

            for item in stores(chunk):
                item.start()

        def multiply(chunk, place):
            return jnp.dot(
                made[lax.rem(chunk, 2), 0],
                weight[:, pl.ds(place, width)],
                preferred_element_type=WIDE,
            )

        def up_copy(chunk):
            slot = lax.rem(chunk, 2)
            return all_blocks(
                upstream, row_slice(chunk, rows), width, up_buf.at[slot], up_sems.at[slot]
            )

        def mixed_copy(chunk):
            return pltpu.make_async_copy(
                mixed.at[row_slice(chunk, rows)], mixed_buf, mixed_sems.at[0]
            )

        def result_copy(chunk):
            slot = lax.rem(chunk, 2)
            return pltpu.make_async_copy(
                result_buf.at[slot], result.at[row_slice(chunk, rows)], result_sems.at[slot]
            )

        def fetch(chunk):
            @pl.when(chunk < chunks)
            def _():
                for item in up_copy(chunk):
                    item.start()

            @pl.when(chunk >= 1)
            def _():
                mixed_copy(chunk - 1).start()

        def sums(chunk):
            slot = lax.rem(chunk, 2)
            stats.clear(chunk)
            for item in up_copy(chunk):
                item.wait()

            def tile(at):
                raw = reduce.raw[at]
                up = up_buf[slot, at].astype(WIDE)
                squares = jnp.sum(raw * raw, axis=1, keepdims=True)
                projected = jnp.sum(gain[...] * up * raw, axis=1, keepdims=True)
                stats.put(chunk, at, squares, projected)

            tiles(rows, tile)
            stats.copy(chunk).start()

        def finish(chunk):
            slot = lax.rem(chunk, 2)
            mixed_copy(chunk).wait()
            stats.copy(chunk).wait_recv()
            spread.clear(chunk)

            @pl.when(chunk >= 2)
            def _():
                result_copy(chunk - 2).wait()

            block = pl.ds(aligned(chip_here() * width, width), width)

            def tile(at):
                squares, projected = stats.get(chunk, at)
                factor = lax.rsqrt(squares / D + EPS)
                raw = reduce.raw[at]
                up = up_buf[slot, at].astype(WIDE)
                pull = factor * factor * factor * projected / D
                spread.put(chunk, at, factor * gain[...] * up - raw * pull)
                gain_grad[...] += jnp.sum(up * raw * factor, axis=0, keepdims=True)
                result_buf[slot, at] = (
                    mixed_buf[at] + reduce.raw[at, block] * factor * gain[:, block]
                ).astype(LOW)

            tiles(rows, tile)
            spread.go(chunk)
            result_copy(chunk).start()

        schedule(chunks, reduce, multiply, fetch, sums, finish, prepare=prepare)
        reduce.end(chunks)
        stats.end(chunks)
        spread.end(chunks)
        for chunk in (chunks - 2, chunks - 1):
            result_copy(chunk).wait()
            for item in stores(chunk):
                item.wait()

    shape = jax.ShapeDtypeStruct
    out = pl.pallas_call(
        kernel,
        out_shape=[
            shape((length, width), LOW),
            shape((2 * chips, length, width), LOW),
            shape((1, half), WIDE),
            shape((length, inner), LOW),
            shape((length, inner), LOW),
            shape((length, inner), LOW),
        ]
        + Reduce.landing(rows, chunks, width, False),
        in_specs=[HBM] * 5 + [VMEM, HBM, HBM],
        out_specs=[HBM, HBM, VMEM] + [HBM] * 4,
        scratch_shapes=[item for group in groups for item in group],
        compiler_params=pltpu.CompilerParams(
            collective_id=collective, has_side_effects=True, vmem_limit_bytes=60 * MIB
        ),
        cost_estimate=pl.CostEstimate(
            flops=6 * length * inner * D, bytes_accessed=16 * length * D, transcendentals=0
        ),
    )(inputs, gate_full, up_full, down_first, down_second, gain, mixed, upstream)
    return out[:6]


def mlp_back(gate_grad, up_grad, gate_full, up_full, inputs, gain, upstream, attn_raw, collective):
    length, inner = gate_grad.shape
    half = attn_raw.shape[1]
    chips = lax.axis_size("gx") // 2
    width = half // chips
    count = lax.axis_size("gy")
    chunks = count
    rows = length // chunks
    shard = D // count
    slots, parts = 2, 4
    piece = inner // parts

    groups = [
        Reduce.scratch(rows, chunks, width, False),
        Stats.scratch(rows, chunks),
        Spread.scratch(rows, chunks, width),
        RingScatter.scratch(shard, inner, slots, parts),
        [
            pltpu.VMEM((rows, half), LOW),
            pltpu.VMEM((2, rows, half), LOW),
            pltpu.SemaphoreType.DMA((chips,)),
            pltpu.SemaphoreType.DMA((2,)),
            pltpu.SemaphoreType.DMA((1,)),
            pltpu.SemaphoreType.DMA((2, parts)),
        ],
        Columns.scratch(length, shard),
        [
            pltpu.VMEM((2, length, inner), LOW),
            pltpu.VMEM((2, D, inner), LOW),
            pltpu.SemaphoreType.DMA((2, 2)),
        ],
    ]

    def kernel(*refs):
        ins, outs, *scratch = take(refs, [8, 6] + [len(g) for g in groups])
        gate_grad, up_grad, gate_full, up_full, inputs, gain, upstream, attn_raw = ins
        grads, weights, load_sems = scratch[6]
        grad_copies = [
            pltpu.make_async_copy((gate_grad, up_grad)[way], grads.at[way], load_sems.at[0, way])
            for way in range(2)
        ]
        weight_copies = [
            pltpu.make_async_copy((gate_full, up_full)[way], weights.at[way], load_sems.at[1, way])
            for way in range(2)
        ]
        mixed_out, grad_out, gain_grad, gate_out, up_out, cross_land = outs
        reduce = Reduce(scratch[0], cross_land, rows, width, False)
        stats = Stats(*scratch[1])
        buffer, local, send, recv = scratch[2]
        spread = Spread(buffer, grad_out, local, send, recv, rows, width)
        total, summed, land, ring_send, ring_recv, credit = scratch[3]
        up_buf, raw_buf, up_sems, raw_sems, mixed_sems, out_sems = scratch[4]
        left = Columns(inputs, shard, *scratch[5])

        def product(way, step, part):
            @pl.when(part == 0)
            def _():
                left.take(ring, way, step)

            @pl.when((part == 0) & (step == 0))
            def _():
                grad_copies[way].wait()

            columns = pl.ds(aligned(part * piece, piece), piece)
            total[way, part] = jnp.dot(
                left.turned[way], grads[way, :, columns], preferred_element_type=WIDE
            )

        ring = RingScatter(
            product, total, summed, land, ring_send, ring_recv, credit, slots, parts
        )
        left.copy(ring.owner(0, 0)).start()
        for item in grad_copies + weight_copies:
            item.start()
        greet(True, True)
        gain_grad[...] = jnp.zeros_like(gain_grad)

        def prepare(chunk):
            @pl.when(chunk == 0)
            def _():
                for item in weight_copies:
                    item.wait()

        def multiply(chunk, place):
            at = row_slice(chunk, rows)
            return nt(grads[0, at], weights[0, pl.ds(place, width)]) + nt(
                grads[1, at], weights[1, pl.ds(place, width)]
            )

        def up_copy(chunk):
            return all_blocks(upstream, row_slice(chunk, rows), width, up_buf, up_sems)

        def raw_copy(chunk):
            slot = lax.rem(chunk, 2)
            return pltpu.make_async_copy(
                attn_raw.at[row_slice(chunk, rows)], raw_buf.at[slot], raw_sems.at[slot]
            )

        def mixed_copy(chunk):
            return pltpu.make_async_copy(
                reduce.raw.at[:, pl.ds(aligned(chip_here() * width, width), width)],
                mixed_out.at[row_slice(chunk, rows)],
                mixed_sems.at[0],
            )

        def fetch(chunk):
            @pl.when(chunk < chunks)
            def _():
                for item in up_copy(chunk):
                    item.start()
                raw_copy(chunk).start()

        def sums(chunk):
            slot = lax.rem(chunk, 2)
            stats.clear(chunk)
            for item in up_copy(chunk):
                item.wait()
            raw_copy(chunk).wait()

            def tile(at):
                upward = reduce.raw[at] + up_buf[at].astype(WIDE)
                reduce.raw[at] = upward
                raw = raw_buf[slot, at].astype(WIDE)
                squares = jnp.sum(raw * raw, axis=1, keepdims=True)
                projected = jnp.sum(gain[...] * upward * raw, axis=1, keepdims=True)
                stats.put(chunk, at, squares, projected)

            tiles(rows, tile)
            stats.copy(chunk).start()
            mixed_copy(chunk).start()

        def finish(chunk):
            slot = lax.rem(chunk, 2)
            stats.copy(chunk).wait_recv()
            spread.clear(chunk)

            def tile(at):
                squares, projected = stats.get(chunk, at)
                factor = lax.rsqrt(squares / D + EPS)
                upward = reduce.raw[at]
                raw = raw_buf[slot, at].astype(WIDE)
                pull = factor * factor * factor * projected / D
                spread.put(chunk, at, factor * gain[...] * upward - raw * pull)
                gain_grad[...] += jnp.sum(upward * raw * factor, axis=0, keepdims=True)

            tiles(rows, tile)
            spread.go(chunk)
            mixed_copy(chunk).wait()

        schedule(chunks, reduce, multiply, fetch, sums, finish, ring.event, ring.events, prepare)
        writes = [
            pltpu.make_async_copy(
                total.at[way, part],
                (gate_out, up_out)[way].at[:, part * piece : (part + 1) * piece],
                out_sems.at[way, part],
            )
            for way in range(2)
            for part in range(parts)
        ]
        for item in writes:
            item.start()
        ring.end()
        reduce.end(chunks)
        stats.end(chunks)
        spread.end(chunks)
        for item in writes:
            item.wait()

    shape = jax.ShapeDtypeStruct
    out = pl.pallas_call(
        kernel,
        out_shape=[
            shape((length, width), WIDE),
            shape((length, D), LOW),
            shape((1, half), WIDE),
            shape((shard, inner), WIDE),
            shape((shard, inner), WIDE),
        ]
        + Reduce.landing(rows, chunks, width, False),
        in_specs=[HBM, HBM, HBM, HBM, HBM, VMEM, HBM, HBM],
        out_specs=[HBM, HBM, VMEM, HBM, HBM, HBM],
        scratch_shapes=[item for group in groups for item in group],
        compiler_params=pltpu.CompilerParams(
            collective_id=collective, has_side_effects=True, vmem_limit_bytes=60 * MIB
        ),
        cost_estimate=pl.CostEstimate(
            flops=8 * length * inner * D, bytes_accessed=16 * length * D, transcendentals=0
        ),
    )(gate_grad, up_grad, gate_full, up_full, inputs, gain, upstream, attn_raw)
    return out[:5]


class Total:
    def __init__(self, land, send, recv):
        self.land, self.send, self.recv = land, send, recv
        self.count = lax.axis_size("gx")

    @staticmethod
    def scratch(length):
        others = lax.axis_size("gx") - 1
        return [
            pltpu.VMEM((others, 8, length), WIDE),
            pltpu.SemaphoreType.DMA((others,)),
            pltpu.SemaphoreType.DMA((others,)),
        ]

    def copies(self, mine):
        return [
            remote(
                mine,
                self.land.at[shift - 1],
                self.send.at[shift - 1],
                self.recv.at[shift - 1],
                {"gx": rank_at(shift)},
            )
            for shift in range(1, self.count)
        ]

    def start(self, mine):
        for item in self.copies(mine):
            item.start()

    def finish(self, mine):
        for item in self.copies(mine):
            item.wait()
        total = mine[...]
        for shift in range(1, self.count):
            total = total + self.land[shift - 1]
        return total


def gather_in(tokens, stack, output_shard, gains, collective):
    length, width = tokens.shape
    _, shard, side = stack.shape
    columns = 2 * side
    count = lax.axis_size("gy")
    chunks = count
    rows = length // chunks
    chips = lax.axis_size("gx") // 2
    parts = 1
    out_columns = output_shard.shape[1]
    out_rows = width // 2
    ahead = chunks // 2 - 1

    groups = [
        RingGather.scratch(parts),
        [
            pltpu.SemaphoreType.DMA((1,)),
            pltpu.SemaphoreType.DMA((2,)),
            pltpu.SemaphoreType.DMA((chips - 1, chunks, 2)),
            pltpu.SemaphoreType.DMA((chips - 1, chunks, 2)),
        ],
        [
            pltpu.VMEM((2, D, side), LOW),
            pltpu.VMEM((2 * chips, length, width), LOW),
            pltpu.VMEM((2, 2, rows, width), WIDE),
            pltpu.VMEM((2, rows, width), LOW),
            pltpu.VMEM((length, STATS), WIDE),
            pltpu.VMEM((8, length), WIDE),
            pltpu.SemaphoreType.DMA((2,)),
            pltpu.SemaphoreType.DMA((2, 3)),
        ],
        Total.scratch(length),
        [
            pltpu.VMEM((chips - 1, 8, width), WIDE),
            pltpu.SemaphoreType.DMA((chips - 1, 2)),
        ],
        RingGather.scratch(1),
        [pltpu.VMEM((count, width, out_columns), LOW)],
    ]

    def kernel(*refs):
        ins, outs, *scratch = take(refs, [4, 8] + [len(g) for g in groups])
        tokens, stack, output_shard, gains = ins
        whole, full, output_full, query_raw, key_raw, values, squares, halves = outs
        out_held = scratch[6][0]
        gain_land, gain_sems = scratch[4]
        own_sem, core_sems, cross_sems, pass_sems = scratch[1]
        weight, held, raw_buf, value_buf, stats, mine = scratch[2][:6]
        copy_sems, out_sems = scratch[2][6:]
        total = Total(*scratch[3])

        def slot(way, owner, part):
            return weight.at[way, pl.ds(aligned(owner * shard, shard), shard)]

        def spill(way, owner, part):
            return full.at[way, pl.ds(aligned(owner * shard, shard), shard)]

        def source(way, part):
            return stack.at[way]

        ring = RingGather(source, slot, spill, parts, *scratch[0])

        def out_slot(way, owner, part):
            return out_held.at[owner, way * out_rows : (way + 1) * out_rows]

        def out_spill(way, owner, part):
            at = pl.ds(aligned(owner * out_columns, out_columns), out_columns)
            return output_full.at[way * out_rows : (way + 1) * out_rows, at]

        def out_source(way, part):
            return output_shard.at[way * out_rows : (way + 1) * out_rows]

        out_ring = RingGather(out_source, out_slot, out_spill, 1, *scratch[5])

        def block(rank, chunk):
            if chunk is None:
                return held.at[rank]
            return held.at[rank, row_slice(chunk, rows)]

        here = lax.axis_index("gx")
        own = pltpu.make_async_copy(tokens, block(here, None), own_sem.at[0])
        core = remote(
            block(here, None), block(here, None), core_sems.at[0], core_sems.at[1], {"gx": other_core()}
        )

        def cross(shift, chunk):
            return remote(
                block(here, chunk),
                block(here, chunk),
                cross_sems.at[shift - 1, chunk, 0],
                cross_sems.at[shift - 1, chunk, 1],
                {"gx": peer_at(shift)},
            )

        def onward(shift, chunk):
            spot = block(peer_at(chips - shift), chunk)
            return remote(
                spot,
                spot,
                pass_sems.at[shift - 1, chunk, 0],
                pass_sems.at[shift - 1, chunk, 1],
                {"gx": other_core()},
            )

        gain_copies = [
            remote(
                gains,
                gain_land.at[shift - 1],
                gain_sems.at[shift - 1, 0],
                gain_sems.at[shift - 1, 1],
                {"gx": peer_at(shift)},
            )
            for shift in range(1, chips)
        ]
        own.start()
        greet("all", True)
        for item in gain_copies:
            item.start()
        ring.begin()
        own.wait()

        def send(chunk):
            for shift in range(1, chips):
                cross(shift, chunk).start()

        loop(chunks, send)
        core.start()

        def step(chunk):
            for shift in range(1, chips):
                cross(shift, chunk).wait_recv()
                onward(shift, chunk).start()

            @pl.when(chunk < ring.events)
            def _():
                ring.event(chunk)

            @pl.when(chunk == ahead - 1)
            def _():
                out_ring.begin()

            @pl.when(chunk >= ahead)
            def _():
                out_ring.event(chunk - ahead)

        loop(chunks, step)
        ring.end()

        def drain(chunk):
            for shift in range(1, chips):
                cross(shift, chunk).wait_send()
                onward(shift, chunk).wait()

        loop(chunks, drain)
        core.wait()
        whole_copy = pltpu.make_async_copy(held, whole, copy_sems.at[0])
        whole_copy.start()

        def stores(chunk):
            slot, at = lax.rem(chunk, 2), row_slice(chunk, rows)
            return [
                pltpu.make_async_copy(raw_buf.at[slot, 0], query_raw.at[at], out_sems.at[slot, 0]),
                pltpu.make_async_copy(raw_buf.at[slot, 1], key_raw.at[at], out_sems.at[slot, 1]),
                pltpu.make_async_copy(value_buf.at[slot], values.at[at], out_sems.at[slot, 2]),
            ]

        lane = lax.broadcasted_iota(jnp.int32, (rows, STATS), 1)

        def project(chunk):
            slot = lax.rem(chunk, 2)
            @pl.when(chunk >= 2)
            def _():
                for item in stores(chunk - 2):
                    item.wait()

            at = row_slice(chunk, rows)
            middle = side - width

            def against(way, columns):
                raw = jnp.zeros((rows, columns.stop - columns.start), WIDE)
                for rank in range(2 * chips):
                    raw = raw + jnp.dot(
                        held[rank, at],
                        weight[way, rank * width : (rank + 1) * width, columns],
                        preferred_element_type=WIDE,
                    )
                return raw

            some = []
            raw_buf[slot, 0] = against(0, slice(0, width))
            raw_buf[slot, 1, :, :middle] = against(0, slice(width, side))
            raw_buf[slot, 1, :, middle:] = against(1, slice(0, middle))
            value_buf[slot] = against(1, slice(middle, side)).astype(LOW)
            for which in range(2):
                raw = raw_buf[slot, which]
                some.append(jnp.sum(raw * raw, axis=1, keepdims=True))
            stats[row_slice(chunk, rows)] = jnp.where(lane == 0, some[0], some[1])
            for item in stores(chunk):
                item.start()

            @pl.when(chunk + chunks - ahead < out_ring.events)
            def _():
                out_ring.event(chunk + chunks - ahead)

        loop(chunks, project)
        mine[...] = stats[...].T[:8]
        total.start(mine)
        for chunk in (chunks - 2, chunks - 1):
            for item in stores(chunk):
                item.wait()
        squares[...] = total.finish(mine)
        whole_copy.wait()
        ring.settle()
        out_ring.end()
        out_ring.settle()
        halves[:, pl.ds(aligned(chip_here() * width, width), width)] = gains[...]
        for shift in range(1, chips):
            gain_copies[shift - 1].wait()
            chip = lax.rem(chip_here() + chips - shift, chips)
            halves[:, pl.ds(aligned(chip * width, width), width)] = gain_land[shift - 1]

    shape = jax.ShapeDtypeStruct
    return pl.pallas_call(
        kernel,
        out_shape=[
            shape((2 * chips, length, width), LOW),
            shape((2, shard * count, side), LOW),
            shape((width, D), LOW),
            shape((length, width), WIDE),
            shape((length, width), WIDE),
            shape((length, width), LOW),
            shape((8, length), WIDE),
            shape((8, chips * width), WIDE),
        ],
        in_specs=[HBM, HBM, HBM, VMEM],
        out_specs=[HBM] * 6 + [VMEM, VMEM],
        scratch_shapes=[item for group in groups for item in group],
        compiler_params=pltpu.CompilerParams(
            collective_id=collective, has_side_effects=True, vmem_limit_bytes=40 * MIB
        ),
        cost_estimate=pl.CostEstimate(
            flops=2 * length * columns * D, bytes_accessed=8 * length * D, transcendentals=0
        ),
    )(tokens, stack, output_shard, gains)


def hidden_back(blocks, down_first, down_second, hidden, silu, slope, collective):
    length, inner = hidden.shape
    count = lax.axis_size("gy")
    chunks = count
    rows = length // chunks
    shard = D // count
    side = inner // 2
    slots, parts = 3, 4
    piece = side // parts
    down_rows = down_first.shape[1]
    tile = min(512, inner)

    groups = [
        RingScatter.scratch(shard, side, slots, parts),
        [
            pltpu.VMEM((2, 2, rows, inner), LOW),
            pltpu.VMEM((2, 2, rows, inner), LOW),
            pltpu.SemaphoreType.DMA((2, 2)),
            pltpu.SemaphoreType.DMA((2, 2)),
            pltpu.SemaphoreType.DMA((2, parts)),
            pltpu.VMEM((count, shard, length), LOW),
            pltpu.VMEM((2, parts, piece, shard), WIDE),
        ],
        [
            pltpu.VMEM((length, D), LOW),
            pltpu.VMEM((inner, D), LOW),
            pltpu.SemaphoreType.DMA((blocks.shape[0],)),
            pltpu.SemaphoreType.DMA((2, count)),
        ],
    ]

    def kernel(*refs):
        ins, outs, *scratch = take(refs, [6, 3] + [len(g) for g in groups])
        blocks, down_first, down_second, hidden, silu, slope = ins
        grad, weight, grad_sems, weight_sems = scratch[2]
        gate_grad, up_grad, weight_grad = outs
        total, summed, land, ring_send, ring_recv, credit = scratch[0]
        given, made, given_sems, made_sems, out_sems, turned, final = scratch[1]

        def product(way, step, part):
            owner = ring.owner(way, step)

            @pl.when((part == 0) & ((step < count // 2) | (step == count - 1)))
            def _():
                turned[owner] = grad[:, pl.ds(aligned(owner * shard, shard), shard)].T

            columns = pl.ds(aligned(way * side + part * piece, piece), piece)
            total[way, part] = jnp.dot(
                turned[owner], hidden[:, columns], preferred_element_type=WIDE
            )

        ring = RingScatter(
            product, total, summed, land, ring_send, ring_recv, credit, slots, parts
        )

        def load(chunk):
            slot = lax.rem(chunk, 2)
            return [
                pltpu.make_async_copy(
                    (slope, silu)[which].at[row_slice(chunk, rows)],
                    given.at[slot, which],
                    given_sems.at[slot, which],
                )
                for which in range(2)
            ]

        def store(chunk):
            slot = lax.rem(chunk, 2)
            return [
                pltpu.make_async_copy(
                    made.at[slot, which],
                    (gate_grad, up_grad)[which].at[row_slice(chunk, rows)],
                    made_sems.at[slot, which],
                )
                for which in range(2)
            ]

        grad_copies = all_blocks(blocks, None, blocks.shape[2], grad, grad_sems)
        weight_copies = all_blocks(
            down_first, None, shard, weight.at[:down_rows], weight_sems.at[0]
        ) + all_blocks(down_second, None, shard, weight.at[down_rows:], weight_sems.at[1])
        for item in grad_copies + weight_copies + load(0):
            item.start()
        greet(False, True)
        for item in grad_copies:
            item.wait()

        def iteration(step):
            slot = lax.rem(step, 2)
            @pl.when(step + 1 < chunks)
            def _():
                for item in load(step + 1):
                    item.start()

            @pl.when(step >= 2)
            def _():
                for item in store(step - 2):
                    item.wait()

            for item in load(step):
                item.wait()

            each = parts // (inner // tile)

            @pl.loop(0, inner // tile)
            def _(index):
                for which in range(each):
                    ring.event(step * parts + index * each + which)

                @pl.when((step == 0) & (index == 0))
                def _():
                    for item in weight_copies:
                        item.wait()

                at = pl.ds(aligned(index * tile, tile), tile)
                hidden_grad = nt(grad[row_slice(step, rows)], weight[at])
                for which in range(2):
                    made[slot, which, :, at] = (
                        hidden_grad * given[slot, which, :, at].astype(WIDE)
                    ).astype(LOW)

            for item in store(step):
                item.start()

        loop(chunks, iteration)
        writes = [
            pltpu.make_async_copy(
                final.at[way, part],
                weight_grad.at[way * side + part * piece : way * side + (part + 1) * piece],
                out_sems.at[way, part],
            )
            for way in range(2)
            for part in range(parts)
        ]
        for way in range(2):
            for part in range(parts):
                final[way, part] = total[way, part].T
        for item in writes:
            item.start()
        for chunk in (chunks - 2, chunks - 1):
            for item in store(chunk):
                item.wait()
        ring.end()
        for item in writes:
            item.wait()

    shape = jax.ShapeDtypeStruct
    return pl.pallas_call(
        kernel,
        out_shape=[
            shape((length, inner), LOW),
            shape((length, inner), LOW),
            shape((inner, shard), WIDE),
        ],
        in_specs=[HBM, HBM, HBM, VMEM, HBM, HBM],
        out_specs=[HBM, HBM, HBM],
        scratch_shapes=[item for group in groups for item in group],
        compiler_params=pltpu.CompilerParams(
            collective_id=collective, has_side_effects=True, vmem_limit_bytes=60 * MIB
        ),
        cost_estimate=pl.CostEstimate(
            flops=4 * length * inner * D, bytes_accessed=16 * length * D, transcendentals=0
        ),
    )(blocks, down_first, down_second, hidden, silu, slope)


def attn_in_back(
    query_back,
    key_back,
    value_grad,
    query_raw,
    key_raw,
    factors,
    projections,
    query_gain,
    key_gain,
    stack,
    inputs,
    mixed_grad,
    gain_parts,
    collective,
):
    length, columns = value_grad.shape[0], 2 * stack.shape[2]
    width = mixed_grad.shape[1]
    count = lax.axis_size("gy")
    chunks = count
    rows = length // chunks
    shard = D // count
    side = columns // 2
    slots, parts = count - 1, 3
    piece = side // parts

    groups = [
        Reduce.scratch(rows, chunks, width, True),
        RingScatter.scratch(shard, side, slots, parts),
        [
            pltpu.VMEM((rows, width), WIDE),
            pltpu.VMEM((2, rows, width), WIDE),
            pltpu.VMEM((length, columns), LOW),
            pltpu.VMEM((length, STATS), WIDE),
            pltpu.VMEM((2, 4, rows, width), WIDE),
            pltpu.VMEM((2, D, side), LOW),
            pltpu.SemaphoreType.DMA((2, 4)),
            pltpu.SemaphoreType.DMA((2,)),
            pltpu.SemaphoreType.DMA((1,)),
            pltpu.SemaphoreType.DMA((2,)),
            pltpu.SemaphoreType.DMA((2, parts)),
        ],
        Columns.scratch(length, shard),
        Total.scratch(length),
        [
            pltpu.VMEM((8, width), WIDE),
            pltpu.VMEM((count - 1, 8, width), WIDE),
            pltpu.SemaphoreType.DMA((count - 1, 2)),
        ],
    ]

    def kernel(*refs):
        ins, outs, *scratch = take(refs, [16, 4] + [len(g) for g in groups])
        query_back, key_back, value_grad, query_raw, key_raw, factors = ins[:6]
        projections, query_gain, key_gain, full, inputs, mixed_grad = ins[6:12]
        gain_parts = ins[12:]
        token_grad, weight_grad, gain_grads, cross_land = outs
        gain_mine, gain_land, gain_sems = scratch[5]
        reduce = Reduce(scratch[0], cross_land, rows, width, True)
        total, summed, land, ring_send, ring_recv, credit = scratch[1]
        mixed_buf, token_buf, grads, projected, given, stack = scratch[2][:6]
        given_sems, whole_sems, mixed_sems, token_sems, out_sems = scratch[2][6:]
        left = Columns(inputs, shard, *scratch[3])
        total_sum = Total(*scratch[4])

        def product(way, step, part):
            @pl.when(part == 0)
            def _():
                left.take(ring, way, step)

            columns = pl.ds(aligned(way * side + part * piece, piece), piece)
            total[way, part] = jnp.dot(
                left.turned[way], grads[:, columns], preferred_element_type=WIDE
            )

        ring = RingScatter(
            product, total, summed, land, ring_send, ring_recv, credit, slots, parts
        )
        def load(chunk):
            slot, at = lax.rem(chunk, 2), row_slice(chunk, rows)
            return [
                pltpu.make_async_copy(
                    source.at[at], given.at[slot, which], given_sems.at[slot, which]
                )
                for which, source in enumerate((query_back, key_back, query_raw, key_raw))
            ]

        value_copy = pltpu.make_async_copy(value_grad, grads.at[:, 2 * width :], whole_sems.at[0])
        stack_copy = pltpu.make_async_copy(full, stack, whole_sems.at[1])
        left.copy(ring.owner(0, 0)).start()
        for item in load(0):
            item.start()
        value_copy.start()
        stack_copy.start()
        chip_columns = pl.ds(aligned(chip_here() * width, width), width)
        gain_mine[...] = jnp.zeros_like(gain_mine)
        for which, part in enumerate(gain_parts):
            gain_mine[which : which + 1] = part[...] if which < 2 else part[:, chip_columns]
        greet("all", False, True)
        total_sum.start(projections)
        gain_copies = [
            remote(
                gain_mine,
                gain_land.at[shift - 1],
                gain_sems.at[shift - 1, 0],
                gain_sems.at[shift - 1, 1],
                {"gy": block_at(shift)},
            )
            for shift in range(1, count)
        ]
        for item in gain_copies:
            item.start()
        sums_here = total_sum.finish(projections)
        projected[...] = jnp.concatenate([sums_here] * (STATS // 8), axis=0).T

        def form(chunk):
            slot = lax.rem(chunk, 2)

            @pl.when(chunk + 1 < chunks)
            def _():
                for item in load(chunk + 1):
                    item.start()

            for item in load(chunk):
                item.wait()

            def some(part):
                at = pl.ds(aligned(chunk * rows + part.start, 32), 32)
                for which, gain in enumerate((query_gain, key_gain)):
                    factor = factors[at, which : which + 1]
                    pull = factor * factor * factor * projected[at, which : which + 1] / D
                    back, raw = given[slot, which, part], given[slot, which + 2, part]
                    grads[at, which * width : (which + 1) * width] = (
                        factor * gain[...] * back - raw * pull
                    ).astype(LOW)

            tiles(rows, some)

        loop(chunks, form)
        value_copy.wait()

        def prepare(chunk):
            @pl.when(chunk == 0)
            def _():
                stack_copy.wait()

        def multiply(chunk, place):
            at = row_slice(chunk, rows)
            return nt(grads[at, :side], stack[0, pl.ds(place, width)]) + nt(
                grads[at, side:], stack[1, pl.ds(place, width)]
            )

        def mixed_copy(chunk):
            return pltpu.make_async_copy(
                mixed_grad.at[row_slice(chunk, rows)], mixed_buf, mixed_sems.at[0]
            )

        def token_copy(chunk):
            slot = lax.rem(chunk, 2)
            return pltpu.make_async_copy(
                token_buf.at[slot], token_grad.at[row_slice(chunk, rows)], token_sems.at[slot]
            )

        def fetch(chunk):
            @pl.when(chunk >= 1)
            def _():
                mixed_copy(chunk - 1).start()

        def sums(chunk):
            pass

        def finish(chunk):
            slot = lax.rem(chunk, 2)
            mixed_copy(chunk).wait()

            @pl.when(chunk >= 2)
            def _():
                token_copy(chunk - 2).wait()

            def some(at):
                token_buf[slot, at] = mixed_buf[at] + reduce.raw[at]

            tiles(rows, some)
            token_copy(chunk).start()

        schedule(chunks, reduce, multiply, fetch, sums, finish, ring.event, ring.events, prepare)
        writes = [
            pltpu.make_async_copy(
                total.at[way, part],
                weight_grad.at[:, way * side + part * piece : way * side + (part + 1) * piece],
                out_sems.at[way, part],
            )
            for way in range(2)
            for part in range(parts)
        ]
        for item in writes:
            item.start()
        gain_total = gain_mine[...]
        for shift in range(1, count):
            gain_copies[shift - 1].wait()
            gain_total = gain_total + gain_land[shift - 1]
        gain_grads[...] = gain_total
        ring.end()
        reduce.end(chunks)
        for chunk in (chunks - 2, chunks - 1):
            token_copy(chunk).wait()
        for item in writes:
            item.wait()

    shape = jax.ShapeDtypeStruct
    out = pl.pallas_call(
        kernel,
        out_shape=[
            shape((length, width), WIDE),
            shape((shard, columns), WIDE),
            shape((8, width), WIDE),
        ]
        + Reduce.landing(rows, chunks, width, True),
        in_specs=[HBM] * 5 + [VMEM] * 4 + [HBM] * 3 + [VMEM] * 4,
        out_specs=[HBM, HBM, VMEM, HBM],
        scratch_shapes=[item for group in groups for item in group],
        compiler_params=pltpu.CompilerParams(
            collective_id=collective, has_side_effects=True, vmem_limit_bytes=60 * MIB
        ),
        cost_estimate=pl.CostEstimate(
            flops=4 * length * columns * D, bytes_accessed=8 * length * D, transcendentals=0
        ),
    )(
        query_back,
        key_back,
        value_grad,
        query_raw,
        key_raw,
        factors,
        projections,
        query_gain,
        key_gain,
        stack,
        inputs,
        mixed_grad,
        *gain_parts,
    )
    return out[:3]


def token_positions(segment):
    length = segment.shape[0]
    labels = jnp.arange(SEGS, dtype=jnp.int32)
    member = (segment[:, None] == labels[None, :]).astype(jnp.int32)
    totals = jnp.sum(member, axis=0)
    starts = jnp.cumsum(totals) - totals
    opening = jnp.sum(member * starts[None, :], axis=1)
    return jnp.arange(length, dtype=jnp.int32) - opening


def rotary_tables(segment):
    place = token_positions(segment).astype(jnp.float32)
    halves = HEAD // 2
    inverse = jnp.exp(jnp.arange(halves, dtype=jnp.float32) * (-2.0 * math.log(THETA) / HEAD))
    angle = place[:, None] * inverse[None, :]
    return (jnp.cos(angle), jnp.sin(angle))


BLOCK = 256
LANES = 128
SCALE = 1.0 / math.sqrt(HEAD)
SCALE_TWO = SCALE * math.log2(math.e)


def turn(values, cosine, sine):
    return values * cosine + pltpu.roll(values, HEAD // 2, 1) * sine


def head_columns(head):
    return slice(head * HEAD, (head + 1) * HEAD)


def nt(left, right):
    return lax.dot_general(left, right, (((1,), (1,)), ((), ())), preferred_element_type=WIDE)


def attend(first_block, query_raw, key_raw, values, factors, query_gain, key_gain, tables, starts):
    length, width = query_raw.shape
    heads = width // HEAD

    def kernel(
        first_block,
        query_raw,
        key_raw,
        values,
        factors,
        query_gain,
        key_gain,
        cosine,
        sine,
        starts,
        queries,
        keys,
        attended,
        peaks,
        peak_columns,
    ):
        @pl.loop(0, length // BLOCK)
        def _(index):
            at = row_slice(index, BLOCK)
            cos, sin = cosine[at], sine[at]
            pairs = ((query_raw, query_gain, queries), (key_raw, key_gain, keys))
            for which, (raw, gain, out) in enumerate(pairs):
                factor = factors[at, which : which + 1]
                for head in range(heads):
                    columns = head_columns(head)
                    normed = raw[at, columns] * factor * gain[:, columns]
                    out[at, columns] = turn(normed, cos, sin).astype(LOW)

        lane = lax.broadcasted_iota(jnp.int32, (BLOCK, LANES), 1)
        row_index = lax.broadcasted_iota(jnp.int32, (BLOCK, BLOCK), 0)
        column_index = lax.broadcasted_iota(jnp.int32, (BLOCK, BLOCK), 1)

        def query_block(index):
            at = row_slice(index, BLOCK)
            start = starts[at]

            def key_block(other, carry):
                there = row_slice(other, BLOCK)
                key_place = column_index + other * BLOCK
                allowed = (key_place >= start) & (key_place <= row_index + index * BLOCK)
                made = []
                for head in range(heads):
                    columns = head_columns(head)
                    peak, total, rows = carry[head]
                    scores = nt(queries[at, columns], keys[there, columns]) * SCALE_TWO
                    scores = jnp.where(allowed, scores, NEGATIVE)
                    higher = jnp.maximum(peak, jnp.max(scores, axis=1, keepdims=True))
                    raised = jnp.exp2(scores - higher)
                    shrink = jnp.exp2(peak - higher)
                    total = total * shrink + jnp.sum(raised, axis=1, keepdims=True)
                    rows = rows * shrink + jnp.dot(
                        raised.astype(LOW), values[there, columns], preferred_element_type=WIDE
                    )
                    made.append((higher, total, rows))
                return tuple(made)

            empty = (
                jnp.full((BLOCK, 1), NEGATIVE, WIDE),
                jnp.zeros((BLOCK, 1), WIDE),
                jnp.zeros((BLOCK, HEAD), WIDE),
            )
            done = lax.fori_loop(first_block[index], index + 1, key_block, (empty,) * heads)
            column = jnp.zeros((BLOCK, LANES), WIDE)
            for head in range(heads):
                peak, total, rows = done[head]
                attended[at, head_columns(head)] = (rows / total).astype(LOW)
                column = jnp.where(lane == head, peak + jnp.log2(total), column)
            peak_columns[at] = column

        loop(length // BLOCK, query_block)
        peaks[...] = peak_columns[...].T[:8]

    shape = jax.ShapeDtypeStruct
    smem = pl.BlockSpec(memory_space=pltpu.SMEM)
    return pl.pallas_call(
        kernel,
        out_shape=[
            shape((length, width), LOW),
            shape((length, width), LOW),
            shape((length, width), LOW),
            shape((8, length), WIDE),
        ],
        in_specs=[smem] + [VMEM] * 9,
        out_specs=[VMEM] * 4,
        scratch_shapes=[pltpu.VMEM((length, LANES), WIDE)],
        compiler_params=pltpu.CompilerParams(vmem_limit_bytes=48 * MIB),
        cost_estimate=pl.CostEstimate(
            flops=2 * length * MAX_LEN * width,
            bytes_accessed=16 * length * width,
            transcendentals=length * MAX_LEN * heads // 2,
        ),
    )(first_block, query_raw, key_raw, values, factors, query_gain, key_gain, *tables, starts)


def attend_back(
    last_block,
    queries,
    keys,
    values,
    attended,
    upstream,
    peaks,
    query_raw,
    key_raw,
    factors,
    query_gain,
    key_gain,
    tables,
    start_row,
    finished,
):
    length, width = query_raw.shape
    heads = width // HEAD

    extra = len(finished)

    def kernel(*refs):
        finished_in = refs[15 : 15 + extra]
        finished_out = refs[21 + extra : 21 + 2 * extra]
        copy_sems = refs[-1]
        copies = [
            pltpu.make_async_copy(finished_in[i], finished_out[i], copy_sems.at[i])
            for i in range(extra)
        ]
        for item in copies:
            item.start()
        work(*refs[:15], *refs[15 + extra : 21 + extra], *refs[21 + 2 * extra : -1])
        for item in copies:
            item.wait()

    def work(
        last_block,
        queries,
        keys,
        values,
        attended,
        upstream,
        peaks,
        query_raw,
        key_raw,
        factors,
        query_gain,
        key_gain,
        cosine,
        sine,
        start_row,
        query_out,
        key_out,
        value_out,
        projections,
        query_gain_grad,
        key_gain_grad,
        query_sum,
        key_sum,
        value_sum,
        columns_scratch,
        deltas,
    ):
        lane = lax.broadcasted_iota(jnp.int32, (BLOCK, LANES), 1)
        query_gain_grad[...] = jnp.zeros_like(query_gain_grad)
        key_gain_grad[...] = jnp.zeros_like(key_gain_grad)

        def prepare(index):
            at = row_slice(index, BLOCK)
            column = jnp.zeros((BLOCK, LANES), WIDE)
            for head in range(heads):
                columns = head_columns(head)
                delta = jnp.sum(
                    attended[at, columns].astype(WIDE) * upstream[at, columns].astype(WIDE),
                    axis=1,
                    keepdims=True,
                )
                column = jnp.where(lane == head, delta, column)
            columns_scratch[at] = column
            query_sum[at] = jnp.zeros((BLOCK, width), WIDE)

        loop(length // BLOCK, prepare)
        deltas[...] = columns_scratch[...].T[:8]
        row_index = lax.broadcasted_iota(jnp.int32, (BLOCK, BLOCK), 0)
        column_index = lax.broadcasted_iota(jnp.int32, (BLOCK, BLOCK), 1)

        def turn_back(at, summed, raw, gain, factor, out, gain_grad):
            cos, sin = cosine[at], sine[at]
            share = jnp.zeros((BLOCK, 1), WIDE)
            for head in range(heads):
                columns = head_columns(head)
                normed = turn(summed(head) * SCALE, cos, -sin)
                out[at, columns] = normed
                weighed = normed * raw[at, columns]
                share += jnp.sum(gain[:, columns] * weighed, axis=1, keepdims=True)
                gain_grad[:, columns] += jnp.sum(weighed * factor, axis=0, keepdims=True)
            return share

        def key_block(index):
            at = row_slice(index, BLOCK)
            key_sum[...] = jnp.zeros_like(key_sum)
            value_sum[...] = jnp.zeros_like(value_sum)

            def query_block(other, carry):
                there = row_slice(other, BLOCK)
                key_place = row_index + index * BLOCK
                allowed = (key_place >= start_row[:, there]) & (
                    key_place <= column_index + other * BLOCK
                )
                for head in range(heads):
                    columns = head_columns(head)
                    scores = nt(keys[at, columns], queries[there, columns]) * SCALE_TWO
                    scores = jnp.where(allowed, scores, NEGATIVE)
                    chance = jnp.exp2(scores - peaks[head : head + 1, there])
                    value_sum[:, columns] += jnp.dot(
                        chance.astype(LOW), upstream[there, columns], preferred_element_type=WIDE
                    )
                    chance_grad = nt(values[at, columns], upstream[there, columns])
                    score_grad = (chance * (chance_grad - deltas[head : head + 1, there])).astype(LOW)
                    key_sum[:, columns] += jnp.dot(
                        score_grad, queries[there, columns], preferred_element_type=WIDE
                    )
                    query_sum[there, columns] += lax.dot_general(
                        score_grad,
                        keys[at, columns],
                        (((0,), (0,)), ((), ())),
                        preferred_element_type=WIDE,
                    )
                return carry

            lax.fori_loop(index, last_block[index] + 1, query_block, 0)
            value_out[at] = value_sum[...].astype(LOW)
            share = turn_back(
                at,
                lambda head: key_sum[:, head_columns(head)],
                key_raw,
                key_gain,
                factors[at, 1:2],
                key_out,
                key_gain_grad,
            )
            columns_scratch[at] = jnp.where(lane == 1, share, 0.0)

        loop(length // BLOCK, key_block)

        def finish(index):
            at = row_slice(index, BLOCK)
            share = turn_back(
                at,
                lambda head: query_sum[at, head_columns(head)],
                query_raw,
                query_gain,
                factors[at, 0:1],
                query_out,
                query_gain_grad,
            )
            columns_scratch[at] += jnp.where(lane == 0, share, 0.0)

        loop(length // BLOCK, finish)
        projections[...] = columns_scratch[...].T[:8]

    shape = jax.ShapeDtypeStruct
    smem = pl.BlockSpec(memory_space=pltpu.SMEM)
    return pl.pallas_call(
        kernel,
        out_shape=[
            shape((length, width), WIDE),
            shape((length, width), WIDE),
            shape((length, width), LOW),
            shape((8, length), WIDE),
            shape((1, width), WIDE),
            shape((1, width), WIDE),
        ]
        + [shape(item.shape, item.dtype) for item in finished],
        in_specs=[smem] + [VMEM] * 14 + [HBM] * extra,
        out_specs=[VMEM] * 6 + [HBM] * extra,
        scratch_shapes=[
            pltpu.VMEM((length, width), WIDE),
            pltpu.VMEM((BLOCK, width), WIDE),
            pltpu.VMEM((BLOCK, width), WIDE),
            pltpu.VMEM((length, LANES), WIDE),
            pltpu.VMEM((8, length), WIDE),
            pltpu.SemaphoreType.DMA((extra,)),
        ],
        compiler_params=pltpu.CompilerParams(vmem_limit_bytes=52 * MIB),
        cost_estimate=pl.CostEstimate(
            flops=5 * length * MAX_LEN * width,
            bytes_accessed=32 * length * width,
            transcendentals=length * MAX_LEN * heads // 2,
        ),
    )(
        last_block,
        queries,
        keys,
        values,
        attended,
        upstream,
        peaks,
        query_raw,
        key_raw,
        factors,
        query_gain,
        key_gain,
        *tables,
        start_row,
        *finished,
    )


def shards(
    tokens,
    query_weight,
    key_weight,
    value_weight,
    output_weight,
    gate_weight,
    up_weight,
    down_weight,
    query_gain,
    key_gain,
    attn_gain,
    mlp_gain,
    seq_ids,
    out_grad,
):
    segment = seq_ids[0]
    length = tokens.shape[0]
    local_width = tokens.shape[1]
    cosine, sine = rotary_tables(segment)
    tables = (
        jnp.concatenate([cosine, cosine], axis=1),
        jnp.concatenate([-sine, sine], axis=1),
    )
    order = jnp.arange(length, dtype=jnp.int32)
    starts = order - token_positions(segment)
    blocks = length // BLOCK
    first_block = starts.reshape(blocks, BLOCK)[:, 0] // BLOCK
    closing = segment.reshape(blocks, BLOCK)[:, -1]
    ends = jnp.sum((segment[None, :] <= closing[:, None]).astype(jnp.int32), axis=1) - 1
    last_block = ends // BLOCK
    gains = jnp.concatenate([attn_gain[None], mlp_gain[None], jnp.zeros((6, local_width))], axis=0)
    query_gain, key_gain = query_gain.reshape(1, -1), key_gain.reshape(1, -1)
    middle = local_width // 2
    pairs = (
        (query_weight, key_weight[:, :middle]),
        (key_weight[:, middle:], value_weight),
    )
    stack = jnp.stack([jnp.concatenate(pair, axis=1) for pair in pairs])
    inputs, attn_stack, output_full, query_raw, key_raw, values, squares, halves = gather_in(
        tokens, stack, output_weight, gains, 1
    )
    attn_half, mlp_half = halves[:1], halves[1:2]
    middle = down_weight.shape[0] // 2
    squares, down_rows = lax.optimization_barrier((squares, down_weight[middle:]))
    down_second = lax.all_gather(down_rows, "gy", axis=0)
    factors = lax.rsqrt(squares[:2].T / D + EPS)
    queries, keys, attended, peaks = attend(
        first_block,
        query_raw,
        key_raw,
        values,
        factors,
        query_gain,
        key_gain,
        tables,
        starts[:, None],
    )
    attn_raw, mixed, mlp_inputs, gate_full, up_full, down_first, upstream = attn_out(
        attended, output_full, attn_half, inputs, out_grad, gate_weight, up_weight, down_weight[:middle], 2
    )
    result, mlp_full, mlp_gain_part, hidden, silu, slope = mlp_forward(
        mlp_inputs, gate_full, up_full, down_first, down_second, mlp_half, mixed, upstream, 3
    )
    gate_grad, up_grad, down_weight_grad = hidden_back(
        mlp_full, down_first, down_second, hidden, silu, slope, 4
    )
    mixed_grad, attn_full, attn_gain_part, gate_weight_grad, up_weight_grad = mlp_back(
        gate_grad, up_grad, gate_full, up_full, mlp_inputs, attn_half, upstream, attn_raw, 5
    )
    output_product = lax.dot_general(
        attended, attn_full, (((0,), (0,)), ((), ())), preferred_element_type=jnp.float32
    )
    output_weight_grad = lax.psum_scatter(
        output_product.astype(jnp.bfloat16), "gy", scatter_dimension=1, tiled=True
    ).astype(jnp.float32)
    attended_grad = lax.dot_general(
        attn_full, output_full, (((1,), (1,)), ((), ())), preferred_element_type=jnp.float32
    ).astype(jnp.bfloat16)
    query_back, key_back, value_grad, projections, query_gain_part, key_gain_part, *done = attend_back(
        last_block,
        queries,
        keys,
        values,
        attended,
        attended_grad,
        peaks,
        query_raw,
        key_raw,
        factors,
        query_gain,
        key_gain,
        tables,
        starts[None, :],
        (result, gate_weight_grad, up_weight_grad, down_weight_grad),
    )
    result, gate_weight_grad, up_weight_grad, down_weight_grad = done
    token_grad, attn_weight_grads, gain_grads = attn_in_back(
        query_back,
        key_back,
        value_grad,
        query_raw,
        key_raw,
        factors,
        projections,
        query_gain,
        key_gain,
        attn_stack,
        inputs,
        mixed_grad,
        (query_gain_part, key_gain_part, attn_gain_part, mlp_gain_part),
        6,
    )
    query_weight_grad = attn_weight_grads[:, :local_width]
    key_weight_grad = attn_weight_grads[:, local_width : 2 * local_width]
    value_weight_grad = attn_weight_grads[:, 2 * local_width :]
    query_gain_grad, key_gain_grad, attn_gain_grad, mlp_gain_grad = (gain_grads[i] for i in range(4))
    return (
        result,
        token_grad,
        query_weight_grad,
        key_weight_grad,
        value_weight_grad,
        output_weight_grad,
        gate_weight_grad,
        up_weight_grad,
        down_weight_grad,
        query_gain_grad,
        key_gain_grad,
        attn_gain_grad,
        mlp_gain_grad,
    )


def solution(mesh):
    return jax.shard_map(
        shards,
        mesh=mesh,
        in_specs=(
            P("gy", "gx"),
            P("gy", "gx"),
            P("gy", "gx"),
            P("gy", "gx"),
            P("gx", "gy"),
            P("gy", "gx"),
            P("gy", "gx"),
            P("gx", "gy"),
            P("gx"),
            P("gx"),
            P("gx"),
            P("gx"),
            P("gy", None),
            P("gy", "gx"),
        ),
        out_specs=(
            P("gy", "gx"),
            P("gy", "gx"),
            P("gy", "gx"),
            P("gy", "gx"),
            P("gy", "gx"),
            P("gx", "gy"),
            P("gy", "gx"),
            P("gy", "gx"),
            P("gx", "gy"),
            P("gx"),
            P("gx"),
            P("gx"),
            P("gx"),
        ),
        check_vma=False,
    )
```

```python
import math

import jax
import jax.numpy as jnp
from jax import lax
from jax.experimental import pallas as pl
from jax.experimental.pallas import tpu as pltpu
from jax.sharding import PartitionSpec as P

D = 2048
HEAD = 128
MAX_LEN = 1024
SEGS = 4


EPS = 1e-06
THETA = 500000.0
NEGATIVE = -1e30


MESH = pl.DeviceIdType.MESH
HBM = pl.BlockSpec(memory_space=pltpu.HBM)
VMEM = pl.BlockSpec(memory_space=pltpu.VMEM)
LOW = jnp.bfloat16
WIDE = jnp.float32
MIB = 1 << 20
LAG = 2
STATS = 128


def core_here():
    return lax.rem(lax.axis_index("gx"), 2)


def chip_here():
    return lax.div(lax.axis_index("gx"), 2)


def other_core():
    return lax.axis_index("gx") + 1 - 2 * core_here()


def peer_at(shift):
    return lax.rem(lax.axis_index("gx") + 2 * shift, lax.axis_size("gx"))


def rank_at(shift):
    return lax.rem(lax.axis_index("gx") + shift, lax.axis_size("gx"))


def block_at(shift):
    return lax.rem(lax.axis_index("gy") + shift, lax.axis_size("gy"))


def ring_place():
    count = lax.axis_size("gy")
    index = lax.axis_index("gy")
    row, side = lax.div(index, 2), lax.rem(index, 2)
    return side * row + (1 - side) * (count - 1 - row)


def ring_device(place):
    count = lax.axis_size("gy")
    place = lax.rem(place + 2 * count, count)
    back = lax.div(place, count // 2)
    row = (1 - back) * place + back * (count - 1 - place)
    return 2 * row + 1 - back


def greet(gx, ring, all_blocks=False):
    barrier = pltpu.get_barrier_semaphore()
    partners = []
    if all_blocks:
        partners += [{"gy": block_at(k)} for k in range(1, lax.axis_size("gy"))]
    if gx == "all":
        partners += [{"gx": rank_at(k)} for k in range(1, lax.axis_size("gx"))]
    elif gx:
        partners.append({"gx": other_core()})
        partners += [{"gx": peer_at(k)} for k in range(1, lax.axis_size("gx") // 2)]
    if ring:
        place = ring_place()
        partners += [{"gy": ring_device(place + 1)}, {"gy": ring_device(place - 1)}]
    for partner in partners:
        pl.semaphore_signal(barrier, inc=1, device_id=partner, device_id_type=MESH)
    pl.semaphore_wait(barrier, len(partners))


def remote(source, target, send, recv, device):
    return pltpu.make_async_remote_copy(
        src_ref=source,
        dst_ref=target,
        send_sem=send,
        recv_sem=recv,
        device_id=device,
        device_id_type=MESH,
    )


def loop(count, body):
    def step(index, carry):
        body(index)
        return carry

    lax.fori_loop(0, count, step, 0)


def aligned(value, factor):
    return pl.multiple_of(value, factor)


class RingGather:
    def __init__(self, sources, slot, spill, parts, send, recv, local, spilled):
        self.sources, self.slot, self.spill, self.parts = sources, slot, spill, parts
        self.send, self.recv, self.local, self.spilled = send, recv, local, spilled
        self.count = lax.axis_size("gy")

    @staticmethod
    def scratch(parts):
        count = lax.axis_size("gy")
        return [
            pltpu.SemaphoreType.DMA((count - 1, 2, parts)),
            pltpu.SemaphoreType.DMA((count - 1, 2, parts)),
            pltpu.SemaphoreType.DMA((2, parts)),
            pltpu.SemaphoreType.DMA((count, 2, parts)),
        ]

    def spill_copy(self, way, step, part):
        place = ring_place()
        owner = ring_device(place - (1 - 2 * way) * step)
        return pltpu.make_async_copy(
            self.slot(way, owner, part),
            self.spill(way, owner, part),
            self.spilled.at[step, way, part],
        )

    def copy(self, way, step, part, behind):
        place = ring_place()
        sign = 1 - 2 * way
        spot = self.slot(way, ring_device(place - sign * (step + behind)), part)
        return remote(
            spot,
            spot,
            self.send.at[step, way, part],
            self.recv.at[step, way, part],
            {"gy": ring_device(place + sign)},
        )

    def begin(self):
        place = [
            pltpu.make_async_copy(
                self.sources(way, part),
                self.slot(way, lax.axis_index("gy"), part),
                self.local.at[way, part],
            )
            for way in range(2)
            for part in range(self.parts)
        ]
        for item in place:
            item.start()
        for item in place:
            item.wait()
        for part in range(self.parts):
            for way in range(2):
                self.copy(way, 0, part, 0).start()
                self.spill_copy(way, 0, part).start()

    @property
    def events(self):
        return (self.count - 2) * self.parts

    def event(self, index):
        step = 1 + lax.div(index, self.parts)
        for part in range(self.parts):

            @pl.when(lax.rem(index, self.parts) == part)
            def _():
                for way in range(2):
                    self.copy(way, step - 1, part, 1).wait_recv()
                    self.copy(way, step, part, 0).start()
                    self.spill_copy(way, step, part).start()

    def end(self):
        for part in range(self.parts):
            for way in range(2):
                self.copy(way, self.count - 2, part, 1).wait_recv()
                self.spill_copy(way, self.count - 1, part).start()

        def drain(step):
            for part in range(self.parts):
                for way in range(2):
                    self.copy(way, step, part, 0).wait_send()

        loop(self.count - 1, drain)

    def settle(self):
        def drain(step):
            for part in range(self.parts):
                for way in range(2):
                    self.spill_copy(way, step, part).wait()

        loop(self.count, drain)


class RingScatter:
    def __init__(self, product, total, sums, land, send, recv, credit, slots, parts):
        self.product, self.total, self.sums, self.land = product, total, sums, land
        self.send, self.recv, self.credit = send, recv, credit
        self.slots, self.parts = slots, parts
        self.count = lax.axis_size("gy")
        self.rows = total.shape[2]

    @staticmethod
    def scratch(rows, columns, slots, parts):
        count = lax.axis_size("gy")
        return [
            pltpu.VMEM((2, parts, rows, columns // parts), WIDE),
            pltpu.VMEM((2, parts, rows, columns // parts), LOW),
            pltpu.VMEM((slots, 2, parts, rows, columns // parts), LOW),
            pltpu.SemaphoreType.DMA((count - 1, 2, parts)),
            pltpu.SemaphoreType.DMA((count - 1, 2, parts)),
            pltpu.SemaphoreType.REGULAR((2, parts)),
        ]

    def copy(self, way, step, part):
        place = ring_place()
        return remote(
            self.sums.at[way, part],
            self.land.at[lax.rem(step, self.slots), way, part],
            self.send.at[step, way, part],
            self.recv.at[step, way, part],
            {"gy": ring_device(place + 1 - 2 * way)},
        )

    def owner(self, way, step):
        sign = 1 - 2 * way
        return ring_device(ring_place() - sign * (1 + step))

    @property
    def events(self):
        return self.count * self.parts

    def event(self, index):
        step, part = lax.div(index, self.parts), lax.rem(index, self.parts)
        last = self.count - 1
        tile = min(self.rows, 32)

        for way in range(2):
            self.product(way, step, part)

        for way in range(2):

            slot = lax.rem(step - 1 + self.slots, self.slots)

            def over(body):
                @pl.loop(0, self.rows // tile)
                def _(index):
                    body(pl.ds(aligned(index * tile, tile), tile))

            @pl.when(step >= 1)
            def _():
                self.copy(way, step - 1, part).wait_recv()

            @pl.when((step >= 1) & (step < last))
            def _():
                self.copy(way, step - 1, part).wait_send()

            @pl.when(step == 0)
            def _():
                def first(rows):
                    self.sums[way, part, rows] = self.total[way, part, rows].astype(LOW)

                over(first)

            @pl.when((step >= 1) & (step < last))
            def _():
                def more(rows):
                    arrived = self.land[slot, way, part, rows].astype(WIDE)
                    self.sums[way, part, rows] = (self.total[way, part, rows] + arrived).astype(LOW)

                over(more)

            @pl.when(step == last)
            def _():
                def final(rows):
                    self.total[way, part, rows] += self.land[slot, way, part, rows].astype(WIDE)

                over(final)

            @pl.when((step >= 1) & (step - 1 + self.slots < last))
            def _():
                upstream = ring_device(ring_place() - (1 - 2 * way))
                pl.semaphore_signal(
                    self.credit.at[way, part],
                    inc=1,
                    device_id={"gy": upstream},
                    device_id_type=MESH,
                )

            @pl.when(step < last)
            def _():
                @pl.when(step >= self.slots)
                def _():
                    pl.semaphore_wait(self.credit.at[way, part], 1)

                self.copy(way, step, part).start()

    def end(self):
        for part in range(self.parts):
            for way in range(2):
                self.copy(way, self.count - 2, part).wait_send()


class Reduce:
    def __init__(self, refs, cross_land, rows, width, scatter):
        (
            self.keep,
            self.core_send,
            self.core_land,
            self.cross,
            self.cross_stage,
            self.raw,
            self.core_sems,
            self.cross_send_sems,
            self.cross_recv_sems,
            self.stage_sems,
        ) = refs
        self.cross_land = cross_land
        self.rows, self.width, self.scatter = rows, width, scatter
        self.chips = lax.axis_size("gx") // 2

    @staticmethod
    def scratch(rows, chunks, width, scatter):
        chips = lax.axis_size("gx") // 2
        half = chips * width
        part = width if scatter else half
        return [
            pltpu.VMEM((1, rows, half), LOW),
            pltpu.VMEM((2, rows, half), LOW),
            pltpu.VMEM((2, rows, half), LOW),
            pltpu.VMEM((LAG + 1, chips, rows, width) if scatter else (LAG + 1, rows, half), LOW),
            pltpu.VMEM((chips - 1, rows, part), LOW),
            pltpu.VMEM((rows, part), WIDE),
            pltpu.SemaphoreType.DMA((2, chunks)),
            pltpu.SemaphoreType.DMA((chips - 1, chunks)),
            pltpu.SemaphoreType.DMA((chips - 1, chunks)),
            pltpu.SemaphoreType.DMA((chips,)),
        ]

    @staticmethod
    def landing(rows, chunks, width, scatter):
        chips = lax.axis_size("gx") // 2
        half = chips * width
        part = width if scatter else half
        return [jax.ShapeDtypeStruct((chips - 1, chunks, rows, part), LOW)]

    def core_copy(self, chunk):
        return remote(
            self.core_send.at[lax.rem(chunk, 2)],
            self.core_land.at[lax.rem(chunk, 2)],
            self.core_sems.at[0, chunk],
            self.core_sems.at[1, chunk],
            {"gx": other_core()},
        )

    def cross_copy(self, shift, chunk):
        source = self.cross.at[lax.rem(chunk, LAG + 1)]
        if self.scatter:
            block = lax.rem(chip_here() + shift, self.chips)
            source = source.at[block]
        return remote(
            source,
            self.cross_land.at[shift - 1, chunk],
            self.cross_send_sems.at[shift - 1, chunk],
            self.cross_recv_sems.at[shift - 1, chunk],
            {"gx": peer_at(shift)},
        )

    def produce(self, chunk, dot):
        @pl.when(chunk >= 2)
        def _():
            self.core_copy(chunk - 2).wait_send()

        slot = lax.rem(chunk, 2)
        core = core_here()
        for chip in range(self.chips):
            place = aligned((2 * chip + 1 - core) * self.width, self.width)
            self.core_send[slot, :, chip * self.width : (chip + 1) * self.width] = dot(
                place
            ).astype(LOW)
        self.core_copy(chunk).start()
        for chip in range(self.chips):
            place = aligned((2 * chip + core) * self.width, self.width)
            self.keep[0, :, chip * self.width : (chip + 1) * self.width] = dot(
                place
            ).astype(LOW)

    def core_sum(self, chunk):
        slot, place = lax.rem(chunk, 2), lax.rem(chunk, LAG + 1)
        self.core_copy(chunk).wait_recv()

        @pl.when(chunk >= LAG + 1)
        def _():
            for shift in range(1, self.chips):
                self.cross_copy(shift, chunk - LAG - 1).wait_send()

        @pl.loop(0, self.rows // 32)
        def _(index):
            rows = pl.ds(aligned(index * 32, 32), 32)
            total = self.keep[0, rows].astype(WIDE) + self.core_land[slot, rows].astype(WIDE)
            if self.scatter:
                for chip in range(self.chips):
                    columns = slice(chip * self.width, (chip + 1) * self.width)
                    self.cross[place, chip, rows] = total[:, columns].astype(LOW)
            else:
                self.cross[place, rows] = total.astype(LOW)

        for shift in range(1, self.chips):
            self.cross_copy(shift, chunk).start()

    def cross_stage_copy(self, shift, chunk):
        return pltpu.make_async_copy(
            self.cross_land.at[shift - 1, chunk],
            self.cross_stage.at[shift - 1],
            self.stage_sems.at[shift],
        )

    def cross_fetch(self, chunk):
        for shift in range(1, self.chips):
            self.cross_copy(shift, chunk).wait_recv()
            self.cross_stage_copy(shift, chunk).start()

    def cross_sum(self, chunk):
        place = lax.rem(chunk, LAG + 1)
        for shift in range(1, self.chips):
            self.cross_stage_copy(shift, chunk).wait()

        @pl.loop(0, self.rows // 32)
        def _(index):
            rows = pl.ds(aligned(index * 32, 32), 32)
            if self.scatter:
                total = self.cross[place, chip_here(), rows].astype(WIDE)
            else:
                total = self.cross[place, rows].astype(WIDE)
            for shift in range(1, self.chips):
                total = total + self.cross_stage[shift - 1, rows].astype(WIDE)
            self.raw[rows] = total

    def end(self, chunks):
        for chunk in (chunks - 2, chunks - 1):
            self.core_copy(chunk).wait_send()
        for chunk in range(chunks - LAG - 1, chunks):
            for shift in range(1, self.chips):
                self.cross_copy(shift, chunk).wait_send()


class Stats:
    def __init__(self, mine, land, sems):
        self.mine, self.land, self.sems = mine, land, sems

    @staticmethod
    def scratch(rows, chunks):
        return [
            pltpu.VMEM((2, rows, STATS), WIDE),
            pltpu.VMEM((2, rows, STATS), WIDE),
            pltpu.SemaphoreType.DMA((2, chunks)),
        ]

    def copy(self, chunk):
        return remote(
            self.mine.at[lax.rem(chunk, 2)],
            self.land.at[lax.rem(chunk, 2)],
            self.sems.at[0, chunk],
            self.sems.at[1, chunk],
            {"gx": other_core()},
        )

    def clear(self, chunk):
        @pl.when(chunk >= 2)
        def _():
            self.copy(chunk - 2).wait_send()

    def put(self, chunk, rows, first, second):
        lane = lax.broadcasted_iota(jnp.int32, (first.shape[0], STATS), 1)
        self.mine[lax.rem(chunk, 2), rows] = jnp.where(lane < STATS // 2, first, second)

    def get(self, chunk, rows):
        total = self.mine[lax.rem(chunk, 2), rows] + self.land[lax.rem(chunk, 2), rows]
        return (total[:, :1], total[:, STATS // 2 : STATS // 2 + 1])

    def end(self, chunks):
        for chunk in (chunks - 2, chunks - 1):
            self.copy(chunk).wait_send()


class Spread:
    def __init__(self, buffer, whole, local, send, recv, rows, width):
        self.buffer, self.whole = buffer, whole
        self.local, self.send, self.recv = local, send, recv
        self.rows, self.width = rows, width
        self.chips = lax.axis_size("gx") // 2

    @staticmethod
    def scratch(rows, chunks, width):
        chips = lax.axis_size("gx") // 2
        return [
            pltpu.VMEM((2, chips, rows, width), LOW),
            pltpu.SemaphoreType.DMA((2, chips)),
            pltpu.SemaphoreType.DMA((chunks, chips)),
            pltpu.SemaphoreType.DMA((chunks, chips)),
        ]

    def pair(self, chunk, chip, core):
        slot = lax.rem(chunk, 2)
        source = self.buffer.at[slot, chip]
        rows = pl.ds(aligned(chunk * self.rows, self.rows), self.rows)
        rank = 2 * chip + core
        if len(self.whole.shape) == 3:
            target = self.whole.at[rank, rows]
        else:
            columns = pl.ds(aligned(rank * self.width, self.width), self.width)
            target = self.whole.at[rows, columns]
        here = pltpu.make_async_copy(source, target, self.local.at[slot, chip])
        away = remote(
            source,
            target,
            self.send.at[chunk, chip],
            self.recv.at[chunk, chip],
            {"gx": other_core()},
        )
        return (here, away)

    def put(self, chunk, rows, values):
        for chip in range(self.chips):
            columns = slice(chip * self.width, (chip + 1) * self.width)
            self.buffer[lax.rem(chunk, 2), chip, rows] = values[:, columns].astype(LOW)

    def clear(self, chunk):
        @pl.when(chunk >= 2)
        def _():
            self.settle(chunk - 2)

    def settle(self, chunk):
        for chip in range(self.chips):
            here, away = self.pair(chunk, chip, core_here())
            here.wait()
            away.wait_send()

    def go(self, chunk):
        for chip in range(self.chips):
            here, away = self.pair(chunk, chip, core_here())
            here.start()
            away.start()

    def end(self, chunks):
        for chunk in (chunks - 2, chunks - 1):
            self.settle(chunk)

        def arrive(chunk):
            for chip in range(self.chips):
                self.pair(chunk, chip, 1 - core_here())[1].wait_recv()

        loop(chunks, arrive)


def row_slice(chunk, rows):
    return pl.ds(aligned(chunk * rows, rows), rows)


def core_blocks(source, chunk, rows, width, buffer, sems):
    return [
        pltpu.make_async_copy(
            source.at[2 * chip + core_here(), row_slice(chunk, rows)],
            buffer.at[:, chip * width : (chip + 1) * width],
            sems.at[chip],
        )
        for chip in range(lax.axis_size("gx") // 2)
    ]


def all_blocks(source, rows, width, buffer, sems):
    return [
        pltpu.make_async_copy(
            source.at[rank] if rows is None else source.at[rank, rows],
            buffer.at[:, rank * width : (rank + 1) * width],
            sems.at[rank],
        )
        for rank in range(source.shape[0])
    ]


def tiles(rows, body):
    @pl.loop(0, rows // 32)
    def _(index):
        body(pl.ds(aligned(index * 32, 32), 32))


def schedule(chunks, reduce, multiply, fetch, sums, finish, event=None, events=0, prepare=None):
    steps = chunks + 1 + LAG

    def ring_events(place):
        if event is not None:
            low = lax.div(place * events, 2 * steps)
            high = lax.div((place + 1) * events, 2 * steps)

            def some(index, carry):
                event(index)
                return carry

            lax.fori_loop(low, high, some, 0)

    def iteration(step):
        ring_events(2 * step)

        @pl.when((step >= LAG) & (step < chunks + LAG))
        def _():
            reduce.cross_fetch(step - LAG)

        @pl.when(step >= LAG)
        def _():
            fetch(step - LAG)

        @pl.when(step < chunks)
        def _():
            if prepare is not None:
                prepare(step)
            reduce.produce(step, lambda place: multiply(step, place))
            reduce.core_sum(step)

        ring_events(2 * step + 1)

        @pl.when(step >= 1 + LAG)
        def _():
            finish(step - 1 - LAG)

        @pl.when((step >= LAG) & (step < chunks + LAG))
        def _():
            reduce.cross_sum(step - LAG)
            sums(step - LAG)

    loop(steps, iteration)


def take(refs, counts):
    groups, start = [], 0
    for count in counts:
        groups.append(refs[start : start + count])
        start += count
    return groups


class Columns:
    def __init__(self, source, shard, left, turned, sem):
        self.source, self.shard = source, shard
        self.left, self.turned, self.sem = left, turned, sem

    @staticmethod
    def scratch(length, shard):
        return [
            pltpu.VMEM((length, shard), LOW),
            pltpu.VMEM((2, shard, length), LOW),
            pltpu.SemaphoreType.DMA((1,)),
        ]

    def copy(self, owner):
        each = self.source.shape[2] // self.shard
        at = pl.ds(aligned(lax.rem(owner, each) * self.shard, self.shard), self.shard)
        source = self.source.at[lax.div(owner, each), :, at]
        return pltpu.make_async_copy(source, self.left, self.sem.at[0])

    def take(self, ring, way, step):
        self.copy(ring.owner(way, step)).wait()
        self.turned[way] = self.left[...].T
        if way == 0:
            self.copy(ring.owner(1, step)).start()
        else:

            @pl.when(step + 1 < ring.count)
            def _():
                self.copy(ring.owner(0, step + 1)).start()


def attn_out(
    attended, weight, gain, tokens, out_grad, gate_shard, up_shard, down_shard, collective
):
    length, width = attended.shape
    chips = lax.axis_size("gx") // 2
    half = chips * width
    count = lax.axis_size("gy")
    chunks = count
    rows = length // chunks
    hidden = gate_shard.shape[1]
    inner = down_shard.shape[0]
    shard = gate_shard.shape[0]
    part_rows = shard // 2
    side = inner // 2
    down_columns = down_shard.shape[1]

    groups = [
        Reduce.scratch(rows, chunks, width, False),
        Stats.scratch(rows, chunks),
        Spread.scratch(rows, chunks, width),
        RingGather.scratch(3),
        [
            pltpu.VMEM((rows, half), LOW),
            pltpu.VMEM((2, rows, half), WIDE),
            pltpu.VMEM((2, rows, half), LOW),
            pltpu.SemaphoreType.DMA((chips,)),
            pltpu.SemaphoreType.DMA((2,)),
            pltpu.SemaphoreType.DMA((2,)),
            pltpu.SemaphoreType.DMA((2,)),
            pltpu.SemaphoreType.DMA((chips - 1, chunks, 2)),
        ],
        [
            pltpu.VMEM((2, D, hidden), LOW),
            pltpu.VMEM((count, inner, down_columns), LOW),
            pltpu.VMEM((chips, length, width), LOW),
        ],
    ]

    def kernel(*refs):
        ins, outs, *scratch = take(refs, [8, 8] + [len(g) for g in groups])
        attended, weight, gain, tokens, out_grad, gate_shard, up_shard, down_shard = ins
        raw_out, mixed_out, low_out, gate_full, up_full, down_full, upstream = outs[:7]
        cross_land = outs[7]
        reduce = Reduce(scratch[0], cross_land, rows, width, False)
        stats = Stats(*scratch[1])
        buffer, local, send, recv = scratch[2]
        spread = Spread(buffer, low_out, local, send, recv, rows, width)
        token_buf, mixed_buf, raw_buf = scratch[4][:3]
        token_sems, mixed_sems, raw_sems, own_sem, up_sems = scratch[4][3:]
        held, held_down, up_land = scratch[5]
        shards_here = (gate_shard, up_shard)

        def place_in(full, down):
            def slot(way, owner, part):
                if part == 2:
                    return down.at[owner, way * side : (way + 1) * side]
                base = owner * shard + part * part_rows
                return full[way].at[pl.ds(aligned(base, part_rows), part_rows)]

            return slot

        slot = place_in((held.at[0], held.at[1]), held_down)
        spill = place_in((gate_full, up_full), down_full)

        def source(way, part):
            if part == 2:
                return down_shard.at[way * side : (way + 1) * side]
            return shards_here[way].at[part * part_rows : (part + 1) * part_rows]

        ring = RingGather(source, slot, spill, 3, *scratch[3])
        own = pltpu.make_async_copy(out_grad, up_land.at[chip_here()], own_sem.at[0])
        up_spill = pltpu.make_async_copy(up_land, upstream, own_sem.at[1])

        def crossings(chunk):
            at = row_slice(chunk, rows)
            return [
                remote(
                    up_land.at[chip_here(), at],
                    up_land.at[chip_here(), at],
                    up_sems.at[shift - 1, chunk, 0],
                    up_sems.at[shift - 1, chunk, 1],
                    {"gx": peer_at(shift)},
                )
                for shift in range(1, chips)
            ]

        own.start()
        greet(True, True)
        ring.begin()
        own.wait()

        def multiply(chunk, place):
            return jnp.dot(
                attended[row_slice(chunk, rows)],
                weight[:, pl.ds(place, width)],
                preferred_element_type=WIDE,
            )

        def prepare(chunk):
            for item in crossings(chunk):
                item.start()

        def token_copies(chunk):
            return core_blocks(tokens, chunk, rows, width, token_buf, token_sems)

        def fetch(chunk):
            @pl.when(chunk >= 1)
            def _():
                for item in token_copies(chunk - 1):
                    item.start()

        def mixed_copy(chunk):
            slot = lax.rem(chunk, 2)
            return pltpu.make_async_copy(
                mixed_buf.at[slot, :, pl.ds(aligned(chip_here() * width, width), width)],
                mixed_out.at[row_slice(chunk, rows)],
                mixed_sems.at[slot],
            )

        def raw_copy(chunk):
            slot = lax.rem(chunk, 2)
            return pltpu.make_async_copy(
                raw_buf.at[slot], raw_out.at[row_slice(chunk, rows)], raw_sems.at[slot]
            )

        def sums(chunk):
            stats.clear(chunk)

            @pl.when(chunk >= 2)
            def _():
                raw_copy(chunk - 2).wait()

            def tile(at):
                raw = reduce.raw[at]
                raw_buf[lax.rem(chunk, 2), at] = raw.astype(LOW)
                squares = jnp.sum(raw * raw, axis=1, keepdims=True)
                stats.put(chunk, at, squares, squares)

            tiles(rows, tile)
            stats.copy(chunk).start()
            raw_copy(chunk).start()

        def finish(chunk):
            slot = lax.rem(chunk, 2)
            for item in token_copies(chunk):
                item.wait()
            stats.copy(chunk).wait_recv()
            spread.clear(chunk)

            @pl.when(chunk >= 2)
            def _():
                mixed_copy(chunk - 2).wait()

            def tile(at):
                squares, _ = stats.get(chunk, at)
                factor = lax.rsqrt(squares / D + EPS)
                mixed = token_buf[at].astype(WIDE) + reduce.raw[at] * factor * gain[...]
                mixed_buf[slot, at] = mixed
                spread.put(chunk, at, mixed)

            tiles(rows, tile)
            spread.go(chunk)
            mixed_copy(chunk).start()

        schedule(chunks, reduce, multiply, fetch, sums, finish, ring.event, ring.events, prepare)
        def drain(chunk):
            for item in crossings(chunk):
                item.wait()

        loop(chunks, drain)
        up_spill.start()
        ring.end()
        up_spill.wait()
        ring.settle()
        reduce.end(chunks)
        stats.end(chunks)
        spread.end(chunks)
        for chunk in (chunks - 2, chunks - 1):
            mixed_copy(chunk).wait()
            raw_copy(chunk).wait()

    shape = jax.ShapeDtypeStruct
    out = pl.pallas_call(
        kernel,
        out_shape=[
            shape((length, half), LOW),
            shape((length, width), WIDE),
            shape((2 * chips, length, width), LOW),
            shape((shard * count, hidden), LOW),
            shape((shard * count, hidden), LOW),
            shape((count, inner, down_columns), LOW),
            shape((chips, length, width), LOW),
        ]
        + Reduce.landing(rows, chunks, width, False),
        in_specs=[VMEM, VMEM, VMEM, HBM, HBM, HBM, HBM, HBM],
        out_specs=[HBM] * 8,
        scratch_shapes=[item for group in groups for item in group],
        compiler_params=pltpu.CompilerParams(
            collective_id=collective, has_side_effects=True, vmem_limit_bytes=60 * MIB
        ),
        cost_estimate=pl.CostEstimate(
            flops=2 * length * width * D, bytes_accessed=8 * length * D, transcendentals=0
        ),
    )(attended, weight, gain, tokens, out_grad, gate_shard, up_shard, down_shard)
    return out[:7]


def mlp_forward(
    inputs, gate_full, up_full, down_first, down_second, gain, mixed, upstream, collective
):
    length, inner = inputs.shape[1], gate_full.shape[1]
    width = mixed.shape[1]
    ranks = inputs.shape[0]
    down_columns = down_first.shape[2]
    down_rows = down_first.shape[1]
    chips = lax.axis_size("gx") // 2
    half = chips * width
    chunks = lax.axis_size("gy")
    rows = length // chunks
    tile = min(512, inner)
    pieces = inner // tile

    groups = [
        Reduce.scratch(rows, chunks, width, False),
        Stats.scratch(rows, chunks),
        Spread.scratch(rows, chunks, width),
        [
            pltpu.VMEM((2, rows, half), LOW),
            pltpu.VMEM((rows, width), WIDE),
            pltpu.VMEM((2, rows, width), LOW),
            pltpu.SemaphoreType.DMA((2, chips)),
            pltpu.SemaphoreType.DMA((1,)),
            pltpu.SemaphoreType.DMA((2,)),
        ],
        [
            pltpu.VMEM((D, inner), LOW),
            pltpu.VMEM((D, inner), LOW),
            pltpu.VMEM((inner, D), LOW),
            pltpu.VMEM((2, rows, D), LOW),
            pltpu.VMEM((2, 3, rows, inner), LOW),
            pltpu.SemaphoreType.DMA((pieces, 2)),
            pltpu.SemaphoreType.DMA((2, chunks)),
            pltpu.SemaphoreType.DMA((2, ranks)),
            pltpu.SemaphoreType.DMA((2, 3)),
        ],
    ]

    def kernel(*refs):
        ins, outs, *scratch = take(refs, [8, 7] + [len(g) for g in groups])
        inputs, gate_full, up_full, down_first, down_second, gain, mixed, upstream = ins
        result, grad_out, gain_grad, hidden_out, silu_out, slope_out, cross_land = outs
        gate_weight, up_weight, weight, row_buf, made = scratch[4][:5]
        piece_sems, weight_sem, row_sems, made_sems = scratch[4][5:]
        reduce = Reduce(scratch[0], cross_land, rows, width, False)
        stats = Stats(*scratch[1])
        buffer, local, send, recv = scratch[2]
        spread = Spread(buffer, grad_out, local, send, recv, rows, width)
        up_buf, mixed_buf, result_buf, up_sems, mixed_sems, result_sems = scratch[3]

        def piece_copies(piece):
            at = pl.ds(aligned(piece * tile, tile), tile)
            return [
                pltpu.make_async_copy(gate_full.at[:, at], gate_weight.at[:, at], piece_sems.at[piece, 0]),
                pltpu.make_async_copy(up_full.at[:, at], up_weight.at[:, at], piece_sems.at[piece, 1]),
            ]

        weight_copies = all_blocks(
            down_first, None, down_columns, weight.at[:down_rows], weight_sem.at[0]
        ) + all_blocks(down_second, None, down_columns, weight.at[down_rows:], weight_sem.at[1])

        def row_copy(chunk):
            slot = lax.rem(chunk, 2)
            return all_blocks(
                inputs, row_slice(chunk, rows), width, row_buf.at[slot], row_sems.at[slot]
            )

        def stores(chunk):
            slot, at = lax.rem(chunk, 2), row_slice(chunk, rows)
            return [
                pltpu.make_async_copy(made.at[slot, which], out.at[at], made_sems.at[slot, which])
                for which, out in enumerate((hidden_out, silu_out, slope_out))
            ]

        for item in row_copy(0):
            item.start()
        for piece in range(pieces):
            for item in piece_copies(piece):
                item.start()
        for item in weight_copies:
            item.start()
        greet(True, False)
        gain_grad[...] = jnp.zeros_like(gain_grad)

        def prepare(chunk):
            slot = lax.rem(chunk, 2)
            for item in row_copy(chunk):
                item.wait()

            @pl.when(chunk + 1 < chunks)
            def _():
                for item in row_copy(chunk + 1):
                    item.start()

            @pl.when(chunk >= 2)
            def _():
                for item in stores(chunk - 2):
                    item.wait()

            @pl.loop(0, pieces)
            def _(piece):
                @pl.when(chunk == 0)
                def _():
                    for item in piece_copies(piece):
                        item.wait()

                at = pl.ds(aligned(piece * tile, tile), tile)
                gate = jnp.dot(row_buf[slot], gate_weight[:, at], preferred_element_type=WIDE)
                up = jnp.dot(row_buf[slot], up_weight[:, at], preferred_element_type=WIDE)
                sigma = jax.nn.sigmoid(gate)
                silu = gate * sigma
                made[slot, 0, :, at] = (silu * up).astype(LOW)
                made[slot, 1, :, at] = silu.astype(LOW)
                made[slot, 2, :, at] = (up * (sigma + silu * (1.0 - sigma))).astype(LOW)

            @pl.when(chunk == 0)
            def _():
                for item in weight_copies:
                    item.wait()

            for item in stores(chunk):
                item.start()

        def multiply(chunk, place):
            return jnp.dot(
                made[lax.rem(chunk, 2), 0],
                weight[:, pl.ds(place, width)],
                preferred_element_type=WIDE,
            )

        def up_copy(chunk):
            slot = lax.rem(chunk, 2)
            return all_blocks(
                upstream, row_slice(chunk, rows), width, up_buf.at[slot], up_sems.at[slot]
            )

        def mixed_copy(chunk):
            return pltpu.make_async_copy(
                mixed.at[row_slice(chunk, rows)], mixed_buf, mixed_sems.at[0]
            )

        def result_copy(chunk):
            slot = lax.rem(chunk, 2)
            return pltpu.make_async_copy(
                result_buf.at[slot], result.at[row_slice(chunk, rows)], result_sems.at[slot]
            )

        def fetch(chunk):
            @pl.when(chunk < chunks)
            def _():
                for item in up_copy(chunk):
                    item.start()

            @pl.when(chunk >= 1)
            def _():
                mixed_copy(chunk - 1).start()

        def sums(chunk):
            slot = lax.rem(chunk, 2)
            stats.clear(chunk)
            for item in up_copy(chunk):
                item.wait()

            def tile(at):
                raw = reduce.raw[at]
                up = up_buf[slot, at].astype(WIDE)
                squares = jnp.sum(raw * raw, axis=1, keepdims=True)
                projected = jnp.sum(gain[...] * up * raw, axis=1, keepdims=True)
                stats.put(chunk, at, squares, projected)

            tiles(rows, tile)
            stats.copy(chunk).start()

        def finish(chunk):
            slot = lax.rem(chunk, 2)
            mixed_copy(chunk).wait()
            stats.copy(chunk).wait_recv()
            spread.clear(chunk)

            @pl.when(chunk >= 2)
            def _():
                result_copy(chunk - 2).wait()

            block = pl.ds(aligned(chip_here() * width, width), width)

            def tile(at):
                squares, projected = stats.get(chunk, at)
                factor = lax.rsqrt(squares / D + EPS)
                raw = reduce.raw[at]
                up = up_buf[slot, at].astype(WIDE)
                pull = factor * factor * factor * projected / D
                spread.put(chunk, at, factor * gain[...] * up - raw * pull)
                gain_grad[...] += jnp.sum(up * raw * factor, axis=0, keepdims=True)
                result_buf[slot, at] = (
                    mixed_buf[at] + reduce.raw[at, block] * factor * gain[:, block]
                ).astype(LOW)

            tiles(rows, tile)
            spread.go(chunk)
            result_copy(chunk).start()

        schedule(chunks, reduce, multiply, fetch, sums, finish, prepare=prepare)
        reduce.end(chunks)
        stats.end(chunks)
        spread.end(chunks)
        for chunk in (chunks - 2, chunks - 1):
            result_copy(chunk).wait()
            for item in stores(chunk):
                item.wait()

    shape = jax.ShapeDtypeStruct
    out = pl.pallas_call(
        kernel,
        out_shape=[
            shape((length, width), LOW),
            shape((2 * chips, length, width), LOW),
            shape((1, half), WIDE),
            shape((length, inner), LOW),
            shape((length, inner), LOW),
            shape((length, inner), LOW),
        ]
        + Reduce.landing(rows, chunks, width, False),
        in_specs=[HBM] * 5 + [VMEM, HBM, HBM],
        out_specs=[HBM, HBM, VMEM] + [HBM] * 4,
        scratch_shapes=[item for group in groups for item in group],
        compiler_params=pltpu.CompilerParams(
            collective_id=collective, has_side_effects=True, vmem_limit_bytes=60 * MIB
        ),
        cost_estimate=pl.CostEstimate(
            flops=6 * length * inner * D, bytes_accessed=16 * length * D, transcendentals=0
        ),
    )(inputs, gate_full, up_full, down_first, down_second, gain, mixed, upstream)
    return out[:6]


def mlp_back(gate_grad, up_grad, gate_full, up_full, inputs, gain, upstream, attn_raw, collective):
    length, inner = gate_grad.shape
    half = attn_raw.shape[1]
    chips = lax.axis_size("gx") // 2
    width = half // chips
    count = lax.axis_size("gy")
    chunks = count
    rows = length // chunks
    shard = D // count
    slots, parts = 2, 4
    piece = inner // parts

    groups = [
        Reduce.scratch(rows, chunks, width, False),
        Stats.scratch(rows, chunks),
        Spread.scratch(rows, chunks, width),
        RingScatter.scratch(shard, inner, slots, parts),
        [
            pltpu.VMEM((rows, half), LOW),
            pltpu.VMEM((2, rows, half), LOW),
            pltpu.SemaphoreType.DMA((chips,)),
            pltpu.SemaphoreType.DMA((2,)),
            pltpu.SemaphoreType.DMA((1,)),
            pltpu.SemaphoreType.DMA((2, parts)),
        ],
        Columns.scratch(length, shard),
        [
            pltpu.VMEM((2, length, inner), LOW),
            pltpu.VMEM((2, D, inner), LOW),
            pltpu.SemaphoreType.DMA((2, 2)),
        ],
    ]

    def kernel(*refs):
        ins, outs, *scratch = take(refs, [8, 6] + [len(g) for g in groups])
        gate_grad, up_grad, gate_full, up_full, inputs, gain, upstream, attn_raw = ins
        grads, weights, load_sems = scratch[6]
        grad_copies = [
            pltpu.make_async_copy((gate_grad, up_grad)[way], grads.at[way], load_sems.at[0, way])
            for way in range(2)
        ]
        weight_copies = [
            pltpu.make_async_copy((gate_full, up_full)[way], weights.at[way], load_sems.at[1, way])
            for way in range(2)
        ]
        mixed_out, grad_out, gain_grad, gate_out, up_out, cross_land = outs
        reduce = Reduce(scratch[0], cross_land, rows, width, False)
        stats = Stats(*scratch[1])
        buffer, local, send, recv = scratch[2]
        spread = Spread(buffer, grad_out, local, send, recv, rows, width)
        total, summed, land, ring_send, ring_recv, credit = scratch[3]
        up_buf, raw_buf, up_sems, raw_sems, mixed_sems, out_sems = scratch[4]
        left = Columns(inputs, shard, *scratch[5])

        def product(way, step, part):
            @pl.when(part == 0)
            def _():
                left.take(ring, way, step)

            @pl.when((part == 0) & (step == 0))
            def _():
                grad_copies[way].wait()

            columns = pl.ds(aligned(part * piece, piece), piece)
            total[way, part] = jnp.dot(
                left.turned[way], grads[way, :, columns], preferred_element_type=WIDE
            )

        ring = RingScatter(
            product, total, summed, land, ring_send, ring_recv, credit, slots, parts
        )
        left.copy(ring.owner(0, 0)).start()
        for item in grad_copies + weight_copies:
            item.start()
        greet(True, True)
        gain_grad[...] = jnp.zeros_like(gain_grad)

        def prepare(chunk):
            @pl.when(chunk == 0)
            def _():
                for item in weight_copies:
                    item.wait()

        def multiply(chunk, place):
            at = row_slice(chunk, rows)
            return nt(grads[0, at], weights[0, pl.ds(place, width)]) + nt(
                grads[1, at], weights[1, pl.ds(place, width)]
            )

        def up_copy(chunk):
            return all_blocks(upstream, row_slice(chunk, rows), width, up_buf, up_sems)

        def raw_copy(chunk):
            slot = lax.rem(chunk, 2)
            return pltpu.make_async_copy(
                attn_raw.at[row_slice(chunk, rows)], raw_buf.at[slot], raw_sems.at[slot]
            )

        def mixed_copy(chunk):
            return pltpu.make_async_copy(
                reduce.raw.at[:, pl.ds(aligned(chip_here() * width, width), width)],
                mixed_out.at[row_slice(chunk, rows)],
                mixed_sems.at[0],
            )

        def fetch(chunk):
            @pl.when(chunk < chunks)
            def _():
                for item in up_copy(chunk):
                    item.start()
                raw_copy(chunk).start()

        def sums(chunk):
            slot = lax.rem(chunk, 2)
            stats.clear(chunk)
            for item in up_copy(chunk):
                item.wait()
            raw_copy(chunk).wait()

            def tile(at):
                upward = reduce.raw[at] + up_buf[at].astype(WIDE)
                reduce.raw[at] = upward
                raw = raw_buf[slot, at].astype(WIDE)
                squares = jnp.sum(raw * raw, axis=1, keepdims=True)
                projected = jnp.sum(gain[...] * upward * raw, axis=1, keepdims=True)
                stats.put(chunk, at, squares, projected)

            tiles(rows, tile)
            stats.copy(chunk).start()
            mixed_copy(chunk).start()

        def finish(chunk):
            slot = lax.rem(chunk, 2)
            stats.copy(chunk).wait_recv()
            spread.clear(chunk)

            def tile(at):
                squares, projected = stats.get(chunk, at)
                factor = lax.rsqrt(squares / D + EPS)
                upward = reduce.raw[at]
                raw = raw_buf[slot, at].astype(WIDE)
                pull = factor * factor * factor * projected / D
                spread.put(chunk, at, factor * gain[...] * upward - raw * pull)
                gain_grad[...] += jnp.sum(upward * raw * factor, axis=0, keepdims=True)

            tiles(rows, tile)
            spread.go(chunk)
            mixed_copy(chunk).wait()

        schedule(chunks, reduce, multiply, fetch, sums, finish, ring.event, ring.events, prepare)
        writes = [
            pltpu.make_async_copy(
                total.at[way, part],
                (gate_out, up_out)[way].at[:, part * piece : (part + 1) * piece],
                out_sems.at[way, part],
            )
            for way in range(2)
            for part in range(parts)
        ]
        for item in writes:
            item.start()
        ring.end()
        reduce.end(chunks)
        stats.end(chunks)
        spread.end(chunks)
        for item in writes:
            item.wait()

    shape = jax.ShapeDtypeStruct
    out = pl.pallas_call(
        kernel,
        out_shape=[
            shape((length, width), WIDE),
            shape((length, D), LOW),
            shape((1, half), WIDE),
            shape((shard, inner), WIDE),
            shape((shard, inner), WIDE),
        ]
        + Reduce.landing(rows, chunks, width, False),
        in_specs=[HBM, HBM, HBM, HBM, HBM, VMEM, HBM, HBM],
        out_specs=[HBM, HBM, VMEM, HBM, HBM, HBM],
        scratch_shapes=[item for group in groups for item in group],
        compiler_params=pltpu.CompilerParams(
            collective_id=collective, has_side_effects=True, vmem_limit_bytes=60 * MIB
        ),
        cost_estimate=pl.CostEstimate(
            flops=8 * length * inner * D, bytes_accessed=16 * length * D, transcendentals=0
        ),
    )(gate_grad, up_grad, gate_full, up_full, inputs, gain, upstream, attn_raw)
    return out[:5]


class Total:
    def __init__(self, land, send, recv):
        self.land, self.send, self.recv = land, send, recv
        self.count = lax.axis_size("gx")

    @staticmethod
    def scratch(length):
        others = lax.axis_size("gx") - 1
        return [
            pltpu.VMEM((others, 8, length), WIDE),
            pltpu.SemaphoreType.DMA((others,)),
            pltpu.SemaphoreType.DMA((others,)),
        ]

    def copies(self, mine):
        return [
            remote(
                mine,
                self.land.at[shift - 1],
                self.send.at[shift - 1],
                self.recv.at[shift - 1],
                {"gx": rank_at(shift)},
            )
            for shift in range(1, self.count)
        ]

    def start(self, mine):
        for item in self.copies(mine):
            item.start()

    def finish(self, mine):
        for item in self.copies(mine):
            item.wait()
        total = mine[...]
        for shift in range(1, self.count):
            total = total + self.land[shift - 1]
        return total


def gather_in(tokens, stack, output_shard, gains, collective):
    length, width = tokens.shape
    _, shard, side = stack.shape
    columns = 2 * side
    count = lax.axis_size("gy")
    chunks = count
    rows = length // chunks
    chips = lax.axis_size("gx") // 2
    parts = 1
    out_columns = output_shard.shape[1]
    out_rows = width // 2
    ahead = chunks - 2

    groups = [
        RingGather.scratch(parts),
        [
            pltpu.SemaphoreType.DMA((1,)),
            pltpu.SemaphoreType.DMA((2,)),
            pltpu.SemaphoreType.DMA((chips - 1, chunks, 2)),
            pltpu.SemaphoreType.DMA((chips - 1, chunks, 2)),
        ],
        [
            pltpu.VMEM((2, D, side), LOW),
            pltpu.VMEM((2 * chips, length, width), LOW),
            pltpu.VMEM((2, 2, rows, width), WIDE),
            pltpu.VMEM((2, rows, width), LOW),
            pltpu.VMEM((length, STATS), WIDE),
            pltpu.VMEM((8, length), WIDE),
            pltpu.SemaphoreType.DMA((2,)),
            pltpu.SemaphoreType.DMA((2, 3)),
        ],
        Total.scratch(length),
        [
            pltpu.VMEM((chips - 1, 8, width), WIDE),
            pltpu.SemaphoreType.DMA((chips - 1, 2)),
        ],
        RingGather.scratch(1),
        [pltpu.VMEM((count, width, out_columns), LOW)],
    ]

    def kernel(*refs):
        ins, outs, *scratch = take(refs, [4, 8] + [len(g) for g in groups])
        tokens, stack, output_shard, gains = ins
        whole, full, output_full, query_raw, key_raw, values, squares, halves = outs
        out_held = scratch[6][0]
        gain_land, gain_sems = scratch[4]
        own_sem, core_sems, cross_sems, pass_sems = scratch[1]
        weight, held, raw_buf, value_buf, stats, mine = scratch[2][:6]
        copy_sems, out_sems = scratch[2][6:]
        total = Total(*scratch[3])

        def slot(way, owner, part):
            return weight.at[way, pl.ds(aligned(owner * shard, shard), shard)]

        def spill(way, owner, part):
            return full.at[way, pl.ds(aligned(owner * shard, shard), shard)]

        def source(way, part):
            return stack.at[way]

        ring = RingGather(source, slot, spill, parts, *scratch[0])

        def out_slot(way, owner, part):
            return out_held.at[owner, way * out_rows : (way + 1) * out_rows]

        def out_spill(way, owner, part):
            at = pl.ds(aligned(owner * out_columns, out_columns), out_columns)
            return output_full.at[way * out_rows : (way + 1) * out_rows, at]

        def out_source(way, part):
            return output_shard.at[way * out_rows : (way + 1) * out_rows]

        out_ring = RingGather(out_source, out_slot, out_spill, 1, *scratch[5])

        def block(rank, chunk):
            if chunk is None:
                return held.at[rank]
            return held.at[rank, row_slice(chunk, rows)]

        here = lax.axis_index("gx")
        own = pltpu.make_async_copy(tokens, block(here, None), own_sem.at[0])
        core = remote(
            block(here, None), block(here, None), core_sems.at[0], core_sems.at[1], {"gx": other_core()}
        )

        def cross(shift, chunk):
            return remote(
                block(here, chunk),
                block(here, chunk),
                cross_sems.at[shift - 1, chunk, 0],
                cross_sems.at[shift - 1, chunk, 1],
                {"gx": peer_at(shift)},
            )

        def onward(shift, chunk):
            spot = block(peer_at(chips - shift), chunk)
            return remote(
                spot,
                spot,
                pass_sems.at[shift - 1, chunk, 0],
                pass_sems.at[shift - 1, chunk, 1],
                {"gx": other_core()},
            )

        gain_copies = [
            remote(
                gains,
                gain_land.at[shift - 1],
                gain_sems.at[shift - 1, 0],
                gain_sems.at[shift - 1, 1],
                {"gx": peer_at(shift)},
            )
            for shift in range(1, chips)
        ]
        own.start()
        greet("all", True)
        for item in gain_copies:
            item.start()
        ring.begin()
        own.wait()

        def send(chunk):
            for shift in range(1, chips):
                cross(shift, chunk).start()

        loop(chunks, send)
        core.start()

        def step(chunk):
            for shift in range(1, chips):
                cross(shift, chunk).wait_recv()
                onward(shift, chunk).start()

            @pl.when(chunk < ring.events)
            def _():
                ring.event(chunk)

            @pl.when(chunk == ahead - 1)
            def _():
                out_ring.begin()

            @pl.when(chunk >= ahead)
            def _():
                out_ring.event(chunk - ahead)

        loop(chunks, step)
        ring.end()

        def drain(chunk):
            for shift in range(1, chips):
                cross(shift, chunk).wait_send()
                onward(shift, chunk).wait()

        loop(chunks, drain)
        core.wait()
        whole_copy = pltpu.make_async_copy(held, whole, copy_sems.at[0])
        whole_copy.start()

        def stores(chunk):
            slot, at = lax.rem(chunk, 2), row_slice(chunk, rows)
            return [
                pltpu.make_async_copy(raw_buf.at[slot, 0], query_raw.at[at], out_sems.at[slot, 0]),
                pltpu.make_async_copy(raw_buf.at[slot, 1], key_raw.at[at], out_sems.at[slot, 1]),
                pltpu.make_async_copy(value_buf.at[slot], values.at[at], out_sems.at[slot, 2]),
            ]

        lane = lax.broadcasted_iota(jnp.int32, (rows, STATS), 1)

        def project(chunk):
            slot = lax.rem(chunk, 2)
            @pl.when(chunk >= 2)
            def _():
                for item in stores(chunk - 2):
                    item.wait()

            at = row_slice(chunk, rows)
            middle = side - width

            def against(way, columns):
                raw = jnp.zeros((rows, columns.stop - columns.start), WIDE)
                for rank in range(2 * chips):
                    raw = raw + jnp.dot(
                        held[rank, at],
                        weight[way, rank * width : (rank + 1) * width, columns],
                        preferred_element_type=WIDE,
                    )
                return raw

            some = []
            raw_buf[slot, 0] = against(0, slice(0, width))
            raw_buf[slot, 1, :, :middle] = against(0, slice(width, side))
            raw_buf[slot, 1, :, middle:] = against(1, slice(0, middle))
            value_buf[slot] = against(1, slice(middle, side)).astype(LOW)
            for which in range(2):
                raw = raw_buf[slot, which]
                some.append(jnp.sum(raw * raw, axis=1, keepdims=True))
            stats[row_slice(chunk, rows)] = jnp.where(lane == 0, some[0], some[1])
            for item in stores(chunk):
                item.start()

            @pl.when(chunk + chunks - ahead < out_ring.events)
            def _():
                out_ring.event(chunk + chunks - ahead)

        loop(chunks, project)
        mine[...] = stats[...].T[:8]
        total.start(mine)
        for chunk in (chunks - 2, chunks - 1):
            for item in stores(chunk):
                item.wait()
        squares[...] = total.finish(mine)
        whole_copy.wait()
        ring.settle()
        out_ring.end()
        out_ring.settle()
        halves[:, pl.ds(aligned(chip_here() * width, width), width)] = gains[...]
        for shift in range(1, chips):
            gain_copies[shift - 1].wait()
            chip = lax.rem(chip_here() + chips - shift, chips)
            halves[:, pl.ds(aligned(chip * width, width), width)] = gain_land[shift - 1]

    shape = jax.ShapeDtypeStruct
    return pl.pallas_call(
        kernel,
        out_shape=[
            shape((2 * chips, length, width), LOW),
            shape((2, shard * count, side), LOW),
            shape((width, D), LOW),
            shape((length, width), WIDE),
            shape((length, width), WIDE),
            shape((length, width), LOW),
            shape((8, length), WIDE),
            shape((8, chips * width), WIDE),
        ],
        in_specs=[HBM, HBM, HBM, VMEM],
        out_specs=[HBM] * 6 + [VMEM, VMEM],
        scratch_shapes=[item for group in groups for item in group],
        compiler_params=pltpu.CompilerParams(
            collective_id=collective, has_side_effects=True, vmem_limit_bytes=40 * MIB
        ),
        cost_estimate=pl.CostEstimate(
            flops=2 * length * columns * D, bytes_accessed=8 * length * D, transcendentals=0
        ),
    )(tokens, stack, output_shard, gains)


def hidden_back(blocks, down_first, down_second, hidden, silu, slope, collective):
    length, inner = hidden.shape
    count = lax.axis_size("gy")
    chunks = count
    rows = length // chunks
    shard = D // count
    side = inner // 2
    slots, parts = 3, 4
    piece = side // parts
    down_rows = down_first.shape[1]
    tile = min(512, inner)

    groups = [
        RingScatter.scratch(shard, side, slots, parts),
        [
            pltpu.VMEM((2, 2, rows, inner), LOW),
            pltpu.VMEM((2, 2, rows, inner), LOW),
            pltpu.SemaphoreType.DMA((2, 2)),
            pltpu.SemaphoreType.DMA((2, 2)),
            pltpu.SemaphoreType.DMA((2, parts)),
            pltpu.VMEM((count, shard, length), LOW),
            pltpu.VMEM((2, parts, piece, shard), WIDE),
        ],
        [
            pltpu.VMEM((length, D), LOW),
            pltpu.VMEM((inner, D), LOW),
            pltpu.SemaphoreType.DMA((blocks.shape[0],)),
            pltpu.SemaphoreType.DMA((2, count)),
        ],
    ]

    def kernel(*refs):
        ins, outs, *scratch = take(refs, [6, 3] + [len(g) for g in groups])
        blocks, down_first, down_second, hidden, silu, slope = ins
        grad, weight, grad_sems, weight_sems = scratch[2]
        gate_grad, up_grad, weight_grad = outs
        total, summed, land, ring_send, ring_recv, credit = scratch[0]
        given, made, given_sems, made_sems, out_sems, turned, final = scratch[1]

        def product(way, step, part):
            owner = ring.owner(way, step)

            @pl.when((part == 0) & ((step < count // 2) | (step == count - 1)))
            def _():
                turned[owner] = grad[:, pl.ds(aligned(owner * shard, shard), shard)].T

            columns = pl.ds(aligned(way * side + part * piece, piece), piece)
            total[way, part] = jnp.dot(
                turned[owner], hidden[:, columns], preferred_element_type=WIDE
            )

        ring = RingScatter(
            product, total, summed, land, ring_send, ring_recv, credit, slots, parts
        )

        def load(chunk):
            slot = lax.rem(chunk, 2)
            return [
                pltpu.make_async_copy(
                    (slope, silu)[which].at[row_slice(chunk, rows)],
                    given.at[slot, which],
                    given_sems.at[slot, which],
                )
                for which in range(2)
            ]

        def store(chunk):
            slot = lax.rem(chunk, 2)
            return [
                pltpu.make_async_copy(
                    made.at[slot, which],
                    (gate_grad, up_grad)[which].at[row_slice(chunk, rows)],
                    made_sems.at[slot, which],
                )
                for which in range(2)
            ]

        grad_copies = all_blocks(blocks, None, blocks.shape[2], grad, grad_sems)
        weight_copies = all_blocks(
            down_first, None, shard, weight.at[:down_rows], weight_sems.at[0]
        ) + all_blocks(down_second, None, shard, weight.at[down_rows:], weight_sems.at[1])
        for item in grad_copies + weight_copies + load(0):
            item.start()
        greet(False, True)
        for item in grad_copies:
            item.wait()

        def iteration(step):
            slot = lax.rem(step, 2)
            @pl.when(step + 1 < chunks)
            def _():
                for item in load(step + 1):
                    item.start()

            @pl.when(step >= 2)
            def _():
                for item in store(step - 2):
                    item.wait()

            for item in load(step):
                item.wait()

            each = parts // (inner // tile)

            @pl.loop(0, inner // tile)
            def _(index):
                for which in range(each):
                    ring.event(step * parts + index * each + which)

                @pl.when((step == 0) & (index == 0))
                def _():
                    for item in weight_copies:
                        item.wait()

                at = pl.ds(aligned(index * tile, tile), tile)
                hidden_grad = nt(grad[row_slice(step, rows)], weight[at])
                for which in range(2):
                    made[slot, which, :, at] = (
                        hidden_grad * given[slot, which, :, at].astype(WIDE)
                    ).astype(LOW)

            for item in store(step):
                item.start()

        loop(chunks, iteration)
        writes = [
            pltpu.make_async_copy(
                final.at[way, part],
                weight_grad.at[way * side + part * piece : way * side + (part + 1) * piece],
                out_sems.at[way, part],
            )
            for way in range(2)
            for part in range(parts)
        ]
        for way in range(2):
            for part in range(parts):
                final[way, part] = total[way, part].T
        for item in writes:
            item.start()
        for chunk in (chunks - 2, chunks - 1):
            for item in store(chunk):
                item.wait()
        ring.end()
        for item in writes:
            item.wait()

    shape = jax.ShapeDtypeStruct
    return pl.pallas_call(
        kernel,
        out_shape=[
            shape((length, inner), LOW),
            shape((length, inner), LOW),
            shape((inner, shard), WIDE),
        ],
        in_specs=[HBM, HBM, HBM, VMEM, HBM, HBM],
        out_specs=[HBM, HBM, HBM],
        scratch_shapes=[item for group in groups for item in group],
        compiler_params=pltpu.CompilerParams(
            collective_id=collective, has_side_effects=True, vmem_limit_bytes=60 * MIB
        ),
        cost_estimate=pl.CostEstimate(
            flops=4 * length * inner * D, bytes_accessed=16 * length * D, transcendentals=0
        ),
    )(blocks, down_first, down_second, hidden, silu, slope)


def attn_in_back(
    query_back,
    key_back,
    value_grad,
    query_raw,
    key_raw,
    factors,
    projections,
    query_gain,
    key_gain,
    stack,
    inputs,
    mixed_grad,
    gain_parts,
    collective,
):
    length, columns = value_grad.shape[0], 2 * stack.shape[2]
    width = mixed_grad.shape[1]
    count = lax.axis_size("gy")
    chunks = count
    rows = length // chunks
    shard = D // count
    side = columns // 2
    slots, parts = count - 1, 3
    piece = side // parts

    groups = [
        Reduce.scratch(rows, chunks, width, True),
        RingScatter.scratch(shard, side, slots, parts),
        [
            pltpu.VMEM((rows, width), WIDE),
            pltpu.VMEM((2, rows, width), WIDE),
            pltpu.VMEM((length, columns), LOW),
            pltpu.VMEM((length, STATS), WIDE),
            pltpu.VMEM((2, 4, rows, width), WIDE),
            pltpu.VMEM((2, D, side), LOW),
            pltpu.SemaphoreType.DMA((2, 4)),
            pltpu.SemaphoreType.DMA((2,)),
            pltpu.SemaphoreType.DMA((1,)),
            pltpu.SemaphoreType.DMA((2,)),
            pltpu.SemaphoreType.DMA((2, parts)),
        ],
        Columns.scratch(length, shard),
        Total.scratch(length),
        [
            pltpu.VMEM((8, width), WIDE),
            pltpu.VMEM((count - 1, 8, width), WIDE),
            pltpu.SemaphoreType.DMA((count - 1, 2)),
        ],
    ]

    def kernel(*refs):
        ins, outs, *scratch = take(refs, [16, 4] + [len(g) for g in groups])
        query_back, key_back, value_grad, query_raw, key_raw, factors = ins[:6]
        projections, query_gain, key_gain, full, inputs, mixed_grad = ins[6:12]
        gain_parts = ins[12:]
        token_grad, weight_grad, gain_grads, cross_land = outs
        gain_mine, gain_land, gain_sems = scratch[5]
        reduce = Reduce(scratch[0], cross_land, rows, width, True)
        total, summed, land, ring_send, ring_recv, credit = scratch[1]
        mixed_buf, token_buf, grads, projected, given, stack = scratch[2][:6]
        given_sems, whole_sems, mixed_sems, token_sems, out_sems = scratch[2][6:]
        left = Columns(inputs, shard, *scratch[3])
        total_sum = Total(*scratch[4])

        def product(way, step, part):
            @pl.when(part == 0)
            def _():
                left.take(ring, way, step)

            columns = pl.ds(aligned(way * side + part * piece, piece), piece)
            total[way, part] = jnp.dot(
                left.turned[way], grads[:, columns], preferred_element_type=WIDE
            )

        ring = RingScatter(
            product, total, summed, land, ring_send, ring_recv, credit, slots, parts
        )
        def load(chunk):
            slot, at = lax.rem(chunk, 2), row_slice(chunk, rows)
            return [
                pltpu.make_async_copy(
                    source.at[at], given.at[slot, which], given_sems.at[slot, which]
                )
                for which, source in enumerate((query_back, key_back, query_raw, key_raw))
            ]

        value_copy = pltpu.make_async_copy(value_grad, grads.at[:, 2 * width :], whole_sems.at[0])
        stack_copy = pltpu.make_async_copy(full, stack, whole_sems.at[1])
        left.copy(ring.owner(0, 0)).start()
        for item in load(0):
            item.start()
        value_copy.start()
        stack_copy.start()
        chip_columns = pl.ds(aligned(chip_here() * width, width), width)
        gain_mine[...] = jnp.zeros_like(gain_mine)
        for which, part in enumerate(gain_parts):
            gain_mine[which : which + 1] = part[...] if which < 2 else part[:, chip_columns]
        greet("all", False, True)
        total_sum.start(projections)
        gain_copies = [
            remote(
                gain_mine,
                gain_land.at[shift - 1],
                gain_sems.at[shift - 1, 0],
                gain_sems.at[shift - 1, 1],
                {"gy": block_at(shift)},
            )
            for shift in range(1, count)
        ]
        for item in gain_copies:
            item.start()
        sums_here = total_sum.finish(projections)
        projected[...] = jnp.concatenate([sums_here] * (STATS // 8), axis=0).T

        def form(chunk):
            slot = lax.rem(chunk, 2)

            @pl.when(chunk + 1 < chunks)
            def _():
                for item in load(chunk + 1):
                    item.start()

            for item in load(chunk):
                item.wait()

            def some(part):
                at = pl.ds(aligned(chunk * rows + part.start, 32), 32)
                for which, gain in enumerate((query_gain, key_gain)):
                    factor = factors[at, which : which + 1]
                    pull = factor * factor * factor * projected[at, which : which + 1] / D
                    back, raw = given[slot, which, part], given[slot, which + 2, part]
                    grads[at, which * width : (which + 1) * width] = (
                        factor * gain[...] * back - raw * pull
                    ).astype(LOW)

            tiles(rows, some)

        loop(chunks, form)
        value_copy.wait()

        def prepare(chunk):
            @pl.when(chunk == 0)
            def _():
                stack_copy.wait()

        def multiply(chunk, place):
            at = row_slice(chunk, rows)
            return nt(grads[at, :side], stack[0, pl.ds(place, width)]) + nt(
                grads[at, side:], stack[1, pl.ds(place, width)]
            )

        def mixed_copy(chunk):
            return pltpu.make_async_copy(
                mixed_grad.at[row_slice(chunk, rows)], mixed_buf, mixed_sems.at[0]
            )

        def token_copy(chunk):
            slot = lax.rem(chunk, 2)
            return pltpu.make_async_copy(
                token_buf.at[slot], token_grad.at[row_slice(chunk, rows)], token_sems.at[slot]
            )

        def fetch(chunk):
            @pl.when(chunk >= 1)
            def _():
                mixed_copy(chunk - 1).start()

        def sums(chunk):
            pass

        def finish(chunk):
            slot = lax.rem(chunk, 2)
            mixed_copy(chunk).wait()

            @pl.when(chunk >= 2)
            def _():
                token_copy(chunk - 2).wait()

            def some(at):
                token_buf[slot, at] = mixed_buf[at] + reduce.raw[at]

            tiles(rows, some)
            token_copy(chunk).start()

        schedule(chunks, reduce, multiply, fetch, sums, finish, ring.event, ring.events, prepare)
        writes = [
            pltpu.make_async_copy(
                total.at[way, part],
                weight_grad.at[:, way * side + part * piece : way * side + (part + 1) * piece],
                out_sems.at[way, part],
            )
            for way in range(2)
            for part in range(parts)
        ]
        for item in writes:
            item.start()
        gain_total = gain_mine[...]
        for shift in range(1, count):
            gain_copies[shift - 1].wait()
            gain_total = gain_total + gain_land[shift - 1]
        gain_grads[...] = gain_total
        ring.end()
        reduce.end(chunks)
        for chunk in (chunks - 2, chunks - 1):
            token_copy(chunk).wait()
        for item in writes:
            item.wait()

    shape = jax.ShapeDtypeStruct
    out = pl.pallas_call(
        kernel,
        out_shape=[
            shape((length, width), WIDE),
            shape((shard, columns), WIDE),
            shape((8, width), WIDE),
        ]
        + Reduce.landing(rows, chunks, width, True),
        in_specs=[HBM] * 5 + [VMEM] * 4 + [HBM] * 3 + [VMEM] * 4,
        out_specs=[HBM, HBM, VMEM, HBM],
        scratch_shapes=[item for group in groups for item in group],
        compiler_params=pltpu.CompilerParams(
            collective_id=collective, has_side_effects=True, vmem_limit_bytes=60 * MIB
        ),
        cost_estimate=pl.CostEstimate(
            flops=4 * length * columns * D, bytes_accessed=8 * length * D, transcendentals=0
        ),
    )(
        query_back,
        key_back,
        value_grad,
        query_raw,
        key_raw,
        factors,
        projections,
        query_gain,
        key_gain,
        stack,
        inputs,
        mixed_grad,
        *gain_parts,
    )
    return out[:3]


def token_positions(segment):
    length = segment.shape[0]
    labels = jnp.arange(SEGS, dtype=jnp.int32)
    member = (segment[:, None] == labels[None, :]).astype(jnp.int32)
    totals = jnp.sum(member, axis=0)
    starts = jnp.cumsum(totals) - totals
    opening = jnp.sum(member * starts[None, :], axis=1)
    return jnp.arange(length, dtype=jnp.int32) - opening


def rotary_tables(segment):
    place = token_positions(segment).astype(jnp.float32)
    halves = HEAD // 2
    inverse = jnp.exp(jnp.arange(halves, dtype=jnp.float32) * (-2.0 * math.log(THETA) / HEAD))
    angle = place[:, None] * inverse[None, :]
    return (jnp.cos(angle), jnp.sin(angle))


BLOCK = 256
LANES = 128
SCALE = 1.0 / math.sqrt(HEAD)
SCALE_TWO = SCALE * math.log2(math.e)


def turn(values, cosine, sine):
    return values * cosine + pltpu.roll(values, HEAD // 2, 1) * sine


def head_columns(head):
    return slice(head * HEAD, (head + 1) * HEAD)


def nt(left, right):
    return lax.dot_general(left, right, (((1,), (1,)), ((), ())), preferred_element_type=WIDE)


def attend(first_block, query_raw, key_raw, values, factors, query_gain, key_gain, tables, starts):
    length, width = query_raw.shape
    heads = width // HEAD

    def kernel(
        first_block,
        query_raw,
        key_raw,
        values,
        factors,
        query_gain,
        key_gain,
        cosine,
        sine,
        starts,
        queries,
        keys,
        attended,
        peaks,
        peak_columns,
    ):
        @pl.loop(0, length // BLOCK)
        def _(index):
            at = row_slice(index, BLOCK)
            cos, sin = cosine[at], sine[at]
            pairs = ((query_raw, query_gain, queries), (key_raw, key_gain, keys))
            for which, (raw, gain, out) in enumerate(pairs):
                factor = factors[at, which : which + 1]
                for head in range(heads):
                    columns = head_columns(head)
                    normed = raw[at, columns] * factor * gain[:, columns]
                    out[at, columns] = turn(normed, cos, sin).astype(LOW)

        lane = lax.broadcasted_iota(jnp.int32, (BLOCK, LANES), 1)
        row_index = lax.broadcasted_iota(jnp.int32, (BLOCK, BLOCK), 0)
        column_index = lax.broadcasted_iota(jnp.int32, (BLOCK, BLOCK), 1)

        def query_block(index):
            at = row_slice(index, BLOCK)
            start = starts[at]

            def key_block(other, carry):
                there = row_slice(other, BLOCK)
                key_place = column_index + other * BLOCK
                allowed = (key_place >= start) & (key_place <= row_index + index * BLOCK)
                made = []
                for head in range(heads):
                    columns = head_columns(head)
                    peak, total, rows = carry[head]
                    scores = nt(queries[at, columns], keys[there, columns]) * SCALE_TWO
                    scores = jnp.where(allowed, scores, NEGATIVE)
                    higher = jnp.maximum(peak, jnp.max(scores, axis=1, keepdims=True))
                    raised = jnp.exp2(scores - higher)
                    shrink = jnp.exp2(peak - higher)
                    total = total * shrink + jnp.sum(raised, axis=1, keepdims=True)
                    rows = rows * shrink + jnp.dot(
                        raised.astype(LOW), values[there, columns], preferred_element_type=WIDE
                    )
                    made.append((higher, total, rows))
                return tuple(made)

            empty = (
                jnp.full((BLOCK, 1), NEGATIVE, WIDE),
                jnp.zeros((BLOCK, 1), WIDE),
                jnp.zeros((BLOCK, HEAD), WIDE),
            )
            done = lax.fori_loop(first_block[index], index + 1, key_block, (empty,) * heads)
            column = jnp.zeros((BLOCK, LANES), WIDE)
            for head in range(heads):
                peak, total, rows = done[head]
                attended[at, head_columns(head)] = (rows / total).astype(LOW)
                column = jnp.where(lane == head, peak + jnp.log2(total), column)
            peak_columns[at] = column

        loop(length // BLOCK, query_block)
        peaks[...] = peak_columns[...].T[:8]

    shape = jax.ShapeDtypeStruct
    smem = pl.BlockSpec(memory_space=pltpu.SMEM)
    return pl.pallas_call(
        kernel,
        out_shape=[
            shape((length, width), LOW),
            shape((length, width), LOW),
            shape((length, width), LOW),
            shape((8, length), WIDE),
        ],
        in_specs=[smem] + [VMEM] * 9,
        out_specs=[VMEM] * 4,
        scratch_shapes=[pltpu.VMEM((length, LANES), WIDE)],
        compiler_params=pltpu.CompilerParams(vmem_limit_bytes=48 * MIB),
        cost_estimate=pl.CostEstimate(
            flops=2 * length * MAX_LEN * width,
            bytes_accessed=16 * length * width,
            transcendentals=length * MAX_LEN * heads // 2,
        ),
    )(first_block, query_raw, key_raw, values, factors, query_gain, key_gain, *tables, starts)


def attend_back(
    last_block,
    queries,
    keys,
    values,
    attended,
    upstream,
    peaks,
    query_raw,
    key_raw,
    factors,
    query_gain,
    key_gain,
    tables,
    start_row,
    finished,
):
    length, width = query_raw.shape
    heads = width // HEAD

    extra = len(finished)

    def kernel(*refs):
        finished_in = refs[15 : 15 + extra]
        finished_out = refs[21 + extra : 21 + 2 * extra]
        held, copy_sems = refs[-1 - extra : -1], refs[-1]
        reads = [
            pltpu.make_async_copy(finished_in[i], held[i], copy_sems.at[0, i])
            for i in range(extra)
        ]
        writes = [
            pltpu.make_async_copy(held[i], finished_out[i], copy_sems.at[1, i])
            for i in range(extra)
        ]
        for item in reads:
            item.start()

        def pass_on():
            for read, write in zip(reads, writes):
                read.wait()
                write.start()

        work(pass_on, *refs[:15], *refs[15 + extra : 21 + extra], *refs[21 + 2 * extra : -1 - extra])
        for item in writes:
            item.wait()

    def work(
        pass_on,
        last_block,
        queries,
        keys,
        values,
        attended,
        upstream,
        peaks,
        query_raw,
        key_raw,
        factors,
        query_gain,
        key_gain,
        cosine,
        sine,
        start_row,
        query_out,
        key_out,
        value_out,
        projections,
        query_gain_grad,
        key_gain_grad,
        query_sum,
        key_sum,
        value_sum,
        columns_scratch,
        deltas,
    ):
        lane = lax.broadcasted_iota(jnp.int32, (BLOCK, LANES), 1)
        query_gain_grad[...] = jnp.zeros_like(query_gain_grad)
        key_gain_grad[...] = jnp.zeros_like(key_gain_grad)

        def prepare(index):
            at = row_slice(index, BLOCK)
            column = jnp.zeros((BLOCK, LANES), WIDE)
            for head in range(heads):
                columns = head_columns(head)
                delta = jnp.sum(
                    attended[at, columns].astype(WIDE) * upstream[at, columns].astype(WIDE),
                    axis=1,
                    keepdims=True,
                )
                column = jnp.where(lane == head, delta, column)
            columns_scratch[at] = column
            query_sum[at] = jnp.zeros((BLOCK, width), WIDE)

        loop(length // BLOCK, prepare)
        deltas[...] = columns_scratch[...].T[:8]
        pass_on()
        row_index = lax.broadcasted_iota(jnp.int32, (BLOCK, BLOCK), 0)
        column_index = lax.broadcasted_iota(jnp.int32, (BLOCK, BLOCK), 1)

        def turn_back(at, summed, raw, gain, factor, out, gain_grad):
            cos, sin = cosine[at], sine[at]
            share = jnp.zeros((BLOCK, 1), WIDE)
            for head in range(heads):
                columns = head_columns(head)
                normed = turn(summed(head) * SCALE, cos, -sin)
                out[at, columns] = normed
                weighed = normed * raw[at, columns]
                share += jnp.sum(gain[:, columns] * weighed, axis=1, keepdims=True)
                gain_grad[:, columns] += jnp.sum(weighed * factor, axis=0, keepdims=True)
            return share

        def key_block(index):
            at = row_slice(index, BLOCK)
            key_sum[...] = jnp.zeros_like(key_sum)
            value_sum[...] = jnp.zeros_like(value_sum)

            def query_block(other, carry):
                there = row_slice(other, BLOCK)
                key_place = row_index + index * BLOCK
                allowed = (key_place >= start_row[:, there]) & (
                    key_place <= column_index + other * BLOCK
                )
                for head in range(heads):
                    columns = head_columns(head)
                    scores = nt(keys[at, columns], queries[there, columns]) * SCALE_TWO
                    scores = jnp.where(allowed, scores, NEGATIVE)
                    chance = jnp.exp2(scores - peaks[head : head + 1, there])
                    value_sum[:, columns] += jnp.dot(
                        chance.astype(LOW), upstream[there, columns], preferred_element_type=WIDE
                    )
                    chance_grad = nt(values[at, columns], upstream[there, columns])
                    score_grad = (chance * (chance_grad - deltas[head : head + 1, there])).astype(LOW)
                    key_sum[:, columns] += jnp.dot(
                        score_grad, queries[there, columns], preferred_element_type=WIDE
                    )
                    query_sum[there, columns] += lax.dot_general(
                        score_grad,
                        keys[at, columns],
                        (((0,), (0,)), ((), ())),
                        preferred_element_type=WIDE,
                    )
                return carry

            lax.fori_loop(index, last_block[index] + 1, query_block, 0)
            value_out[at] = value_sum[...].astype(LOW)
            share = turn_back(
                at,
                lambda head: key_sum[:, head_columns(head)],
                key_raw,
                key_gain,
                factors[at, 1:2],
                key_out,
                key_gain_grad,
            )
            columns_scratch[at] = jnp.where(lane == 1, share, 0.0)

        loop(length // BLOCK, key_block)

        def finish(index):
            at = row_slice(index, BLOCK)
            share = turn_back(
                at,
                lambda head: query_sum[at, head_columns(head)],
                query_raw,
                query_gain,
                factors[at, 0:1],
                query_out,
                query_gain_grad,
            )
            columns_scratch[at] += jnp.where(lane == 0, share, 0.0)

        loop(length // BLOCK, finish)
        projections[...] = columns_scratch[...].T[:8]

    shape = jax.ShapeDtypeStruct
    smem = pl.BlockSpec(memory_space=pltpu.SMEM)
    return pl.pallas_call(
        kernel,
        out_shape=[
            shape((length, width), WIDE),
            shape((length, width), WIDE),
            shape((length, width), LOW),
            shape((8, length), WIDE),
            shape((1, width), WIDE),
            shape((1, width), WIDE),
        ]
        + [shape(item.shape, item.dtype) for item in finished],
        in_specs=[smem] + [VMEM] * 14 + [HBM] * extra,
        out_specs=[VMEM] * 6 + [HBM] * extra,
        scratch_shapes=[
            pltpu.VMEM((length, width), WIDE),
            pltpu.VMEM((BLOCK, width), WIDE),
            pltpu.VMEM((BLOCK, width), WIDE),
            pltpu.VMEM((length, LANES), WIDE),
            pltpu.VMEM((8, length), WIDE),
        ]
        + [pltpu.VMEM(item.shape, item.dtype) for item in finished]
        + [pltpu.SemaphoreType.DMA((2, extra))],
        compiler_params=pltpu.CompilerParams(vmem_limit_bytes=52 * MIB),
        cost_estimate=pl.CostEstimate(
            flops=5 * length * MAX_LEN * width,
            bytes_accessed=32 * length * width,
            transcendentals=length * MAX_LEN * heads // 2,
        ),
    )(
        last_block,
        queries,
        keys,
        values,
        attended,
        upstream,
        peaks,
        query_raw,
        key_raw,
        factors,
        query_gain,
        key_gain,
        *tables,
        start_row,
        *finished,
    )


def shards(
    tokens,
    query_weight,
    key_weight,
    value_weight,
    output_weight,
    gate_weight,
    up_weight,
    down_weight,
    query_gain,
    key_gain,
    attn_gain,
    mlp_gain,
    seq_ids,
    out_grad,
):
    segment = seq_ids[0]
    length = tokens.shape[0]
    local_width = tokens.shape[1]
    cosine, sine = rotary_tables(segment)
    tables = (
        jnp.concatenate([cosine, cosine], axis=1),
        jnp.concatenate([-sine, sine], axis=1),
    )
    order = jnp.arange(length, dtype=jnp.int32)
    starts = order - token_positions(segment)
    blocks = length // BLOCK
    first_block = starts.reshape(blocks, BLOCK)[:, 0] // BLOCK
    closing = segment.reshape(blocks, BLOCK)[:, -1]
    ends = jnp.sum((segment[None, :] <= closing[:, None]).astype(jnp.int32), axis=1) - 1
    last_block = ends // BLOCK
    gains = jnp.concatenate([attn_gain[None], mlp_gain[None], jnp.zeros((6, local_width))], axis=0)
    query_gain, key_gain = query_gain.reshape(1, -1), key_gain.reshape(1, -1)
    middle = local_width // 2
    pairs = (
        (query_weight, key_weight[:, :middle]),
        (key_weight[:, middle:], value_weight),
    )
    stack = jnp.stack([jnp.concatenate(pair, axis=1) for pair in pairs])
    inputs, attn_stack, output_full, query_raw, key_raw, values, squares, halves = gather_in(
        tokens, stack, output_weight, gains, 1
    )
    attn_half, mlp_half = halves[:1], halves[1:2]
    middle = down_weight.shape[0] // 2
    squares, down_rows = lax.optimization_barrier((squares, down_weight[middle:]))
    down_second = lax.all_gather(down_rows, "gy", axis=0)
    factors = lax.rsqrt(squares[:2].T / D + EPS)
    queries, keys, attended, peaks = attend(
        first_block,
        query_raw,
        key_raw,
        values,
        factors,
        query_gain,
        key_gain,
        tables,
        starts[:, None],
    )
    attn_raw, mixed, mlp_inputs, gate_full, up_full, down_first, upstream = attn_out(
        attended, output_full, attn_half, inputs, out_grad, gate_weight, up_weight, down_weight[:middle], 2
    )
    result, mlp_full, mlp_gain_part, hidden, silu, slope = mlp_forward(
        mlp_inputs, gate_full, up_full, down_first, down_second, mlp_half, mixed, upstream, 3
    )
    gate_grad, up_grad, down_weight_grad = hidden_back(
        mlp_full, down_first, down_second, hidden, silu, slope, 4
    )
    mixed_grad, attn_full, attn_gain_part, gate_weight_grad, up_weight_grad = mlp_back(
        gate_grad, up_grad, gate_full, up_full, mlp_inputs, attn_half, upstream, attn_raw, 5
    )
    output_product = lax.dot_general(
        attended, attn_full, (((0,), (0,)), ((), ())), preferred_element_type=jnp.float32
    )
    output_weight_grad = lax.psum_scatter(
        output_product.astype(jnp.bfloat16), "gy", scatter_dimension=1, tiled=True
    ).astype(jnp.float32)
    attended_grad = lax.dot_general(
        attn_full, output_full, (((1,), (1,)), ((), ())), preferred_element_type=jnp.float32
    ).astype(jnp.bfloat16)
    query_back, key_back, value_grad, projections, query_gain_part, key_gain_part, *done = attend_back(
        last_block,
        queries,
        keys,
        values,
        attended,
        attended_grad,
        peaks,
        query_raw,
        key_raw,
        factors,
        query_gain,
        key_gain,
        tables,
        starts[None, :],
        (result, gate_weight_grad, up_weight_grad, down_weight_grad),
    )
    result, gate_weight_grad, up_weight_grad, down_weight_grad = done
    token_grad, attn_weight_grads, gain_grads = attn_in_back(
        query_back,
        key_back,
        value_grad,
        query_raw,
        key_raw,
        factors,
        projections,
        query_gain,
        key_gain,
        attn_stack,
        inputs,
        mixed_grad,
        (query_gain_part, key_gain_part, attn_gain_part, mlp_gain_part),
        6,
    )
    query_weight_grad = attn_weight_grads[:, :local_width]
    key_weight_grad = attn_weight_grads[:, local_width : 2 * local_width]
    value_weight_grad = attn_weight_grads[:, 2 * local_width :]
    query_gain_grad, key_gain_grad, attn_gain_grad, mlp_gain_grad = (gain_grads[i] for i in range(4))
    return (
        result,
        token_grad,
        query_weight_grad,
        key_weight_grad,
        value_weight_grad,
        output_weight_grad,
        gate_weight_grad,
        up_weight_grad,
        down_weight_grad,
        query_gain_grad,
        key_gain_grad,
        attn_gain_grad,
        mlp_gain_grad,
    )


def solution(mesh):
    return jax.shard_map(
        shards,
        mesh=mesh,
        in_specs=(
            P("gy", "gx"),
            P("gy", "gx"),
            P("gy", "gx"),
            P("gy", "gx"),
            P("gx", "gy"),
            P("gy", "gx"),
            P("gy", "gx"),
            P("gx", "gy"),
            P("gx"),
            P("gx"),
            P("gx"),
            P("gx"),
            P("gy", None),
            P("gy", "gx"),
        ),
        out_specs=(
            P("gy", "gx"),
            P("gy", "gx"),
            P("gy", "gx"),
            P("gy", "gx"),
            P("gy", "gx"),
            P("gx", "gy"),
            P("gy", "gx"),
            P("gy", "gx"),
            P("gx", "gy"),
            P("gx"),
            P("gx"),
            P("gx"),
            P("gx"),
        ),
        check_vma=False,
    )
```

```python
import math

import jax
import jax.numpy as jnp
from jax import lax
from jax.experimental import pallas as pl
from jax.experimental.pallas import tpu as pltpu
from jax.sharding import PartitionSpec as P

D = 2048
HEAD = 128
MAX_LEN = 1024
SEGS = 4


EPS = 1e-06
THETA = 500000.0
NEGATIVE = -1e30


MESH = pl.DeviceIdType.MESH
HBM = pl.BlockSpec(memory_space=pltpu.HBM)
VMEM = pl.BlockSpec(memory_space=pltpu.VMEM)
LOW = jnp.bfloat16
WIDE = jnp.float32
MIB = 1 << 20
LAG = 2
STATS = 128


def core_here():
    return lax.rem(lax.axis_index("gx"), 2)


def chip_here():
    return lax.div(lax.axis_index("gx"), 2)


def other_core():
    return lax.axis_index("gx") + 1 - 2 * core_here()


def peer_at(shift):
    return lax.rem(lax.axis_index("gx") + 2 * shift, lax.axis_size("gx"))


def rank_at(shift):
    return lax.rem(lax.axis_index("gx") + shift, lax.axis_size("gx"))


def block_at(shift):
    return lax.rem(lax.axis_index("gy") + shift, lax.axis_size("gy"))


def ring_place():
    count = lax.axis_size("gy")
    index = lax.axis_index("gy")
    row, side = lax.div(index, 2), lax.rem(index, 2)
    return side * row + (1 - side) * (count - 1 - row)


def ring_device(place):
    count = lax.axis_size("gy")
    place = lax.rem(place + 2 * count, count)
    back = lax.div(place, count // 2)
    row = (1 - back) * place + back * (count - 1 - place)
    return 2 * row + 1 - back


def greet(gx, ring, all_blocks=False):
    barrier = pltpu.get_barrier_semaphore()
    partners = []
    if all_blocks:
        partners += [{"gy": block_at(k)} for k in range(1, lax.axis_size("gy"))]
    if gx == "all":
        partners += [{"gx": rank_at(k)} for k in range(1, lax.axis_size("gx"))]
    elif gx:
        partners.append({"gx": other_core()})
        partners += [{"gx": peer_at(k)} for k in range(1, lax.axis_size("gx") // 2)]
    if ring:
        place = ring_place()
        partners += [{"gy": ring_device(place + 1)}, {"gy": ring_device(place - 1)}]
    for partner in partners:
        pl.semaphore_signal(barrier, inc=1, device_id=partner, device_id_type=MESH)
    pl.semaphore_wait(barrier, len(partners))


def remote(source, target, send, recv, device):
    return pltpu.make_async_remote_copy(
        src_ref=source,
        dst_ref=target,
        send_sem=send,
        recv_sem=recv,
        device_id=device,
        device_id_type=MESH,
    )


def loop(count, body):
    def step(index, carry):
        body(index)
        return carry

    lax.fori_loop(0, count, step, 0)


def aligned(value, factor):
    return pl.multiple_of(value, factor)


class RingGather:
    def __init__(self, sources, slot, spill, parts, send, recv, local, spilled):
        self.sources, self.slot, self.spill, self.parts = sources, slot, spill, parts
        self.send, self.recv, self.local, self.spilled = send, recv, local, spilled
        self.count = lax.axis_size("gy")

    @staticmethod
    def scratch(parts):
        count = lax.axis_size("gy")
        return [
            pltpu.SemaphoreType.DMA((count - 1, 2, parts)),
            pltpu.SemaphoreType.DMA((count - 1, 2, parts)),
            pltpu.SemaphoreType.DMA((2, parts)),
            pltpu.SemaphoreType.DMA((count, 2, parts)),
        ]

    def spill_copy(self, way, step, part):
        place = ring_place()
        owner = ring_device(place - (1 - 2 * way) * step)
        return pltpu.make_async_copy(
            self.slot(way, owner, part),
            self.spill(way, owner, part),
            self.spilled.at[step, way, part],
        )

    def copy(self, way, step, part, behind):
        place = ring_place()
        sign = 1 - 2 * way
        spot = self.slot(way, ring_device(place - sign * (step + behind)), part)
        return remote(
            spot,
            spot,
            self.send.at[step, way, part],
            self.recv.at[step, way, part],
            {"gy": ring_device(place + sign)},
        )

    def begin(self):
        place = [
            pltpu.make_async_copy(
                self.sources(way, part),
                self.slot(way, lax.axis_index("gy"), part),
                self.local.at[way, part],
            )
            for way in range(2)
            for part in range(self.parts)
        ]
        for item in place:
            item.start()
        for item in place:
            item.wait()
        for part in range(self.parts):
            for way in range(2):
                self.copy(way, 0, part, 0).start()
                self.spill_copy(way, 0, part).start()

    @property
    def events(self):
        return (self.count - 2) * self.parts

    def event(self, index):
        step = 1 + lax.div(index, self.parts)
        for part in range(self.parts):

            @pl.when(lax.rem(index, self.parts) == part)
            def _():
                for way in range(2):
                    self.copy(way, step - 1, part, 1).wait_recv()
                    self.copy(way, step, part, 0).start()
                    self.spill_copy(way, step, part).start()

    def end(self):
        for part in range(self.parts):
            for way in range(2):
                self.copy(way, self.count - 2, part, 1).wait_recv()
                self.spill_copy(way, self.count - 1, part).start()

        def drain(step):
            for part in range(self.parts):
                for way in range(2):
                    self.copy(way, step, part, 0).wait_send()

        loop(self.count - 1, drain)

    def settle(self):
        def drain(step):
            for part in range(self.parts):
                for way in range(2):
                    self.spill_copy(way, step, part).wait()

        loop(self.count, drain)


class RingScatter:
    def __init__(self, product, total, sums, land, send, recv, credit, slots, parts):
        self.product, self.total, self.sums, self.land = product, total, sums, land
        self.send, self.recv, self.credit = send, recv, credit
        self.slots, self.parts = slots, parts
        self.count = lax.axis_size("gy")
        self.rows = total.shape[2]

    @staticmethod
    def scratch(rows, columns, slots, parts):
        count = lax.axis_size("gy")
        return [
            pltpu.VMEM((2, parts, rows, columns // parts), WIDE),
            pltpu.VMEM((2, parts, rows, columns // parts), LOW),
            pltpu.VMEM((slots, 2, parts, rows, columns // parts), LOW),
            pltpu.SemaphoreType.DMA((count - 1, 2, parts)),
            pltpu.SemaphoreType.DMA((count - 1, 2, parts)),
            pltpu.SemaphoreType.REGULAR((2, parts)),
        ]

    def copy(self, way, step, part):
        place = ring_place()
        return remote(
            self.sums.at[way, part],
            self.land.at[lax.rem(step, self.slots), way, part],
            self.send.at[step, way, part],
            self.recv.at[step, way, part],
            {"gy": ring_device(place + 1 - 2 * way)},
        )

    def owner(self, way, step):
        sign = 1 - 2 * way
        return ring_device(ring_place() - sign * (1 + step))

    @property
    def events(self):
        return self.count * self.parts

    def event(self, index):
        step, part = lax.div(index, self.parts), lax.rem(index, self.parts)
        last = self.count - 1
        tile = min(self.rows, 32)

        for way in range(2):
            self.product(way, step, part)

        for way in range(2):

            slot = lax.rem(step - 1 + self.slots, self.slots)

            def over(body):
                @pl.loop(0, self.rows // tile)
                def _(index):
                    body(pl.ds(aligned(index * tile, tile), tile))

            @pl.when(step >= 1)
            def _():
                self.copy(way, step - 1, part).wait_recv()

            @pl.when((step >= 1) & (step < last))
            def _():
                self.copy(way, step - 1, part).wait_send()

            @pl.when(step == 0)
            def _():
                def first(rows):
                    self.sums[way, part, rows] = self.total[way, part, rows].astype(LOW)

                over(first)

            @pl.when((step >= 1) & (step < last))
            def _():
                def more(rows):
                    arrived = self.land[slot, way, part, rows].astype(WIDE)
                    self.sums[way, part, rows] = (self.total[way, part, rows] + arrived).astype(LOW)

                over(more)

            @pl.when(step == last)
            def _():
                def final(rows):
                    self.total[way, part, rows] += self.land[slot, way, part, rows].astype(WIDE)

                over(final)

            @pl.when((step >= 1) & (step - 1 + self.slots < last))
            def _():
                upstream = ring_device(ring_place() - (1 - 2 * way))
                pl.semaphore_signal(
                    self.credit.at[way, part],
                    inc=1,
                    device_id={"gy": upstream},
                    device_id_type=MESH,
                )

            @pl.when(step < last)
            def _():
                @pl.when(step >= self.slots)
                def _():
                    pl.semaphore_wait(self.credit.at[way, part], 1)

                self.copy(way, step, part).start()

    def end(self):
        for part in range(self.parts):
            for way in range(2):
                self.copy(way, self.count - 2, part).wait_send()


class Reduce:
    def __init__(self, refs, cross_land, rows, width, scatter):
        (
            self.keep,
            self.core_send,
            self.core_land,
            self.cross,
            self.cross_stage,
            self.raw,
            self.core_sems,
            self.cross_send_sems,
            self.cross_recv_sems,
            self.stage_sems,
        ) = refs
        self.cross_land = cross_land
        self.rows, self.width, self.scatter = rows, width, scatter
        self.chips = lax.axis_size("gx") // 2

    @staticmethod
    def scratch(rows, chunks, width, scatter):
        chips = lax.axis_size("gx") // 2
        half = chips * width
        part = width if scatter else half
        return [
            pltpu.VMEM((1, rows, half), LOW),
            pltpu.VMEM((2, rows, half), LOW),
            pltpu.VMEM((2, rows, half), LOW),
            pltpu.VMEM((LAG + 1, chips, rows, width) if scatter else (LAG + 1, rows, half), LOW),
            pltpu.VMEM((chips - 1, rows, part), LOW),
            pltpu.VMEM((rows, part), WIDE),
            pltpu.SemaphoreType.DMA((2, chunks)),
            pltpu.SemaphoreType.DMA((chips - 1, chunks)),
            pltpu.SemaphoreType.DMA((chips - 1, chunks)),
            pltpu.SemaphoreType.DMA((chips,)),
        ]

    @staticmethod
    def landing(rows, chunks, width, scatter):
        chips = lax.axis_size("gx") // 2
        half = chips * width
        part = width if scatter else half
        return [jax.ShapeDtypeStruct((chips - 1, chunks, rows, part), LOW)]

    def core_copy(self, chunk):
        return remote(
            self.core_send.at[lax.rem(chunk, 2)],
            self.core_land.at[lax.rem(chunk, 2)],
            self.core_sems.at[0, chunk],
            self.core_sems.at[1, chunk],
            {"gx": other_core()},
        )

    def cross_copy(self, shift, chunk):
        source = self.cross.at[lax.rem(chunk, LAG + 1)]
        if self.scatter:
            block = lax.rem(chip_here() + shift, self.chips)
            source = source.at[block]
        return remote(
            source,
            self.cross_land.at[shift - 1, chunk],
            self.cross_send_sems.at[shift - 1, chunk],
            self.cross_recv_sems.at[shift - 1, chunk],
            {"gx": peer_at(shift)},
        )

    def produce(self, chunk, dot):
        @pl.when(chunk >= 2)
        def _():
            self.core_copy(chunk - 2).wait_send()

        slot = lax.rem(chunk, 2)
        core = core_here()
        for chip in range(self.chips):
            place = aligned((2 * chip + 1 - core) * self.width, self.width)
            self.core_send[slot, :, chip * self.width : (chip + 1) * self.width] = dot(
                place
            ).astype(LOW)
        self.core_copy(chunk).start()
        for chip in range(self.chips):
            place = aligned((2 * chip + core) * self.width, self.width)
            self.keep[0, :, chip * self.width : (chip + 1) * self.width] = dot(
                place
            ).astype(LOW)

    def core_sum(self, chunk):
        slot, place = lax.rem(chunk, 2), lax.rem(chunk, LAG + 1)
        self.core_copy(chunk).wait_recv()

        @pl.when(chunk >= LAG + 1)
        def _():
            for shift in range(1, self.chips):
                self.cross_copy(shift, chunk - LAG - 1).wait_send()

        @pl.loop(0, self.rows // 32)
        def _(index):
            rows = pl.ds(aligned(index * 32, 32), 32)
            total = self.keep[0, rows].astype(WIDE) + self.core_land[slot, rows].astype(WIDE)
            if self.scatter:
                for chip in range(self.chips):
                    columns = slice(chip * self.width, (chip + 1) * self.width)
                    self.cross[place, chip, rows] = total[:, columns].astype(LOW)
            else:
                self.cross[place, rows] = total.astype(LOW)

        for shift in range(1, self.chips):
            self.cross_copy(shift, chunk).start()

    def cross_stage_copy(self, shift, chunk):
        return pltpu.make_async_copy(
            self.cross_land.at[shift - 1, chunk],
            self.cross_stage.at[shift - 1],
            self.stage_sems.at[shift],
        )

    def cross_fetch(self, chunk):
        for shift in range(1, self.chips):
            self.cross_copy(shift, chunk).wait_recv()
            self.cross_stage_copy(shift, chunk).start()

    def cross_sum(self, chunk):
        place = lax.rem(chunk, LAG + 1)
        for shift in range(1, self.chips):
            self.cross_stage_copy(shift, chunk).wait()

        @pl.loop(0, self.rows // 32)
        def _(index):
            rows = pl.ds(aligned(index * 32, 32), 32)
            if self.scatter:
                total = self.cross[place, chip_here(), rows].astype(WIDE)
            else:
                total = self.cross[place, rows].astype(WIDE)
            for shift in range(1, self.chips):
                total = total + self.cross_stage[shift - 1, rows].astype(WIDE)
            self.raw[rows] = total

    def end(self, chunks):
        for chunk in (chunks - 2, chunks - 1):
            self.core_copy(chunk).wait_send()
        for chunk in range(chunks - LAG - 1, chunks):
            for shift in range(1, self.chips):
                self.cross_copy(shift, chunk).wait_send()


class Stats:
    def __init__(self, mine, land, sems):
        self.mine, self.land, self.sems = mine, land, sems

    @staticmethod
    def scratch(rows, chunks):
        return [
            pltpu.VMEM((2, rows, STATS), WIDE),
            pltpu.VMEM((2, rows, STATS), WIDE),
            pltpu.SemaphoreType.DMA((2, chunks)),
        ]

    def copy(self, chunk):
        return remote(
            self.mine.at[lax.rem(chunk, 2)],
            self.land.at[lax.rem(chunk, 2)],
            self.sems.at[0, chunk],
            self.sems.at[1, chunk],
            {"gx": other_core()},
        )

    def clear(self, chunk):
        @pl.when(chunk >= 2)
        def _():
            self.copy(chunk - 2).wait_send()

    def put(self, chunk, rows, first, second):
        lane = lax.broadcasted_iota(jnp.int32, (first.shape[0], STATS), 1)
        self.mine[lax.rem(chunk, 2), rows] = jnp.where(lane < STATS // 2, first, second)

    def get(self, chunk, rows):
        total = self.mine[lax.rem(chunk, 2), rows] + self.land[lax.rem(chunk, 2), rows]
        return (total[:, :1], total[:, STATS // 2 : STATS // 2 + 1])

    def end(self, chunks):
        for chunk in (chunks - 2, chunks - 1):
            self.copy(chunk).wait_send()


class Spread:
    def __init__(self, buffer, whole, local, send, recv, rows, width):
        self.buffer, self.whole = buffer, whole
        self.local, self.send, self.recv = local, send, recv
        self.rows, self.width = rows, width
        self.chips = lax.axis_size("gx") // 2

    @staticmethod
    def scratch(rows, chunks, width):
        chips = lax.axis_size("gx") // 2
        return [
            pltpu.VMEM((2, chips, rows, width), LOW),
            pltpu.SemaphoreType.DMA((2, chips)),
            pltpu.SemaphoreType.DMA((chunks, chips)),
            pltpu.SemaphoreType.DMA((chunks, chips)),
        ]

    def pair(self, chunk, chip, core):
        slot = lax.rem(chunk, 2)
        source = self.buffer.at[slot, chip]
        rows = pl.ds(aligned(chunk * self.rows, self.rows), self.rows)
        rank = 2 * chip + core
        if len(self.whole.shape) == 3:
            target = self.whole.at[rank, rows]
        else:
            columns = pl.ds(aligned(rank * self.width, self.width), self.width)
            target = self.whole.at[rows, columns]
        here = pltpu.make_async_copy(source, target, self.local.at[slot, chip])
        away = remote(
            source,
            target,
            self.send.at[chunk, chip],
            self.recv.at[chunk, chip],
            {"gx": other_core()},
        )
        return (here, away)

    def put(self, chunk, rows, values):
        for chip in range(self.chips):
            columns = slice(chip * self.width, (chip + 1) * self.width)
            self.buffer[lax.rem(chunk, 2), chip, rows] = values[:, columns].astype(LOW)

    def clear(self, chunk):
        @pl.when(chunk >= 2)
        def _():
            self.settle(chunk - 2)

    def settle(self, chunk):
        for chip in range(self.chips):
            here, away = self.pair(chunk, chip, core_here())
            here.wait()
            away.wait_send()

    def go(self, chunk):
        for chip in range(self.chips):
            here, away = self.pair(chunk, chip, core_here())
            here.start()
            away.start()

    def end(self, chunks):
        for chunk in (chunks - 2, chunks - 1):
            self.settle(chunk)

        def arrive(chunk):
            for chip in range(self.chips):
                self.pair(chunk, chip, 1 - core_here())[1].wait_recv()

        loop(chunks, arrive)


def row_slice(chunk, rows):
    return pl.ds(aligned(chunk * rows, rows), rows)


def core_blocks(source, chunk, rows, width, buffer, sems):
    return [
        pltpu.make_async_copy(
            source.at[2 * chip + core_here(), row_slice(chunk, rows)],
            buffer.at[:, chip * width : (chip + 1) * width],
            sems.at[chip],
        )
        for chip in range(lax.axis_size("gx") // 2)
    ]


def all_blocks(source, rows, width, buffer, sems):
    return [
        pltpu.make_async_copy(
            source.at[rank] if rows is None else source.at[rank, rows],
            buffer.at[:, rank * width : (rank + 1) * width],
            sems.at[rank],
        )
        for rank in range(source.shape[0])
    ]


def tiles(rows, body):
    @pl.loop(0, rows // 32)
    def _(index):
        body(pl.ds(aligned(index * 32, 32), 32))


def schedule(chunks, reduce, multiply, fetch, sums, finish, event=None, events=0, prepare=None):
    steps = chunks + 1 + LAG

    def ring_events(place):
        if event is not None:
            low = lax.div(place * events, 2 * steps)
            high = lax.div((place + 1) * events, 2 * steps)

            def some(index, carry):
                event(index)
                return carry

            lax.fori_loop(low, high, some, 0)

    def iteration(step):
        ring_events(2 * step)

        @pl.when((step >= LAG) & (step < chunks + LAG))
        def _():
            reduce.cross_fetch(step - LAG)

        @pl.when(step >= LAG)
        def _():
            fetch(step - LAG)

        @pl.when(step < chunks)
        def _():
            if prepare is not None:
                prepare(step)
            reduce.produce(step, lambda place: multiply(step, place))
            reduce.core_sum(step)

        ring_events(2 * step + 1)

        @pl.when(step >= 1 + LAG)
        def _():
            finish(step - 1 - LAG)

        @pl.when((step >= LAG) & (step < chunks + LAG))
        def _():
            reduce.cross_sum(step - LAG)
            sums(step - LAG)

    loop(steps, iteration)


def take(refs, counts):
    groups, start = [], 0
    for count in counts:
        groups.append(refs[start : start + count])
        start += count
    return groups


class Columns:
    def __init__(self, source, shard, left, turned, sem):
        self.source, self.shard = source, shard
        self.left, self.turned, self.sem = left, turned, sem

    @staticmethod
    def scratch(length, shard):
        return [
            pltpu.VMEM((length, shard), LOW),
            pltpu.VMEM((2, shard, length), LOW),
            pltpu.SemaphoreType.DMA((1,)),
        ]

    def copy(self, owner):
        each = self.source.shape[2] // self.shard
        at = pl.ds(aligned(lax.rem(owner, each) * self.shard, self.shard), self.shard)
        source = self.source.at[lax.div(owner, each), :, at]
        return pltpu.make_async_copy(source, self.left, self.sem.at[0])

    def take(self, ring, way, step):
        self.copy(ring.owner(way, step)).wait()
        self.turned[way] = self.left[...].T
        if way == 0:
            self.copy(ring.owner(1, step)).start()
        else:

            @pl.when(step + 1 < ring.count)
            def _():
                self.copy(ring.owner(0, step + 1)).start()


def attn_out(
    attended, weight, gain, tokens, out_grad, gate_shard, up_shard, down_shard, collective
):
    length, width = attended.shape
    chips = lax.axis_size("gx") // 2
    half = chips * width
    count = lax.axis_size("gy")
    chunks = count
    rows = length // chunks
    hidden = gate_shard.shape[1]
    inner = down_shard.shape[0]
    shard = gate_shard.shape[0]
    part_rows = shard // 2
    side = inner // 2
    down_columns = down_shard.shape[1]

    groups = [
        Reduce.scratch(rows, chunks, width, False),
        Stats.scratch(rows, chunks),
        Spread.scratch(rows, chunks, width),
        RingGather.scratch(3),
        [
            pltpu.VMEM((rows, half), LOW),
            pltpu.VMEM((2, rows, half), WIDE),
            pltpu.VMEM((2, rows, half), LOW),
            pltpu.SemaphoreType.DMA((chips,)),
            pltpu.SemaphoreType.DMA((2,)),
            pltpu.SemaphoreType.DMA((2,)),
            pltpu.SemaphoreType.DMA((2,)),
            pltpu.SemaphoreType.DMA((chips - 1, chunks, 2)),
        ],
        [
            pltpu.VMEM((2, D, hidden), LOW),
            pltpu.VMEM((count, inner, down_columns), LOW),
            pltpu.VMEM((chips, length, width), LOW),
        ],
    ]

    def kernel(*refs):
        ins, outs, *scratch = take(refs, [8, 8] + [len(g) for g in groups])
        attended, weight, gain, tokens, out_grad, gate_shard, up_shard, down_shard = ins
        raw_out, mixed_out, low_out, gate_full, up_full, down_full, upstream = outs[:7]
        cross_land = outs[7]
        reduce = Reduce(scratch[0], cross_land, rows, width, False)
        stats = Stats(*scratch[1])
        buffer, local, send, recv = scratch[2]
        spread = Spread(buffer, low_out, local, send, recv, rows, width)
        token_buf, mixed_buf, raw_buf = scratch[4][:3]
        token_sems, mixed_sems, raw_sems, own_sem, up_sems = scratch[4][3:]
        held, held_down, up_land = scratch[5]
        shards_here = (gate_shard, up_shard)

        def place_in(full, down):
            def slot(way, owner, part):
                if part == 2:
                    return down.at[owner, way * side : (way + 1) * side]
                base = owner * shard + part * part_rows
                return full[way].at[pl.ds(aligned(base, part_rows), part_rows)]

            return slot

        slot = place_in((held.at[0], held.at[1]), held_down)
        spill = place_in((gate_full, up_full), down_full)

        def source(way, part):
            if part == 2:
                return down_shard.at[way * side : (way + 1) * side]
            return shards_here[way].at[part * part_rows : (part + 1) * part_rows]

        ring = RingGather(source, slot, spill, 3, *scratch[3])
        own = pltpu.make_async_copy(out_grad, up_land.at[chip_here()], own_sem.at[0])
        up_spill = pltpu.make_async_copy(up_land, upstream, own_sem.at[1])

        def crossings(chunk):
            at = row_slice(chunk, rows)
            return [
                remote(
                    up_land.at[chip_here(), at],
                    up_land.at[chip_here(), at],
                    up_sems.at[shift - 1, chunk, 0],
                    up_sems.at[shift - 1, chunk, 1],
                    {"gx": peer_at(shift)},
                )
                for shift in range(1, chips)
            ]

        own.start()
        greet(True, True)
        ring.begin()
        own.wait()

        def multiply(chunk, place):
            return jnp.dot(
                attended[row_slice(chunk, rows)],
                weight[:, pl.ds(place, width)],
                preferred_element_type=WIDE,
            )

        def prepare(chunk):
            for item in crossings(chunk):
                item.start()

        def token_copies(chunk):
            return core_blocks(tokens, chunk, rows, width, token_buf, token_sems)

        def fetch(chunk):
            @pl.when(chunk >= 1)
            def _():
                for item in token_copies(chunk - 1):
                    item.start()

        def mixed_copy(chunk):
            slot = lax.rem(chunk, 2)
            return pltpu.make_async_copy(
                mixed_buf.at[slot, :, pl.ds(aligned(chip_here() * width, width), width)],
                mixed_out.at[row_slice(chunk, rows)],
                mixed_sems.at[slot],
            )

        def raw_copy(chunk):
            slot = lax.rem(chunk, 2)
            return pltpu.make_async_copy(
                raw_buf.at[slot], raw_out.at[row_slice(chunk, rows)], raw_sems.at[slot]
            )

        def sums(chunk):
            stats.clear(chunk)

            @pl.when(chunk >= 2)
            def _():
                raw_copy(chunk - 2).wait()

            def tile(at):
                raw = reduce.raw[at]
                raw_buf[lax.rem(chunk, 2), at] = raw.astype(LOW)
                squares = jnp.sum(raw * raw, axis=1, keepdims=True)
                stats.put(chunk, at, squares, squares)

            tiles(rows, tile)
            stats.copy(chunk).start()
            raw_copy(chunk).start()

        def finish(chunk):
            slot = lax.rem(chunk, 2)
            for item in token_copies(chunk):
                item.wait()
            stats.copy(chunk).wait_recv()
            spread.clear(chunk)

            @pl.when(chunk >= 2)
            def _():
                mixed_copy(chunk - 2).wait()

            def tile(at):
                squares, _ = stats.get(chunk, at)
                factor = lax.rsqrt(squares / D + EPS)
                mixed = token_buf[at].astype(WIDE) + reduce.raw[at] * factor * gain[...]
                mixed_buf[slot, at] = mixed
                spread.put(chunk, at, mixed)

            tiles(rows, tile)
            spread.go(chunk)
            mixed_copy(chunk).start()

        schedule(chunks, reduce, multiply, fetch, sums, finish, ring.event, ring.events, prepare)
        def drain(chunk):
            for item in crossings(chunk):
                item.wait()

        loop(chunks, drain)
        up_spill.start()
        ring.end()
        up_spill.wait()
        ring.settle()
        reduce.end(chunks)
        stats.end(chunks)
        spread.end(chunks)
        for chunk in (chunks - 2, chunks - 1):
            mixed_copy(chunk).wait()
            raw_copy(chunk).wait()

    shape = jax.ShapeDtypeStruct
    out = pl.pallas_call(
        kernel,
        out_shape=[
            shape((length, half), LOW),
            shape((length, width), WIDE),
            shape((2 * chips, length, width), LOW),
            shape((shard * count, hidden), LOW),
            shape((shard * count, hidden), LOW),
            shape((count, inner, down_columns), LOW),
            shape((chips, length, width), LOW),
        ]
        + Reduce.landing(rows, chunks, width, False),
        in_specs=[VMEM, VMEM, VMEM, HBM, HBM, HBM, HBM, HBM],
        out_specs=[HBM] * 8,
        scratch_shapes=[item for group in groups for item in group],
        compiler_params=pltpu.CompilerParams(
            collective_id=collective, has_side_effects=True, vmem_limit_bytes=60 * MIB
        ),
        cost_estimate=pl.CostEstimate(
            flops=2 * length * width * D, bytes_accessed=8 * length * D, transcendentals=0
        ),
    )(attended, weight, gain, tokens, out_grad, gate_shard, up_shard, down_shard)
    return out[:7]


def mlp_forward(
    inputs, gate_full, up_full, down_first, down_second, gain, mixed, upstream, collective
):
    length, inner = inputs.shape[1], gate_full.shape[1]
    width = mixed.shape[1]
    ranks = inputs.shape[0]
    down_columns = down_first.shape[2]
    down_rows = down_first.shape[1]
    chips = lax.axis_size("gx") // 2
    half = chips * width
    chunks = lax.axis_size("gy")
    rows = length // chunks
    tile = min(512, inner)
    pieces = inner // tile

    groups = [
        Reduce.scratch(rows, chunks, width, False),
        Stats.scratch(rows, chunks),
        Spread.scratch(rows, chunks, width),
        [
            pltpu.VMEM((2, rows, half), LOW),
            pltpu.VMEM((rows, width), WIDE),
            pltpu.VMEM((2, rows, width), LOW),
            pltpu.SemaphoreType.DMA((2, chips)),
            pltpu.SemaphoreType.DMA((1,)),
            pltpu.SemaphoreType.DMA((2,)),
        ],
        [
            pltpu.VMEM((D, inner), LOW),
            pltpu.VMEM((D, inner), LOW),
            pltpu.VMEM((inner, D), LOW),
            pltpu.VMEM((2, rows, D), LOW),
            pltpu.VMEM((2, 3, rows, inner), LOW),
            pltpu.SemaphoreType.DMA((pieces, 2)),
            pltpu.SemaphoreType.DMA((2, chunks)),
            pltpu.SemaphoreType.DMA((2, ranks)),
            pltpu.SemaphoreType.DMA((2, 3)),
        ],
    ]

    def kernel(*refs):
        ins, outs, *scratch = take(refs, [8, 7] + [len(g) for g in groups])
        inputs, gate_full, up_full, down_first, down_second, gain, mixed, upstream = ins
        result, grad_out, gain_grad, hidden_out, silu_out, slope_out, cross_land = outs
        gate_weight, up_weight, weight, row_buf, made = scratch[4][:5]
        piece_sems, weight_sem, row_sems, made_sems = scratch[4][5:]
        reduce = Reduce(scratch[0], cross_land, rows, width, False)
        stats = Stats(*scratch[1])
        buffer, local, send, recv = scratch[2]
        spread = Spread(buffer, grad_out, local, send, recv, rows, width)
        up_buf, mixed_buf, result_buf, up_sems, mixed_sems, result_sems = scratch[3]

        def piece_copies(piece):
            at = pl.ds(aligned(piece * tile, tile), tile)
            return [
                pltpu.make_async_copy(gate_full.at[:, at], gate_weight.at[:, at], piece_sems.at[piece, 0]),
                pltpu.make_async_copy(up_full.at[:, at], up_weight.at[:, at], piece_sems.at[piece, 1]),
            ]

        weight_copies = all_blocks(
            down_first, None, down_columns, weight.at[:down_rows], weight_sem.at[0]
        ) + all_blocks(down_second, None, down_columns, weight.at[down_rows:], weight_sem.at[1])

        def row_copy(chunk):
            slot = lax.rem(chunk, 2)
            return all_blocks(
                inputs, row_slice(chunk, rows), width, row_buf.at[slot], row_sems.at[slot]
            )

        def stores(chunk):
            slot, at = lax.rem(chunk, 2), row_slice(chunk, rows)
            return [
                pltpu.make_async_copy(made.at[slot, which], out.at[at], made_sems.at[slot, which])
                for which, out in enumerate((hidden_out, silu_out, slope_out))
            ]

        for item in row_copy(0):
            item.start()
        for piece in range(pieces):
            for item in piece_copies(piece):
                item.start()
        for item in weight_copies:
            item.start()
        greet(True, False)
        gain_grad[...] = jnp.zeros_like(gain_grad)

        def prepare(chunk):
            slot = lax.rem(chunk, 2)
            for item in row_copy(chunk):
                item.wait()

            @pl.when(chunk + 1 < chunks)
            def _():
                for item in row_copy(chunk + 1):
                    item.start()

            @pl.when(chunk >= 2)
            def _():
                for item in stores(chunk - 2):
                    item.wait()

            @pl.loop(0, pieces)
            def _(piece):
                @pl.when(chunk == 0)
                def _():
                    for item in piece_copies(piece):
                        item.wait()

                at = pl.ds(aligned(piece * tile, tile), tile)
                gate = jnp.dot(row_buf[slot], gate_weight[:, at], preferred_element_type=WIDE)
                up = jnp.dot(row_buf[slot], up_weight[:, at], preferred_element_type=WIDE)
                sigma = jax.nn.sigmoid(gate)
                silu = gate * sigma
                made[slot, 0, :, at] = (silu * up).astype(LOW)
                made[slot, 1, :, at] = silu.astype(LOW)
                made[slot, 2, :, at] = (up * (sigma + silu * (1.0 - sigma))).astype(LOW)

            @pl.when(chunk == 0)
            def _():
                for item in weight_copies:
                    item.wait()

            for item in stores(chunk):
                item.start()

        def multiply(chunk, place):
            return jnp.dot(
                made[lax.rem(chunk, 2), 0],
                weight[:, pl.ds(place, width)],
                preferred_element_type=WIDE,
            )

        def up_copy(chunk):
            slot = lax.rem(chunk, 2)
            return all_blocks(
                upstream, row_slice(chunk, rows), width, up_buf.at[slot], up_sems.at[slot]
            )

        def mixed_copy(chunk):
            return pltpu.make_async_copy(
                mixed.at[row_slice(chunk, rows)], mixed_buf, mixed_sems.at[0]
            )

        def result_copy(chunk):
            slot = lax.rem(chunk, 2)
            return pltpu.make_async_copy(
                result_buf.at[slot], result.at[row_slice(chunk, rows)], result_sems.at[slot]
            )

        def fetch(chunk):
            @pl.when(chunk < chunks)
            def _():
                for item in up_copy(chunk):
                    item.start()

            @pl.when(chunk >= 1)
            def _():
                mixed_copy(chunk - 1).start()

        def sums(chunk):
            slot = lax.rem(chunk, 2)
            stats.clear(chunk)
            for item in up_copy(chunk):
                item.wait()

            def tile(at):
                raw = reduce.raw[at]
                up = up_buf[slot, at].astype(WIDE)
                squares = jnp.sum(raw * raw, axis=1, keepdims=True)
                projected = jnp.sum(gain[...] * up * raw, axis=1, keepdims=True)
                stats.put(chunk, at, squares, projected)

            tiles(rows, tile)
            stats.copy(chunk).start()

        def finish(chunk):
            slot = lax.rem(chunk, 2)
            mixed_copy(chunk).wait()
            stats.copy(chunk).wait_recv()
            spread.clear(chunk)

            @pl.when(chunk >= 2)
            def _():
                result_copy(chunk - 2).wait()

            block = pl.ds(aligned(chip_here() * width, width), width)

            def tile(at):
                squares, projected = stats.get(chunk, at)
                factor = lax.rsqrt(squares / D + EPS)
                raw = reduce.raw[at]
                up = up_buf[slot, at].astype(WIDE)
                pull = factor * factor * factor * projected / D
                spread.put(chunk, at, factor * gain[...] * up - raw * pull)
                gain_grad[...] += jnp.sum(up * raw * factor, axis=0, keepdims=True)
                result_buf[slot, at] = (
                    mixed_buf[at] + reduce.raw[at, block] * factor * gain[:, block]
                ).astype(LOW)

            tiles(rows, tile)
            spread.go(chunk)
            result_copy(chunk).start()

        schedule(chunks, reduce, multiply, fetch, sums, finish, prepare=prepare)
        reduce.end(chunks)
        stats.end(chunks)
        spread.end(chunks)
        for chunk in (chunks - 2, chunks - 1):
            result_copy(chunk).wait()
            for item in stores(chunk):
                item.wait()

    shape = jax.ShapeDtypeStruct
    out = pl.pallas_call(
        kernel,
        out_shape=[
            shape((length, width), LOW),
            shape((2 * chips, length, width), LOW),
            shape((1, half), WIDE),
            shape((length, inner), LOW),
            shape((length, inner), LOW),
            shape((length, inner), LOW),
        ]
        + Reduce.landing(rows, chunks, width, False),
        in_specs=[HBM] * 5 + [VMEM, HBM, HBM],
        out_specs=[HBM, HBM, VMEM] + [HBM] * 4,
        scratch_shapes=[item for group in groups for item in group],
        compiler_params=pltpu.CompilerParams(
            collective_id=collective, has_side_effects=True, vmem_limit_bytes=60 * MIB
        ),
        cost_estimate=pl.CostEstimate(
            flops=6 * length * inner * D, bytes_accessed=16 * length * D, transcendentals=0
        ),
    )(inputs, gate_full, up_full, down_first, down_second, gain, mixed, upstream)
    return out[:6]


def mlp_back(gate_grad, up_grad, gate_full, up_full, inputs, gain, upstream, attn_raw, collective):
    length, inner = gate_grad.shape
    half = attn_raw.shape[1]
    chips = lax.axis_size("gx") // 2
    width = half // chips
    count = lax.axis_size("gy")
    chunks = count
    rows = length // chunks
    shard = D // count
    slots, parts = 2, 4
    piece = inner // parts

    groups = [
        Reduce.scratch(rows, chunks, width, False),
        Stats.scratch(rows, chunks),
        Spread.scratch(rows, chunks, width),
        RingScatter.scratch(shard, inner, slots, parts),
        [
            pltpu.VMEM((rows, half), LOW),
            pltpu.VMEM((2, rows, half), LOW),
            pltpu.SemaphoreType.DMA((chips,)),
            pltpu.SemaphoreType.DMA((2,)),
            pltpu.SemaphoreType.DMA((1,)),
            pltpu.SemaphoreType.DMA((2, parts)),
        ],
        Columns.scratch(length, shard),
        [
            pltpu.VMEM((2, length, inner), LOW),
            pltpu.VMEM((2, D, inner), LOW),
            pltpu.SemaphoreType.DMA((2, 2)),
        ],
    ]

    def kernel(*refs):
        ins, outs, *scratch = take(refs, [8, 6] + [len(g) for g in groups])
        gate_grad, up_grad, gate_full, up_full, inputs, gain, upstream, attn_raw = ins
        grads, weights, load_sems = scratch[6]
        grad_copies = [
            pltpu.make_async_copy((gate_grad, up_grad)[way], grads.at[way], load_sems.at[0, way])
            for way in range(2)
        ]
        weight_copies = [
            pltpu.make_async_copy((gate_full, up_full)[way], weights.at[way], load_sems.at[1, way])
            for way in range(2)
        ]
        mixed_out, grad_out, gain_grad, gate_out, up_out, cross_land = outs
        reduce = Reduce(scratch[0], cross_land, rows, width, False)
        stats = Stats(*scratch[1])
        buffer, local, send, recv = scratch[2]
        spread = Spread(buffer, grad_out, local, send, recv, rows, width)
        total, summed, land, ring_send, ring_recv, credit = scratch[3]
        up_buf, raw_buf, up_sems, raw_sems, mixed_sems, out_sems = scratch[4]
        left = Columns(inputs, shard, *scratch[5])

        def product(way, step, part):
            @pl.when(part == 0)
            def _():
                left.take(ring, way, step)

            @pl.when((part == 0) & (step == 0))
            def _():
                grad_copies[way].wait()

            columns = pl.ds(aligned(part * piece, piece), piece)
            total[way, part] = jnp.dot(
                left.turned[way], grads[way, :, columns], preferred_element_type=WIDE
            )

        ring = RingScatter(
            product, total, summed, land, ring_send, ring_recv, credit, slots, parts
        )
        left.copy(ring.owner(0, 0)).start()
        for item in grad_copies + weight_copies:
            item.start()
        greet(True, True)
        gain_grad[...] = jnp.zeros_like(gain_grad)

        def prepare(chunk):
            @pl.when(chunk == 0)
            def _():
                for item in weight_copies:
                    item.wait()

        def multiply(chunk, place):
            at = row_slice(chunk, rows)
            return nt(grads[0, at], weights[0, pl.ds(place, width)]) + nt(
                grads[1, at], weights[1, pl.ds(place, width)]
            )

        def up_copy(chunk):
            return all_blocks(upstream, row_slice(chunk, rows), width, up_buf, up_sems)

        def raw_copy(chunk):
            slot = lax.rem(chunk, 2)
            return pltpu.make_async_copy(
                attn_raw.at[row_slice(chunk, rows)], raw_buf.at[slot], raw_sems.at[slot]
            )

        def mixed_copy(chunk):
            return pltpu.make_async_copy(
                reduce.raw.at[:, pl.ds(aligned(chip_here() * width, width), width)],
                mixed_out.at[row_slice(chunk, rows)],
                mixed_sems.at[0],
            )

        def fetch(chunk):
            @pl.when(chunk < chunks)
            def _():
                for item in up_copy(chunk):
                    item.start()
                raw_copy(chunk).start()

        def sums(chunk):
            slot = lax.rem(chunk, 2)
            stats.clear(chunk)
            for item in up_copy(chunk):
                item.wait()
            raw_copy(chunk).wait()

            def tile(at):
                upward = reduce.raw[at] + up_buf[at].astype(WIDE)
                reduce.raw[at] = upward
                raw = raw_buf[slot, at].astype(WIDE)
                squares = jnp.sum(raw * raw, axis=1, keepdims=True)
                projected = jnp.sum(gain[...] * upward * raw, axis=1, keepdims=True)
                stats.put(chunk, at, squares, projected)

            tiles(rows, tile)
            stats.copy(chunk).start()
            mixed_copy(chunk).start()

        def finish(chunk):
            slot = lax.rem(chunk, 2)
            stats.copy(chunk).wait_recv()
            spread.clear(chunk)

            def tile(at):
                squares, projected = stats.get(chunk, at)
                factor = lax.rsqrt(squares / D + EPS)
                upward = reduce.raw[at]
                raw = raw_buf[slot, at].astype(WIDE)
                pull = factor * factor * factor * projected / D
                spread.put(chunk, at, factor * gain[...] * upward - raw * pull)
                gain_grad[...] += jnp.sum(upward * raw * factor, axis=0, keepdims=True)

            tiles(rows, tile)
            spread.go(chunk)
            mixed_copy(chunk).wait()

        schedule(chunks, reduce, multiply, fetch, sums, finish, ring.event, ring.events, prepare)
        writes = [
            pltpu.make_async_copy(
                total.at[way, part],
                (gate_out, up_out)[way].at[:, part * piece : (part + 1) * piece],
                out_sems.at[way, part],
            )
            for way in range(2)
            for part in range(parts)
        ]
        for item in writes:
            item.start()
        ring.end()
        reduce.end(chunks)
        stats.end(chunks)
        spread.end(chunks)
        for item in writes:
            item.wait()

    shape = jax.ShapeDtypeStruct
    out = pl.pallas_call(
        kernel,
        out_shape=[
            shape((length, width), WIDE),
            shape((length, D), LOW),
            shape((1, half), WIDE),
            shape((shard, inner), WIDE),
            shape((shard, inner), WIDE),
        ]
        + Reduce.landing(rows, chunks, width, False),
        in_specs=[HBM, HBM, HBM, HBM, HBM, VMEM, HBM, HBM],
        out_specs=[HBM, HBM, VMEM, HBM, HBM, HBM],
        scratch_shapes=[item for group in groups for item in group],
        compiler_params=pltpu.CompilerParams(
            collective_id=collective, has_side_effects=True, vmem_limit_bytes=60 * MIB
        ),
        cost_estimate=pl.CostEstimate(
            flops=8 * length * inner * D, bytes_accessed=16 * length * D, transcendentals=0
        ),
    )(gate_grad, up_grad, gate_full, up_full, inputs, gain, upstream, attn_raw)
    return out[:5]


class Total:
    def __init__(self, land, send, recv):
        self.land, self.send, self.recv = land, send, recv
        self.count = lax.axis_size("gx")

    @staticmethod
    def scratch(length):
        others = lax.axis_size("gx") - 1
        return [
            pltpu.VMEM((others, 8, length), WIDE),
            pltpu.SemaphoreType.DMA((others,)),
            pltpu.SemaphoreType.DMA((others,)),
        ]

    def copies(self, mine):
        return [
            remote(
                mine,
                self.land.at[shift - 1],
                self.send.at[shift - 1],
                self.recv.at[shift - 1],
                {"gx": rank_at(shift)},
            )
            for shift in range(1, self.count)
        ]

    def start(self, mine):
        for item in self.copies(mine):
            item.start()

    def finish(self, mine):
        for item in self.copies(mine):
            item.wait()
        total = mine[...]
        for shift in range(1, self.count):
            total = total + self.land[shift - 1]
        return total


def gather_in(tokens, stack, output_shard, gains, collective):
    length, width = tokens.shape
    _, shard, side = stack.shape
    columns = 2 * side
    count = lax.axis_size("gy")
    chunks = count
    rows = length // chunks
    chips = lax.axis_size("gx") // 2
    parts = 1
    out_columns = output_shard.shape[1]
    out_rows = width // 2
    ahead = chunks - 3

    groups = [
        RingGather.scratch(parts),
        [
            pltpu.SemaphoreType.DMA((1,)),
            pltpu.SemaphoreType.DMA((2,)),
            pltpu.SemaphoreType.DMA((chips - 1, chunks, 2)),
            pltpu.SemaphoreType.DMA((chips - 1, chunks, 2)),
        ],
        [
            pltpu.VMEM((2, D, side), LOW),
            pltpu.VMEM((2 * chips, length, width), LOW),
            pltpu.VMEM((2, 2, rows, width), WIDE),
            pltpu.VMEM((2, rows, width), LOW),
            pltpu.VMEM((length, STATS), WIDE),
            pltpu.VMEM((8, length), WIDE),
            pltpu.SemaphoreType.DMA((2,)),
            pltpu.SemaphoreType.DMA((2, 3)),
        ],
        Total.scratch(length),
        [
            pltpu.VMEM((chips - 1, 8, width), WIDE),
            pltpu.SemaphoreType.DMA((chips - 1, 2)),
        ],
        RingGather.scratch(1),
        [pltpu.VMEM((count, width, out_columns), LOW)],
    ]

    def kernel(*refs):
        ins, outs, *scratch = take(refs, [4, 8] + [len(g) for g in groups])
        tokens, stack, output_shard, gains = ins
        whole, full, output_full, query_raw, key_raw, values, squares, halves = outs
        out_held = scratch[6][0]
        gain_land, gain_sems = scratch[4]
        own_sem, core_sems, cross_sems, pass_sems = scratch[1]
        weight, held, raw_buf, value_buf, stats, mine = scratch[2][:6]
        copy_sems, out_sems = scratch[2][6:]
        total = Total(*scratch[3])

        def slot(way, owner, part):
            return weight.at[way, pl.ds(aligned(owner * shard, shard), shard)]

        def spill(way, owner, part):
            return full.at[way, pl.ds(aligned(owner * shard, shard), shard)]

        def source(way, part):
            return stack.at[way]

        ring = RingGather(source, slot, spill, parts, *scratch[0])

        def out_slot(way, owner, part):
            return out_held.at[owner, way * out_rows : (way + 1) * out_rows]

        def out_spill(way, owner, part):
            at = pl.ds(aligned(owner * out_columns, out_columns), out_columns)
            return output_full.at[way * out_rows : (way + 1) * out_rows, at]

        def out_source(way, part):
            return output_shard.at[way * out_rows : (way + 1) * out_rows]

        out_ring = RingGather(out_source, out_slot, out_spill, 1, *scratch[5])

        def block(rank, chunk):
            if chunk is None:
                return held.at[rank]
            return held.at[rank, row_slice(chunk, rows)]

        here = lax.axis_index("gx")
        own = pltpu.make_async_copy(tokens, block(here, None), own_sem.at[0])
        core = remote(
            block(here, None), block(here, None), core_sems.at[0], core_sems.at[1], {"gx": other_core()}
        )

        def cross(shift, chunk):
            return remote(
                block(here, chunk),
                block(here, chunk),
                cross_sems.at[shift - 1, chunk, 0],
                cross_sems.at[shift - 1, chunk, 1],
                {"gx": peer_at(shift)},
            )

        def onward(shift, chunk):
            spot = block(peer_at(chips - shift), chunk)
            return remote(
                spot,
                spot,
                pass_sems.at[shift - 1, chunk, 0],
                pass_sems.at[shift - 1, chunk, 1],
                {"gx": other_core()},
            )

        gain_copies = [
            remote(
                gains,
                gain_land.at[shift - 1],
                gain_sems.at[shift - 1, 0],
                gain_sems.at[shift - 1, 1],
                {"gx": peer_at(shift)},
            )
            for shift in range(1, chips)
        ]
        own.start()
        greet("all", True)
        for item in gain_copies:
            item.start()
        ring.begin()
        own.wait()

        def send(chunk):
            for shift in range(1, chips):
                cross(shift, chunk).start()

        loop(chunks, send)
        core.start()

        def step(chunk):
            for shift in range(1, chips):
                cross(shift, chunk).wait_recv()
                onward(shift, chunk).start()

            @pl.when(chunk < ring.events)
            def _():
                ring.event(chunk)

            @pl.when(chunk == ahead - 1)
            def _():
                out_ring.begin()

            @pl.when(chunk >= ahead)
            def _():
                out_ring.event(chunk - ahead)

        loop(chunks, step)
        ring.end()

        def drain(chunk):
            for shift in range(1, chips):
                cross(shift, chunk).wait_send()
                onward(shift, chunk).wait()

        loop(chunks, drain)
        core.wait()
        whole_copy = pltpu.make_async_copy(held, whole, copy_sems.at[0])
        whole_copy.start()

        def stores(chunk):
            slot, at = lax.rem(chunk, 2), row_slice(chunk, rows)
            return [
                pltpu.make_async_copy(raw_buf.at[slot, 0], query_raw.at[at], out_sems.at[slot, 0]),
                pltpu.make_async_copy(raw_buf.at[slot, 1], key_raw.at[at], out_sems.at[slot, 1]),
                pltpu.make_async_copy(value_buf.at[slot], values.at[at], out_sems.at[slot, 2]),
            ]

        lane = lax.broadcasted_iota(jnp.int32, (rows, STATS), 1)

        def project(chunk):
            slot = lax.rem(chunk, 2)
            @pl.when(chunk >= 2)
            def _():
                for item in stores(chunk - 2):
                    item.wait()

            at = row_slice(chunk, rows)
            middle = side - width

            row = jnp.concatenate([held[rank, at] for rank in range(2 * chips)], axis=1)

            def against(way, columns):
                return jnp.dot(row, weight[way, :, columns], preferred_element_type=WIDE)

            some = []
            raw_buf[slot, 0] = against(0, slice(0, width))
            raw_buf[slot, 1, :, :middle] = against(0, slice(width, side))
            raw_buf[slot, 1, :, middle:] = against(1, slice(0, middle))
            value_buf[slot] = against(1, slice(middle, side)).astype(LOW)
            for which in range(2):
                raw = raw_buf[slot, which]
                some.append(jnp.sum(raw * raw, axis=1, keepdims=True))
            stats[row_slice(chunk, rows)] = jnp.where(lane == 0, some[0], some[1])
            for item in stores(chunk):
                item.start()

            @pl.when(chunk + chunks - ahead < out_ring.events)
            def _():
                out_ring.event(chunk + chunks - ahead)

        loop(chunks, project)
        mine[...] = stats[...].T[:8]
        total.start(mine)
        for chunk in (chunks - 2, chunks - 1):
            for item in stores(chunk):
                item.wait()
        squares[...] = total.finish(mine)
        whole_copy.wait()
        ring.settle()
        out_ring.end()
        out_ring.settle()
        halves[:, pl.ds(aligned(chip_here() * width, width), width)] = gains[...]
        for shift in range(1, chips):
            gain_copies[shift - 1].wait()
            chip = lax.rem(chip_here() + chips - shift, chips)
            halves[:, pl.ds(aligned(chip * width, width), width)] = gain_land[shift - 1]

    shape = jax.ShapeDtypeStruct
    return pl.pallas_call(
        kernel,
        out_shape=[
            shape((2 * chips, length, width), LOW),
            shape((2, shard * count, side), LOW),
            shape((width, D), LOW),
            shape((length, width), WIDE),
            shape((length, width), WIDE),
            shape((length, width), LOW),
            shape((8, length), WIDE),
            shape((8, chips * width), WIDE),
        ],
        in_specs=[HBM, HBM, HBM, VMEM],
        out_specs=[HBM] * 6 + [VMEM, VMEM],
        scratch_shapes=[item for group in groups for item in group],
        compiler_params=pltpu.CompilerParams(
            collective_id=collective, has_side_effects=True, vmem_limit_bytes=40 * MIB
        ),
        cost_estimate=pl.CostEstimate(
            flops=2 * length * columns * D, bytes_accessed=8 * length * D, transcendentals=0
        ),
    )(tokens, stack, output_shard, gains)


def hidden_back(blocks, down_first, down_second, hidden, silu, slope, collective):
    length, inner = hidden.shape
    count = lax.axis_size("gy")
    chunks = count
    rows = length // chunks
    shard = D // count
    side = inner // 2
    slots, parts = 3, 4
    piece = side // parts
    down_rows = down_first.shape[1]
    tile = min(512, inner)

    groups = [
        RingScatter.scratch(shard, side, slots, parts),
        [
            pltpu.VMEM((2, 2, rows, inner), LOW),
            pltpu.VMEM((2, 2, rows, inner), LOW),
            pltpu.SemaphoreType.DMA((2, 2)),
            pltpu.SemaphoreType.DMA((2, 2)),
            pltpu.SemaphoreType.DMA((2, parts)),
            pltpu.VMEM((count, shard, length), LOW),
            pltpu.VMEM((2, parts, piece, shard), WIDE),
        ],
        [
            pltpu.VMEM((length, D), LOW),
            pltpu.VMEM((inner, D), LOW),
            pltpu.SemaphoreType.DMA((blocks.shape[0],)),
            pltpu.SemaphoreType.DMA((2, count)),
        ],
    ]

    def kernel(*refs):
        ins, outs, *scratch = take(refs, [6, 3] + [len(g) for g in groups])
        blocks, down_first, down_second, hidden, silu, slope = ins
        grad, weight, grad_sems, weight_sems = scratch[2]
        gate_grad, up_grad, weight_grad = outs
        total, summed, land, ring_send, ring_recv, credit = scratch[0]
        given, made, given_sems, made_sems, out_sems, turned, final = scratch[1]

        def product(way, step, part):
            owner = ring.owner(way, step)

            @pl.when((part == 0) & ((step < count // 2) | (step == count - 1)))
            def _():
                turned[owner] = grad[:, pl.ds(aligned(owner * shard, shard), shard)].T

            columns = pl.ds(aligned(way * side + part * piece, piece), piece)
            total[way, part] = jnp.dot(
                turned[owner], hidden[:, columns], preferred_element_type=WIDE
            )

        ring = RingScatter(
            product, total, summed, land, ring_send, ring_recv, credit, slots, parts
        )

        def load(chunk):
            slot = lax.rem(chunk, 2)
            return [
                pltpu.make_async_copy(
                    (slope, silu)[which].at[row_slice(chunk, rows)],
                    given.at[slot, which],
                    given_sems.at[slot, which],
                )
                for which in range(2)
            ]

        def store(chunk):
            slot = lax.rem(chunk, 2)
            return [
                pltpu.make_async_copy(
                    made.at[slot, which],
                    (gate_grad, up_grad)[which].at[row_slice(chunk, rows)],
                    made_sems.at[slot, which],
                )
                for which in range(2)
            ]

        grad_copies = all_blocks(blocks, None, blocks.shape[2], grad, grad_sems)
        weight_copies = all_blocks(
            down_first, None, shard, weight.at[:down_rows], weight_sems.at[0]
        ) + all_blocks(down_second, None, shard, weight.at[down_rows:], weight_sems.at[1])
        for item in grad_copies + weight_copies + load(0):
            item.start()
        greet(False, True)
        for item in grad_copies:
            item.wait()

        def iteration(step):
            slot = lax.rem(step, 2)
            @pl.when(step + 1 < chunks)
            def _():
                for item in load(step + 1):
                    item.start()

            @pl.when(step >= 2)
            def _():
                for item in store(step - 2):
                    item.wait()

            for item in load(step):
                item.wait()

            each = parts // (inner // tile)

            @pl.loop(0, inner // tile)
            def _(index):
                for which in range(each):
                    ring.event(step * parts + index * each + which)

                @pl.when((step == 0) & (index == 0))
                def _():
                    for item in weight_copies:
                        item.wait()

                at = pl.ds(aligned(index * tile, tile), tile)
                hidden_grad = nt(grad[row_slice(step, rows)], weight[at])
                for which in range(2):
                    made[slot, which, :, at] = (
                        hidden_grad * given[slot, which, :, at].astype(WIDE)
                    ).astype(LOW)

            for item in store(step):
                item.start()

        loop(chunks, iteration)
        writes = [
            pltpu.make_async_copy(
                final.at[way, part],
                weight_grad.at[way * side + part * piece : way * side + (part + 1) * piece],
                out_sems.at[way, part],
            )
            for way in range(2)
            for part in range(parts)
        ]
        for way in range(2):
            for part in range(parts):
                final[way, part] = total[way, part].T
        for item in writes:
            item.start()
        for chunk in (chunks - 2, chunks - 1):
            for item in store(chunk):
                item.wait()
        ring.end()
        for item in writes:
            item.wait()

    shape = jax.ShapeDtypeStruct
    return pl.pallas_call(
        kernel,
        out_shape=[
            shape((length, inner), LOW),
            shape((length, inner), LOW),
            shape((inner, shard), WIDE),
        ],
        in_specs=[HBM, HBM, HBM, VMEM, HBM, HBM],
        out_specs=[HBM, HBM, HBM],
        scratch_shapes=[item for group in groups for item in group],
        compiler_params=pltpu.CompilerParams(
            collective_id=collective, has_side_effects=True, vmem_limit_bytes=60 * MIB
        ),
        cost_estimate=pl.CostEstimate(
            flops=4 * length * inner * D, bytes_accessed=16 * length * D, transcendentals=0
        ),
    )(blocks, down_first, down_second, hidden, silu, slope)


def attn_in_back(
    query_back,
    key_back,
    value_grad,
    query_raw,
    key_raw,
    factors,
    projections,
    query_gain,
    key_gain,
    stack,
    inputs,
    mixed_grad,
    gain_parts,
    collective,
):
    length, columns = value_grad.shape[0], 2 * stack.shape[2]
    width = mixed_grad.shape[1]
    count = lax.axis_size("gy")
    chunks = count
    rows = length // chunks
    shard = D // count
    side = columns // 2
    slots, parts = count - 1, 3
    piece = side // parts

    groups = [
        Reduce.scratch(rows, chunks, width, True),
        RingScatter.scratch(shard, side, slots, parts),
        [
            pltpu.VMEM((rows, width), WIDE),
            pltpu.VMEM((2, rows, width), WIDE),
            pltpu.VMEM((length, columns), LOW),
            pltpu.VMEM((length, STATS), WIDE),
            pltpu.VMEM((2, 4, rows, width), WIDE),
            pltpu.VMEM((2, D, side), LOW),
            pltpu.SemaphoreType.DMA((2, 4)),
            pltpu.SemaphoreType.DMA((2,)),
            pltpu.SemaphoreType.DMA((1,)),
            pltpu.SemaphoreType.DMA((2,)),
            pltpu.SemaphoreType.DMA((2, parts)),
        ],
        Columns.scratch(length, shard),
        Total.scratch(length),
        [
            pltpu.VMEM((8, width), WIDE),
            pltpu.VMEM((count - 1, 8, width), WIDE),
            pltpu.SemaphoreType.DMA((count - 1, 2)),
        ],
    ]

    def kernel(*refs):
        ins, outs, *scratch = take(refs, [16, 4] + [len(g) for g in groups])
        query_back, key_back, value_grad, query_raw, key_raw, factors = ins[:6]
        projections, query_gain, key_gain, full, inputs, mixed_grad = ins[6:12]
        gain_parts = ins[12:]
        token_grad, weight_grad, gain_grads, cross_land = outs
        gain_mine, gain_land, gain_sems = scratch[5]
        reduce = Reduce(scratch[0], cross_land, rows, width, True)
        total, summed, land, ring_send, ring_recv, credit = scratch[1]
        mixed_buf, token_buf, grads, projected, given, stack = scratch[2][:6]
        given_sems, whole_sems, mixed_sems, token_sems, out_sems = scratch[2][6:]
        left = Columns(inputs, shard, *scratch[3])
        total_sum = Total(*scratch[4])

        def product(way, step, part):
            @pl.when(part == 0)
            def _():
                left.take(ring, way, step)

            columns = pl.ds(aligned(way * side + part * piece, piece), piece)
            total[way, part] = jnp.dot(
                left.turned[way], grads[:, columns], preferred_element_type=WIDE
            )

        ring = RingScatter(
            product, total, summed, land, ring_send, ring_recv, credit, slots, parts
        )
        def load(chunk):
            slot, at = lax.rem(chunk, 2), row_slice(chunk, rows)
            return [
                pltpu.make_async_copy(
                    source.at[at], given.at[slot, which], given_sems.at[slot, which]
                )
                for which, source in enumerate((query_back, key_back, query_raw, key_raw))
            ]

        value_copy = pltpu.make_async_copy(value_grad, grads.at[:, 2 * width :], whole_sems.at[0])
        stack_copy = pltpu.make_async_copy(full, stack, whole_sems.at[1])
        left.copy(ring.owner(0, 0)).start()
        for item in load(0):
            item.start()
        value_copy.start()
        stack_copy.start()
        chip_columns = pl.ds(aligned(chip_here() * width, width), width)
        gain_mine[...] = jnp.zeros_like(gain_mine)
        for which, part in enumerate(gain_parts):
            gain_mine[which : which + 1] = part[...] if which < 2 else part[:, chip_columns]
        greet("all", False, True)
        total_sum.start(projections)
        gain_copies = [
            remote(
                gain_mine,
                gain_land.at[shift - 1],
                gain_sems.at[shift - 1, 0],
                gain_sems.at[shift - 1, 1],
                {"gy": block_at(shift)},
            )
            for shift in range(1, count)
        ]
        for item in gain_copies:
            item.start()
        sums_here = total_sum.finish(projections)
        projected[...] = jnp.concatenate([sums_here] * (STATS // 8), axis=0).T

        def form(chunk):
            slot = lax.rem(chunk, 2)

            @pl.when(chunk + 1 < chunks)
            def _():
                for item in load(chunk + 1):
                    item.start()

            for item in load(chunk):
                item.wait()

            def some(part):
                at = pl.ds(aligned(chunk * rows + part.start, 32), 32)
                for which, gain in enumerate((query_gain, key_gain)):
                    factor = factors[at, which : which + 1]
                    pull = factor * factor * factor * projected[at, which : which + 1] / D
                    back, raw = given[slot, which, part], given[slot, which + 2, part]
                    grads[at, which * width : (which + 1) * width] = (
                        factor * gain[...] * back - raw * pull
                    ).astype(LOW)

            tiles(rows, some)

        loop(chunks, form)
        value_copy.wait()

        def prepare(chunk):
            @pl.when(chunk == 0)
            def _():
                stack_copy.wait()

        def multiply(chunk, place):
            at = row_slice(chunk, rows)
            return nt(grads[at, :side], stack[0, pl.ds(place, width)]) + nt(
                grads[at, side:], stack[1, pl.ds(place, width)]
            )

        def mixed_copy(chunk):
            return pltpu.make_async_copy(
                mixed_grad.at[row_slice(chunk, rows)], mixed_buf, mixed_sems.at[0]
            )

        def token_copy(chunk):
            slot = lax.rem(chunk, 2)
            return pltpu.make_async_copy(
                token_buf.at[slot], token_grad.at[row_slice(chunk, rows)], token_sems.at[slot]
            )

        def fetch(chunk):
            @pl.when(chunk >= 1)
            def _():
                mixed_copy(chunk - 1).start()

        def sums(chunk):
            pass

        def finish(chunk):
            slot = lax.rem(chunk, 2)
            mixed_copy(chunk).wait()

            @pl.when(chunk >= 2)
            def _():
                token_copy(chunk - 2).wait()

            def some(at):
                token_buf[slot, at] = mixed_buf[at] + reduce.raw[at]

            tiles(rows, some)
            token_copy(chunk).start()

        schedule(chunks, reduce, multiply, fetch, sums, finish, ring.event, ring.events, prepare)
        writes = [
            pltpu.make_async_copy(
                total.at[way, part],
                weight_grad.at[:, way * side + part * piece : way * side + (part + 1) * piece],
                out_sems.at[way, part],
            )
            for way in range(2)
            for part in range(parts)
        ]
        for item in writes:
            item.start()
        gain_total = gain_mine[...]
        for shift in range(1, count):
            gain_copies[shift - 1].wait()
            gain_total = gain_total + gain_land[shift - 1]
        gain_grads[...] = gain_total
        ring.end()
        reduce.end(chunks)
        for chunk in (chunks - 2, chunks - 1):
            token_copy(chunk).wait()
        for item in writes:
            item.wait()

    shape = jax.ShapeDtypeStruct
    out = pl.pallas_call(
        kernel,
        out_shape=[
            shape((length, width), WIDE),
            shape((shard, columns), WIDE),
            shape((8, width), WIDE),
        ]
        + Reduce.landing(rows, chunks, width, True),
        in_specs=[HBM] * 5 + [VMEM] * 4 + [HBM] * 3 + [VMEM] * 4,
        out_specs=[HBM, HBM, VMEM, HBM],
        scratch_shapes=[item for group in groups for item in group],
        compiler_params=pltpu.CompilerParams(
            collective_id=collective, has_side_effects=True, vmem_limit_bytes=60 * MIB
        ),
        cost_estimate=pl.CostEstimate(
            flops=4 * length * columns * D, bytes_accessed=8 * length * D, transcendentals=0
        ),
    )(
        query_back,
        key_back,
        value_grad,
        query_raw,
        key_raw,
        factors,
        projections,
        query_gain,
        key_gain,
        stack,
        inputs,
        mixed_grad,
        *gain_parts,
    )
    return out[:3]


def token_positions(segment):
    length = segment.shape[0]
    labels = jnp.arange(SEGS, dtype=jnp.int32)
    member = (segment[:, None] == labels[None, :]).astype(jnp.int32)
    totals = jnp.sum(member, axis=0)
    starts = jnp.cumsum(totals) - totals
    opening = jnp.sum(member * starts[None, :], axis=1)
    return jnp.arange(length, dtype=jnp.int32) - opening


def rotary_tables(segment):
    place = token_positions(segment).astype(jnp.float32)
    halves = HEAD // 2
    inverse = jnp.exp(jnp.arange(halves, dtype=jnp.float32) * (-2.0 * math.log(THETA) / HEAD))
    angle = place[:, None] * inverse[None, :]
    return (jnp.cos(angle), jnp.sin(angle))


BLOCK = 256
LANES = 128
SCALE = 1.0 / math.sqrt(HEAD)
SCALE_TWO = SCALE * math.log2(math.e)


def turn(values, cosine, sine):
    return values * cosine + pltpu.roll(values, HEAD // 2, 1) * sine


def head_columns(head):
    return slice(head * HEAD, (head + 1) * HEAD)


def nt(left, right):
    return lax.dot_general(left, right, (((1,), (1,)), ((), ())), preferred_element_type=WIDE)


def attend(first_block, query_raw, key_raw, values, factors, query_gain, key_gain, tables, starts):
    length, width = query_raw.shape
    heads = width // HEAD

    def kernel(
        first_block,
        query_raw,
        key_raw,
        values,
        factors,
        query_gain,
        key_gain,
        cosine,
        sine,
        starts,
        queries,
        keys,
        attended,
        peaks,
        peak_columns,
    ):
        @pl.loop(0, length // BLOCK)
        def _(index):
            at = row_slice(index, BLOCK)
            cos, sin = cosine[at], sine[at]
            pairs = ((query_raw, query_gain, queries), (key_raw, key_gain, keys))
            for which, (raw, gain, out) in enumerate(pairs):
                factor = factors[at, which : which + 1]
                for head in range(heads):
                    columns = head_columns(head)
                    normed = raw[at, columns] * factor * gain[:, columns]
                    out[at, columns] = turn(normed, cos, sin).astype(LOW)

        lane = lax.broadcasted_iota(jnp.int32, (BLOCK, LANES), 1)
        row_index = lax.broadcasted_iota(jnp.int32, (BLOCK, BLOCK), 0)
        column_index = lax.broadcasted_iota(jnp.int32, (BLOCK, BLOCK), 1)

        def query_block(index):
            at = row_slice(index, BLOCK)
            start = starts[at]

            def key_block(other, carry):
                there = row_slice(other, BLOCK)
                key_place = column_index + other * BLOCK
                allowed = (key_place >= start) & (key_place <= row_index + index * BLOCK)
                made = []
                for head in range(heads):
                    columns = head_columns(head)
                    peak, total, rows = carry[head]
                    scores = nt(queries[at, columns], keys[there, columns]) * SCALE_TWO
                    scores = jnp.where(allowed, scores, NEGATIVE)
                    higher = jnp.maximum(peak, jnp.max(scores, axis=1, keepdims=True))
                    raised = jnp.exp2(scores - higher)
                    shrink = jnp.exp2(peak - higher)
                    total = total * shrink + jnp.sum(raised, axis=1, keepdims=True)
                    rows = rows * shrink + jnp.dot(
                        raised.astype(LOW), values[there, columns], preferred_element_type=WIDE
                    )
                    made.append((higher, total, rows))
                return tuple(made)

            empty = (
                jnp.full((BLOCK, 1), NEGATIVE, WIDE),
                jnp.zeros((BLOCK, 1), WIDE),
                jnp.zeros((BLOCK, HEAD), WIDE),
            )
            done = lax.fori_loop(first_block[index], index + 1, key_block, (empty,) * heads)
            column = jnp.zeros((BLOCK, LANES), WIDE)
            for head in range(heads):
                peak, total, rows = done[head]
                attended[at, head_columns(head)] = (rows / total).astype(LOW)
                column = jnp.where(lane == head, peak + jnp.log2(total), column)
            peak_columns[at] = column

        loop(length // BLOCK, query_block)
        peaks[...] = peak_columns[...].T[:8]

    shape = jax.ShapeDtypeStruct
    smem = pl.BlockSpec(memory_space=pltpu.SMEM)
    return pl.pallas_call(
        kernel,
        out_shape=[
            shape((length, width), LOW),
            shape((length, width), LOW),
            shape((length, width), LOW),
            shape((8, length), WIDE),
        ],
        in_specs=[smem] + [VMEM] * 9,
        out_specs=[VMEM] * 4,
        scratch_shapes=[pltpu.VMEM((length, LANES), WIDE)],
        compiler_params=pltpu.CompilerParams(vmem_limit_bytes=48 * MIB),
        cost_estimate=pl.CostEstimate(
            flops=2 * length * MAX_LEN * width,
            bytes_accessed=16 * length * width,
            transcendentals=length * MAX_LEN * heads // 2,
        ),
    )(first_block, query_raw, key_raw, values, factors, query_gain, key_gain, *tables, starts)


def attend_back(
    last_block,
    queries,
    keys,
    values,
    attended,
    upstream,
    peaks,
    query_raw,
    key_raw,
    factors,
    query_gain,
    key_gain,
    tables,
    start_row,
    finished,
):
    length, width = query_raw.shape
    heads = width // HEAD

    extra = len(finished)

    def kernel(*refs):
        finished_in = refs[15 : 15 + extra]
        finished_out = refs[21 + extra : 21 + 2 * extra]
        held, copy_sems = refs[-1 - extra : -1], refs[-1]
        reads = [
            pltpu.make_async_copy(finished_in[i], held[i], copy_sems.at[0, i])
            for i in range(extra)
        ]
        writes = [
            pltpu.make_async_copy(held[i], finished_out[i], copy_sems.at[1, i])
            for i in range(extra)
        ]
        for item in reads:
            item.start()

        def pass_on():
            for read, write in zip(reads, writes):
                read.wait()
                write.start()

        work(pass_on, *refs[:15], *refs[15 + extra : 21 + extra], *refs[21 + 2 * extra : -1 - extra])
        for item in writes:
            item.wait()

    def work(
        pass_on,
        last_block,
        queries,
        keys,
        values,
        attended,
        upstream,
        peaks,
        query_raw,
        key_raw,
        factors,
        query_gain,
        key_gain,
        cosine,
        sine,
        start_row,
        query_out,
        key_out,
        value_out,
        projections,
        query_gain_grad,
        key_gain_grad,
        query_sum,
        key_sum,
        value_sum,
        columns_scratch,
        deltas,
    ):
        lane = lax.broadcasted_iota(jnp.int32, (BLOCK, LANES), 1)
        query_gain_grad[...] = jnp.zeros_like(query_gain_grad)
        key_gain_grad[...] = jnp.zeros_like(key_gain_grad)

        def prepare(index):
            at = row_slice(index, BLOCK)
            column = jnp.zeros((BLOCK, LANES), WIDE)
            for head in range(heads):
                columns = head_columns(head)
                delta = jnp.sum(
                    attended[at, columns].astype(WIDE) * upstream[at, columns].astype(WIDE),
                    axis=1,
                    keepdims=True,
                )
                column = jnp.where(lane == head, delta, column)
            columns_scratch[at] = column
            query_sum[at] = jnp.zeros((BLOCK, width), WIDE)

        loop(length // BLOCK, prepare)
        deltas[...] = columns_scratch[...].T[:8]
        pass_on()
        row_index = lax.broadcasted_iota(jnp.int32, (BLOCK, BLOCK), 0)
        column_index = lax.broadcasted_iota(jnp.int32, (BLOCK, BLOCK), 1)

        def turn_back(at, summed, raw, gain, factor, out, gain_grad):
            cos, sin = cosine[at], sine[at]
            share = jnp.zeros((BLOCK, 1), WIDE)
            for head in range(heads):
                columns = head_columns(head)
                normed = turn(summed(head) * SCALE, cos, -sin)
                out[at, columns] = normed
                weighed = normed * raw[at, columns]
                share += jnp.sum(gain[:, columns] * weighed, axis=1, keepdims=True)
                gain_grad[:, columns] += jnp.sum(weighed * factor, axis=0, keepdims=True)
            return share

        def key_block(index):
            at = row_slice(index, BLOCK)
            key_sum[...] = jnp.zeros_like(key_sum)
            value_sum[...] = jnp.zeros_like(value_sum)

            def query_block(other, carry):
                there = row_slice(other, BLOCK)
                key_place = row_index + index * BLOCK
                allowed = (key_place >= start_row[:, there]) & (
                    key_place <= column_index + other * BLOCK
                )
                for head in range(heads):
                    columns = head_columns(head)
                    scores = nt(keys[at, columns], queries[there, columns]) * SCALE_TWO
                    scores = jnp.where(allowed, scores, NEGATIVE)
                    chance = jnp.exp2(scores - peaks[head : head + 1, there])
                    value_sum[:, columns] += jnp.dot(
                        chance.astype(LOW), upstream[there, columns], preferred_element_type=WIDE
                    )
                    chance_grad = nt(values[at, columns], upstream[there, columns])
                    score_grad = (chance * (chance_grad - deltas[head : head + 1, there])).astype(LOW)
                    key_sum[:, columns] += jnp.dot(
                        score_grad, queries[there, columns], preferred_element_type=WIDE
                    )
                    query_sum[there, columns] += lax.dot_general(
                        score_grad,
                        keys[at, columns],
                        (((0,), (0,)), ((), ())),
                        preferred_element_type=WIDE,
                    )
                return carry

            lax.fori_loop(index, last_block[index] + 1, query_block, 0)
            value_out[at] = value_sum[...].astype(LOW)
            share = turn_back(
                at,
                lambda head: key_sum[:, head_columns(head)],
                key_raw,
                key_gain,
                factors[at, 1:2],
                key_out,
                key_gain_grad,
            )
            columns_scratch[at] = jnp.where(lane == 1, share, 0.0)

        loop(length // BLOCK, key_block)

        def finish(index):
            at = row_slice(index, BLOCK)
            share = turn_back(
                at,
                lambda head: query_sum[at, head_columns(head)],
                query_raw,
                query_gain,
                factors[at, 0:1],
                query_out,
                query_gain_grad,
            )
            columns_scratch[at] += jnp.where(lane == 0, share, 0.0)

        loop(length // BLOCK, finish)
        projections[...] = columns_scratch[...].T[:8]

    shape = jax.ShapeDtypeStruct
    smem = pl.BlockSpec(memory_space=pltpu.SMEM)
    return pl.pallas_call(
        kernel,
        out_shape=[
            shape((length, width), WIDE),
            shape((length, width), WIDE),
            shape((length, width), LOW),
            shape((8, length), WIDE),
            shape((1, width), WIDE),
            shape((1, width), WIDE),
        ]
        + [shape(item.shape, item.dtype) for item in finished],
        in_specs=[smem] + [VMEM] * 14 + [HBM] * extra,
        out_specs=[VMEM] * 6 + [HBM] * extra,
        scratch_shapes=[
            pltpu.VMEM((length, width), WIDE),
            pltpu.VMEM((BLOCK, width), WIDE),
            pltpu.VMEM((BLOCK, width), WIDE),
            pltpu.VMEM((length, LANES), WIDE),
            pltpu.VMEM((8, length), WIDE),
        ]
        + [pltpu.VMEM(item.shape, item.dtype) for item in finished]
        + [pltpu.SemaphoreType.DMA((2, extra))],
        compiler_params=pltpu.CompilerParams(vmem_limit_bytes=52 * MIB),
        cost_estimate=pl.CostEstimate(
            flops=5 * length * MAX_LEN * width,
            bytes_accessed=32 * length * width,
            transcendentals=length * MAX_LEN * heads // 2,
        ),
    )(
        last_block,
        queries,
        keys,
        values,
        attended,
        upstream,
        peaks,
        query_raw,
        key_raw,
        factors,
        query_gain,
        key_gain,
        *tables,
        start_row,
        *finished,
    )


def shards(
    tokens,
    query_weight,
    key_weight,
    value_weight,
    output_weight,
    gate_weight,
    up_weight,
    down_weight,
    query_gain,
    key_gain,
    attn_gain,
    mlp_gain,
    seq_ids,
    out_grad,
):
    segment = seq_ids[0]
    length = tokens.shape[0]
    local_width = tokens.shape[1]
    cosine, sine = rotary_tables(segment)
    tables = (
        jnp.concatenate([cosine, cosine], axis=1),
        jnp.concatenate([-sine, sine], axis=1),
    )
    order = jnp.arange(length, dtype=jnp.int32)
    starts = order - token_positions(segment)
    blocks = length // BLOCK
    first_block = starts.reshape(blocks, BLOCK)[:, 0] // BLOCK
    closing = segment.reshape(blocks, BLOCK)[:, -1]
    ends = jnp.sum((segment[None, :] <= closing[:, None]).astype(jnp.int32), axis=1) - 1
    last_block = ends // BLOCK
    gains = jnp.concatenate([attn_gain[None], mlp_gain[None], jnp.zeros((6, local_width))], axis=0)
    query_gain, key_gain = query_gain.reshape(1, -1), key_gain.reshape(1, -1)
    middle = local_width // 2
    pairs = (
        (query_weight, key_weight[:, :middle]),
        (key_weight[:, middle:], value_weight),
    )
    stack = jnp.stack([jnp.concatenate(pair, axis=1) for pair in pairs])
    inputs, attn_stack, output_full, query_raw, key_raw, values, squares, halves = gather_in(
        tokens, stack, output_weight, gains, 1
    )
    attn_half, mlp_half = halves[:1], halves[1:2]
    middle = down_weight.shape[0] // 4 * 3
    squares, down_rows = lax.optimization_barrier((squares, down_weight[middle:]))
    down_second = lax.all_gather(down_rows, "gy", axis=0)
    factors = lax.rsqrt(squares[:2].T / D + EPS)
    queries, keys, attended, peaks = attend(
        first_block,
        query_raw,
        key_raw,
        values,
        factors,
        query_gain,
        key_gain,
        tables,
        starts[:, None],
    )
    attn_raw, mixed, mlp_inputs, gate_full, up_full, down_first, upstream = attn_out(
        attended, output_full, attn_half, inputs, out_grad, gate_weight, up_weight, down_weight[:middle], 2
    )
    result, mlp_full, mlp_gain_part, hidden, silu, slope = mlp_forward(
        mlp_inputs, gate_full, up_full, down_first, down_second, mlp_half, mixed, upstream, 3
    )
    gate_grad, up_grad, down_weight_grad = hidden_back(
        mlp_full, down_first, down_second, hidden, silu, slope, 4
    )
    mixed_grad, attn_full, attn_gain_part, gate_weight_grad, up_weight_grad = mlp_back(
        gate_grad, up_grad, gate_full, up_full, mlp_inputs, attn_half, upstream, attn_raw, 5
    )
    output_product = lax.dot_general(
        attended, attn_full, (((0,), (0,)), ((), ())), preferred_element_type=jnp.float32
    )
    output_weight_grad = lax.psum_scatter(
        output_product.astype(jnp.bfloat16), "gy", scatter_dimension=1, tiled=True
    ).astype(jnp.float32)
    attended_grad = lax.dot_general(
        attn_full, output_full, (((1,), (1,)), ((), ())), preferred_element_type=jnp.float32
    ).astype(jnp.bfloat16)
    query_back, key_back, value_grad, projections, query_gain_part, key_gain_part, *done = attend_back(
        last_block,
        queries,
        keys,
        values,
        attended,
        attended_grad,
        peaks,
        query_raw,
        key_raw,
        factors,
        query_gain,
        key_gain,
        tables,
        starts[None, :],
        (result, gate_weight_grad, up_weight_grad, down_weight_grad),
    )
    result, gate_weight_grad, up_weight_grad, down_weight_grad = done
    token_grad, attn_weight_grads, gain_grads = attn_in_back(
        query_back,
        key_back,
        value_grad,
        query_raw,
        key_raw,
        factors,
        projections,
        query_gain,
        key_gain,
        attn_stack,
        inputs,
        mixed_grad,
        (query_gain_part, key_gain_part, attn_gain_part, mlp_gain_part),
        6,
    )
    query_weight_grad = attn_weight_grads[:, :local_width]
    key_weight_grad = attn_weight_grads[:, local_width : 2 * local_width]
    value_weight_grad = attn_weight_grads[:, 2 * local_width :]
    query_gain_grad, key_gain_grad, attn_gain_grad, mlp_gain_grad = (gain_grads[i] for i in range(4))
    return (
        result,
        token_grad,
        query_weight_grad,
        key_weight_grad,
        value_weight_grad,
        output_weight_grad,
        gate_weight_grad,
        up_weight_grad,
        down_weight_grad,
        query_gain_grad,
        key_gain_grad,
        attn_gain_grad,
        mlp_gain_grad,
    )


def solution(mesh):
    return jax.shard_map(
        shards,
        mesh=mesh,
        in_specs=(
            P("gy", "gx"),
            P("gy", "gx"),
            P("gy", "gx"),
            P("gy", "gx"),
            P("gx", "gy"),
            P("gy", "gx"),
            P("gy", "gx"),
            P("gx", "gy"),
            P("gx"),
            P("gx"),
            P("gx"),
            P("gx"),
            P("gy", None),
            P("gy", "gx"),
        ),
        out_specs=(
            P("gy", "gx"),
            P("gy", "gx"),
            P("gy", "gx"),
            P("gy", "gx"),
            P("gy", "gx"),
            P("gx", "gy"),
            P("gy", "gx"),
            P("gy", "gx"),
            P("gx", "gy"),
            P("gx"),
            P("gx"),
            P("gx"),
            P("gx"),
        ),
        check_vma=False,
    )
```
